32 devices in a mesh: dp: 32 (over z, y, x, core).
Axes of the slice: x: 2, y: 2, z: 4, core: 2. Of those that a mesh axis runs over, the one named last changes fastest.
Arguments:
- inputs: bfloat16 [8192, 1024], P('dp'), may hold values from -6 to 6
- lengths: int32 [16], replicated, may hold values from 288 to 512, as said below
- attention_projections: bfloat16 [4, 1024, 1024], P(None, 'dp'), may hold values from -0.1875 to 0.1875
- channel_key_weight: bfloat16 [1024, 4096], P('dp'), may hold values from -0.1875 to 0.1875
- channel_value_weight: bfloat16 [4096, 1024], P('dp'), may hold values from -0.09375 to 0.09375
- lowrank_down_weight: bfloat16 [1024, 256], P('dp'), may hold values from -0.1875 to 0.1875
- lowrank_up_weight: bfloat16 [256, 1024], P(None, 'dp'), may hold values from -0.5 to 0.5
- per_feature_parameters: bfloat16 [18, 1024], P(None, 'dp'), may hold values from -7 to 2
- cotangent: bfloat16 [8192, 1024], P('dp'), may hold values from -6 to 6
Outputs:
- output: bfloat16 [8192, 1024], P('dp')
- grad_inputs: float32 [8192, 1024], P('dp')
- grad_att_weights: float32 [4, 1024, 1024], P(None, 'dp')
- grad_ffn_key: float32 [1024, 4096], P('dp')
- grad_ffn_value: float32 [4096, 1024], P('dp')
- grad_lora_down: float32 [1024, 256], P('dp')
- grad_lora_up: float32 [256, 1024], P(None, 'dp')
- grad_vectors: float32 [18, 1024], P(None, 'dp')
The draws below stay inside these ranges and needn't reach their ends.
Inputs may be any that keep to these rules, and one draw needn't show every extreme that they name: Sequence s holds lengths[s] valid tokens at the start of its 512 slots, the rest are padding; in every draw one sequence is full and one holds exactly 288.
All inputs are finite; a program needn't handle non-finite values.
Results may differ from the reference program's by a relative error of at most 0.012.
The reference program's roundings to bfloat16 on the way count: a program that leaves them out, or rounds other values in their place, can miss the bound.
Values may be sent and summed in bfloat16 or wider, within the bound.
No kernel may reach another device: no remote copies, remote signals or barrier semaphores. Data moves between devices by JAX's collectives and lax.ppermute only.
A program may use at most 448 MiB of HBM per device.

```python
import math
import jax
import jax.numpy as jnp
from jax import lax

EMBED_DIMENSION = 1024
FF = 4096
HEADS = 16
HEAD_SIZE = 64
DECAY_RANK = 64
RATE_RANK = 64
GATE_INNER_WIDTH = 128
LOWRANK_WIDTH = 256
SEQ_LEN = 512
SEQS = 16
TOKENS = 8192
LEN_MIN = 288


def draw_lengths(key, part):
    key = jax.random.fold_in(key, 11)
    key_draw, key_full, key_short = jax.random.split(key, 3)
    drawn = jax.random.randint(key_draw, (SEQS,), LEN_MIN, SEQ_LEN + 1)
    full_seq = jax.random.randint(key_full, (), 0, SEQS)
    short_seq = (full_seq + 1 + jax.random.randint(key_short, (), 0, SEQS - 1)) % SEQS
    drawn = drawn.at[full_seq].set(SEQ_LEN)
    drawn = drawn.at[short_seq].set(LEN_MIN)
    return drawn.astype(jnp.int32)


def draw_per_feature_parameters(key, part):
    key = jax.random.fold_in(key, 23)
    sampling_seeds = jax.random.split(key, 8)
    sequence_blending = jax.random.uniform(sampling_seeds[0], (7, EMBED_DIMENSION), jnp.float32, 0.0, 1.0)
    forgetting_baseline = jax.random.uniform(sampling_seeds[1], (1, EMBED_DIMENSION), jnp.float32, -7.0, 2.0)
    replacement_baseline = jax.random.uniform(sampling_seeds[2], (1, EMBED_DIMENSION), jnp.float32, -2.0, 2.0)
    lookup_stretch_entries = jax.random.uniform(sampling_seeds[3], (1, EMBED_DIMENSION), jnp.float32, 0.5, 1.2)
    lookup_replace_entries = jax.random.uniform(sampling_seeds[4], (1, EMBED_DIMENSION), jnp.float32, 0.5, 1.5)
    extra_term_coefficients = 0.1 * jax.random.normal(sampling_seeds[5], (1, EMBED_DIMENSION), jnp.float32)
    multiplier_list = 1.0 + 0.15 * jax.random.normal(sampling_seeds[6], (3, EMBED_DIMENSION), jnp.float32)
    additive_shift_list = 0.2 * jax.random.normal(sampling_seeds[7], (3, EMBED_DIMENSION), jnp.float32)
    piled_entries = jnp.concatenate([sequence_blending, forgetting_baseline, replacement_baseline, lookup_stretch_entries, lookup_replace_entries, extra_term_coefficients, multiplier_list[0:1], additive_shift_list[0:1], multiplier_list[1:2], additive_shift_list[1:2], multiplier_list[2:3], additive_shift_list[2:3]], axis=0)
    return piled_entries.astype(jnp.bfloat16)


def level_of(own_key, shape, cuts, least, top_value):
    level, own = 1.0, jax.random.fold_in(own_key, 6)
    for position, parts in cuts:
        steps = jnp.exp(jax.random.uniform(jax.random.fold_in(own, position), (parts,), jnp.float32, least / len(cuts), top_value / len(cuts)))
        level = level * jnp.repeat(steps, shape[position] // parts).reshape([-1 if axis == position else 1 for axis in range(len(shape))])
    return level


def normal_values(stream_key, extent, deviation, reach, shards=(), held_as=jnp.bfloat16):
    gain = level_of(stream_key, extent, shards, -0.22, 0.18) if shards else 1.0
    values = jax.random.normal(stream_key, extent, jnp.float32) * deviation * gain
    return jnp.minimum(jnp.maximum(values, -reach), reach).astype(held_as)


def setup_inputs(seed: int = 0) -> dict:
    key_list = jax.random.split(jax.random.key(seed), 10)
    return {
        "inputs": normal_values(key_list[0], (TOKENS, EMBED_DIMENSION), 1.0, 6.0, ((0, 32),)),
        "lengths": draw_lengths(jax.random.fold_in(key_list[9], 71), 0),
        "attention_projections": normal_values(key_list[2], (4, EMBED_DIMENSION, EMBED_DIMENSION), EMBED_DIMENSION ** -0.5, 0.1875, ((1, 32),)),
        "channel_key_weight": normal_values(key_list[3], (EMBED_DIMENSION, FF), EMBED_DIMENSION ** -0.5, 0.1875, ((0, 32),)),
        "channel_value_weight": normal_values(key_list[4], (FF, EMBED_DIMENSION), FF ** -0.5, 0.09375, ((0, 32),)),
        "lowrank_down_weight": normal_values(key_list[5], (EMBED_DIMENSION, LOWRANK_WIDTH), EMBED_DIMENSION ** -0.5, 0.1875, ((0, 32),)),
        "lowrank_up_weight": normal_values(key_list[6], (LOWRANK_WIDTH, EMBED_DIMENSION), GATE_INNER_WIDTH ** -0.5, 0.5, ((1, 32),)),
        "per_feature_parameters": draw_per_feature_parameters(jax.random.fold_in(key_list[9], 71), 0),
        "cotangent": normal_values(key_list[8], (TOKENS, EMBED_DIMENSION), 1.0, 6.0, ((0, 32),)),
    }


PRECISE = lax.Precision.HIGHEST

@jax.custom_vjp
def low(v):
    return lax.optimization_barrier(v.astype(jnp.bfloat16)).astype(jnp.float32)

@jax.custom_vjp
def low_back(v):
    return v

def low_keep(v):
    return (low(v), None)

def low_pass(kept, grad):
    return (grad,)

def back_keep(v):
    return (v, None)

def back_low(kept, grad):
    return (low(grad),)
low.defvjp(low_keep, low_pass)
low_back.defvjp(back_keep, back_low)

def norm_rows(features, gain_row, offset_row):
    average = lax.optimization_barrier(jnp.mean(features, axis=-1, keepdims=True))
    centred = features - average
    variance = lax.optimization_barrier(jnp.mean(centred * centred, axis=-1, keepdims=True))
    return centred * lax.rsqrt(variance + 1e-05) * gain_row + offset_row

def earlier_rows(features):
    return jnp.concatenate([jnp.zeros_like(features[:, :1]), features[:, :-1]], axis=1)

def apply_projection(operand, weight_matrix):
    return jnp.einsum('gtd,de->gte', operand, weight_matrix, precision=PRECISE)

def split_into_sections(features):
    return features.reshape(features.shape[:-1] + (HEADS, HEAD_SIZE))

def token_scan(receptance_entries, decays, lookup_source_entries, payload_entries, alphas, betas):
    groups, length = (receptance_entries.shape[0], receptance_entries.shape[1])
    block_size = math.gcd(length, 64)
    block_count = length // block_size

    def to_blocks(features):
        return split_into_sections(features).reshape(groups, block_count, block_size, HEADS, HEAD_SIZE).transpose(1, 2, 0, 3, 4)

    def one_token(carried, inputs_now):
        query_now, decay_now, key_now, value_now, alpha_now, beta_now = inputs_now
        removed = jnp.einsum('ghvk,ghk->ghv', carried, alpha_now, precision=PRECISE)
        carried = carried * decay_now[:, :, None, :] + removed[..., None] * beta_now[:, :, None, :] + value_now[..., None] * key_now[:, :, None, :]
        return (carried, jnp.einsum('ghvk,ghk->ghv', carried, query_now, precision=PRECISE))

    def one_block(carried, inputs_now):
        return lax.scan(one_token, carried, inputs_now)
    initial = jnp.zeros((groups, HEADS, HEAD_SIZE, HEAD_SIZE), jnp.float32)
    blocked = tuple((to_blocks(features) for features in (receptance_entries, decays, lookup_source_entries, payload_entries, alphas, betas)))
    _, outputs = lax.scan(jax.checkpoint(one_block), initial, blocked)
    return outputs.transpose(2, 0, 1, 3, 4).reshape(groups, length, HEADS * HEAD_SIZE)

def block_forward(weight_matrices, tokens, live_mask):
    attention_projections, channel_key_weight, channel_value_weight, lowrank_down_weight, lowrank_up_weight, per_feature_parameters = weight_matrices
    rate_offset_index = DECAY_RANK
    gate_offset_index = DECAY_RANK + RATE_RANK
    normed = norm_rows(tokens, per_feature_parameters[12], per_feature_parameters[13])
    change = earlier_rows(normed) - normed
    mixed_token_rows = [low(normed + change * per_feature_parameters[which]) for which in range(6)]
    receptance_entries = low_back(apply_projection(mixed_token_rows[0], attention_projections[0]))
    lookup_entry_list = low_back(apply_projection(mixed_token_rows[2], attention_projections[1]))
    payload_entries = low_back(apply_projection(mixed_token_rows[3], attention_projections[2]))
    decay_logits = low_back(apply_projection(mixed_token_rows[1], lowrank_down_weight[:, :rate_offset_index]))
    rate_logits = low_back(apply_projection(mixed_token_rows[4], lowrank_down_weight[:, rate_offset_index:gate_offset_index]))
    gate_logits = low_back(apply_projection(mixed_token_rows[5], lowrank_down_weight[:, gate_offset_index:]))
    decay_lowrank = low_back(apply_projection(low(jnp.tanh(decay_logits)), lowrank_up_weight[:rate_offset_index]))
    rate_lowrank = low_back(apply_projection(low(rate_logits), lowrank_up_weight[rate_offset_index:gate_offset_index]))
    sigmoid_factors = low_back(apply_projection(low(jax.nn.sigmoid(gate_logits)), lowrank_up_weight[gate_offset_index:]))
    log_decay = -jnp.exp(-jax.nn.softplus(-(per_feature_parameters[7] + decay_lowrank)) - 0.5) * live_mask
    rates = jax.nn.sigmoid(per_feature_parameters[8] + rate_lowrank)
    scaled = split_into_sections(lookup_entry_list * per_feature_parameters[9])
    unit_keys = (scaled * lax.rsqrt(lax.optimization_barrier(jnp.sum(scaled * scaled, axis=-1, keepdims=True)) + 1e-06)).reshape(lookup_entry_list.shape)
    lookup_source_entries = lookup_entry_list * (1.0 + (rates - 1.0) * per_feature_parameters[10]) * live_mask
    betas = unit_keys * rates * live_mask
    blended_memory_entries = token_scan(receptance_entries, jnp.exp(log_decay), lookup_source_entries, payload_entries, -unit_keys, betas)
    heads_out = split_into_sections(blended_memory_entries)
    centred = heads_out - lax.optimization_barrier(jnp.mean(heads_out, axis=-1, keepdims=True))
    variance = lax.optimization_barrier(jnp.mean(centred * centred, axis=-1, keepdims=True))
    per_section_layout = (centred * lax.rsqrt(variance + 0.00064)).reshape(lookup_entry_list.shape) * per_feature_parameters[16] + per_feature_parameters[17]
    extra_term_share = lax.optimization_barrier(jnp.sum(split_into_sections(receptance_entries * lookup_source_entries * per_feature_parameters[11]), axis=-1, keepdims=True)) * split_into_sections(payload_entries)
    masked_result = low((per_section_layout + extra_term_share.reshape(lookup_entry_list.shape)) * sigmoid_factors)
    residual = tokens + low_back(apply_projection(masked_result, attention_projections[3]))
    second = norm_rows(residual, per_feature_parameters[14], per_feature_parameters[15])
    ffn_in = low(second + (earlier_rows(second) - second) * per_feature_parameters[6])
    hidden = low(jnp.square(jax.nn.relu(low_back(apply_projection(ffn_in, channel_key_weight)))))
    return (residual + low_back(apply_projection(hidden, channel_value_weight))) * live_mask

def reference(inputs, lengths, attention_projections, channel_key_weight, channel_value_weight, lowrank_down_weight, lowrank_up_weight, per_feature_parameters, cotangent):
    group = math.gcd(SEQS, max(1, 4096 // SEQ_LEN))
    shape_grouped = (SEQS // group, group, SEQ_LEN, EMBED_DIMENSION)
    positions = jnp.arange(SEQ_LEN, dtype=jnp.int32)
    live_mask = (positions[None, :] < lengths[:, None].astype(jnp.int32)).astype(jnp.float32)
    live_grouped = live_mask.reshape(SEQS // group, group, SEQ_LEN, 1)
    tokens = inputs.astype(jnp.float32).reshape(shape_grouped)
    weight_matrices = tuple((weight_matrix.astype(jnp.float32) for weight_matrix in (attention_projections, channel_key_weight, channel_value_weight, lowrank_down_weight, lowrank_up_weight, per_feature_parameters)))

    def whole(tokens_grouped, weights_now):

        def one_group(grouped_rows):
            return block_forward(weights_now, grouped_rows[0], grouped_rows[1])
        return lax.map(jax.checkpoint(one_group), (tokens_grouped, live_grouped))
    result, pullback = jax.vjp(whole, tokens, weight_matrices)
    grad_tokens, grad_weights = pullback(cotangent.astype(jnp.float32).reshape(shape_grouped))
    return (result.reshape(TOKENS, EMBED_DIMENSION).astype(jnp.bfloat16), grad_tokens.reshape(TOKENS, EMBED_DIMENSION), grad_weights[0], grad_weights[1], grad_weights[2], grad_weights[3], grad_weights[4], grad_weights[5])
```

```python
from functools import partial

import jax
import jax.numpy as jnp
from jax import lax
from jax.experimental import pallas as pl
from jax.experimental.pallas import tpu as pltpu
from jax.sharding import PartitionSpec as P

HEADS = 16
HEAD_SIZE = 64
DECAY_RANK = 64
RATE_RANK = 64
EMBED = 1024
OWN = EMBED // 2
PRECISE = lax.Precision.HIGHEST


CHUNK = 64
LANES = 256
GROUP_HEADS = 4
STEP_CHUNKS = 2

NN = (((1,), (0,)), ((), ()))
NT = (((1,), (1,)), ((), ()))
TN = (((0,), (0,)), ((), ()))


def halves(x):
    high = x.astype(jnp.bfloat16)
    return high, (x - high.astype(jnp.float32)).astype(jnp.bfloat16)


def dot32(a, b, dims):
    return lax.dot_general(a, b, dims, preferred_element_type=jnp.float32)


def mul(left, right, dims=NN):
    rows = left[0].shape[0]
    both = dot32(jnp.concatenate(left, axis=0), right[0], dims)
    return both[:rows] + both[rows:] + dot32(left[0], right[1], dims)


def tmul(left, right, masks):
    full = (
        dot32(left[0], right[0], TN) + dot32(left[1], right[0], TN) + dot32(left[0], right[1], TN)
    )
    return sum(full[h * CHUNK : (h + 1) * CHUNK] * masks[h][:1].astype(jnp.float32) for h in range(GROUP_HEADS))


def spread(pair, masks):
    return tuple(
        jnp.concatenate([part * masks[h] for h in range(GROUP_HEADS)], axis=0) for part in pair
    )


def stack(first, second):
    return tuple(jnp.concatenate([x, y], axis=0) for x, y in zip(first, second))


def head_masks():
    lane = lax.broadcasted_iota(jnp.int32, (CHUNK, LANES), 1) // CHUNK
    return [(lane == h).astype(jnp.float32).astype(jnp.bfloat16) for h in range(GROUP_HEADS)]


def places():
    row = lax.broadcasted_iota(jnp.int32, (CHUNK, LANES), 0)
    col = lax.broadcasted_iota(jnp.int32, (CHUNK, LANES), 1) % CHUNK
    return row, col


def running_sum(x, upper=False):
    row = lax.broadcasted_iota(jnp.int32, (CHUNK, CHUNK), 0)
    col = lax.broadcasted_iota(jnp.int32, (CHUNK, CHUNK), 1)
    ones = (row <= col if upper else col <= row).astype(jnp.float32).astype(jnp.bfloat16)
    high, rest = halves(x)
    low = (x - high.astype(jnp.float32) - rest.astype(jnp.float32)).astype(jnp.bfloat16)
    return dot32(ones, high, NN) + dot32(ones, rest, NN) + dot32(ones, low, NN)


def scaled_forms(q, w, k, a, b):
    total = running_sum(w)
    before = total - w
    middle = total[CHUNK // 2 - 1 : CHUNK // 2]
    end = total[CHUNK - 1 :]
    ea = jnp.exp(before - middle)
    eq = jnp.exp(total - middle)
    eb = jnp.exp(middle - total)
    ee = jnp.exp(end - total)
    return (a * ea, q * eq, b * eb, k * eb, b * ee, k * ee), (ea, eq, eb, ee), (jnp.exp(middle), jnp.exp(end))


def each(fn, *columns):
    return [fn(*row) for row in zip(*columns)]


def forward_kernel(
    q_ref, w_ref, k_ref, v_ref, a_ref, b_ref,
    o_ref, t_ref, aqb_ref, aak_ref, aqk_ref, wide_ref, y_ref, z_ref, trt_ref, qe_ref,
    state_ref,
):
    @pl.when(pl.program_id(0) == 0)
    def _():
        state_ref[...] = jnp.zeros_like(state_ref)

    masks = head_masks()
    row, col = places()
    strict = (col < row).astype(jnp.float32)
    within = (col <= row).astype(jnp.float32)
    eye = (col == row).astype(jnp.float32)
    units = [
        (slice(c * CHUNK, (c + 1) * CHUNK), slice(g * LANES, (g + 1) * LANES))
        for c in range(STEP_CHUNKS)
        for g in range(2)
    ]
    load = lambda ref: [ref[u] for u in units]
    q, w, k, v, a, b = (load(ref) for ref in (q_ref, w_ref, k_ref, v_ref, a_ref, b_ref))
    forms = each(scaled_forms, q, w, k, a, b)
    ah, qh, bh, kh, bt, kt = ([f[0][i] for f in forms] for i in range(6))
    emid = [f[2][0] for f in forms]
    eend = [f[2][1] for f in forms]
    aq = each(lambda x, y: halves(jnp.concatenate([x, y], axis=0)), ah, qh)
    with_b = each(lambda l, r: mul(l, spread(halves(r), masks), NT), aq, bh)
    with_k = each(lambda l, r: mul(l, spread(halves(r), masks), NT), aq, kh)
    aab = [x[:CHUNK] * strict for x in with_b]
    aqb = [halves(x[CHUNK:] * within) for x in with_b]
    aak = [halves(x[:CHUNK] * strict) for x in with_k]
    aqk = [halves(x[CHUNK:] * within) for x in with_k]
    p = [halves(x * (row // 8 == col // 8)) for x in aab]
    t = [eye + x * (row // 8 == col // 8) for x in aab]
    p2 = each(lambda x: halves(mul(x, spread(x, masks))), p)
    both = each(lambda x, y: mul(stack(x, halves(y)), spread(x, masks)), p2, t)
    p4 = [halves(x[:CHUNK]) for x in both]
    t = each(lambda x, y: x + y[CHUNK:], t, both)
    t = each(lambda x, y: x + mul(halves(x), spread(y, masks)), t, p4)
    for size in (8, 16, 32):
        corner = ((row // size) % 2 == 1) & (col // size == row // size - 1)
        ts = [halves(x) for x in t]
        n = [halves(x * corner) for x in aab]
        tn = each(lambda x, y: halves(mul(x, spread(y, masks))), ts, n)
        t = each(lambda x, y, z: x + mul(y, spread(z, masks)), t, tn, ts)
    ts = [halves(x) for x in t]
    vs = [halves(x) for x in v]
    vm = [spread(x, masks) for x in vs]
    wide = each(lambda x, y, e: mul(x, spread(halves(y * e), masks)), ts, ah, emid)
    r0 = each(mul, aak, vm)
    y0 = each(lambda x, y: mul(x, spread(halves(y), masks)), ts, r0)
    wides = [halves(x) for x in wide]
    qe = each(lambda x, e, y, z: x * e + mul(y, spread(z, masks)), qh, emid, aqb, wides)
    y0s = [halves(x) for x in y0]
    part = each(lambda x, y, z, u: mul(x, spread(y, masks)) + mul(z, u), aqb, y0s, aqk, vm)
    bts = [halves(x) for x in bt]
    diag = [eye * e for e in eend]
    tr = each(lambda x, y, d: tmul(x, y, masks) + d, bts, wides, diag)
    trt = each(lambda x, y, d: tmul(y, x, masks) + d, bts, wides, diag)
    inject = each(lambda x, y, z, u: tmul(stack(x, halves(y)), stack(z, u), masks), bts, kt, y0s, vs)
    wq = each(lambda x, y: stack(x, halves(y)), wides, qe)
    z = []
    out = []
    for c in range(STEP_CHUNKS):
        for g in range(2):
            i = c * 2 + g
            now = state_ref[g]
            nows = spread(halves(now), masks)
            state_ref[g] = mul(halves(tr[i]), nows) + inject[i]
            z.append(now)
            out.append(mul(wq[i], nows))
    for i, u in enumerate(units):
        o_ref[u] = out[i][CHUNK:] + part[i]
        y_ref[u] = out[i][:CHUNK] + y0[i]
        t_ref[u] = t[i]
        aqb_ref[u] = with_b[i][CHUNK:] * within
        aak_ref[u] = with_k[i][:CHUNK] * strict
        aqk_ref[u] = with_k[i][CHUNK:] * within
        wide_ref[u] = wide[i]
        z_ref[u] = z[i]
        trt_ref[u] = trt[i]
        qe_ref[u] = qe[i]


def backward_kernel(
    q_ref, w_ref, k_ref, v_ref, a_ref, b_ref,
    t_ref, aqb_ref, aak_ref, aqk_ref, y_ref, z_ref, trt_ref, qe_ref, do_ref,
    dq_ref, dw_ref, dk_ref, dv_ref, da_ref, db_ref,
    state_ref,
):
    @pl.when(pl.program_id(0) == 0)
    def _():
        state_ref[...] = jnp.zeros_like(state_ref)

    masks = head_masks()
    row, col = places()
    strict = (col < row).astype(jnp.float32)
    within = (col <= row).astype(jnp.float32)
    units = [
        (slice(c * CHUNK, (c + 1) * CHUNK), slice(g * LANES, (g + 1) * LANES))
        for c in range(STEP_CHUNKS)
        for g in range(2)
    ]
    load = lambda ref: [ref[u] for u in units]
    q, w, k, v, a, b = (load(ref) for ref in (q_ref, w_ref, k_ref, v_ref, a_ref, b_ref))
    do = [halves(x) for x in load(do_ref)]
    qe, trt, t, aqb, aak, aqk, ys = (
        [halves(x) for x in load(ref)]
        for ref in (qe_ref, trt_ref, t_ref, aqb_ref, aak_ref, aqk_ref, y_ref)
    )
    z = load(z_ref)
    vs = [halves(x) for x in v]
    h = each(lambda x, y: tmul(x, y, masks), qe, do)
    dz = [None] * len(units)
    for c in reversed(range(STEP_CHUNKS)):
        for g in range(2):
            i = c * 2 + g
            now = state_ref[g]
            dz[i] = now
            state_ref[g] = mul(trt[i], spread(halves(now), masks)) + h[i]
    dzs = [spread(halves(x), masks) for x in dz]
    zs = [spread(halves(x), masks) for x in z]
    forms = each(scaled_forms, q, w, k, a, b)
    ah, qh, bh, kh, bt, kt = ([f[0][i] for f in forms] for i in range(6))
    ea, eq, eb, ee = ([f[1][i] for f in forms] for i in range(4))
    emid = [f[2][0] for f in forms]
    eend = [f[2][1] for f in forms]
    from_end = each(lambda x, y, s: mul(halves(jnp.concatenate([x, y], axis=0)), s), bt, kt, dzs)
    dy = each(lambda x, y, s: halves(tmul(x, y, masks) + s[:CHUNK]), aqb, do, from_end)
    dr = each(lambda x, y: halves(tmul(x, y, masks)), t, dy)
    ro = each(stack, dr, do)
    dv = each(lambda x, y, s, f: tmul(stack(x, y), s, masks) + f[CHUNK:], aak, aqk, ro, from_end)
    mask2 = jnp.concatenate([strict, within], axis=0)
    dab = each(lambda s, y: halves(mul(s, spread(y, masks), NT) * mask2), ro, ys)
    dak = each(lambda s, y: halves(mul(s, spread(y, masks), NT) * mask2), ro, vs)
    dst = each(lambda s, y: mul(s, y, NT), ro, zs)
    daq = each(
        lambda s, e, x, bb, y, kk: s * e + mul(x, spread(halves(bb), masks)) + mul(y, spread(halves(kk), masks)),
        dst, emid, dab, bh, dak, kh,
    )
    aq = each(lambda x, y: halves(jnp.concatenate([x, y], axis=0)), ah, qh)
    dbh = each(lambda x, y: tmul(x, y, masks), dab, aq)
    dkh = each(lambda x, y: tmul(x, y, masks), dak, aq)
    dend = each(lambda y, x, s: mul(stack(y, x), s, NT), ys, vs, dzs)
    ones = jnp.ones((8, LANES), jnp.bfloat16)
    for i, u in enumerate(units):
        da = daq[i][:CHUNK] * ea[i]
        dq = daq[i][CHUNK:] * eq[i]
        dbt = dend[i][:CHUNK] * ee[i]
        dkt = dend[i][CHUNK:] * ee[i]
        db = dbh[i] * eb[i] + dbt
        dk = dkh[i] * eb[i] + dkt
        pa = da * a[i]
        diff = dq * q[i] - db * b[i] - dk * k[i] + pa
        zz = spread(halves(z[i] * dz[i]), masks)
        carry = (dot32(ones, zz[0], NT) + dot32(ones, zz[1], NT))[:1] * eend[i]
        carry = carry + jnp.sum(dbt * b[i] + dkt * k[i], axis=0, keepdims=True)
        dw_ref[u] = running_sum(diff, upper=True) - pa + carry
        da_ref[u] = da
        dq_ref[u] = dq
        db_ref[u] = db
        dk_ref[u] = dk
        dv_ref[u] = dv[i]


def wkv_forward(q, w, k, v, a, b):
    tokens, width = q.shape
    rows = CHUNK * STEP_CHUNKS
    spec = pl.BlockSpec((rows, width), lambda i: (i, 0))
    shape = jax.ShapeDtypeStruct((tokens, width), jnp.float32)
    return pl.pallas_call(
        forward_kernel,
        grid=(tokens // rows,),
        in_specs=[spec] * 6,
        out_specs=[spec] * 10,
        out_shape=[shape] * 10,
        scratch_shapes=[pltpu.VMEM((2, CHUNK, LANES), jnp.float32)],
        compiler_params=pltpu.CompilerParams(vmem_limit_bytes=48 << 20),
        name="wkv_forward",
    )(q, w, k, v, a, b)


def wkv_backward(q, w, k, v, a, b, saved, do):
    tokens, width = q.shape
    rows = CHUNK * STEP_CHUNKS
    steps = tokens // rows
    spec = pl.BlockSpec((rows, width), lambda i: (steps - 1 - i, 0))
    shape = jax.ShapeDtypeStruct((tokens, width), jnp.float32)
    return pl.pallas_call(
        backward_kernel,
        grid=(steps,),
        in_specs=[spec] * 15,
        out_specs=[spec] * 6,
        out_shape=[shape] * 6,
        scratch_shapes=[pltpu.VMEM((2, CHUNK, LANES), jnp.float32)],
        compiler_params=pltpu.CompilerParams(vmem_limit_bytes=48 << 20),
        name="wkv_backward",
    )(q, w, k, v, a, b, *saved, do)


def swap(block, mask):
    size = lax.axis_size("dp")
    return lax.ppermute(block, "dp", [(i, i ^ mask) for i in range(size)])


def bit_of(mask):
    return (lax.axis_index("dp") // mask) % 2


def in_order(mask, own, other, axis):
    lower = bit_of(mask) == 0
    return jnp.where(
        lower, jnp.concatenate([own, other], axis=axis), jnp.concatenate([other, own], axis=axis)
    )


def chip_masks():
    size = lax.axis_size("dp")
    masks = []
    while 2 << len(masks) < size:
        masks.append(2 << len(masks))
    return masks


def order_of(kind):
    masks = chip_masks()
    near, far = masks[:2], masks[2:][::-1]
    return far + (near[::-1] if kind == 0 else near)


def gather_chips(block, kind):
    order = order_of(kind)
    held = block[None]
    for mask in order:
        held = in_order(mask, held, swap(held, mask), 0)
        held = held.reshape((-1,) + block.shape)
    steps = len(order)
    held = held.reshape((2,) * steps + block.shape)
    applied = order[::-1]
    wanted = [applied.index(mask) for mask in chip_masks()[::-1]]
    held = held.transpose(tuple(wanted) + tuple(range(steps, steps + block.ndim)))
    return held.reshape((-1,) + block.shape)


def scatter_chips(parts, kind):
    order = order_of(kind)[::-1]
    axes = chip_masks()[::-1]
    shape = parts.shape[1:]
    held = parts.reshape((2,) * len(axes) + shape)
    for mask in order:
        place = axes.index(mask)
        axes = axes[:place] + axes[place + 1 :]
        bit = bit_of(mask)
        own = lax.dynamic_index_in_dim(held, bit, place, keepdims=False)
        other = lax.dynamic_index_in_dim(held, 1 - bit, place, keepdims=False)
        held = own + swap(other.astype(jnp.bfloat16), mask).astype(jnp.float32)
    return held


def norm_rows(features, gain_row, offset_row):
    average = jnp.mean(features, axis=-1, keepdims=True)
    centred = features - average
    variance = jnp.mean(centred * centred, axis=-1, keepdims=True)
    return centred * lax.rsqrt(variance + 1e-05) * gain_row + offset_row


def product(operand, weight_matrix):
    return jnp.dot(operand, weight_matrix, preferred_element_type=jnp.float32)


def input_gradient_rows(upstream_gradient, weight_matrix):
    return lax.dot_general(
        upstream_gradient,
        weight_matrix,
        (((1,), (1,)), ((), ())),
        preferred_element_type=jnp.float32,
    )


def weight_gradient(operand, upstream_gradient):
    return lax.dot_general(
        operand, upstream_gradient, (((0,), (0,)), ((), ())), preferred_element_type=jnp.float32
    )


def earlier(rows):
    return jnp.concatenate([jnp.zeros_like(rows[:1]), rows[:-1]], axis=0)


def front_mix(tokens, vectors):
    normed = norm_rows(tokens, vectors[12], vectors[13])
    change = earlier(normed) - normed
    return tuple((normed + change * vectors[which] for which in range(6)))


def lowrank_middle(decay_logits, rate_logits, gate_logits):
    return (jnp.tanh(decay_logits), rate_logits, jax.nn.sigmoid(gate_logits))


def head_sums(features):
    row = lax.broadcasted_iota(jnp.int32, (OWN, OWN), 0) // HEAD_SIZE
    col = lax.broadcasted_iota(jnp.int32, (OWN, OWN), 1) // HEAD_SIZE
    return jnp.dot(features, (row == col).astype(jnp.float32), precision=PRECISE)


def prepare(keys, decay_low, rate_low, vectors, live):
    log_decay = -jnp.exp(-jax.nn.softplus(-(vectors[7] + decay_low)) - 0.5) * live
    rates = jax.nn.sigmoid(vectors[8] + rate_low)
    scaled = keys * vectors[9]
    unit_keys = scaled * lax.rsqrt(head_sums(scaled * scaled) + 1e-06)
    key_in = keys * (1.0 + (rates - 1.0) * vectors[10]) * live
    return (log_decay, -unit_keys, unit_keys * rates * live, key_in)


def output_mix(mixed_state, queries, key_in, values, gate_rows, vectors):
    centred = mixed_state - head_sums(mixed_state) / HEAD_SIZE
    variance = head_sums(centred * centred) / HEAD_SIZE
    grouped = centred * lax.rsqrt(variance + 0.00064) * vectors[16] + vectors[17]
    bonus = head_sums(queries * key_in * vectors[11]) * values
    return (grouped + bonus) * gate_rows


def ffn_mix(residual, vectors):
    second = norm_rows(residual, vectors[14], vectors[15])
    return second + (earlier(second) - second) * vectors[6]


def squared(pre_act):
    return jnp.square(jax.nn.relu(pre_act))


def narrow(x):
    return x.astype(jnp.bfloat16)


def local(
    inputs,
    lengths,
    attention_projections,
    channel_key_weight,
    channel_value_weight,
    lowrank_down_weight,
    lowrank_up_weight,
    per_feature_parameters,
    cotangent,
):
    devices = lax.axis_size("dp")
    chips = devices // 2
    device = lax.axis_index("dp")
    chip, core = device // 2, device % 2
    row_count = inputs.shape[0]
    slots = 2 * row_count
    share = EMBED // devices
    pair_share = 2 * share
    units = channel_value_weight.shape[0]
    half_units = chips * units

    cut = attention_projections.transpose(1, 0, 2).reshape(share, 4, 2, OWN)
    key_cut = channel_key_weight.reshape(share, chips, 2, units)

    def columns(which):
        return jnp.concatenate(
            [
                lax.dynamic_index_in_dim(cut, which, 2, keepdims=False).reshape(share, 4 * OWN),
                lax.dynamic_index_in_dim(key_cut, which, 2, keepdims=False).reshape(
                    share, half_units
                ),
            ],
            axis=1,
        )

    pair_rows = in_order(1, columns(core), swap(columns(1 - core), 1), 0)
    misc = jnp.concatenate(
        [
            lowrank_down_weight,
            lowrank_up_weight.T,
            jnp.pad(per_feature_parameters.T, ((0, 0), (0, 128 - 18))),
        ],
        axis=1,
    )
    misc_all = gather_chips(misc, 1)
    first = gather_chips(pair_rows[:, :OWN], 0).reshape(EMBED, OWN)
    second_third = gather_chips(pair_rows[:, OWN : 3 * OWN], 1).reshape(EMBED, 2 * OWN)
    key_all = gather_chips(pair_rows[:, 3 * OWN :], 0).reshape(EMBED, OWN + half_units)
    value_weight = gather_chips(channel_value_weight, 1).reshape(half_units, EMBED)
    w_r, w_k, w_v = first, second_third[:, :OWN], second_third[:, OWN:]
    w_o_own, key_weight = key_all[:, :OWN], key_all[:, OWN:]
    w_o = in_order(1, w_o_own, swap(w_o_own, 1), 1)
    misc_all = in_order(1, misc_all[:, None], swap(misc_all, 1)[:, None], 1).reshape(EMBED, -1)
    down = misc_all[:, :256]
    up_t = lax.dynamic_slice_in_dim(misc_all[:, 256:512], core * OWN, OWN, 0)
    vectors = misc_all[:, 512:530].T.astype(jnp.float32)
    own_vectors = lax.dynamic_slice_in_dim(vectors, core * OWN, OWN, 1)

    tokens = in_order(1, inputs, swap(inputs, 1), 0).astype(jnp.float32)
    cot = in_order(1, cotangent, swap(cotangent, 1), 0).astype(jnp.float32)
    length = lax.dynamic_index_in_dim(lengths, chip, 0, keepdims=False)
    live = (lax.iota(jnp.int32, slots) < length).astype(jnp.float32)[:, None]
    cuts = ((0, 64), (64, 128), (128, 256))

    mixes, front_pull = jax.vjp(front_mix, tokens, vectors)
    mixes = [narrow(x) for x in mixes]
    queries = product(mixes[0], w_r)
    keys = product(mixes[2], w_k)
    values = product(mixes[3], w_v)
    logits = [product(mixes[m], down[:, lo:hi]) for m, (lo, hi) in zip((1, 4, 5), cuts)]
    hid, hid_pull = jax.vjp(lowrank_middle, *logits)
    hid = [narrow(x) for x in hid]
    decay_low, rate_low, gate_rows = (
        input_gradient_rows(x, up_t[:, lo:hi]) for x, (lo, hi) in zip(hid, cuts)
    )
    prepared, prepare_pull = jax.vjp(
        partial(prepare, live=live), keys, decay_low, rate_low, own_vectors
    )
    log_decay, alphas, betas, key_in = prepared
    terms = (queries, log_decay, key_in, values, alphas, betas)
    forward = wkv_forward(*terms)
    saved = [forward[i] for i in (1, 2, 3, 4, 6, 7, 8, 9)]
    gated, output_pull = jax.vjp(
        output_mix, forward[0], queries, key_in, values, gate_rows, own_vectors
    )
    gated = narrow(gated)
    gated_all = in_order(1, gated, swap(gated, 1), 1)
    residual = tokens + product(gated_all, w_o)
    ffn_in, ffn_pull = jax.vjp(ffn_mix, residual, vectors)
    ffn_in = narrow(ffn_in)
    pre_act = product(ffn_in, key_weight)
    hidden, square_pull = jax.vjp(squared, pre_act)
    hidden = narrow(hidden)
    ffn_part = product(hidden, value_weight)

    def own_rows(x, which):
        return lax.dynamic_slice_in_dim(x, which * row_count, row_count, 0)

    ffn_out = own_rows(ffn_part, core) + swap(own_rows(ffn_part, 1 - core), 1)
    output = narrow((own_rows(residual, core) + ffn_out) * own_rows(live, core))

    out_grad = cot * live
    out_narrow = narrow(out_grad)
    grad_value = weight_gradient(hidden, out_narrow)
    (pre_grad,) = square_pull(input_gradient_rows(out_narrow, value_weight))
    pre_narrow = narrow(pre_grad)
    grad_key = weight_gradient(ffn_in, pre_narrow)
    ffn_in_grad = input_gradient_rows(pre_narrow, key_weight)
    ffn_in_grad = ffn_in_grad + swap(ffn_in_grad, 1)
    residual_part, ffn_vector_grad = ffn_pull(ffn_in_grad)
    residual_grad = out_grad + residual_part
    attended_grad = narrow(residual_grad)
    grad_o = weight_gradient(
        gated_all, lax.dynamic_slice_in_dim(attended_grad, core * OWN, OWN, 1)
    )
    gated_grad = input_gradient_rows(
        attended_grad, lax.dynamic_slice_in_dim(w_o, core * OWN, OWN, 0)
    )
    state_grad, queries_part, key_in_part, values_part, gate_grad, output_vector_grad = output_pull(
        gated_grad
    )
    back = wkv_backward(*terms, saved, state_grad)
    key_grad, decay_grad, rate_grad, prepare_vector_grad = prepare_pull(
        (back[1], back[4], back[5], back[2] + key_in_part)
    )
    query_narrow = narrow(back[0] + queries_part)
    key_narrow = narrow(key_grad)
    value_narrow = narrow(back[3] + values_part)
    low_narrow = [narrow(decay_grad), narrow(rate_grad), narrow(gate_grad)]
    grad_up = jnp.concatenate([weight_gradient(g, h) for g, h in zip(low_narrow, hid)], axis=1)
    logit_grads = hid_pull(
        tuple(product(g, up_t[:, lo:hi]) for g, (lo, hi) in zip(low_narrow, cuts))
    )
    logit_narrow = [narrow(g) for g in logit_grads]
    grad_down = jnp.concatenate(
        [weight_gradient(mixes[m], g) for m, g in zip((1, 4, 5), logit_narrow)], axis=1
    )
    mix_grads = (
        input_gradient_rows(query_narrow, w_r),
        input_gradient_rows(logit_narrow[0], down[:, :64]),
        input_gradient_rows(key_narrow, w_k),
        input_gradient_rows(value_narrow, w_v),
        input_gradient_rows(logit_narrow[1], down[:, 64:128]),
        input_gradient_rows(logit_narrow[2], down[:, 128:]),
    )
    token_part, front_vector_grad = front_pull(mix_grads)
    input_gradient = (
        own_rows(residual_grad, core)
        + own_rows(token_part, core)
        + swap(own_rows(token_part, 1 - core), 1)
    )
    own_vector_grad = prepare_vector_grad + output_vector_grad
    vector_grad = front_vector_grad + 0.5 * ffn_vector_grad
    vector_grad = vector_grad + lax.dynamic_update_slice(
        jnp.zeros_like(vector_grad), own_vector_grad, (0, core * OWN)
    )

    value_sum = scatter_chips(grad_value.reshape(chips, units, EMBED), 1)
    grad_r, grad_k, grad_v = (
        weight_gradient(mixes[m], g)
        for m, g in zip((0, 2, 3), (query_narrow, key_narrow, value_narrow))
    )
    key_sum = scatter_chips(grad_key.reshape(chips, pair_share, half_units), 0)
    att = jnp.stack([grad_r, grad_k, grad_v, grad_o], axis=1).reshape(chips, pair_share, 4 * OWN)
    att_sum = jnp.concatenate(
        [scatter_chips(att[:, :, : 2 * OWN], 0), scatter_chips(att[:, :, 2 * OWN :], 1)], axis=1
    )
    pair_sum = jnp.concatenate([att_sum, key_sum], axis=1).reshape(2, share, -1)
    mine = lax.dynamic_index_in_dim(pair_sum, core, 0, keepdims=False)
    theirs = swap(lax.dynamic_index_in_dim(pair_sum, 1 - core, 0, keepdims=False), 1)
    shard_mixer = in_order(
        1,
        mine[:, : 4 * OWN].reshape(share, 4, 1, OWN),
        theirs[:, : 4 * OWN].reshape(share, 4, 1, OWN),
        2,
    )
    shard_mixer = shard_mixer.reshape(share, 4, EMBED).transpose(1, 0, 2)
    shard_key = in_order(
        1,
        mine[:, 4 * OWN :].reshape(share, chips, 1, units),
        theirs[:, 4 * OWN :].reshape(share, chips, 1, units),
        2,
    ).reshape(share, 2 * half_units)
    up_full = lax.dynamic_update_slice(
        jnp.zeros((EMBED, 256), jnp.float32), grad_up, (core * OWN, 0)
    )
    misc_grad = jnp.concatenate(
        [grad_down, up_full, jnp.pad(vector_grad.T, ((0, 0), (0, 128 - 18)))], axis=1
    ).reshape(chips, 2, share, 640)
    misc_mine = lax.dynamic_index_in_dim(misc_grad, core, 1, keepdims=False)
    misc_other = lax.dynamic_index_in_dim(misc_grad, 1 - core, 1, keepdims=False)
    misc_sum = scatter_chips(misc_mine + swap(misc_other, 1), 1)
    return (
        output,
        input_gradient,
        shard_mixer,
        shard_key,
        value_sum,
        misc_sum[:, :256],
        misc_sum[:, 256:512].T,
        misc_sum[:, 512:530].T,
    )


def solution(mesh):
    in_specs = (
        P("dp", None),
        P(),
        P(None, "dp", None),
        P("dp", None),
        P("dp", None),
        P("dp", None),
        P(None, "dp"),
        P(None, "dp"),
        P("dp", None),
    )
    out_specs = (
        P("dp", None),
        P("dp", None),
        P(None, "dp", None),
        P("dp", None),
        P("dp", None),
        P("dp", None),
        P(None, "dp"),
        P(None, "dp"),
    )
    return jax.shard_map(local, mesh=mesh, in_specs=in_specs, out_specs=out_specs, check_vma=False)
```

```python
from functools import partial

import jax
import jax.numpy as jnp
from jax import lax
from jax.experimental import pallas as pl
from jax.experimental.pallas import tpu as pltpu
from jax.sharding import PartitionSpec as P

HEADS = 16
HEAD_SIZE = 64
DECAY_RANK = 64
RATE_RANK = 64
EMBED = 1024
OWN = EMBED // 2
PRECISE = lax.Precision.HIGHEST


CHUNK = 64
LANES = 256
GROUP_HEADS = 4
STEP_CHUNKS = 2

NN = (((1,), (0,)), ((), ()))
NT = (((1,), (1,)), ((), ()))
TN = (((0,), (0,)), ((), ()))


def halves(x):
    high = x.astype(jnp.bfloat16)
    return high, (x - high.astype(jnp.float32)).astype(jnp.bfloat16)


def dot32(a, b, dims):
    return lax.dot_general(a, b, dims, preferred_element_type=jnp.float32)


def mul(left, right, dims=NN):
    rows = left[0].shape[0]
    both = dot32(jnp.concatenate(left, axis=0), right[0], dims)
    return both[:rows] + both[rows:] + dot32(left[0], right[1], dims)


def tmul(left, right, masks):
    full = (
        dot32(left[0], right[0], TN) + dot32(left[1], right[0], TN) + dot32(left[0], right[1], TN)
    )
    return sum(full[h * CHUNK : (h + 1) * CHUNK] * masks[h][:1].astype(jnp.float32) for h in range(GROUP_HEADS))


def spread(pair, masks):
    return tuple(
        jnp.concatenate([part * masks[h] for h in range(GROUP_HEADS)], axis=0) for part in pair
    )


def stack(first, second):
    return tuple(jnp.concatenate([x, y], axis=0) for x, y in zip(first, second))


def head_masks():
    lane = lax.broadcasted_iota(jnp.int32, (CHUNK, LANES), 1) // CHUNK
    return [(lane == h).astype(jnp.float32).astype(jnp.bfloat16) for h in range(GROUP_HEADS)]


def places():
    row = lax.broadcasted_iota(jnp.int32, (CHUNK, LANES), 0)
    col = lax.broadcasted_iota(jnp.int32, (CHUNK, LANES), 1) % CHUNK
    return row, col


def running_sum(x, upper=False):
    row = lax.broadcasted_iota(jnp.int32, (CHUNK, CHUNK), 0)
    col = lax.broadcasted_iota(jnp.int32, (CHUNK, CHUNK), 1)
    ones = (row <= col if upper else col <= row).astype(jnp.float32).astype(jnp.bfloat16)
    high, rest = halves(x)
    low = (x - high.astype(jnp.float32) - rest.astype(jnp.float32)).astype(jnp.bfloat16)
    return dot32(ones, high, NN) + dot32(ones, rest, NN) + dot32(ones, low, NN)


def scaled_forms(q, w, k, a, b):
    total = running_sum(w)
    before = total - w
    middle = total[CHUNK // 2 - 1 : CHUNK // 2]
    end = total[CHUNK - 1 :]
    ea = jnp.exp(before - middle)
    eq = jnp.exp(total - middle)
    eb = jnp.exp(middle - total)
    ee = jnp.exp(end - total)
    return (a * ea, q * eq, b * eb, k * eb, b * ee, k * ee), (ea, eq, eb, ee), (jnp.exp(middle), jnp.exp(end))


def each(fn, *columns):
    return [fn(*row) for row in zip(*columns)]


def forward_kernel(
    q_ref, w_ref, k_ref, v_ref, a_ref, b_ref,
    o_ref, t_ref, aqb_ref, aak_ref, aqk_ref, wide_ref, y_ref, z_ref, trt_ref, qe_ref,
    state_ref,
):
    @pl.when(pl.program_id(0) == 0)
    def _():
        state_ref[...] = jnp.zeros_like(state_ref)

    masks = head_masks()
    row, col = places()
    strict = (col < row).astype(jnp.float32)
    within = (col <= row).astype(jnp.float32)
    eye = (col == row).astype(jnp.float32)
    units = [
        (slice(c * CHUNK, (c + 1) * CHUNK), slice(g * LANES, (g + 1) * LANES))
        for c in range(STEP_CHUNKS)
        for g in range(2)
    ]
    load = lambda ref: [ref[u] for u in units]
    q, w, k, v, a, b = (load(ref) for ref in (q_ref, w_ref, k_ref, v_ref, a_ref, b_ref))
    forms = each(scaled_forms, q, w, k, a, b)
    ah, qh, bh, kh, bt, kt = ([f[0][i] for f in forms] for i in range(6))
    emid = [f[2][0] for f in forms]
    eend = [f[2][1] for f in forms]
    aq = each(lambda x, y: halves(jnp.concatenate([x, y], axis=0)), ah, qh)
    with_b = each(lambda l, r: mul(l, spread(halves(r), masks), NT), aq, bh)
    with_k = each(lambda l, r: mul(l, spread(halves(r), masks), NT), aq, kh)
    aab = [x[:CHUNK] * strict for x in with_b]
    aqb = [halves(x[CHUNK:] * within) for x in with_b]
    aak = [halves(x[:CHUNK] * strict) for x in with_k]
    aqk = [halves(x[CHUNK:] * within) for x in with_k]
    p = [halves(x * (row // 8 == col // 8)) for x in aab]
    t = [eye + x * (row // 8 == col // 8) for x in aab]
    p2 = each(lambda x: halves(mul(x, spread(x, masks))), p)
    both = each(lambda x, y: mul(stack(x, halves(y)), spread(x, masks)), p2, t)
    p4 = [halves(x[:CHUNK]) for x in both]
    t = each(lambda x, y: x + y[CHUNK:], t, both)
    t = each(lambda x, y: x + mul(halves(x), spread(y, masks)), t, p4)
    for size in (8, 16, 32):
        corner = ((row // size) % 2 == 1) & (col // size == row // size - 1)
        ts = [halves(x) for x in t]
        n = [halves(x * corner) for x in aab]
        tn = each(lambda x, y: halves(mul(x, spread(y, masks))), ts, n)
        t = each(lambda x, y, z: x + mul(y, spread(z, masks)), t, tn, ts)
    ts = [halves(x) for x in t]
    vs = [halves(x) for x in v]
    vm = [spread(x, masks) for x in vs]
    wide = each(lambda x, y, e: mul(x, spread(halves(y * e), masks)), ts, ah, emid)
    r0 = each(mul, aak, vm)
    y0 = each(lambda x, y: mul(x, spread(halves(y), masks)), ts, r0)
    wides = [halves(x) for x in wide]
    qe = each(lambda x, e, y, z: x * e + mul(y, spread(z, masks)), qh, emid, aqb, wides)
    y0s = [halves(x) for x in y0]
    part = each(lambda x, y, z, u: mul(x, spread(y, masks)) + mul(z, u), aqb, y0s, aqk, vm)
    bts = [halves(x) for x in bt]
    diag = [eye * e for e in eend]
    tr = each(lambda x, y, d: tmul(x, y, masks) + d, bts, wides, diag)
    trt = each(lambda x, y, d: tmul(y, x, masks) + d, bts, wides, diag)
    inject = each(lambda x, y, z, u: tmul(stack(x, halves(y)), stack(z, u), masks), bts, kt, y0s, vs)
    wq = each(lambda x, y: stack(x, halves(y)), wides, qe)
    z = []
    out = []
    for c in range(STEP_CHUNKS):
        for g in range(2):
            i = c * 2 + g
            now = state_ref[g]
            nows = spread(halves(now), masks)
            state_ref[g] = mul(halves(tr[i]), nows) + inject[i]
            z.append(now)
            out.append(mul(wq[i], nows))
    for i, u in enumerate(units):
        o_ref[u] = out[i][CHUNK:] + part[i]
        y_ref[u] = out[i][:CHUNK] + y0[i]
        t_ref[u] = t[i]
        aqb_ref[u] = with_b[i][CHUNK:] * within
        aak_ref[u] = with_k[i][:CHUNK] * strict
        aqk_ref[u] = with_k[i][CHUNK:] * within
        wide_ref[u] = wide[i]
        z_ref[u] = z[i]
        trt_ref[u] = trt[i]
        qe_ref[u] = qe[i]


def backward_kernel(
    q_ref, w_ref, k_ref, v_ref, a_ref, b_ref,
    t_ref, aqb_ref, aak_ref, aqk_ref, y_ref, z_ref, trt_ref, qe_ref, do_ref,
    dq_ref, dw_ref, dk_ref, dv_ref, da_ref, db_ref,
    state_ref,
):
    @pl.when(pl.program_id(0) == 0)
    def _():
        state_ref[...] = jnp.zeros_like(state_ref)

    masks = head_masks()
    row, col = places()
    strict = (col < row).astype(jnp.float32)
    within = (col <= row).astype(jnp.float32)
    units = [
        (slice(c * CHUNK, (c + 1) * CHUNK), slice(g * LANES, (g + 1) * LANES))
        for c in range(STEP_CHUNKS)
        for g in range(2)
    ]
    load = lambda ref: [ref[u] for u in units]
    q, w, k, v, a, b = (load(ref) for ref in (q_ref, w_ref, k_ref, v_ref, a_ref, b_ref))
    do = [halves(x) for x in load(do_ref)]
    qe, trt, t, aqb, aak, aqk, ys = (
        [halves(x) for x in load(ref)]
        for ref in (qe_ref, trt_ref, t_ref, aqb_ref, aak_ref, aqk_ref, y_ref)
    )
    z = load(z_ref)
    vs = [halves(x) for x in v]
    h = each(lambda x, y: tmul(x, y, masks), qe, do)
    dz = [None] * len(units)
    for c in reversed(range(STEP_CHUNKS)):
        for g in range(2):
            i = c * 2 + g
            now = state_ref[g]
            dz[i] = now
            state_ref[g] = mul(trt[i], spread(halves(now), masks)) + h[i]
    dzs = [spread(halves(x), masks) for x in dz]
    zs = [spread(halves(x), masks) for x in z]
    forms = each(scaled_forms, q, w, k, a, b)
    ah, qh, bh, kh, bt, kt = ([f[0][i] for f in forms] for i in range(6))
    ea, eq, eb, ee = ([f[1][i] for f in forms] for i in range(4))
    emid = [f[2][0] for f in forms]
    eend = [f[2][1] for f in forms]
    from_end = each(lambda x, y, s: mul(halves(jnp.concatenate([x, y], axis=0)), s), bt, kt, dzs)
    dy = each(lambda x, y, s: halves(tmul(x, y, masks) + s[:CHUNK]), aqb, do, from_end)
    dr = each(lambda x, y: halves(tmul(x, y, masks)), t, dy)
    ro = each(stack, dr, do)
    dv = each(lambda x, y, s, f: tmul(stack(x, y), s, masks) + f[CHUNK:], aak, aqk, ro, from_end)
    mask2 = jnp.concatenate([strict, within], axis=0)
    dab = each(lambda s, y: halves(mul(s, spread(y, masks), NT) * mask2), ro, ys)
    dak = each(lambda s, y: halves(mul(s, spread(y, masks), NT) * mask2), ro, vs)
    dst = each(lambda s, y: mul(s, y, NT), ro, zs)
    daq = each(
        lambda s, e, x, bb, y, kk: s * e + mul(x, spread(halves(bb), masks)) + mul(y, spread(halves(kk), masks)),
        dst, emid, dab, bh, dak, kh,
    )
    aq = each(lambda x, y: halves(jnp.concatenate([x, y], axis=0)), ah, qh)
    dbh = each(lambda x, y: tmul(x, y, masks), dab, aq)
    dkh = each(lambda x, y: tmul(x, y, masks), dak, aq)
    dend = each(lambda y, x, s: mul(stack(y, x), s, NT), ys, vs, dzs)
    ones = jnp.ones((8, LANES), jnp.bfloat16)
    for i, u in enumerate(units):
        da = daq[i][:CHUNK] * ea[i]
        dq = daq[i][CHUNK:] * eq[i]
        dbt = dend[i][:CHUNK] * ee[i]
        dkt = dend[i][CHUNK:] * ee[i]
        db = dbh[i] * eb[i] + dbt
        dk = dkh[i] * eb[i] + dkt
        pa = da * a[i]
        diff = dq * q[i] - db * b[i] - dk * k[i] + pa
        zz = spread(halves(z[i] * dz[i]), masks)
        carry = (dot32(ones, zz[0], NT) + dot32(ones, zz[1], NT))[:1] * eend[i]
        carry = carry + jnp.sum(dbt * b[i] + dkt * k[i], axis=0, keepdims=True)
        dw_ref[u] = running_sum(diff, upper=True) - pa + carry
        da_ref[u] = da
        dq_ref[u] = dq
        db_ref[u] = db
        dk_ref[u] = dk
        dv_ref[u] = dv[i]


def wkv_forward(q, w, k, v, a, b):
    tokens, width = q.shape
    rows = CHUNK * STEP_CHUNKS
    spec = pl.BlockSpec((rows, width), lambda i: (i, 0))
    shape = jax.ShapeDtypeStruct((tokens, width), jnp.float32)
    return pl.pallas_call(
        forward_kernel,
        grid=(tokens // rows,),
        in_specs=[spec] * 6,
        out_specs=[spec] * 10,
        out_shape=[shape] * 10,
        scratch_shapes=[pltpu.VMEM((2, CHUNK, LANES), jnp.float32)],
        compiler_params=pltpu.CompilerParams(vmem_limit_bytes=48 << 20),
        name="wkv_forward",
    )(q, w, k, v, a, b)


def wkv_backward(q, w, k, v, a, b, saved, do):
    tokens, width = q.shape
    rows = CHUNK * STEP_CHUNKS
    steps = tokens // rows
    spec = pl.BlockSpec((rows, width), lambda i: (steps - 1 - i, 0))
    shape = jax.ShapeDtypeStruct((tokens, width), jnp.float32)
    return pl.pallas_call(
        backward_kernel,
        grid=(steps,),
        in_specs=[spec] * 15,
        out_specs=[spec] * 6,
        out_shape=[shape] * 6,
        scratch_shapes=[pltpu.VMEM((2, CHUNK, LANES), jnp.float32)],
        compiler_params=pltpu.CompilerParams(vmem_limit_bytes=48 << 20),
        name="wkv_backward",
    )(q, w, k, v, a, b, *saved, do)


def swap(block, mask):
    size = lax.axis_size("dp")
    return lax.ppermute(block, "dp", [(i, i ^ mask) for i in range(size)])


def bit_of(mask):
    return (lax.axis_index("dp") // mask) % 2


def in_order(mask, own, other, axis):
    lower = bit_of(mask) == 0
    return jnp.where(
        lower, jnp.concatenate([own, other], axis=axis), jnp.concatenate([other, own], axis=axis)
    )


def chip_masks():
    size = lax.axis_size("dp")
    masks = []
    while 2 << len(masks) < size:
        masks.append(2 << len(masks))
    return masks


def order_of(kind):
    masks = chip_masks()
    near, far = masks[:2], masks[2:][::-1]
    return [far + near[::-1], far + near, near + far][kind]


def after(x, *others):
    return lax.optimization_barrier((x,) + others)[0]


class Gather:
    def __init__(self, block, kind):
        self.order = order_of(kind)
        self.held = block[None]
        self.other = None
        self.at = 0

    def step(self, *wait):
        if self.at == len(self.order):
            return self
        if self.other is not None:
            self.held = jnp.concatenate([self.held, self.other], axis=0)
        held = after(self.held, *wait) if wait else self.held
        self.other = swap(held, self.order[self.at])
        self.at += 1
        return self

    def run(self):
        while self.at < len(self.order):
            self.step()
        return self

    def places(self):
        out = [0]
        for mask in self.order:
            out = out + [p ^ (mask // 2) for p in out]
        return out


def place_kernel(places, rows, count, *refs):
    held, other, out, sems = refs[:count], refs[count : 2 * count], refs[2 * count : 3 * count], refs[-1]
    chip = lax.axis_index("dp") // 2
    half = len(places[0]) // 2
    copies = []
    for i in range(count):
        for j, place in enumerate(places[i]):
            source = held[i].at[j] if j < half else other[i].at[j - half]
            start = pl.multiple_of((chip ^ place) * rows[i], rows[i])
            copies.append(
                pltpu.make_async_copy(source, out[i].at[pl.ds(start, rows[i])], sems.at[len(copies)])
            )
    for copy in copies:
        copy.start()
    for copy in copies:
        copy.wait()


def assemble(*gathers):
    gathers = [g.run() for g in gathers]
    shapes = [g.held.shape[1:] for g in gathers]
    if any(shape[0] % 16 for shape in shapes):
        return [assemble_plain(g) for g in gathers]
    places = [g.places() for g in gathers]
    outs = [
        jax.ShapeDtypeStruct((len(p) * s[0],) + s[1:], g.held.dtype)
        for p, s, g in zip(places, shapes, gathers)
    ]
    space = pl.BlockSpec(memory_space=pl.ANY)
    return pl.pallas_call(
        partial(place_kernel, places, [s[0] for s in shapes], len(gathers)),
        in_specs=[space] * (2 * len(gathers)),
        out_specs=[space] * len(gathers),
        out_shape=outs,
        scratch_shapes=[pltpu.SemaphoreType.DMA((sum(len(p) for p in places),))],
        name="assemble",
    )(*[g.held for g in gathers], *[g.other for g in gathers])


def assemble_plain(gather):
    steps = len(gather.order)
    block = gather.held.shape[1:]
    held = jnp.concatenate([gather.held, gather.other], axis=0).reshape((2,) * steps + block)
    for place, mask in enumerate(gather.order[::-1]):
        held = jnp.where(bit_of(mask) == 0, held, jnp.flip(held, place))
    applied = gather.order[::-1]
    wanted = [applied.index(mask) for mask in chip_masks()[::-1]]
    held = held.transpose(tuple(wanted) + tuple(range(steps, steps + len(block))))
    return held.reshape((-1,) + block[1:])


class Scatter:
    def __init__(self, parts, kind):
        self.order = order_of(kind)[::-1]
        self.axes = chip_masks()[::-1]
        shape = parts.shape[1:]
        self.sources = [parts.reshape((2,) * len(self.axes) + shape)]
        self.sent = None

    def put(self, *wait):
        self.mask = self.order.pop(0)
        place = self.axes.index(self.mask)
        self.axes = self.axes[:place] + self.axes[place + 1 :]
        bit = bit_of(self.mask)
        pick = lambda x, which: lax.dynamic_index_in_dim(x, which, place, keepdims=False)
        send = sum(pick(x, 1 - bit).astype(jnp.float32) for x in self.sources).astype(jnp.bfloat16)
        self.sources = [pick(x, bit) for x in self.sources]
        return after(send, *wait) if wait else send

    def get(self, received):
        self.sources.append(received)

    def step(self, *wait):
        if not self.order:
            return self
        self.sent = self.put(*wait)
        self.get(swap(self.sent, self.mask))
        return self

    def run(self):
        while self.order:
            self.step()
        return self

    def total(self):
        return sum(x.astype(jnp.float32) for x in self.sources)


def norm_rows(features, gain_row, offset_row):
    average = jnp.mean(features, axis=-1, keepdims=True)
    centred = features - average
    variance = jnp.mean(centred * centred, axis=-1, keepdims=True)
    return centred * lax.rsqrt(variance + 1e-05) * gain_row + offset_row


def product(operand, weight_matrix):
    return jnp.dot(operand, weight_matrix, preferred_element_type=jnp.float32)


def input_gradient_rows(upstream_gradient, weight_matrix):
    return lax.dot_general(
        upstream_gradient,
        weight_matrix,
        (((1,), (1,)), ((), ())),
        preferred_element_type=jnp.float32,
    )


def weight_gradient(operand, upstream_gradient):
    return lax.dot_general(
        operand, upstream_gradient, (((0,), (0,)), ((), ())), preferred_element_type=jnp.float32
    )


def earlier(rows):
    return jnp.concatenate([jnp.zeros_like(rows[:1]), rows[:-1]], axis=0)


def front_mix(tokens, vectors):
    normed = norm_rows(tokens, vectors[12], vectors[13])
    change = earlier(normed) - normed
    return tuple((normed + change * vectors[which] for which in range(6)))


def lowrank_middle(decay_logits, rate_logits, gate_logits):
    return (jnp.tanh(decay_logits), rate_logits, jax.nn.sigmoid(gate_logits))


def head_sums(features):
    row = lax.broadcasted_iota(jnp.int32, (OWN, OWN), 0) // HEAD_SIZE
    col = lax.broadcasted_iota(jnp.int32, (OWN, OWN), 1) // HEAD_SIZE
    return jnp.dot(features, (row == col).astype(jnp.float32), precision=PRECISE)


def prepare(keys, decay_low, rate_low, vectors, live):
    log_decay = -jnp.exp(-jax.nn.softplus(-(vectors[7] + decay_low)) - 0.5) * live
    rates = jax.nn.sigmoid(vectors[8] + rate_low)
    scaled = keys * vectors[9]
    unit_keys = scaled * lax.rsqrt(head_sums(scaled * scaled) + 1e-06)
    key_in = keys * (1.0 + (rates - 1.0) * vectors[10]) * live
    return (log_decay, -unit_keys, unit_keys * rates * live, key_in)


def output_mix(mixed_state, queries, key_in, values, gate_rows, vectors):
    centred = mixed_state - head_sums(mixed_state) / HEAD_SIZE
    variance = head_sums(centred * centred) / HEAD_SIZE
    grouped = centred * lax.rsqrt(variance + 0.00064) * vectors[16] + vectors[17]
    bonus = head_sums(queries * key_in * vectors[11]) * values
    return (grouped + bonus) * gate_rows


def ffn_mix(residual, vectors):
    second = norm_rows(residual, vectors[14], vectors[15])
    return second + (earlier(second) - second) * vectors[6]


def squared(pre_act):
    return jnp.square(jax.nn.relu(pre_act))


def narrow(x):
    return x.astype(jnp.bfloat16)


def local(
    inputs,
    lengths,
    attention_projections,
    channel_key_weight,
    channel_value_weight,
    lowrank_down_weight,
    lowrank_up_weight,
    per_feature_parameters,
    cotangent,
):
    devices = lax.axis_size("dp")
    chips = devices // 2
    device = lax.axis_index("dp")
    chip, core = device // 2, device % 2
    row_count = inputs.shape[0]
    slots = 2 * row_count
    share = EMBED // devices
    pair_share = 2 * share
    units = channel_value_weight.shape[0]
    half_units = chips * units

    cut = attention_projections.reshape(4, share, 2, OWN)
    key_cut = channel_key_weight.reshape(share, chips, 2, units)

    def columns(which):
        return lax.dynamic_index_in_dim(cut, which, 2, keepdims=False)

    def key_columns(which):
        return lax.dynamic_index_in_dim(key_cut, which, 2, keepdims=False).reshape(share, half_units)

    tokens = in_order(1, inputs, swap(inputs, 1), 0).astype(jnp.float32)
    misc = jnp.concatenate(
        [
            lowrank_down_weight,
            lowrank_up_weight.T,
            jnp.pad(per_feature_parameters.T, ((0, 0), (0, 128 - 18))),
        ],
        axis=1,
    )
    small = Gather(misc, 0).step()
    own_columns, other_columns = columns(core), columns(1 - core)
    pair_rows = in_order(1, own_columns[:3], swap(other_columns[:3], 1), 1)
    small.step()
    parts = [Gather(pair_rows[i], kind) for i, kind in ((0, 0), (1, 1), (2, 2))]
    for part in parts:
        part.step()
    small.step()
    for part in parts:
        part.step()
    small.step()
    later_rows = in_order(1, own_columns[3], swap(other_columns[3], 1), 0)
    key_rows = in_order(1, key_columns(core), swap(key_columns(1 - core), 1), 0)
    z_done = parts[0].other
    w_o_part = Gather(later_rows, 2)
    key_parts = [Gather(key_rows[:, : half_units // 2], 0), Gather(key_rows[:, half_units // 2 :], 1)]
    value_parts = [
        Gather(channel_value_weight[:, :OWN], 0), Gather(channel_value_weight[:, OWN:], 1)
    ]
    for part in key_parts:
        part.step(z_done)
    for part in parts:
        part.step()
    for part in key_parts:
        part.step()
    w_o_part.step(z_done)
    for part in parts:
        part.run()
    w_r, w_k, w_v = assemble(*parts)
    w_o_part.step()
    for part in value_parts:
        part.step(key_parts[0].other, key_parts[1].other)
    for part in key_parts:
        part.step()
    w_o_part.step()
    for part in value_parts:
        part.step()
    for part in key_parts:
        part.run()
    w_o_part.run()
    for part in value_parts:
        part.run()
    (w_o_own,) = assemble(w_o_part)
    w_o = in_order(1, w_o_own, swap(w_o_own, 1), 1)
    key_weights = assemble(*key_parts)
    value_weights = assemble(*value_parts)
    (misc_all,) = assemble(small)
    misc_all = misc_all.reshape(chips, share, -1)
    misc_all = in_order(1, misc_all[:, None], swap(misc_all, 1)[:, None], 1).reshape(EMBED, -1)
    down = misc_all[:, :256]
    up_t = lax.dynamic_slice_in_dim(misc_all[:, 256:512], core * OWN, OWN, 0)
    vectors = misc_all[:, 512:530].T.astype(jnp.float32)
    own_vectors = lax.dynamic_slice_in_dim(vectors, core * OWN, OWN, 1)
    cot = in_order(1, cotangent, swap(cotangent, 1), 0).astype(jnp.float32)
    length = lax.dynamic_index_in_dim(lengths, chip, 0, keepdims=False)
    live = (lax.iota(jnp.int32, slots) < length).astype(jnp.float32)[:, None]
    cuts = ((0, 64), (64, 128), (128, 256))

    mixes, front_pull = jax.vjp(front_mix, tokens, vectors)
    mixes = [narrow(x) for x in mixes]
    queries = product(mixes[0], w_r)
    keys = product(mixes[2], w_k)
    values = product(mixes[3], w_v)
    logits = [product(mixes[m], down[:, lo:hi]) for m, (lo, hi) in zip((1, 4, 5), cuts)]
    hid, hid_pull = jax.vjp(lowrank_middle, *logits)
    hid = [narrow(x) for x in hid]
    decay_low, rate_low, gate_rows = (
        input_gradient_rows(x, up_t[:, lo:hi]) for x, (lo, hi) in zip(hid, cuts)
    )
    prepared, prepare_pull = jax.vjp(
        partial(prepare, live=live), keys, decay_low, rate_low, own_vectors
    )
    log_decay, alphas, betas, key_in = prepared
    terms = (queries, log_decay, key_in, values, alphas, betas)
    forward = wkv_forward(*terms)
    saved = [forward[i] for i in (1, 2, 3, 4, 6, 7, 8, 9)]
    gated, output_pull = jax.vjp(
        output_mix, forward[0], queries, key_in, values, gate_rows, own_vectors
    )
    gated = narrow(gated)
    gated_all = in_order(1, gated, swap(gated, 1), 1)
    residual = tokens + product(gated_all, w_o)
    ffn_in, ffn_pull = jax.vjp(ffn_mix, residual, vectors)
    ffn_in = narrow(ffn_in)
    pre_act = [product(ffn_in, x) for x in key_weights]
    hidden = [narrow(squared(x)) for x in pre_act]
    half = half_units // 2

    def own_rows(x, which):
        return lax.dynamic_slice_in_dim(x, which * row_count, row_count, 0)

    out_grad = cot * live
    out_narrow = narrow(out_grad)
    hidden_all = jnp.concatenate(hidden, axis=1)
    ffn_part = jnp.concatenate([product(hidden_all, x) for x in value_weights], axis=1)
    hidden_grad = sum(
        input_gradient_rows(out_narrow[:, i * OWN : (i + 1) * OWN], x)
        for i, x in enumerate(value_weights)
    )
    value_scatter = [
        Scatter(
            narrow(weight_gradient(hidden_all, out_narrow[:, i * OWN : (i + 1) * OWN])).reshape(
                chips, units, OWN
            ),
            i,
        )
        for i in range(2)
    ]
    for part in value_scatter:
        part.step()
    pre_narrow = [
        narrow(2.0 * jax.nn.relu(x) * hidden_grad[:, i * half : (i + 1) * half])
        for i, x in enumerate(pre_act)
    ]
    key_scatter = [
        Scatter(narrow(weight_gradient(ffn_in, x)).reshape(chips, pair_share, half), i)
        for i, x in enumerate(pre_narrow)
    ]
    ffn_in_grad = sum(input_gradient_rows(x, y) for x, y in zip(pre_narrow, key_weights))
    ffn_in_grad = ffn_in_grad + swap(ffn_in_grad, 1)
    for part in key_scatter:
        part.step(ffn_in_grad)
    ffn_out = own_rows(ffn_part, core) + swap(own_rows(ffn_part, 1 - core), 1)
    output = narrow((own_rows(residual, core) + ffn_out) * own_rows(live, core))
    residual_part, ffn_vector_grad = ffn_pull(ffn_in_grad)
    residual_grad = out_grad + residual_part
    attended_grad = narrow(residual_grad)
    grad_o = weight_gradient(
        gated_all, lax.dynamic_slice_in_dim(attended_grad, core * OWN, OWN, 1)
    )
    gated_grad = input_gradient_rows(
        attended_grad, lax.dynamic_slice_in_dim(w_o, core * OWN, OWN, 0)
    )
    state_grad, queries_part, key_in_part, values_part, gate_grad, output_vector_grad = output_pull(
        gated_grad
    )
    o_scatter = Scatter(narrow(grad_o).reshape(chips, pair_share, OWN), 2)
    for part in value_scatter:
        part.step()
    o_scatter.step()
    state_grad = after(state_grad, *[x.sent for x in value_scatter], o_scatter.sent)
    back = wkv_backward(*terms, saved, state_grad)
    for part in key_scatter:
        part.step(back[0])
    for part in value_scatter:
        part.step(back[0])
    o_scatter.step(back[0])
    key_grad, decay_grad, rate_grad, prepare_vector_grad = prepare_pull(
        (back[1], back[4], back[5], back[2] + key_in_part)
    )
    query_narrow = narrow(back[0] + queries_part)
    key_narrow = narrow(key_grad)
    value_narrow = narrow(back[3] + values_part)
    low_narrow = [narrow(decay_grad), narrow(rate_grad), narrow(gate_grad)]
    grad_up = jnp.concatenate([weight_gradient(g, h) for g, h in zip(low_narrow, hid)], axis=1)
    logit_grads = hid_pull(
        tuple(product(g, up_t[:, lo:hi]) for g, (lo, hi) in zip(low_narrow, cuts))
    )
    logit_narrow = [narrow(g) for g in logit_grads]
    grad_down = jnp.concatenate(
        [weight_gradient(mixes[m], g) for m, g in zip((1, 4, 5), logit_narrow)], axis=1
    )
    mix_grads = (
        input_gradient_rows(query_narrow, w_r),
        input_gradient_rows(logit_narrow[0], down[:, :64]),
        input_gradient_rows(key_narrow, w_k),
        input_gradient_rows(value_narrow, w_v),
        input_gradient_rows(logit_narrow[1], down[:, 64:128]),
        input_gradient_rows(logit_narrow[2], down[:, 128:]),
    )
    token_part, front_vector_grad = front_pull(mix_grads)
    input_gradient = (
        own_rows(residual_grad, core)
        + own_rows(token_part, core)
        + swap(own_rows(token_part, 1 - core), 1)
    )
    own_vector_grad = prepare_vector_grad + output_vector_grad
    vector_grad = front_vector_grad + 0.5 * ffn_vector_grad
    vector_grad = vector_grad + lax.dynamic_update_slice(
        jnp.zeros_like(vector_grad), own_vector_grad, (0, core * OWN)
    )

    att_scatter = [
        Scatter(narrow(weight_gradient(mixes[m], g)).reshape(chips, pair_share, OWN), kind)
        for m, g, kind in zip((0, 2, 3), (query_narrow, key_narrow, value_narrow), (0, 1, 2))
    ]
    for part in att_scatter:
        part.step()
    for part in value_scatter + key_scatter + [o_scatter]:
        part.run()
    for part in att_scatter:
        part.run()
    value_sum = jnp.concatenate([x.total() for x in value_scatter], axis=1)
    pair_sum = jnp.concatenate(
        [x.total() for x in att_scatter + [o_scatter] + key_scatter], axis=1
    ).reshape(2, share, -1)
    mine = lax.dynamic_index_in_dim(pair_sum, core, 0, keepdims=False)
    theirs = swap(lax.dynamic_index_in_dim(pair_sum, 1 - core, 0, keepdims=False), 1)
    shard_mixer = jnp.stack(
        [
            in_order(1, mine[:, i * OWN : (i + 1) * OWN], theirs[:, i * OWN : (i + 1) * OWN], 1)
            for i in range(4)
        ]
    )
    shard_key = in_order(
        1,
        mine[:, 4 * OWN :].reshape(share, chips, 1, units),
        theirs[:, 4 * OWN :].reshape(share, chips, 1, units),
        2,
    ).reshape(share, 2 * half_units)
    up_full = lax.dynamic_update_slice(
        jnp.zeros((EMBED, 256), jnp.float32), grad_up, (core * OWN, 0)
    )
    misc_grad = jnp.concatenate(
        [grad_down, up_full, jnp.pad(vector_grad.T, ((0, 0), (0, 128 - 18)))], axis=1
    ).reshape(chips, 2, share, 640)
    misc_mine = lax.dynamic_index_in_dim(misc_grad, core, 1, keepdims=False)
    misc_other = lax.dynamic_index_in_dim(misc_grad, 1 - core, 1, keepdims=False)
    misc_sum = Scatter(misc_mine + swap(misc_other, 1), 0).run().total()
    return (
        output,
        input_gradient,
        shard_mixer,
        shard_key,
        value_sum,
        misc_sum[:, :256],
        misc_sum[:, 256:512].T,
        misc_sum[:, 512:530].T,
    )


def solution(mesh):
    in_specs = (
        P("dp", None),
        P(),
        P(None, "dp", None),
        P("dp", None),
        P("dp", None),
        P("dp", None),
        P(None, "dp"),
        P(None, "dp"),
        P("dp", None),
    )
    out_specs = (
        P("dp", None),
        P("dp", None),
        P(None, "dp", None),
        P("dp", None),
        P("dp", None),
        P("dp", None),
        P(None, "dp"),
        P(None, "dp"),
    )
    return jax.shard_map(local, mesh=mesh, in_specs=in_specs, out_specs=out_specs, check_vma=False)
```

```python
from functools import partial

import jax
import jax.numpy as jnp
from jax import lax
from jax.experimental import pallas as pl
from jax.experimental.pallas import tpu as pltpu
from jax.sharding import PartitionSpec as P

HEADS = 16
HEAD_SIZE = 64
DECAY_RANK = 64
RATE_RANK = 64
EMBED = 1024
OWN = EMBED // 2
PRECISE = lax.Precision.HIGHEST


CHUNK = 64
LANES = 256
GROUP_HEADS = 4
STEP_CHUNKS = 2

NN = (((1,), (0,)), ((), ()))
NT = (((1,), (1,)), ((), ()))
TN = (((0,), (0,)), ((), ()))


def halves(x):
    high = x.astype(jnp.bfloat16)
    return high, (x - high.astype(jnp.float32)).astype(jnp.bfloat16)


def dot32(a, b, dims):
    return lax.dot_general(a, b, dims, preferred_element_type=jnp.float32)


def mul(left, right, dims=NN):
    rows = left[0].shape[0]
    both = dot32(jnp.concatenate(left, axis=0), right[0], dims)
    return both[:rows] + both[rows:] + dot32(left[0], right[1], dims)


def tmul(left, right, masks):
    full = (
        dot32(left[0], right[0], TN) + dot32(left[1], right[0], TN) + dot32(left[0], right[1], TN)
    )
    return sum(full[h * CHUNK : (h + 1) * CHUNK] * masks[h][:1].astype(jnp.float32) for h in range(GROUP_HEADS))


def spread(pair, masks):
    return tuple(
        jnp.concatenate([part * masks[h] for h in range(GROUP_HEADS)], axis=0) for part in pair
    )


def stack(first, second):
    return tuple(jnp.concatenate([x, y], axis=0) for x, y in zip(first, second))


def head_masks():
    lane = lax.broadcasted_iota(jnp.int32, (CHUNK, LANES), 1) // CHUNK
    return [(lane == h).astype(jnp.float32).astype(jnp.bfloat16) for h in range(GROUP_HEADS)]


def places():
    row = lax.broadcasted_iota(jnp.int32, (CHUNK, LANES), 0)
    col = lax.broadcasted_iota(jnp.int32, (CHUNK, LANES), 1) % CHUNK
    return row, col


def running_sum(x, upper=False):
    row = lax.broadcasted_iota(jnp.int32, (CHUNK, CHUNK), 0)
    col = lax.broadcasted_iota(jnp.int32, (CHUNK, CHUNK), 1)
    ones = (row <= col if upper else col <= row).astype(jnp.float32).astype(jnp.bfloat16)
    high, rest = halves(x)
    low = (x - high.astype(jnp.float32) - rest.astype(jnp.float32)).astype(jnp.bfloat16)
    return dot32(ones, high, NN) + dot32(ones, rest, NN) + dot32(ones, low, NN)


def scaled_forms(q, w, k, a, b):
    total = running_sum(w)
    before = total - w
    middle = total[CHUNK // 2 - 1 : CHUNK // 2]
    end = total[CHUNK - 1 :]
    ea = jnp.exp(before - middle)
    eq = jnp.exp(total - middle)
    eb = jnp.exp(middle - total)
    ee = jnp.exp(end - total)
    return (a * ea, q * eq, b * eb, k * eb, b * ee, k * ee), (ea, eq, eb, ee), (jnp.exp(middle), jnp.exp(end))


def each(fn, *columns):
    return [fn(*row) for row in zip(*columns)]


def block_ones():
    row = lax.broadcasted_iota(jnp.int32, (LANES, LANES), 0) // CHUNK
    col = lax.broadcasted_iota(jnp.int32, (LANES, LANES), 1) // CHUNK
    return (row == col).astype(jnp.float32).astype(jnp.bfloat16)


def head_sum(x, ones):
    rows = x.shape[0]
    both = dot32(jnp.concatenate(halves(x), axis=0), ones, NN)
    return both[:rows] + both[rows:]


def prepared(keys, decay_low, rate_low, live, vec, ones):
    sig = jax.nn.sigmoid(vec[0] + decay_low)
    log_decay = (-0.6065306597126334) * sig * live
    rates = jax.nn.sigmoid(vec[1] + rate_low)
    scaled = keys * vec[2]
    inverse = lax.rsqrt(head_sum(scaled * scaled, ones) + 1e-06)
    unit_keys = scaled * inverse
    factor = (1.0 + (rates - 1.0) * vec[3]) * live
    return log_decay, keys * factor, -unit_keys, unit_keys * rates * live, sig, rates, inverse, factor


def read_out(o, q, k, v, vec, ones):
    centred = o - head_sum(o, ones) * (1.0 / CHUNK)
    scale = lax.rsqrt(head_sum(centred * centred, ones) * (1.0 / CHUNK) + 0.00064)
    normed = centred * scale
    weight = head_sum(q * k * vec[4], ones)
    return normed, scale, weight, normed * vec[5] + vec[6] + weight * v


def unit_slices():
    return [
        (slice(c * CHUNK, (c + 1) * CHUNK), slice(g * LANES, (g + 1) * LANES))
        for c in range(STEP_CHUNKS)
        for g in range(2)
    ]


def unit_live(length, step):
    row = lax.broadcasted_iota(jnp.int32, (CHUNK, LANES), 0)
    start = step * (STEP_CHUNKS * CHUNK)
    live = [(row + (start + c * CHUNK) < length).astype(jnp.float32) for c in range(STEP_CHUNKS)]
    return [live[c] for c in range(STEP_CHUNKS) for g in range(2)]


def unit_vectors(vec_ref):
    vec = [[vec_ref[i : i + 1, g * LANES : (g + 1) * LANES] for i in range(7)] for g in range(2)]
    return [vec[g] for c in range(STEP_CHUNKS) for g in range(2)]


def forward_kernel(
    len_ref, vec_ref, q_ref, keys_ref, v_ref, dl_ref, rl_ref, gate_ref,
    out_ref, o_ref, t_ref, aqb_ref, aak_ref, aqk_ref, y_ref, z_ref, trt_ref, qe_ref,
    state_ref,
):
    @pl.when(pl.program_id(0) == 0)
    def _():
        state_ref[...] = jnp.zeros_like(state_ref)

    masks = head_masks()
    row, col = places()
    strict = (col < row).astype(jnp.float32)
    within = (col <= row).astype(jnp.float32)
    eye = (col == row).astype(jnp.float32)
    ones = block_ones()
    units = unit_slices()
    live = unit_live(len_ref[0], pl.program_id(0))
    vec = unit_vectors(vec_ref)
    load = lambda ref: [ref[u] for u in units]
    q, keys, v = load(q_ref), load(keys_ref), load(v_ref)
    ready = each(
        lambda x, y, z, m, n: prepared(x, y, z, m, n, ones), keys, load(dl_ref), load(rl_ref), live, vec
    )
    w, k, a, b = ([x[i] for x in ready] for i in range(4))
    forms = each(scaled_forms, q, w, k, a, b)
    ah, qh, bh, kh, bt, kt = ([f[0][i] for f in forms] for i in range(6))
    emid = [f[2][0] for f in forms]
    eend = [f[2][1] for f in forms]
    aq = each(lambda x, y: halves(jnp.concatenate([x, y], axis=0)), ah, qh)
    with_b = each(lambda l, r: mul(l, spread(halves(r), masks), NT), aq, bh)
    with_k = each(lambda l, r: mul(l, spread(halves(r), masks), NT), aq, kh)
    aab = [x[:CHUNK] * strict for x in with_b]
    aqb = [halves(x[CHUNK:] * within) for x in with_b]
    aak = [halves(x[:CHUNK] * strict) for x in with_k]
    aqk = [halves(x[CHUNK:] * within) for x in with_k]
    p = [halves(x * (row // 8 == col // 8)) for x in aab]
    t = [eye + x * (row // 8 == col // 8) for x in aab]
    p2 = each(lambda x: halves(mul(x, spread(x, masks))), p)
    both = each(lambda x, y: mul(stack(x, halves(y)), spread(x, masks)), p2, t)
    p4 = [halves(x[:CHUNK]) for x in both]
    t = each(lambda x, y: x + y[CHUNK:], t, both)
    t = each(lambda x, y: x + mul(halves(x), spread(y, masks)), t, p4)
    for size in (8, 16, 32):
        corner = ((row // size) % 2 == 1) & (col // size == row // size - 1)
        ts = [halves(x) for x in t]
        n = [halves(x * corner) for x in aab]
        tn = each(lambda x, y: halves(mul(x, spread(y, masks))), ts, n)
        t = each(lambda x, y, z: x + mul(y, spread(z, masks)), t, tn, ts)
    ts = [halves(x) for x in t]
    vs = [halves(x) for x in v]
    vm = [spread(x, masks) for x in vs]
    wide = each(lambda x, y, e: mul(x, spread(halves(y * e), masks)), ts, ah, emid)
    r0 = each(mul, aak, vm)
    y0 = each(lambda x, y: mul(x, spread(halves(y), masks)), ts, r0)
    wides = [halves(x) for x in wide]
    qe = each(lambda x, e, y, z: x * e + mul(y, spread(z, masks)), qh, emid, aqb, wides)
    y0s = [halves(x) for x in y0]
    part = each(lambda x, y, z, u: mul(x, spread(y, masks)) + mul(z, u), aqb, y0s, aqk, vm)
    bts = [halves(x) for x in bt]
    diag = [eye * e for e in eend]
    tr = each(lambda x, y, d: tmul(x, y, masks) + d, bts, wides, diag)
    trt = each(lambda x, y, d: tmul(y, x, masks) + d, bts, wides, diag)
    inject = each(lambda x, y, z, u: tmul(stack(x, halves(y)), stack(z, u), masks), bts, kt, y0s, vs)
    wq = each(lambda x, y: stack(x, halves(y)), wides, qe)
    z = []
    out = []
    for c in range(STEP_CHUNKS):
        for g in range(2):
            i = c * 2 + g
            now = state_ref[g]
            nows = spread(halves(now), masks)
            state_ref[g] = mul(halves(tr[i]), nows) + inject[i]
            z.append(now)
            out.append(mul(wq[i], nows))
    o = each(lambda x, y: x[CHUNK:] + y, out, part)
    mixed = each(lambda x, y, z, m, n: read_out(x, y, z, m, n, ones)[3], o, q, k, v, vec)
    for i, u in enumerate(units):
        out_ref[u] = (mixed[i] * gate_ref[u]).astype(jnp.bfloat16)
        o_ref[u] = o[i]
        y_ref[u] = out[i][:CHUNK] + y0[i]
        t_ref[u] = t[i]
        aqb_ref[u] = with_b[i][CHUNK:] * within
        aak_ref[u] = with_k[i][:CHUNK] * strict
        aqk_ref[u] = with_k[i][CHUNK:] * within
        z_ref[u] = z[i]
        trt_ref[u] = trt[i]
        qe_ref[u] = qe[i]


def backward_kernel(
    len_ref, vec_ref, q_ref, keys_ref, v_ref, dl_ref, rl_ref, gate_ref, g_ref, o_ref,
    t_ref, aqb_ref, aak_ref, aqk_ref, y_ref, z_ref, trt_ref, qe_ref,
    dq_ref, dkeys_ref, dv_ref, ddl_ref, drl_ref, dgate_ref, dvec_ref,
    state_ref,
):
    step = pl.num_programs(0) - 1 - pl.program_id(0)

    @pl.when(pl.program_id(0) == 0)
    def _():
        state_ref[...] = jnp.zeros_like(state_ref)
        dvec_ref[...] = jnp.zeros_like(dvec_ref)

    masks = head_masks()
    row, col = places()
    strict = (col < row).astype(jnp.float32)
    within = (col <= row).astype(jnp.float32)
    ones = block_ones()
    units = unit_slices()
    live = unit_live(len_ref[0], step)
    vec = unit_vectors(vec_ref)
    load = lambda ref: [ref[u] for u in units]
    q, keys, v, g = load(q_ref), load(keys_ref), load(v_ref), load(g_ref)
    ready = each(
        lambda x, y, z, m, n: prepared(x, y, z, m, n, ones), keys, load(dl_ref), load(rl_ref), live, vec
    )
    w, k, a, b, sig, rates, inverse, factor = ([x[i] for x in ready] for i in range(8))
    seen = each(lambda x, y, z, m, n: read_out(x, y, z, m, n, ones), load(o_ref), q, k, v, vec)
    normed, scale, weight, mixed = ([x[i] for x in seen] for i in range(4))
    gate = load(gate_ref)
    dgate = each(lambda x, y: x * y, g, mixed)
    dmix = each(lambda x, y: x * y, g, gate)
    dn = each(lambda x, n: x * n[5], dmix, vec)
    do = each(
        lambda x, n, r: r
        * (x - head_sum(x, ones) * (1.0 / CHUNK) - n * (head_sum(x * n, ones) * (1.0 / CHUNK))),
        dn, normed, scale,
    )
    dweight = each(lambda x, y: head_sum(x * y, ones), dmix, v)
    do = [halves(x) for x in do]
    qe, trt, t, aqb, aak, aqk, ys = (
        [halves(x) for x in load(ref)]
        for ref in (qe_ref, trt_ref, t_ref, aqb_ref, aak_ref, aqk_ref, y_ref)
    )
    z = load(z_ref)
    vs = [halves(x) for x in v]
    h = each(lambda x, y: tmul(x, y, masks), qe, do)
    dz = [None] * len(units)
    for c in reversed(range(STEP_CHUNKS)):
        for g in range(2):
            i = c * 2 + g
            now = state_ref[g]
            dz[i] = now
            state_ref[g] = mul(trt[i], spread(halves(now), masks)) + h[i]
    dzs = [spread(halves(x), masks) for x in dz]
    zs = [spread(halves(x), masks) for x in z]
    forms = each(scaled_forms, q, w, k, a, b)
    ah, qh, bh, kh, bt, kt = ([f[0][i] for f in forms] for i in range(6))
    ea, eq, eb, ee = ([f[1][i] for f in forms] for i in range(4))
    emid = [f[2][0] for f in forms]
    eend = [f[2][1] for f in forms]
    from_end = each(lambda x, y, s: mul(halves(jnp.concatenate([x, y], axis=0)), s), bt, kt, dzs)
    dy = each(lambda x, y, s: halves(tmul(x, y, masks) + s[:CHUNK]), aqb, do, from_end)
    dr = each(lambda x, y: halves(tmul(x, y, masks)), t, dy)
    ro = each(stack, dr, do)
    dv = each(lambda x, y, s, f: tmul(stack(x, y), s, masks) + f[CHUNK:], aak, aqk, ro, from_end)
    mask2 = jnp.concatenate([strict, within], axis=0)
    dab = each(lambda s, y: halves(mul(s, spread(y, masks), NT) * mask2), ro, ys)
    dak = each(lambda s, y: halves(mul(s, spread(y, masks), NT) * mask2), ro, vs)
    dst = each(lambda s, y: mul(s, y, NT), ro, zs)
    daq = each(
        lambda s, e, x, bb, y, kk: s * e + mul(x, spread(halves(bb), masks)) + mul(y, spread(halves(kk), masks)),
        dst, emid, dab, bh, dak, kh,
    )
    aq = each(lambda x, y: halves(jnp.concatenate([x, y], axis=0)), ah, qh)
    dbh = each(lambda x, y: tmul(x, y, masks), dab, aq)
    dkh = each(lambda x, y: tmul(x, y, masks), dak, aq)
    dend = each(lambda y, x, s: mul(stack(y, x), s, NT), ys, vs, dzs)
    row_of_ones = jnp.ones((8, LANES), jnp.bfloat16)
    sums = lambda x: jnp.sum(x, axis=0, keepdims=True)
    for i, u in enumerate(units):
        da = daq[i][:CHUNK] * ea[i]
        dq = daq[i][CHUNK:] * eq[i]
        dbt = dend[i][:CHUNK] * ee[i]
        dkt = dend[i][CHUNK:] * ee[i]
        db = dbh[i] * eb[i] + dbt
        dk = dkh[i] * eb[i] + dkt
        pa = da * a[i]
        diff = dq * q[i] - db * b[i] - dk * k[i] + pa
        zz = spread(halves(z[i] * dz[i]), masks)
        carry = (dot32(row_of_ones, zz[0], NT) + dot32(row_of_ones, zz[1], NT))[:1] * eend[i]
        carry = carry + sums(dbt * b[i] + dkt * k[i])
        dw = running_sum(diff, upper=True) - pa + carry
        from_bonus = dweight[i] * vec[i][4]
        dk = dk + from_bonus * q[i]
        dq_ref[u] = (dq + from_bonus * k[i]).astype(jnp.bfloat16)
        dv_ref[u] = (dv[i] + weight[i] * dmix[i]).astype(jnp.bfloat16)
        dgate_ref[u] = dgate[i].astype(jnp.bfloat16)
        unit_keys = -a[i]
        db = db * live[i]
        du = db * rates[i] - da
        dscaled = inverse[i] * (du - unit_keys * head_sum(du * unit_keys, ones))
        dkl = dk * keys[i] * live[i]
        drl = (db * unit_keys + dkl * vec[i][3]) * rates[i] * (1.0 - rates[i])
        ddl = dw * w[i] * (1.0 - sig[i])
        dkeys_ref[u] = (dk * factor[i] + dscaled * vec[i][2]).astype(jnp.bfloat16)
        ddl_ref[u] = ddl.astype(jnp.bfloat16)
        drl_ref[u] = drl.astype(jnp.bfloat16)
        parts = (
            ddl, drl, dscaled * keys[i], dkl * (rates[i] - 1.0),
            dweight[i] * q[i] * k[i], dmix[i] * normed[i], dmix[i],
        )
        lanes = u[1]
        for j, x in enumerate(parts):
            dvec_ref[j : j + 1, lanes] += sums(x)


def wkv_calls(tokens, width):
    rows = CHUNK * STEP_CHUNKS
    steps = tokens // rows
    params = dict(
        grid=(steps,),
        scratch_shapes=[pltpu.VMEM((2, CHUNK, LANES), jnp.float32)],
        compiler_params=pltpu.CompilerParams(vmem_limit_bytes=56 << 20),
        cost_estimate=pl.CostEstimate(
            flops=25_000_000_000, bytes_accessed=16 << 20, transcendentals=0
        ),
    )
    shape = lambda dtype: jax.ShapeDtypeStruct((tokens, width), dtype)
    return rows, steps, params, shape


def wkv_forward(length, vec, *arrays):
    tokens, width = arrays[0].shape
    rows, steps, params, shape = wkv_calls(tokens, width)
    spec = pl.BlockSpec((rows, width), lambda i: (i, 0))
    return pl.pallas_call(
        forward_kernel,
        in_specs=[
            pl.BlockSpec(memory_space=pltpu.SMEM), pl.BlockSpec((8, width), lambda i: (0, 0)),
        ]
        + [spec] * 6,
        out_specs=[spec] * 10,
        out_shape=[shape(jnp.bfloat16)] + [shape(jnp.float32)] * 9,
        name="wkv_forward",
        **params,
    )(length, vec, *arrays)


def wkv_backward(length, vec, *arrays):
    tokens, width = arrays[0].shape
    rows, steps, params, shape = wkv_calls(tokens, width)
    spec = pl.BlockSpec((rows, width), lambda i: (steps - 1 - i, 0))
    whole = pl.BlockSpec((8, width), lambda i: (0, 0))
    return pl.pallas_call(
        backward_kernel,
        in_specs=[pl.BlockSpec(memory_space=pltpu.SMEM), whole] + [spec] * 16,
        out_specs=[spec] * 6 + [whole],
        out_shape=[shape(jnp.bfloat16)] * 6 + [jax.ShapeDtypeStruct((8, width), jnp.float32)],
        name="wkv_backward",
        **params,
    )(length, vec, *arrays)


def swap(block, mask):
    size = lax.axis_size("dp")
    return lax.ppermute(block, "dp", [(i, i ^ mask) for i in range(size)])


def bit_of(mask):
    return (lax.axis_index("dp") // mask) % 2


def in_order(mask, own, other, axis):
    lower = bit_of(mask) == 0
    return jnp.where(
        lower, jnp.concatenate([own, other], axis=axis), jnp.concatenate([other, own], axis=axis)
    )


def chip_masks():
    size = lax.axis_size("dp")
    masks = []
    while 2 << len(masks) < size:
        masks.append(2 << len(masks))
    return masks


def steps_of(kind):
    masks = chip_masks()
    near, far = [[mask] for mask in masks[:2]], masks[2:][::-1]
    first = [[far[0], far[1], far[0] | far[1]]] if len(far) == 2 else [[mask] for mask in far]
    return [first + near[::-1], first + near, near + first][kind]


def meet(movers, *arrays):
    held = lax.optimization_barrier(tuple(tuple(m.arrived) for m in movers) + arrays)
    for mover, arrived in zip(movers, held):
        mover.arrived = list(arrived)
    return held[len(movers) :]


class Gather:
    def __init__(self, block, kind, places=(0,)):
        self.steps = steps_of(kind)
        self.held = block[None]
        self.places = [0]
        self.arrived = []
        self.masks = []

    def merge(self):
        if self.arrived:
            self.held = jnp.concatenate([self.held] + self.arrived, axis=0)
            self.places = self.places + [p ^ (m // 2) for m in self.masks for p in self.places]
            self.arrived = []

    def step(self):
        if self.steps:
            self.merge()
            self.masks = self.steps.pop(0)
            self.arrived = [swap(self.held, mask) for mask in self.masks]
        return self

    def run(self):
        while self.steps:
            self.step()
        return self

    def split(self, kinds):
        width = self.held.shape[-1] // len(kinds)
        out = []
        for i, kind in enumerate(kinds):
            part = Gather.__new__(Gather)
            cut = slice(i * width, (i + 1) * width)
            part.steps = steps_of(kind)[len(steps_of(kind)) - len(self.steps) :]
            part.held = self.held[..., cut]
            part.arrived = [x[..., cut] for x in self.arrived]
            part.places, part.masks = self.places, self.masks
            out.append(part)
        return out


def place_kernel(places, cuts, width, *refs):
    sources, outs = refs[: len(places)], refs[len(places) :]
    chip = lax.axis_index("dp") // 2
    for source, (lane, list_of) in zip(sources, places):
        for j, place in enumerate(list_of):
            for out, (first, rows) in zip(outs, cuts):
                start = pl.multiple_of((chip ^ place) * rows, rows)
                out[pl.ds(start, rows), lane : lane + width] = source[j, first : first + rows]


def assemble(gathers, cuts=None):
    gathers = [g.run() for g in gathers]
    rows, width = gathers[0].held.shape[1:]
    cuts = cuts or ((0, rows),)
    sources, places = [], []
    for i, g in enumerate(gathers):
        sources += [g.held] + g.arrived
        shifts = [0] + [mask // 2 for mask in g.masks]
        places += [(i * width, [p ^ shift for p in g.places]) for shift in shifts]
    count = lax.axis_size("dp") // 2
    if any(n % 16 for _, n in cuts):
        return assemble_plain(sources, places, cuts, width, count)
    total = width * len(gathers)
    space = pl.BlockSpec(memory_space=pltpu.VMEM)
    return pl.pallas_call(
        partial(place_kernel, places, cuts, width),
        in_specs=[space] * len(sources),
        out_specs=[space] * len(cuts),
        out_shape=[jax.ShapeDtypeStruct((count * n, total), sources[0].dtype) for _, n in cuts],
        compiler_params=pltpu.CompilerParams(vmem_limit_bytes=32 << 20),
        cost_estimate=pl.CostEstimate(flops=0, bytes_accessed=8 << 20, transcendentals=0),
        name="assemble",
    )(*sources)


def assemble_plain(sources, places, cuts, width, count):
    chip = lax.axis_index("dp") // 2
    columns = []
    for lane in sorted({lane for lane, _ in places}):
        blocks = jnp.concatenate([x for x, (at, _) in zip(sources, places) if at == lane])
        where = [p for at, list_of in places if at == lane for p in list_of]
        blocks = jnp.stack([blocks[where.index(i)] for i in range(count)])
        columns.append(jnp.take(blocks, chip ^ lax.iota(jnp.int32, count), axis=0))
    blocks = jnp.concatenate(columns, axis=-1)
    return [
        blocks[:, first : first + n].reshape(count * n, blocks.shape[-1]) for first, n in cuts
    ]


class Scatter:
    def __init__(self, parts, kind):
        self.steps = steps_of(kind)[::-1]
        self.axes = chip_masks()[::-1]
        shape = parts.shape[1:]
        self.sources = [parts.reshape((2,) * len(self.axes) + shape)]
        self.arrived = []

    def pick(self, mask, gone):
        out = []
        for x in self.sources:
            for place in reversed(range(len(self.axes))):
                axis = self.axes[place]
                if axis in gone:
                    which = bit_of(axis) if not mask & axis else 1 - bit_of(axis)
                    x = lax.dynamic_index_in_dim(x, which, place, keepdims=False)
            out.append(x)
        return out

    def merge(self):
        self.sources = self.sources + self.arrived
        self.arrived = []

    def step(self):
        if self.steps:
            self.merge()
            masks = self.steps.pop(0)
            gone = [axis for axis in self.axes if any(mask & axis for mask in masks)]
            sends = [
                sum(x.astype(jnp.float32) for x in self.pick(mask, gone)).astype(jnp.bfloat16)
                for mask in masks
            ]
            self.sources = self.pick(0, gone)
            self.axes = [axis for axis in self.axes if axis not in gone]
            self.arrived = [swap(x, mask) for x, mask in zip(sends, masks)]
        return self

    def run(self):
        while self.steps:
            self.step()
        return self

    def total(self):
        self.merge()
        return sum(x.astype(jnp.float32) for x in self.sources)

    @staticmethod
    def join(parts):
        out = Scatter.__new__(Scatter)
        out.steps, out.axes, out.arrived = parts[0].steps, parts[0].axes, []
        out.sources = [jnp.concatenate([part.total() for part in parts], axis=-1)]
        return out


def norm_rows(features, gain_row, offset_row):
    average = jnp.mean(features, axis=-1, keepdims=True)
    centred = features - average
    variance = jnp.mean(centred * centred, axis=-1, keepdims=True)
    return centred * lax.rsqrt(variance + 1e-05) * gain_row + offset_row


def product(operand, weight_matrix):
    return jnp.dot(operand, weight_matrix, preferred_element_type=jnp.float32)


def input_gradient_rows(upstream_gradient, weight_matrix):
    return lax.dot_general(
        upstream_gradient,
        weight_matrix,
        (((1,), (1,)), ((), ())),
        preferred_element_type=jnp.float32,
    )


def weight_gradient(operand, upstream_gradient):
    return lax.dot_general(
        operand, upstream_gradient, (((0,), (0,)), ((), ())), preferred_element_type=jnp.float32
    )


def earlier(rows):
    return jnp.concatenate([jnp.zeros_like(rows[:1]), rows[:-1]], axis=0)


def front_mix(tokens, vectors):
    normed = norm_rows(tokens, vectors[12], vectors[13])
    change = earlier(normed) - normed
    return tuple((normed + change * vectors[which] for which in range(6)))


def lowrank_middle(decay_logits, rate_logits, gate_logits):
    return (jnp.tanh(decay_logits), rate_logits, jax.nn.sigmoid(gate_logits))


def ffn_mix(residual, vectors):
    second = norm_rows(residual, vectors[14], vectors[15])
    return second + (earlier(second) - second) * vectors[6]


def squared(pre_act):
    return jnp.square(jax.nn.relu(pre_act))


def narrow(x):
    return x.astype(jnp.bfloat16)


def local(
    inputs,
    lengths,
    attention_projections,
    channel_key_weight,
    channel_value_weight,
    lowrank_down_weight,
    lowrank_up_weight,
    per_feature_parameters,
    cotangent,
):
    devices = lax.axis_size("dp")
    chips = devices // 2
    device = lax.axis_index("dp")
    chip, core = device // 2, device % 2
    row_count = inputs.shape[0]
    slots = 2 * row_count
    share = EMBED // devices
    pair_share = 2 * share
    units = channel_value_weight.shape[0]
    half_units = chips * units

    def own_cut(x, which):
        return lax.dynamic_slice_in_dim(x, which * OWN, OWN, x.ndim - 1)

    def own_rows(x, which):
        return lax.dynamic_slice_in_dim(x, which * row_count, row_count, 0)

    cuts = ((0, 64), (64, 128), (128, 256))

    pair_rows = in_order(
        1,
        own_cut(attention_projections, core),
        swap(own_cut(attention_projections, 1 - core), 1),
        1,
    )
    lora = jnp.concatenate([lowrank_down_weight, lowrank_up_weight.T], axis=1)
    vector_rows = jnp.pad(per_feature_parameters.T, ((0, 0), (0, 128 - 18)))
    vector_rows = vector_rows.reshape(share // 4, OWN)
    first_rows = 3 * pair_share
    misc_rows = share + share // 4 + (share // 4) % 16
    block = jnp.concatenate(
        [
            pair_rows[:3].reshape(first_rows, OWN),
            lora,
            jnp.pad(vector_rows, ((0, (share // 4) % 16), (0, 0))),
        ],
        axis=0,
    )
    first = Gather(block, 0).step()
    w_o_part = Gather(pair_rows[3], 2).step()
    raw, cotangent_in, key_in_rows = meet(
        [first, w_o_part], inputs, cotangent, channel_key_weight
    )
    first = first.split((0, 1))
    for part in first:
        part.step()
    w_o_part.step()
    key_cut = key_in_rows.reshape(share, chips, 2, units)

    def key_columns(which):
        return lax.dynamic_index_in_dim(key_cut, which, 2, keepdims=False).reshape(share, half_units)

    key_part = Gather(
        in_order(1, key_columns(core), swap(key_columns(1 - core), 1), 0), 0
    ).step()
    tokens = in_order(1, raw, swap(raw, 1), 0).astype(jnp.float32)
    cot = in_order(1, cotangent_in, swap(cotangent_in, 1), 0).astype(jnp.float32)
    tokens, cot = meet(first, tokens, cot)
    for part in first:
        part.step()
    value_block, tokens = meet(first + [key_part, w_o_part], channel_value_weight, tokens)
    w_r, w_k, w_v, misc = assemble(
        first, [(i * pair_share, pair_share) for i in range(3)] + [(first_rows, misc_rows)]
    )
    key_parts = key_part.split((0, 1))
    for part in key_parts:
        part.step()
    value_part = Gather(value_block, 0).step()
    misc = misc.reshape(chips, 1, misc_rows, OWN)
    misc = in_order(1, misc, swap(misc, 1), 1)
    lora = misc[:, :, :share].reshape(EMBED, OWN)
    down, up_t = lora[:, :256], lax.dynamic_slice_in_dim(lora[:, 256:], core * OWN, OWN, 0)
    vectors = misc[:, :, share : share + share // 4].reshape(EMBED, 128)[:, :18].T
    vectors = vectors.astype(jnp.float32)
    own_vectors = own_cut(vectors, core)
    used = jnp.concatenate([own_vectors[7:12], own_vectors[16:18], own_vectors[:1]], axis=0)
    length = lax.dynamic_index_in_dim(lengths, chip, 0)
    live = (lax.iota(jnp.int32, slots) < length).astype(jnp.float32)[:, None]

    mixes, front_pull = jax.vjp(front_mix, tokens, vectors)
    mixes = [narrow(x) for x in mixes]
    queries = product(mixes[0], w_r)
    keys = product(mixes[2], w_k)
    values = product(mixes[3], w_v)
    logits = [product(mixes[m], down[:, lo:hi]) for m, (lo, hi) in zip((1, 4, 5), cuts)]
    hid, hid_pull = jax.vjp(lowrank_middle, *logits)
    hid = [narrow(x) for x in hid]
    lows = [input_gradient_rows(x, up_t[:, lo:hi]) for x, (lo, hi) in zip(hid, cuts)]
    terms = meet(key_parts, queries, keys, values, *lows)
    for part in key_parts:
        part.step()
    w_o_part.step()
    gated, *saved = wkv_forward(length, used, *terms)
    (gated,) = meet(key_parts + [value_part, w_o_part], gated)
    value_parts = value_part.split((0, 1))
    for part in value_parts:
        part.step()
    gated_all = in_order(1, gated, swap(gated, 1), 1)
    (w_o_own,) = assemble([w_o_part])
    w_o = in_order(1, w_o_own, swap(w_o_own, 1), 1)
    (key_weight,) = assemble(key_parts)
    residual = tokens + product(gated_all, w_o)
    ffn_in, ffn_pull = jax.vjp(ffn_mix, residual, vectors)
    ffn_in = narrow(ffn_in)
    pre_act = product(ffn_in, key_weight)
    hidden = narrow(squared(pre_act))
    pre_act, hidden = meet(value_parts, pre_act, hidden)
    for part in value_parts:
        part.step()
    out_grad = cot * live
    out_narrow = narrow(out_grad)
    value_scatter = [
        Scatter(
            narrow(weight_gradient(hidden, out_narrow[:, i * OWN : (i + 1) * OWN])).reshape(
                chips, units, OWN
            ),
            i,
        ).step()
        for i in range(2)
    ]
    hidden, pre_act, out_narrow = meet(value_parts, hidden, pre_act, out_narrow)
    (value_weight,) = assemble(value_parts)

    pre_grad = 2.0 * jax.nn.relu(pre_act) * input_gradient_rows(out_narrow, value_weight)
    pre_narrow = narrow(pre_grad)
    ffn_in_grad = input_gradient_rows(pre_narrow, key_weight)
    ffn_in_grad = ffn_in_grad + swap(ffn_in_grad, 1)
    ffn_part = product(hidden, value_weight)
    grad_key = narrow(weight_gradient(ffn_in, pre_narrow)).reshape(chips, pair_share, half_units)
    ffn_in_grad, grad_key, ffn_part = meet(value_scatter, ffn_in_grad, grad_key, ffn_part)
    ffn_out = own_rows(ffn_part, core) + swap(own_rows(ffn_part, 1 - core), 1)
    output = narrow((own_rows(residual, core) + ffn_out) * own_rows(live, core))
    for part in value_scatter:
        part.step()
    half = half_units // 2
    key_scatter = [
        Scatter(grad_key[:, :, i * half : (i + 1) * half], i).step() for i in range(2)
    ]
    residual_part, ffn_vector_grad = ffn_pull(ffn_in_grad)
    residual_grad = out_grad + residual_part
    attended_grad = narrow(residual_grad)
    gated_grad = input_gradient_rows(
        attended_grad, lax.dynamic_slice_in_dim(w_o, core * OWN, OWN, 0)
    )
    grad_o = narrow(weight_gradient(gated_all, own_cut(attended_grad, core)))
    gated_grad, grad_o = meet(value_scatter, gated_grad, grad_o)
    value_scatter = Scatter.join(value_scatter).step()
    query_narrow, key_narrow, value_narrow, *low_narrow, own_vector_grad = meet(
        key_scatter, *wkv_backward(length, used, *terms, gated_grad, *saved)
    )
    for part in key_scatter:
        part.step()
    grad_r, grad_k, grad_v = (
        narrow(weight_gradient(mixes[m], g))
        for m, g in zip((0, 2, 3), (query_narrow, key_narrow, value_narrow))
    )
    att_scatter = [
        Scatter(jnp.concatenate(x, axis=1).reshape(chips, pair_share, 2 * OWN), i).step()
        for i, x in enumerate(((grad_r, grad_o), (grad_k, grad_v)))
    ]
    grad_up = jnp.concatenate([weight_gradient(g, h) for g, h in zip(low_narrow, hid)], axis=1)
    logit_grads = hid_pull(
        tuple(product(g, up_t[:, lo:hi]) for g, (lo, hi) in zip(low_narrow, cuts))
    )
    logit_narrow = [narrow(g) for g in logit_grads]
    logit_narrow = meet(key_scatter, *logit_narrow)
    key_scatter = Scatter.join(key_scatter).step()
    grad_down = jnp.concatenate(
        [weight_gradient(mixes[m], g) for m, g in zip((1, 4, 5), logit_narrow)], axis=1
    )
    mix_grads = (
        input_gradient_rows(query_narrow, w_r),
        input_gradient_rows(logit_narrow[0], down[:, :64]),
        input_gradient_rows(key_narrow, w_k),
        input_gradient_rows(value_narrow, w_v),
        input_gradient_rows(logit_narrow[1], down[:, 64:128]),
        input_gradient_rows(logit_narrow[2], down[:, 128:]),
    )
    token_part, front_vector_grad = front_pull(mix_grads)
    own_full = jnp.zeros((18, OWN), jnp.float32)
    own_full = own_full.at[7:12].set(own_vector_grad[:5]).at[16:18].set(own_vector_grad[5:7])
    vector_grad = front_vector_grad + 0.5 * ffn_vector_grad
    vector_grad = vector_grad + lax.dynamic_update_slice(
        jnp.zeros_like(vector_grad), own_full, (0, core * OWN)
    )
    up_full = lax.dynamic_update_slice(
        jnp.zeros((EMBED, 256), jnp.float32), grad_up, (core * OWN, 0)
    )
    misc_grad = jnp.concatenate(
        [grad_down, up_full, jnp.pad(vector_grad.T, ((0, 0), (0, 128 - 18)))], axis=1
    ).reshape(chips, 2, share, 640)
    misc_mine = lax.dynamic_index_in_dim(misc_grad, core, 1, keepdims=False)
    misc_other = lax.dynamic_index_in_dim(misc_grad, 1 - core, 1, keepdims=False)
    misc_sum = misc_mine + swap(misc_other, 1)
    misc_sum, token_part = meet(att_scatter, misc_sum, token_part)
    for part in att_scatter:
        part.step()
    misc_scatter = Scatter(misc_sum, 0).step()
    input_gradient = (
        own_rows(residual_grad, core)
        + own_rows(token_part, core)
        + swap(own_rows(token_part, 1 - core), 1)
    )
    meet(att_scatter + [misc_scatter, key_scatter, value_scatter])
    att_scatter = Scatter.join(att_scatter).step()
    misc_scatter.step()
    meet([misc_scatter])
    misc_scatter.run()
    value_sum = value_scatter.run().total()
    key_sum = key_scatter.run().total()
    att_sum = att_scatter.run().total()
    misc_sum = misc_scatter.total()
    pair_sum = jnp.concatenate([att_sum, key_sum], axis=1).reshape(2, share, -1)
    mine = lax.dynamic_index_in_dim(pair_sum, core, 0, keepdims=False)
    theirs = swap(lax.dynamic_index_in_dim(pair_sum, 1 - core, 0, keepdims=False), 1)
    shard_mixer = jnp.stack(
        [
            in_order(1, mine[:, i * OWN : (i + 1) * OWN], theirs[:, i * OWN : (i + 1) * OWN], 1)
            for i in (0, 2, 3, 1)
        ]
    )
    shard_key = in_order(
        1,
        mine[:, 4 * OWN :].reshape(share, chips, 1, units),
        theirs[:, 4 * OWN :].reshape(share, chips, 1, units),
        2,
    ).reshape(share, 2 * half_units)
    return (
        output,
        input_gradient,
        shard_mixer,
        shard_key,
        value_sum,
        misc_sum[:, :256],
        misc_sum[:, 256:512].T,
        misc_sum[:, 512:530].T,
    )


def solution(mesh):
    in_specs = (
        P("dp", None),
        P(),
        P(None, "dp", None),
        P("dp", None),
        P("dp", None),
        P("dp", None),
        P(None, "dp"),
        P(None, "dp"),
        P("dp", None),
    )
    out_specs = (
        P("dp", None),
        P("dp", None),
        P(None, "dp", None),
        P("dp", None),
        P("dp", None),
        P("dp", None),
        P(None, "dp"),
        P(None, "dp"),
    )
    return jax.shard_map(local, mesh=mesh, in_specs=in_specs, out_specs=out_specs, check_vma=False)
```

```python
from functools import partial

import jax
import jax.numpy as jnp
from jax import lax
from jax.experimental import pallas as pl
from jax.experimental.pallas import tpu as pltpu
from jax.sharding import PartitionSpec as P

HEADS = 16
HEAD_SIZE = 64
DECAY_RANK = 64
RATE_RANK = 64
EMBED = 1024
OWN = EMBED // 2
PRECISE = lax.Precision.HIGHEST


CHUNK = 64
LANES = 256
GROUP_HEADS = 4
STEP_CHUNKS = 2
SMALL = pl.CostEstimate(flops=1, bytes_accessed=1, transcendentals=0)

NN = (((1,), (0,)), ((), ()))
NT = (((1,), (1,)), ((), ()))
TN = (((0,), (0,)), ((), ()))


def halves(x):
    high = x.astype(jnp.bfloat16)
    return high, (x - high.astype(jnp.float32)).astype(jnp.bfloat16)


def dot32(a, b, dims):
    return lax.dot_general(a, b, dims, preferred_element_type=jnp.float32)


def mul(left, right, dims=NN):
    rows = left[0].shape[0]
    both = dot32(jnp.concatenate(left, axis=0), right[0], dims)
    return both[:rows] + both[rows:] + dot32(left[0], right[1], dims)


def tmul(left, right, masks):
    full = (
        dot32(left[0], right[0], TN) + dot32(left[1], right[0], TN) + dot32(left[0], right[1], TN)
    )
    return sum(full[h * CHUNK : (h + 1) * CHUNK] * masks[h][:1].astype(jnp.float32) for h in range(GROUP_HEADS))


def spread(pair, masks):
    return tuple(
        jnp.concatenate([part * masks[h] for h in range(GROUP_HEADS)], axis=0) for part in pair
    )


def stack(first, second):
    return tuple(jnp.concatenate([x, y], axis=0) for x, y in zip(first, second))


def head_masks():
    lane = lax.broadcasted_iota(jnp.int32, (CHUNK, LANES), 1) // CHUNK
    return [(lane == h).astype(jnp.float32).astype(jnp.bfloat16) for h in range(GROUP_HEADS)]


def places():
    row = lax.broadcasted_iota(jnp.int32, (CHUNK, LANES), 0)
    col = lax.broadcasted_iota(jnp.int32, (CHUNK, LANES), 1) % CHUNK
    return row, col


def running_sum(x, upper=False):
    row = lax.broadcasted_iota(jnp.int32, (CHUNK, CHUNK), 0)
    col = lax.broadcasted_iota(jnp.int32, (CHUNK, CHUNK), 1)
    ones = (row <= col if upper else col <= row).astype(jnp.float32).astype(jnp.bfloat16)
    high, rest = halves(x)
    low = (x - high.astype(jnp.float32) - rest.astype(jnp.float32)).astype(jnp.bfloat16)
    return dot32(ones, high, NN) + dot32(ones, rest, NN) + dot32(ones, low, NN)


def scaled_forms(q, w, k, a, b):
    total = running_sum(w)
    before = total - w
    middle = total[CHUNK // 2 - 1 : CHUNK // 2]
    end = total[CHUNK - 1 :]
    ea = jnp.exp(before - middle)
    eq = jnp.exp(total - middle)
    eb = jnp.exp(middle - total)
    ee = jnp.exp(end - total)
    return (a * ea, q * eq, b * eb, k * eb, b * ee, k * ee), (ea, eq, eb, ee), (jnp.exp(middle), jnp.exp(end))


def each(fn, *columns):
    return [fn(*row) for row in zip(*columns)]


def block_ones():
    row = lax.broadcasted_iota(jnp.int32, (LANES, LANES), 0) // CHUNK
    col = lax.broadcasted_iota(jnp.int32, (LANES, LANES), 1) // CHUNK
    return (row == col).astype(jnp.float32).astype(jnp.bfloat16)


def head_sum(x, ones):
    rows = x.shape[0]
    both = dot32(jnp.concatenate(halves(x), axis=0), ones, NN)
    return both[:rows] + both[rows:]


def prepared(keys, decay_low, rate_low, live, vec, ones):
    sig = jax.nn.sigmoid(vec[0] + decay_low)
    log_decay = (-0.6065306597126334) * sig * live
    rates = jax.nn.sigmoid(vec[1] + rate_low)
    scaled = keys * vec[2]
    inverse = lax.rsqrt(head_sum(scaled * scaled, ones) + 1e-06)
    unit_keys = scaled * inverse
    factor = (1.0 + (rates - 1.0) * vec[3]) * live
    return log_decay, keys * factor, -unit_keys, unit_keys * rates * live, sig, rates, inverse, factor


def read_out(o, q, k, v, vec, ones):
    centred = o - head_sum(o, ones) * (1.0 / CHUNK)
    scale = lax.rsqrt(head_sum(centred * centred, ones) * (1.0 / CHUNK) + 0.00064)
    normed = centred * scale
    weight = head_sum(q * k * vec[4], ones)
    return normed, scale, weight, normed * vec[5] + vec[6] + weight * v


def unit_slices():
    return [
        (slice(c * CHUNK, (c + 1) * CHUNK), slice(g * LANES, (g + 1) * LANES))
        for c in range(STEP_CHUNKS)
        for g in range(2)
    ]


def unit_live(length, step):
    row = lax.broadcasted_iota(jnp.int32, (CHUNK, LANES), 0)
    start = step * (STEP_CHUNKS * CHUNK)
    live = [(row + (start + c * CHUNK) < length).astype(jnp.float32) for c in range(STEP_CHUNKS)]
    return [live[c] for c in range(STEP_CHUNKS) for g in range(2)]


def unit_vectors(vec_ref):
    vec = [[vec_ref[i : i + 1, g * LANES : (g + 1) * LANES] for i in range(7)] for g in range(2)]
    return [vec[g] for c in range(STEP_CHUNKS) for g in range(2)]


def forward_kernel(
    len_ref, vec_ref, q_ref, keys_ref, v_ref, dl_ref, rl_ref, gate_ref,
    out_ref, o_ref, t_ref, aqb_ref, aak_ref, aqk_ref, y_ref, z_ref, trt_ref, qe_ref,
    state_ref,
):
    @pl.when(pl.program_id(0) == 0)
    def _():
        state_ref[...] = jnp.zeros_like(state_ref)

    masks = head_masks()
    row, col = places()
    strict = (col < row).astype(jnp.float32)
    within = (col <= row).astype(jnp.float32)
    eye = (col == row).astype(jnp.float32)
    ones = block_ones()
    units = unit_slices()
    live = unit_live(len_ref[0], pl.program_id(0))
    vec = unit_vectors(vec_ref)
    load = lambda ref: [ref[u] for u in units]
    q, keys, v = load(q_ref), load(keys_ref), load(v_ref)
    ready = each(
        lambda x, y, z, m, n: prepared(x, y, z, m, n, ones), keys, load(dl_ref), load(rl_ref), live, vec
    )
    w, k, a, b = ([x[i] for x in ready] for i in range(4))
    forms = each(scaled_forms, q, w, k, a, b)
    ah, qh, bh, kh, bt, kt = ([f[0][i] for f in forms] for i in range(6))
    emid = [f[2][0] for f in forms]
    eend = [f[2][1] for f in forms]
    aq = each(lambda x, y: halves(jnp.concatenate([x, y], axis=0)), ah, qh)
    with_b = each(lambda l, r: mul(l, spread(halves(r), masks), NT), aq, bh)
    with_k = each(lambda l, r: mul(l, spread(halves(r), masks), NT), aq, kh)
    aab = [x[:CHUNK] * strict for x in with_b]
    aqb = [halves(x[CHUNK:] * within) for x in with_b]
    aak = [halves(x[:CHUNK] * strict) for x in with_k]
    aqk = [halves(x[CHUNK:] * within) for x in with_k]
    p = [halves(x * (row // 8 == col // 8)) for x in aab]
    t = [eye + x * (row // 8 == col // 8) for x in aab]
    p2 = each(lambda x: halves(mul(x, spread(x, masks))), p)
    both = each(lambda x, y: mul(stack(x, halves(y)), spread(x, masks)), p2, t)
    p4 = [halves(x[:CHUNK]) for x in both]
    t = each(lambda x, y: x + y[CHUNK:], t, both)
    t = each(lambda x, y: x + mul(halves(x), spread(y, masks)), t, p4)
    for size in (8, 16, 32):
        corner = ((row // size) % 2 == 1) & (col // size == row // size - 1)
        ts = [halves(x) for x in t]
        n = [halves(x * corner) for x in aab]
        tn = each(lambda x, y: halves(mul(x, spread(y, masks))), ts, n)
        t = each(lambda x, y, z: x + mul(y, spread(z, masks)), t, tn, ts)
    ts = [halves(x) for x in t]
    vs = [halves(x) for x in v]
    vm = [spread(x, masks) for x in vs]
    wide = each(lambda x, y, e: mul(x, spread(halves(y * e), masks)), ts, ah, emid)
    r0 = each(mul, aak, vm)
    y0 = each(lambda x, y: mul(x, spread(halves(y), masks)), ts, r0)
    wides = [halves(x) for x in wide]
    qe = each(lambda x, e, y, z: x * e + mul(y, spread(z, masks)), qh, emid, aqb, wides)
    y0s = [halves(x) for x in y0]
    part = each(lambda x, y, z, u: mul(x, spread(y, masks)) + mul(z, u), aqb, y0s, aqk, vm)
    bts = [halves(x) for x in bt]
    diag = [eye * e for e in eend]
    tr = each(lambda x, y, d: tmul(x, y, masks) + d, bts, wides, diag)
    trt = each(lambda x, y, d: tmul(y, x, masks) + d, bts, wides, diag)
    inject = each(lambda x, y, z, u: tmul(stack(x, halves(y)), stack(z, u), masks), bts, kt, y0s, vs)
    wq = each(lambda x, y: stack(x, halves(y)), wides, qe)
    z = []
    out = []
    for c in range(STEP_CHUNKS):
        for g in range(2):
            i = c * 2 + g
            now = state_ref[g]
            nows = spread(halves(now), masks)
            state_ref[g] = mul(halves(tr[i]), nows) + inject[i]
            z.append(now)
            out.append(mul(wq[i], nows))
    o = each(lambda x, y: x[CHUNK:] + y, out, part)
    mixed = each(lambda x, y, z, m, n: read_out(x, y, z, m, n, ones)[3], o, q, k, v, vec)
    for i, u in enumerate(units):
        out_ref[u] = (mixed[i] * gate_ref[u]).astype(jnp.bfloat16)
        o_ref[u] = o[i]
        y_ref[u] = out[i][:CHUNK] + y0[i]
        t_ref[u] = t[i]
        aqb_ref[u] = with_b[i][CHUNK:] * within
        aak_ref[u] = with_k[i][:CHUNK] * strict
        aqk_ref[u] = with_k[i][CHUNK:] * within
        z_ref[u] = z[i]
        trt_ref[u] = trt[i]
        qe_ref[u] = qe[i]


def backward_kernel(
    len_ref, vec_ref, q_ref, keys_ref, v_ref, dl_ref, rl_ref, gate_ref, g_ref, o_ref,
    t_ref, aqb_ref, aak_ref, aqk_ref, y_ref, z_ref, trt_ref, qe_ref,
    dq_ref, dkeys_ref, dv_ref, ddl_ref, drl_ref, dgate_ref, dvec_ref,
    state_ref,
):
    step = pl.num_programs(0) - 1 - pl.program_id(0)

    @pl.when(pl.program_id(0) == 0)
    def _():
        state_ref[...] = jnp.zeros_like(state_ref)
        dvec_ref[...] = jnp.zeros_like(dvec_ref)

    masks = head_masks()
    row, col = places()
    strict = (col < row).astype(jnp.float32)
    within = (col <= row).astype(jnp.float32)
    ones = block_ones()
    units = unit_slices()
    live = unit_live(len_ref[0], step)
    vec = unit_vectors(vec_ref)
    load = lambda ref: [ref[u] for u in units]
    q, keys, v, g = load(q_ref), load(keys_ref), load(v_ref), load(g_ref)
    ready = each(
        lambda x, y, z, m, n: prepared(x, y, z, m, n, ones), keys, load(dl_ref), load(rl_ref), live, vec
    )
    w, k, a, b, sig, rates, inverse, factor = ([x[i] for x in ready] for i in range(8))
    seen = each(lambda x, y, z, m, n: read_out(x, y, z, m, n, ones), load(o_ref), q, k, v, vec)
    normed, scale, weight, mixed = ([x[i] for x in seen] for i in range(4))
    gate = load(gate_ref)
    dgate = each(lambda x, y: x * y, g, mixed)
    dmix = each(lambda x, y: x * y, g, gate)
    dn = each(lambda x, n: x * n[5], dmix, vec)
    do = each(
        lambda x, n, r: r
        * (x - head_sum(x, ones) * (1.0 / CHUNK) - n * (head_sum(x * n, ones) * (1.0 / CHUNK))),
        dn, normed, scale,
    )
    dweight = each(lambda x, y: head_sum(x * y, ones), dmix, v)
    do = [halves(x) for x in do]
    qe, trt, t, aqb, aak, aqk, ys = (
        [halves(x) for x in load(ref)]
        for ref in (qe_ref, trt_ref, t_ref, aqb_ref, aak_ref, aqk_ref, y_ref)
    )
    z = load(z_ref)
    vs = [halves(x) for x in v]
    h = each(lambda x, y: tmul(x, y, masks), qe, do)
    dz = [None] * len(units)
    for c in reversed(range(STEP_CHUNKS)):
        for g in range(2):
            i = c * 2 + g
            now = state_ref[g]
            dz[i] = now
            state_ref[g] = mul(trt[i], spread(halves(now), masks)) + h[i]
    dzs = [spread(halves(x), masks) for x in dz]
    zs = [spread(halves(x), masks) for x in z]
    forms = each(scaled_forms, q, w, k, a, b)
    ah, qh, bh, kh, bt, kt = ([f[0][i] for f in forms] for i in range(6))
    ea, eq, eb, ee = ([f[1][i] for f in forms] for i in range(4))
    emid = [f[2][0] for f in forms]
    eend = [f[2][1] for f in forms]
    from_end = each(lambda x, y, s: mul(halves(jnp.concatenate([x, y], axis=0)), s), bt, kt, dzs)
    dy = each(lambda x, y, s: halves(tmul(x, y, masks) + s[:CHUNK]), aqb, do, from_end)
    dr = each(lambda x, y: halves(tmul(x, y, masks)), t, dy)
    ro = each(stack, dr, do)
    dv = each(lambda x, y, s, f: tmul(stack(x, y), s, masks) + f[CHUNK:], aak, aqk, ro, from_end)
    mask2 = jnp.concatenate([strict, within], axis=0)
    dab = each(lambda s, y: halves(mul(s, spread(y, masks), NT) * mask2), ro, ys)
    dak = each(lambda s, y: halves(mul(s, spread(y, masks), NT) * mask2), ro, vs)
    dst = each(lambda s, y: mul(s, y, NT), ro, zs)
    daq = each(
        lambda s, e, x, bb, y, kk: s * e + mul(x, spread(halves(bb), masks)) + mul(y, spread(halves(kk), masks)),
        dst, emid, dab, bh, dak, kh,
    )
    aq = each(lambda x, y: halves(jnp.concatenate([x, y], axis=0)), ah, qh)
    dbh = each(lambda x, y: tmul(x, y, masks), dab, aq)
    dkh = each(lambda x, y: tmul(x, y, masks), dak, aq)
    dend = each(lambda y, x, s: mul(stack(y, x), s, NT), ys, vs, dzs)
    row_of_ones = jnp.ones((8, LANES), jnp.bfloat16)
    sums = lambda x: jnp.sum(x, axis=0, keepdims=True)
    for i, u in enumerate(units):
        da = daq[i][:CHUNK] * ea[i]
        dq = daq[i][CHUNK:] * eq[i]
        dbt = dend[i][:CHUNK] * ee[i]
        dkt = dend[i][CHUNK:] * ee[i]
        db = dbh[i] * eb[i] + dbt
        dk = dkh[i] * eb[i] + dkt
        pa = da * a[i]
        diff = dq * q[i] - db * b[i] - dk * k[i] + pa
        zz = spread(halves(z[i] * dz[i]), masks)
        carry = (dot32(row_of_ones, zz[0], NT) + dot32(row_of_ones, zz[1], NT))[:1] * eend[i]
        carry = carry + sums(dbt * b[i] + dkt * k[i])
        dw = running_sum(diff, upper=True) - pa + carry
        from_bonus = dweight[i] * vec[i][4]
        dk = dk + from_bonus * q[i]
        dq_ref[u] = (dq + from_bonus * k[i]).astype(jnp.bfloat16)
        dv_ref[u] = (dv[i] + weight[i] * dmix[i]).astype(jnp.bfloat16)
        dgate_ref[u] = dgate[i].astype(jnp.bfloat16)
        unit_keys = -a[i]
        db = db * live[i]
        du = db * rates[i] - da
        dscaled = inverse[i] * (du - unit_keys * head_sum(du * unit_keys, ones))
        dkl = dk * keys[i] * live[i]
        drl = (db * unit_keys + dkl * vec[i][3]) * rates[i] * (1.0 - rates[i])
        ddl = dw * w[i] * (1.0 - sig[i])
        dkeys_ref[u] = (dk * factor[i] + dscaled * vec[i][2]).astype(jnp.bfloat16)
        ddl_ref[u] = ddl.astype(jnp.bfloat16)
        drl_ref[u] = drl.astype(jnp.bfloat16)
        parts = (
            ddl, drl, dscaled * keys[i], dkl * (rates[i] - 1.0),
            dweight[i] * q[i] * k[i], dmix[i] * normed[i], dmix[i],
        )
        lanes = u[1]
        for j, x in enumerate(parts):
            dvec_ref[j : j + 1, lanes] += sums(x)


def wkv_calls(tokens, width):
    rows = CHUNK * STEP_CHUNKS
    steps = tokens // rows
    params = dict(
        grid=(steps,),
        scratch_shapes=[pltpu.VMEM((2, CHUNK, LANES), jnp.float32)],
        compiler_params=pltpu.CompilerParams(vmem_limit_bytes=56 << 20),
        cost_estimate=SMALL,
    )
    shape = lambda dtype: jax.ShapeDtypeStruct((tokens, width), dtype)
    return rows, steps, params, shape


def wkv_forward(length, vec, *arrays):
    tokens, width = arrays[0].shape
    rows, steps, params, shape = wkv_calls(tokens, width)
    spec = pl.BlockSpec((rows, width), lambda i: (i, 0))
    return pl.pallas_call(
        forward_kernel,
        in_specs=[
            pl.BlockSpec(memory_space=pltpu.SMEM), pl.BlockSpec((8, width), lambda i: (0, 0)),
        ]
        + [spec] * 6,
        out_specs=[spec] * 10,
        out_shape=[shape(jnp.bfloat16)] + [shape(jnp.float32)] * 9,
        name="wkv_forward",
        **params,
    )(length, vec, *arrays)


def wkv_backward(length, vec, *arrays):
    tokens, width = arrays[0].shape
    rows, steps, params, shape = wkv_calls(tokens, width)
    spec = pl.BlockSpec((rows, width), lambda i: (steps - 1 - i, 0))
    whole = pl.BlockSpec((8, width), lambda i: (0, 0))
    return pl.pallas_call(
        backward_kernel,
        in_specs=[pl.BlockSpec(memory_space=pltpu.SMEM), whole] + [spec] * 16,
        out_specs=[spec] * 6 + [whole],
        out_shape=[shape(jnp.bfloat16)] * 6 + [jax.ShapeDtypeStruct((8, width), jnp.float32)],
        name="wkv_backward",
        **params,
    )(length, vec, *arrays)
ROWS = 128


def row_norm(x):
    centred = x - jnp.mean(x, axis=-1, keepdims=True)
    scale = lax.rsqrt(jnp.mean(centred * centred, axis=-1, keepdims=True) + 1e-05)
    return centred * scale, scale


def shifted(x, edge, down):
    rows = x.shape[0]
    row = lax.broadcasted_iota(jnp.int32, x.shape, 0)
    if down:
        return jnp.where(row == 0, edge, pltpu.roll(x, 1, 0))
    return jnp.where(row == rows - 1, edge, pltpu.roll(x, rows - 1, 0))


def below(x, upper):
    lane = lax.broadcasted_iota(jnp.int32, x.shape, 1)
    keep = (lane >= DECAY_RANK) if upper else (lane < DECAY_RANK)
    return jnp.where(keep, x, jnp.zeros_like(x))


def front_kernel(
    x_ref, vec_ref, wr_ref, wk_ref, wv_ref, down_ref, up_ref,
    m0_ref, m1_ref, m2_ref, m3_ref, m4_ref, m5_ref,
    q_ref, k_ref, v_ref, dl_ref, rl_ref, gate_ref, hid_ref,
    edge_ref,
):
    @pl.when(pl.program_id(0) == 0)
    def _():
        edge_ref[...] = jnp.zeros_like(edge_ref)

    unit, _ = row_norm(x_ref[...].astype(jnp.float32))
    normed = unit * vec_ref[12:13] + vec_ref[13:14]
    change = shifted(normed, edge_ref[:1], True) - normed
    edge_ref[:1] = normed[ROWS - 1 :]
    mixes = []
    for j, ref in enumerate((m0_ref, m1_ref, m2_ref, m3_ref, m4_ref, m5_ref)):
        mixes.append((normed + change * vec_ref[j : j + 1]).astype(jnp.bfloat16))
        ref[...] = mixes[j]
    q_ref[...] = dot32(mixes[0], wr_ref[...], NN)
    k_ref[...] = dot32(mixes[2], wk_ref[...], NN)
    v_ref[...] = dot32(mixes[3], wv_ref[...], NN)
    first = down_ref[:, :128]
    pre_decay, pre_rate = dot32(mixes[1], first, NN), dot32(mixes[4], first, NN)
    pre_gate = dot32(mixes[5], down_ref[:, 128:], NN)
    lane = lax.broadcasted_iota(jnp.int32, pre_decay.shape, 1)
    pair = jnp.where(lane < DECAY_RANK, jnp.tanh(pre_decay), pre_rate)
    gate = jax.nn.sigmoid(pre_gate)
    hid_ref[:, :128] = pair
    hid_ref[:, 128:] = gate
    narrow_pair = pair.astype(jnp.bfloat16)
    dl_ref[...] = dot32(below(narrow_pair, False), up_ref[:, :128], NT)
    rl_ref[...] = dot32(below(narrow_pair, True), up_ref[:, :128], NT)
    gate_ref[...] = dot32(gate.astype(jnp.bfloat16), up_ref[:, 128:], NT)


def front_forward(x, vectors, w_r, w_k, w_v, down, up):
    tokens, width = x.shape
    wide = pl.BlockSpec((ROWS, width), lambda i: (i, 0))
    own = pl.BlockSpec((ROWS, OWN), lambda i: (i, 0))
    hid = pl.BlockSpec((ROWS, 256), lambda i: (i, 0))
    whole = lambda a: pl.BlockSpec(a.shape, lambda i: (0, 0))
    shape = jax.ShapeDtypeStruct
    return pl.pallas_call(
        front_kernel,
        grid=(tokens // ROWS,),
        in_specs=[wide] + [whole(a) for a in (vectors, w_r, w_k, w_v, down, up)],
        out_specs=[wide] * 6 + [own] * 6 + [hid],
        out_shape=[shape((tokens, width), jnp.bfloat16)] * 6
        + [shape((tokens, OWN), jnp.float32)] * 6
        + [shape((tokens, 256), jnp.float32)],
        scratch_shapes=[pltpu.VMEM((8, width), jnp.float32)],
        compiler_params=pltpu.CompilerParams(vmem_limit_bytes=48 << 20),
        cost_estimate=SMALL,
        name="front_forward",
    )(x, vectors, w_r, w_k, w_v, down, up)


def front_back_kernel(
    x_ref, before_ref, vec_ref, wr_ref, wk_ref, wv_ref, down_ref, up_ref,
    m1_ref, m4_ref, m5_ref, hid_ref,
    dq_ref, dk_ref, dv_ref, ddl_ref, drl_ref, dgate_ref, own_vec_ref, ffn_vec_ref,
    dx_ref, misc_ref,
    edge_ref, sums_ref,
):
    step = pl.num_programs(0) - 1 - pl.program_id(0)
    core = lax.axis_index("dp") % 2
    own_start = pl.multiple_of(core * OWN, OWN)

    @pl.when(pl.program_id(0) == 0)
    def _():
        edge_ref[...] = jnp.zeros_like(edge_ref)
        sums_ref[...] = jnp.zeros_like(sums_ref)
        misc_ref[...] = jnp.zeros_like(misc_ref)

    unit, scale = row_norm(x_ref[...].astype(jnp.float32))
    gain, offset = vec_ref[12:13], vec_ref[13:14]
    normed = unit * gain + offset
    tail, _ = row_norm(before_ref[...].astype(jnp.float32))
    edge = (tail[15:] * gain + offset) * jnp.where(step == 0, 0.0, 1.0)
    change = shifted(normed, edge, True) - normed
    ddl, drl, dgate = ddl_ref[...], drl_ref[...], dgate_ref[...]
    hid = hid_ref[...]
    pair, gate = hid[:, :128], hid[:, 128:]
    lane = lax.broadcasted_iota(jnp.int32, pair.shape, 1)
    first_up, last_up = up_ref[:, :128], up_ref[:, 128:]
    pair_grad = jnp.where(
        lane < DECAY_RANK,
        dot32(ddl, first_up, NN) * (1.0 - pair * pair),
        dot32(drl, first_up, NN),
    ).astype(jnp.bfloat16)
    gate_grad = (dot32(dgate, last_up, NN) * gate * (1.0 - gate)).astype(jnp.bfloat16)
    narrow_pair, narrow_gate = pair.astype(jnp.bfloat16), gate.astype(jnp.bfloat16)
    own_rows = pl.ds(own_start, OWN)
    misc_ref[own_rows, 256:384] += dot32(ddl, below(narrow_pair, False), TN) + dot32(
        drl, below(narrow_pair, True), TN
    )
    misc_ref[own_rows, 384:512] += dot32(dgate, narrow_gate, TN)
    decay_part, rate_part = below(pair_grad, False), below(pair_grad, True)
    misc_ref[:, :128] += dot32(m1_ref[...], decay_part, TN) + dot32(m4_ref[...], rate_part, TN)
    misc_ref[:, 128:256] += dot32(m5_ref[...], gate_grad, TN)
    first_down = down_ref[:, :128]
    grads = (
        lambda: dot32(dq_ref[...], wr_ref[...], NT),
        lambda: dot32(decay_part, first_down, NT),
        lambda: dot32(dk_ref[...], wk_ref[...], NT),
        lambda: dot32(dv_ref[...], wv_ref[...], NT),
        lambda: dot32(rate_part, first_down, NT),
        lambda: dot32(gate_grad, down_ref[:, 128:], NT),
    )
    total = jnp.zeros_like(change)
    moved = jnp.zeros_like(change)
    for j, grad in enumerate(grads):
        now = grad()
        total = total + now
        moved = moved + now * vec_ref[j : j + 1]
        sums_ref[j : j + 1] += jnp.sum(now * change, axis=0, keepdims=True)
    dnormed = total - moved + shifted(moved, edge_ref[:1], False)
    edge_ref[:1] = moved[:1]
    sums_ref[12:13] += jnp.sum(dnormed * unit, axis=0, keepdims=True)
    sums_ref[13:14] += jnp.sum(dnormed, axis=0, keepdims=True)
    dunit = dnormed * gain
    dx_ref[...] = scale * (
        dunit
        - jnp.mean(dunit, axis=-1, keepdims=True)
        - unit * jnp.mean(dunit * unit, axis=-1, keepdims=True)
    )

    @pl.when(step == 0)
    def _():
        sums_ref[6:7] = ffn_vec_ref[0:1] * 0.5
        sums_ref[14:16] = ffn_vec_ref[1:3] * 0.5
        zeros = jnp.zeros((1, OWN), jnp.float32)
        for target, source in ((7, 0), (8, 1), (9, 2), (10, 3), (11, 4), (16, 5), (17, 6)):
            mine = own_vec_ref[source : source + 1]
            sums_ref[target : target + 1] = jnp.concatenate(
                [jnp.where(core == 0, mine, zeros), jnp.where(core == 0, zeros, mine)], axis=1
            )
        for block in range(EMBED // 128):
            lanes = slice(block * 128, (block + 1) * 128)
            misc_ref[lanes, 512:640] = sums_ref[:, lanes].T


def front_backward(
    x, vectors, w_r, w_k, w_v, down, up, mixes, hid, grads, own_vec, ffn_vec
):
    tokens, width = x.shape
    steps = tokens // ROWS
    wide = pl.BlockSpec((ROWS, width), lambda i: (steps - 1 - i, 0))
    before = pl.BlockSpec(
        (16, width), lambda i: (jnp.maximum((steps - 1 - i) * (ROWS // 16) - 1, 0), 0)
    )
    own = pl.BlockSpec((ROWS, OWN), lambda i: (steps - 1 - i, 0))
    hid_spec = pl.BlockSpec((ROWS, 256), lambda i: (steps - 1 - i, 0))
    whole = lambda a: pl.BlockSpec(a.shape, lambda i: (0, 0))
    shape = jax.ShapeDtypeStruct
    return pl.pallas_call(
        front_back_kernel,
        grid=(steps,),
        in_specs=[wide, before]
        + [whole(a) for a in (vectors, w_r, w_k, w_v, down, up)]
        + [wide] * 3
        + [hid_spec]
        + [own] * 6
        + [whole(own_vec), whole(ffn_vec)],
        out_specs=[wide, pl.BlockSpec((EMBED, 640), lambda i: (0, 0))],
        out_shape=[shape((tokens, width), jnp.float32), shape((EMBED, 640), jnp.float32)],
        scratch_shapes=[
            pltpu.VMEM((8, width), jnp.float32), pltpu.VMEM((128, width), jnp.float32),
        ],
        compiler_params=pltpu.CompilerParams(vmem_limit_bytes=48 << 20),
        cost_estimate=SMALL,
        name="front_backward",
    )(x, x, vectors, w_r, w_k, w_v, down, up, *mixes, hid, *grads, own_vec, ffn_vec)


def ffn_back_kernel(
    len_ref, res_ref, before_ref, cot_ref, mine_ref, other_ref, vec_ref, wo_ref,
    grad_ref, narrow_ref, gated_ref, dvec_ref,
    edge_ref,
):
    step = pl.num_programs(0) - 1 - pl.program_id(0)

    @pl.when(pl.program_id(0) == 0)
    def _():
        edge_ref[...] = jnp.zeros_like(edge_ref)
        dvec_ref[...] = jnp.zeros_like(dvec_ref)

    gain, offset, coefficient = vec_ref[14:15], vec_ref[15:16], vec_ref[6:7]
    unit, scale = row_norm(res_ref[...])
    normed = unit * gain + offset
    tail, _ = row_norm(before_ref[...])
    edge = (tail[7:] * gain + offset) * jnp.where(step == 0, 0.0, 1.0)
    change = shifted(normed, edge, True) - normed
    grad = mine_ref[...].astype(jnp.float32) + other_ref[...].astype(jnp.float32)
    moved = grad * coefficient
    dnormed = grad - moved + shifted(moved, edge_ref[:1], False)
    edge_ref[:1] = moved[:1]
    sums = lambda x: jnp.sum(x, axis=0, keepdims=True)
    dvec_ref[0:1] += sums(grad * change)
    dvec_ref[1:2] += sums(dnormed * unit)
    dvec_ref[2:3] += sums(dnormed)
    dunit = dnormed * gain
    row = lax.broadcasted_iota(jnp.int32, grad.shape, 0) + step * ROWS
    out_grad = jnp.where(row < len_ref[0], cot_ref[...].astype(jnp.float32), 0.0)
    total = out_grad + scale * (
        dunit
        - jnp.mean(dunit, axis=-1, keepdims=True)
        - unit * jnp.mean(dunit * unit, axis=-1, keepdims=True)
    )
    grad_ref[...] = total
    small = total.astype(jnp.bfloat16)
    narrow_ref[...] = small
    gated_ref[...] = dot32(small, wo_ref[...], NT)


def ffn_backward(length, residual, cot, mine, other, vectors, w_o_rows):
    tokens, width = residual.shape
    steps = tokens // ROWS
    wide = pl.BlockSpec((ROWS, width), lambda i: (steps - 1 - i, 0))
    before = pl.BlockSpec(
        (8, width), lambda i: (jnp.maximum((steps - 1 - i) * (ROWS // 8) - 1, 0), 0)
    )
    own = pl.BlockSpec((ROWS, OWN), lambda i: (steps - 1 - i, 0))
    whole = lambda a: pl.BlockSpec(a.shape, lambda i: (0, 0))
    shape = jax.ShapeDtypeStruct
    return pl.pallas_call(
        ffn_back_kernel,
        grid=(steps,),
        in_specs=[pl.BlockSpec(memory_space=pltpu.SMEM), wide, before]
        + [wide] * 3
        + [whole(vectors), whole(w_o_rows)],
        out_specs=[wide, wide, own, pl.BlockSpec((8, width), lambda i: (0, 0))],
        out_shape=[
            shape((tokens, width), jnp.float32),
            shape((tokens, width), jnp.bfloat16),
            shape((tokens, OWN), jnp.float32),
            shape((8, width), jnp.float32),
        ],
        scratch_shapes=[pltpu.VMEM((8, width), jnp.float32)],
        compiler_params=pltpu.CompilerParams(vmem_limit_bytes=48 << 20),
        cost_estimate=SMALL,
        name="ffn_backward",
    )(length, residual, residual, cot, mine, other, vectors, w_o_rows)


def att_grad_kernel(m0_ref, m2_ref, m3_ref, gated_ref, dq_ref, dk_ref, dv_ref, da_ref,
                    send_a, keep_a, send_b, keep_b):
    chip = lax.axis_index("dp") // 2
    by_x, by_y = chip % 2 == 0, (chip // 2) % 2 == 0
    core = lax.axis_index("dp") % 2
    da = da_ref[:, pl.ds(pl.multiple_of(core * OWN, OWN), OWN)]
    first = ((m0_ref, dq_ref[...]), (gated_ref, da))
    second = ((m2_ref, dk_ref[...]), (m3_ref, dv_ref[...]))
    for half, ((left_a, right_a), (left_b, right_b)) in enumerate(zip(first, second)):
        lanes = slice(half * OWN, (half + 1) * OWN)
        for z in range(4):
            rows = slice(z * 256, (z + 1) * 256)
            block = dot32(left_a[:, rows], right_a, TN).astype(jnp.bfloat16)
            for y in range(2):
                low, high = block[y * 128 : y * 128 + 64], block[y * 128 + 64 : y * 128 + 128]
                send_a[2 * z + y, :, lanes] = jnp.where(by_x, high, low)
                keep_a[2 * z + y, :, lanes] = jnp.where(by_x, low, high)
            block = dot32(left_b[:, rows], right_b, TN).astype(jnp.bfloat16)
            for x in range(2):
                low, high = block[x * 64 : x * 64 + 64], block[128 + x * 64 : 128 + x * 64 + 64]
                send_b[2 * z + x, :, lanes] = jnp.where(by_y, high, low)
                keep_b[2 * z + x, :, lanes] = jnp.where(by_y, low, high)


def att_gradients(mixes, gated, grads, attended_grad):
    space = pl.BlockSpec(memory_space=pltpu.VMEM)
    return pl.pallas_call(
        att_grad_kernel,
        in_specs=[space] * 8,
        out_specs=[space] * 4,
        out_shape=[jax.ShapeDtypeStruct((8, 64, 2 * OWN), jnp.bfloat16)] * 4,
        compiler_params=pltpu.CompilerParams(vmem_limit_bytes=40 << 20),
        cost_estimate=SMALL,
        name="att_gradients",
    )(*mixes, gated, *grads, attended_grad)


def swap(block, mask):
    size = lax.axis_size("dp")
    return lax.ppermute(block, "dp", [(i, i ^ mask) for i in range(size)])


def bit_of(mask):
    return (lax.axis_index("dp") // mask) % 2


def in_order(mask, own, other, axis):
    lower = bit_of(mask) == 0
    return jnp.where(
        lower, jnp.concatenate([own, other], axis=axis), jnp.concatenate([other, own], axis=axis)
    )


def chip_masks():
    size = lax.axis_size("dp")
    masks = []
    while 2 << len(masks) < size:
        masks.append(2 << len(masks))
    return masks


def steps_of(kind):
    masks = chip_masks()
    near, far = [[mask] for mask in masks[:2]], masks[2:][::-1]
    first = [[far[0], far[1], far[0] | far[1]]] if len(far) == 2 else [[mask] for mask in far]
    return [first + near[::-1], first + near, near + first][kind]


def meet(movers, *arrays):
    held = lax.optimization_barrier(tuple(tuple(m.arrived) for m in movers) + arrays)
    for mover, arrived in zip(movers, held):
        mover.arrived = list(arrived)
    return held[len(movers) :]


class Gather:
    def __init__(self, block, kind, places=(0,)):
        self.steps = steps_of(kind)
        self.held = block[None]
        self.places = [0]
        self.arrived = []
        self.masks = []

    def merge(self):
        if self.arrived:
            self.held = jnp.concatenate([self.held] + self.arrived, axis=0)
            self.places = self.places + [p ^ (m // 2) for m in self.masks for p in self.places]
            self.arrived = []

    def step(self):
        if self.steps:
            self.merge()
            self.masks = self.steps.pop(0)
            self.arrived = [swap(self.held, mask) for mask in self.masks]
        return self

    def run(self):
        while self.steps:
            self.step()
        return self

    def split(self, kinds):
        width = self.held.shape[-1] // len(kinds)
        out = []
        for i, kind in enumerate(kinds):
            part = Gather.__new__(Gather)
            cut = slice(i * width, (i + 1) * width)
            part.steps = steps_of(kind)[len(steps_of(kind)) - len(self.steps) :]
            part.held = self.held[..., cut]
            part.arrived = [x[..., cut] for x in self.arrived]
            part.places, part.masks = self.places, self.masks
            out.append(part)
        return out


def place_kernel(places, cuts, *refs):
    sources, outs = refs[: len(places)], refs[len(places) :]
    chip = lax.axis_index("dp") // 2
    for source, (part, list_of) in zip(sources, places):
        for j, place in enumerate(list_of):
            for out, (first, rows, lane, width) in zip(outs, cuts):
                start = pl.multiple_of((chip ^ place) * rows, rows)
                out[pl.ds(start, rows), part * width : (part + 1) * width] = source[
                    j, first : first + rows, lane : lane + width
                ]


def assemble(gathers, cuts=None):
    gathers = [g.run() for g in gathers]
    rows, width = gathers[0].held.shape[1:]
    cuts = cuts or ((0, rows, 0, width),)
    sources, places = [], []
    for i, g in enumerate(gathers):
        sources += [g.held] + g.arrived
        shifts = [0] + [mask // 2 for mask in g.masks]
        places += [(i, [p ^ shift for p in g.places]) for shift in shifts]
    count = lax.axis_size("dp") // 2
    if any(cut[1] % 16 for cut in cuts):
        return assemble_plain(sources, places, cuts, count)
    space = pl.BlockSpec(memory_space=pltpu.VMEM)
    return pl.pallas_call(
        partial(place_kernel, places, cuts),
        in_specs=[space] * len(sources),
        out_specs=[space] * len(cuts),
        out_shape=[
            jax.ShapeDtypeStruct((count * n, w * len(gathers)), sources[0].dtype)
            for _, n, _, w in cuts
        ],
        compiler_params=pltpu.CompilerParams(vmem_limit_bytes=32 << 20),
        cost_estimate=SMALL,
        name="assemble",
    )(*sources)


def assemble_plain(sources, places, cuts, count):
    chip = lax.axis_index("dp") // 2
    parts = []
    for part in sorted({part for part, _ in places}):
        blocks = jnp.concatenate([x for x, (at, _) in zip(sources, places) if at == part])
        where = [p for at, list_of in places if at == part for p in list_of]
        blocks = jnp.stack([blocks[where.index(i)] for i in range(count)])
        parts.append(jnp.take(blocks, chip ^ lax.iota(jnp.int32, count), axis=0))
    return [
        jnp.concatenate([x[:, first : first + n, lane : lane + w] for x in parts], axis=-1).reshape(
            count * n, -1
        )
        for first, n, lane, w in cuts
    ]


class Scatter:
    def __init__(self, parts, kind):
        self.steps = steps_of(kind)[::-1]
        self.axes = chip_masks()[::-1]
        shape = parts.shape[1:]
        self.sources = [parts.reshape((2,) * len(self.axes) + shape)]
        self.arrived = []

    def pick(self, mask, gone):
        out = []
        for x in self.sources:
            for place in reversed(range(len(self.axes))):
                axis = self.axes[place]
                if axis in gone:
                    which = bit_of(axis) if not mask & axis else 1 - bit_of(axis)
                    x = lax.dynamic_index_in_dim(x, which, place, keepdims=False)
            out.append(x)
        return out

    def merge(self):
        self.sources = self.sources + self.arrived
        self.arrived = []

    def step(self):
        if self.steps:
            self.merge()
            masks = self.steps.pop(0)
            gone = [axis for axis in self.axes if any(mask & axis for mask in masks)]
            sends = [
                sum(x.astype(jnp.float32) for x in self.pick(mask, gone)).astype(jnp.bfloat16)
                for mask in masks
            ]
            self.sources = self.pick(0, gone)
            self.axes = [axis for axis in self.axes if axis not in gone]
            self.sent = sends
            self.arrived = [swap(x, mask) for x, mask in zip(sends, masks)]
        return self

    def run(self):
        while self.steps:
            self.step()
        return self

    def total(self):
        self.merge()
        return sum(x.astype(jnp.float32) for x in self.sources)

    @classmethod
    def begun(cls, sent, kept, kind):
        out = cls.__new__(cls)
        out.steps = steps_of(kind)[::-1]
        masks = out.steps.pop(0)
        out.axes = [axis for axis in chip_masks()[::-1] if axis not in masks]
        out.sources = [kept.reshape((2,) * len(out.axes) + kept.shape[1:])]
        out.sent = [sent.reshape(out.sources[0].shape)]
        out.arrived = [swap(out.sent[0], masks[0])]
        return out

    @staticmethod
    def join(parts):
        out = Scatter.__new__(Scatter)
        out.steps, out.axes, out.arrived = parts[0].steps, parts[0].axes, []
        out.sources = [jnp.concatenate([part.total() for part in parts], axis=-1)]
        return out


def norm_rows(features, gain_row, offset_row):
    average = jnp.mean(features, axis=-1, keepdims=True)
    centred = features - average
    variance = jnp.mean(centred * centred, axis=-1, keepdims=True)
    return centred * lax.rsqrt(variance + 1e-05) * gain_row + offset_row


def product(operand, weight_matrix):
    return jnp.dot(operand, weight_matrix, preferred_element_type=jnp.float32)


def input_gradient_rows(upstream_gradient, weight_matrix):
    return lax.dot_general(
        upstream_gradient,
        weight_matrix,
        (((1,), (1,)), ((), ())),
        preferred_element_type=jnp.float32,
    )


def weight_gradient(operand, upstream_gradient):
    return lax.dot_general(
        operand, upstream_gradient, (((0,), (0,)), ((), ())), preferred_element_type=jnp.float32
    )


def earlier(rows):
    return jnp.concatenate([jnp.zeros_like(rows[:1]), rows[:-1]], axis=0)


def ffn_mix(residual, vectors):
    second = norm_rows(residual, vectors[14], vectors[15])
    return second + (earlier(second) - second) * vectors[6]


def narrow(x):
    return x.astype(jnp.bfloat16)


def local(
    inputs,
    lengths,
    attention_projections,
    channel_key_weight,
    channel_value_weight,
    lowrank_down_weight,
    lowrank_up_weight,
    per_feature_parameters,
    cotangent,
):
    devices = lax.axis_size("dp")
    chips = devices // 2
    device = lax.axis_index("dp")
    chip, core = device // 2, device % 2
    row_count = inputs.shape[0]
    slots = 2 * row_count
    share = EMBED // devices
    pair_share = 2 * share
    units = channel_value_weight.shape[0]
    half_units = chips * units

    def own_cut(x, which):
        return lax.dynamic_slice_in_dim(x, which * OWN, OWN, x.ndim - 1)

    def own_rows(x, which):
        return lax.dynamic_slice_in_dim(x, which * row_count, row_count, 0)

    pair_rows = in_order(
        1,
        own_cut(attention_projections, core),
        swap(own_cut(attention_projections, 1 - core), 1),
        1,
    )
    lora = jnp.concatenate([lowrank_down_weight, lowrank_up_weight.T], axis=1)
    vector_rows = jnp.pad(per_feature_parameters.T, ((0, 0), (0, 128 - 18)))
    vector_rows = vector_rows.reshape(share // 4, OWN)
    first_rows = 3 * pair_share
    misc_rows = share + share // 4 + (share // 4) % 16
    block = jnp.concatenate(
        [
            pair_rows[:3].reshape(first_rows, OWN),
            lora,
            jnp.pad(vector_rows, ((0, (share // 4) % 16), (0, 0))),
        ],
        axis=0,
    )
    first = Gather(block, 0).step()
    key_cut = channel_key_weight.reshape(share, chips, 2, units)

    def key_columns(which):
        return lax.dynamic_index_in_dim(key_cut, which, 2, keepdims=False).reshape(share, half_units)

    half = half_units // 2
    quarter = OWN // 2
    key_rows = in_order(1, key_columns(core), swap(key_columns(1 - core), 1), 0)
    key_rows = jnp.concatenate(
        [pair_rows[3, :, :quarter], key_rows[:, :half], pair_rows[3, :, quarter:], key_rows[:, half:]],
        axis=1,
    )
    (key_rows,) = meet([first], key_rows)
    first = first.split((0, 1))
    for part in first:
        part.step()
    key_part = Gather(key_rows, 0).step()
    tokens = in_order(1, inputs, swap(inputs, 1), 0)
    cot = in_order(1, cotangent, swap(cotangent, 1), 0)
    tokens, cot = meet(first, tokens, cot)
    for part in first:
        part.step()
    value_block, tokens = meet(first + [key_part], channel_value_weight, tokens)
    w_r, w_k, w_v, misc = assemble(
        first,
        [(i * pair_share, pair_share, 0, quarter) for i in range(3)]
        + [(first_rows, misc_rows, 0, quarter)],
    )
    key_parts = key_part.split((0, 1))
    for part in key_parts:
        part.step()
    misc = misc.reshape(chips, 1, misc_rows, OWN)
    misc = in_order(1, misc, swap(misc, 1), 1)
    lora = misc[:, :, :share].reshape(EMBED, OWN)
    down, up_t = lora[:, :256], lax.dynamic_slice_in_dim(lora[:, 256:], core * OWN, OWN, 0)
    vectors = misc[:, :, share : share + share // 4].reshape(EMBED, 128)[:, :18].T
    vectors = vectors.astype(jnp.float32)
    own_vectors = own_cut(vectors, core)
    used = jnp.concatenate([own_vectors[7:12], own_vectors[16:18], own_vectors[:1]], axis=0)
    length = lax.dynamic_index_in_dim(lengths, chip, 0)
    live = (lax.iota(jnp.int32, slots) < length)[:, None]

    *mixes, queries, keys, values, decay_low, rate_low, gate_rows, hid = front_forward(
        tokens, vectors, w_r, w_k, w_v, down, up_t
    )
    terms = meet(key_parts, queries, keys, values, decay_low, rate_low, gate_rows)
    for part in key_parts:
        part.step()
    value_part = Gather(value_block, 0).step()
    gated, *saved = wkv_forward(length, used, *terms)
    gated, cot, tokens = meet(key_parts + [value_part], gated, cot, tokens)
    value_parts = value_part.split((0, 1))
    for part in value_parts:
        part.step()
    gated_all = in_order(1, gated, swap(gated, 1), 1)
    key_weight, w_o_own = assemble(
        key_parts, ((0, pair_share, quarter, half), (0, pair_share, 0, quarter))
    )
    w_o = in_order(1, w_o_own, swap(w_o_own, 1), 1)
    residual = tokens.astype(jnp.float32) + product(gated_all, w_o)
    ffn_in = narrow(ffn_mix(residual, vectors))
    positive = jax.nn.relu(product(ffn_in, key_weight))
    hidden = narrow(jnp.square(positive))
    positive, hidden = meet(value_parts, positive, hidden)
    for part in value_parts:
        part.step()
    out_narrow = jnp.where(live, cot, jnp.zeros_like(cot))
    value_scatter = [
        Scatter(
            narrow(weight_gradient(hidden, out_narrow[:, i * OWN : (i + 1) * OWN])).reshape(
                chips, units, OWN
            ),
            i,
        ).step()
        for i in range(2)
    ]
    hidden, positive, out_narrow, *_ = meet(
        value_parts, hidden, positive, out_narrow, *[x for m in value_scatter for x in m.sent]
    )
    (value_weight,) = assemble(value_parts)

    pre_narrow = narrow(2.0 * positive * input_gradient_rows(out_narrow, value_weight))
    ffn_in_grad = narrow(input_gradient_rows(pre_narrow, key_weight))
    other_grad = swap(ffn_in_grad, 1)
    ffn_in_grad, other_grad, pre_narrow, hidden = meet(
        [], ffn_in_grad, other_grad, pre_narrow, hidden
    )
    residual_grad, attended_grad, gated_grad, ffn_vec = ffn_backward(
        length, residual, cot, ffn_in_grad, other_grad, vectors,
        lax.dynamic_slice_in_dim(w_o, core * OWN, OWN, 0),
    )
    grad_key = narrow(weight_gradient(ffn_in, pre_narrow)).reshape(chips, pair_share, half_units)
    gated_grad, grad_key = meet(value_scatter, gated_grad, grad_key)
    for part in value_scatter:
        part.step()
    key_scatter = [
        Scatter(grad_key[:, :, i * half : (i + 1) * half], i).step() for i in range(2)
    ]
    gated_grad, *_ = meet(
        [], gated_grad, *[x for m in value_scatter + key_scatter for x in m.sent]
    )
    *low_grads, own_vec = meet(
        key_scatter + value_scatter, *wkv_backward(length, used, *terms, gated_grad, *saved)
    )
    for part in key_scatter:
        part.step()
    if pair_share == 64:
        sent_a, kept_a, sent_b, kept_b = att_gradients(
            (mixes[0], mixes[2], mixes[3]), gated_all, low_grads[:3], attended_grad
        )
        att_scatter = [Scatter.begun(sent_a, kept_a, 0), Scatter.begun(sent_b, kept_b, 1)]
    else:
        grads = [weight_gradient(mixes[m], g) for m, g in zip((0, 2, 3), low_grads)]
        grad_o = weight_gradient(gated_all, own_cut(attended_grad, core))
        att_scatter = [
            Scatter(narrow(jnp.concatenate(x, axis=1)).reshape(chips, pair_share, 2 * OWN), i).step()
            for i, x in enumerate(((grads[0], grad_o), (grads[1], grads[2])))
        ]
    value_scatter = Scatter.join(value_scatter).step()
    own_vec, *_ = meet(
        [], own_vec, *[x for m in att_scatter + key_scatter + [value_scatter] for x in m.sent]
    )
    token_part, misc_grad = front_backward(
        tokens, vectors, w_r, w_k, w_v, down, up_t, (mixes[1], mixes[4], mixes[5]), hid,
        low_grads, own_vec, ffn_vec,
    )
    ffn_part = product(hidden, value_weight)
    token_part, misc_grad = meet(key_scatter + att_scatter, token_part, misc_grad)
    key_scatter = Scatter.join(key_scatter).step()
    for part in att_scatter:
        part.step()
    misc_grad = misc_grad.reshape(chips, 2, share, 640)
    misc_mine = lax.dynamic_index_in_dim(misc_grad, core, 1, keepdims=False)
    misc_other = narrow(lax.dynamic_index_in_dim(misc_grad, 1 - core, 1, keepdims=False))
    misc_scatter = Scatter(misc_mine + swap(misc_other, 1).astype(jnp.float32), 0).step()
    ffn_out = own_rows(ffn_part, core) + swap(own_rows(ffn_part, 1 - core), 1)
    output = narrow(jnp.where(own_rows(live, core), own_rows(residual, core) + ffn_out, 0.0))
    input_gradient = (
        own_rows(residual_grad, core)
        + own_rows(token_part, core)
        + swap(own_rows(token_part, 1 - core), 1)
    )
    meet(att_scatter + [misc_scatter, value_scatter])
    att_scatter = Scatter.join(att_scatter).step()
    misc_scatter.step()
    meet([misc_scatter, key_scatter])
    misc_scatter.run()
    value_sum = value_scatter.run().total()
    key_sum = key_scatter.run().total()
    att_sum = att_scatter.run().total()
    misc_sum = misc_scatter.total()
    pair_sum = jnp.concatenate([att_sum, key_sum], axis=1).reshape(2, share, -1)
    mine = lax.dynamic_index_in_dim(pair_sum, core, 0, keepdims=False)
    theirs = swap(lax.dynamic_index_in_dim(pair_sum, 1 - core, 0, keepdims=False), 1)
    shard_mixer = jnp.stack(
        [
            in_order(1, mine[:, i * OWN : (i + 1) * OWN], theirs[:, i * OWN : (i + 1) * OWN], 1)
            for i in (0, 2, 3, 1)
        ]
    )
    shard_key = in_order(
        1,
        mine[:, 4 * OWN :].reshape(share, chips, 1, units),
        theirs[:, 4 * OWN :].reshape(share, chips, 1, units),
        2,
    ).reshape(share, 2 * half_units)
    return (
        output,
        input_gradient,
        shard_mixer,
        shard_key,
        value_sum,
        misc_sum[:, :256],
        misc_sum[:, 256:512].T,
        misc_sum[:, 512:530].T,
    )


def solution(mesh):
    in_specs = (
        P("dp", None),
        P(),
        P(None, "dp", None),
        P("dp", None),
        P("dp", None),
        P("dp", None),
        P(None, "dp"),
        P(None, "dp"),
        P("dp", None),
    )
    out_specs = (
        P("dp", None),
        P("dp", None),
        P(None, "dp", None),
        P("dp", None),
        P("dp", None),
        P("dp", None),
        P(None, "dp"),
        P(None, "dp"),
    )
    return jax.shard_map(local, mesh=mesh, in_specs=in_specs, out_specs=out_specs, check_vma=False)
```

```python
from functools import partial

import jax
import jax.numpy as jnp
from jax import lax
from jax.experimental import pallas as pl
from jax.experimental.pallas import tpu as pltpu
from jax.sharding import PartitionSpec as P

HEADS = 16
HEAD_SIZE = 64
DECAY_RANK = 64
RATE_RANK = 64
EMBED = 1024
OWN = EMBED // 2
PRECISE = lax.Precision.HIGHEST


CHUNK = 64
LANES = 256
GROUP_HEADS = 4
STEP_CHUNKS = 2
SMALL = pl.CostEstimate(flops=1, bytes_accessed=1, transcendentals=0)

NN = (((1,), (0,)), ((), ()))
NT = (((1,), (1,)), ((), ()))
TN = (((0,), (0,)), ((), ()))


def halves(x):
    high = x.astype(jnp.bfloat16)
    return high, (x - high.astype(jnp.float32)).astype(jnp.bfloat16)


def dot32(a, b, dims):
    return lax.dot_general(a, b, dims, preferred_element_type=jnp.float32)


def mul(left, right, dims=NN):
    rows = left[0].shape[0]
    both = dot32(jnp.concatenate(left, axis=0), right[0], dims)
    return both[:rows] + both[rows:] + dot32(left[0], right[1], dims)


def tmul(left, right, masks):
    full = (
        dot32(left[0], right[0], TN) + dot32(left[1], right[0], TN) + dot32(left[0], right[1], TN)
    )
    return sum(full[h * CHUNK : (h + 1) * CHUNK] * masks[h][:1].astype(jnp.float32) for h in range(GROUP_HEADS))


def spread(pair, masks):
    return tuple(
        jnp.concatenate([part * masks[h] for h in range(GROUP_HEADS)], axis=0) for part in pair
    )


def stack(first, second):
    return tuple(jnp.concatenate([x, y], axis=0) for x, y in zip(first, second))


def head_masks():
    lane = lax.broadcasted_iota(jnp.int32, (CHUNK, LANES), 1) // CHUNK
    return [(lane == h).astype(jnp.float32).astype(jnp.bfloat16) for h in range(GROUP_HEADS)]


def places():
    row = lax.broadcasted_iota(jnp.int32, (CHUNK, LANES), 0)
    col = lax.broadcasted_iota(jnp.int32, (CHUNK, LANES), 1) % CHUNK
    return row, col


def running_sum(x, upper=False):
    row = lax.broadcasted_iota(jnp.int32, (CHUNK, CHUNK), 0)
    col = lax.broadcasted_iota(jnp.int32, (CHUNK, CHUNK), 1)
    ones = (row <= col if upper else col <= row).astype(jnp.float32).astype(jnp.bfloat16)
    high, rest = halves(x)
    low = (x - high.astype(jnp.float32) - rest.astype(jnp.float32)).astype(jnp.bfloat16)
    return dot32(ones, high, NN) + dot32(ones, rest, NN) + dot32(ones, low, NN)


def scaled_forms(q, w, k, a, b):
    total = running_sum(w)
    before = total - w
    middle = total[CHUNK // 2 - 1 : CHUNK // 2]
    end = total[CHUNK - 1 :]
    ea = jnp.exp(before - middle)
    eq = jnp.exp(total - middle)
    eb = jnp.exp(middle - total)
    ee = jnp.exp(end - total)
    return (a * ea, q * eq, b * eb, k * eb, b * ee, k * ee), (ea, eq, eb, ee), (jnp.exp(middle), jnp.exp(end))


def each(fn, *columns):
    return [fn(*row) for row in zip(*columns)]


def block_ones():
    row = lax.broadcasted_iota(jnp.int32, (LANES, LANES), 0) // CHUNK
    col = lax.broadcasted_iota(jnp.int32, (LANES, LANES), 1) // CHUNK
    return (row == col).astype(jnp.float32).astype(jnp.bfloat16)


def head_sum(x, ones):
    rows = x.shape[0]
    both = dot32(jnp.concatenate(halves(x), axis=0), ones, NN)
    return both[:rows] + both[rows:]


def prepared(keys, decay_low, rate_low, live, vec, ones):
    sig = jax.nn.sigmoid(vec[0] + decay_low)
    log_decay = (-0.6065306597126334) * sig * live
    rates = jax.nn.sigmoid(vec[1] + rate_low)
    scaled = keys * vec[2]
    inverse = lax.rsqrt(head_sum(scaled * scaled, ones) + 1e-06)
    unit_keys = scaled * inverse
    factor = (1.0 + (rates - 1.0) * vec[3]) * live
    return log_decay, keys * factor, -unit_keys, unit_keys * rates * live, sig, rates, inverse, factor


def read_out(o, q, k, v, vec, ones):
    centred = o - head_sum(o, ones) * (1.0 / CHUNK)
    scale = lax.rsqrt(head_sum(centred * centred, ones) * (1.0 / CHUNK) + 0.00064)
    normed = centred * scale
    weight = head_sum(q * k * vec[4], ones)
    return normed, scale, weight, normed * vec[5] + vec[6] + weight * v


def unit_slices():
    return [
        (slice(c * CHUNK, (c + 1) * CHUNK), slice(g * LANES, (g + 1) * LANES))
        for c in range(STEP_CHUNKS)
        for g in range(2)
    ]


def unit_live(length, step):
    row = lax.broadcasted_iota(jnp.int32, (CHUNK, LANES), 0)
    start = step * (STEP_CHUNKS * CHUNK)
    live = [(row + (start + c * CHUNK) < length).astype(jnp.float32) for c in range(STEP_CHUNKS)]
    return [live[c] for c in range(STEP_CHUNKS) for g in range(2)]


def unit_vectors(vec_ref):
    vec = [[vec_ref[i : i + 1, g * LANES : (g + 1) * LANES] for i in range(7)] for g in range(2)]
    return [vec[g] for c in range(STEP_CHUNKS) for g in range(2)]


def forward_kernel(base, *refs):
    len_ref, vec_ref, start_ref, q_ref, keys_ref, v_ref, dl_ref, rl_ref, gate_ref = refs[:9]
    (
        out_ref, o_ref, t_ref, aqb_ref, aak_ref, aqk_ref, y_ref, z_ref, trt_ref, qe_ref, state_ref,
    ) = refs[-11:]

    @pl.when(pl.program_id(0) == 0)
    def _():
        state_ref[...] = start_ref[...]

    masks = head_masks()
    row, col = places()
    strict = (col < row).astype(jnp.float32)
    within = (col <= row).astype(jnp.float32)
    eye = (col == row).astype(jnp.float32)
    ones = block_ones()
    units = unit_slices()
    live = unit_live(len_ref[0], pl.program_id(0) + base)
    vec = unit_vectors(vec_ref)
    load = lambda ref: [ref[u] for u in units]
    q, keys, v = load(q_ref), load(keys_ref), load(v_ref)
    ready = each(
        lambda x, y, z, m, n: prepared(x, y, z, m, n, ones), keys, load(dl_ref), load(rl_ref), live, vec
    )
    w, k, a, b = ([x[i] for x in ready] for i in range(4))
    forms = each(scaled_forms, q, w, k, a, b)
    ah, qh, bh, kh, bt, kt = ([f[0][i] for f in forms] for i in range(6))
    emid = [f[2][0] for f in forms]
    eend = [f[2][1] for f in forms]
    aq = each(lambda x, y: halves(jnp.concatenate([x, y], axis=0)), ah, qh)
    with_b = each(lambda l, r: mul(l, spread(halves(r), masks), NT), aq, bh)
    with_k = each(lambda l, r: mul(l, spread(halves(r), masks), NT), aq, kh)
    aab = [x[:CHUNK] * strict for x in with_b]
    aqb = [halves(x[CHUNK:] * within) for x in with_b]
    aak = [halves(x[:CHUNK] * strict) for x in with_k]
    aqk = [halves(x[CHUNK:] * within) for x in with_k]
    p = [halves(x * (row // 8 == col // 8)) for x in aab]
    t = [eye + x * (row // 8 == col // 8) for x in aab]
    p2 = each(lambda x: halves(mul(x, spread(x, masks))), p)
    both = each(lambda x, y: mul(stack(x, halves(y)), spread(x, masks)), p2, t)
    p4 = [halves(x[:CHUNK]) for x in both]
    t = each(lambda x, y: x + y[CHUNK:], t, both)
    t = each(lambda x, y: x + mul(halves(x), spread(y, masks)), t, p4)
    for size in (8, 16, 32):
        corner = ((row // size) % 2 == 1) & (col // size == row // size - 1)
        ts = [halves(x) for x in t]
        n = [halves(x * corner) for x in aab]
        tn = each(lambda x, y: halves(mul(x, spread(y, masks))), ts, n)
        t = each(lambda x, y, z: x + mul(y, spread(z, masks)), t, tn, ts)
    ts = [halves(x) for x in t]
    vs = [halves(x) for x in v]
    vm = [spread(x, masks) for x in vs]
    wide = each(lambda x, y, e: mul(x, spread(halves(y * e), masks)), ts, ah, emid)
    r0 = each(mul, aak, vm)
    y0 = each(lambda x, y: mul(x, spread(halves(y), masks)), ts, r0)
    wides = [halves(x) for x in wide]
    qe = each(lambda x, e, y, z: x * e + mul(y, spread(z, masks)), qh, emid, aqb, wides)
    y0s = [halves(x) for x in y0]
    part = each(lambda x, y, z, u: mul(x, spread(y, masks)) + mul(z, u), aqb, y0s, aqk, vm)
    bts = [halves(x) for x in bt]
    diag = [eye * e for e in eend]
    tr = each(lambda x, y, d: tmul(x, y, masks) + d, bts, wides, diag)
    trt = each(lambda x, y, d: tmul(y, x, masks) + d, bts, wides, diag)
    inject = each(lambda x, y, z, u: tmul(stack(x, halves(y)), stack(z, u), masks), bts, kt, y0s, vs)
    wq = each(lambda x, y: stack(x, halves(y)), wides, qe)
    z = []
    out = []
    for c in range(STEP_CHUNKS):
        for g in range(2):
            i = c * 2 + g
            now = state_ref[g]
            nows = spread(halves(now), masks)
            state_ref[g] = mul(halves(tr[i]), nows) + inject[i]
            z.append(now)
            out.append(mul(wq[i], nows))
    o = each(lambda x, y: x[CHUNK:] + y, out, part)
    mixed = each(lambda x, y, z, m, n: read_out(x, y, z, m, n, ones)[3], o, q, k, v, vec)
    for i, u in enumerate(units):
        out_ref[u] = (mixed[i] * gate_ref[u]).astype(jnp.bfloat16)
        o_ref[u] = o[i]
        y_ref[u] = out[i][:CHUNK] + y0[i]
        t_ref[u] = t[i]
        aqb_ref[u] = with_b[i][CHUNK:] * within
        aak_ref[u] = with_k[i][:CHUNK] * strict
        aqk_ref[u] = with_k[i][CHUNK:] * within
        z_ref[u] = z[i]
        trt_ref[u] = trt[i]
        qe_ref[u] = qe[i]


def backward_kernel(base, *refs):
    (
        len_ref, vec_ref, start_ref, sums_ref, q_ref, keys_ref, v_ref, dl_ref, rl_ref, gate_ref,
        g_ref, o_ref, t_ref, aqb_ref, aak_ref, aqk_ref, y_ref, z_ref, trt_ref, qe_ref,
    ) = refs[:20]
    dq_ref, dkeys_ref, dv_ref, ddl_ref, drl_ref, dgate_ref, dvec_ref, state_ref = refs[-8:]
    step = base + pl.num_programs(0) - 1 - pl.program_id(0)

    @pl.when(pl.program_id(0) == 0)
    def _():
        state_ref[...] = start_ref[...]
        dvec_ref[...] = sums_ref[...]

    masks = head_masks()
    row, col = places()
    strict = (col < row).astype(jnp.float32)
    within = (col <= row).astype(jnp.float32)
    ones = block_ones()
    units = unit_slices()
    live = unit_live(len_ref[0], step)
    vec = unit_vectors(vec_ref)
    load = lambda ref: [ref[u] for u in units]
    q, keys, v, g = load(q_ref), load(keys_ref), load(v_ref), load(g_ref)
    ready = each(
        lambda x, y, z, m, n: prepared(x, y, z, m, n, ones), keys, load(dl_ref), load(rl_ref), live, vec
    )
    w, k, a, b, sig, rates, inverse, factor = ([x[i] for x in ready] for i in range(8))
    seen = each(lambda x, y, z, m, n: read_out(x, y, z, m, n, ones), load(o_ref), q, k, v, vec)
    normed, scale, weight, mixed = ([x[i] for x in seen] for i in range(4))
    gate = load(gate_ref)
    dgate = each(lambda x, y: x * y, g, mixed)
    dmix = each(lambda x, y: x * y, g, gate)
    dn = each(lambda x, n: x * n[5], dmix, vec)
    do = each(
        lambda x, n, r: r
        * (x - head_sum(x, ones) * (1.0 / CHUNK) - n * (head_sum(x * n, ones) * (1.0 / CHUNK))),
        dn, normed, scale,
    )
    dweight = each(lambda x, y: head_sum(x * y, ones), dmix, v)
    do = [halves(x) for x in do]
    qe, trt, t, aqb, aak, aqk, ys = (
        [halves(x) for x in load(ref)]
        for ref in (qe_ref, trt_ref, t_ref, aqb_ref, aak_ref, aqk_ref, y_ref)
    )
    z = load(z_ref)
    vs = [halves(x) for x in v]
    h = each(lambda x, y: tmul(x, y, masks), qe, do)
    dz = [None] * len(units)
    for c in reversed(range(STEP_CHUNKS)):
        for g in range(2):
            i = c * 2 + g
            now = state_ref[g]
            dz[i] = now
            state_ref[g] = mul(trt[i], spread(halves(now), masks)) + h[i]
    dzs = [spread(halves(x), masks) for x in dz]
    zs = [spread(halves(x), masks) for x in z]
    forms = each(scaled_forms, q, w, k, a, b)
    ah, qh, bh, kh, bt, kt = ([f[0][i] for f in forms] for i in range(6))
    ea, eq, eb, ee = ([f[1][i] for f in forms] for i in range(4))
    emid = [f[2][0] for f in forms]
    eend = [f[2][1] for f in forms]
    from_end = each(lambda x, y, s: mul(halves(jnp.concatenate([x, y], axis=0)), s), bt, kt, dzs)
    dy = each(lambda x, y, s: halves(tmul(x, y, masks) + s[:CHUNK]), aqb, do, from_end)
    dr = each(lambda x, y: halves(tmul(x, y, masks)), t, dy)
    ro = each(stack, dr, do)
    dv = each(lambda x, y, s, f: tmul(stack(x, y), s, masks) + f[CHUNK:], aak, aqk, ro, from_end)
    mask2 = jnp.concatenate([strict, within], axis=0)
    dab = each(lambda s, y: halves(mul(s, spread(y, masks), NT) * mask2), ro, ys)
    dak = each(lambda s, y: halves(mul(s, spread(y, masks), NT) * mask2), ro, vs)
    dst = each(lambda s, y: mul(s, y, NT), ro, zs)
    daq = each(
        lambda s, e, x, bb, y, kk: s * e + mul(x, spread(halves(bb), masks)) + mul(y, spread(halves(kk), masks)),
        dst, emid, dab, bh, dak, kh,
    )
    aq = each(lambda x, y: halves(jnp.concatenate([x, y], axis=0)), ah, qh)
    dbh = each(lambda x, y: tmul(x, y, masks), dab, aq)
    dkh = each(lambda x, y: tmul(x, y, masks), dak, aq)
    dend = each(lambda y, x, s: mul(stack(y, x), s, NT), ys, vs, dzs)
    row_of_ones = jnp.ones((8, LANES), jnp.bfloat16)
    sums = lambda x: jnp.sum(x, axis=0, keepdims=True)
    for i, u in enumerate(units):
        da = daq[i][:CHUNK] * ea[i]
        dq = daq[i][CHUNK:] * eq[i]
        dbt = dend[i][:CHUNK] * ee[i]
        dkt = dend[i][CHUNK:] * ee[i]
        db = dbh[i] * eb[i] + dbt
        dk = dkh[i] * eb[i] + dkt
        pa = da * a[i]
        diff = dq * q[i] - db * b[i] - dk * k[i] + pa
        zz = spread(halves(z[i] * dz[i]), masks)
        carry = (dot32(row_of_ones, zz[0], NT) + dot32(row_of_ones, zz[1], NT))[:1] * eend[i]
        carry = carry + sums(dbt * b[i] + dkt * k[i])
        dw = running_sum(diff, upper=True) - pa + carry
        from_bonus = dweight[i] * vec[i][4]
        dk = dk + from_bonus * q[i]
        dq_ref[u] = (dq + from_bonus * k[i]).astype(jnp.bfloat16)
        dv_ref[u] = (dv[i] + weight[i] * dmix[i]).astype(jnp.bfloat16)
        dgate_ref[u] = dgate[i].astype(jnp.bfloat16)
        unit_keys = -a[i]
        db = db * live[i]
        du = db * rates[i] - da
        dscaled = inverse[i] * (du - unit_keys * head_sum(du * unit_keys, ones))
        dkl = dk * keys[i] * live[i]
        drl = (db * unit_keys + dkl * vec[i][3]) * rates[i] * (1.0 - rates[i])
        ddl = dw * w[i] * (1.0 - sig[i])
        dkeys_ref[u] = (dk * factor[i] + dscaled * vec[i][2]).astype(jnp.bfloat16)
        ddl_ref[u] = ddl.astype(jnp.bfloat16)
        drl_ref[u] = drl.astype(jnp.bfloat16)
        parts = (
            ddl, drl, dscaled * keys[i], dkl * (rates[i] - 1.0),
            dweight[i] * q[i] * k[i], dmix[i] * normed[i], dmix[i],
        )
        lanes = u[1]
        for j, x in enumerate(parts):
            dvec_ref[j : j + 1, lanes] += sums(x)


def wkv_call(kernel, base, steps, small, arrays, outs, sums, previous, name):
    tokens, width = arrays[0].shape
    rows = CHUNK * STEP_CHUNKS
    last = base + steps - 1
    turned = kernel is backward_kernel
    spec = pl.BlockSpec((rows, width), lambda i: (last - i if turned else base + i, 0))
    state = pl.BlockSpec((2, CHUNK, LANES), lambda i: (0, 0, 0))
    whole = pl.BlockSpec((8, width), lambda i: (0, 0))
    shape = jax.ShapeDtypeStruct
    first = [pl.BlockSpec(memory_space=pltpu.SMEM), whole, state] + [whole] * sums
    held = list(previous or ())
    start = len(first) + len(arrays)
    return pl.pallas_call(
        partial(kernel, base),
        grid=(steps,),
        in_specs=first + [spec] * len(arrays) + [pl.BlockSpec(memory_space=pl.ANY)] * len(held),
        out_specs=[spec] * len(outs) + [whole] * sums + [state],
        out_shape=[shape((tokens, width), dtype) for dtype in outs]
        + [shape((8, width), jnp.float32)] * sums
        + [shape((2, CHUNK, LANES), jnp.float32)],
        input_output_aliases={start + i: i for i in range(len(held))},
        compiler_params=pltpu.CompilerParams(vmem_limit_bytes=56 << 20),
        cost_estimate=SMALL,
        name=name,
    )(*small, *arrays, *held)


def wkv_forward(base, steps, length, vec, state, arrays, previous=None):
    outs = [jnp.bfloat16] + [jnp.float32] * 9
    return wkv_call(
        forward_kernel, base, steps, (length, vec, state), arrays, outs, 0, previous, "wkv_forward"
    )


def wkv_backward(base, steps, length, vec, state, sums, arrays, previous=None):
    outs = [jnp.bfloat16] * 6
    return wkv_call(
        backward_kernel, base, steps, (length, vec, state, sums), arrays, outs, 1, previous,
        "wkv_backward",
    )


ROWS = 128


def row_norm(x):
    centred = x - jnp.mean(x, axis=-1, keepdims=True)
    scale = lax.rsqrt(jnp.mean(centred * centred, axis=-1, keepdims=True) + 1e-05)
    return centred * scale, scale


def shifted(x, edge, down):
    rows = x.shape[0]
    row = lax.broadcasted_iota(jnp.int32, x.shape, 0)
    if down:
        return jnp.where(row == 0, edge, pltpu.roll(x, 1, 0))
    return jnp.where(row == rows - 1, edge, pltpu.roll(x, rows - 1, 0))


def below(x, upper):
    lane = lax.broadcasted_iota(jnp.int32, x.shape, 1)
    keep = (lane >= DECAY_RANK) if upper else (lane < DECAY_RANK)
    return jnp.where(keep, x, jnp.zeros_like(x))


def front_kernel(
    x_ref, vec_ref, down_ref, up_ref,
    m0_ref, m1_ref, m2_ref, m3_ref, m4_ref, m5_ref,
    dl_ref, rl_ref, gate_ref, hid_ref,
    edge_ref,
):
    @pl.when(pl.program_id(0) == 0)
    def _():
        edge_ref[...] = jnp.zeros_like(edge_ref)

    unit, _ = row_norm(x_ref[...].astype(jnp.float32))
    normed = unit * vec_ref[12:13] + vec_ref[13:14]
    change = shifted(normed, edge_ref[:1], True) - normed
    edge_ref[:1] = normed[ROWS - 1 :]
    mixes = []
    for j, ref in enumerate((m0_ref, m1_ref, m2_ref, m3_ref, m4_ref, m5_ref)):
        mixes.append((normed + change * vec_ref[j : j + 1]).astype(jnp.bfloat16))
        ref[...] = mixes[j]
    first = down_ref[:, :128]
    pre_decay, pre_rate = dot32(mixes[1], first, NN), dot32(mixes[4], first, NN)
    pre_gate = dot32(mixes[5], down_ref[:, 128:], NN)
    lane = lax.broadcasted_iota(jnp.int32, pre_decay.shape, 1)
    pair = jnp.where(lane < DECAY_RANK, jnp.tanh(pre_decay), pre_rate)
    gate = jax.nn.sigmoid(pre_gate)
    hid_ref[:, :128] = pair
    hid_ref[:, 128:] = gate
    narrow_pair = pair.astype(jnp.bfloat16)
    dl_ref[...] = dot32(below(narrow_pair, False), up_ref[:, :128], NT)
    rl_ref[...] = dot32(below(narrow_pair, True), up_ref[:, :128], NT)
    gate_ref[...] = dot32(gate.astype(jnp.bfloat16), up_ref[:, 128:], NT)


def front_forward(x, vectors, down, up):
    tokens, width = x.shape
    wide = pl.BlockSpec((ROWS, width), lambda i: (i, 0))
    own = pl.BlockSpec((ROWS, OWN), lambda i: (i, 0))
    hid = pl.BlockSpec((ROWS, 256), lambda i: (i, 0))
    whole = lambda a: pl.BlockSpec(a.shape, lambda i: (0, 0))
    shape = jax.ShapeDtypeStruct
    return pl.pallas_call(
        front_kernel,
        grid=(tokens // ROWS,),
        in_specs=[wide] + [whole(a) for a in (vectors, down, up)],
        out_specs=[wide] * 6 + [own] * 3 + [hid],
        out_shape=[shape((tokens, width), jnp.bfloat16)] * 6
        + [shape((tokens, OWN), jnp.float32)] * 3
        + [shape((tokens, 256), jnp.float32)],
        scratch_shapes=[pltpu.VMEM((8, width), jnp.float32)],
        compiler_params=pltpu.CompilerParams(vmem_limit_bytes=48 << 20),
        cost_estimate=SMALL,
        name="front_forward",
    )(x, vectors, down, up)


def front_back_kernel(
    x_ref, before_ref, vec_ref, wr_ref, wk_ref, wv_ref, down_ref, up_ref,
    m1_ref, m4_ref, m5_ref, hid_ref,
    dq_ref, dk_ref, dv_ref, ddl_ref, drl_ref, dgate_ref, own_vec_ref, ffn_vec_ref,
    dx_ref, misc_ref,
    edge_ref, sums_ref,
):
    step = pl.num_programs(0) - 1 - pl.program_id(0)
    core = lax.axis_index("dp") % 2
    own_start = pl.multiple_of(core * OWN, OWN)

    @pl.when(pl.program_id(0) == 0)
    def _():
        edge_ref[...] = jnp.zeros_like(edge_ref)
        sums_ref[...] = jnp.zeros_like(sums_ref)
        misc_ref[...] = jnp.zeros_like(misc_ref)

    unit, scale = row_norm(x_ref[...].astype(jnp.float32))
    gain, offset = vec_ref[12:13], vec_ref[13:14]
    normed = unit * gain + offset
    tail, _ = row_norm(before_ref[...].astype(jnp.float32))
    edge = (tail[15:] * gain + offset) * jnp.where(step == 0, 0.0, 1.0)
    change = shifted(normed, edge, True) - normed
    ddl, drl, dgate = ddl_ref[...], drl_ref[...], dgate_ref[...]
    hid = hid_ref[...]
    pair, gate = hid[:, :128], hid[:, 128:]
    lane = lax.broadcasted_iota(jnp.int32, pair.shape, 1)
    first_up, last_up = up_ref[:, :128], up_ref[:, 128:]
    pair_grad = jnp.where(
        lane < DECAY_RANK,
        dot32(ddl, first_up, NN) * (1.0 - pair * pair),
        dot32(drl, first_up, NN),
    ).astype(jnp.bfloat16)
    gate_grad = (dot32(dgate, last_up, NN) * gate * (1.0 - gate)).astype(jnp.bfloat16)
    narrow_pair, narrow_gate = pair.astype(jnp.bfloat16), gate.astype(jnp.bfloat16)
    own_rows = pl.ds(own_start, OWN)
    misc_ref[own_rows, 256:384] += dot32(ddl, below(narrow_pair, False), TN) + dot32(
        drl, below(narrow_pair, True), TN
    )
    misc_ref[own_rows, 384:512] += dot32(dgate, narrow_gate, TN)
    decay_part, rate_part = below(pair_grad, False), below(pair_grad, True)
    misc_ref[:, :128] += dot32(m1_ref[...], decay_part, TN) + dot32(m4_ref[...], rate_part, TN)
    misc_ref[:, 128:256] += dot32(m5_ref[...], gate_grad, TN)
    first_down = down_ref[:, :128]
    grads = (
        lambda: dot32(dq_ref[...], wr_ref[...], NT),
        lambda: dot32(decay_part, first_down, NT),
        lambda: dot32(dk_ref[...], wk_ref[...], NT),
        lambda: dot32(dv_ref[...], wv_ref[...], NT),
        lambda: dot32(rate_part, first_down, NT),
        lambda: dot32(gate_grad, down_ref[:, 128:], NT),
    )
    total = jnp.zeros_like(change)
    moved = jnp.zeros_like(change)
    for j, grad in enumerate(grads):
        now = grad()
        total = total + now
        moved = moved + now * vec_ref[j : j + 1]
        sums_ref[j : j + 1] += jnp.sum(now * change, axis=0, keepdims=True)
    dnormed = total - moved + shifted(moved, edge_ref[:1], False)
    edge_ref[:1] = moved[:1]
    sums_ref[12:13] += jnp.sum(dnormed * unit, axis=0, keepdims=True)
    sums_ref[13:14] += jnp.sum(dnormed, axis=0, keepdims=True)
    dunit = dnormed * gain
    dx_ref[...] = scale * (
        dunit
        - jnp.mean(dunit, axis=-1, keepdims=True)
        - unit * jnp.mean(dunit * unit, axis=-1, keepdims=True)
    )

    @pl.when(step == 0)
    def _():
        sums_ref[6:7] = ffn_vec_ref[0:1] * 0.5
        sums_ref[14:16] = ffn_vec_ref[1:3] * 0.5
        zeros = jnp.zeros((1, OWN), jnp.float32)
        for target, source in ((7, 0), (8, 1), (9, 2), (10, 3), (11, 4), (16, 5), (17, 6)):
            mine = own_vec_ref[source : source + 1]
            sums_ref[target : target + 1] = jnp.concatenate(
                [jnp.where(core == 0, mine, zeros), jnp.where(core == 0, zeros, mine)], axis=1
            )
        for block in range(EMBED // 128):
            lanes = slice(block * 128, (block + 1) * 128)
            misc_ref[lanes, 512:640] = sums_ref[:, lanes].T


def front_backward(
    x, vectors, w_r, w_k, w_v, down, up, mixes, hid, grads, own_vec, ffn_vec
):
    tokens, width = x.shape
    steps = tokens // ROWS
    wide = pl.BlockSpec((ROWS, width), lambda i: (steps - 1 - i, 0))
    before = pl.BlockSpec(
        (16, width), lambda i: (jnp.maximum((steps - 1 - i) * (ROWS // 16) - 1, 0), 0)
    )
    own = pl.BlockSpec((ROWS, OWN), lambda i: (steps - 1 - i, 0))
    hid_spec = pl.BlockSpec((ROWS, 256), lambda i: (steps - 1 - i, 0))
    whole = lambda a: pl.BlockSpec(a.shape, lambda i: (0, 0))
    shape = jax.ShapeDtypeStruct
    return pl.pallas_call(
        front_back_kernel,
        grid=(steps,),
        in_specs=[wide, before]
        + [whole(a) for a in (vectors, w_r, w_k, w_v, down, up)]
        + [wide] * 3
        + [hid_spec]
        + [own] * 6
        + [whole(own_vec), whole(ffn_vec)],
        out_specs=[wide, pl.BlockSpec((EMBED, 640), lambda i: (0, 0))],
        out_shape=[shape((tokens, width), jnp.float32), shape((EMBED, 640), jnp.float32)],
        scratch_shapes=[
            pltpu.VMEM((8, width), jnp.float32), pltpu.VMEM((128, width), jnp.float32),
        ],
        compiler_params=pltpu.CompilerParams(vmem_limit_bytes=48 << 20),
        cost_estimate=SMALL,
        name="front_backward",
    )(x, x, vectors, w_r, w_k, w_v, down, up, *mixes, hid, *grads, own_vec, ffn_vec)


def ffn_back_kernel(
    len_ref, res_ref, before_ref, cot_ref, mine_ref, other_ref, vec_ref, wo_ref,
    grad_ref, narrow_ref, gated_ref, dvec_ref,
    edge_ref,
):
    step = pl.num_programs(0) - 1 - pl.program_id(0)

    @pl.when(pl.program_id(0) == 0)
    def _():
        edge_ref[...] = jnp.zeros_like(edge_ref)
        dvec_ref[...] = jnp.zeros_like(dvec_ref)

    gain, offset, coefficient = vec_ref[14:15], vec_ref[15:16], vec_ref[6:7]
    unit, scale = row_norm(res_ref[...])
    normed = unit * gain + offset
    tail, _ = row_norm(before_ref[...])
    edge = (tail[7:] * gain + offset) * jnp.where(step == 0, 0.0, 1.0)
    change = shifted(normed, edge, True) - normed
    grad = mine_ref[...].astype(jnp.float32) + other_ref[...].astype(jnp.float32)
    moved = grad * coefficient
    dnormed = grad - moved + shifted(moved, edge_ref[:1], False)
    edge_ref[:1] = moved[:1]
    sums = lambda x: jnp.sum(x, axis=0, keepdims=True)
    dvec_ref[0:1] += sums(grad * change)
    dvec_ref[1:2] += sums(dnormed * unit)
    dvec_ref[2:3] += sums(dnormed)
    dunit = dnormed * gain
    row = lax.broadcasted_iota(jnp.int32, grad.shape, 0) + step * ROWS
    out_grad = jnp.where(row < len_ref[0], cot_ref[...].astype(jnp.float32), 0.0)
    total = out_grad + scale * (
        dunit
        - jnp.mean(dunit, axis=-1, keepdims=True)
        - unit * jnp.mean(dunit * unit, axis=-1, keepdims=True)
    )
    grad_ref[...] = total
    small = total.astype(jnp.bfloat16)
    narrow_ref[...] = small
    gated_ref[...] = dot32(small, wo_ref[...], NT)


def ffn_backward(length, residual, cot, mine, other, vectors, w_o_rows):
    tokens, width = residual.shape
    steps = tokens // ROWS
    wide = pl.BlockSpec((ROWS, width), lambda i: (steps - 1 - i, 0))
    before = pl.BlockSpec(
        (8, width), lambda i: (jnp.maximum((steps - 1 - i) * (ROWS // 8) - 1, 0), 0)
    )
    own = pl.BlockSpec((ROWS, OWN), lambda i: (steps - 1 - i, 0))
    whole = lambda a: pl.BlockSpec(a.shape, lambda i: (0, 0))
    shape = jax.ShapeDtypeStruct
    return pl.pallas_call(
        ffn_back_kernel,
        grid=(steps,),
        in_specs=[pl.BlockSpec(memory_space=pltpu.SMEM), wide, before]
        + [wide] * 3
        + [whole(vectors), whole(w_o_rows)],
        out_specs=[wide, wide, own, pl.BlockSpec((8, width), lambda i: (0, 0))],
        out_shape=[
            shape((tokens, width), jnp.float32),
            shape((tokens, width), jnp.bfloat16),
            shape((tokens, OWN), jnp.float32),
            shape((8, width), jnp.float32),
        ],
        scratch_shapes=[pltpu.VMEM((8, width), jnp.float32)],
        compiler_params=pltpu.CompilerParams(vmem_limit_bytes=48 << 20),
        cost_estimate=SMALL,
        name="ffn_backward",
    )(length, residual, residual, cot, mine, other, vectors, w_o_rows)


def att_grad_kernel(m0_ref, m2_ref, m3_ref, dq_ref, dk_ref, dv_ref, send_a, keep_a, send_b, keep_b, whole_c):
    chip = lax.axis_index("dp") // 2
    by_x, by_y = chip % 2 == 0, (chip // 2) % 2 == 0
    dq, dk, dv = dq_ref[...], dk_ref[...], dv_ref[...]
    for z in range(4):
        rows = slice(z * 256, (z + 1) * 256)
        block = dot32(m0_ref[:, rows], dq, TN).astype(jnp.bfloat16)
        for y in range(2):
            low, high = block[y * 128 : y * 128 + 64], block[y * 128 + 64 : y * 128 + 128]
            send_a[2 * z + y] = jnp.where(by_x, high, low)
            keep_a[2 * z + y] = jnp.where(by_x, low, high)
        block = dot32(m2_ref[:, rows], dk, TN).astype(jnp.bfloat16)
        for x in range(2):
            low, high = block[x * 64 : x * 64 + 64], block[128 + x * 64 : 128 + x * 64 + 64]
            send_b[2 * z + x] = jnp.where(by_y, high, low)
            keep_b[2 * z + x] = jnp.where(by_y, low, high)
        whole_c[rows] = dot32(m3_ref[:, rows], dv, TN).astype(jnp.bfloat16)


def att_gradients(mixes, grads):
    space = pl.BlockSpec(memory_space=pltpu.VMEM)
    shape = jax.ShapeDtypeStruct
    return pl.pallas_call(
        att_grad_kernel,
        in_specs=[space] * 6,
        out_specs=[space] * 5,
        out_shape=[shape((8, 64, OWN), jnp.bfloat16)] * 4 + [shape((EMBED, OWN), jnp.bfloat16)],
        compiler_params=pltpu.CompilerParams(vmem_limit_bytes=40 << 20),
        cost_estimate=SMALL,
        name="att_gradients",
    )(*mixes, *grads)


def swap(block, mask):
    size = lax.axis_size("dp")
    return lax.ppermute(block, "dp", [(i, i ^ mask) for i in range(size)])


def bit_of(mask):
    return (lax.axis_index("dp") // mask) % 2


def in_order(mask, own, other, axis):
    lower = bit_of(mask) == 0
    return jnp.where(
        lower, jnp.concatenate([own, other], axis=axis), jnp.concatenate([other, own], axis=axis)
    )


def chip_masks():
    size = lax.axis_size("dp")
    masks = []
    while 2 << len(masks) < size:
        masks.append(2 << len(masks))
    return masks


def steps_of(kind):
    masks = chip_masks()
    near, far = [[mask] for mask in masks[:2]], masks[2:][::-1]
    single = [[mask] for mask in far]
    first = [[far[0], far[1], far[0] | far[1]]] if len(far) == 2 else single
    return [
        first + near[::-1], first + near, near + first, single + near[::-1], single + near
    ][kind]


def meet(movers, *arrays):
    held = lax.optimization_barrier(tuple(tuple(m.arrived) for m in movers) + arrays)
    for mover, arrived in zip(movers, held):
        mover.arrived = list(arrived)
    return held[len(movers) :]


class Gather:
    def __init__(self, block, kind, places=(0,)):
        self.steps = steps_of(kind)
        self.held = block[None]
        self.places = [0]
        self.arrived = []
        self.masks = []

    def merge(self):
        if self.arrived:
            self.held = jnp.concatenate([self.held] + self.arrived, axis=0)
            self.places = self.places + [p ^ (m // 2) for m in self.masks for p in self.places]
            self.arrived = []

    def step(self):
        if self.steps:
            self.merge()
            self.masks = self.steps.pop(0)
            self.arrived = [swap(self.held, mask) for mask in self.masks]
        return self

    def run(self):
        while self.steps:
            self.step()
        return self

    def split(self, kinds):
        width = self.held.shape[-1] // len(kinds)
        out = []
        for i, kind in enumerate(kinds):
            part = Gather.__new__(Gather)
            cut = slice(i * width, (i + 1) * width)
            part.steps = steps_of(kind)[len(steps_of(kind)) - len(self.steps) :]
            part.held = self.held[..., cut]
            part.arrived = [x[..., cut] for x in self.arrived]
            part.places, part.masks = self.places, self.masks
            out.append(part)
        return out


def place_kernel(places, cuts, *refs):
    sources, outs = refs[: len(places)], refs[len(places) :]
    chip = lax.axis_index("dp") // 2
    for source, (part, list_of) in zip(sources, places):
        for j, place in enumerate(list_of):
            for out, (first, rows, lanes) in zip(outs, cuts):
                start = pl.multiple_of((chip ^ place) * rows, rows)
                lane, width = lanes[part]
                at = sum(w for _, w in lanes[:part])
                out[pl.ds(start, rows), at : at + width] = source[
                    j, first : first + rows, lane : lane + width
                ]


def assemble(gathers, cuts=None):
    gathers = [g.run() for g in gathers]
    rows = gathers[0].held.shape[1]
    cuts = cuts or ((0, rows, [(0, g.held.shape[2]) for g in gathers]),)
    sources, places = [], []
    for i, g in enumerate(gathers):
        sources += [g.held] + g.arrived
        shifts = [0] + [mask // 2 for mask in g.masks]
        places += [(i, [p ^ shift for p in g.places]) for shift in shifts]
    count = lax.axis_size("dp") // 2
    if any(cut[1] % 16 for cut in cuts):
        return assemble_plain(sources, places, cuts, count)
    space = pl.BlockSpec(memory_space=pltpu.VMEM)
    return pl.pallas_call(
        partial(place_kernel, places, cuts),
        in_specs=[space] * len(sources),
        out_specs=[space] * len(cuts),
        out_shape=[
            jax.ShapeDtypeStruct((count * n, sum(w for _, w in lanes)), sources[0].dtype)
            for _, n, lanes in cuts
        ],
        compiler_params=pltpu.CompilerParams(vmem_limit_bytes=32 << 20),
        cost_estimate=SMALL,
        name="assemble",
    )(*sources)


def assemble_plain(sources, places, cuts, count):
    chip = lax.axis_index("dp") // 2
    parts = []
    for part in sorted({part for part, _ in places}):
        blocks = jnp.concatenate([x for x, (at, _) in zip(sources, places) if at == part])
        where = [p for at, list_of in places if at == part for p in list_of]
        blocks = jnp.stack([blocks[where.index(i)] for i in range(count)])
        parts.append(jnp.take(blocks, chip ^ lax.iota(jnp.int32, count), axis=0))
    return [
        jnp.concatenate(
            [x[:, first : first + n, at : at + w] for x, (at, w) in zip(parts, lanes)], axis=-1
        ).reshape(count * n, -1)
        for first, n, lanes in cuts
    ]


class Scatter:
    def __init__(self, parts, kind):
        self.steps = steps_of(kind)[::-1]
        self.axes = chip_masks()[::-1]
        shape = parts.shape[1:]
        self.sources = [parts.reshape((2,) * len(self.axes) + shape)]
        self.arrived = []

    def pick(self, mask, gone):
        out = []
        for x in self.sources:
            for place in reversed(range(len(self.axes))):
                axis = self.axes[place]
                if axis in gone:
                    which = bit_of(axis) if not mask & axis else 1 - bit_of(axis)
                    x = lax.dynamic_index_in_dim(x, which, place, keepdims=False)
            out.append(x)
        return out

    def merge(self):
        self.sources = self.sources + self.arrived
        self.arrived = []

    def step(self):
        if self.steps:
            self.merge()
            masks = self.steps.pop(0)
            gone = [axis for axis in self.axes if any(mask & axis for mask in masks)]
            sends = [
                sum(x.astype(jnp.float32) for x in self.pick(mask, gone)).astype(jnp.bfloat16)
                for mask in masks
            ]
            self.sources = self.pick(0, gone)
            self.axes = [axis for axis in self.axes if axis not in gone]
            self.sent = sends
            self.arrived = [swap(x, mask) for x, mask in zip(sends, masks)]
        return self

    def run(self):
        while self.steps:
            self.step()
        return self

    def total(self):
        self.merge()
        return sum(x.astype(jnp.float32) for x in self.sources)

    @classmethod
    def begun(cls, sent, kept, kind):
        out = cls.__new__(cls)
        out.steps = steps_of(kind)[::-1]
        masks = out.steps.pop(0)
        out.axes = [axis for axis in chip_masks()[::-1] if axis not in masks]
        out.sources = [kept.reshape((2,) * len(out.axes) + kept.shape[1:])]
        out.sent = [sent.reshape(out.sources[0].shape)]
        out.arrived = [swap(out.sent[0], masks[0])]
        return out

    @staticmethod
    def join(parts):
        out = Scatter.__new__(Scatter)
        out.steps, out.axes, out.arrived = parts[0].steps, parts[0].axes, []
        out.sources = [jnp.concatenate([part.total() for part in parts], axis=-1)]
        return out


def norm_rows(features, gain_row, offset_row):
    average = jnp.mean(features, axis=-1, keepdims=True)
    centred = features - average
    variance = jnp.mean(centred * centred, axis=-1, keepdims=True)
    return centred * lax.rsqrt(variance + 1e-05) * gain_row + offset_row


def product(operand, weight_matrix):
    return jnp.dot(operand, weight_matrix, preferred_element_type=jnp.float32)


def input_gradient_rows(upstream_gradient, weight_matrix):
    return lax.dot_general(
        upstream_gradient,
        weight_matrix,
        (((1,), (1,)), ((), ())),
        preferred_element_type=jnp.float32,
    )


def weight_gradient(operand, upstream_gradient):
    return lax.dot_general(
        operand, upstream_gradient, (((0,), (0,)), ((), ())), preferred_element_type=jnp.float32
    )


def earlier(rows):
    return jnp.concatenate([jnp.zeros_like(rows[:1]), rows[:-1]], axis=0)


def ffn_mix(residual, vectors):
    second = norm_rows(residual, vectors[14], vectors[15])
    return second + (earlier(second) - second) * vectors[6]


def narrow(x):
    return x.astype(jnp.bfloat16)


def local(
    inputs,
    lengths,
    attention_projections,
    channel_key_weight,
    channel_value_weight,
    lowrank_down_weight,
    lowrank_up_weight,
    per_feature_parameters,
    cotangent,
):
    devices = lax.axis_size("dp")
    chips = devices // 2
    device = lax.axis_index("dp")
    chip, core = device // 2, device % 2
    row_count = inputs.shape[0]
    slots = 2 * row_count
    share = EMBED // devices
    pair_share = 2 * share
    units = channel_value_weight.shape[0]
    half_units = chips * units

    def own_cut(x, which):
        return lax.dynamic_slice_in_dim(x, which * OWN, OWN, x.ndim - 1)

    def own_rows(x, which):
        return lax.dynamic_slice_in_dim(x, which * row_count, row_count, 0)

    pair_rows = in_order(
        1,
        own_cut(attention_projections, core),
        swap(own_cut(attention_projections, 1 - core), 1),
        1,
    )
    lora = jnp.concatenate(
        [
            lowrank_down_weight,
            lowrank_up_weight.T,
            jnp.pad(per_feature_parameters.T, ((0, 0), (0, 128 - 18))),
        ],
        axis=1,
    )
    lora = lax.all_gather(lora, "dp", axis=0, tiled=True)
    down, up_t = lora[:, :256], lax.dynamic_slice_in_dim(lora[:, 256:512], core * OWN, OWN, 0)
    vectors = lora[:, 512:530].T.astype(jnp.float32)
    own_vectors = own_cut(vectors, core)
    used = jnp.concatenate([own_vectors[7:12], own_vectors[16:18], own_vectors[:1]], axis=0)
    first = Gather(pair_rows[:3].reshape(3 * pair_share, OWN), 0).step()
    value_late = Gather(channel_value_weight[:, OWN:], 2).step().step()
    key_cut = channel_key_weight.reshape(share, chips, 2, units)

    def key_columns(which):
        return lax.dynamic_index_in_dim(key_cut, which, 2, keepdims=False).reshape(share, half_units)

    half = half_units // 2
    quarter = OWN // 2
    key_rows = in_order(1, key_columns(core), swap(key_columns(1 - core), 1), 0)
    key_rows = jnp.concatenate(
        [pair_rows[3, :, :quarter], key_rows[:, :half], pair_rows[3, :, quarter:], key_rows[:, half:]],
        axis=1,
    )
    (key_rows,) = meet([first, value_late], key_rows)
    first = first.split((0, 1))
    for part in first:
        part.step()
    key_part = Gather(key_rows, 3).step()
    tokens = in_order(1, inputs, swap(inputs, 1), 0)
    cot = in_order(1, cotangent, swap(cotangent, 1), 0)
    tokens, cot = meet(first + [key_part], tokens, cot)
    for part in first:
        part.step()
    key_part.step()
    length = lax.dynamic_index_in_dim(lengths, chip, 0)
    live = (lax.iota(jnp.int32, slots) < length)[:, None]

    *mixes, decay_low, rate_low, gate_rows, hid = front_forward(tokens, vectors, down, up_t)
    mixes = meet(first + [key_part], *mixes)
    key_parts = key_part.split((3, 4))
    for part in key_parts:
        part.step()
    w_r, w_k, w_v = assemble(
        first, [(i * pair_share, pair_share, [(0, quarter)] * 2) for i in range(3)]
    )
    queries = product(mixes[0], w_r)
    keys = product(mixes[2], w_k)
    values = product(mixes[3], w_v)
    terms = [queries, keys, values, decay_low, rate_low, gate_rows]
    blocks = slots // (CHUNK * STEP_CHUNKS)
    early = blocks // 2
    zero_state = jnp.zeros((2, CHUNK, LANES), jnp.float32)
    *before, state = wkv_forward(0, early, length, used, zero_state, terms)
    state, value_block = meet(key_parts, state, channel_value_weight[:, :OWN])
    for part in key_parts:
        part.step()
    value_part = Gather(value_block, 0).step()
    value_late.step()
    gated, *saved, _ = wkv_forward(early, blocks - early, length, used, state, terms, before)
    gated_all = in_order(1, gated, swap(gated, 1), 1)
    gated_all, cot, tokens = meet(key_parts + [value_part], gated_all, cot, tokens)
    value_parts = value_part.split((0, 1))
    for part in value_parts:
        part.step()
    key_weight, w_o_own = assemble(
        key_parts,
        ((0, pair_share, [(quarter, half)] * 2), (0, pair_share, [(0, quarter)] * 2)),
    )
    w_o = in_order(1, w_o_own, swap(w_o_own, 1), 1)
    residual = tokens.astype(jnp.float32) + product(gated_all, w_o)
    ffn_in = narrow(ffn_mix(residual, vectors))
    positive = jax.nn.relu(product(ffn_in, key_weight))
    hidden = narrow(jnp.square(positive))
    positive, hidden = meet(value_parts, positive, hidden)
    for part in value_parts:
        part.step()
    out_narrow = jnp.where(live, cot, jnp.zeros_like(cot))
    value_cuts = ((0, quarter), (quarter, OWN), (OWN, EMBED))
    value_grads = [
        narrow(weight_gradient(hidden, out_narrow[:, lo:hi])).reshape(chips, units, hi - lo)
        for lo, hi in value_cuts
    ]
    hidden, positive, out_narrow, *value_grads = meet(
        value_parts + [value_late], hidden, positive, out_narrow, *value_grads
    )
    (value_weight,) = assemble(value_parts + [value_late])

    value_scatter = [Scatter(x, kind).step() for kind, x in enumerate(value_grads)]
    pre_narrow = narrow(2.0 * positive * input_gradient_rows(out_narrow, value_weight))
    ffn_in_grad = narrow(input_gradient_rows(pre_narrow, key_weight))
    other_grad = swap(ffn_in_grad, 1)
    grad_key = narrow(weight_gradient(ffn_in, pre_narrow)).reshape(chips, pair_share, half_units)
    ffn_in_grad, other_grad, grad_key, hidden = meet(
        [], ffn_in_grad, other_grad, grad_key, hidden
    )
    key_scatter = [
        Scatter(grad_key[:, :, i * half : (i + 1) * half], i).step() for i in range(2)
    ]
    residual_grad, attended_grad, gated_grad, ffn_vec = ffn_backward(
        length, residual, cot, ffn_in_grad, other_grad, vectors,
        lax.dynamic_slice_in_dim(w_o, core * OWN, OWN, 0),
    )
    grad_o = narrow(weight_gradient(gated_all, own_cut(attended_grad, core)))
    gated_grad, grad_o, *_ = meet(
        [], gated_grad, grad_o, *[x for m in key_scatter for x in m.sent]
    )
    o_scatter = Scatter(grad_o.reshape(chips, pair_share, OWN), 2)
    terms = [*terms, gated_grad, *saved]
    zero_sums = jnp.zeros((8, OWN), jnp.float32)
    *before, sums, state = wkv_backward(
        early, blocks - early, length, used, zero_state, zero_sums, terms
    )
    state, sums = meet(value_scatter[:2] + key_scatter, state, sums)
    for part in value_scatter[:2] + key_scatter:
        part.step()
    *low_grads, own_vec, _ = wkv_backward(0, early, length, used, state, sums, terms, before)
    *low_grads, own_vec = meet(value_scatter + key_scatter, *low_grads, own_vec)
    if pair_share == 64:
        sent_a, kept_a, sent_b, kept_b, grad_v = att_gradients(
            (mixes[0], mixes[2], mixes[3]), low_grads[:3]
        )
        att_scatter = [
            Scatter.begun(sent_a, kept_a, 0),
            Scatter.begun(sent_b, kept_b, 1),
            Scatter(grad_v.reshape(chips, pair_share, OWN), 2).step(),
        ]
    else:
        att_scatter = [
            Scatter(narrow(weight_gradient(mixes[m], g)).reshape(chips, pair_share, OWN), kind).step()
            for kind, (m, g) in enumerate(zip((0, 2, 3), low_grads))
        ]
    value_late_scatter = value_scatter[2].step()
    value_scatter = Scatter.join(value_scatter[:2]).step()
    o_scatter.step()
    key_scatter = Scatter.join(key_scatter).step()
    own_vec, *_ = meet([], own_vec, *[x for m in att_scatter for x in m.sent])
    token_part, misc_grad = front_backward(
        tokens, vectors, w_r, w_k, w_v, down, up_t, (mixes[1], mixes[4], mixes[5]), hid,
        low_grads, own_vec, ffn_vec,
    )
    token_part, misc_grad = meet(att_scatter + [value_late_scatter], token_part, misc_grad)
    for part in att_scatter:
        part.step()
    value_late_scatter.step()
    misc_grad = misc_grad.reshape(chips, 2, share, 640)
    misc_mine = lax.dynamic_index_in_dim(misc_grad, core, 1, keepdims=False)
    misc_other = narrow(lax.dynamic_index_in_dim(misc_grad, 1 - core, 1, keepdims=False))
    misc_scatter = Scatter(misc_mine + swap(misc_other, 1).astype(jnp.float32), 0).step()
    ffn_part = product(hidden, value_weight)
    ffn_out = own_rows(ffn_part, core) + swap(own_rows(ffn_part, 1 - core), 1)
    output = narrow(jnp.where(own_rows(live, core), own_rows(residual, core) + ffn_out, 0.0))
    input_gradient = (
        own_rows(residual_grad, core)
        + own_rows(token_part, core)
        + swap(own_rows(token_part, 1 - core), 1)
    )
    meet(att_scatter + [o_scatter, misc_scatter, value_scatter])
    v_scatter = att_scatter[2].step()
    att_scatter = Scatter.join(att_scatter[:2]).step()
    misc_scatter.step()
    o_scatter.step()
    meet([misc_scatter, o_scatter, key_scatter])
    misc_scatter.step()
    o_scatter.step()
    value_sum = jnp.concatenate(
        [value_scatter.run().total(), value_late_scatter.run().total()], axis=1
    )
    sums = [m.run().total() for m in (att_scatter, v_scatter, o_scatter, key_scatter)]
    misc_sum = misc_scatter.run().total()
    pair_sum = jnp.concatenate(sums, axis=1).reshape(2, share, -1)
    mine = lax.dynamic_index_in_dim(pair_sum, core, 0, keepdims=False)
    theirs = swap(lax.dynamic_index_in_dim(pair_sum, 1 - core, 0, keepdims=False), 1)
    shard_mixer = jnp.stack(
        [
            in_order(1, mine[:, i * OWN : (i + 1) * OWN], theirs[:, i * OWN : (i + 1) * OWN], 1)
            for i in range(4)
        ]
    )
    shard_key = in_order(
        1,
        mine[:, 4 * OWN :].reshape(share, chips, 1, units),
        theirs[:, 4 * OWN :].reshape(share, chips, 1, units),
        2,
    ).reshape(share, 2 * half_units)
    return (
        output,
        input_gradient,
        shard_mixer,
        shard_key,
        value_sum,
        misc_sum[:, :256],
        misc_sum[:, 256:512].T,
        misc_sum[:, 512:530].T,
    )


def solution(mesh):
    in_specs = (
        P("dp", None),
        P(),
        P(None, "dp", None),
        P("dp", None),
        P("dp", None),
        P("dp", None),
        P(None, "dp"),
        P(None, "dp"),
        P("dp", None),
    )
    out_specs = (
        P("dp", None),
        P("dp", None),
        P(None, "dp", None),
        P("dp", None),
        P("dp", None),
        P("dp", None),
        P(None, "dp"),
        P(None, "dp"),
    )
    return jax.shard_map(local, mesh=mesh, in_specs=in_specs, out_specs=out_specs, check_vma=False)
```

```python
from functools import partial

import jax
import jax.numpy as jnp
from jax import lax
from jax.experimental import pallas as pl
from jax.experimental.pallas import tpu as pltpu
from jax.sharding import PartitionSpec as P

HEADS = 16
HEAD_SIZE = 64
DECAY_RANK = 64
RATE_RANK = 64
EMBED = 1024
OWN = EMBED // 2
PRECISE = lax.Precision.HIGHEST


CHUNK = 64
LANES = 256
GROUP_HEADS = 4
STEP_CHUNKS = 2
SMALL = pl.CostEstimate(flops=1, bytes_accessed=1, transcendentals=0)

NN = (((1,), (0,)), ((), ()))
NT = (((1,), (1,)), ((), ()))
TN = (((0,), (0,)), ((), ()))


def halves(x):
    high = x.astype(jnp.bfloat16)
    return high, (x - high.astype(jnp.float32)).astype(jnp.bfloat16)


def dot32(a, b, dims):
    return lax.dot_general(a, b, dims, preferred_element_type=jnp.float32)


def mul(left, right, dims=NN):
    rows = left[0].shape[0]
    both = dot32(jnp.concatenate(left, axis=0), right[0], dims)
    return both[:rows] + both[rows:] + dot32(left[0], right[1], dims)


def tmul(left, right, masks):
    full = (
        dot32(left[0], right[0], TN) + dot32(left[1], right[0], TN) + dot32(left[0], right[1], TN)
    )
    return sum(full[h * CHUNK : (h + 1) * CHUNK] * masks[h][:1].astype(jnp.float32) for h in range(GROUP_HEADS))


def spread(pair, masks):
    return tuple(
        jnp.concatenate([part * masks[h] for h in range(GROUP_HEADS)], axis=0) for part in pair
    )


def stack(first, second):
    return tuple(jnp.concatenate([x, y], axis=0) for x, y in zip(first, second))


def head_masks():
    lane = lax.broadcasted_iota(jnp.int32, (CHUNK, LANES), 1) // CHUNK
    return [(lane == h).astype(jnp.float32).astype(jnp.bfloat16) for h in range(GROUP_HEADS)]


def places():
    row = lax.broadcasted_iota(jnp.int32, (CHUNK, LANES), 0)
    col = lax.broadcasted_iota(jnp.int32, (CHUNK, LANES), 1) % CHUNK
    return row, col


def running_sum(x, upper=False):
    row = lax.broadcasted_iota(jnp.int32, (CHUNK, CHUNK), 0)
    col = lax.broadcasted_iota(jnp.int32, (CHUNK, CHUNK), 1)
    ones = (row <= col if upper else col <= row).astype(jnp.float32).astype(jnp.bfloat16)
    high, rest = halves(x)
    low = (x - high.astype(jnp.float32) - rest.astype(jnp.float32)).astype(jnp.bfloat16)
    return dot32(ones, high, NN) + dot32(ones, rest, NN) + dot32(ones, low, NN)


def scaled_forms(q, w, k, a, b):
    total = running_sum(w)
    before = total - w
    middle = total[CHUNK // 2 - 1 : CHUNK // 2]
    end = total[CHUNK - 1 :]
    ea = jnp.exp(before - middle)
    eq = jnp.exp(total - middle)
    eb = jnp.exp(middle - total)
    ee = jnp.exp(end - total)
    return (a * ea, q * eq, b * eb, k * eb, b * ee, k * ee), (ea, eq, eb, ee), (jnp.exp(middle), jnp.exp(end))


def each(fn, *columns):
    return [fn(*row) for row in zip(*columns)]


def block_ones():
    row = lax.broadcasted_iota(jnp.int32, (LANES, LANES), 0) // CHUNK
    col = lax.broadcasted_iota(jnp.int32, (LANES, LANES), 1) // CHUNK
    return (row == col).astype(jnp.float32).astype(jnp.bfloat16)


def head_sum(x, ones):
    rows = x.shape[0]
    both = dot32(jnp.concatenate(halves(x), axis=0), ones, NN)
    return both[:rows] + both[rows:]


def prepared(keys, decay_low, rate_low, live, vec, ones):
    sig = jax.nn.sigmoid(vec[0] + decay_low)
    log_decay = (-0.6065306597126334) * sig * live
    rates = jax.nn.sigmoid(vec[1] + rate_low)
    scaled = keys * vec[2]
    inverse = lax.rsqrt(head_sum(scaled * scaled, ones) + 1e-06)
    unit_keys = scaled * inverse
    factor = (1.0 + (rates - 1.0) * vec[3]) * live
    return log_decay, keys * factor, -unit_keys, unit_keys * rates * live, sig, rates, inverse, factor


def read_out(o, q, k, v, vec, ones):
    centred = o - head_sum(o, ones) * (1.0 / CHUNK)
    scale = lax.rsqrt(head_sum(centred * centred, ones) * (1.0 / CHUNK) + 0.00064)
    normed = centred * scale
    weight = head_sum(q * k * vec[4], ones)
    return normed, scale, weight, normed * vec[5] + vec[6] + weight * v


def unit_slices():
    return [
        (slice(c * CHUNK, (c + 1) * CHUNK), slice(g * LANES, (g + 1) * LANES))
        for c in range(STEP_CHUNKS)
        for g in range(2)
    ]


def unit_live(length, step):
    row = lax.broadcasted_iota(jnp.int32, (CHUNK, LANES), 0)
    start = step * (STEP_CHUNKS * CHUNK)
    live = [(row + (start + c * CHUNK) < length).astype(jnp.float32) for c in range(STEP_CHUNKS)]
    return [live[c] for c in range(STEP_CHUNKS) for g in range(2)]


def unit_vectors(vec_ref):
    vec = [[vec_ref[i : i + 1, g * LANES : (g + 1) * LANES] for i in range(7)] for g in range(2)]
    return [vec[g] for c in range(STEP_CHUNKS) for g in range(2)]


def forward_kernel(base, *refs):
    len_ref, vec_ref, start_ref, q_ref, keys_ref, v_ref, dl_ref, rl_ref, gate_ref = refs[:9]
    (
        out_ref, o_ref, t_ref, aqb_ref, aak_ref, aqk_ref, y_ref, z_ref, trt_ref, qe_ref, state_ref,
    ) = refs[-11:]

    @pl.when(pl.program_id(0) == 0)
    def _():
        state_ref[...] = start_ref[...]

    masks = head_masks()
    row, col = places()
    strict = (col < row).astype(jnp.float32)
    within = (col <= row).astype(jnp.float32)
    eye = (col == row).astype(jnp.float32)
    ones = block_ones()
    units = unit_slices()
    live = unit_live(len_ref[0], pl.program_id(0) + base)
    vec = unit_vectors(vec_ref)
    load = lambda ref: [ref[u] for u in units]
    q, keys, v = load(q_ref), load(keys_ref), load(v_ref)
    ready = each(
        lambda x, y, z, m, n: prepared(x, y, z, m, n, ones), keys, load(dl_ref), load(rl_ref), live, vec
    )
    w, k, a, b = ([x[i] for x in ready] for i in range(4))
    forms = each(scaled_forms, q, w, k, a, b)
    ah, qh, bh, kh, bt, kt = ([f[0][i] for f in forms] for i in range(6))
    emid = [f[2][0] for f in forms]
    eend = [f[2][1] for f in forms]
    aq = each(lambda x, y: halves(jnp.concatenate([x, y], axis=0)), ah, qh)
    with_b = each(lambda l, r: mul(l, spread(halves(r), masks), NT), aq, bh)
    with_k = each(lambda l, r: mul(l, spread(halves(r), masks), NT), aq, kh)
    aab = [x[:CHUNK] * strict for x in with_b]
    aqb = [halves(x[CHUNK:] * within) for x in with_b]
    aak = [halves(x[:CHUNK] * strict) for x in with_k]
    aqk = [halves(x[CHUNK:] * within) for x in with_k]
    p = [halves(x * (row // 8 == col // 8)) for x in aab]
    t = [eye + x * (row // 8 == col // 8) for x in aab]
    p2 = each(lambda x: halves(mul(x, spread(x, masks))), p)
    both = each(lambda x, y: mul(stack(x, halves(y)), spread(x, masks)), p2, t)
    p4 = [halves(x[:CHUNK]) for x in both]
    t = each(lambda x, y: x + y[CHUNK:], t, both)
    t = each(lambda x, y: x + mul(halves(x), spread(y, masks)), t, p4)
    for size in (8, 16, 32):
        corner = ((row // size) % 2 == 1) & (col // size == row // size - 1)
        ts = [halves(x) for x in t]
        n = [halves(x * corner) for x in aab]
        tn = each(lambda x, y: halves(mul(x, spread(y, masks))), ts, n)
        t = each(lambda x, y, z: x + mul(y, spread(z, masks)), t, tn, ts)
    ts = [halves(x) for x in t]
    vs = [halves(x) for x in v]
    vm = [spread(x, masks) for x in vs]
    wide = each(lambda x, y, e: mul(x, spread(halves(y * e), masks)), ts, ah, emid)
    r0 = each(mul, aak, vm)
    y0 = each(lambda x, y: mul(x, spread(halves(y), masks)), ts, r0)
    wides = [halves(x) for x in wide]
    qe = each(lambda x, e, y, z: x * e + mul(y, spread(z, masks)), qh, emid, aqb, wides)
    y0s = [halves(x) for x in y0]
    part = each(lambda x, y, z, u: mul(x, spread(y, masks)) + mul(z, u), aqb, y0s, aqk, vm)
    bts = [halves(x) for x in bt]
    diag = [eye * e for e in eend]
    tr = each(lambda x, y, d: tmul(x, y, masks) + d, bts, wides, diag)
    trt = each(lambda x, y, d: tmul(y, x, masks) + d, bts, wides, diag)
    inject = each(lambda x, y, z, u: tmul(stack(x, halves(y)), stack(z, u), masks), bts, kt, y0s, vs)
    wq = each(lambda x, y: stack(x, halves(y)), wides, qe)
    z = []
    out = []
    for c in range(STEP_CHUNKS):
        for g in range(2):
            i = c * 2 + g
            now = state_ref[g]
            nows = spread(halves(now), masks)
            state_ref[g] = mul(halves(tr[i]), nows) + inject[i]
            z.append(now)
            out.append(mul(wq[i], nows))
    o = each(lambda x, y: x[CHUNK:] + y, out, part)
    mixed = each(lambda x, y, z, m, n: read_out(x, y, z, m, n, ones)[3], o, q, k, v, vec)
    for i, u in enumerate(units):
        out_ref[u] = (mixed[i] * gate_ref[u]).astype(jnp.bfloat16)
        o_ref[u] = o[i]
        y_ref[u] = out[i][:CHUNK] + y0[i]
        t_ref[u] = t[i]
        aqb_ref[u] = with_b[i][CHUNK:] * within
        aak_ref[u] = with_k[i][:CHUNK] * strict
        aqk_ref[u] = with_k[i][CHUNK:] * within
        z_ref[u] = z[i]
        trt_ref[u] = trt[i]
        qe_ref[u] = qe[i]


def backward_kernel(base, *refs):
    (
        len_ref, vec_ref, start_ref, sums_ref, q_ref, keys_ref, v_ref, dl_ref, rl_ref, gate_ref,
        g_ref, o_ref, t_ref, aqb_ref, aak_ref, aqk_ref, y_ref, z_ref, trt_ref, qe_ref,
    ) = refs[:20]
    dq_ref, dkeys_ref, dv_ref, ddl_ref, drl_ref, dgate_ref, dvec_ref, state_ref = refs[-8:]
    step = base + pl.num_programs(0) - 1 - pl.program_id(0)

    @pl.when(pl.program_id(0) == 0)
    def _():
        state_ref[...] = start_ref[...]
        dvec_ref[...] = sums_ref[...]

    masks = head_masks()
    row, col = places()
    strict = (col < row).astype(jnp.float32)
    within = (col <= row).astype(jnp.float32)
    ones = block_ones()
    units = unit_slices()
    live = unit_live(len_ref[0], step)
    vec = unit_vectors(vec_ref)
    load = lambda ref: [ref[u] for u in units]
    q, keys, v, g = load(q_ref), load(keys_ref), load(v_ref), load(g_ref)
    ready = each(
        lambda x, y, z, m, n: prepared(x, y, z, m, n, ones), keys, load(dl_ref), load(rl_ref), live, vec
    )
    w, k, a, b, sig, rates, inverse, factor = ([x[i] for x in ready] for i in range(8))
    seen = each(lambda x, y, z, m, n: read_out(x, y, z, m, n, ones), load(o_ref), q, k, v, vec)
    normed, scale, weight, mixed = ([x[i] for x in seen] for i in range(4))
    gate = load(gate_ref)
    dgate = each(lambda x, y: x * y, g, mixed)
    dmix = each(lambda x, y: x * y, g, gate)
    dn = each(lambda x, n: x * n[5], dmix, vec)
    do = each(
        lambda x, n, r: r
        * (x - head_sum(x, ones) * (1.0 / CHUNK) - n * (head_sum(x * n, ones) * (1.0 / CHUNK))),
        dn, normed, scale,
    )
    dweight = each(lambda x, y: head_sum(x * y, ones), dmix, v)
    do = [halves(x) for x in do]
    qe, trt, t, aqb, aak, aqk, ys = (
        [halves(x) for x in load(ref)]
        for ref in (qe_ref, trt_ref, t_ref, aqb_ref, aak_ref, aqk_ref, y_ref)
    )
    z = load(z_ref)
    vs = [halves(x) for x in v]
    h = each(lambda x, y: tmul(x, y, masks), qe, do)
    dz = [None] * len(units)
    for c in reversed(range(STEP_CHUNKS)):
        for g in range(2):
            i = c * 2 + g
            now = state_ref[g]
            dz[i] = now
            state_ref[g] = mul(trt[i], spread(halves(now), masks)) + h[i]
    dzs = [spread(halves(x), masks) for x in dz]
    zs = [spread(halves(x), masks) for x in z]
    forms = each(scaled_forms, q, w, k, a, b)
    ah, qh, bh, kh, bt, kt = ([f[0][i] for f in forms] for i in range(6))
    ea, eq, eb, ee = ([f[1][i] for f in forms] for i in range(4))
    emid = [f[2][0] for f in forms]
    eend = [f[2][1] for f in forms]
    from_end = each(lambda x, y, s: mul(halves(jnp.concatenate([x, y], axis=0)), s), bt, kt, dzs)
    dy = each(lambda x, y, s: halves(tmul(x, y, masks) + s[:CHUNK]), aqb, do, from_end)
    dr = each(lambda x, y: halves(tmul(x, y, masks)), t, dy)
    ro = each(stack, dr, do)
    dv = each(lambda x, y, s, f: tmul(stack(x, y), s, masks) + f[CHUNK:], aak, aqk, ro, from_end)
    mask2 = jnp.concatenate([strict, within], axis=0)
    dab = each(lambda s, y: halves(mul(s, spread(y, masks), NT) * mask2), ro, ys)
    dak = each(lambda s, y: halves(mul(s, spread(y, masks), NT) * mask2), ro, vs)
    dst = each(lambda s, y: mul(s, y, NT), ro, zs)
    daq = each(
        lambda s, e, x, bb, y, kk: s * e + mul(x, spread(halves(bb), masks)) + mul(y, spread(halves(kk), masks)),
        dst, emid, dab, bh, dak, kh,
    )
    aq = each(lambda x, y: halves(jnp.concatenate([x, y], axis=0)), ah, qh)
    dbh = each(lambda x, y: tmul(x, y, masks), dab, aq)
    dkh = each(lambda x, y: tmul(x, y, masks), dak, aq)
    dend = each(lambda y, x, s: mul(stack(y, x), s, NT), ys, vs, dzs)
    row_of_ones = jnp.ones((8, LANES), jnp.bfloat16)
    sums = lambda x: jnp.sum(x, axis=0, keepdims=True)
    for i, u in enumerate(units):
        da = daq[i][:CHUNK] * ea[i]
        dq = daq[i][CHUNK:] * eq[i]
        dbt = dend[i][:CHUNK] * ee[i]
        dkt = dend[i][CHUNK:] * ee[i]
        db = dbh[i] * eb[i] + dbt
        dk = dkh[i] * eb[i] + dkt
        pa = da * a[i]
        diff = dq * q[i] - db * b[i] - dk * k[i] + pa
        zz = spread(halves(z[i] * dz[i]), masks)
        carry = (dot32(row_of_ones, zz[0], NT) + dot32(row_of_ones, zz[1], NT))[:1] * eend[i]
        carry = carry + sums(dbt * b[i] + dkt * k[i])
        dw = running_sum(diff, upper=True) - pa + carry
        from_bonus = dweight[i] * vec[i][4]
        dk = dk + from_bonus * q[i]
        dq_ref[u] = (dq + from_bonus * k[i]).astype(jnp.bfloat16)
        dv_ref[u] = (dv[i] + weight[i] * dmix[i]).astype(jnp.bfloat16)
        dgate_ref[u] = dgate[i].astype(jnp.bfloat16)
        unit_keys = -a[i]
        db = db * live[i]
        du = db * rates[i] - da
        dscaled = inverse[i] * (du - unit_keys * head_sum(du * unit_keys, ones))
        dkl = dk * keys[i] * live[i]
        drl = (db * unit_keys + dkl * vec[i][3]) * rates[i] * (1.0 - rates[i])
        ddl = dw * w[i] * (1.0 - sig[i])
        dkeys_ref[u] = (dk * factor[i] + dscaled * vec[i][2]).astype(jnp.bfloat16)
        ddl_ref[u] = ddl.astype(jnp.bfloat16)
        drl_ref[u] = drl.astype(jnp.bfloat16)
        parts = (
            ddl, drl, dscaled * keys[i], dkl * (rates[i] - 1.0),
            dweight[i] * q[i] * k[i], dmix[i] * normed[i], dmix[i],
        )
        lanes = u[1]
        for j, x in enumerate(parts):
            dvec_ref[j : j + 1, lanes] += sums(x)


def wkv_call(kernel, base, steps, small, arrays, outs, sums, previous, name):
    tokens, width = arrays[0].shape
    rows = CHUNK * STEP_CHUNKS
    last = base + steps - 1
    turned = kernel is backward_kernel
    spec = pl.BlockSpec((rows, width), lambda i: (last - i if turned else base + i, 0))
    state = pl.BlockSpec((2, CHUNK, LANES), lambda i: (0, 0, 0))
    whole = pl.BlockSpec((8, width), lambda i: (0, 0))
    shape = jax.ShapeDtypeStruct
    first = [pl.BlockSpec(memory_space=pltpu.SMEM), whole, state] + [whole] * sums
    held = list(previous or ())
    start = len(first) + len(arrays)
    return pl.pallas_call(
        partial(kernel, base),
        grid=(steps,),
        in_specs=first + [spec] * len(arrays) + [pl.BlockSpec(memory_space=pl.ANY)] * len(held),
        out_specs=[spec] * len(outs) + [whole] * sums + [state],
        out_shape=[shape((tokens, width), dtype) for dtype in outs]
        + [shape((8, width), jnp.float32)] * sums
        + [shape((2, CHUNK, LANES), jnp.float32)],
        input_output_aliases={start + i: i for i in range(len(held))},
        compiler_params=pltpu.CompilerParams(vmem_limit_bytes=56 << 20),
        cost_estimate=SMALL,
        name=name,
    )(*small, *arrays, *held)


def wkv_forward(base, steps, length, vec, state, arrays, previous=None):
    outs = [jnp.bfloat16] + [jnp.float32] * 9
    return wkv_call(
        forward_kernel, base, steps, (length, vec, state), arrays, outs, 0, previous, "wkv_forward"
    )


def wkv_backward(base, steps, length, vec, state, sums, arrays, previous=None):
    outs = [jnp.bfloat16] * 6
    return wkv_call(
        backward_kernel, base, steps, (length, vec, state, sums), arrays, outs, 1, previous,
        "wkv_backward",
    )


ROWS = 128


def row_norm(x):
    centred = x - jnp.mean(x, axis=-1, keepdims=True)
    scale = lax.rsqrt(jnp.mean(centred * centred, axis=-1, keepdims=True) + 1e-05)
    return centred * scale, scale


def shifted(x, edge, down):
    rows = x.shape[0]
    row = lax.broadcasted_iota(jnp.int32, x.shape, 0)
    if down:
        return jnp.where(row == 0, edge, pltpu.roll(x, 1, 0))
    return jnp.where(row == rows - 1, edge, pltpu.roll(x, rows - 1, 0))


def below(x, upper):
    lane = lax.broadcasted_iota(jnp.int32, x.shape, 1)
    keep = (lane >= DECAY_RANK) if upper else (lane < DECAY_RANK)
    return jnp.where(keep, x, jnp.zeros_like(x))


def front_kernel(
    x_ref, vec_ref, wr_ref, wk_ref, wv_ref, down_ref, up_ref,
    m0_ref, m1_ref, m2_ref, m3_ref, m4_ref, m5_ref,
    q_ref, k_ref, v_ref, dl_ref, rl_ref, gate_ref, hid_ref,
    edge_ref,
):
    @pl.when(pl.program_id(0) == 0)
    def _():
        edge_ref[...] = jnp.zeros_like(edge_ref)

    unit, _ = row_norm(x_ref[...].astype(jnp.float32))
    normed = unit * vec_ref[12:13] + vec_ref[13:14]
    change = shifted(normed, edge_ref[:1], True) - normed
    edge_ref[:1] = normed[ROWS - 1 :]
    mixes = []
    for j, ref in enumerate((m0_ref, m1_ref, m2_ref, m3_ref, m4_ref, m5_ref)):
        mixes.append((normed + change * vec_ref[j : j + 1]).astype(jnp.bfloat16))
        ref[...] = mixes[j]
    q_ref[...] = dot32(mixes[0], wr_ref[...], NN)
    k_ref[...] = dot32(mixes[2], wk_ref[...], NN)
    v_ref[...] = dot32(mixes[3], wv_ref[...], NN)
    first = down_ref[:, :128]
    pre_decay, pre_rate = dot32(mixes[1], first, NN), dot32(mixes[4], first, NN)
    pre_gate = dot32(mixes[5], down_ref[:, 128:], NN)
    lane = lax.broadcasted_iota(jnp.int32, pre_decay.shape, 1)
    pair = jnp.where(lane < DECAY_RANK, jnp.tanh(pre_decay), pre_rate)
    gate = jax.nn.sigmoid(pre_gate)
    hid_ref[:, :128] = pair
    hid_ref[:, 128:] = gate
    narrow_pair = pair.astype(jnp.bfloat16)
    dl_ref[...] = dot32(below(narrow_pair, False), up_ref[:, :128], NT)
    rl_ref[...] = dot32(below(narrow_pair, True), up_ref[:, :128], NT)
    gate_ref[...] = dot32(gate.astype(jnp.bfloat16), up_ref[:, 128:], NT)


def front_forward(x, vectors, w_r, w_k, w_v, down, up):
    tokens, width = x.shape
    wide = pl.BlockSpec((ROWS, width), lambda i: (i, 0))
    own = pl.BlockSpec((ROWS, OWN), lambda i: (i, 0))
    hid = pl.BlockSpec((ROWS, 256), lambda i: (i, 0))
    whole = lambda a: pl.BlockSpec(a.shape, lambda i: (0, 0))
    shape = jax.ShapeDtypeStruct
    return pl.pallas_call(
        front_kernel,
        grid=(tokens // ROWS,),
        in_specs=[wide] + [whole(a) for a in (vectors, w_r, w_k, w_v, down, up)],
        out_specs=[wide] * 6 + [own] * 6 + [hid],
        out_shape=[shape((tokens, width), jnp.bfloat16)] * 6
        + [shape((tokens, OWN), jnp.float32)] * 6
        + [shape((tokens, 256), jnp.float32)],
        scratch_shapes=[pltpu.VMEM((8, width), jnp.float32)],
        compiler_params=pltpu.CompilerParams(vmem_limit_bytes=48 << 20),
        cost_estimate=SMALL,
        name="front_forward",
    )(x, vectors, w_r, w_k, w_v, down, up)


def front_back_kernel(
    x_ref, before_ref, vec_ref, wr_ref, wk_ref, wv_ref, down_ref, up_ref,
    m1_ref, m4_ref, m5_ref, hid_ref,
    dq_ref, dk_ref, dv_ref, ddl_ref, drl_ref, dgate_ref, own_vec_ref, ffn_vec_ref,
    dx_ref, misc_ref,
    edge_ref, sums_ref,
):
    step = pl.num_programs(0) - 1 - pl.program_id(0)
    core = lax.axis_index("dp") % 2
    own_start = pl.multiple_of(core * OWN, OWN)

    @pl.when(pl.program_id(0) == 0)
    def _():
        edge_ref[...] = jnp.zeros_like(edge_ref)
        sums_ref[...] = jnp.zeros_like(sums_ref)
        misc_ref[...] = jnp.zeros_like(misc_ref)

    unit, scale = row_norm(x_ref[...].astype(jnp.float32))
    gain, offset = vec_ref[12:13], vec_ref[13:14]
    normed = unit * gain + offset
    tail, _ = row_norm(before_ref[...].astype(jnp.float32))
    edge = (tail[15:] * gain + offset) * jnp.where(step == 0, 0.0, 1.0)
    change = shifted(normed, edge, True) - normed
    ddl, drl, dgate = ddl_ref[...], drl_ref[...], dgate_ref[...]
    hid = hid_ref[...]
    pair, gate = hid[:, :128], hid[:, 128:]
    lane = lax.broadcasted_iota(jnp.int32, pair.shape, 1)
    first_up, last_up = up_ref[:, :128], up_ref[:, 128:]
    pair_grad = jnp.where(
        lane < DECAY_RANK,
        dot32(ddl, first_up, NN) * (1.0 - pair * pair),
        dot32(drl, first_up, NN),
    ).astype(jnp.bfloat16)
    gate_grad = (dot32(dgate, last_up, NN) * gate * (1.0 - gate)).astype(jnp.bfloat16)
    narrow_pair, narrow_gate = pair.astype(jnp.bfloat16), gate.astype(jnp.bfloat16)
    own_rows = pl.ds(own_start, OWN)
    misc_ref[own_rows, 256:384] += dot32(ddl, below(narrow_pair, False), TN) + dot32(
        drl, below(narrow_pair, True), TN
    )
    misc_ref[own_rows, 384:512] += dot32(dgate, narrow_gate, TN)
    decay_part, rate_part = below(pair_grad, False), below(pair_grad, True)
    misc_ref[:, :128] += dot32(m1_ref[...], decay_part, TN) + dot32(m4_ref[...], rate_part, TN)
    misc_ref[:, 128:256] += dot32(m5_ref[...], gate_grad, TN)
    first_down = down_ref[:, :128]
    grads = (
        lambda: dot32(dq_ref[...], wr_ref[...], NT),
        lambda: dot32(decay_part, first_down, NT),
        lambda: dot32(dk_ref[...], wk_ref[...], NT),
        lambda: dot32(dv_ref[...], wv_ref[...], NT),
        lambda: dot32(rate_part, first_down, NT),
        lambda: dot32(gate_grad, down_ref[:, 128:], NT),
    )
    total = jnp.zeros_like(change)
    moved = jnp.zeros_like(change)
    for j, grad in enumerate(grads):
        now = grad()
        total = total + now
        moved = moved + now * vec_ref[j : j + 1]
        sums_ref[j : j + 1] += jnp.sum(now * change, axis=0, keepdims=True)
    dnormed = total - moved + shifted(moved, edge_ref[:1], False)
    edge_ref[:1] = moved[:1]
    sums_ref[12:13] += jnp.sum(dnormed * unit, axis=0, keepdims=True)
    sums_ref[13:14] += jnp.sum(dnormed, axis=0, keepdims=True)
    dunit = dnormed * gain
    dx_ref[...] = scale * (
        dunit
        - jnp.mean(dunit, axis=-1, keepdims=True)
        - unit * jnp.mean(dunit * unit, axis=-1, keepdims=True)
    )

    @pl.when(step == 0)
    def _():
        sums_ref[6:7] = ffn_vec_ref[0:1] * 0.5
        sums_ref[14:16] = ffn_vec_ref[1:3] * 0.5
        zeros = jnp.zeros((1, OWN), jnp.float32)
        for target, source in ((7, 0), (8, 1), (9, 2), (10, 3), (11, 4), (16, 5), (17, 6)):
            mine = own_vec_ref[source : source + 1]
            sums_ref[target : target + 1] = jnp.concatenate(
                [jnp.where(core == 0, mine, zeros), jnp.where(core == 0, zeros, mine)], axis=1
            )
        for block in range(EMBED // 128):
            lanes = slice(block * 128, (block + 1) * 128)
            misc_ref[lanes, 512:640] = sums_ref[:, lanes].T


def front_backward(
    x, vectors, w_r, w_k, w_v, down, up, mixes, hid, grads, own_vec, ffn_vec
):
    tokens, width = x.shape
    steps = tokens // ROWS
    wide = pl.BlockSpec((ROWS, width), lambda i: (steps - 1 - i, 0))
    before = pl.BlockSpec(
        (16, width), lambda i: (jnp.maximum((steps - 1 - i) * (ROWS // 16) - 1, 0), 0)
    )
    own = pl.BlockSpec((ROWS, OWN), lambda i: (steps - 1 - i, 0))
    hid_spec = pl.BlockSpec((ROWS, 256), lambda i: (steps - 1 - i, 0))
    whole = lambda a: pl.BlockSpec(a.shape, lambda i: (0, 0))
    shape = jax.ShapeDtypeStruct
    return pl.pallas_call(
        front_back_kernel,
        grid=(steps,),
        in_specs=[wide, before]
        + [whole(a) for a in (vectors, w_r, w_k, w_v, down, up)]
        + [wide] * 3
        + [hid_spec]
        + [own] * 6
        + [whole(own_vec), whole(ffn_vec)],
        out_specs=[wide, pl.BlockSpec((EMBED, 640), lambda i: (0, 0))],
        out_shape=[shape((tokens, width), jnp.float32), shape((EMBED, 640), jnp.float32)],
        scratch_shapes=[
            pltpu.VMEM((8, width), jnp.float32), pltpu.VMEM((128, width), jnp.float32),
        ],
        compiler_params=pltpu.CompilerParams(vmem_limit_bytes=48 << 20),
        cost_estimate=SMALL,
        name="front_backward",
    )(x, x, vectors, w_r, w_k, w_v, down, up, *mixes, hid, *grads, own_vec, ffn_vec)


def ffn_back_kernel(
    len_ref, res_ref, before_ref, cot_ref, mine_ref, other_ref, vec_ref, wo_ref,
    grad_ref, narrow_ref, gated_ref, dvec_ref,
    edge_ref,
):
    step = pl.num_programs(0) - 1 - pl.program_id(0)

    @pl.when(pl.program_id(0) == 0)
    def _():
        edge_ref[...] = jnp.zeros_like(edge_ref)
        dvec_ref[...] = jnp.zeros_like(dvec_ref)

    gain, offset, coefficient = vec_ref[14:15], vec_ref[15:16], vec_ref[6:7]
    unit, scale = row_norm(res_ref[...])
    normed = unit * gain + offset
    tail, _ = row_norm(before_ref[...])
    edge = (tail[7:] * gain + offset) * jnp.where(step == 0, 0.0, 1.0)
    change = shifted(normed, edge, True) - normed
    grad = mine_ref[...].astype(jnp.float32) + other_ref[...].astype(jnp.float32)
    moved = grad * coefficient
    dnormed = grad - moved + shifted(moved, edge_ref[:1], False)
    edge_ref[:1] = moved[:1]
    sums = lambda x: jnp.sum(x, axis=0, keepdims=True)
    dvec_ref[0:1] += sums(grad * change)
    dvec_ref[1:2] += sums(dnormed * unit)
    dvec_ref[2:3] += sums(dnormed)
    dunit = dnormed * gain
    row = lax.broadcasted_iota(jnp.int32, grad.shape, 0) + step * ROWS
    out_grad = jnp.where(row < len_ref[0], cot_ref[...].astype(jnp.float32), 0.0)
    total = out_grad + scale * (
        dunit
        - jnp.mean(dunit, axis=-1, keepdims=True)
        - unit * jnp.mean(dunit * unit, axis=-1, keepdims=True)
    )
    grad_ref[...] = total
    small = total.astype(jnp.bfloat16)
    narrow_ref[...] = small
    gated_ref[...] = dot32(small, wo_ref[...], NT)


def ffn_backward(length, residual, cot, mine, other, vectors, w_o_rows):
    tokens, width = residual.shape
    steps = tokens // ROWS
    wide = pl.BlockSpec((ROWS, width), lambda i: (steps - 1 - i, 0))
    before = pl.BlockSpec(
        (8, width), lambda i: (jnp.maximum((steps - 1 - i) * (ROWS // 8) - 1, 0), 0)
    )
    own = pl.BlockSpec((ROWS, OWN), lambda i: (steps - 1 - i, 0))
    whole = lambda a: pl.BlockSpec(a.shape, lambda i: (0, 0))
    shape = jax.ShapeDtypeStruct
    return pl.pallas_call(
        ffn_back_kernel,
        grid=(steps,),
        in_specs=[pl.BlockSpec(memory_space=pltpu.SMEM), wide, before]
        + [wide] * 3
        + [whole(vectors), whole(w_o_rows)],
        out_specs=[wide, wide, own, pl.BlockSpec((8, width), lambda i: (0, 0))],
        out_shape=[
            shape((tokens, width), jnp.float32),
            shape((tokens, width), jnp.bfloat16),
            shape((tokens, OWN), jnp.float32),
            shape((8, width), jnp.float32),
        ],
        scratch_shapes=[pltpu.VMEM((8, width), jnp.float32)],
        compiler_params=pltpu.CompilerParams(vmem_limit_bytes=48 << 20),
        cost_estimate=SMALL,
        name="ffn_backward",
    )(length, residual, residual, cot, mine, other, vectors, w_o_rows)


def att_grad_kernel(m0_ref, m2_ref, m3_ref, gated_ref, dq_ref, dk_ref, dv_ref, da_ref,
                    send_a, keep_a, send_b, keep_b):
    chip = lax.axis_index("dp") // 2
    by_x, by_y = chip % 2 == 0, (chip // 2) % 2 == 0
    core = lax.axis_index("dp") % 2
    da = da_ref[:, pl.ds(pl.multiple_of(core * OWN, OWN), OWN)]
    first = ((m0_ref, dq_ref[...]), (gated_ref, da))
    second = ((m2_ref, dk_ref[...]), (m3_ref, dv_ref[...]))
    for half, ((left_a, right_a), (left_b, right_b)) in enumerate(zip(first, second)):
        lanes = slice(half * OWN, (half + 1) * OWN)
        for z in range(4):
            rows = slice(z * 256, (z + 1) * 256)
            block = dot32(left_a[:, rows], right_a, TN).astype(jnp.bfloat16)
            for y in range(2):
                low, high = block[y * 128 : y * 128 + 64], block[y * 128 + 64 : y * 128 + 128]
                send_a[2 * z + y, :, lanes] = jnp.where(by_x, high, low)
                keep_a[2 * z + y, :, lanes] = jnp.where(by_x, low, high)
            block = dot32(left_b[:, rows], right_b, TN).astype(jnp.bfloat16)
            for x in range(2):
                low, high = block[x * 64 : x * 64 + 64], block[128 + x * 64 : 128 + x * 64 + 64]
                send_b[2 * z + x, :, lanes] = jnp.where(by_y, high, low)
                keep_b[2 * z + x, :, lanes] = jnp.where(by_y, low, high)


def att_gradients(mixes, gated, grads, attended_grad):
    space = pl.BlockSpec(memory_space=pltpu.VMEM)
    return pl.pallas_call(
        att_grad_kernel,
        in_specs=[space] * 8,
        out_specs=[space] * 4,
        out_shape=[jax.ShapeDtypeStruct((8, 64, 2 * OWN), jnp.bfloat16)] * 4,
        compiler_params=pltpu.CompilerParams(vmem_limit_bytes=40 << 20),
        cost_estimate=SMALL,
        name="att_gradients",
    )(*mixes, gated, *grads, attended_grad)


def swap(block, mask):
    size = lax.axis_size("dp")
    return lax.ppermute(block, "dp", [(i, i ^ mask) for i in range(size)])


def bit_of(mask):
    return (lax.axis_index("dp") // mask) % 2


def in_order(mask, own, other, axis):
    lower = bit_of(mask) == 0
    return jnp.where(
        lower, jnp.concatenate([own, other], axis=axis), jnp.concatenate([other, own], axis=axis)
    )


def chip_masks():
    size = lax.axis_size("dp")
    masks = []
    while 2 << len(masks) < size:
        masks.append(2 << len(masks))
    return masks


def steps_of(kind):
    masks = chip_masks()
    near, far = [[mask] for mask in masks[:2]], masks[2:][::-1]
    single = [[mask] for mask in far]
    first = [[far[0], far[1], far[0] | far[1]]] if len(far) == 2 else single
    both = [[masks[0], masks[1], masks[0] | masks[1]]] if len(masks) > 1 else near
    return [first + near[::-1], first + near, near + first, first + both][kind]


def meet(movers, *arrays):
    held = lax.optimization_barrier(tuple(tuple(m.arrived) for m in movers) + arrays)
    for mover, arrived in zip(movers, held):
        mover.arrived = list(arrived)
    return held[len(movers) :]


class Gather:
    def __init__(self, block, kind, places=(0,)):
        self.steps = steps_of(kind)
        self.held = block[None]
        self.places = [0]
        self.arrived = []
        self.masks = []

    def merge(self):
        if self.arrived:
            self.held = jnp.concatenate([self.held] + self.arrived, axis=0)
            self.places = self.places + [p ^ (m // 2) for m in self.masks for p in self.places]
            self.arrived = []

    def step(self):
        if self.steps:
            self.merge()
            self.masks = self.steps.pop(0)
            self.arrived = [swap(self.held, mask) for mask in self.masks]
        return self

    def run(self):
        while self.steps:
            self.step()
        return self

    def split(self, kinds):
        width = self.held.shape[-1] // len(kinds)
        out = []
        for i, kind in enumerate(kinds):
            part = Gather.__new__(Gather)
            cut = slice(i * width, (i + 1) * width)
            part.steps = steps_of(kind)[len(steps_of(kind)) - len(self.steps) :]
            part.held = self.held[..., cut]
            part.arrived = [x[..., cut] for x in self.arrived]
            part.places, part.masks = self.places, self.masks
            out.append(part)
        return out


def place_kernel(places, cuts, *refs):
    sources, outs = refs[: len(places)], refs[len(places) :]
    chip = lax.axis_index("dp") // 2
    for source, (part, list_of) in zip(sources, places):
        for j, place in enumerate(list_of):
            for out, (first, rows, lanes) in zip(outs, cuts):
                start = pl.multiple_of((chip ^ place) * rows, rows)
                lane, width = lanes[part]
                at = sum(w for _, w in lanes[:part])
                out[pl.ds(start, rows), at : at + width] = source[
                    j, first : first + rows, lane : lane + width
                ]


def assemble(gathers, cuts=None):
    gathers = [g.run() for g in gathers]
    rows = gathers[0].held.shape[1]
    cuts = cuts or ((0, rows, [(0, g.held.shape[2]) for g in gathers]),)
    sources, places = [], []
    for i, g in enumerate(gathers):
        sources += [g.held] + g.arrived
        shifts = [0] + [mask // 2 for mask in g.masks]
        places += [(i, [p ^ shift for p in g.places]) for shift in shifts]
    count = lax.axis_size("dp") // 2
    if any(cut[1] % 16 for cut in cuts):
        return assemble_plain(sources, places, cuts, count)
    space = pl.BlockSpec(memory_space=pltpu.VMEM)
    return pl.pallas_call(
        partial(place_kernel, places, cuts),
        in_specs=[space] * len(sources),
        out_specs=[space] * len(cuts),
        out_shape=[
            jax.ShapeDtypeStruct((count * n, sum(w for _, w in lanes)), sources[0].dtype)
            for _, n, lanes in cuts
        ],
        compiler_params=pltpu.CompilerParams(vmem_limit_bytes=32 << 20),
        cost_estimate=SMALL,
        name="assemble",
    )(*sources)


def assemble_plain(sources, places, cuts, count):
    chip = lax.axis_index("dp") // 2
    parts = []
    for part in sorted({part for part, _ in places}):
        blocks = jnp.concatenate([x for x, (at, _) in zip(sources, places) if at == part])
        where = [p for at, list_of in places if at == part for p in list_of]
        blocks = jnp.stack([blocks[where.index(i)] for i in range(count)])
        parts.append(jnp.take(blocks, chip ^ lax.iota(jnp.int32, count), axis=0))
    return [
        jnp.concatenate(
            [x[:, first : first + n, at : at + w] for x, (at, w) in zip(parts, lanes)], axis=-1
        ).reshape(count * n, -1)
        for first, n, lanes in cuts
    ]


class Scatter:
    def __init__(self, parts, kind):
        self.steps = steps_of(kind)[::-1]
        self.axes = chip_masks()[::-1]
        shape = parts.shape[1:]
        self.sources = [parts.reshape((2,) * len(self.axes) + shape)]
        self.arrived = []

    def pick(self, mask, gone):
        out = []
        for x in self.sources:
            for place in reversed(range(len(self.axes))):
                axis = self.axes[place]
                if axis in gone:
                    which = bit_of(axis) if not mask & axis else 1 - bit_of(axis)
                    x = lax.dynamic_index_in_dim(x, which, place, keepdims=False)
            out.append(x)
        return out

    def merge(self):
        self.sources = self.sources + self.arrived
        self.arrived = []

    def step(self):
        if self.steps:
            self.merge()
            masks = self.steps.pop(0)
            gone = [axis for axis in self.axes if any(mask & axis for mask in masks)]
            sends = [
                sum(x.astype(jnp.float32) for x in self.pick(mask, gone)).astype(jnp.bfloat16)
                for mask in masks
            ]
            self.sources = self.pick(0, gone)
            self.axes = [axis for axis in self.axes if axis not in gone]
            self.sent = sends
            self.arrived = [swap(x, mask) for x, mask in zip(sends, masks)]
        return self

    def run(self):
        while self.steps:
            self.step()
        return self

    def total(self):
        self.merge()
        return sum(x.astype(jnp.float32) for x in self.sources)

    @classmethod
    def begun(cls, sent, kept, kind):
        out = cls.__new__(cls)
        out.steps = steps_of(kind)[::-1]
        masks = out.steps.pop(0)
        out.axes = [axis for axis in chip_masks()[::-1] if axis not in masks]
        out.sources = [kept.reshape((2,) * len(out.axes) + kept.shape[1:])]
        out.sent = [sent.reshape(out.sources[0].shape)]
        out.arrived = [swap(out.sent[0], masks[0])]
        return out

    @staticmethod
    def join(parts, rows):
        out = Scatter.__new__(Scatter)
        out.steps, out.axes, out.arrived = parts[0].steps, parts[0].axes, []
        pieces = []
        for part in parts:
            total = part.total()
            pieces += [total[..., at : at + rows, :] for at in range(0, total.shape[-2], rows)]
        out.sources = [jnp.concatenate(pieces, axis=-1)]
        return out


def norm_rows(features, gain_row, offset_row):
    average = jnp.mean(features, axis=-1, keepdims=True)
    centred = features - average
    variance = jnp.mean(centred * centred, axis=-1, keepdims=True)
    return centred * lax.rsqrt(variance + 1e-05) * gain_row + offset_row


def product(operand, weight_matrix):
    return jnp.dot(operand, weight_matrix, preferred_element_type=jnp.float32)


def input_gradient_rows(upstream_gradient, weight_matrix):
    return lax.dot_general(
        upstream_gradient,
        weight_matrix,
        (((1,), (1,)), ((), ())),
        preferred_element_type=jnp.float32,
    )


def weight_gradient(operand, upstream_gradient):
    return lax.dot_general(
        operand, upstream_gradient, (((0,), (0,)), ((), ())), preferred_element_type=jnp.float32
    )


def earlier(rows):
    return jnp.concatenate([jnp.zeros_like(rows[:1]), rows[:-1]], axis=0)


def ffn_mix(residual, vectors):
    second = norm_rows(residual, vectors[14], vectors[15])
    return second + (earlier(second) - second) * vectors[6]


def narrow(x):
    return x.astype(jnp.bfloat16)


def local(
    inputs,
    lengths,
    attention_projections,
    channel_key_weight,
    channel_value_weight,
    lowrank_down_weight,
    lowrank_up_weight,
    per_feature_parameters,
    cotangent,
):
    devices = lax.axis_size("dp")
    chips = devices // 2
    device = lax.axis_index("dp")
    chip, core = device // 2, device % 2
    row_count = inputs.shape[0]
    slots = 2 * row_count
    share = EMBED // devices
    pair_share = 2 * share
    units = channel_value_weight.shape[0]
    half_units = chips * units

    def own_cut(x, which):
        return lax.dynamic_slice_in_dim(x, which * OWN, OWN, x.ndim - 1)

    def own_rows(x, which):
        return lax.dynamic_slice_in_dim(x, which * row_count, row_count, 0)

    pair_rows = in_order(
        1,
        own_cut(attention_projections, core),
        swap(own_cut(attention_projections, 1 - core), 1),
        1,
    )
    lora = jnp.concatenate([lowrank_down_weight, lowrank_up_weight.T], axis=1)
    vector_rows = jnp.pad(per_feature_parameters.T, ((0, 0), (0, 128 - 18)))
    vector_rows = vector_rows.reshape(share // 4, OWN)
    first_rows = 3 * pair_share
    misc_rows = share + share // 4 + (share // 4) % 16
    block = jnp.concatenate(
        [
            pair_rows[:3].reshape(first_rows, OWN),
            lora,
            jnp.pad(vector_rows, ((0, (share // 4) % 16), (0, 0))),
        ],
        axis=0,
    )
    half = half_units // 2
    quarter = OWN // 2
    late = EMBED - quarter
    first = Gather(block, 0).step()
    out_rows = jnp.concatenate([pair_rows[3, :, :quarter], pair_rows[3, :, quarter:]], axis=0)
    late_part = Gather(jnp.concatenate([channel_value_weight[:, late:], out_rows], axis=1), 2)
    late_part.step().step()
    key_in, raw, cot, _ = meet([], channel_key_weight, inputs, cotangent, pair_rows)
    key_cut = key_in.reshape(share, chips, 2, units)

    def key_columns(which):
        return lax.dynamic_index_in_dim(key_cut, which, 2, keepdims=False).reshape(share, half_units)

    key_rows = in_order(1, key_columns(core), swap(key_columns(1 - core), 1), 0)
    (key_rows,) = meet([first, late_part], key_rows)
    first = first.split((0, 1))
    for part in first:
        part.step()
    tokens = in_order(1, raw, swap(raw, 1), 0)
    cot = in_order(1, cot, swap(cot, 1), 0)
    tokens, cot, key_rows = meet(first, tokens, cot, key_rows)
    for part in first:
        part.step()
    key_part = Gather(key_rows, 0).step()
    value_block, tokens = meet(first + [key_part], channel_value_weight[:, :late], tokens)
    key_parts = key_part.split((0, 1))
    for part in key_parts:
        part.step()
    value_part = Gather(value_block, 0).step()
    w_r, w_k, w_v, misc = assemble(
        first,
        [(i * pair_share, pair_share, [(0, quarter)] * 2) for i in range(3)]
        + [(first_rows, misc_rows, [(0, quarter)] * 2)],
    )
    misc = misc.reshape(chips, 1, misc_rows, OWN)
    misc = in_order(1, misc, swap(misc, 1), 1)
    lora = misc[:, :, :share].reshape(EMBED, OWN)
    down, up_t = lora[:, :256], lax.dynamic_slice_in_dim(lora[:, 256:], core * OWN, OWN, 0)
    vectors = misc[:, :, share : share + share // 4].reshape(EMBED, 128)[:, :18].T
    vectors = vectors.astype(jnp.float32)
    own_vectors = own_cut(vectors, core)
    used = jnp.concatenate([own_vectors[7:12], own_vectors[16:18], own_vectors[:1]], axis=0)
    length = lax.dynamic_index_in_dim(lengths, chip, 0)
    live = (lax.iota(jnp.int32, slots) < length)[:, None]

    *mixes, queries, keys, values, decay_low, rate_low, gate_rows, hid = front_forward(
        tokens, vectors, w_r, w_k, w_v, down, up_t
    )
    terms = meet(key_parts + [value_part], queries, keys, values, decay_low, rate_low, gate_rows)
    for part in key_parts:
        part.step()
    value_parts = value_part.split((0, 1))
    for part in value_parts:
        part.step()
    late_part.step()
    blocks = slots // (CHUNK * STEP_CHUNKS)
    early = blocks // 2
    zero_state = jnp.zeros((2, CHUNK, LANES), jnp.float32)
    gated, *saved, _ = wkv_forward(0, blocks, length, used, zero_state, terms)
    gated, cot, tokens = meet(key_parts + value_parts + [late_part], gated, cot, tokens)
    for part in value_parts:
        part.step()
    gated_all = in_order(1, gated, swap(gated, 1), 1)
    (key_weight,) = assemble(key_parts)
    value_late, w_o_own = assemble(
        [late_part], ((0, units, [(0, quarter)]), (0, units, [(quarter, quarter)]))
    )
    w_o_own = w_o_own.reshape(chips, 2, pair_share, quarter)
    w_o_own = jnp.concatenate([w_o_own[:, 0], w_o_own[:, 1]], axis=-1).reshape(EMBED, OWN)
    w_o = in_order(1, w_o_own, swap(w_o_own, 1), 1)
    residual = tokens.astype(jnp.float32) + product(gated_all, w_o)
    ffn_in = narrow(ffn_mix(residual, vectors))
    positive = jax.nn.relu(product(ffn_in, key_weight))
    hidden = narrow(jnp.square(positive))
    out_narrow = jnp.where(live, cot, jnp.zeros_like(cot))
    value_cuts = ((0, quarter), (quarter, OWN), (OWN, EMBED))
    value_grads = [
        narrow(weight_gradient(hidden, out_narrow[:, lo:hi])).reshape(chips, units, hi - lo)
        for lo, hi in value_cuts
    ]
    hidden, positive, out_narrow, *value_grads = meet(
        value_parts, hidden, positive, out_narrow, *value_grads
    )
    (value_weight,) = assemble(value_parts)

    value_scatter = [Scatter(x, kind).step() for kind, x in enumerate(value_grads)]
    hidden_grad = input_gradient_rows(out_narrow[:, :late], value_weight)
    hidden_grad = hidden_grad + input_gradient_rows(out_narrow[:, late:], value_late)
    pre_narrow = narrow(2.0 * positive * hidden_grad)
    ffn_in_grad = narrow(input_gradient_rows(pre_narrow, key_weight))
    other_grad = swap(ffn_in_grad, 1)
    grad_key = narrow(weight_gradient(ffn_in, pre_narrow)).reshape(chips, pair_share, half_units)
    ffn_in_grad, other_grad, grad_key, hidden = meet(
        [], ffn_in_grad, other_grad, grad_key, hidden
    )
    key_scatter = [
        Scatter(grad_key[:, :, i * half : (i + 1) * half], i).step() for i in range(2)
    ]
    residual_grad, attended_grad, gated_grad, ffn_vec = ffn_backward(
        length, residual, cot, ffn_in_grad, other_grad, vectors,
        lax.dynamic_slice_in_dim(w_o, core * OWN, OWN, 0),
    )
    gated_grad, *_ = meet(
        value_scatter[:2], gated_grad, *[x for m in key_scatter for x in m.sent]
    )
    for part in value_scatter[:2]:
        part.step()
    terms = [*terms, gated_grad, *saved]
    zero_sums = jnp.zeros((8, OWN), jnp.float32)
    *before, sums, state = wkv_backward(
        early, blocks - early, length, used, zero_state, zero_sums, terms
    )
    state, sums = meet(value_scatter + key_scatter, state, sums)
    for part in key_scatter + [value_scatter[2]]:
        part.step()
    *low_grads, own_vec, _ = wkv_backward(0, early, length, used, state, sums, terms, before)
    *low_grads, own_vec = meet(key_scatter + [value_scatter[2]], *low_grads, own_vec)
    if pair_share == 64:
        sent_a, kept_a, sent_b, kept_b = att_gradients(
            (mixes[0], mixes[2], mixes[3]), gated_all, low_grads[:3], attended_grad
        )
        att_scatter = [Scatter.begun(sent_a, kept_a, 0), Scatter.begun(sent_b, kept_b, 1)]
    else:
        grads = [weight_gradient(mixes[m], g) for m, g in zip((0, 2, 3), low_grads)]
        grad_o = weight_gradient(gated_all, own_cut(attended_grad, core))
        att_scatter = [
            Scatter(narrow(jnp.concatenate(x, axis=1)).reshape(chips, pair_share, 2 * OWN), i).step()
            for i, x in enumerate(((grads[0], grad_o), (grads[1], grads[2])))
        ]
    ffn_scatter = Scatter.join(key_scatter + value_scatter[:2], pair_share).step()
    value_late_scatter = value_scatter[2].step()
    own_vec, *_ = meet([], own_vec, *[x for m in att_scatter for x in m.sent])
    token_part, misc_grad = front_backward(
        tokens, vectors, w_r, w_k, w_v, down, up_t, (mixes[1], mixes[4], mixes[5]), hid,
        low_grads, own_vec, ffn_vec,
    )
    misc_grad = misc_grad.reshape(chips, 2, share, 640)
    misc_mine = lax.dynamic_index_in_dim(misc_grad, core, 1, keepdims=False)
    misc_other = narrow(lax.dynamic_index_in_dim(misc_grad, 1 - core, 1, keepdims=False))
    misc_sum = misc_mine + swap(misc_other, 1).astype(jnp.float32)
    token_part, misc_sum = meet(att_scatter, token_part, misc_sum)
    for part in att_scatter:
        part.step()
    misc_sum = jnp.concatenate([misc_sum[..., :320], misc_sum[..., 320:]], axis=1)
    misc_scatter = Scatter(misc_sum, 3).step()
    ffn_part = product(hidden, jnp.concatenate([value_weight, value_late], axis=1))
    ffn_out = own_rows(ffn_part, core) + swap(own_rows(ffn_part, 1 - core), 1)
    output = narrow(jnp.where(own_rows(live, core), own_rows(residual, core) + ffn_out, 0.0))
    input_gradient = (
        own_rows(residual_grad, core)
        + own_rows(token_part, core)
        + swap(own_rows(token_part, 1 - core), 1)
    )
    output, input_gradient = meet(
        att_scatter + [misc_scatter, ffn_scatter, value_late_scatter], output, input_gradient
    )
    last = Scatter.join(att_scatter + [misc_scatter], pair_share).step()
    ffn_sum = ffn_scatter.run().total()
    value_late_sum = value_late_scatter.run().total()
    ffn_sum, value_late_sum = meet([last], ffn_sum, value_late_sum)
    last_sum = last.run().total()
    ratio = units // pair_share
    value_sum = jnp.concatenate(
        [
            ffn_sum[:, half_units + at * quarter : half_units + (at + 1) * quarter]
            for at in range(2 * ratio)
        ],
        axis=1,
    )
    value_sum = value_sum.reshape(pair_share, 2, ratio, quarter).transpose(2, 0, 1, 3)
    value_sum = jnp.concatenate([value_sum.reshape(units, OWN), value_late_sum], axis=1)
    misc_sum = last_sum[:, 4 * OWN :]
    misc_sum = jnp.concatenate([misc_sum[:share], misc_sum[share:]], axis=1)
    pair_sum = jnp.concatenate([last_sum[:, : 4 * OWN], ffn_sum[:, :half_units]], axis=1)
    pair_sum = pair_sum.reshape(2, share, -1)
    mine = lax.dynamic_index_in_dim(pair_sum, core, 0, keepdims=False)
    theirs = swap(lax.dynamic_index_in_dim(pair_sum, 1 - core, 0, keepdims=False), 1)
    shard_mixer = jnp.stack(
        [
            in_order(1, mine[:, i * OWN : (i + 1) * OWN], theirs[:, i * OWN : (i + 1) * OWN], 1)
            for i in (0, 2, 3, 1)
        ]
    )
    shard_key = in_order(
        1,
        mine[:, 4 * OWN :].reshape(share, chips, 1, units),
        theirs[:, 4 * OWN :].reshape(share, chips, 1, units),
        2,
    ).reshape(share, 2 * half_units)
    return (
        output,
        input_gradient,
        shard_mixer,
        shard_key,
        value_sum,
        misc_sum[:, :256],
        misc_sum[:, 256:512].T,
        misc_sum[:, 512:530].T,
    )


def solution(mesh):
    in_specs = (
        P("dp", None),
        P(),
        P(None, "dp", None),
        P("dp", None),
        P("dp", None),
        P("dp", None),
        P(None, "dp"),
        P(None, "dp"),
        P("dp", None),
    )
    out_specs = (
        P("dp", None),
        P("dp", None),
        P(None, "dp", None),
        P("dp", None),
        P("dp", None),
        P("dp", None),
        P(None, "dp"),
        P(None, "dp"),
    )
    return jax.shard_map(local, mesh=mesh, in_specs=in_specs, out_specs=out_specs, check_vma=False)
```

```python
from functools import partial

import jax
import jax.numpy as jnp
from jax import lax
from jax.experimental import pallas as pl
from jax.experimental.pallas import tpu as pltpu
from jax.sharding import PartitionSpec as P

HEADS = 16
HEAD_SIZE = 64
DECAY_RANK = 64
RATE_RANK = 64
EMBED = 1024
OWN = EMBED // 2
PRECISE = lax.Precision.HIGHEST


CHUNK = 64
LANES = 256
GROUP_HEADS = 4
STEP_CHUNKS = 2
SMALL = pl.CostEstimate(flops=1, bytes_accessed=1, transcendentals=0)

NN = (((1,), (0,)), ((), ()))
NT = (((1,), (1,)), ((), ()))
TN = (((0,), (0,)), ((), ()))


def halves(x):
    high = x.astype(jnp.bfloat16)
    return high, (x - high.astype(jnp.float32)).astype(jnp.bfloat16)


def dot32(a, b, dims):
    return lax.dot_general(a, b, dims, preferred_element_type=jnp.float32)


def mul(left, right, dims=NN):
    rows = left[0].shape[0]
    both = dot32(jnp.concatenate(left, axis=0), right[0], dims)
    return both[:rows] + both[rows:] + dot32(left[0], right[1], dims)


def tmul(left, right, masks):
    full = (
        dot32(left[0], right[0], TN) + dot32(left[1], right[0], TN) + dot32(left[0], right[1], TN)
    )
    return sum(full[h * CHUNK : (h + 1) * CHUNK] * masks[h][:1].astype(jnp.float32) for h in range(GROUP_HEADS))


def spread(pair, masks):
    return tuple(
        jnp.concatenate([part * masks[h] for h in range(GROUP_HEADS)], axis=0) for part in pair
    )


def stack(first, second):
    return tuple(jnp.concatenate([x, y], axis=0) for x, y in zip(first, second))


def head_masks():
    lane = lax.broadcasted_iota(jnp.int32, (CHUNK, LANES), 1) // CHUNK
    return [(lane == h).astype(jnp.float32).astype(jnp.bfloat16) for h in range(GROUP_HEADS)]


def places():
    row = lax.broadcasted_iota(jnp.int32, (CHUNK, LANES), 0)
    col = lax.broadcasted_iota(jnp.int32, (CHUNK, LANES), 1) % CHUNK
    return row, col


def running_sum(x, upper=False):
    row = lax.broadcasted_iota(jnp.int32, (CHUNK, CHUNK), 0)
    col = lax.broadcasted_iota(jnp.int32, (CHUNK, CHUNK), 1)
    ones = (row <= col if upper else col <= row).astype(jnp.float32).astype(jnp.bfloat16)
    high, rest = halves(x)
    low = (x - high.astype(jnp.float32) - rest.astype(jnp.float32)).astype(jnp.bfloat16)
    return dot32(ones, high, NN) + dot32(ones, rest, NN) + dot32(ones, low, NN)


def scaled_forms(q, w, k, a, b):
    total = running_sum(w)
    before = total - w
    middle = total[CHUNK // 2 - 1 : CHUNK // 2]
    end = total[CHUNK - 1 :]
    ea = jnp.exp(before - middle)
    eq = jnp.exp(total - middle)
    eb = jnp.exp(middle - total)
    ee = jnp.exp(end - total)
    return (a * ea, q * eq, b * eb, k * eb, b * ee, k * ee), (ea, eq, eb, ee), (jnp.exp(middle), jnp.exp(end))


def each(fn, *columns):
    return [fn(*row) for row in zip(*columns)]


def block_ones():
    row = lax.broadcasted_iota(jnp.int32, (LANES, LANES), 0) // CHUNK
    col = lax.broadcasted_iota(jnp.int32, (LANES, LANES), 1) // CHUNK
    return (row == col).astype(jnp.float32).astype(jnp.bfloat16)


def head_sum(x, ones):
    rows = x.shape[0]
    both = dot32(jnp.concatenate(halves(x), axis=0), ones, NN)
    return both[:rows] + both[rows:]


def prepared(keys, decay_low, rate_low, live, vec, ones):
    sig = jax.nn.sigmoid(vec[0] + decay_low)
    log_decay = (-0.6065306597126334) * sig * live
    rates = jax.nn.sigmoid(vec[1] + rate_low)
    scaled = keys * vec[2]
    inverse = lax.rsqrt(head_sum(scaled * scaled, ones) + 1e-06)
    unit_keys = scaled * inverse
    factor = (1.0 + (rates - 1.0) * vec[3]) * live
    return log_decay, keys * factor, -unit_keys, unit_keys * rates * live, sig, rates, inverse, factor


def read_out(o, q, k, v, vec, ones):
    centred = o - head_sum(o, ones) * (1.0 / CHUNK)
    scale = lax.rsqrt(head_sum(centred * centred, ones) * (1.0 / CHUNK) + 0.00064)
    normed = centred * scale
    weight = head_sum(q * k * vec[4], ones)
    return normed, scale, weight, normed * vec[5] + vec[6] + weight * v


def unit_slices():
    return [
        (slice(c * CHUNK, (c + 1) * CHUNK), slice(g * LANES, (g + 1) * LANES))
        for c in range(STEP_CHUNKS)
        for g in range(2)
    ]


def unit_live(length, step):
    row = lax.broadcasted_iota(jnp.int32, (CHUNK, LANES), 0)
    start = step * (STEP_CHUNKS * CHUNK)
    live = [(row + (start + c * CHUNK) < length).astype(jnp.float32) for c in range(STEP_CHUNKS)]
    return [live[c] for c in range(STEP_CHUNKS) for g in range(2)]


def unit_vectors(vec_ref):
    vec = [[vec_ref[i : i + 1, g * LANES : (g + 1) * LANES] for i in range(7)] for g in range(2)]
    return [vec[g] for c in range(STEP_CHUNKS) for g in range(2)]


def forward_kernel(base, *refs):
    len_ref, vec_ref, start_ref, q_ref, keys_ref, v_ref, dl_ref, rl_ref, gate_ref = refs[:9]
    (
        out_ref, o_ref, t_ref, aqb_ref, aak_ref, aqk_ref, y_ref, z_ref, trt_ref, qe_ref, state_ref,
    ) = refs[-11:]

    @pl.when(pl.program_id(0) == 0)
    def _():
        state_ref[...] = start_ref[...]

    masks = head_masks()
    row, col = places()
    strict = (col < row).astype(jnp.float32)
    within = (col <= row).astype(jnp.float32)
    eye = (col == row).astype(jnp.float32)
    ones = block_ones()
    units = unit_slices()
    live = unit_live(len_ref[0], pl.program_id(0) + base)
    vec = unit_vectors(vec_ref)
    load = lambda ref: [ref[u] for u in units]
    q, keys, v = load(q_ref), load(keys_ref), load(v_ref)
    ready = each(
        lambda x, y, z, m, n: prepared(x, y, z, m, n, ones), keys, load(dl_ref), load(rl_ref), live, vec
    )
    w, k, a, b = ([x[i] for x in ready] for i in range(4))
    forms = each(scaled_forms, q, w, k, a, b)
    ah, qh, bh, kh, bt, kt = ([f[0][i] for f in forms] for i in range(6))
    emid = [f[2][0] for f in forms]
    eend = [f[2][1] for f in forms]
    aq = each(lambda x, y: halves(jnp.concatenate([x, y], axis=0)), ah, qh)
    with_b = each(lambda l, r: mul(l, spread(halves(r), masks), NT), aq, bh)
    with_k = each(lambda l, r: mul(l, spread(halves(r), masks), NT), aq, kh)
    aab = [x[:CHUNK] * strict for x in with_b]
    aqb = [halves(x[CHUNK:] * within) for x in with_b]
    aak = [halves(x[:CHUNK] * strict) for x in with_k]
    aqk = [halves(x[CHUNK:] * within) for x in with_k]
    p = [halves(x * (row // 8 == col // 8)) for x in aab]
    t = [eye + x * (row // 8 == col // 8) for x in aab]
    p2 = each(lambda x: halves(mul(x, spread(x, masks))), p)
    both = each(lambda x, y: mul(stack(x, halves(y)), spread(x, masks)), p2, t)
    p4 = [halves(x[:CHUNK]) for x in both]
    t = each(lambda x, y: x + y[CHUNK:], t, both)
    t = each(lambda x, y: x + mul(halves(x), spread(y, masks)), t, p4)
    for size in (8, 16, 32):
        corner = ((row // size) % 2 == 1) & (col // size == row // size - 1)
        ts = [halves(x) for x in t]
        n = [halves(x * corner) for x in aab]
        tn = each(lambda x, y: halves(mul(x, spread(y, masks))), ts, n)
        t = each(lambda x, y, z: x + mul(y, spread(z, masks)), t, tn, ts)
    ts = [halves(x) for x in t]
    vs = [halves(x) for x in v]
    vm = [spread(x, masks) for x in vs]
    wide = each(lambda x, y, e: mul(x, spread(halves(y * e), masks)), ts, ah, emid)
    r0 = each(mul, aak, vm)
    y0 = each(lambda x, y: mul(x, spread(halves(y), masks)), ts, r0)
    wides = [halves(x) for x in wide]
    qe = each(lambda x, e, y, z: x * e + mul(y, spread(z, masks)), qh, emid, aqb, wides)
    y0s = [halves(x) for x in y0]
    part = each(lambda x, y, z, u: mul(x, spread(y, masks)) + mul(z, u), aqb, y0s, aqk, vm)
    bts = [halves(x) for x in bt]
    diag = [eye * e for e in eend]
    tr = each(lambda x, y, d: tmul(x, y, masks) + d, bts, wides, diag)
    trt = each(lambda x, y, d: tmul(y, x, masks) + d, bts, wides, diag)
    inject = each(lambda x, y, z, u: tmul(stack(x, halves(y)), stack(z, u), masks), bts, kt, y0s, vs)
    wq = each(lambda x, y: stack(x, halves(y)), wides, qe)
    z = []
    out = []
    for c in range(STEP_CHUNKS):
        for g in range(2):
            i = c * 2 + g
            now = state_ref[g]
            nows = spread(halves(now), masks)
            state_ref[g] = mul(halves(tr[i]), nows) + inject[i]
            z.append(now)
            out.append(mul(wq[i], nows))
    o = each(lambda x, y: x[CHUNK:] + y, out, part)
    mixed = each(lambda x, y, z, m, n: read_out(x, y, z, m, n, ones)[3], o, q, k, v, vec)
    for i, u in enumerate(units):
        out_ref[u] = (mixed[i] * gate_ref[u]).astype(jnp.bfloat16)
        o_ref[u] = o[i]
        y_ref[u] = out[i][:CHUNK] + y0[i]
        t_ref[u] = t[i]
        aqb_ref[u] = with_b[i][CHUNK:] * within
        aak_ref[u] = with_k[i][:CHUNK] * strict
        aqk_ref[u] = with_k[i][CHUNK:] * within
        z_ref[u] = z[i]
        trt_ref[u] = trt[i]
        qe_ref[u] = qe[i]


def backward_kernel(base, *refs):
    (
        len_ref, vec_ref, start_ref, sums_ref, q_ref, keys_ref, v_ref, dl_ref, rl_ref, gate_ref,
        g_ref, o_ref, t_ref, aqb_ref, aak_ref, aqk_ref, y_ref, z_ref, trt_ref, qe_ref,
    ) = refs[:20]
    dq_ref, dkeys_ref, dv_ref, ddl_ref, drl_ref, dgate_ref, dvec_ref, state_ref = refs[-8:]
    step = base + pl.num_programs(0) - 1 - pl.program_id(0)

    @pl.when(pl.program_id(0) == 0)
    def _():
        state_ref[...] = start_ref[...]
        dvec_ref[...] = sums_ref[...]

    masks = head_masks()
    row, col = places()
    strict = (col < row).astype(jnp.float32)
    within = (col <= row).astype(jnp.float32)
    ones = block_ones()
    units = unit_slices()
    live = unit_live(len_ref[0], step)
    vec = unit_vectors(vec_ref)
    load = lambda ref: [ref[u] for u in units]
    q, keys, v, g = load(q_ref), load(keys_ref), load(v_ref), load(g_ref)
    ready = each(
        lambda x, y, z, m, n: prepared(x, y, z, m, n, ones), keys, load(dl_ref), load(rl_ref), live, vec
    )
    w, k, a, b, sig, rates, inverse, factor = ([x[i] for x in ready] for i in range(8))
    seen = each(lambda x, y, z, m, n: read_out(x, y, z, m, n, ones), load(o_ref), q, k, v, vec)
    normed, scale, weight, mixed = ([x[i] for x in seen] for i in range(4))
    gate = load(gate_ref)
    dgate = each(lambda x, y: x * y, g, mixed)
    dmix = each(lambda x, y: x * y, g, gate)
    dn = each(lambda x, n: x * n[5], dmix, vec)
    do = each(
        lambda x, n, r: r
        * (x - head_sum(x, ones) * (1.0 / CHUNK) - n * (head_sum(x * n, ones) * (1.0 / CHUNK))),
        dn, normed, scale,
    )
    dweight = each(lambda x, y: head_sum(x * y, ones), dmix, v)
    do = [halves(x) for x in do]
    qe, trt, t, aqb, aak, aqk, ys = (
        [halves(x) for x in load(ref)]
        for ref in (qe_ref, trt_ref, t_ref, aqb_ref, aak_ref, aqk_ref, y_ref)
    )
    z = load(z_ref)
    vs = [halves(x) for x in v]
    h = each(lambda x, y: tmul(x, y, masks), qe, do)
    dz = [None] * len(units)
    for c in reversed(range(STEP_CHUNKS)):
        for g in range(2):
            i = c * 2 + g
            now = state_ref[g]
            dz[i] = now
            state_ref[g] = mul(trt[i], spread(halves(now), masks)) + h[i]
    dzs = [spread(halves(x), masks) for x in dz]
    zs = [spread(halves(x), masks) for x in z]
    forms = each(scaled_forms, q, w, k, a, b)
    ah, qh, bh, kh, bt, kt = ([f[0][i] for f in forms] for i in range(6))
    ea, eq, eb, ee = ([f[1][i] for f in forms] for i in range(4))
    emid = [f[2][0] for f in forms]
    eend = [f[2][1] for f in forms]
    from_end = each(lambda x, y, s: mul(halves(jnp.concatenate([x, y], axis=0)), s), bt, kt, dzs)
    dy = each(lambda x, y, s: halves(tmul(x, y, masks) + s[:CHUNK]), aqb, do, from_end)
    dr = each(lambda x, y: halves(tmul(x, y, masks)), t, dy)
    ro = each(stack, dr, do)
    dv = each(lambda x, y, s, f: tmul(stack(x, y), s, masks) + f[CHUNK:], aak, aqk, ro, from_end)
    mask2 = jnp.concatenate([strict, within], axis=0)
    dab = each(lambda s, y: halves(mul(s, spread(y, masks), NT) * mask2), ro, ys)
    dak = each(lambda s, y: halves(mul(s, spread(y, masks), NT) * mask2), ro, vs)
    dst = each(lambda s, y: mul(s, y, NT), ro, zs)
    daq = each(
        lambda s, e, x, bb, y, kk: s * e + mul(x, spread(halves(bb), masks)) + mul(y, spread(halves(kk), masks)),
        dst, emid, dab, bh, dak, kh,
    )
    aq = each(lambda x, y: halves(jnp.concatenate([x, y], axis=0)), ah, qh)
    dbh = each(lambda x, y: tmul(x, y, masks), dab, aq)
    dkh = each(lambda x, y: tmul(x, y, masks), dak, aq)
    dend = each(lambda y, x, s: mul(stack(y, x), s, NT), ys, vs, dzs)
    row_of_ones = jnp.ones((8, LANES), jnp.bfloat16)
    sums = lambda x: jnp.sum(x, axis=0, keepdims=True)
    for i, u in enumerate(units):
        da = daq[i][:CHUNK] * ea[i]
        dq = daq[i][CHUNK:] * eq[i]
        dbt = dend[i][:CHUNK] * ee[i]
        dkt = dend[i][CHUNK:] * ee[i]
        db = dbh[i] * eb[i] + dbt
        dk = dkh[i] * eb[i] + dkt
        pa = da * a[i]
        diff = dq * q[i] - db * b[i] - dk * k[i] + pa
        zz = spread(halves(z[i] * dz[i]), masks)
        carry = (dot32(row_of_ones, zz[0], NT) + dot32(row_of_ones, zz[1], NT))[:1] * eend[i]
        carry = carry + sums(dbt * b[i] + dkt * k[i])
        dw = running_sum(diff, upper=True) - pa + carry
        from_bonus = dweight[i] * vec[i][4]
        dk = dk + from_bonus * q[i]
        dq_ref[u] = (dq + from_bonus * k[i]).astype(jnp.bfloat16)
        dv_ref[u] = (dv[i] + weight[i] * dmix[i]).astype(jnp.bfloat16)
        dgate_ref[u] = dgate[i].astype(jnp.bfloat16)
        unit_keys = -a[i]
        db = db * live[i]
        du = db * rates[i] - da
        dscaled = inverse[i] * (du - unit_keys * head_sum(du * unit_keys, ones))
        dkl = dk * keys[i] * live[i]
        drl = (db * unit_keys + dkl * vec[i][3]) * rates[i] * (1.0 - rates[i])
        ddl = dw * w[i] * (1.0 - sig[i])
        dkeys_ref[u] = (dk * factor[i] + dscaled * vec[i][2]).astype(jnp.bfloat16)
        ddl_ref[u] = ddl.astype(jnp.bfloat16)
        drl_ref[u] = drl.astype(jnp.bfloat16)
        parts = (
            ddl, drl, dscaled * keys[i], dkl * (rates[i] - 1.0),
            dweight[i] * q[i] * k[i], dmix[i] * normed[i], dmix[i],
        )
        lanes = u[1]
        for j, x in enumerate(parts):
            dvec_ref[j : j + 1, lanes] += sums(x)


def wkv_call(kernel, base, steps, small, arrays, outs, sums, previous, name):
    tokens, width = arrays[0].shape
    rows = CHUNK * STEP_CHUNKS
    last = base + steps - 1
    turned = kernel is backward_kernel
    spec = pl.BlockSpec((rows, width), lambda i: (last - i if turned else base + i, 0))
    state = pl.BlockSpec((2, CHUNK, LANES), lambda i: (0, 0, 0))
    whole = pl.BlockSpec((8, width), lambda i: (0, 0))
    shape = jax.ShapeDtypeStruct
    first = [pl.BlockSpec(memory_space=pltpu.SMEM), whole, state] + [whole] * sums
    held = list(previous or ())
    start = len(first) + len(arrays)
    return pl.pallas_call(
        partial(kernel, base),
        grid=(steps,),
        in_specs=first + [spec] * len(arrays) + [pl.BlockSpec(memory_space=pl.ANY)] * len(held),
        out_specs=[spec] * len(outs) + [whole] * sums + [state],
        out_shape=[shape((tokens, width), dtype) for dtype in outs]
        + [shape((8, width), jnp.float32)] * sums
        + [shape((2, CHUNK, LANES), jnp.float32)],
        input_output_aliases={start + i: i for i in range(len(held))},
        compiler_params=pltpu.CompilerParams(vmem_limit_bytes=56 << 20),
        cost_estimate=SMALL,
        name=name,
    )(*small, *arrays, *held)


def wkv_forward(base, steps, length, vec, state, arrays, previous=None):
    outs = [jnp.bfloat16] + [jnp.float32] * 9
    return wkv_call(
        forward_kernel, base, steps, (length, vec, state), arrays, outs, 0, previous, "wkv_forward"
    )


def wkv_backward(base, steps, length, vec, state, sums, arrays, previous=None):
    outs = [jnp.bfloat16] * 6
    return wkv_call(
        backward_kernel, base, steps, (length, vec, state, sums), arrays, outs, 1, previous,
        "wkv_backward",
    )


ROWS = 128


def row_norm(x):
    centred = x - jnp.mean(x, axis=-1, keepdims=True)
    scale = lax.rsqrt(jnp.mean(centred * centred, axis=-1, keepdims=True) + 1e-05)
    return centred * scale, scale


def shifted(x, edge, down):
    rows = x.shape[0]
    row = lax.broadcasted_iota(jnp.int32, x.shape, 0)
    if down:
        return jnp.where(row == 0, edge, pltpu.roll(x, 1, 0))
    return jnp.where(row == rows - 1, edge, pltpu.roll(x, rows - 1, 0))


def below(x, upper):
    lane = lax.broadcasted_iota(jnp.int32, x.shape, 1)
    keep = (lane >= DECAY_RANK) if upper else (lane < DECAY_RANK)
    return jnp.where(keep, x, jnp.zeros_like(x))


def front_kernel(
    x_ref, vec_ref, wr_ref, wk_ref, wv_ref, down_ref, up_ref,
    m0_ref, m1_ref, m2_ref, m3_ref, m4_ref, m5_ref,
    q_ref, k_ref, v_ref, dl_ref, rl_ref, gate_ref, hid_ref,
    edge_ref,
):
    @pl.when(pl.program_id(0) == 0)
    def _():
        edge_ref[...] = jnp.zeros_like(edge_ref)

    unit, _ = row_norm(x_ref[...].astype(jnp.float32))
    normed = unit * vec_ref[12:13] + vec_ref[13:14]
    change = shifted(normed, edge_ref[:1], True) - normed
    edge_ref[:1] = normed[ROWS - 1 :]
    mixes = []
    for j, ref in enumerate((m0_ref, m1_ref, m2_ref, m3_ref, m4_ref, m5_ref)):
        mixes.append((normed + change * vec_ref[j : j + 1]).astype(jnp.bfloat16))
        ref[...] = mixes[j]
    q_ref[...] = dot32(mixes[0], wr_ref[...], NN)
    k_ref[...] = dot32(mixes[2], wk_ref[...], NN)
    v_ref[...] = dot32(mixes[3], wv_ref[...], NN)
    first = down_ref[:, :128]
    pre_decay, pre_rate = dot32(mixes[1], first, NN), dot32(mixes[4], first, NN)
    pre_gate = dot32(mixes[5], down_ref[:, 128:], NN)
    lane = lax.broadcasted_iota(jnp.int32, pre_decay.shape, 1)
    pair = jnp.where(lane < DECAY_RANK, jnp.tanh(pre_decay), pre_rate)
    gate = jax.nn.sigmoid(pre_gate)
    hid_ref[:, :128] = pair
    hid_ref[:, 128:] = gate
    narrow_pair = pair.astype(jnp.bfloat16)
    dl_ref[...] = dot32(below(narrow_pair, False), up_ref[:, :128], NT)
    rl_ref[...] = dot32(below(narrow_pair, True), up_ref[:, :128], NT)
    gate_ref[...] = dot32(gate.astype(jnp.bfloat16), up_ref[:, 128:], NT)


def front_forward(x, vectors, w_r, w_k, w_v, down, up):
    tokens, width = x.shape
    wide = pl.BlockSpec((ROWS, width), lambda i: (i, 0))
    own = pl.BlockSpec((ROWS, OWN), lambda i: (i, 0))
    hid = pl.BlockSpec((ROWS, 256), lambda i: (i, 0))
    whole = lambda a: pl.BlockSpec(a.shape, lambda i: (0, 0))
    shape = jax.ShapeDtypeStruct
    return pl.pallas_call(
        front_kernel,
        grid=(tokens // ROWS,),
        in_specs=[wide] + [whole(a) for a in (vectors, w_r, w_k, w_v, down, up)],
        out_specs=[wide] * 6 + [own] * 6 + [hid],
        out_shape=[shape((tokens, width), jnp.bfloat16)] * 6
        + [shape((tokens, OWN), jnp.float32)] * 6
        + [shape((tokens, 256), jnp.float32)],
        scratch_shapes=[pltpu.VMEM((8, width), jnp.float32)],
        compiler_params=pltpu.CompilerParams(vmem_limit_bytes=48 << 20),
        cost_estimate=SMALL,
        name="front_forward",
    )(x, vectors, w_r, w_k, w_v, down, up)


def front_back_kernel(
    x_ref, before_ref, vec_ref, wr_ref, wk_ref, wv_ref, down_ref, up_ref,
    m1_ref, m4_ref, m5_ref, hid_ref,
    dq_ref, dk_ref, dv_ref, ddl_ref, drl_ref, dgate_ref, own_vec_ref, ffn_vec_ref,
    dx_ref, misc_ref,
    edge_ref, sums_ref,
):
    step = pl.num_programs(0) - 1 - pl.program_id(0)
    core = lax.axis_index("dp") % 2
    own_start = pl.multiple_of(core * OWN, OWN)

    @pl.when(pl.program_id(0) == 0)
    def _():
        edge_ref[...] = jnp.zeros_like(edge_ref)
        sums_ref[...] = jnp.zeros_like(sums_ref)
        misc_ref[...] = jnp.zeros_like(misc_ref)

    unit, scale = row_norm(x_ref[...].astype(jnp.float32))
    gain, offset = vec_ref[12:13], vec_ref[13:14]
    normed = unit * gain + offset
    tail, _ = row_norm(before_ref[...].astype(jnp.float32))
    edge = (tail[15:] * gain + offset) * jnp.where(step == 0, 0.0, 1.0)
    change = shifted(normed, edge, True) - normed
    ddl, drl, dgate = ddl_ref[...], drl_ref[...], dgate_ref[...]
    hid = hid_ref[...]
    pair, gate = hid[:, :128], hid[:, 128:]
    lane = lax.broadcasted_iota(jnp.int32, pair.shape, 1)
    first_up, last_up = up_ref[:, :128], up_ref[:, 128:]
    pair_grad = jnp.where(
        lane < DECAY_RANK,
        dot32(ddl, first_up, NN) * (1.0 - pair * pair),
        dot32(drl, first_up, NN),
    ).astype(jnp.bfloat16)
    gate_grad = (dot32(dgate, last_up, NN) * gate * (1.0 - gate)).astype(jnp.bfloat16)
    narrow_pair, narrow_gate = pair.astype(jnp.bfloat16), gate.astype(jnp.bfloat16)
    own_rows = pl.ds(own_start, OWN)
    misc_ref[own_rows, 256:384] += dot32(ddl, below(narrow_pair, False), TN) + dot32(
        drl, below(narrow_pair, True), TN
    )
    misc_ref[own_rows, 384:512] += dot32(dgate, narrow_gate, TN)
    decay_part, rate_part = below(pair_grad, False), below(pair_grad, True)
    misc_ref[:, :128] += dot32(m1_ref[...], decay_part, TN) + dot32(m4_ref[...], rate_part, TN)
    misc_ref[:, 128:256] += dot32(m5_ref[...], gate_grad, TN)
    first_down = down_ref[:, :128]
    grads = (
        lambda: dot32(dq_ref[...], wr_ref[...], NT),
        lambda: dot32(decay_part, first_down, NT),
        lambda: dot32(dk_ref[...], wk_ref[...], NT),
        lambda: dot32(dv_ref[...], wv_ref[...], NT),
        lambda: dot32(rate_part, first_down, NT),
        lambda: dot32(gate_grad, down_ref[:, 128:], NT),
    )
    total = jnp.zeros_like(change)
    moved = jnp.zeros_like(change)
    for j, grad in enumerate(grads):
        now = grad()
        total = total + now
        moved = moved + now * vec_ref[j : j + 1]
        sums_ref[j : j + 1] += jnp.sum(now * change, axis=0, keepdims=True)
    dnormed = total - moved + shifted(moved, edge_ref[:1], False)
    edge_ref[:1] = moved[:1]
    sums_ref[12:13] += jnp.sum(dnormed * unit, axis=0, keepdims=True)
    sums_ref[13:14] += jnp.sum(dnormed, axis=0, keepdims=True)
    dunit = dnormed * gain
    dx_ref[...] = scale * (
        dunit
        - jnp.mean(dunit, axis=-1, keepdims=True)
        - unit * jnp.mean(dunit * unit, axis=-1, keepdims=True)
    )

    @pl.when(step == 0)
    def _():
        sums_ref[6:7] = ffn_vec_ref[0:1] * 0.5
        sums_ref[14:16] = ffn_vec_ref[1:3] * 0.5
        zeros = jnp.zeros((1, OWN), jnp.float32)
        for target, source in ((7, 0), (8, 1), (9, 2), (10, 3), (11, 4), (16, 5), (17, 6)):
            mine = own_vec_ref[source : source + 1]
            sums_ref[target : target + 1] = jnp.concatenate(
                [jnp.where(core == 0, mine, zeros), jnp.where(core == 0, zeros, mine)], axis=1
            )
        for block in range(EMBED // 128):
            lanes = slice(block * 128, (block + 1) * 128)
            misc_ref[lanes, 512:640] = sums_ref[:, lanes].T


def front_backward(
    x, vectors, w_r, w_k, w_v, down, up, mixes, hid, grads, own_vec, ffn_vec
):
    tokens, width = x.shape
    steps = tokens // ROWS
    wide = pl.BlockSpec((ROWS, width), lambda i: (steps - 1 - i, 0))
    before = pl.BlockSpec(
        (16, width), lambda i: (jnp.maximum((steps - 1 - i) * (ROWS // 16) - 1, 0), 0)
    )
    own = pl.BlockSpec((ROWS, OWN), lambda i: (steps - 1 - i, 0))
    hid_spec = pl.BlockSpec((ROWS, 256), lambda i: (steps - 1 - i, 0))
    whole = lambda a: pl.BlockSpec(a.shape, lambda i: (0, 0))
    shape = jax.ShapeDtypeStruct
    return pl.pallas_call(
        front_back_kernel,
        grid=(steps,),
        in_specs=[wide, before]
        + [whole(a) for a in (vectors, w_r, w_k, w_v, down, up)]
        + [wide] * 3
        + [hid_spec]
        + [own] * 6
        + [whole(own_vec), whole(ffn_vec)],
        out_specs=[wide, pl.BlockSpec((EMBED, 640), lambda i: (0, 0))],
        out_shape=[shape((tokens, width), jnp.float32), shape((EMBED, 640), jnp.float32)],
        scratch_shapes=[
            pltpu.VMEM((8, width), jnp.float32), pltpu.VMEM((128, width), jnp.float32),
        ],
        compiler_params=pltpu.CompilerParams(vmem_limit_bytes=48 << 20),
        cost_estimate=SMALL,
        name="front_backward",
    )(x, x, vectors, w_r, w_k, w_v, down, up, *mixes, hid, *grads, own_vec, ffn_vec)


def ffn_back_kernel(
    len_ref, res_ref, before_ref, cot_ref, mine_ref, other_ref, vec_ref, wo_ref,
    grad_ref, narrow_ref, gated_ref, dvec_ref,
    edge_ref,
):
    step = pl.num_programs(0) - 1 - pl.program_id(0)

    @pl.when(pl.program_id(0) == 0)
    def _():
        edge_ref[...] = jnp.zeros_like(edge_ref)
        dvec_ref[...] = jnp.zeros_like(dvec_ref)

    gain, offset, coefficient = vec_ref[14:15], vec_ref[15:16], vec_ref[6:7]
    unit, scale = row_norm(res_ref[...])
    normed = unit * gain + offset
    tail, _ = row_norm(before_ref[...])
    edge = (tail[7:] * gain + offset) * jnp.where(step == 0, 0.0, 1.0)
    change = shifted(normed, edge, True) - normed
    grad = mine_ref[...].astype(jnp.float32) + other_ref[...].astype(jnp.float32)
    moved = grad * coefficient
    dnormed = grad - moved + shifted(moved, edge_ref[:1], False)
    edge_ref[:1] = moved[:1]
    sums = lambda x: jnp.sum(x, axis=0, keepdims=True)
    dvec_ref[0:1] += sums(grad * change)
    dvec_ref[1:2] += sums(dnormed * unit)
    dvec_ref[2:3] += sums(dnormed)
    dunit = dnormed * gain
    row = lax.broadcasted_iota(jnp.int32, grad.shape, 0) + step * ROWS
    out_grad = jnp.where(row < len_ref[0], cot_ref[...].astype(jnp.float32), 0.0)
    total = out_grad + scale * (
        dunit
        - jnp.mean(dunit, axis=-1, keepdims=True)
        - unit * jnp.mean(dunit * unit, axis=-1, keepdims=True)
    )
    grad_ref[...] = total
    small = total.astype(jnp.bfloat16)
    narrow_ref[...] = small
    gated_ref[...] = dot32(small, wo_ref[...], NT)


def ffn_backward(length, residual, cot, mine, other, vectors, w_o_rows):
    tokens, width = residual.shape
    steps = tokens // ROWS
    wide = pl.BlockSpec((ROWS, width), lambda i: (steps - 1 - i, 0))
    before = pl.BlockSpec(
        (8, width), lambda i: (jnp.maximum((steps - 1 - i) * (ROWS // 8) - 1, 0), 0)
    )
    own = pl.BlockSpec((ROWS, OWN), lambda i: (steps - 1 - i, 0))
    whole = lambda a: pl.BlockSpec(a.shape, lambda i: (0, 0))
    shape = jax.ShapeDtypeStruct
    return pl.pallas_call(
        ffn_back_kernel,
        grid=(steps,),
        in_specs=[pl.BlockSpec(memory_space=pltpu.SMEM), wide, before]
        + [wide] * 3
        + [whole(vectors), whole(w_o_rows)],
        out_specs=[wide, wide, own, pl.BlockSpec((8, width), lambda i: (0, 0))],
        out_shape=[
            shape((tokens, width), jnp.float32),
            shape((tokens, width), jnp.bfloat16),
            shape((tokens, OWN), jnp.float32),
            shape((8, width), jnp.float32),
        ],
        scratch_shapes=[pltpu.VMEM((8, width), jnp.float32)],
        compiler_params=pltpu.CompilerParams(vmem_limit_bytes=48 << 20),
        cost_estimate=SMALL,
        name="ffn_backward",
    )(length, residual, residual, cot, mine, other, vectors, w_o_rows)


def att_grad_kernel(m0_ref, m2_ref, m3_ref, dq_ref, dk_ref, dv_ref, send_a, keep_a, send_b, keep_b, whole_c):
    chip = lax.axis_index("dp") // 2
    by_x, by_y = chip % 2 == 0, (chip // 2) % 2 == 0
    dq, dk, dv = dq_ref[...], dk_ref[...], dv_ref[...]
    for z in range(4):
        rows = slice(z * 256, (z + 1) * 256)
        block = dot32(m0_ref[:, rows], dq, TN).astype(jnp.bfloat16)
        for y in range(2):
            low, high = block[y * 128 : y * 128 + 64], block[y * 128 + 64 : y * 128 + 128]
            send_a[2 * z + y] = jnp.where(by_x, high, low)
            keep_a[2 * z + y] = jnp.where(by_x, low, high)
        block = dot32(m2_ref[:, rows], dk, TN).astype(jnp.bfloat16)
        for x in range(2):
            low, high = block[x * 64 : x * 64 + 64], block[128 + x * 64 : 128 + x * 64 + 64]
            send_b[2 * z + x] = jnp.where(by_y, high, low)
            keep_b[2 * z + x] = jnp.where(by_y, low, high)
        whole_c[rows] = dot32(m3_ref[:, rows], dv, TN).astype(jnp.bfloat16)


def att_gradients(mixes, grads):
    space = pl.BlockSpec(memory_space=pltpu.VMEM)
    shape = jax.ShapeDtypeStruct
    return pl.pallas_call(
        att_grad_kernel,
        in_specs=[space] * 6,
        out_specs=[space] * 5,
        out_shape=[shape((8, 64, OWN), jnp.bfloat16)] * 4 + [shape((EMBED, OWN), jnp.bfloat16)],
        compiler_params=pltpu.CompilerParams(vmem_limit_bytes=40 << 20),
        cost_estimate=SMALL,
        name="att_gradients",
    )(*mixes, *grads)


def swap(block, mask):
    size = lax.axis_size("dp")
    return lax.ppermute(block, "dp", [(i, i ^ mask) for i in range(size)])


def bit_of(mask):
    return (lax.axis_index("dp") // mask) % 2


def in_order(mask, own, other, axis):
    lower = bit_of(mask) == 0
    return jnp.where(
        lower, jnp.concatenate([own, other], axis=axis), jnp.concatenate([other, own], axis=axis)
    )


def chip_masks():
    size = lax.axis_size("dp")
    masks = []
    while 2 << len(masks) < size:
        masks.append(2 << len(masks))
    return masks


def steps_of(kind):
    masks = chip_masks()
    near, far = masks[:2], masks[2:][::-1]
    return [far + near[::-1], far + near, near + far][kind]


def meet(movers, *arrays):
    held = lax.optimization_barrier(tuple(tuple(m.arrived) for m in movers) + arrays)
    for mover, arrived in zip(movers, held):
        mover.arrived = list(arrived)
    return held[len(movers) :]


class Gather:
    def __init__(self, block, kind):
        self.steps = steps_of(kind)
        self.held = block[None]
        self.places = [0]
        self.arrived = []
        self.mask = 0

    def step(self):
        if self.steps:
            if self.arrived:
                self.held = jnp.concatenate([self.held] + self.arrived, axis=0)
                self.places = self.places + [p ^ (self.mask // 2) for p in self.places]
            self.mask = self.steps.pop(0)
            self.arrived = [swap(self.held, self.mask)]
        return self

    def run(self):
        while self.steps:
            self.step()
        return self

    def split(self, kinds):
        width = self.held.shape[-1] // len(kinds)
        out = []
        for i, kind in enumerate(kinds):
            part = Gather.__new__(Gather)
            cut = slice(i * width, (i + 1) * width)
            part.steps = steps_of(kind)[len(steps_of(kind)) - len(self.steps) :]
            part.held = self.held[..., cut]
            part.arrived = [x[..., cut] for x in self.arrived]
            part.places, part.mask = self.places, self.mask
            out.append(part)
        return out


def place_kernel(places, cuts, *refs):
    sources, outs = refs[: len(places)], refs[len(places) :]
    chip = lax.axis_index("dp") // 2
    for source, (part, list_of) in zip(sources, places):
        for j, place in enumerate(list_of):
            for out, (first, rows, lanes) in zip(outs, cuts):
                start = pl.multiple_of((chip ^ place) * rows, rows)
                lane, width = lanes[part]
                at = sum(w for _, w in lanes[:part])
                out[pl.ds(start, rows), at : at + width] = source[
                    j, first : first + rows, lane : lane + width
                ]


def assemble(gathers, cuts=None):
    gathers = [g.run() for g in gathers]
    rows = gathers[0].held.shape[1]
    cuts = cuts or ((0, rows, [(0, g.held.shape[2]) for g in gathers]),)
    sources, places = [], []
    for i, g in enumerate(gathers):
        sources += [g.held] + g.arrived
        shifts = (0, g.mask // 2)
        places += [(i, [p ^ shift for p in g.places]) for shift in shifts]
    count = lax.axis_size("dp") // 2
    if any(cut[1] % 16 for cut in cuts):
        return assemble_plain(sources, places, cuts, count)
    space = pl.BlockSpec(memory_space=pltpu.VMEM)
    return pl.pallas_call(
        partial(place_kernel, places, cuts),
        in_specs=[space] * len(sources),
        out_specs=[space] * len(cuts),
        out_shape=[
            jax.ShapeDtypeStruct((count * n, sum(w for _, w in lanes)), sources[0].dtype)
            for _, n, lanes in cuts
        ],
        compiler_params=pltpu.CompilerParams(vmem_limit_bytes=32 << 20),
        cost_estimate=SMALL,
        name="assemble",
    )(*sources)


def assemble_plain(sources, places, cuts, count):
    chip = lax.axis_index("dp") // 2
    parts = []
    for part in sorted({part for part, _ in places}):
        blocks = jnp.concatenate([x for x, (at, _) in zip(sources, places) if at == part])
        where = [p for at, list_of in places if at == part for p in list_of]
        blocks = jnp.stack([blocks[where.index(i)] for i in range(count)])
        parts.append(jnp.take(blocks, chip ^ lax.iota(jnp.int32, count), axis=0))
    return [
        jnp.concatenate(
            [x[:, first : first + n, at : at + w] for x, (at, w) in zip(parts, lanes)], axis=-1
        ).reshape(count * n, -1)
        for first, n, lanes in cuts
    ]


class Scatter:
    def __init__(self, parts, kind):
        self.steps = steps_of(kind)[::-1]
        self.axes = chip_masks()[::-1]
        self.sources = [parts.reshape((2,) * len(self.axes) + parts.shape[1:])]
        self.arrived = []

    def step(self):
        if self.steps:
            sources = self.sources + self.arrived
            mask = self.steps.pop(0)
            place = self.axes.index(mask)
            self.axes = self.axes[:place] + self.axes[place + 1 :]
            bit = bit_of(mask)
            pick = lambda x, which: lax.dynamic_index_in_dim(x, which, place, keepdims=False)
            send = sum(pick(x, 1 - bit).astype(jnp.float32) for x in sources)
            self.sent = send.astype(jnp.bfloat16)
            self.sources = [pick(x, bit) for x in sources]
            self.arrived = [swap(self.sent, mask)]
        return self

    def run(self):
        while self.steps:
            self.step()
        return self

    def total(self):
        return sum(x.astype(jnp.float32) for x in self.sources + self.arrived)

    @classmethod
    def begun(cls, sent, kept, kind):
        out = cls.__new__(cls)
        out.steps = steps_of(kind)[::-1]
        mask = out.steps.pop(0)
        out.axes = [axis for axis in chip_masks()[::-1] if axis != mask]
        out.sources = [kept.reshape((2,) * len(out.axes) + kept.shape[1:])]
        out.sent = sent.reshape(out.sources[0].shape)
        out.arrived = [swap(out.sent, mask)]
        return out

    @staticmethod
    def join(parts, rows):
        out = Scatter.__new__(Scatter)
        out.steps, out.axes, out.arrived = parts[0].steps, parts[0].axes, []
        pieces = []
        for part in parts:
            total = part.total()
            pieces += [total[..., at : at + rows, :] for at in range(0, total.shape[-2], rows)]
        out.sources = [jnp.concatenate(pieces, axis=-1)]
        return out


def norm_rows(features, gain_row, offset_row):
    average = jnp.mean(features, axis=-1, keepdims=True)
    centred = features - average
    variance = jnp.mean(centred * centred, axis=-1, keepdims=True)
    return centred * lax.rsqrt(variance + 1e-05) * gain_row + offset_row


def product(operand, weight_matrix):
    return jnp.dot(operand, weight_matrix, preferred_element_type=jnp.float32)


def input_gradient_rows(upstream_gradient, weight_matrix):
    return lax.dot_general(
        upstream_gradient,
        weight_matrix,
        (((1,), (1,)), ((), ())),
        preferred_element_type=jnp.float32,
    )


def weight_gradient(operand, upstream_gradient):
    return lax.dot_general(
        operand, upstream_gradient, (((0,), (0,)), ((), ())), preferred_element_type=jnp.float32
    )


def earlier(rows):
    return jnp.concatenate([jnp.zeros_like(rows[:1]), rows[:-1]], axis=0)


def ffn_mix(residual, vectors):
    second = norm_rows(residual, vectors[14], vectors[15])
    return second + (earlier(second) - second) * vectors[6]


def narrow(x):
    return x.astype(jnp.bfloat16)


def local(
    inputs,
    lengths,
    attention_projections,
    channel_key_weight,
    channel_value_weight,
    lowrank_down_weight,
    lowrank_up_weight,
    per_feature_parameters,
    cotangent,
):
    devices = lax.axis_size("dp")
    chips = devices // 2
    device = lax.axis_index("dp")
    chip, core = device // 2, device % 2
    row_count = inputs.shape[0]
    slots = 2 * row_count
    share = EMBED // devices
    pair_share = 2 * share
    units = channel_value_weight.shape[0]
    half_units = chips * units

    def own_cut(x, which):
        return lax.dynamic_slice_in_dim(x, which * OWN, OWN, x.ndim - 1)

    def own_rows(x, which):
        return lax.dynamic_slice_in_dim(x, which * row_count, row_count, 0)

    pair_rows = in_order(
        1,
        own_cut(attention_projections, core),
        swap(own_cut(attention_projections, 1 - core), 1),
        1,
    )
    lora = jnp.concatenate([lowrank_down_weight, lowrank_up_weight.T], axis=1)
    vector_rows = jnp.pad(per_feature_parameters.T, ((0, 0), (0, 128 - 18)))
    vector_rows = vector_rows.reshape(share // 4, OWN)
    first_rows = 3 * pair_share
    misc_rows = share + share // 4 + (share // 4) % 16
    block = jnp.concatenate(
        [
            pair_rows[:3].reshape(first_rows, OWN),
            lora,
            jnp.pad(vector_rows, ((0, (share // 4) % 16), (0, 0))),
        ],
        axis=0,
    )
    half = half_units // 2
    quarter = OWN // 2
    first = Gather(block, 0).step()
    late_part = Gather(channel_value_weight[:, OWN:], 2).step()
    key_in, raw, cot, _ = meet([], channel_key_weight, inputs, cotangent, pair_rows)
    key_cut = key_in.reshape(share, chips, 2, units)

    def key_columns(which):
        return lax.dynamic_index_in_dim(key_cut, which, 2, keepdims=False).reshape(share, half_units)

    key_rows = in_order(1, key_columns(core), swap(key_columns(1 - core), 1), 0)
    key_rows = jnp.concatenate(
        [pair_rows[3, :, :quarter], key_rows[:, :half], pair_rows[3, :, quarter:], key_rows[:, half:]],
        axis=1,
    )
    key_rows, raw, cot = meet([first, late_part], key_rows, raw, cot)
    first.step()
    late_part.step()
    tokens = in_order(1, raw, swap(raw, 1), 0)
    cot = in_order(1, cot, swap(cot, 1), 0)
    key_rows, tokens, cot = meet([first, late_part], key_rows, tokens, cot)
    first = first.split((0, 1))
    for part in first:
        part.step()
    key_part = Gather(key_rows, 0).step()
    tokens, value_block = meet(first + [key_part], tokens, channel_value_weight[:, :OWN])
    for part in first:
        part.step()
    key_part.step()
    value_part = Gather(value_block, 0).step()
    tokens, cot = meet(first + [key_part, value_part], tokens, cot)
    key_parts = key_part.split((0, 1))
    for part in key_parts:
        part.step()
    w_r, w_k, w_v, misc = assemble(
        first,
        [(i * pair_share, pair_share, [(0, quarter)] * 2) for i in range(3)]
        + [(first_rows, misc_rows, [(0, quarter)] * 2)],
    )
    misc = misc.reshape(chips, 1, misc_rows, OWN)
    misc = in_order(1, misc, swap(misc, 1), 1)
    value_part.step()
    late_part.step()
    lora = misc[:, :, :share].reshape(EMBED, OWN)
    down, up_t = lora[:, :256], lax.dynamic_slice_in_dim(lora[:, 256:], core * OWN, OWN, 0)
    vectors = misc[:, :, share : share + share // 4].reshape(EMBED, 128)[:, :18].T
    vectors = vectors.astype(jnp.float32)
    own_vectors = own_cut(vectors, core)
    used = jnp.concatenate([own_vectors[7:12], own_vectors[16:18], own_vectors[:1]], axis=0)
    length = lax.dynamic_index_in_dim(lengths, chip, 0)
    live = (lax.iota(jnp.int32, slots) < length)[:, None]

    *mixes, queries, keys, values, decay_low, rate_low, gate_rows, hid = front_forward(
        tokens, vectors, w_r, w_k, w_v, down, up_t
    )
    terms = meet(
        key_parts + [value_part, late_part],
        queries, keys, values, decay_low, rate_low, gate_rows,
    )
    value_parts = value_part.split((0, 1))
    for part in key_parts + value_parts:
        part.step()
    late_part.step()
    blocks = slots // (CHUNK * STEP_CHUNKS)
    early = blocks // 2
    zero_state = jnp.zeros((2, CHUNK, LANES), jnp.float32)
    gated, *saved, _ = wkv_forward(0, blocks, length, used, zero_state, terms)
    gated, cot, tokens = meet(key_parts + value_parts + [late_part], gated, cot, tokens)
    for part in value_parts:
        part.step()
    gated_all = in_order(1, gated, swap(gated, 1), 1)
    key_weight, w_o_own = assemble(
        key_parts,
        ((0, pair_share, [(quarter, half)] * 2), (0, pair_share, [(0, quarter)] * 2)),
    )
    w_o = in_order(1, w_o_own, swap(w_o_own, 1), 1)
    residual = tokens.astype(jnp.float32) + product(gated_all, w_o)
    ffn_in = narrow(ffn_mix(residual, vectors))
    positive = jax.nn.relu(product(ffn_in, key_weight))
    hidden = narrow(jnp.square(positive))
    out_narrow = jnp.where(live, cot, jnp.zeros_like(cot))
    value_cuts = ((0, quarter), (quarter, OWN), (OWN, EMBED))
    value_grads = [
        narrow(weight_gradient(hidden, out_narrow[:, lo:hi])).reshape(chips, units, hi - lo)
        for lo, hi in value_cuts
    ]
    hidden, positive, out_narrow, *value_grads = meet(
        value_parts, hidden, positive, out_narrow, *value_grads
    )
    (value_weight,) = assemble(value_parts + [late_part])

    value_scatter = [Scatter(x, kind).step() for kind, x in enumerate(value_grads[:2])]
    pre_narrow = narrow(2.0 * positive * input_gradient_rows(out_narrow, value_weight))
    ffn_in_grad = narrow(input_gradient_rows(pre_narrow, key_weight))
    other_grad = swap(ffn_in_grad, 1)
    grad_key = narrow(weight_gradient(ffn_in, pre_narrow)).reshape(chips, pair_share, half_units)
    ffn_in_grad, other_grad, grad_key, hidden = meet(
        [], ffn_in_grad, other_grad, grad_key, hidden
    )
    key_scatter = [
        Scatter(grad_key[:, :, i * half : (i + 1) * half], i).step() for i in range(2)
    ]
    residual_grad, attended_grad, gated_grad, ffn_vec = ffn_backward(
        length, residual, cot, ffn_in_grad, other_grad, vectors,
        lax.dynamic_slice_in_dim(w_o, core * OWN, OWN, 0),
    )
    grad_o = narrow(weight_gradient(gated_all, own_cut(attended_grad, core)))
    gated_grad, grad_o, *_ = meet(
        value_scatter, gated_grad, grad_o, *[m.sent for m in key_scatter]
    )
    for part in value_scatter:
        part.step()
    late_scatter = Scatter(
        jnp.concatenate([value_grads[2], grad_o.reshape(chips, pair_share, OWN)], axis=1), 2
    ).step()
    terms = [*terms, gated_grad, *saved]
    zero_sums = jnp.zeros((8, OWN), jnp.float32)
    *before, sums, state = wkv_backward(
        early, blocks - early, length, used, zero_state, zero_sums, terms
    )
    state, sums = meet(value_scatter + key_scatter, state, sums)
    for part in key_scatter:
        part.step()
    ffn_part = product(hidden, value_weight)
    ffn_out = own_rows(ffn_part, core) + swap(own_rows(ffn_part, 1 - core), 1)
    *low_grads, own_vec, _ = wkv_backward(0, early, length, used, state, sums, terms, before)
    *low_grads, own_vec, ffn_out = meet(
        key_scatter + [late_scatter], *low_grads, own_vec, ffn_out
    )
    if pair_share == 64:
        sent_a, kept_a, sent_b, kept_b, grad_v = att_gradients(
            (mixes[0], mixes[2], mixes[3]), low_grads[:3]
        )
        att_scatter = [
            Scatter.begun(sent_a, kept_a, 0),
            Scatter.begun(sent_b, kept_b, 1),
            Scatter(grad_v.reshape(chips, pair_share, OWN), 2).step(),
        ]
    else:
        att_scatter = [
            Scatter(narrow(weight_gradient(mixes[m], g)).reshape(chips, pair_share, OWN), kind).step()
            for kind, (m, g) in enumerate(zip((0, 2, 3), low_grads))
        ]
    ffn_scatter = Scatter.join(key_scatter + value_scatter, pair_share).step()
    late_scatter.step()
    own_vec, *_ = meet([], own_vec, *[m.sent for m in att_scatter])
    token_part, misc_grad = front_backward(
        tokens, vectors, w_r, w_k, w_v, down, up_t, (mixes[1], mixes[4], mixes[5]), hid,
        low_grads, own_vec, ffn_vec,
    )
    misc_grad = misc_grad.reshape(chips, 2, share, 640)
    misc_mine = lax.dynamic_index_in_dim(misc_grad, core, 1, keepdims=False)
    misc_other = narrow(lax.dynamic_index_in_dim(misc_grad, 1 - core, 1, keepdims=False))
    misc_sum = misc_mine + swap(misc_other, 1).astype(jnp.float32)
    token_part, misc_sum = meet(
        att_scatter + [ffn_scatter, late_scatter], token_part, misc_sum
    )
    for part in att_scatter:
        part.step()
    ffn_scatter.step()
    misc_scatter = Scatter(misc_sum, 2).step()
    output = narrow(jnp.where(own_rows(live, core), own_rows(residual, core) + ffn_out, 0.0))
    token_part, output = meet(att_scatter + [ffn_scatter, misc_scatter], token_part, output)
    att_pair = Scatter.join(att_scatter[:2], pair_share).step()
    v_scatter = att_scatter[2].step()
    late_scatter.step()
    misc_scatter.step()
    input_gradient = (
        own_rows(residual_grad, core)
        + own_rows(token_part, core)
        + swap(own_rows(token_part, 1 - core), 1)
    )
    (input_gradient,) = meet(
        [att_pair, v_scatter, late_scatter, misc_scatter], input_gradient
    )
    att_pair.step()
    v_scatter.step()
    late_scatter.step()
    misc_scatter.step()
    ffn_sum = ffn_scatter.run().total()
    (ffn_sum,) = meet([att_pair, v_scatter, late_scatter, misc_scatter], ffn_sum)
    misc_sum = misc_scatter.run().total()
    late_sum = late_scatter.run().total()
    ratio = units // pair_share
    value_sum = jnp.concatenate(
        [
            ffn_sum[:, half_units + at * quarter : half_units + (at + 1) * quarter]
            for at in range(2 * ratio)
        ],
        axis=1,
    )
    value_sum = value_sum.reshape(pair_share, 2, ratio, quarter).transpose(2, 0, 1, 3)
    value_sum = jnp.concatenate([value_sum.reshape(units, OWN), late_sum[:units]], axis=1)
    pair_sum = jnp.concatenate(
        [att_pair.run().total(), v_scatter.run().total(), late_sum[units:], ffn_sum[:, :half_units]],
        axis=1,
    )
    pair_sum = pair_sum.reshape(2, share, -1)
    mine = lax.dynamic_index_in_dim(pair_sum, core, 0, keepdims=False)
    theirs = swap(lax.dynamic_index_in_dim(pair_sum, 1 - core, 0, keepdims=False), 1)
    shard_mixer = jnp.stack(
        [
            in_order(1, mine[:, i * OWN : (i + 1) * OWN], theirs[:, i * OWN : (i + 1) * OWN], 1)
            for i in range(4)
        ]
    )
    shard_key = in_order(
        1,
        mine[:, 4 * OWN :].reshape(share, chips, 1, units),
        theirs[:, 4 * OWN :].reshape(share, chips, 1, units),
        2,
    ).reshape(share, 2 * half_units)
    return (
        output,
        input_gradient,
        shard_mixer,
        shard_key,
        value_sum,
        misc_sum[:, :256],
        misc_sum[:, 256:512].T,
        misc_sum[:, 512:530].T,
    )


def solution(mesh):
    in_specs = (
        P("dp", None),
        P(),
        P(None, "dp", None),
        P("dp", None),
        P("dp", None),
        P("dp", None),
        P(None, "dp"),
        P(None, "dp"),
        P("dp", None),
    )
    out_specs = (
        P("dp", None),
        P("dp", None),
        P(None, "dp", None),
        P("dp", None),
        P("dp", None),
        P("dp", None),
        P(None, "dp"),
        P(None, "dp"),
    )
    return jax.shard_map(local, mesh=mesh, in_specs=in_specs, out_specs=out_specs, check_vma=False)
```

```python
from functools import partial

import jax
import jax.numpy as jnp
from jax import lax
from jax.experimental import pallas as pl
from jax.experimental.pallas import tpu as pltpu
from jax.sharding import PartitionSpec as P

HEADS = 16
HEAD_SIZE = 64
DECAY_RANK = 64
RATE_RANK = 64
EMBED = 1024
OWN = EMBED // 2
PRECISE = lax.Precision.HIGHEST


CHUNK = 64
LANES = 256
GROUP_HEADS = 4
STEP_CHUNKS = 2
SMALL = pl.CostEstimate(flops=1, bytes_accessed=1, transcendentals=0)

NN = (((1,), (0,)), ((), ()))
NT = (((1,), (1,)), ((), ()))
TN = (((0,), (0,)), ((), ()))


def halves(x):
    high = x.astype(jnp.bfloat16)
    return high, (x - high.astype(jnp.float32)).astype(jnp.bfloat16)


def dot32(a, b, dims):
    return lax.dot_general(a, b, dims, preferred_element_type=jnp.float32)


def mul(left, right, dims=NN):
    rows = left[0].shape[0]
    both = dot32(jnp.concatenate(left, axis=0), right[0], dims)
    return both[:rows] + both[rows:] + dot32(left[0], right[1], dims)


def tmul(left, right, masks):
    full = (
        dot32(left[0], right[0], TN) + dot32(left[1], right[0], TN) + dot32(left[0], right[1], TN)
    )
    return sum(full[h * CHUNK : (h + 1) * CHUNK] * masks[h][:1].astype(jnp.float32) for h in range(GROUP_HEADS))


def spread(pair, masks):
    return tuple(
        jnp.concatenate([part * masks[h] for h in range(GROUP_HEADS)], axis=0) for part in pair
    )


def stack(first, second):
    return tuple(jnp.concatenate([x, y], axis=0) for x, y in zip(first, second))


def head_masks():
    lane = lax.broadcasted_iota(jnp.int32, (CHUNK, LANES), 1) // CHUNK
    return [(lane == h).astype(jnp.float32).astype(jnp.bfloat16) for h in range(GROUP_HEADS)]


def places():
    row = lax.broadcasted_iota(jnp.int32, (CHUNK, LANES), 0)
    col = lax.broadcasted_iota(jnp.int32, (CHUNK, LANES), 1) % CHUNK
    return row, col


def running_sum(x, upper=False):
    row = lax.broadcasted_iota(jnp.int32, (CHUNK, CHUNK), 0)
    col = lax.broadcasted_iota(jnp.int32, (CHUNK, CHUNK), 1)
    ones = (row <= col if upper else col <= row).astype(jnp.float32).astype(jnp.bfloat16)
    high, rest = halves(x)
    low = (x - high.astype(jnp.float32) - rest.astype(jnp.float32)).astype(jnp.bfloat16)
    return dot32(ones, high, NN) + dot32(ones, rest, NN) + dot32(ones, low, NN)


def scaled_forms(q, w, k, a, b):
    total = running_sum(w)
    before = total - w
    middle = total[CHUNK // 2 - 1 : CHUNK // 2]
    end = total[CHUNK - 1 :]
    ea = jnp.exp(before - middle)
    eq = jnp.exp(total - middle)
    eb = jnp.exp(middle - total)
    ee = jnp.exp(end - total)
    return (a * ea, q * eq, b * eb, k * eb, b * ee, k * ee), (ea, eq, eb, ee), (jnp.exp(middle), jnp.exp(end))


def each(fn, *columns):
    return [fn(*row) for row in zip(*columns)]


def block_ones():
    row = lax.broadcasted_iota(jnp.int32, (LANES, LANES), 0) // CHUNK
    col = lax.broadcasted_iota(jnp.int32, (LANES, LANES), 1) // CHUNK
    return (row == col).astype(jnp.float32).astype(jnp.bfloat16)


def head_sum(x, ones):
    rows = x.shape[0]
    both = dot32(jnp.concatenate(halves(x), axis=0), ones, NN)
    return both[:rows] + both[rows:]


def prepared(keys, decay_low, rate_low, live, vec, ones):
    sig = jax.nn.sigmoid(vec[0] + decay_low)
    log_decay = (-0.6065306597126334) * sig * live
    rates = jax.nn.sigmoid(vec[1] + rate_low)
    scaled = keys * vec[2]
    inverse = lax.rsqrt(head_sum(scaled * scaled, ones) + 1e-06)
    unit_keys = scaled * inverse
    factor = (1.0 + (rates - 1.0) * vec[3]) * live
    return log_decay, keys * factor, -unit_keys, unit_keys * rates * live, sig, rates, inverse, factor


def read_out(o, q, k, v, vec, ones):
    centred = o - head_sum(o, ones) * (1.0 / CHUNK)
    scale = lax.rsqrt(head_sum(centred * centred, ones) * (1.0 / CHUNK) + 0.00064)
    normed = centred * scale
    weight = head_sum(q * k * vec[4], ones)
    return normed, scale, weight, normed * vec[5] + vec[6] + weight * v


def unit_slices():
    return [
        (slice(c * CHUNK, (c + 1) * CHUNK), slice(g * LANES, (g + 1) * LANES))
        for c in range(STEP_CHUNKS)
        for g in range(2)
    ]


def unit_live(length, step):
    row = lax.broadcasted_iota(jnp.int32, (CHUNK, LANES), 0)
    start = step * (STEP_CHUNKS * CHUNK)
    live = [(row + (start + c * CHUNK) < length).astype(jnp.float32) for c in range(STEP_CHUNKS)]
    return [live[c] for c in range(STEP_CHUNKS) for g in range(2)]


def unit_vectors(vec_ref):
    vec = [[vec_ref[i : i + 1, g * LANES : (g + 1) * LANES] for i in range(7)] for g in range(2)]
    return [vec[g] for c in range(STEP_CHUNKS) for g in range(2)]


def forward_kernel(base, *refs):
    len_ref, vec_ref, start_ref, q_ref, keys_ref, v_ref, dl_ref, rl_ref, gate_ref = refs[:9]
    (
        out_ref, o_ref, t_ref, aqb_ref, aak_ref, aqk_ref, y_ref, z_ref, trt_ref, qe_ref, state_ref,
    ) = refs[-11:]

    @pl.when(pl.program_id(0) == 0)
    def _():
        state_ref[...] = start_ref[...]

    masks = head_masks()
    row, col = places()
    strict = (col < row).astype(jnp.float32)
    within = (col <= row).astype(jnp.float32)
    eye = (col == row).astype(jnp.float32)
    ones = block_ones()
    units = unit_slices()
    live = unit_live(len_ref[0], pl.program_id(0) + base)
    vec = unit_vectors(vec_ref)
    load = lambda ref: [ref[u] for u in units]
    q, keys, v = load(q_ref), load(keys_ref), load(v_ref)
    ready = each(
        lambda x, y, z, m, n: prepared(x, y, z, m, n, ones), keys, load(dl_ref), load(rl_ref), live, vec
    )
    w, k, a, b = ([x[i] for x in ready] for i in range(4))
    forms = each(scaled_forms, q, w, k, a, b)
    ah, qh, bh, kh, bt, kt = ([f[0][i] for f in forms] for i in range(6))
    emid = [f[2][0] for f in forms]
    eend = [f[2][1] for f in forms]
    aq = each(lambda x, y: halves(jnp.concatenate([x, y], axis=0)), ah, qh)
    with_b = each(lambda l, r: mul(l, spread(halves(r), masks), NT), aq, bh)
    with_k = each(lambda l, r: mul(l, spread(halves(r), masks), NT), aq, kh)
    aab = [x[:CHUNK] * strict for x in with_b]
    aqb = [halves(x[CHUNK:] * within) for x in with_b]
    aak = [halves(x[:CHUNK] * strict) for x in with_k]
    aqk = [halves(x[CHUNK:] * within) for x in with_k]
    p = [halves(x * (row // 8 == col // 8)) for x in aab]
    t = [eye + x * (row // 8 == col // 8) for x in aab]
    p2 = each(lambda x: halves(mul(x, spread(x, masks))), p)
    both = each(lambda x, y: mul(stack(x, halves(y)), spread(x, masks)), p2, t)
    p4 = [halves(x[:CHUNK]) for x in both]
    t = each(lambda x, y: x + y[CHUNK:], t, both)
    t = each(lambda x, y: x + mul(halves(x), spread(y, masks)), t, p4)
    for size in (8, 16, 32):
        corner = ((row // size) % 2 == 1) & (col // size == row // size - 1)
        ts = [halves(x) for x in t]
        n = [halves(x * corner) for x in aab]
        tn = each(lambda x, y: halves(mul(x, spread(y, masks))), ts, n)
        t = each(lambda x, y, z: x + mul(y, spread(z, masks)), t, tn, ts)
    ts = [halves(x) for x in t]
    vs = [halves(x) for x in v]
    vm = [spread(x, masks) for x in vs]
    wide = each(lambda x, y, e: mul(x, spread(halves(y * e), masks)), ts, ah, emid)
    r0 = each(mul, aak, vm)
    y0 = each(lambda x, y: mul(x, spread(halves(y), masks)), ts, r0)
    wides = [halves(x) for x in wide]
    qe = each(lambda x, e, y, z: x * e + mul(y, spread(z, masks)), qh, emid, aqb, wides)
    y0s = [halves(x) for x in y0]
    part = each(lambda x, y, z, u: mul(x, spread(y, masks)) + mul(z, u), aqb, y0s, aqk, vm)
    bts = [halves(x) for x in bt]
    diag = [eye * e for e in eend]
    tr = each(lambda x, y, d: tmul(x, y, masks) + d, bts, wides, diag)
    trt = each(lambda x, y, d: tmul(y, x, masks) + d, bts, wides, diag)
    inject = each(lambda x, y, z, u: tmul(stack(x, halves(y)), stack(z, u), masks), bts, kt, y0s, vs)
    wq = each(lambda x, y: stack(x, halves(y)), wides, qe)
    z = []
    out = []
    for c in range(STEP_CHUNKS):
        for g in range(2):
            i = c * 2 + g
            now = state_ref[g]
            nows = spread(halves(now), masks)
            state_ref[g] = mul(halves(tr[i]), nows) + inject[i]
            z.append(now)
            out.append(mul(wq[i], nows))
    o = each(lambda x, y: x[CHUNK:] + y, out, part)
    mixed = each(lambda x, y, z, m, n: read_out(x, y, z, m, n, ones)[3], o, q, k, v, vec)
    for i, u in enumerate(units):
        out_ref[u] = (mixed[i] * gate_ref[u]).astype(jnp.bfloat16)
        o_ref[u] = o[i]
        y_ref[u] = out[i][:CHUNK] + y0[i]
        t_ref[u] = t[i]
        aqb_ref[u] = with_b[i][CHUNK:] * within
        aak_ref[u] = with_k[i][:CHUNK] * strict
        aqk_ref[u] = with_k[i][CHUNK:] * within
        z_ref[u] = z[i]
        trt_ref[u] = trt[i]
        qe_ref[u] = qe[i]


def backward_kernel(base, *refs):
    (
        len_ref, vec_ref, start_ref, sums_ref, q_ref, keys_ref, v_ref, dl_ref, rl_ref, gate_ref,
        g_ref, o_ref, t_ref, aqb_ref, aak_ref, aqk_ref, y_ref, z_ref, trt_ref, qe_ref,
    ) = refs[:20]
    dq_ref, dkeys_ref, dv_ref, ddl_ref, drl_ref, dgate_ref, dvec_ref, state_ref = refs[-8:]
    step = base + pl.num_programs(0) - 1 - pl.program_id(0)

    @pl.when(pl.program_id(0) == 0)
    def _():
        state_ref[...] = start_ref[...]
        dvec_ref[...] = sums_ref[...]

    masks = head_masks()
    row, col = places()
    strict = (col < row).astype(jnp.float32)
    within = (col <= row).astype(jnp.float32)
    ones = block_ones()
    units = unit_slices()
    live = unit_live(len_ref[0], step)
    vec = unit_vectors(vec_ref)
    load = lambda ref: [ref[u] for u in units]
    q, keys, v, g = load(q_ref), load(keys_ref), load(v_ref), load(g_ref)
    ready = each(
        lambda x, y, z, m, n: prepared(x, y, z, m, n, ones), keys, load(dl_ref), load(rl_ref), live, vec
    )
    w, k, a, b, sig, rates, inverse, factor = ([x[i] for x in ready] for i in range(8))
    seen = each(lambda x, y, z, m, n: read_out(x, y, z, m, n, ones), load(o_ref), q, k, v, vec)
    normed, scale, weight, mixed = ([x[i] for x in seen] for i in range(4))
    gate = load(gate_ref)
    dgate = each(lambda x, y: x * y, g, mixed)
    dmix = each(lambda x, y: x * y, g, gate)
    dn = each(lambda x, n: x * n[5], dmix, vec)
    do = each(
        lambda x, n, r: r
        * (x - head_sum(x, ones) * (1.0 / CHUNK) - n * (head_sum(x * n, ones) * (1.0 / CHUNK))),
        dn, normed, scale,
    )
    dweight = each(lambda x, y: head_sum(x * y, ones), dmix, v)
    do = [halves(x) for x in do]
    qe, trt, t, aqb, aak, aqk, ys = (
        [halves(x) for x in load(ref)]
        for ref in (qe_ref, trt_ref, t_ref, aqb_ref, aak_ref, aqk_ref, y_ref)
    )
    z = load(z_ref)
    vs = [halves(x) for x in v]
    h = each(lambda x, y: tmul(x, y, masks), qe, do)
    dz = [None] * len(units)
    for c in reversed(range(STEP_CHUNKS)):
        for g in range(2):
            i = c * 2 + g
            now = state_ref[g]
            dz[i] = now
            state_ref[g] = mul(trt[i], spread(halves(now), masks)) + h[i]
    dzs = [spread(halves(x), masks) for x in dz]
    zs = [spread(halves(x), masks) for x in z]
    forms = each(scaled_forms, q, w, k, a, b)
    ah, qh, bh, kh, bt, kt = ([f[0][i] for f in forms] for i in range(6))
    ea, eq, eb, ee = ([f[1][i] for f in forms] for i in range(4))
    emid = [f[2][0] for f in forms]
    eend = [f[2][1] for f in forms]
    from_end = each(lambda x, y, s: mul(halves(jnp.concatenate([x, y], axis=0)), s), bt, kt, dzs)
    dy = each(lambda x, y, s: halves(tmul(x, y, masks) + s[:CHUNK]), aqb, do, from_end)
    dr = each(lambda x, y: halves(tmul(x, y, masks)), t, dy)
    ro = each(stack, dr, do)
    dv = each(lambda x, y, s, f: tmul(stack(x, y), s, masks) + f[CHUNK:], aak, aqk, ro, from_end)
    mask2 = jnp.concatenate([strict, within], axis=0)
    dab = each(lambda s, y: halves(mul(s, spread(y, masks), NT) * mask2), ro, ys)
    dak = each(lambda s, y: halves(mul(s, spread(y, masks), NT) * mask2), ro, vs)
    dst = each(lambda s, y: mul(s, y, NT), ro, zs)
    daq = each(
        lambda s, e, x, bb, y, kk: s * e + mul(x, spread(halves(bb), masks)) + mul(y, spread(halves(kk), masks)),
        dst, emid, dab, bh, dak, kh,
    )
    aq = each(lambda x, y: halves(jnp.concatenate([x, y], axis=0)), ah, qh)
    dbh = each(lambda x, y: tmul(x, y, masks), dab, aq)
    dkh = each(lambda x, y: tmul(x, y, masks), dak, aq)
    dend = each(lambda y, x, s: mul(stack(y, x), s, NT), ys, vs, dzs)
    row_of_ones = jnp.ones((8, LANES), jnp.bfloat16)
    sums = lambda x: jnp.sum(x, axis=0, keepdims=True)
    for i, u in enumerate(units):
        da = daq[i][:CHUNK] * ea[i]
        dq = daq[i][CHUNK:] * eq[i]
        dbt = dend[i][:CHUNK] * ee[i]
        dkt = dend[i][CHUNK:] * ee[i]
        db = dbh[i] * eb[i] + dbt
        dk = dkh[i] * eb[i] + dkt
        pa = da * a[i]
        diff = dq * q[i] - db * b[i] - dk * k[i] + pa
        zz = spread(halves(z[i] * dz[i]), masks)
        carry = (dot32(row_of_ones, zz[0], NT) + dot32(row_of_ones, zz[1], NT))[:1] * eend[i]
        carry = carry + sums(dbt * b[i] + dkt * k[i])
        dw = running_sum(diff, upper=True) - pa + carry
        from_bonus = dweight[i] * vec[i][4]
        dk = dk + from_bonus * q[i]
        dq_ref[u] = (dq + from_bonus * k[i]).astype(jnp.bfloat16)
        dv_ref[u] = (dv[i] + weight[i] * dmix[i]).astype(jnp.bfloat16)
        dgate_ref[u] = dgate[i].astype(jnp.bfloat16)
        unit_keys = -a[i]
        db = db * live[i]
        du = db * rates[i] - da
        dscaled = inverse[i] * (du - unit_keys * head_sum(du * unit_keys, ones))
        dkl = dk * keys[i] * live[i]
        drl = (db * unit_keys + dkl * vec[i][3]) * rates[i] * (1.0 - rates[i])
        ddl = dw * w[i] * (1.0 - sig[i])
        dkeys_ref[u] = (dk * factor[i] + dscaled * vec[i][2]).astype(jnp.bfloat16)
        ddl_ref[u] = ddl.astype(jnp.bfloat16)
        drl_ref[u] = drl.astype(jnp.bfloat16)
        parts = (
            ddl, drl, dscaled * keys[i], dkl * (rates[i] - 1.0),
            dweight[i] * q[i] * k[i], dmix[i] * normed[i], dmix[i],
        )
        lanes = u[1]
        for j, x in enumerate(parts):
            dvec_ref[j : j + 1, lanes] += sums(x)


def wkv_call(kernel, base, steps, small, arrays, outs, sums, previous, name):
    tokens, width = arrays[0].shape
    rows = CHUNK * STEP_CHUNKS
    last = base + steps - 1
    turned = kernel is backward_kernel
    spec = pl.BlockSpec((rows, width), lambda i: (last - i if turned else base + i, 0))
    state = pl.BlockSpec((2, CHUNK, LANES), lambda i: (0, 0, 0))
    whole = pl.BlockSpec((8, width), lambda i: (0, 0))
    shape = jax.ShapeDtypeStruct
    first = [pl.BlockSpec(memory_space=pltpu.SMEM), whole, state] + [whole] * sums
    held = list(previous or ())
    start = len(first) + len(arrays)
    return pl.pallas_call(
        partial(kernel, base),
        grid=(steps,),
        in_specs=first + [spec] * len(arrays) + [pl.BlockSpec(memory_space=pl.ANY)] * len(held),
        out_specs=[spec] * len(outs) + [whole] * sums + [state],
        out_shape=[shape((tokens, width), dtype) for dtype in outs]
        + [shape((8, width), jnp.float32)] * sums
        + [shape((2, CHUNK, LANES), jnp.float32)],
        input_output_aliases={start + i: i for i in range(len(held))},
        compiler_params=pltpu.CompilerParams(vmem_limit_bytes=56 << 20),
        cost_estimate=SMALL,
        name=name,
    )(*small, *arrays, *held)


def wkv_forward(base, steps, length, vec, state, arrays, previous=None):
    outs = [jnp.bfloat16] + [jnp.float32] * 9
    return wkv_call(
        forward_kernel, base, steps, (length, vec, state), arrays, outs, 0, previous, "wkv_forward"
    )


def wkv_backward(base, steps, length, vec, state, sums, arrays, previous=None):
    outs = [jnp.bfloat16] * 6
    return wkv_call(
        backward_kernel, base, steps, (length, vec, state, sums), arrays, outs, 1, previous,
        "wkv_backward",
    )


ROWS = 128


def row_norm(x):
    centred = x - jnp.mean(x, axis=-1, keepdims=True)
    scale = lax.rsqrt(jnp.mean(centred * centred, axis=-1, keepdims=True) + 1e-05)
    return centred * scale, scale


def shifted(x, edge, down):
    rows = x.shape[0]
    row = lax.broadcasted_iota(jnp.int32, x.shape, 0)
    if down:
        return jnp.where(row == 0, edge, pltpu.roll(x, 1, 0))
    return jnp.where(row == rows - 1, edge, pltpu.roll(x, rows - 1, 0))


def below(x, upper):
    lane = lax.broadcasted_iota(jnp.int32, x.shape, 1)
    keep = (lane >= DECAY_RANK) if upper else (lane < DECAY_RANK)
    return jnp.where(keep, x, jnp.zeros_like(x))


def front_kernel(
    x_ref, vec_ref, wr_ref, wk_ref, wv_ref, down_ref, up_ref,
    m0_ref, m1_ref, m2_ref, m3_ref, m4_ref, m5_ref,
    q_ref, k_ref, v_ref, dl_ref, rl_ref, gate_ref, hid_ref,
    edge_ref,
):
    @pl.when(pl.program_id(0) == 0)
    def _():
        edge_ref[...] = jnp.zeros_like(edge_ref)

    unit, _ = row_norm(x_ref[...].astype(jnp.float32))
    normed = unit * vec_ref[12:13] + vec_ref[13:14]
    change = shifted(normed, edge_ref[:1], True) - normed
    edge_ref[:1] = normed[ROWS - 1 :]
    mixes = []
    for j, ref in enumerate((m0_ref, m1_ref, m2_ref, m3_ref, m4_ref, m5_ref)):
        mixes.append((normed + change * vec_ref[j : j + 1]).astype(jnp.bfloat16))
        ref[...] = mixes[j]
    q_ref[...] = dot32(mixes[0], wr_ref[...], NN)
    k_ref[...] = dot32(mixes[2], wk_ref[...], NN)
    v_ref[...] = dot32(mixes[3], wv_ref[...], NN)
    first = down_ref[:, :128]
    pre_decay, pre_rate = dot32(mixes[1], first, NN), dot32(mixes[4], first, NN)
    pre_gate = dot32(mixes[5], down_ref[:, 128:], NN)
    lane = lax.broadcasted_iota(jnp.int32, pre_decay.shape, 1)
    pair = jnp.where(lane < DECAY_RANK, jnp.tanh(pre_decay), pre_rate)
    gate = jax.nn.sigmoid(pre_gate)
    hid_ref[:, :128] = pair
    hid_ref[:, 128:] = gate
    narrow_pair = pair.astype(jnp.bfloat16)
    dl_ref[...] = dot32(below(narrow_pair, False), up_ref[:, :128], NT)
    rl_ref[...] = dot32(below(narrow_pair, True), up_ref[:, :128], NT)
    gate_ref[...] = dot32(gate.astype(jnp.bfloat16), up_ref[:, 128:], NT)


def front_forward(x, vectors, w_r, w_k, w_v, down, up):
    tokens, width = x.shape
    wide = pl.BlockSpec((ROWS, width), lambda i: (i, 0))
    own = pl.BlockSpec((ROWS, OWN), lambda i: (i, 0))
    hid = pl.BlockSpec((ROWS, 256), lambda i: (i, 0))
    whole = lambda a: pl.BlockSpec(a.shape, lambda i: (0, 0))
    shape = jax.ShapeDtypeStruct
    return pl.pallas_call(
        front_kernel,
        grid=(tokens // ROWS,),
        in_specs=[wide] + [whole(a) for a in (vectors, w_r, w_k, w_v, down, up)],
        out_specs=[wide] * 6 + [own] * 6 + [hid],
        out_shape=[shape((tokens, width), jnp.bfloat16)] * 6
        + [shape((tokens, OWN), jnp.float32)] * 6
        + [shape((tokens, 256), jnp.float32)],
        scratch_shapes=[pltpu.VMEM((8, width), jnp.float32)],
        compiler_params=pltpu.CompilerParams(vmem_limit_bytes=48 << 20),
        cost_estimate=SMALL,
        name="front_forward",
    )(x, vectors, w_r, w_k, w_v, down, up)


def front_back_kernel(
    x_ref, before_ref, vec_ref, wr_ref, wk_ref, wv_ref, down_ref, up_ref,
    m1_ref, m4_ref, m5_ref, hid_ref,
    dq_ref, dk_ref, dv_ref, ddl_ref, drl_ref, dgate_ref, own_vec_ref, ffn_vec_ref,
    dx_ref, misc_ref,
    edge_ref, sums_ref,
):
    step = pl.num_programs(0) - 1 - pl.program_id(0)
    core = lax.axis_index("dp") % 2
    own_start = pl.multiple_of(core * OWN, OWN)

    @pl.when(pl.program_id(0) == 0)
    def _():
        edge_ref[...] = jnp.zeros_like(edge_ref)
        sums_ref[...] = jnp.zeros_like(sums_ref)
        misc_ref[...] = jnp.zeros_like(misc_ref)

    unit, scale = row_norm(x_ref[...].astype(jnp.float32))
    gain, offset = vec_ref[12:13], vec_ref[13:14]
    normed = unit * gain + offset
    tail, _ = row_norm(before_ref[...].astype(jnp.float32))
    edge = (tail[15:] * gain + offset) * jnp.where(step == 0, 0.0, 1.0)
    change = shifted(normed, edge, True) - normed
    ddl, drl, dgate = ddl_ref[...], drl_ref[...], dgate_ref[...]
    hid = hid_ref[...]
    pair, gate = hid[:, :128], hid[:, 128:]
    lane = lax.broadcasted_iota(jnp.int32, pair.shape, 1)
    first_up, last_up = up_ref[:, :128], up_ref[:, 128:]
    pair_grad = jnp.where(
        lane < DECAY_RANK,
        dot32(ddl, first_up, NN) * (1.0 - pair * pair),
        dot32(drl, first_up, NN),
    ).astype(jnp.bfloat16)
    gate_grad = (dot32(dgate, last_up, NN) * gate * (1.0 - gate)).astype(jnp.bfloat16)
    narrow_pair, narrow_gate = pair.astype(jnp.bfloat16), gate.astype(jnp.bfloat16)
    own_rows = pl.ds(own_start, OWN)
    misc_ref[own_rows, 256:384] += dot32(ddl, below(narrow_pair, False), TN) + dot32(
        drl, below(narrow_pair, True), TN
    )
    misc_ref[own_rows, 384:512] += dot32(dgate, narrow_gate, TN)
    decay_part, rate_part = below(pair_grad, False), below(pair_grad, True)
    misc_ref[:, :128] += dot32(m1_ref[...], decay_part, TN) + dot32(m4_ref[...], rate_part, TN)
    misc_ref[:, 128:256] += dot32(m5_ref[...], gate_grad, TN)
    first_down = down_ref[:, :128]
    grads = (
        lambda: dot32(dq_ref[...], wr_ref[...], NT),
        lambda: dot32(decay_part, first_down, NT),
        lambda: dot32(dk_ref[...], wk_ref[...], NT),
        lambda: dot32(dv_ref[...], wv_ref[...], NT),
        lambda: dot32(rate_part, first_down, NT),
        lambda: dot32(gate_grad, down_ref[:, 128:], NT),
    )
    total = jnp.zeros_like(change)
    moved = jnp.zeros_like(change)
    for j, grad in enumerate(grads):
        now = grad()
        total = total + now
        moved = moved + now * vec_ref[j : j + 1]
        sums_ref[j : j + 1] += jnp.sum(now * change, axis=0, keepdims=True)
    dnormed = total - moved + shifted(moved, edge_ref[:1], False)
    edge_ref[:1] = moved[:1]
    sums_ref[12:13] += jnp.sum(dnormed * unit, axis=0, keepdims=True)
    sums_ref[13:14] += jnp.sum(dnormed, axis=0, keepdims=True)
    dunit = dnormed * gain
    dx_ref[...] = scale * (
        dunit
        - jnp.mean(dunit, axis=-1, keepdims=True)
        - unit * jnp.mean(dunit * unit, axis=-1, keepdims=True)
    )

    @pl.when(step == 0)
    def _():
        sums_ref[6:7] = ffn_vec_ref[0:1] * 0.5
        sums_ref[14:16] = ffn_vec_ref[1:3] * 0.5
        zeros = jnp.zeros((1, OWN), jnp.float32)
        for target, source in ((7, 0), (8, 1), (9, 2), (10, 3), (11, 4), (16, 5), (17, 6)):
            mine = own_vec_ref[source : source + 1]
            sums_ref[target : target + 1] = jnp.concatenate(
                [jnp.where(core == 0, mine, zeros), jnp.where(core == 0, zeros, mine)], axis=1
            )
        for block in range(EMBED // 128):
            lanes = slice(block * 128, (block + 1) * 128)
            misc_ref[lanes, 512:640] = sums_ref[:, lanes].T


def front_backward(
    x, vectors, w_r, w_k, w_v, down, up, mixes, hid, grads, own_vec, ffn_vec
):
    tokens, width = x.shape
    steps = tokens // ROWS
    wide = pl.BlockSpec((ROWS, width), lambda i: (steps - 1 - i, 0))
    before = pl.BlockSpec(
        (16, width), lambda i: (jnp.maximum((steps - 1 - i) * (ROWS // 16) - 1, 0), 0)
    )
    own = pl.BlockSpec((ROWS, OWN), lambda i: (steps - 1 - i, 0))
    hid_spec = pl.BlockSpec((ROWS, 256), lambda i: (steps - 1 - i, 0))
    whole = lambda a: pl.BlockSpec(a.shape, lambda i: (0, 0))
    shape = jax.ShapeDtypeStruct
    return pl.pallas_call(
        front_back_kernel,
        grid=(steps,),
        in_specs=[wide, before]
        + [whole(a) for a in (vectors, w_r, w_k, w_v, down, up)]
        + [wide] * 3
        + [hid_spec]
        + [own] * 6
        + [whole(own_vec), whole(ffn_vec)],
        out_specs=[wide, pl.BlockSpec((EMBED, 640), lambda i: (0, 0))],
        out_shape=[shape((tokens, width), jnp.float32), shape((EMBED, 640), jnp.float32)],
        scratch_shapes=[
            pltpu.VMEM((8, width), jnp.float32), pltpu.VMEM((128, width), jnp.float32),
        ],
        compiler_params=pltpu.CompilerParams(vmem_limit_bytes=48 << 20),
        cost_estimate=SMALL,
        name="front_backward",
    )(x, x, vectors, w_r, w_k, w_v, down, up, *mixes, hid, *grads, own_vec, ffn_vec)


def ffn_back_kernel(
    len_ref, res_ref, before_ref, cot_ref, mine_ref, other_ref, vec_ref, wo_ref,
    grad_ref, narrow_ref, gated_ref, dvec_ref,
    edge_ref,
):
    step = pl.num_programs(0) - 1 - pl.program_id(0)

    @pl.when(pl.program_id(0) == 0)
    def _():
        edge_ref[...] = jnp.zeros_like(edge_ref)
        dvec_ref[...] = jnp.zeros_like(dvec_ref)

    gain, offset, coefficient = vec_ref[14:15], vec_ref[15:16], vec_ref[6:7]
    unit, scale = row_norm(res_ref[...])
    normed = unit * gain + offset
    tail, _ = row_norm(before_ref[...])
    edge = (tail[7:] * gain + offset) * jnp.where(step == 0, 0.0, 1.0)
    change = shifted(normed, edge, True) - normed
    grad = mine_ref[...].astype(jnp.float32) + other_ref[...].astype(jnp.float32)
    moved = grad * coefficient
    dnormed = grad - moved + shifted(moved, edge_ref[:1], False)
    edge_ref[:1] = moved[:1]
    sums = lambda x: jnp.sum(x, axis=0, keepdims=True)
    dvec_ref[0:1] += sums(grad * change)
    dvec_ref[1:2] += sums(dnormed * unit)
    dvec_ref[2:3] += sums(dnormed)
    dunit = dnormed * gain
    row = lax.broadcasted_iota(jnp.int32, grad.shape, 0) + step * ROWS
    out_grad = jnp.where(row < len_ref[0], cot_ref[...].astype(jnp.float32), 0.0)
    total = out_grad + scale * (
        dunit
        - jnp.mean(dunit, axis=-1, keepdims=True)
        - unit * jnp.mean(dunit * unit, axis=-1, keepdims=True)
    )
    grad_ref[...] = total
    small = total.astype(jnp.bfloat16)
    narrow_ref[...] = small
    gated_ref[...] = dot32(small, wo_ref[...], NT)


def ffn_backward(length, residual, cot, mine, other, vectors, w_o_rows):
    tokens, width = residual.shape
    steps = tokens // ROWS
    wide = pl.BlockSpec((ROWS, width), lambda i: (steps - 1 - i, 0))
    before = pl.BlockSpec(
        (8, width), lambda i: (jnp.maximum((steps - 1 - i) * (ROWS // 8) - 1, 0), 0)
    )
    own = pl.BlockSpec((ROWS, OWN), lambda i: (steps - 1 - i, 0))
    whole = lambda a: pl.BlockSpec(a.shape, lambda i: (0, 0))
    shape = jax.ShapeDtypeStruct
    return pl.pallas_call(
        ffn_back_kernel,
        grid=(steps,),
        in_specs=[pl.BlockSpec(memory_space=pltpu.SMEM), wide, before]
        + [wide] * 3
        + [whole(vectors), whole(w_o_rows)],
        out_specs=[wide, wide, own, pl.BlockSpec((8, width), lambda i: (0, 0))],
        out_shape=[
            shape((tokens, width), jnp.float32),
            shape((tokens, width), jnp.bfloat16),
            shape((tokens, OWN), jnp.float32),
            shape((8, width), jnp.float32),
        ],
        scratch_shapes=[pltpu.VMEM((8, width), jnp.float32)],
        compiler_params=pltpu.CompilerParams(vmem_limit_bytes=48 << 20),
        cost_estimate=SMALL,
        name="ffn_backward",
    )(length, residual, residual, cot, mine, other, vectors, w_o_rows)


def att_grad_kernel(m0_ref, m2_ref, m3_ref, dq_ref, dk_ref, dv_ref, send_a, keep_a, send_b, keep_b):
    chip = lax.axis_index("dp") // 2
    by_x, by_y = chip % 2 == 0, (chip // 2) % 2 == 0
    quarter = OWN // 2
    dv = dv_ref[...]
    first = ((m0_ref, dq_ref[...], 0, OWN), (m3_ref, dv[:, :quarter], OWN, quarter))
    second = ((m2_ref, dk_ref[...], 0, OWN), (m3_ref, dv[:, quarter:], OWN, quarter))
    for z in range(4):
        rows = slice(z * 256, (z + 1) * 256)
        for left, right, lane, width in first:
            block = dot32(left[:, rows], right, TN).astype(jnp.bfloat16)
            lanes = slice(lane, lane + width)
            for y in range(2):
                low, high = block[y * 128 : y * 128 + 64], block[y * 128 + 64 : y * 128 + 128]
                send_a[2 * z + y, :, lanes] = jnp.where(by_x, high, low)
                keep_a[2 * z + y, :, lanes] = jnp.where(by_x, low, high)
        for left, right, lane, width in second:
            block = dot32(left[:, rows], right, TN).astype(jnp.bfloat16)
            lanes = slice(lane, lane + width)
            for x in range(2):
                low, high = block[x * 64 : x * 64 + 64], block[128 + x * 64 : 128 + x * 64 + 64]
                send_b[2 * z + x, :, lanes] = jnp.where(by_y, high, low)
                keep_b[2 * z + x, :, lanes] = jnp.where(by_y, low, high)


def att_gradients(mixes, grads):
    space = pl.BlockSpec(memory_space=pltpu.VMEM)
    return pl.pallas_call(
        att_grad_kernel,
        in_specs=[space] * 6,
        out_specs=[space] * 4,
        out_shape=[jax.ShapeDtypeStruct((8, 64, OWN + OWN // 2), jnp.bfloat16)] * 4,
        compiler_params=pltpu.CompilerParams(vmem_limit_bytes=40 << 20),
        cost_estimate=SMALL,
        name="att_gradients",
    )(*mixes, *grads)


def swap(block, mask):
    size = lax.axis_size("dp")
    return lax.ppermute(block, "dp", [(i, i ^ mask) for i in range(size)])


def bit_of(mask):
    return (lax.axis_index("dp") // mask) % 2


def in_order(mask, own, other, axis):
    lower = bit_of(mask) == 0
    return jnp.where(
        lower, jnp.concatenate([own, other], axis=axis), jnp.concatenate([other, own], axis=axis)
    )


def chip_masks():
    size = lax.axis_size("dp")
    masks = []
    while 2 << len(masks) < size:
        masks.append(2 << len(masks))
    return masks


def steps_of(kind):
    masks = chip_masks()
    near, far = [[mask] for mask in masks[:2]], masks[2:][::-1]
    single = [[mask] for mask in far]
    first = [[far[0], far[1], far[0] | far[1]]] if len(far) == 2 else single
    both = [[masks[0], masks[1], masks[0] | masks[1]]] if len(masks) > 1 else near
    return [first + near[::-1], first + near, near + first, first + both][kind]


def meet(movers, *arrays):
    held = lax.optimization_barrier(tuple(tuple(m.arrived) for m in movers) + arrays)
    for mover, arrived in zip(movers, held):
        mover.arrived = list(arrived)
    return held[len(movers) :]


class Gather:
    def __init__(self, block, kind, places=(0,)):
        self.steps = steps_of(kind)
        self.held = block[None]
        self.places = [0]
        self.arrived = []
        self.masks = []

    def merge(self):
        if self.arrived:
            self.held = jnp.concatenate([self.held] + self.arrived, axis=0)
            self.places = self.places + [p ^ (m // 2) for m in self.masks for p in self.places]
            self.arrived = []

    def step(self):
        if self.steps:
            self.merge()
            self.masks = self.steps.pop(0)
            self.arrived = [swap(self.held, mask) for mask in self.masks]
        return self

    def run(self):
        while self.steps:
            self.step()
        return self

    def split(self, kinds):
        width = self.held.shape[-1] // len(kinds)
        out = []
        for i, kind in enumerate(kinds):
            part = Gather.__new__(Gather)
            cut = slice(i * width, (i + 1) * width)
            part.steps = steps_of(kind)[len(steps_of(kind)) - len(self.steps) :]
            part.held = self.held[..., cut]
            part.arrived = [x[..., cut] for x in self.arrived]
            part.places, part.masks = self.places, self.masks
            out.append(part)
        return out


def place_kernel(places, cuts, *refs):
    sources, outs = refs[: len(places)], refs[len(places) :]
    chip = lax.axis_index("dp") // 2
    for source, (part, list_of) in zip(sources, places):
        for j, place in enumerate(list_of):
            for out, (first, rows, lanes) in zip(outs, cuts):
                start = pl.multiple_of((chip ^ place) * rows, rows)
                lane, width = lanes[part]
                at = sum(w for _, w in lanes[:part])
                out[pl.ds(start, rows), at : at + width] = source[
                    j, first : first + rows, lane : lane + width
                ]


def assemble(gathers, cuts=None):
    gathers = [g.run() for g in gathers]
    rows = gathers[0].held.shape[1]
    cuts = cuts or ((0, rows, [(0, g.held.shape[2]) for g in gathers]),)
    sources, places = [], []
    for i, g in enumerate(gathers):
        sources += [g.held] + g.arrived
        shifts = [0] + [mask // 2 for mask in g.masks]
        places += [(i, [p ^ shift for p in g.places]) for shift in shifts]
    count = lax.axis_size("dp") // 2
    if any(cut[1] % 16 for cut in cuts):
        return assemble_plain(sources, places, cuts, count)
    space = pl.BlockSpec(memory_space=pltpu.VMEM)
    return pl.pallas_call(
        partial(place_kernel, places, cuts),
        in_specs=[space] * len(sources),
        out_specs=[space] * len(cuts),
        out_shape=[
            jax.ShapeDtypeStruct((count * n, sum(w for _, w in lanes)), sources[0].dtype)
            for _, n, lanes in cuts
        ],
        compiler_params=pltpu.CompilerParams(vmem_limit_bytes=32 << 20),
        cost_estimate=SMALL,
        name="assemble",
    )(*sources)


def assemble_plain(sources, places, cuts, count):
    chip = lax.axis_index("dp") // 2
    parts = []
    for part in sorted({part for part, _ in places}):
        blocks = jnp.concatenate([x for x, (at, _) in zip(sources, places) if at == part])
        where = [p for at, list_of in places if at == part for p in list_of]
        blocks = jnp.stack([blocks[where.index(i)] for i in range(count)])
        parts.append(jnp.take(blocks, chip ^ lax.iota(jnp.int32, count), axis=0))
    return [
        jnp.concatenate(
            [x[:, first : first + n, at : at + w] for x, (at, w) in zip(parts, lanes)], axis=-1
        ).reshape(count * n, -1)
        for first, n, lanes in cuts
    ]


class Scatter:
    def __init__(self, parts, kind):
        self.steps = steps_of(kind)[::-1]
        self.axes = chip_masks()[::-1]
        shape = parts.shape[1:]
        self.sources = [parts.reshape((2,) * len(self.axes) + shape)]
        self.arrived = []

    def pick(self, mask, gone):
        out = []
        for x in self.sources:
            for place in reversed(range(len(self.axes))):
                axis = self.axes[place]
                if axis in gone:
                    which = bit_of(axis) if not mask & axis else 1 - bit_of(axis)
                    x = lax.dynamic_index_in_dim(x, which, place, keepdims=False)
            out.append(x)
        return out

    def merge(self):
        self.sources = self.sources + self.arrived
        self.arrived = []

    def step(self):
        if self.steps:
            self.merge()
            masks = self.steps.pop(0)
            gone = [axis for axis in self.axes if any(mask & axis for mask in masks)]
            sends = [
                sum(x.astype(jnp.float32) for x in self.pick(mask, gone)).astype(jnp.bfloat16)
                for mask in masks
            ]
            self.sources = self.pick(0, gone)
            self.axes = [axis for axis in self.axes if axis not in gone]
            self.sent = sends
            self.arrived = [swap(x, mask) for x, mask in zip(sends, masks)]
        return self

    def run(self):
        while self.steps:
            self.step()
        return self

    def total(self):
        self.merge()
        return sum(x.astype(jnp.float32) for x in self.sources)

    @classmethod
    def begun(cls, sent, kept, kind):
        out = cls.__new__(cls)
        out.steps = steps_of(kind)[::-1]
        masks = out.steps.pop(0)
        out.axes = [axis for axis in chip_masks()[::-1] if axis not in masks]
        out.sources = [kept.reshape((2,) * len(out.axes) + kept.shape[1:])]
        out.sent = [sent.reshape(out.sources[0].shape)]
        out.arrived = [swap(out.sent[0], masks[0])]
        return out

    @staticmethod
    def join(parts, rows):
        out = Scatter.__new__(Scatter)
        out.steps, out.axes, out.arrived = parts[0].steps, parts[0].axes, []
        pieces = []
        for part in parts:
            total = part.total()
            pieces += [total[..., at : at + rows, :] for at in range(0, total.shape[-2], rows)]
        out.sources = [jnp.concatenate(pieces, axis=-1)]
        return out


def norm_rows(features, gain_row, offset_row):
    average = jnp.mean(features, axis=-1, keepdims=True)
    centred = features - average
    variance = jnp.mean(centred * centred, axis=-1, keepdims=True)
    return centred * lax.rsqrt(variance + 1e-05) * gain_row + offset_row


def product(operand, weight_matrix):
    return jnp.dot(operand, weight_matrix, preferred_element_type=jnp.float32)


def input_gradient_rows(upstream_gradient, weight_matrix):
    return lax.dot_general(
        upstream_gradient,
        weight_matrix,
        (((1,), (1,)), ((), ())),
        preferred_element_type=jnp.float32,
    )


def weight_gradient(operand, upstream_gradient):
    return lax.dot_general(
        operand, upstream_gradient, (((0,), (0,)), ((), ())), preferred_element_type=jnp.float32
    )


def earlier(rows):
    return jnp.concatenate([jnp.zeros_like(rows[:1]), rows[:-1]], axis=0)


def ffn_mix(residual, vectors):
    second = norm_rows(residual, vectors[14], vectors[15])
    return second + (earlier(second) - second) * vectors[6]


def narrow(x):
    return x.astype(jnp.bfloat16)


def local(
    inputs,
    lengths,
    attention_projections,
    channel_key_weight,
    channel_value_weight,
    lowrank_down_weight,
    lowrank_up_weight,
    per_feature_parameters,
    cotangent,
):
    devices = lax.axis_size("dp")
    chips = devices // 2
    device = lax.axis_index("dp")
    chip, core = device // 2, device % 2
    row_count = inputs.shape[0]
    slots = 2 * row_count
    share = EMBED // devices
    pair_share = 2 * share
    units = channel_value_weight.shape[0]
    half_units = chips * units

    def own_cut(x, which):
        return lax.dynamic_slice_in_dim(x, which * OWN, OWN, x.ndim - 1)

    def own_rows(x, which):
        return lax.dynamic_slice_in_dim(x, which * row_count, row_count, 0)

    pair_rows = in_order(
        1,
        own_cut(attention_projections, core),
        swap(own_cut(attention_projections, 1 - core), 1),
        1,
    )
    lora = jnp.concatenate([lowrank_down_weight, lowrank_up_weight.T], axis=1)
    vector_rows = jnp.pad(per_feature_parameters.T, ((0, 0), (0, 128 - 18)))
    vector_rows = vector_rows.reshape(share // 4, OWN)
    first_rows = 3 * pair_share
    misc_rows = share + share // 4 + (share // 4) % 16
    block = jnp.concatenate(
        [
            pair_rows[:3].reshape(first_rows, OWN),
            lora,
            jnp.pad(vector_rows, ((0, (share // 4) % 16), (0, 0))),
        ],
        axis=0,
    )
    half = half_units // 2
    quarter = OWN // 2
    cores = [list(range(k, devices, 2)) for k in range(2)]
    first = Gather(block, 0).step()
    out_rows = jnp.concatenate([pair_rows[3, :share], pair_rows[3, share:]], axis=1)
    slow = lax.all_gather(
        jnp.concatenate([channel_value_weight, out_rows], axis=0), "dp", axis_index_groups=cores
    )
    key_in, raw, cot, _ = meet([], channel_key_weight, inputs, cotangent, pair_rows)
    key_cut = key_in.reshape(share, chips, 2, units)

    def key_columns(which):
        return lax.dynamic_index_in_dim(key_cut, which, 2, keepdims=False).reshape(share, half_units)

    key_rows = in_order(1, key_columns(core), swap(key_columns(1 - core), 1), 0)
    (key_rows,) = meet([first], key_rows)
    first = first.split((0, 1))
    for part in first:
        part.step()
    tokens = in_order(1, raw, swap(raw, 1), 0)
    cot = in_order(1, cot, swap(cot, 1), 0)
    tokens, cot, key_rows = meet(first, tokens, cot, key_rows)
    for part in first:
        part.step()
    key_part = Gather(key_rows, 0).step()
    (tokens,) = meet(first + [key_part], tokens)
    key_parts = key_part.split((0, 1))
    for part in key_parts:
        part.step()
    w_r, w_k, w_v, misc = assemble(
        first,
        [(i * pair_share, pair_share, [(0, quarter)] * 2) for i in range(3)]
        + [(first_rows, misc_rows, [(0, quarter)] * 2)],
    )
    misc = misc.reshape(chips, 1, misc_rows, OWN)
    misc = in_order(1, misc, swap(misc, 1), 1)
    lora = misc[:, :, :share].reshape(EMBED, OWN)
    down, up_t = lora[:, :256], lax.dynamic_slice_in_dim(lora[:, 256:], core * OWN, OWN, 0)
    vectors = misc[:, :, share : share + share // 4].reshape(EMBED, 128)[:, :18].T
    vectors = vectors.astype(jnp.float32)
    own_vectors = own_cut(vectors, core)
    used = jnp.concatenate([own_vectors[7:12], own_vectors[16:18], own_vectors[:1]], axis=0)
    length = lax.dynamic_index_in_dim(lengths, chip, 0)
    live = (lax.iota(jnp.int32, slots) < length)[:, None]

    *mixes, queries, keys, values, decay_low, rate_low, gate_rows, hid = front_forward(
        tokens, vectors, w_r, w_k, w_v, down, up_t
    )
    terms = meet(key_parts, queries, keys, values, decay_low, rate_low, gate_rows)
    for part in key_parts:
        part.step()
    blocks = slots // (CHUNK * STEP_CHUNKS)
    early = blocks // 2
    zero_state = jnp.zeros((2, CHUNK, LANES), jnp.float32)
    gated, *saved, _ = wkv_forward(0, blocks, length, used, zero_state, terms)
    gated, cot, tokens, slow = meet(key_parts, gated, cot, tokens, slow)
    gated_all = in_order(1, gated, swap(gated, 1), 1)
    (key_weight,) = assemble(key_parts)
    value_weight = slow[:, :units].reshape(half_units, EMBED)
    w_o_own = slow[:, units:]
    w_o_own = jnp.concatenate([w_o_own[..., :OWN], w_o_own[..., OWN:]], axis=1).reshape(EMBED, OWN)
    w_o = in_order(1, w_o_own, swap(w_o_own, 1), 1)
    residual = tokens.astype(jnp.float32) + product(gated_all, w_o)
    ffn_in = narrow(ffn_mix(residual, vectors))
    positive = jax.nn.relu(product(ffn_in, key_weight))
    hidden = narrow(jnp.square(positive))
    out_narrow = jnp.where(live, cot, jnp.zeros_like(cot))
    grad_value = narrow(weight_gradient(hidden, out_narrow))
    hidden, positive, out_narrow, grad_value = meet([], hidden, positive, out_narrow, grad_value)
    value_sum = lax.psum_scatter(
        grad_value, "dp", scatter_dimension=0, axis_index_groups=cores, tiled=True
    ).astype(jnp.float32)

    pre_narrow = narrow(2.0 * positive * input_gradient_rows(out_narrow, value_weight))
    ffn_in_grad = narrow(input_gradient_rows(pre_narrow, key_weight))
    other_grad = swap(ffn_in_grad, 1)
    grad_key = narrow(weight_gradient(ffn_in, pre_narrow)).reshape(chips, pair_share, half_units)
    residual_grad, attended_grad, gated_grad, ffn_vec = ffn_backward(
        length, residual, cot, ffn_in_grad, other_grad, vectors,
        lax.dynamic_slice_in_dim(w_o, core * OWN, OWN, 0),
    )
    grad_o = narrow(weight_gradient(gated_all, own_cut(attended_grad, core)))
    grad_o = grad_o.reshape(chips, pair_share, OWN)
    key_scatter = [
        Scatter(
            jnp.concatenate(
                [
                    grad_key[:, :, i * half : (i + 1) * half],
                    grad_o[:, :, i * quarter : (i + 1) * quarter],
                ],
                axis=-1,
            ),
            i,
        ).step()
        for i in range(2)
    ]
    gated_grad, *_ = meet([], gated_grad, *[x for m in key_scatter for x in m.sent])
    terms = [*terms, gated_grad, *saved]
    zero_sums = jnp.zeros((8, OWN), jnp.float32)
    *before, sums, state = wkv_backward(
        early, blocks - early, length, used, zero_state, zero_sums, terms
    )
    state, sums, hidden = meet(key_scatter, state, sums, hidden)
    for part in key_scatter:
        part.step()
    *low_grads, own_vec, _ = wkv_backward(0, early, length, used, state, sums, terms, before)
    *low_grads, own_vec = meet(key_scatter, *low_grads, own_vec)
    if pair_share == 64:
        sent_a, kept_a, sent_b, kept_b = att_gradients(
            (mixes[0], mixes[2], mixes[3]), low_grads[:3]
        )
        att_scatter = [Scatter.begun(sent_a, kept_a, 0), Scatter.begun(sent_b, kept_b, 1)]
    else:
        grads = [narrow(weight_gradient(mixes[m], g)) for m, g in zip((0, 2, 3), low_grads)]
        att_scatter = [
            Scatter(jnp.concatenate(x, axis=1).reshape(chips, pair_share, 3 * quarter), i).step()
            for i, x in enumerate(
                ((grads[0], grads[2][:, :quarter]), (grads[1], grads[2][:, quarter:]))
            )
        ]
    own_vec, *_ = meet([], own_vec, *[x for m in att_scatter for x in m.sent])
    ffn_scatter = Scatter.join(key_scatter, pair_share).step()
    token_part, misc_grad = front_backward(
        tokens, vectors, w_r, w_k, w_v, down, up_t, (mixes[1], mixes[4], mixes[5]), hid,
        low_grads, own_vec, ffn_vec,
    )
    token_part, misc_grad = meet(att_scatter, token_part, misc_grad)
    for part in att_scatter:
        part.step()
    misc_grad = misc_grad.reshape(chips, 2, share, 640)
    misc_mine = lax.dynamic_index_in_dim(misc_grad, core, 1, keepdims=False)
    misc_other = narrow(lax.dynamic_index_in_dim(misc_grad, 1 - core, 1, keepdims=False))
    misc_sum = misc_mine + swap(misc_other, 1).astype(jnp.float32)
    misc_sum = jnp.concatenate([misc_sum[..., :320], misc_sum[..., 320:]], axis=1)
    (misc_sum,) = meet([ffn_scatter], misc_sum)
    misc_scatter = Scatter(misc_sum, 3).step()
    (token_part,) = meet(att_scatter + [misc_scatter], token_part)
    last = Scatter.join(att_scatter + [misc_scatter], pair_share).step()
    ffn_part = product(hidden, value_weight)
    ffn_out = own_rows(ffn_part, core) + swap(own_rows(ffn_part, 1 - core), 1)
    output = narrow(jnp.where(own_rows(live, core), own_rows(residual, core) + ffn_out, 0.0))
    input_gradient = (
        own_rows(residual_grad, core)
        + own_rows(token_part, core)
        + swap(own_rows(token_part, 1 - core), 1)
    )
    ffn_sum = ffn_scatter.run().total()
    output, input_gradient, ffn_sum = meet([last], output, input_gradient, ffn_sum)
    last_sum = last.run().total()
    wide = 3 * quarter
    misc_sum = last_sum[:, 2 * wide :]
    misc_sum = jnp.concatenate([misc_sum[:share], misc_sum[share:]], axis=1)
    each_half = half + quarter
    pair_sum = jnp.concatenate(
        [
            last_sum[:, :OWN],
            last_sum[:, wide : wide + OWN],
            last_sum[:, OWN:wide],
            last_sum[:, wide + OWN : 2 * wide],
            ffn_sum[:, half:each_half],
            ffn_sum[:, each_half + half :],
            ffn_sum[:, :half],
            ffn_sum[:, each_half : each_half + half],
        ],
        axis=1,
    )
    pair_sum = pair_sum.reshape(2, share, -1)
    mine = lax.dynamic_index_in_dim(pair_sum, core, 0, keepdims=False)
    theirs = swap(lax.dynamic_index_in_dim(pair_sum, 1 - core, 0, keepdims=False), 1)
    shard_mixer = jnp.stack(
        [
            in_order(1, mine[:, i * OWN : (i + 1) * OWN], theirs[:, i * OWN : (i + 1) * OWN], 1)
            for i in range(4)
        ]
    )
    shard_key = in_order(
        1,
        mine[:, 4 * OWN :].reshape(share, chips, 1, units),
        theirs[:, 4 * OWN :].reshape(share, chips, 1, units),
        2,
    ).reshape(share, 2 * half_units)
    return (
        output,
        input_gradient,
        shard_mixer,
        shard_key,
        value_sum,
        misc_sum[:, :256],
        misc_sum[:, 256:512].T,
        misc_sum[:, 512:530].T,
    )


def solution(mesh):
    in_specs = (
        P("dp", None),
        P(),
        P(None, "dp", None),
        P("dp", None),
        P("dp", None),
        P("dp", None),
        P(None, "dp"),
        P(None, "dp"),
        P("dp", None),
    )
    out_specs = (
        P("dp", None),
        P("dp", None),
        P(None, "dp", None),
        P("dp", None),
        P("dp", None),
        P("dp", None),
        P(None, "dp"),
        P(None, "dp"),
    )
    return jax.shard_map(local, mesh=mesh, in_specs=in_specs, out_specs=out_specs, check_vma=False)
```

```python
from functools import partial

import jax
import jax.numpy as jnp
from jax import lax
from jax.experimental import pallas as pl
from jax.experimental.pallas import tpu as pltpu
from jax.sharding import PartitionSpec as P

HEADS = 16
HEAD_SIZE = 64
DECAY_RANK = 64
RATE_RANK = 64
EMBED = 1024
OWN = EMBED // 2
PRECISE = lax.Precision.HIGHEST


CHUNK = 64
LANES = 256
GROUP_HEADS = 4
STEP_CHUNKS = 2
SMALL = pl.CostEstimate(flops=1, bytes_accessed=1, transcendentals=0)

NN = (((1,), (0,)), ((), ()))
NT = (((1,), (1,)), ((), ()))
TN = (((0,), (0,)), ((), ()))


def halves(x):
    high = x.astype(jnp.bfloat16)
    return high, (x - high.astype(jnp.float32)).astype(jnp.bfloat16)


def dot32(a, b, dims):
    return lax.dot_general(a, b, dims, preferred_element_type=jnp.float32)


def mul(left, right, dims=NN):
    rows = left[0].shape[0]
    both = dot32(jnp.concatenate(left, axis=0), right[0], dims)
    return both[:rows] + both[rows:] + dot32(left[0], right[1], dims)


def tmul(left, right, masks):
    full = (
        dot32(left[0], right[0], TN) + dot32(left[1], right[0], TN) + dot32(left[0], right[1], TN)
    )
    return sum(full[h * CHUNK : (h + 1) * CHUNK] * masks[h][:1].astype(jnp.float32) for h in range(GROUP_HEADS))


def spread(pair, masks):
    return tuple(
        jnp.concatenate([part * masks[h] for h in range(GROUP_HEADS)], axis=0) for part in pair
    )


def stack(first, second):
    return tuple(jnp.concatenate([x, y], axis=0) for x, y in zip(first, second))


def head_masks():
    lane = lax.broadcasted_iota(jnp.int32, (CHUNK, LANES), 1) // CHUNK
    return [(lane == h).astype(jnp.float32).astype(jnp.bfloat16) for h in range(GROUP_HEADS)]


def places():
    row = lax.broadcasted_iota(jnp.int32, (CHUNK, LANES), 0)
    col = lax.broadcasted_iota(jnp.int32, (CHUNK, LANES), 1) % CHUNK
    return row, col


def running_sum(x, upper=False):
    row = lax.broadcasted_iota(jnp.int32, (CHUNK, CHUNK), 0)
    col = lax.broadcasted_iota(jnp.int32, (CHUNK, CHUNK), 1)
    ones = (row <= col if upper else col <= row).astype(jnp.float32).astype(jnp.bfloat16)
    high, rest = halves(x)
    low = (x - high.astype(jnp.float32) - rest.astype(jnp.float32)).astype(jnp.bfloat16)
    return dot32(ones, high, NN) + dot32(ones, rest, NN) + dot32(ones, low, NN)


def scaled_forms(q, w, k, a, b):
    total = running_sum(w)
    before = total - w
    middle = total[CHUNK // 2 - 1 : CHUNK // 2]
    end = total[CHUNK - 1 :]
    ea = jnp.exp(before - middle)
    eq = jnp.exp(total - middle)
    eb = jnp.exp(middle - total)
    ee = jnp.exp(end - total)
    return (a * ea, q * eq, b * eb, k * eb, b * ee, k * ee), (ea, eq, eb, ee), (jnp.exp(middle), jnp.exp(end))


def each(fn, *columns):
    return [fn(*row) for row in zip(*columns)]


def block_ones():
    row = lax.broadcasted_iota(jnp.int32, (LANES, LANES), 0) // CHUNK
    col = lax.broadcasted_iota(jnp.int32, (LANES, LANES), 1) // CHUNK
    return (row == col).astype(jnp.float32).astype(jnp.bfloat16)


def head_sum(x, ones):
    rows = x.shape[0]
    both = dot32(jnp.concatenate(halves(x), axis=0), ones, NN)
    return both[:rows] + both[rows:]


def prepared(keys, decay_low, rate_low, live, vec, ones):
    sig = jax.nn.sigmoid(vec[0] + decay_low)
    log_decay = (-0.6065306597126334) * sig * live
    rates = jax.nn.sigmoid(vec[1] + rate_low)
    scaled = keys * vec[2]
    inverse = lax.rsqrt(head_sum(scaled * scaled, ones) + 1e-06)
    unit_keys = scaled * inverse
    factor = (1.0 + (rates - 1.0) * vec[3]) * live
    return log_decay, keys * factor, -unit_keys, unit_keys * rates * live, sig, rates, inverse, factor


def read_out(o, q, k, v, vec, ones):
    centred = o - head_sum(o, ones) * (1.0 / CHUNK)
    scale = lax.rsqrt(head_sum(centred * centred, ones) * (1.0 / CHUNK) + 0.00064)
    normed = centred * scale
    weight = head_sum(q * k * vec[4], ones)
    return normed, scale, weight, normed * vec[5] + vec[6] + weight * v


def unit_slices():
    return [
        (slice(c * CHUNK, (c + 1) * CHUNK), slice(g * LANES, (g + 1) * LANES))
        for c in range(STEP_CHUNKS)
        for g in range(2)
    ]


def unit_live(length, step):
    row = lax.broadcasted_iota(jnp.int32, (CHUNK, LANES), 0)
    start = step * (STEP_CHUNKS * CHUNK)
    live = [(row + (start + c * CHUNK) < length).astype(jnp.float32) for c in range(STEP_CHUNKS)]
    return [live[c] for c in range(STEP_CHUNKS) for g in range(2)]


def unit_vectors(vec_ref):
    vec = [[vec_ref[i : i + 1, g * LANES : (g + 1) * LANES] for i in range(7)] for g in range(2)]
    return [vec[g] for c in range(STEP_CHUNKS) for g in range(2)]


def forward_kernel(base, *refs):
    len_ref, vec_ref, start_ref, q_ref, keys_ref, v_ref, dl_ref, rl_ref, gate_ref = refs[:9]
    (
        out_ref, o_ref, t_ref, aqb_ref, aak_ref, aqk_ref, y_ref, z_ref, trt_ref, qe_ref, state_ref,
    ) = refs[-11:]

    @pl.when(pl.program_id(0) == 0)
    def _():
        state_ref[...] = start_ref[...]

    masks = head_masks()
    row, col = places()
    strict = (col < row).astype(jnp.float32)
    within = (col <= row).astype(jnp.float32)
    eye = (col == row).astype(jnp.float32)
    ones = block_ones()
    units = unit_slices()
    live = unit_live(len_ref[0], pl.program_id(0) + base)
    vec = unit_vectors(vec_ref)
    load = lambda ref: [ref[u] for u in units]
    q, keys, v = load(q_ref), load(keys_ref), load(v_ref)
    ready = each(
        lambda x, y, z, m, n: prepared(x, y, z, m, n, ones), keys, load(dl_ref), load(rl_ref), live, vec
    )
    w, k, a, b = ([x[i] for x in ready] for i in range(4))
    forms = each(scaled_forms, q, w, k, a, b)
    ah, qh, bh, kh, bt, kt = ([f[0][i] for f in forms] for i in range(6))
    emid = [f[2][0] for f in forms]
    eend = [f[2][1] for f in forms]
    aq = each(lambda x, y: halves(jnp.concatenate([x, y], axis=0)), ah, qh)
    with_b = each(lambda l, r: mul(l, spread(halves(r), masks), NT), aq, bh)
    with_k = each(lambda l, r: mul(l, spread(halves(r), masks), NT), aq, kh)
    aab = [x[:CHUNK] * strict for x in with_b]
    aqb = [halves(x[CHUNK:] * within) for x in with_b]
    aak = [halves(x[:CHUNK] * strict) for x in with_k]
    aqk = [halves(x[CHUNK:] * within) for x in with_k]
    p = [halves(x * (row // 8 == col // 8)) for x in aab]
    t = [eye + x * (row // 8 == col // 8) for x in aab]
    p2 = each(lambda x: halves(mul(x, spread(x, masks))), p)
    both = each(lambda x, y: mul(stack(x, halves(y)), spread(x, masks)), p2, t)
    p4 = [halves(x[:CHUNK]) for x in both]
    t = each(lambda x, y: x + y[CHUNK:], t, both)
    t = each(lambda x, y: x + mul(halves(x), spread(y, masks)), t, p4)
    for size in (8, 16, 32):
        corner = ((row // size) % 2 == 1) & (col // size == row // size - 1)
        ts = [halves(x) for x in t]
        n = [halves(x * corner) for x in aab]
        tn = each(lambda x, y: halves(mul(x, spread(y, masks))), ts, n)
        t = each(lambda x, y, z: x + mul(y, spread(z, masks)), t, tn, ts)
    ts = [halves(x) for x in t]
    vs = [halves(x) for x in v]
    vm = [spread(x, masks) for x in vs]
    wide = each(lambda x, y, e: mul(x, spread(halves(y * e), masks)), ts, ah, emid)
    r0 = each(mul, aak, vm)
    y0 = each(lambda x, y: mul(x, spread(halves(y), masks)), ts, r0)
    wides = [halves(x) for x in wide]
    qe = each(lambda x, e, y, z: x * e + mul(y, spread(z, masks)), qh, emid, aqb, wides)
    y0s = [halves(x) for x in y0]
    part = each(lambda x, y, z, u: mul(x, spread(y, masks)) + mul(z, u), aqb, y0s, aqk, vm)
    bts = [halves(x) for x in bt]
    diag = [eye * e for e in eend]
    tr = each(lambda x, y, d: tmul(x, y, masks) + d, bts, wides, diag)
    trt = each(lambda x, y, d: tmul(y, x, masks) + d, bts, wides, diag)
    inject = each(lambda x, y, z, u: tmul(stack(x, halves(y)), stack(z, u), masks), bts, kt, y0s, vs)
    wq = each(lambda x, y: stack(x, halves(y)), wides, qe)
    z = []
    out = []
    for c in range(STEP_CHUNKS):
        for g in range(2):
            i = c * 2 + g
            now = state_ref[g]
            nows = spread(halves(now), masks)
            state_ref[g] = mul(halves(tr[i]), nows) + inject[i]
            z.append(now)
            out.append(mul(wq[i], nows))
    o = each(lambda x, y: x[CHUNK:] + y, out, part)
    mixed = each(lambda x, y, z, m, n: read_out(x, y, z, m, n, ones)[3], o, q, k, v, vec)
    for i, u in enumerate(units):
        out_ref[u] = (mixed[i] * gate_ref[u]).astype(jnp.bfloat16)
        o_ref[u] = o[i]
        y_ref[u] = out[i][:CHUNK] + y0[i]
        t_ref[u] = t[i]
        aqb_ref[u] = with_b[i][CHUNK:] * within
        aak_ref[u] = with_k[i][:CHUNK] * strict
        aqk_ref[u] = with_k[i][CHUNK:] * within
        z_ref[u] = z[i]
        trt_ref[u] = trt[i]
        qe_ref[u] = qe[i]


def backward_kernel(base, *refs):
    (
        len_ref, vec_ref, start_ref, sums_ref, q_ref, keys_ref, v_ref, dl_ref, rl_ref, gate_ref,
        g_ref, o_ref, t_ref, aqb_ref, aak_ref, aqk_ref, y_ref, z_ref, trt_ref, qe_ref,
    ) = refs[:20]
    dq_ref, dkeys_ref, dv_ref, ddl_ref, drl_ref, dgate_ref, dvec_ref, state_ref = refs[-8:]
    step = base + pl.num_programs(0) - 1 - pl.program_id(0)

    @pl.when(pl.program_id(0) == 0)
    def _():
        state_ref[...] = start_ref[...]
        dvec_ref[...] = sums_ref[...]

    masks = head_masks()
    row, col = places()
    strict = (col < row).astype(jnp.float32)
    within = (col <= row).astype(jnp.float32)
    ones = block_ones()
    units = unit_slices()
    live = unit_live(len_ref[0], step)
    vec = unit_vectors(vec_ref)
    load = lambda ref: [ref[u] for u in units]
    q, keys, v, g = load(q_ref), load(keys_ref), load(v_ref), load(g_ref)
    ready = each(
        lambda x, y, z, m, n: prepared(x, y, z, m, n, ones), keys, load(dl_ref), load(rl_ref), live, vec
    )
    w, k, a, b, sig, rates, inverse, factor = ([x[i] for x in ready] for i in range(8))
    seen = each(lambda x, y, z, m, n: read_out(x, y, z, m, n, ones), load(o_ref), q, k, v, vec)
    normed, scale, weight, mixed = ([x[i] for x in seen] for i in range(4))
    gate = load(gate_ref)
    dgate = each(lambda x, y: x * y, g, mixed)
    dmix = each(lambda x, y: x * y, g, gate)
    dn = each(lambda x, n: x * n[5], dmix, vec)
    do = each(
        lambda x, n, r: r
        * (x - head_sum(x, ones) * (1.0 / CHUNK) - n * (head_sum(x * n, ones) * (1.0 / CHUNK))),
        dn, normed, scale,
    )
    dweight = each(lambda x, y: head_sum(x * y, ones), dmix, v)
    do = [halves(x) for x in do]
    qe, trt, t, aqb, aak, aqk, ys = (
        [halves(x) for x in load(ref)]
        for ref in (qe_ref, trt_ref, t_ref, aqb_ref, aak_ref, aqk_ref, y_ref)
    )
    z = load(z_ref)
    vs = [halves(x) for x in v]
    h = each(lambda x, y: tmul(x, y, masks), qe, do)
    dz = [None] * len(units)
    for c in reversed(range(STEP_CHUNKS)):
        for g in range(2):
            i = c * 2 + g
            now = state_ref[g]
            dz[i] = now
            state_ref[g] = mul(trt[i], spread(halves(now), masks)) + h[i]
    dzs = [spread(halves(x), masks) for x in dz]
    zs = [spread(halves(x), masks) for x in z]
    forms = each(scaled_forms, q, w, k, a, b)
    ah, qh, bh, kh, bt, kt = ([f[0][i] for f in forms] for i in range(6))
    ea, eq, eb, ee = ([f[1][i] for f in forms] for i in range(4))
    emid = [f[2][0] for f in forms]
    eend = [f[2][1] for f in forms]
    from_end = each(lambda x, y, s: mul(halves(jnp.concatenate([x, y], axis=0)), s), bt, kt, dzs)
    dy = each(lambda x, y, s: halves(tmul(x, y, masks) + s[:CHUNK]), aqb, do, from_end)
    dr = each(lambda x, y: halves(tmul(x, y, masks)), t, dy)
    ro = each(stack, dr, do)
    dv = each(lambda x, y, s, f: tmul(stack(x, y), s, masks) + f[CHUNK:], aak, aqk, ro, from_end)
    mask2 = jnp.concatenate([strict, within], axis=0)
    dab = each(lambda s, y: halves(mul(s, spread(y, masks), NT) * mask2), ro, ys)
    dak = each(lambda s, y: halves(mul(s, spread(y, masks), NT) * mask2), ro, vs)
    dst = each(lambda s, y: mul(s, y, NT), ro, zs)
    daq = each(
        lambda s, e, x, bb, y, kk: s * e + mul(x, spread(halves(bb), masks)) + mul(y, spread(halves(kk), masks)),
        dst, emid, dab, bh, dak, kh,
    )
    aq = each(lambda x, y: halves(jnp.concatenate([x, y], axis=0)), ah, qh)
    dbh = each(lambda x, y: tmul(x, y, masks), dab, aq)
    dkh = each(lambda x, y: tmul(x, y, masks), dak, aq)
    dend = each(lambda y, x, s: mul(stack(y, x), s, NT), ys, vs, dzs)
    row_of_ones = jnp.ones((8, LANES), jnp.bfloat16)
    sums = lambda x: jnp.sum(x, axis=0, keepdims=True)
    for i, u in enumerate(units):
        da = daq[i][:CHUNK] * ea[i]
        dq = daq[i][CHUNK:] * eq[i]
        dbt = dend[i][:CHUNK] * ee[i]
        dkt = dend[i][CHUNK:] * ee[i]
        db = dbh[i] * eb[i] + dbt
        dk = dkh[i] * eb[i] + dkt
        pa = da * a[i]
        diff = dq * q[i] - db * b[i] - dk * k[i] + pa
        zz = spread(halves(z[i] * dz[i]), masks)
        carry = (dot32(row_of_ones, zz[0], NT) + dot32(row_of_ones, zz[1], NT))[:1] * eend[i]
        carry = carry + sums(dbt * b[i] + dkt * k[i])
        dw = running_sum(diff, upper=True) - pa + carry
        from_bonus = dweight[i] * vec[i][4]
        dk = dk + from_bonus * q[i]
        dq_ref[u] = (dq + from_bonus * k[i]).astype(jnp.bfloat16)
        dv_ref[u] = (dv[i] + weight[i] * dmix[i]).astype(jnp.bfloat16)
        dgate_ref[u] = dgate[i].astype(jnp.bfloat16)
        unit_keys = -a[i]
        db = db * live[i]
        du = db * rates[i] - da
        dscaled = inverse[i] * (du - unit_keys * head_sum(du * unit_keys, ones))
        dkl = dk * keys[i] * live[i]
        drl = (db * unit_keys + dkl * vec[i][3]) * rates[i] * (1.0 - rates[i])
        ddl = dw * w[i] * (1.0 - sig[i])
        dkeys_ref[u] = (dk * factor[i] + dscaled * vec[i][2]).astype(jnp.bfloat16)
        ddl_ref[u] = ddl.astype(jnp.bfloat16)
        drl_ref[u] = drl.astype(jnp.bfloat16)
        parts = (
            ddl, drl, dscaled * keys[i], dkl * (rates[i] - 1.0),
            dweight[i] * q[i] * k[i], dmix[i] * normed[i], dmix[i],
        )
        lanes = u[1]
        for j, x in enumerate(parts):
            dvec_ref[j : j + 1, lanes] += sums(x)


def wkv_call(kernel, base, steps, small, arrays, outs, sums, previous, name):
    tokens, width = arrays[0].shape
    rows = CHUNK * STEP_CHUNKS
    last = base + steps - 1
    turned = kernel is backward_kernel
    spec = pl.BlockSpec((rows, width), lambda i: (last - i if turned else base + i, 0))
    state = pl.BlockSpec((2, CHUNK, LANES), lambda i: (0, 0, 0))
    whole = pl.BlockSpec((8, width), lambda i: (0, 0))
    shape = jax.ShapeDtypeStruct
    first = [pl.BlockSpec(memory_space=pltpu.SMEM), whole, state] + [whole] * sums
    held = list(previous or ())
    start = len(first) + len(arrays)
    return pl.pallas_call(
        partial(kernel, base),
        grid=(steps,),
        in_specs=first + [spec] * len(arrays) + [pl.BlockSpec(memory_space=pl.ANY)] * len(held),
        out_specs=[spec] * len(outs) + [whole] * sums + [state],
        out_shape=[shape((tokens, width), dtype) for dtype in outs]
        + [shape((8, width), jnp.float32)] * sums
        + [shape((2, CHUNK, LANES), jnp.float32)],
        input_output_aliases={start + i: i for i in range(len(held))},
        compiler_params=pltpu.CompilerParams(vmem_limit_bytes=56 << 20),
        cost_estimate=SMALL,
        name=name,
    )(*small, *arrays, *held)


def wkv_forward(base, steps, length, vec, state, arrays, previous=None):
    outs = [jnp.bfloat16] + [jnp.float32] * 9
    return wkv_call(
        forward_kernel, base, steps, (length, vec, state), arrays, outs, 0, previous, "wkv_forward"
    )


def wkv_backward(base, steps, length, vec, state, sums, arrays, previous=None):
    outs = [jnp.bfloat16] * 6
    return wkv_call(
        backward_kernel, base, steps, (length, vec, state, sums), arrays, outs, 1, previous,
        "wkv_backward",
    )


ROWS = 128


def row_norm(x):
    centred = x - jnp.mean(x, axis=-1, keepdims=True)
    scale = lax.rsqrt(jnp.mean(centred * centred, axis=-1, keepdims=True) + 1e-05)
    return centred * scale, scale


def shifted(x, edge, down):
    rows = x.shape[0]
    row = lax.broadcasted_iota(jnp.int32, x.shape, 0)
    if down:
        return jnp.where(row == 0, edge, pltpu.roll(x, 1, 0))
    return jnp.where(row == rows - 1, edge, pltpu.roll(x, rows - 1, 0))


def below(x, upper):
    lane = lax.broadcasted_iota(jnp.int32, x.shape, 1)
    keep = (lane >= DECAY_RANK) if upper else (lane < DECAY_RANK)
    return jnp.where(keep, x, jnp.zeros_like(x))


def front_kernel(
    x_ref, vec_ref, wr_ref, wk_ref, wv_ref, down_ref, up_ref,
    m0_ref, m1_ref, m2_ref, m3_ref, m4_ref, m5_ref,
    q_ref, k_ref, v_ref, dl_ref, rl_ref, gate_ref, hid_ref,
    edge_ref,
):
    @pl.when(pl.program_id(0) == 0)
    def _():
        edge_ref[...] = jnp.zeros_like(edge_ref)

    unit, _ = row_norm(x_ref[...].astype(jnp.float32))
    normed = unit * vec_ref[12:13] + vec_ref[13:14]
    change = shifted(normed, edge_ref[:1], True) - normed
    edge_ref[:1] = normed[ROWS - 1 :]
    mixes = []
    for j, ref in enumerate((m0_ref, m1_ref, m2_ref, m3_ref, m4_ref, m5_ref)):
        mixes.append((normed + change * vec_ref[j : j + 1]).astype(jnp.bfloat16))
        ref[...] = mixes[j]
    q_ref[...] = dot32(mixes[0], wr_ref[...], NN)
    k_ref[...] = dot32(mixes[2], wk_ref[...], NN)
    v_ref[...] = dot32(mixes[3], wv_ref[...], NN)
    first = down_ref[:, :128]
    pre_decay, pre_rate = dot32(mixes[1], first, NN), dot32(mixes[4], first, NN)
    pre_gate = dot32(mixes[5], down_ref[:, 128:], NN)
    lane = lax.broadcasted_iota(jnp.int32, pre_decay.shape, 1)
    pair = jnp.where(lane < DECAY_RANK, jnp.tanh(pre_decay), pre_rate)
    gate = jax.nn.sigmoid(pre_gate)
    hid_ref[:, :128] = pair
    hid_ref[:, 128:] = gate
    narrow_pair = pair.astype(jnp.bfloat16)
    dl_ref[...] = dot32(below(narrow_pair, False), up_ref[:, :128], NT)
    rl_ref[...] = dot32(below(narrow_pair, True), up_ref[:, :128], NT)
    gate_ref[...] = dot32(gate.astype(jnp.bfloat16), up_ref[:, 128:], NT)


def front_forward(x, vectors, w_r, w_k, w_v, down, up):
    tokens, width = x.shape
    wide = pl.BlockSpec((ROWS, width), lambda i: (i, 0))
    own = pl.BlockSpec((ROWS, OWN), lambda i: (i, 0))
    hid = pl.BlockSpec((ROWS, 256), lambda i: (i, 0))
    whole = lambda a: pl.BlockSpec(a.shape, lambda i: (0, 0))
    shape = jax.ShapeDtypeStruct
    return pl.pallas_call(
        front_kernel,
        grid=(tokens // ROWS,),
        in_specs=[wide] + [whole(a) for a in (vectors, w_r, w_k, w_v, down, up)],
        out_specs=[wide] * 6 + [own] * 6 + [hid],
        out_shape=[shape((tokens, width), jnp.bfloat16)] * 6
        + [shape((tokens, OWN), jnp.float32)] * 6
        + [shape((tokens, 256), jnp.float32)],
        scratch_shapes=[pltpu.VMEM((8, width), jnp.float32)],
        compiler_params=pltpu.CompilerParams(vmem_limit_bytes=48 << 20),
        cost_estimate=SMALL,
        name="front_forward",
    )(x, vectors, w_r, w_k, w_v, down, up)


def front_back_kernel(
    x_ref, before_ref, vec_ref, wr_ref, wk_ref, wv_ref, down_ref, up_ref,
    m1_ref, m4_ref, m5_ref, hid_ref,
    dq_ref, dk_ref, dv_ref, ddl_ref, drl_ref, dgate_ref, own_vec_ref, ffn_vec_ref,
    dx_ref, misc_ref,
    edge_ref, sums_ref,
):
    step = pl.num_programs(0) - 1 - pl.program_id(0)
    core = lax.axis_index("dp") % 2
    own_start = pl.multiple_of(core * OWN, OWN)

    @pl.when(pl.program_id(0) == 0)
    def _():
        edge_ref[...] = jnp.zeros_like(edge_ref)
        sums_ref[...] = jnp.zeros_like(sums_ref)
        misc_ref[...] = jnp.zeros_like(misc_ref)

    unit, scale = row_norm(x_ref[...].astype(jnp.float32))
    gain, offset = vec_ref[12:13], vec_ref[13:14]
    normed = unit * gain + offset
    tail, _ = row_norm(before_ref[...].astype(jnp.float32))
    edge = (tail[15:] * gain + offset) * jnp.where(step == 0, 0.0, 1.0)
    change = shifted(normed, edge, True) - normed
    ddl, drl, dgate = ddl_ref[...], drl_ref[...], dgate_ref[...]
    hid = hid_ref[...]
    pair, gate = hid[:, :128], hid[:, 128:]
    lane = lax.broadcasted_iota(jnp.int32, pair.shape, 1)
    first_up, last_up = up_ref[:, :128], up_ref[:, 128:]
    pair_grad = jnp.where(
        lane < DECAY_RANK,
        dot32(ddl, first_up, NN) * (1.0 - pair * pair),
        dot32(drl, first_up, NN),
    ).astype(jnp.bfloat16)
    gate_grad = (dot32(dgate, last_up, NN) * gate * (1.0 - gate)).astype(jnp.bfloat16)
    narrow_pair, narrow_gate = pair.astype(jnp.bfloat16), gate.astype(jnp.bfloat16)
    own_rows = pl.ds(own_start, OWN)
    misc_ref[own_rows, 256:384] += dot32(ddl, below(narrow_pair, False), TN) + dot32(
        drl, below(narrow_pair, True), TN
    )
    misc_ref[own_rows, 384:512] += dot32(dgate, narrow_gate, TN)
    decay_part, rate_part = below(pair_grad, False), below(pair_grad, True)
    misc_ref[:, :128] += dot32(m1_ref[...], decay_part, TN) + dot32(m4_ref[...], rate_part, TN)
    misc_ref[:, 128:256] += dot32(m5_ref[...], gate_grad, TN)
    first_down = down_ref[:, :128]
    grads = (
        lambda: dot32(dq_ref[...], wr_ref[...], NT),
        lambda: dot32(decay_part, first_down, NT),
        lambda: dot32(dk_ref[...], wk_ref[...], NT),
        lambda: dot32(dv_ref[...], wv_ref[...], NT),
        lambda: dot32(rate_part, first_down, NT),
        lambda: dot32(gate_grad, down_ref[:, 128:], NT),
    )
    total = jnp.zeros_like(change)
    moved = jnp.zeros_like(change)
    for j, grad in enumerate(grads):
        now = grad()
        total = total + now
        moved = moved + now * vec_ref[j : j + 1]
        sums_ref[j : j + 1] += jnp.sum(now * change, axis=0, keepdims=True)
    dnormed = total - moved + shifted(moved, edge_ref[:1], False)
    edge_ref[:1] = moved[:1]
    sums_ref[12:13] += jnp.sum(dnormed * unit, axis=0, keepdims=True)
    sums_ref[13:14] += jnp.sum(dnormed, axis=0, keepdims=True)
    dunit = dnormed * gain
    dx_ref[...] = scale * (
        dunit
        - jnp.mean(dunit, axis=-1, keepdims=True)
        - unit * jnp.mean(dunit * unit, axis=-1, keepdims=True)
    )

    @pl.when(step == 0)
    def _():
        sums_ref[6:7] = ffn_vec_ref[0:1] * 0.5
        sums_ref[14:16] = ffn_vec_ref[1:3] * 0.5
        zeros = jnp.zeros((1, OWN), jnp.float32)
        for target, source in ((7, 0), (8, 1), (9, 2), (10, 3), (11, 4), (16, 5), (17, 6)):
            mine = own_vec_ref[source : source + 1]
            sums_ref[target : target + 1] = jnp.concatenate(
                [jnp.where(core == 0, mine, zeros), jnp.where(core == 0, zeros, mine)], axis=1
            )
        for block in range(EMBED // 128):
            lanes = slice(block * 128, (block + 1) * 128)
            misc_ref[lanes, 512:640] = sums_ref[:, lanes].T


def front_backward(
    x, vectors, w_r, w_k, w_v, down, up, mixes, hid, grads, own_vec, ffn_vec
):
    tokens, width = x.shape
    steps = tokens // ROWS
    wide = pl.BlockSpec((ROWS, width), lambda i: (steps - 1 - i, 0))
    before = pl.BlockSpec(
        (16, width), lambda i: (jnp.maximum((steps - 1 - i) * (ROWS // 16) - 1, 0), 0)
    )
    own = pl.BlockSpec((ROWS, OWN), lambda i: (steps - 1 - i, 0))
    hid_spec = pl.BlockSpec((ROWS, 256), lambda i: (steps - 1 - i, 0))
    whole = lambda a: pl.BlockSpec(a.shape, lambda i: (0, 0))
    shape = jax.ShapeDtypeStruct
    return pl.pallas_call(
        front_back_kernel,
        grid=(steps,),
        in_specs=[wide, before]
        + [whole(a) for a in (vectors, w_r, w_k, w_v, down, up)]
        + [wide] * 3
        + [hid_spec]
        + [own] * 6
        + [whole(own_vec), whole(ffn_vec)],
        out_specs=[wide, pl.BlockSpec((EMBED, 640), lambda i: (0, 0))],
        out_shape=[shape((tokens, width), jnp.float32), shape((EMBED, 640), jnp.float32)],
        scratch_shapes=[
            pltpu.VMEM((8, width), jnp.float32), pltpu.VMEM((128, width), jnp.float32),
        ],
        compiler_params=pltpu.CompilerParams(vmem_limit_bytes=48 << 20),
        cost_estimate=SMALL,
        name="front_backward",
    )(x, x, vectors, w_r, w_k, w_v, down, up, *mixes, hid, *grads, own_vec, ffn_vec)


def ffn_back_kernel(
    len_ref, res_ref, before_ref, cot_ref, mine_ref, other_ref, vec_ref, wo_ref,
    grad_ref, narrow_ref, gated_ref, dvec_ref,
    edge_ref,
):
    step = pl.num_programs(0) - 1 - pl.program_id(0)

    @pl.when(pl.program_id(0) == 0)
    def _():
        edge_ref[...] = jnp.zeros_like(edge_ref)
        dvec_ref[...] = jnp.zeros_like(dvec_ref)

    gain, offset, coefficient = vec_ref[14:15], vec_ref[15:16], vec_ref[6:7]
    unit, scale = row_norm(res_ref[...])
    normed = unit * gain + offset
    tail, _ = row_norm(before_ref[...])
    edge = (tail[7:] * gain + offset) * jnp.where(step == 0, 0.0, 1.0)
    change = shifted(normed, edge, True) - normed
    grad = mine_ref[...].astype(jnp.float32) + other_ref[...].astype(jnp.float32)
    moved = grad * coefficient
    dnormed = grad - moved + shifted(moved, edge_ref[:1], False)
    edge_ref[:1] = moved[:1]
    sums = lambda x: jnp.sum(x, axis=0, keepdims=True)
    dvec_ref[0:1] += sums(grad * change)
    dvec_ref[1:2] += sums(dnormed * unit)
    dvec_ref[2:3] += sums(dnormed)
    dunit = dnormed * gain
    row = lax.broadcasted_iota(jnp.int32, grad.shape, 0) + step * ROWS
    out_grad = jnp.where(row < len_ref[0], cot_ref[...].astype(jnp.float32), 0.0)
    total = out_grad + scale * (
        dunit
        - jnp.mean(dunit, axis=-1, keepdims=True)
        - unit * jnp.mean(dunit * unit, axis=-1, keepdims=True)
    )
    grad_ref[...] = total
    small = total.astype(jnp.bfloat16)
    narrow_ref[...] = small
    gated_ref[...] = dot32(small, wo_ref[...], NT)


def ffn_backward(length, residual, cot, mine, other, vectors, w_o_rows):
    tokens, width = residual.shape
    steps = tokens // ROWS
    wide = pl.BlockSpec((ROWS, width), lambda i: (steps - 1 - i, 0))
    before = pl.BlockSpec(
        (8, width), lambda i: (jnp.maximum((steps - 1 - i) * (ROWS // 8) - 1, 0), 0)
    )
    own = pl.BlockSpec((ROWS, OWN), lambda i: (steps - 1 - i, 0))
    whole = lambda a: pl.BlockSpec(a.shape, lambda i: (0, 0))
    shape = jax.ShapeDtypeStruct
    return pl.pallas_call(
        ffn_back_kernel,
        grid=(steps,),
        in_specs=[pl.BlockSpec(memory_space=pltpu.SMEM), wide, before]
        + [wide] * 3
        + [whole(vectors), whole(w_o_rows)],
        out_specs=[wide, wide, own, pl.BlockSpec((8, width), lambda i: (0, 0))],
        out_shape=[
            shape((tokens, width), jnp.float32),
            shape((tokens, width), jnp.bfloat16),
            shape((tokens, OWN), jnp.float32),
            shape((8, width), jnp.float32),
        ],
        scratch_shapes=[pltpu.VMEM((8, width), jnp.float32)],
        compiler_params=pltpu.CompilerParams(vmem_limit_bytes=48 << 20),
        cost_estimate=SMALL,
        name="ffn_backward",
    )(length, residual, residual, cot, mine, other, vectors, w_o_rows)


def att_grad_kernel(m0_ref, m2_ref, m3_ref, dq_ref, dk_ref, dv_ref, send_a, keep_a, send_b, keep_b):
    chip = lax.axis_index("dp") // 2
    by_x, by_y = chip % 2 == 0, (chip // 2) % 2 == 0
    quarter = OWN // 2
    dv = dv_ref[...]
    first = ((m0_ref, dq_ref[...], 0, OWN), (m3_ref, dv[:, :quarter], OWN, quarter))
    second = ((m2_ref, dk_ref[...], 0, OWN), (m3_ref, dv[:, quarter:], OWN, quarter))
    for z in range(4):
        rows = slice(z * 256, (z + 1) * 256)
        for left, right, lane, width in first:
            block = dot32(left[:, rows], right, TN).astype(jnp.bfloat16)
            lanes = slice(lane, lane + width)
            for y in range(2):
                low, high = block[y * 128 : y * 128 + 64], block[y * 128 + 64 : y * 128 + 128]
                send_a[2 * z + y, :, lanes] = jnp.where(by_x, high, low)
                keep_a[2 * z + y, :, lanes] = jnp.where(by_x, low, high)
        for left, right, lane, width in second:
            block = dot32(left[:, rows], right, TN).astype(jnp.bfloat16)
            lanes = slice(lane, lane + width)
            for x in range(2):
                low, high = block[x * 64 : x * 64 + 64], block[128 + x * 64 : 128 + x * 64 + 64]
                send_b[2 * z + x, :, lanes] = jnp.where(by_y, high, low)
                keep_b[2 * z + x, :, lanes] = jnp.where(by_y, low, high)


def att_gradients(mixes, grads):
    space = pl.BlockSpec(memory_space=pltpu.VMEM)
    return pl.pallas_call(
        att_grad_kernel,
        in_specs=[space] * 6,
        out_specs=[space] * 4,
        out_shape=[jax.ShapeDtypeStruct((8, 64, OWN + OWN // 2), jnp.bfloat16)] * 4,
        compiler_params=pltpu.CompilerParams(vmem_limit_bytes=40 << 20),
        cost_estimate=SMALL,
        name="att_gradients",
    )(*mixes, *grads)


def swap(block, mask):
    size = lax.axis_size("dp")
    return lax.ppermute(block, "dp", [(i, i ^ mask) for i in range(size)])


def bit_of(mask):
    return (lax.axis_index("dp") // mask) % 2


def in_order(mask, own, other, axis):
    lower = bit_of(mask) == 0
    return jnp.where(
        lower, jnp.concatenate([own, other], axis=axis), jnp.concatenate([other, own], axis=axis)
    )


def chip_masks():
    size = lax.axis_size("dp")
    masks = []
    while 2 << len(masks) < size:
        masks.append(2 << len(masks))
    return masks


def steps_of(kind):
    masks = chip_masks()
    near, far = [[mask] for mask in masks[:2]], [[mask] for mask in masks[2:][::-1]]
    first = [[far[0][0], far[1][0], far[0][0] | far[1][0]]] if len(far) == 2 else far
    return [first + near[::-1], first + near, far + near[::-1], far + near, near + far][kind]


def meet(movers, *arrays):
    held = lax.optimization_barrier(tuple(tuple(m.arrived) for m in movers) + arrays)
    for mover, arrived in zip(movers, held):
        mover.arrived = list(arrived)
    return held[len(movers) :]


class Gather:
    def __init__(self, block, kind, places=(0,)):
        self.steps = steps_of(kind)
        self.held = block[None]
        self.places = [0]
        self.arrived = []
        self.masks = []

    def merge(self):
        if self.arrived:
            self.held = jnp.concatenate([self.held] + self.arrived, axis=0)
            self.places = self.places + [p ^ (m // 2) for m in self.masks for p in self.places]
            self.arrived = []

    def step(self):
        if self.steps:
            self.merge()
            self.masks = self.steps.pop(0)
            self.arrived = [swap(self.held, mask) for mask in self.masks]
        return self

    def run(self):
        while self.steps:
            self.step()
        return self

    def split(self, kinds):
        width = self.held.shape[-1] // len(kinds)
        out = []
        for i, kind in enumerate(kinds):
            part = Gather.__new__(Gather)
            cut = slice(i * width, (i + 1) * width)
            part.steps = steps_of(kind)[len(steps_of(kind)) - len(self.steps) :]
            part.held = self.held[..., cut]
            part.arrived = [x[..., cut] for x in self.arrived]
            part.places, part.masks = self.places, self.masks
            out.append(part)
        return out


def place_kernel(places, cuts, *refs):
    sources, outs = refs[: len(places)], refs[len(places) :]
    chip = lax.axis_index("dp") // 2
    for source, (part, list_of) in zip(sources, places):
        for j, place in enumerate(list_of):
            for out, (first, rows, lanes) in zip(outs, cuts):
                start = pl.multiple_of((chip ^ place) * rows, rows)
                lane, width = lanes[part]
                at = sum(w for _, w in lanes[:part])
                out[pl.ds(start, rows), at : at + width] = source[
                    j, first : first + rows, lane : lane + width
                ]


def assemble(gathers, cuts=None):
    gathers = [g.run() for g in gathers]
    rows = gathers[0].held.shape[1]
    cuts = cuts or ((0, rows, [(0, g.held.shape[2]) for g in gathers]),)
    sources, places = [], []
    for i, g in enumerate(gathers):
        sources += [g.held] + g.arrived
        shifts = [0] + [mask // 2 for mask in g.masks]
        places += [(i, [p ^ shift for p in g.places]) for shift in shifts]
    count = lax.axis_size("dp") // 2
    if any(cut[1] % 16 for cut in cuts):
        return assemble_plain(sources, places, cuts, count)
    space = pl.BlockSpec(memory_space=pltpu.VMEM)
    return pl.pallas_call(
        partial(place_kernel, places, cuts),
        in_specs=[space] * len(sources),
        out_specs=[space] * len(cuts),
        out_shape=[
            jax.ShapeDtypeStruct((count * n, sum(w for _, w in lanes)), sources[0].dtype)
            for _, n, lanes in cuts
        ],
        compiler_params=pltpu.CompilerParams(vmem_limit_bytes=32 << 20),
        cost_estimate=SMALL,
        name="assemble",
    )(*sources)


def assemble_plain(sources, places, cuts, count):
    chip = lax.axis_index("dp") // 2
    parts = []
    for part in sorted({part for part, _ in places}):
        blocks = jnp.concatenate([x for x, (at, _) in zip(sources, places) if at == part])
        where = [p for at, list_of in places if at == part for p in list_of]
        blocks = jnp.stack([blocks[where.index(i)] for i in range(count)])
        parts.append(jnp.take(blocks, chip ^ lax.iota(jnp.int32, count), axis=0))
    return [
        jnp.concatenate(
            [x[:, first : first + n, at : at + w] for x, (at, w) in zip(parts, lanes)], axis=-1
        ).reshape(count * n, -1)
        for first, n, lanes in cuts
    ]


class Scatter:
    def __init__(self, parts, kind):
        self.steps = steps_of(kind)[::-1]
        self.axes = chip_masks()[::-1]
        self.sources = [parts.reshape((2,) * len(self.axes) + parts.shape[1:])]
        self.arrived = []
        self.sent = None

    @classmethod
    def begun(cls, sent, kept, kind):
        out = cls.__new__(cls)
        out.steps = steps_of(kind)[::-1]
        out.axes = [axis for axis in chip_masks()[::-1] if axis != out.steps[0][0]]
        out.sources = [kept.reshape((2,) * len(out.axes) + kept.shape[1:])]
        out.arrived = []
        out.sent = [sent.reshape(out.sources[0].shape)]
        return out

    def pick(self, sources, mask, gone):
        out = []
        for x in sources:
            for place in reversed(range(len(self.axes))):
                axis = self.axes[place]
                if axis in gone:
                    which = bit_of(axis) if not mask & axis else 1 - bit_of(axis)
                    x = lax.dynamic_index_in_dim(x, which, place, keepdims=False)
            out.append(x)
        return out

    def prepare(self):
        if self.sent is not None:
            return self
        masks = self.steps[0]
        sources = self.sources + self.arrived
        gone = [axis for axis in self.axes if any(mask & axis for mask in masks)]
        self.sent = [
            sum(x.astype(jnp.float32) for x in self.pick(sources, mask, gone)).astype(jnp.bfloat16)
            for mask in masks
        ]
        self.sources = self.pick(sources, 0, gone)
        self.axes = [axis for axis in self.axes if axis not in gone]
        self.arrived = []
        return self

    def step(self):
        return together([self])[0]

    def run(self):
        while self.steps:
            self.step()
        return self

    def total(self):
        return sum(x.astype(jnp.float32) for x in self.sources + self.arrived)

    @staticmethod
    def join(parts, rows):
        out = Scatter.__new__(Scatter)
        out.steps, out.axes, out.arrived, out.sent = parts[0].steps, parts[0].axes, [], None
        pieces = []
        for part in parts:
            total = part.total()
            pieces += [total[..., at : at + rows, :] for at in range(0, total.shape[-2], rows)]
        out.sources = [jnp.concatenate(pieces, axis=-1)]
        return out


def together(parts):
    if not parts[0].steps:
        return parts
    for part in parts:
        part.prepare()
    for i, mask in enumerate(parts[0].steps[0]):
        sent = [part.sent[i] for part in parts]
        got = swap(sent[0] if len(sent) == 1 else jnp.concatenate(sent, axis=-1), mask)
        at = 0
        for part, x in zip(parts, sent):
            part.arrived.append(got[..., at : at + x.shape[-1]])
            at += x.shape[-1]
    for part in parts:
        part.steps.pop(0)
        part.sent = None
    return parts


def norm_rows(features, gain_row, offset_row):
    average = jnp.mean(features, axis=-1, keepdims=True)
    centred = features - average
    variance = jnp.mean(centred * centred, axis=-1, keepdims=True)
    return centred * lax.rsqrt(variance + 1e-05) * gain_row + offset_row


def product(operand, weight_matrix):
    return jnp.dot(operand, weight_matrix, preferred_element_type=jnp.float32)


def input_gradient_rows(upstream_gradient, weight_matrix):
    return lax.dot_general(
        upstream_gradient,
        weight_matrix,
        (((1,), (1,)), ((), ())),
        preferred_element_type=jnp.float32,
    )


def weight_gradient(operand, upstream_gradient):
    return lax.dot_general(
        operand, upstream_gradient, (((0,), (0,)), ((), ())), preferred_element_type=jnp.float32
    )


def earlier(rows):
    return jnp.concatenate([jnp.zeros_like(rows[:1]), rows[:-1]], axis=0)


def ffn_mix(residual, vectors):
    second = norm_rows(residual, vectors[14], vectors[15])
    return second + (earlier(second) - second) * vectors[6]


def narrow(x):
    return x.astype(jnp.bfloat16)


def local(
    inputs,
    lengths,
    attention_projections,
    channel_key_weight,
    channel_value_weight,
    lowrank_down_weight,
    lowrank_up_weight,
    per_feature_parameters,
    cotangent,
):
    devices = lax.axis_size("dp")
    chips = devices // 2
    device = lax.axis_index("dp")
    chip, core = device // 2, device % 2
    row_count = inputs.shape[0]
    slots = 2 * row_count
    share = EMBED // devices
    pair_share = 2 * share
    units = channel_value_weight.shape[0]
    half_units = chips * units

    def own_cut(x, which):
        return lax.dynamic_slice_in_dim(x, which * OWN, OWN, x.ndim - 1)

    def own_rows(x, which):
        return lax.dynamic_slice_in_dim(x, which * row_count, row_count, 0)

    pair_rows = in_order(
        1,
        own_cut(attention_projections, core),
        swap(own_cut(attention_projections, 1 - core), 1),
        1,
    )
    lora = jnp.concatenate([lowrank_down_weight, lowrank_up_weight.T], axis=1)
    vector_rows = jnp.pad(per_feature_parameters.T, ((0, 0), (0, 128 - 18)))
    vector_rows = vector_rows.reshape(share // 4, OWN)
    first_rows = 3 * pair_share
    misc_rows = share + share // 4 + (share // 4) % 16
    block = jnp.concatenate(
        [
            pair_rows[:3].reshape(first_rows, OWN),
            lora,
            jnp.pad(vector_rows, ((0, (share // 4) % 16), (0, 0))),
        ],
        axis=0,
    )
    half = half_units // 2
    quarter = OWN // 2
    first = Gather(block, 0).step()
    w_o_part = Gather(pair_rows[3], 4).step().step()
    key_in, raw, cot, _ = meet([], channel_key_weight, inputs, cotangent, pair_rows)
    key_cut = key_in.reshape(share, chips, 2, units)

    def key_columns(which):
        return lax.dynamic_index_in_dim(key_cut, which, 2, keepdims=False).reshape(share, half_units)

    key_rows = in_order(1, key_columns(core), swap(key_columns(1 - core), 1), 0)
    tokens = in_order(1, raw, swap(raw, 1), 0)
    cot = in_order(1, cot, swap(cot, 1), 0)
    key_rows, tokens, cot = meet([first, w_o_part], key_rows, tokens, cot)
    first = first.split((0, 1))
    for part in first:
        part.step()
    key_part = Gather(key_rows, 2).step()
    tokens, value_block = meet(first + [key_part], tokens, channel_value_weight)
    for part in first:
        part.step()
    key_part.step()
    value_part = Gather(value_block, 2).step()
    (tokens,) = meet(first + [key_part, value_part, w_o_part], tokens)
    key_parts = key_part.split((2, 3))
    for part in key_parts:
        part.step()
    w_r, w_k, w_v, misc = assemble(
        first,
        [(i * pair_share, pair_share, [(0, quarter)] * 2) for i in range(3)]
        + [(first_rows, misc_rows, [(0, quarter)] * 2)],
    )
    misc = misc.reshape(chips, 1, misc_rows, OWN)
    misc = in_order(1, misc, swap(misc, 1), 1)
    value_part.step()
    w_o_part.step()
    lora = misc[:, :, :share].reshape(EMBED, OWN)
    down, up_t = lora[:, :256], lax.dynamic_slice_in_dim(lora[:, 256:], core * OWN, OWN, 0)
    vectors = misc[:, :, share : share + share // 4].reshape(EMBED, 128)[:, :18].T
    vectors = vectors.astype(jnp.float32)
    own_vectors = own_cut(vectors, core)
    used = jnp.concatenate([own_vectors[7:12], own_vectors[16:18], own_vectors[:1]], axis=0)
    length = lax.dynamic_index_in_dim(lengths, chip, 0)
    live = (lax.iota(jnp.int32, slots) < length)[:, None]

    *mixes, queries, keys, values, decay_low, rate_low, gate_rows, hid = front_forward(
        tokens, vectors, w_r, w_k, w_v, down, up_t
    )
    terms = meet(
        key_parts + [value_part, w_o_part],
        queries, keys, values, decay_low, rate_low, gate_rows,
    )
    value_parts = value_part.split((2, 3))
    for part in key_parts + value_parts:
        part.step()
    w_o_part.step()
    blocks = slots // (CHUNK * STEP_CHUNKS)
    early = blocks // 2
    zero_state = jnp.zeros((2, CHUNK, LANES), jnp.float32)
    gated, *saved, _ = wkv_forward(0, blocks, length, used, zero_state, terms)
    gated, cot, tokens = meet(key_parts + value_parts + [w_o_part], gated, cot, tokens)
    for part in value_parts:
        part.step()
    gated_all = in_order(1, gated, swap(gated, 1), 1)
    (w_o_own,) = assemble([w_o_part])
    w_o = in_order(1, w_o_own, swap(w_o_own, 1), 1)
    (key_weight,) = assemble(key_parts)
    residual = tokens.astype(jnp.float32) + product(gated_all, w_o)
    ffn_in = narrow(ffn_mix(residual, vectors))
    positive = jax.nn.relu(product(ffn_in, key_weight))
    hidden = narrow(jnp.square(positive))
    out_narrow = jnp.where(live, cot, jnp.zeros_like(cot))
    value_cuts = ((0, quarter), (quarter, OWN), (OWN, EMBED))
    value_grads = [
        narrow(weight_gradient(hidden, out_narrow[:, lo:hi])).reshape(chips, units, hi - lo)
        for lo, hi in value_cuts
    ]
    hidden, positive, out_narrow, *value_grads = meet(
        value_parts, hidden, positive, out_narrow, *value_grads
    )
    (value_weight,) = assemble(value_parts)

    value_scatter = [Scatter(x, kind).step() for kind, x in zip((2, 3, 4), value_grads)]
    late_scatter = value_scatter.pop()
    pre_narrow = narrow(2.0 * positive * input_gradient_rows(out_narrow, value_weight))
    ffn_in_grad = narrow(input_gradient_rows(pre_narrow, key_weight))
    other_grad = swap(ffn_in_grad, 1)
    grad_key = narrow(weight_gradient(ffn_in, pre_narrow)).reshape(chips, pair_share, half_units)
    residual_grad, attended_grad, gated_grad, ffn_vec = ffn_backward(
        length, residual, cot, ffn_in_grad, other_grad, vectors,
        lax.dynamic_slice_in_dim(w_o, core * OWN, OWN, 0),
    )
    grad_o = narrow(weight_gradient(gated_all, own_cut(attended_grad, core)))
    grad_o = grad_o.reshape(chips, pair_share, OWN)
    key_scatter = [
        Scatter(
            jnp.concatenate(
                [
                    grad_key[:, :, i * half : (i + 1) * half],
                    grad_o[:, :, i * quarter : (i + 1) * quarter],
                ],
                axis=-1,
            ),
            2 + i,
        ).prepare()
        for i in range(2)
    ]
    gated_grad, *sent = meet([], gated_grad, *[m.sent[0] for m in key_scatter])
    for part, x in zip(key_scatter, sent):
        part.sent = [x]
        part.step()
    terms = [*terms, gated_grad, *saved]
    zero_sums = jnp.zeros((8, OWN), jnp.float32)
    *before, sums, state = wkv_backward(
        early, blocks - early, length, used, zero_state, zero_sums, terms
    )
    state, sums, hidden = meet(value_scatter + [late_scatter], state, sums, hidden)
    for part in value_scatter:
        part.step()
    late_scatter.step()
    *low_grads, own_vec, _ = wkv_backward(0, early, length, used, state, sums, terms, before)
    *low_grads, own_vec = meet(key_scatter + value_scatter, *low_grads, own_vec)
    for part in key_scatter:
        part.step()
    value_scatter = Scatter.join(value_scatter, pair_share).step()
    if pair_share == 64:
        sent_a, kept_a, sent_b, kept_b = att_gradients(
            (mixes[0], mixes[2], mixes[3]), low_grads[:3]
        )
        att_scatter = [Scatter.begun(sent_a, kept_a, 2), Scatter.begun(sent_b, kept_b, 3)]
    else:
        grads = [narrow(weight_gradient(mixes[m], g)) for m, g in zip((0, 2, 3), low_grads)]
        att_scatter = [
            Scatter(jnp.concatenate(x, axis=1).reshape(chips, pair_share, 3 * quarter), 2 + i)
            for i, x in enumerate(
                ((grads[0], grads[2][:, :quarter]), (grads[1], grads[2][:, quarter:]))
            )
        ]
    token_part, misc_grad = front_backward(
        tokens, vectors, w_r, w_k, w_v, down, up_t, (mixes[1], mixes[4], mixes[5]), hid,
        low_grads, own_vec, ffn_vec,
    )
    token_part, misc_grad = meet(key_scatter + [value_scatter, late_scatter], token_part, misc_grad)
    misc_grad = narrow(misc_grad).reshape(chips, pair_share, 640)
    misc_scatter = [Scatter(misc_grad[..., :320], 2), Scatter(misc_grad[..., 320:], 3)]
    pairs = list(zip(att_scatter, misc_scatter))
    for pair in pairs:
        together(pair)
    key_scatter = Scatter.join(key_scatter, pair_share).step()
    value_scatter.step()
    late_scatter.step()
    last_parts = att_scatter + misc_scatter
    (token_part,) = meet(last_parts + [key_scatter, value_scatter, late_scatter], token_part)
    for pair in pairs:
        together(pair)
    key_scatter.step()
    late_scatter.step()
    ffn_part = product(hidden, value_weight)
    ffn_out = own_rows(ffn_part, core) + swap(own_rows(ffn_part, 1 - core), 1)
    output = narrow(jnp.where(own_rows(live, core), own_rows(residual, core) + ffn_out, 0.0))
    (token_part, output) = meet(last_parts + [key_scatter, late_scatter], token_part, output)
    last = Scatter.join(last_parts, pair_share)
    if len(last.steps) == 2:
        last.steps = [[last.steps[0][0], last.steps[1][0], last.steps[0][0] | last.steps[1][0]]]
    last.step()
    input_gradient = (
        own_rows(residual_grad, core)
        + own_rows(token_part, core)
        + swap(own_rows(token_part, 1 - core), 1)
    )
    value_sum, late_sum, key_sum = (
        x.run().total() for x in (value_scatter, late_scatter, key_scatter)
    )
    ratio = units // pair_share
    value_sum = jnp.concatenate(
        [
            jnp.concatenate([value_sum[:, (at + ratio * i) * quarter :][:, :quarter] for i in range(2)], 1)
            for at in range(ratio)
        ]
        ,
        axis=0,
    )
    value_sum = jnp.concatenate([value_sum, late_sum], axis=1)
    input_gradient, value_sum, key_sum = meet([last], input_gradient, value_sum, key_sum)
    last_sum = last.run().total()
    wide = 3 * quarter
    each_half = half + quarter
    pair_sum = jnp.concatenate(
        [
            last_sum[:, :OWN],
            last_sum[:, wide : wide + OWN],
            last_sum[:, OWN:wide],
            last_sum[:, wide + OWN : 2 * wide],
            key_sum[:, half:each_half],
            key_sum[:, each_half + half :],
            key_sum[:, :half],
            key_sum[:, each_half : each_half + half],
            last_sum[:, 2 * wide :],
        ],
        axis=1,
    )
    pair_sum = pair_sum.reshape(2, share, -1)
    mine = lax.dynamic_index_in_dim(pair_sum, core, 0, keepdims=False)
    theirs = swap(lax.dynamic_index_in_dim(pair_sum, 1 - core, 0, keepdims=False), 1)
    shard_mixer = jnp.stack(
        [
            in_order(1, mine[:, i * OWN : (i + 1) * OWN], theirs[:, i * OWN : (i + 1) * OWN], 1)
            for i in range(4)
        ]
    )
    key_end = 4 * OWN + half_units
    shard_key = in_order(
        1,
        mine[:, 4 * OWN : key_end].reshape(share, chips, 1, units),
        theirs[:, 4 * OWN : key_end].reshape(share, chips, 1, units),
        2,
    ).reshape(share, 2 * half_units)
    misc_sum = mine[:, key_end:] + theirs[:, key_end:]
    return (
        output,
        input_gradient,
        shard_mixer,
        shard_key,
        value_sum,
        misc_sum[:, :256],
        misc_sum[:, 256:512].T,
        misc_sum[:, 512:530].T,
    )


def solution(mesh):
    in_specs = (
        P("dp", None),
        P(),
        P(None, "dp", None),
        P("dp", None),
        P("dp", None),
        P("dp", None),
        P(None, "dp"),
        P(None, "dp"),
        P("dp", None),
    )
    out_specs = (
        P("dp", None),
        P("dp", None),
        P(None, "dp", None),
        P("dp", None),
        P("dp", None),
        P("dp", None),
        P(None, "dp"),
        P(None, "dp"),
    )
    return jax.shard_map(local, mesh=mesh, in_specs=in_specs, out_specs=out_specs, check_vma=False)
```

```python
from functools import partial

import jax
import jax.numpy as jnp
from jax import lax
from jax.experimental import pallas as pl
from jax.experimental.pallas import tpu as pltpu
from jax.sharding import PartitionSpec as P

HEADS = 16
HEAD_SIZE = 64
DECAY_RANK = 64
RATE_RANK = 64
EMBED = 1024
OWN = EMBED // 2
PRECISE = lax.Precision.HIGHEST


CHUNK = 64
LANES = 256
GROUP_HEADS = 4
STEP_CHUNKS = 2
SMALL = pl.CostEstimate(flops=1, bytes_accessed=1, transcendentals=0)

NN = (((1,), (0,)), ((), ()))
NT = (((1,), (1,)), ((), ()))
TN = (((0,), (0,)), ((), ()))


def halves(x):
    high = x.astype(jnp.bfloat16)
    return high, (x - high.astype(jnp.float32)).astype(jnp.bfloat16)


def dot32(a, b, dims):
    return lax.dot_general(a, b, dims, preferred_element_type=jnp.float32)


def mul(left, right, dims=NN):
    rows = left[0].shape[0]
    both = dot32(jnp.concatenate(left, axis=0), right[0], dims)
    return both[:rows] + both[rows:] + dot32(left[0], right[1], dims)


def tmul(left, right, masks):
    full = (
        dot32(left[0], right[0], TN) + dot32(left[1], right[0], TN) + dot32(left[0], right[1], TN)
    )
    return sum(full[h * CHUNK : (h + 1) * CHUNK] * masks[h][:1].astype(jnp.float32) for h in range(GROUP_HEADS))


def spread(pair, masks):
    return tuple(
        jnp.concatenate([part * masks[h] for h in range(GROUP_HEADS)], axis=0) for part in pair
    )


def stack(first, second):
    return tuple(jnp.concatenate([x, y], axis=0) for x, y in zip(first, second))


def head_masks():
    lane = lax.broadcasted_iota(jnp.int32, (CHUNK, LANES), 1) // CHUNK
    return [(lane == h).astype(jnp.float32).astype(jnp.bfloat16) for h in range(GROUP_HEADS)]


def places():
    row = lax.broadcasted_iota(jnp.int32, (CHUNK, LANES), 0)
    col = lax.broadcasted_iota(jnp.int32, (CHUNK, LANES), 1) % CHUNK
    return row, col


def running_sum(x, upper=False):
    row = lax.broadcasted_iota(jnp.int32, (CHUNK, CHUNK), 0)
    col = lax.broadcasted_iota(jnp.int32, (CHUNK, CHUNK), 1)
    ones = (row <= col if upper else col <= row).astype(jnp.float32).astype(jnp.bfloat16)
    high, rest = halves(x)
    low = (x - high.astype(jnp.float32) - rest.astype(jnp.float32)).astype(jnp.bfloat16)
    return dot32(ones, high, NN) + dot32(ones, rest, NN) + dot32(ones, low, NN)


def scaled_forms(q, w, k, a, b):
    total = running_sum(w)
    before = total - w
    middle = total[CHUNK // 2 - 1 : CHUNK // 2]
    end = total[CHUNK - 1 :]
    ea = jnp.exp(before - middle)
    eq = jnp.exp(total - middle)
    eb = jnp.exp(middle - total)
    ee = jnp.exp(end - total)
    return (a * ea, q * eq, b * eb, k * eb, b * ee, k * ee), (ea, eq, eb, ee), (jnp.exp(middle), jnp.exp(end))


def each(fn, *columns):
    return [fn(*row) for row in zip(*columns)]


def block_ones():
    row = lax.broadcasted_iota(jnp.int32, (LANES, LANES), 0) // CHUNK
    col = lax.broadcasted_iota(jnp.int32, (LANES, LANES), 1) // CHUNK
    return (row == col).astype(jnp.float32).astype(jnp.bfloat16)


def head_sum(x, ones):
    rows = x.shape[0]
    both = dot32(jnp.concatenate(halves(x), axis=0), ones, NN)
    return both[:rows] + both[rows:]


def prepared(keys, decay_low, rate_low, live, vec, ones):
    sig = jax.nn.sigmoid(vec[0] + decay_low)
    log_decay = (-0.6065306597126334) * sig * live
    rates = jax.nn.sigmoid(vec[1] + rate_low)
    scaled = keys * vec[2]
    inverse = lax.rsqrt(head_sum(scaled * scaled, ones) + 1e-06)
    unit_keys = scaled * inverse
    factor = (1.0 + (rates - 1.0) * vec[3]) * live
    return log_decay, keys * factor, -unit_keys, unit_keys * rates * live, sig, rates, inverse, factor


def read_out(o, q, k, v, vec, ones):
    centred = o - head_sum(o, ones) * (1.0 / CHUNK)
    scale = lax.rsqrt(head_sum(centred * centred, ones) * (1.0 / CHUNK) + 0.00064)
    normed = centred * scale
    weight = head_sum(q * k * vec[4], ones)
    return normed, scale, weight, normed * vec[5] + vec[6] + weight * v


def unit_slices():
    return [
        (slice(c * CHUNK, (c + 1) * CHUNK), slice(g * LANES, (g + 1) * LANES))
        for c in range(STEP_CHUNKS)
        for g in range(2)
    ]


def unit_live(length, step):
    row = lax.broadcasted_iota(jnp.int32, (CHUNK, LANES), 0)
    start = step * (STEP_CHUNKS * CHUNK)
    live = [(row + (start + c * CHUNK) < length).astype(jnp.float32) for c in range(STEP_CHUNKS)]
    return [live[c] for c in range(STEP_CHUNKS) for g in range(2)]


def unit_vectors(vec_ref):
    vec = [[vec_ref[i : i + 1, g * LANES : (g + 1) * LANES] for i in range(7)] for g in range(2)]
    return [vec[g] for c in range(STEP_CHUNKS) for g in range(2)]


def forward_kernel(base, *refs):
    len_ref, vec_ref, start_ref, q_ref, keys_ref, v_ref, dl_ref, rl_ref, gate_ref = refs[:9]
    (
        out_ref, o_ref, t_ref, aqb_ref, aak_ref, aqk_ref, y_ref, z_ref, trt_ref, qe_ref, state_ref,
    ) = refs[-11:]

    @pl.when(pl.program_id(0) == 0)
    def _():
        state_ref[...] = start_ref[...]

    masks = head_masks()
    row, col = places()
    strict = (col < row).astype(jnp.float32)
    within = (col <= row).astype(jnp.float32)
    eye = (col == row).astype(jnp.float32)
    ones = block_ones()
    units = unit_slices()
    live = unit_live(len_ref[0], pl.program_id(0) + base)
    vec = unit_vectors(vec_ref)
    load = lambda ref: [ref[u] for u in units]
    q, keys, v = load(q_ref), load(keys_ref), load(v_ref)
    ready = each(
        lambda x, y, z, m, n: prepared(x, y, z, m, n, ones), keys, load(dl_ref), load(rl_ref), live, vec
    )
    w, k, a, b = ([x[i] for x in ready] for i in range(4))
    forms = each(scaled_forms, q, w, k, a, b)
    ah, qh, bh, kh, bt, kt = ([f[0][i] for f in forms] for i in range(6))
    emid = [f[2][0] for f in forms]
    eend = [f[2][1] for f in forms]
    aq = each(lambda x, y: halves(jnp.concatenate([x, y], axis=0)), ah, qh)
    with_b = each(lambda l, r: mul(l, spread(halves(r), masks), NT), aq, bh)
    with_k = each(lambda l, r: mul(l, spread(halves(r), masks), NT), aq, kh)
    aab = [x[:CHUNK] * strict for x in with_b]
    aqb = [halves(x[CHUNK:] * within) for x in with_b]
    aak = [halves(x[:CHUNK] * strict) for x in with_k]
    aqk = [halves(x[CHUNK:] * within) for x in with_k]
    p = [halves(x * (row // 8 == col // 8)) for x in aab]
    t = [eye + x * (row // 8 == col // 8) for x in aab]
    p2 = each(lambda x: halves(mul(x, spread(x, masks))), p)
    both = each(lambda x, y: mul(stack(x, halves(y)), spread(x, masks)), p2, t)
    p4 = [halves(x[:CHUNK]) for x in both]
    t = each(lambda x, y: x + y[CHUNK:], t, both)
    t = each(lambda x, y: x + mul(halves(x), spread(y, masks)), t, p4)
    for size in (8, 16, 32):
        corner = ((row // size) % 2 == 1) & (col // size == row // size - 1)
        ts = [halves(x) for x in t]
        n = [halves(x * corner) for x in aab]
        tn = each(lambda x, y: halves(mul(x, spread(y, masks))), ts, n)
        t = each(lambda x, y, z: x + mul(y, spread(z, masks)), t, tn, ts)
    ts = [halves(x) for x in t]
    vs = [halves(x) for x in v]
    vm = [spread(x, masks) for x in vs]
    wide = each(lambda x, y, e: mul(x, spread(halves(y * e), masks)), ts, ah, emid)
    r0 = each(mul, aak, vm)
    y0 = each(lambda x, y: mul(x, spread(halves(y), masks)), ts, r0)
    wides = [halves(x) for x in wide]
    qe = each(lambda x, e, y, z: x * e + mul(y, spread(z, masks)), qh, emid, aqb, wides)
    y0s = [halves(x) for x in y0]
    part = each(lambda x, y, z, u: mul(x, spread(y, masks)) + mul(z, u), aqb, y0s, aqk, vm)
    bts = [halves(x) for x in bt]
    diag = [eye * e for e in eend]
    tr = each(lambda x, y, d: tmul(x, y, masks) + d, bts, wides, diag)
    trt = each(lambda x, y, d: tmul(y, x, masks) + d, bts, wides, diag)
    inject = each(lambda x, y, z, u: tmul(stack(x, halves(y)), stack(z, u), masks), bts, kt, y0s, vs)
    wq = each(lambda x, y: stack(x, halves(y)), wides, qe)
    z = []
    out = []
    for c in range(STEP_CHUNKS):
        for g in range(2):
            i = c * 2 + g
            now = state_ref[g]
            nows = spread(halves(now), masks)
            state_ref[g] = mul(halves(tr[i]), nows) + inject[i]
            z.append(now)
            out.append(mul(wq[i], nows))
    o = each(lambda x, y: x[CHUNK:] + y, out, part)
    mixed = each(lambda x, y, z, m, n: read_out(x, y, z, m, n, ones)[3], o, q, k, v, vec)
    for i, u in enumerate(units):
        out_ref[u] = (mixed[i] * gate_ref[u]).astype(jnp.bfloat16)
        o_ref[u] = o[i]
        y_ref[u] = out[i][:CHUNK] + y0[i]
        t_ref[u] = t[i]
        aqb_ref[u] = with_b[i][CHUNK:] * within
        aak_ref[u] = with_k[i][:CHUNK] * strict
        aqk_ref[u] = with_k[i][CHUNK:] * within
        z_ref[u] = z[i]
        trt_ref[u] = trt[i]
        qe_ref[u] = qe[i]


def backward_kernel(base, *refs):
    (
        len_ref, vec_ref, start_ref, sums_ref, q_ref, keys_ref, v_ref, dl_ref, rl_ref, gate_ref,
        g_ref, o_ref, t_ref, aqb_ref, aak_ref, aqk_ref, y_ref, z_ref, trt_ref, qe_ref,
    ) = refs[:20]
    dq_ref, dkeys_ref, dv_ref, ddl_ref, drl_ref, dgate_ref, dvec_ref, state_ref = refs[-8:]
    step = base + pl.num_programs(0) - 1 - pl.program_id(0)

    @pl.when(pl.program_id(0) == 0)
    def _():
        state_ref[...] = start_ref[...]
        dvec_ref[...] = sums_ref[...]

    masks = head_masks()
    row, col = places()
    strict = (col < row).astype(jnp.float32)
    within = (col <= row).astype(jnp.float32)
    ones = block_ones()
    units = unit_slices()
    live = unit_live(len_ref[0], step)
    vec = unit_vectors(vec_ref)
    load = lambda ref: [ref[u] for u in units]
    q, keys, v, g = load(q_ref), load(keys_ref), load(v_ref), load(g_ref)
    ready = each(
        lambda x, y, z, m, n: prepared(x, y, z, m, n, ones), keys, load(dl_ref), load(rl_ref), live, vec
    )
    w, k, a, b, sig, rates, inverse, factor = ([x[i] for x in ready] for i in range(8))
    seen = each(lambda x, y, z, m, n: read_out(x, y, z, m, n, ones), load(o_ref), q, k, v, vec)
    normed, scale, weight, mixed = ([x[i] for x in seen] for i in range(4))
    gate = load(gate_ref)
    dgate = each(lambda x, y: x * y, g, mixed)
    dmix = each(lambda x, y: x * y, g, gate)
    dn = each(lambda x, n: x * n[5], dmix, vec)
    do = each(
        lambda x, n, r: r
        * (x - head_sum(x, ones) * (1.0 / CHUNK) - n * (head_sum(x * n, ones) * (1.0 / CHUNK))),
        dn, normed, scale,
    )
    dweight = each(lambda x, y: head_sum(x * y, ones), dmix, v)
    do = [halves(x) for x in do]
    qe, trt, t, aqb, aak, aqk, ys = (
        [halves(x) for x in load(ref)]
        for ref in (qe_ref, trt_ref, t_ref, aqb_ref, aak_ref, aqk_ref, y_ref)
    )
    z = load(z_ref)
    vs = [halves(x) for x in v]
    h = each(lambda x, y: tmul(x, y, masks), qe, do)
    dz = [None] * len(units)
    for c in reversed(range(STEP_CHUNKS)):
        for g in range(2):
            i = c * 2 + g
            now = state_ref[g]
            dz[i] = now
            state_ref[g] = mul(trt[i], spread(halves(now), masks)) + h[i]
    dzs = [spread(halves(x), masks) for x in dz]
    zs = [spread(halves(x), masks) for x in z]
    forms = each(scaled_forms, q, w, k, a, b)
    ah, qh, bh, kh, bt, kt = ([f[0][i] for f in forms] for i in range(6))
    ea, eq, eb, ee = ([f[1][i] for f in forms] for i in range(4))
    emid = [f[2][0] for f in forms]
    eend = [f[2][1] for f in forms]
    from_end = each(lambda x, y, s: mul(halves(jnp.concatenate([x, y], axis=0)), s), bt, kt, dzs)
    dy = each(lambda x, y, s: halves(tmul(x, y, masks) + s[:CHUNK]), aqb, do, from_end)
    dr = each(lambda x, y: halves(tmul(x, y, masks)), t, dy)
    ro = each(stack, dr, do)
    dv = each(lambda x, y, s, f: tmul(stack(x, y), s, masks) + f[CHUNK:], aak, aqk, ro, from_end)
    mask2 = jnp.concatenate([strict, within], axis=0)
    dab = each(lambda s, y: halves(mul(s, spread(y, masks), NT) * mask2), ro, ys)
    dak = each(lambda s, y: halves(mul(s, spread(y, masks), NT) * mask2), ro, vs)
    dst = each(lambda s, y: mul(s, y, NT), ro, zs)
    daq = each(
        lambda s, e, x, bb, y, kk: s * e + mul(x, spread(halves(bb), masks)) + mul(y, spread(halves(kk), masks)),
        dst, emid, dab, bh, dak, kh,
    )
    aq = each(lambda x, y: halves(jnp.concatenate([x, y], axis=0)), ah, qh)
    dbh = each(lambda x, y: tmul(x, y, masks), dab, aq)
    dkh = each(lambda x, y: tmul(x, y, masks), dak, aq)
    dend = each(lambda y, x, s: mul(stack(y, x), s, NT), ys, vs, dzs)
    row_of_ones = jnp.ones((8, LANES), jnp.bfloat16)
    sums = lambda x: jnp.sum(x, axis=0, keepdims=True)
    for i, u in enumerate(units):
        da = daq[i][:CHUNK] * ea[i]
        dq = daq[i][CHUNK:] * eq[i]
        dbt = dend[i][:CHUNK] * ee[i]
        dkt = dend[i][CHUNK:] * ee[i]
        db = dbh[i] * eb[i] + dbt
        dk = dkh[i] * eb[i] + dkt
        pa = da * a[i]
        diff = dq * q[i] - db * b[i] - dk * k[i] + pa
        zz = spread(halves(z[i] * dz[i]), masks)
        carry = (dot32(row_of_ones, zz[0], NT) + dot32(row_of_ones, zz[1], NT))[:1] * eend[i]
        carry = carry + sums(dbt * b[i] + dkt * k[i])
        dw = running_sum(diff, upper=True) - pa + carry
        from_bonus = dweight[i] * vec[i][4]
        dk = dk + from_bonus * q[i]
        dq_ref[u] = (dq + from_bonus * k[i]).astype(jnp.bfloat16)
        dv_ref[u] = (dv[i] + weight[i] * dmix[i]).astype(jnp.bfloat16)
        dgate_ref[u] = dgate[i].astype(jnp.bfloat16)
        unit_keys = -a[i]
        db = db * live[i]
        du = db * rates[i] - da
        dscaled = inverse[i] * (du - unit_keys * head_sum(du * unit_keys, ones))
        dkl = dk * keys[i] * live[i]
        drl = (db * unit_keys + dkl * vec[i][3]) * rates[i] * (1.0 - rates[i])
        ddl = dw * w[i] * (1.0 - sig[i])
        dkeys_ref[u] = (dk * factor[i] + dscaled * vec[i][2]).astype(jnp.bfloat16)
        ddl_ref[u] = ddl.astype(jnp.bfloat16)
        drl_ref[u] = drl.astype(jnp.bfloat16)
        parts = (
            ddl, drl, dscaled * keys[i], dkl * (rates[i] - 1.0),
            dweight[i] * q[i] * k[i], dmix[i] * normed[i], dmix[i],
        )
        lanes = u[1]
        for j, x in enumerate(parts):
            dvec_ref[j : j + 1, lanes] += sums(x)


def wkv_call(kernel, base, steps, small, arrays, outs, sums, previous, name):
    tokens, width = arrays[0].shape
    rows = CHUNK * STEP_CHUNKS
    last = base + steps - 1
    turned = kernel is backward_kernel
    spec = pl.BlockSpec((rows, width), lambda i: (last - i if turned else base + i, 0))
    state = pl.BlockSpec((2, CHUNK, LANES), lambda i: (0, 0, 0))
    whole = pl.BlockSpec((8, width), lambda i: (0, 0))
    shape = jax.ShapeDtypeStruct
    first = [pl.BlockSpec(memory_space=pltpu.SMEM), whole, state] + [whole] * sums
    held = list(previous or ())
    start = len(first) + len(arrays)
    return pl.pallas_call(
        partial(kernel, base),
        grid=(steps,),
        in_specs=first + [spec] * len(arrays) + [pl.BlockSpec(memory_space=pl.ANY)] * len(held),
        out_specs=[spec] * len(outs) + [whole] * sums + [state],
        out_shape=[shape((tokens, width), dtype) for dtype in outs]
        + [shape((8, width), jnp.float32)] * sums
        + [shape((2, CHUNK, LANES), jnp.float32)],
        input_output_aliases={start + i: i for i in range(len(held))},
        compiler_params=pltpu.CompilerParams(vmem_limit_bytes=56 << 20),
        cost_estimate=SMALL,
        name=name,
    )(*small, *arrays, *held)


def wkv_forward(base, steps, length, vec, state, arrays, previous=None):
    outs = [jnp.bfloat16] + [jnp.float32] * 9
    return wkv_call(
        forward_kernel, base, steps, (length, vec, state), arrays, outs, 0, previous, "wkv_forward"
    )


def wkv_backward(base, steps, length, vec, state, sums, arrays, previous=None):
    outs = [jnp.bfloat16] * 6
    return wkv_call(
        backward_kernel, base, steps, (length, vec, state, sums), arrays, outs, 1, previous,
        "wkv_backward",
    )


ROWS = 128


def row_norm(x):
    centred = x - jnp.mean(x, axis=-1, keepdims=True)
    scale = lax.rsqrt(jnp.mean(centred * centred, axis=-1, keepdims=True) + 1e-05)
    return centred * scale, scale


def shifted(x, edge, down):
    rows = x.shape[0]
    row = lax.broadcasted_iota(jnp.int32, x.shape, 0)
    if down:
        return jnp.where(row == 0, edge, pltpu.roll(x, 1, 0))
    return jnp.where(row == rows - 1, edge, pltpu.roll(x, rows - 1, 0))


def below(x, upper):
    lane = lax.broadcasted_iota(jnp.int32, x.shape, 1)
    keep = (lane >= DECAY_RANK) if upper else (lane < DECAY_RANK)
    return jnp.where(keep, x, jnp.zeros_like(x))


def front_kernel(
    x_ref, vec_ref, wr_ref, wk_ref, wv_ref, down_ref, up_ref,
    m0_ref, m1_ref, m2_ref, m3_ref, m4_ref, m5_ref,
    q_ref, k_ref, v_ref, dl_ref, rl_ref, gate_ref, hid_ref,
    edge_ref,
):
    @pl.when(pl.program_id(0) == 0)
    def _():
        edge_ref[...] = jnp.zeros_like(edge_ref)

    unit, _ = row_norm(x_ref[...].astype(jnp.float32))
    normed = unit * vec_ref[12:13] + vec_ref[13:14]
    change = shifted(normed, edge_ref[:1], True) - normed
    edge_ref[:1] = normed[ROWS - 1 :]
    mixes = []
    for j, ref in enumerate((m0_ref, m1_ref, m2_ref, m3_ref, m4_ref, m5_ref)):
        mixes.append((normed + change * vec_ref[j : j + 1]).astype(jnp.bfloat16))
        ref[...] = mixes[j]
    q_ref[...] = dot32(mixes[0], wr_ref[...], NN)
    k_ref[...] = dot32(mixes[2], wk_ref[...], NN)
    v_ref[...] = dot32(mixes[3], wv_ref[...], NN)
    first = down_ref[:, :128]
    pre_decay, pre_rate = dot32(mixes[1], first, NN), dot32(mixes[4], first, NN)
    pre_gate = dot32(mixes[5], down_ref[:, 128:], NN)
    lane = lax.broadcasted_iota(jnp.int32, pre_decay.shape, 1)
    pair = jnp.where(lane < DECAY_RANK, jnp.tanh(pre_decay), pre_rate)
    gate = jax.nn.sigmoid(pre_gate)
    hid_ref[:, :128] = pair
    hid_ref[:, 128:] = gate
    narrow_pair = pair.astype(jnp.bfloat16)
    dl_ref[...] = dot32(below(narrow_pair, False), up_ref[:, :128], NT)
    rl_ref[...] = dot32(below(narrow_pair, True), up_ref[:, :128], NT)
    gate_ref[...] = dot32(gate.astype(jnp.bfloat16), up_ref[:, 128:], NT)


def front_forward(x, vectors, w_r, w_k, w_v, down, up):
    tokens, width = x.shape
    wide = pl.BlockSpec((ROWS, width), lambda i: (i, 0))
    own = pl.BlockSpec((ROWS, OWN), lambda i: (i, 0))
    hid = pl.BlockSpec((ROWS, 256), lambda i: (i, 0))
    whole = lambda a: pl.BlockSpec(a.shape, lambda i: (0, 0))
    shape = jax.ShapeDtypeStruct
    return pl.pallas_call(
        front_kernel,
        grid=(tokens // ROWS,),
        in_specs=[wide] + [whole(a) for a in (vectors, w_r, w_k, w_v, down, up)],
        out_specs=[wide] * 6 + [own] * 6 + [hid],
        out_shape=[shape((tokens, width), jnp.bfloat16)] * 6
        + [shape((tokens, OWN), jnp.float32)] * 6
        + [shape((tokens, 256), jnp.float32)],
        scratch_shapes=[pltpu.VMEM((8, width), jnp.float32)],
        compiler_params=pltpu.CompilerParams(vmem_limit_bytes=48 << 20),
        cost_estimate=SMALL,
        name="front_forward",
    )(x, vectors, w_r, w_k, w_v, down, up)


def front_back_kernel(
    x_ref, before_ref, vec_ref, wr_ref, wk_ref, wv_ref, down_ref, up_ref,
    m1_ref, m4_ref, m5_ref, hid_ref,
    dq_ref, dk_ref, dv_ref, ddl_ref, drl_ref, dgate_ref, own_vec_ref, ffn_vec_ref,
    dx_ref, misc_ref,
    edge_ref, sums_ref,
):
    step = pl.num_programs(0) - 1 - pl.program_id(0)
    core = lax.axis_index("dp") % 2
    own_start = pl.multiple_of(core * OWN, OWN)

    @pl.when(pl.program_id(0) == 0)
    def _():
        edge_ref[...] = jnp.zeros_like(edge_ref)
        sums_ref[...] = jnp.zeros_like(sums_ref)
        misc_ref[...] = jnp.zeros_like(misc_ref)

    unit, scale = row_norm(x_ref[...].astype(jnp.float32))
    gain, offset = vec_ref[12:13], vec_ref[13:14]
    normed = unit * gain + offset
    tail, _ = row_norm(before_ref[...].astype(jnp.float32))
    edge = (tail[15:] * gain + offset) * jnp.where(step == 0, 0.0, 1.0)
    change = shifted(normed, edge, True) - normed
    ddl, drl, dgate = ddl_ref[...], drl_ref[...], dgate_ref[...]
    hid = hid_ref[...]
    pair, gate = hid[:, :128], hid[:, 128:]
    lane = lax.broadcasted_iota(jnp.int32, pair.shape, 1)
    first_up, last_up = up_ref[:, :128], up_ref[:, 128:]
    pair_grad = jnp.where(
        lane < DECAY_RANK,
        dot32(ddl, first_up, NN) * (1.0 - pair * pair),
        dot32(drl, first_up, NN),
    ).astype(jnp.bfloat16)
    gate_grad = (dot32(dgate, last_up, NN) * gate * (1.0 - gate)).astype(jnp.bfloat16)
    narrow_pair, narrow_gate = pair.astype(jnp.bfloat16), gate.astype(jnp.bfloat16)
    own_rows = pl.ds(own_start, OWN)
    misc_ref[own_rows, 256:384] += dot32(ddl, below(narrow_pair, False), TN) + dot32(
        drl, below(narrow_pair, True), TN
    )
    misc_ref[own_rows, 384:512] += dot32(dgate, narrow_gate, TN)
    decay_part, rate_part = below(pair_grad, False), below(pair_grad, True)
    misc_ref[:, :128] += dot32(m1_ref[...], decay_part, TN) + dot32(m4_ref[...], rate_part, TN)
    misc_ref[:, 128:256] += dot32(m5_ref[...], gate_grad, TN)
    first_down = down_ref[:, :128]
    grads = (
        lambda: dot32(dq_ref[...], wr_ref[...], NT),
        lambda: dot32(decay_part, first_down, NT),
        lambda: dot32(dk_ref[...], wk_ref[...], NT),
        lambda: dot32(dv_ref[...], wv_ref[...], NT),
        lambda: dot32(rate_part, first_down, NT),
        lambda: dot32(gate_grad, down_ref[:, 128:], NT),
    )
    total = jnp.zeros_like(change)
    moved = jnp.zeros_like(change)
    for j, grad in enumerate(grads):
        now = grad()
        total = total + now
        moved = moved + now * vec_ref[j : j + 1]
        sums_ref[j : j + 1] += jnp.sum(now * change, axis=0, keepdims=True)
    dnormed = total - moved + shifted(moved, edge_ref[:1], False)
    edge_ref[:1] = moved[:1]
    sums_ref[12:13] += jnp.sum(dnormed * unit, axis=0, keepdims=True)
    sums_ref[13:14] += jnp.sum(dnormed, axis=0, keepdims=True)
    dunit = dnormed * gain
    dx_ref[...] = scale * (
        dunit
        - jnp.mean(dunit, axis=-1, keepdims=True)
        - unit * jnp.mean(dunit * unit, axis=-1, keepdims=True)
    )

    @pl.when(step == 0)
    def _():
        sums_ref[6:7] = ffn_vec_ref[0:1] * 0.5
        sums_ref[14:16] = ffn_vec_ref[1:3] * 0.5
        zeros = jnp.zeros((1, OWN), jnp.float32)
        for target, source in ((7, 0), (8, 1), (9, 2), (10, 3), (11, 4), (16, 5), (17, 6)):
            mine = own_vec_ref[source : source + 1]
            sums_ref[target : target + 1] = jnp.concatenate(
                [jnp.where(core == 0, mine, zeros), jnp.where(core == 0, zeros, mine)], axis=1
            )
        for block in range(EMBED // 128):
            lanes = slice(block * 128, (block + 1) * 128)
            misc_ref[lanes, 512:640] = sums_ref[:, lanes].T


def front_backward(
    x, vectors, w_r, w_k, w_v, down, up, mixes, hid, grads, own_vec, ffn_vec
):
    tokens, width = x.shape
    steps = tokens // ROWS
    wide = pl.BlockSpec((ROWS, width), lambda i: (steps - 1 - i, 0))
    before = pl.BlockSpec(
        (16, width), lambda i: (jnp.maximum((steps - 1 - i) * (ROWS // 16) - 1, 0), 0)
    )
    own = pl.BlockSpec((ROWS, OWN), lambda i: (steps - 1 - i, 0))
    hid_spec = pl.BlockSpec((ROWS, 256), lambda i: (steps - 1 - i, 0))
    whole = lambda a: pl.BlockSpec(a.shape, lambda i: (0, 0))
    shape = jax.ShapeDtypeStruct
    return pl.pallas_call(
        front_back_kernel,
        grid=(steps,),
        in_specs=[wide, before]
        + [whole(a) for a in (vectors, w_r, w_k, w_v, down, up)]
        + [wide] * 3
        + [hid_spec]
        + [own] * 6
        + [whole(own_vec), whole(ffn_vec)],
        out_specs=[wide, pl.BlockSpec((EMBED, 640), lambda i: (0, 0))],
        out_shape=[shape((tokens, width), jnp.float32), shape((EMBED, 640), jnp.float32)],
        scratch_shapes=[
            pltpu.VMEM((8, width), jnp.float32), pltpu.VMEM((128, width), jnp.float32),
        ],
        compiler_params=pltpu.CompilerParams(vmem_limit_bytes=48 << 20),
        cost_estimate=SMALL,
        name="front_backward",
    )(x, x, vectors, w_r, w_k, w_v, down, up, *mixes, hid, *grads, own_vec, ffn_vec)


def ffn_back_kernel(
    len_ref, res_ref, before_ref, cot_ref, mine_ref, other_ref, vec_ref, wo_ref,
    grad_ref, narrow_ref, gated_ref, dvec_ref,
    edge_ref,
):
    step = pl.num_programs(0) - 1 - pl.program_id(0)

    @pl.when(pl.program_id(0) == 0)
    def _():
        edge_ref[...] = jnp.zeros_like(edge_ref)
        dvec_ref[...] = jnp.zeros_like(dvec_ref)

    gain, offset, coefficient = vec_ref[14:15], vec_ref[15:16], vec_ref[6:7]
    unit, scale = row_norm(res_ref[...])
    normed = unit * gain + offset
    tail, _ = row_norm(before_ref[...])
    edge = (tail[7:] * gain + offset) * jnp.where(step == 0, 0.0, 1.0)
    change = shifted(normed, edge, True) - normed
    grad = mine_ref[...].astype(jnp.float32) + other_ref[...].astype(jnp.float32)
    moved = grad * coefficient
    dnormed = grad - moved + shifted(moved, edge_ref[:1], False)
    edge_ref[:1] = moved[:1]
    sums = lambda x: jnp.sum(x, axis=0, keepdims=True)
    dvec_ref[0:1] += sums(grad * change)
    dvec_ref[1:2] += sums(dnormed * unit)
    dvec_ref[2:3] += sums(dnormed)
    dunit = dnormed * gain
    row = lax.broadcasted_iota(jnp.int32, grad.shape, 0) + step * ROWS
    out_grad = jnp.where(row < len_ref[0], cot_ref[...].astype(jnp.float32), 0.0)
    total = out_grad + scale * (
        dunit
        - jnp.mean(dunit, axis=-1, keepdims=True)
        - unit * jnp.mean(dunit * unit, axis=-1, keepdims=True)
    )
    grad_ref[...] = total
    small = total.astype(jnp.bfloat16)
    narrow_ref[...] = small
    gated_ref[...] = dot32(small, wo_ref[...], NT)


def ffn_backward(length, residual, cot, mine, other, vectors, w_o_rows):
    tokens, width = residual.shape
    steps = tokens // ROWS
    wide = pl.BlockSpec((ROWS, width), lambda i: (steps - 1 - i, 0))
    before = pl.BlockSpec(
        (8, width), lambda i: (jnp.maximum((steps - 1 - i) * (ROWS // 8) - 1, 0), 0)
    )
    own = pl.BlockSpec((ROWS, OWN), lambda i: (steps - 1 - i, 0))
    whole = lambda a: pl.BlockSpec(a.shape, lambda i: (0, 0))
    shape = jax.ShapeDtypeStruct
    return pl.pallas_call(
        ffn_back_kernel,
        grid=(steps,),
        in_specs=[pl.BlockSpec(memory_space=pltpu.SMEM), wide, before]
        + [wide] * 3
        + [whole(vectors), whole(w_o_rows)],
        out_specs=[wide, wide, own, pl.BlockSpec((8, width), lambda i: (0, 0))],
        out_shape=[
            shape((tokens, width), jnp.float32),
            shape((tokens, width), jnp.bfloat16),
            shape((tokens, OWN), jnp.float32),
            shape((8, width), jnp.float32),
        ],
        scratch_shapes=[pltpu.VMEM((8, width), jnp.float32)],
        compiler_params=pltpu.CompilerParams(vmem_limit_bytes=48 << 20),
        cost_estimate=SMALL,
        name="ffn_backward",
    )(length, residual, residual, cot, mine, other, vectors, w_o_rows)


def att_grad_kernel(m0_ref, m2_ref, m3_ref, dq_ref, dk_ref, dv_ref, send_a, keep_a, send_b, keep_b):
    chip = lax.axis_index("dp") // 2
    by_x, by_y = chip % 2 == 0, (chip // 2) % 2 == 0
    quarter = OWN // 2
    dv = dv_ref[...]
    first = ((m0_ref, dq_ref[...], 0, OWN), (m3_ref, dv[:, :quarter], OWN, quarter))
    second = ((m2_ref, dk_ref[...], 0, OWN), (m3_ref, dv[:, quarter:], OWN, quarter))
    for z in range(4):
        rows = slice(z * 256, (z + 1) * 256)
        for left, right, lane, width in first:
            block = dot32(left[:, rows], right, TN).astype(jnp.bfloat16)
            lanes = slice(lane, lane + width)
            for y in range(2):
                low, high = block[y * 128 : y * 128 + 64], block[y * 128 + 64 : y * 128 + 128]
                send_a[2 * z + y, :, lanes] = jnp.where(by_x, high, low)
                keep_a[2 * z + y, :, lanes] = jnp.where(by_x, low, high)
        for left, right, lane, width in second:
            block = dot32(left[:, rows], right, TN).astype(jnp.bfloat16)
            lanes = slice(lane, lane + width)
            for x in range(2):
                low, high = block[x * 64 : x * 64 + 64], block[128 + x * 64 : 128 + x * 64 + 64]
                send_b[2 * z + x, :, lanes] = jnp.where(by_y, high, low)
                keep_b[2 * z + x, :, lanes] = jnp.where(by_y, low, high)


def att_gradients(mixes, grads):
    space = pl.BlockSpec(memory_space=pltpu.VMEM)
    return pl.pallas_call(
        att_grad_kernel,
        in_specs=[space] * 6,
        out_specs=[space] * 4,
        out_shape=[jax.ShapeDtypeStruct((8, 64, OWN + OWN // 2), jnp.bfloat16)] * 4,
        compiler_params=pltpu.CompilerParams(vmem_limit_bytes=40 << 20),
        cost_estimate=SMALL,
        name="att_gradients",
    )(*mixes, *grads)


def swap(block, mask):
    size = lax.axis_size("dp")
    return lax.ppermute(block, "dp", [(i, i ^ mask) for i in range(size)])


def bit_of(mask):
    return (lax.axis_index("dp") // mask) % 2


def in_order(mask, own, other, axis):
    lower = bit_of(mask) == 0
    return jnp.where(
        lower, jnp.concatenate([own, other], axis=axis), jnp.concatenate([other, own], axis=axis)
    )


def chip_masks():
    size = lax.axis_size("dp")
    masks = []
    while 2 << len(masks) < size:
        masks.append(2 << len(masks))
    return masks


def steps_of(kind):
    masks = chip_masks()
    near, far = [[mask] for mask in masks[:2]], [[mask] for mask in masks[2:][::-1]]
    first = [[far[0][0], far[1][0], far[0][0] | far[1][0]]] if len(far) == 2 else far
    return [first + near[::-1], first + near, far + near[::-1], far + near, near + far][kind]


def meet(movers, *arrays):
    held = lax.optimization_barrier(tuple(tuple(m.arrived) for m in movers) + arrays)
    for mover, arrived in zip(movers, held):
        mover.arrived = list(arrived)
    return held[len(movers) :]


class Gather:
    def __init__(self, block, kind, places=(0,)):
        self.steps = steps_of(kind)
        self.held = block[None]
        self.places = [0]
        self.arrived = []
        self.masks = []

    def merge(self):
        if self.arrived:
            self.held = jnp.concatenate([self.held] + self.arrived, axis=0)
            self.places = self.places + [p ^ (m // 2) for m in self.masks for p in self.places]
            self.arrived = []

    def step(self):
        if self.steps:
            self.merge()
            self.masks = self.steps.pop(0)
            self.arrived = [swap(self.held, mask) for mask in self.masks]
        return self

    def run(self):
        while self.steps:
            self.step()
        return self

    def split(self, kinds):
        width = self.held.shape[-1] // len(kinds)
        out = []
        for i, kind in enumerate(kinds):
            part = Gather.__new__(Gather)
            cut = slice(i * width, (i + 1) * width)
            part.steps = steps_of(kind)[len(steps_of(kind)) - len(self.steps) :]
            part.held = self.held[..., cut]
            part.arrived = [x[..., cut] for x in self.arrived]
            part.places, part.masks = self.places, self.masks
            out.append(part)
        return out


def place_kernel(places, cuts, *refs):
    sources, outs = refs[: len(places)], refs[len(places) :]
    chip = lax.axis_index("dp") // 2
    for source, (part, list_of) in zip(sources, places):
        for j, place in enumerate(list_of):
            for out, (first, rows, lanes) in zip(outs, cuts):
                start = pl.multiple_of((chip ^ place) * rows, rows)
                lane, width = lanes[part]
                at = sum(w for _, w in lanes[:part])
                out[pl.ds(start, rows), at : at + width] = source[
                    j, first : first + rows, lane : lane + width
                ]


def assemble(gathers, cuts=None):
    gathers = [g.run() for g in gathers]
    rows = gathers[0].held.shape[1]
    cuts = cuts or ((0, rows, [(0, g.held.shape[2]) for g in gathers]),)
    sources, places = [], []
    for i, g in enumerate(gathers):
        sources += [g.held] + g.arrived
        shifts = [0] + [mask // 2 for mask in g.masks]
        places += [(i, [p ^ shift for p in g.places]) for shift in shifts]
    count = lax.axis_size("dp") // 2
    if any(cut[1] % 16 for cut in cuts):
        return assemble_plain(sources, places, cuts, count)
    space = pl.BlockSpec(memory_space=pltpu.VMEM)
    return pl.pallas_call(
        partial(place_kernel, places, cuts),
        in_specs=[space] * len(sources),
        out_specs=[space] * len(cuts),
        out_shape=[
            jax.ShapeDtypeStruct((count * n, sum(w for _, w in lanes)), sources[0].dtype)
            for _, n, lanes in cuts
        ],
        compiler_params=pltpu.CompilerParams(vmem_limit_bytes=32 << 20),
        cost_estimate=SMALL,
        name="assemble",
    )(*sources)


def assemble_plain(sources, places, cuts, count):
    chip = lax.axis_index("dp") // 2
    parts = []
    for part in sorted({part for part, _ in places}):
        blocks = jnp.concatenate([x for x, (at, _) in zip(sources, places) if at == part])
        where = [p for at, list_of in places if at == part for p in list_of]
        blocks = jnp.stack([blocks[where.index(i)] for i in range(count)])
        parts.append(jnp.take(blocks, chip ^ lax.iota(jnp.int32, count), axis=0))
    return [
        jnp.concatenate(
            [x[:, first : first + n, at : at + w] for x, (at, w) in zip(parts, lanes)], axis=-1
        ).reshape(count * n, -1)
        for first, n, lanes in cuts
    ]


class Scatter:
    def __init__(self, parts, kind):
        self.steps = steps_of(kind)[::-1]
        self.axes = chip_masks()[::-1]
        self.sources = [parts.reshape((2,) * len(self.axes) + parts.shape[1:])]
        self.arrived = []
        self.sent = None

    @classmethod
    def begun(cls, sent, kept, kind):
        out = cls.__new__(cls)
        out.steps = steps_of(kind)[::-1]
        out.axes = [axis for axis in chip_masks()[::-1] if axis != out.steps[0][0]]
        out.sources = [kept.reshape((2,) * len(out.axes) + kept.shape[1:])]
        out.arrived = []
        out.sent = [sent.reshape(out.sources[0].shape)]
        return out

    def pick(self, sources, mask, gone):
        out = []
        for x in sources:
            for place in reversed(range(len(self.axes))):
                axis = self.axes[place]
                if axis in gone:
                    which = bit_of(axis) if not mask & axis else 1 - bit_of(axis)
                    x = lax.dynamic_index_in_dim(x, which, place, keepdims=False)
            out.append(x)
        return out

    def prepare(self):
        if self.sent is not None:
            return self
        masks = self.steps[0]
        sources = self.sources + self.arrived
        gone = [axis for axis in self.axes if any(mask & axis for mask in masks)]
        self.sent = [
            sum(x.astype(jnp.float32) for x in self.pick(sources, mask, gone)).astype(jnp.bfloat16)
            for mask in masks
        ]
        self.sources = self.pick(sources, 0, gone)
        self.axes = [axis for axis in self.axes if axis not in gone]
        self.arrived = []
        return self

    def step(self):
        return together([self])[0]

    def run(self):
        while self.steps:
            self.step()
        return self

    def total(self):
        return sum(x.astype(jnp.float32) for x in self.sources + self.arrived)


def together(parts):
    if not parts[0].steps:
        return parts
    for part in parts:
        part.prepare()
    for i, mask in enumerate(parts[0].steps[0]):
        sent = [part.sent[i] for part in parts]
        got = swap(sent[0] if len(sent) == 1 else jnp.concatenate(sent, axis=-1), mask)
        at = 0
        for part, x in zip(parts, sent):
            part.arrived.append(got[..., at : at + x.shape[-1]])
            at += x.shape[-1]
    for part in parts:
        part.steps.pop(0)
        part.sent = None
    return parts


def norm_rows(features, gain_row, offset_row):
    average = jnp.mean(features, axis=-1, keepdims=True)
    centred = features - average
    variance = jnp.mean(centred * centred, axis=-1, keepdims=True)
    return centred * lax.rsqrt(variance + 1e-05) * gain_row + offset_row


def product(operand, weight_matrix):
    return jnp.dot(operand, weight_matrix, preferred_element_type=jnp.float32)


def input_gradient_rows(upstream_gradient, weight_matrix):
    return lax.dot_general(
        upstream_gradient,
        weight_matrix,
        (((1,), (1,)), ((), ())),
        preferred_element_type=jnp.float32,
    )


def weight_gradient(operand, upstream_gradient):
    return lax.dot_general(
        operand, upstream_gradient, (((0,), (0,)), ((), ())), preferred_element_type=jnp.float32
    )


def earlier(rows):
    return jnp.concatenate([jnp.zeros_like(rows[:1]), rows[:-1]], axis=0)


def ffn_mix(residual, vectors):
    second = norm_rows(residual, vectors[14], vectors[15])
    return second + (earlier(second) - second) * vectors[6]


def narrow(x):
    return x.astype(jnp.bfloat16)


def local(
    inputs,
    lengths,
    attention_projections,
    channel_key_weight,
    channel_value_weight,
    lowrank_down_weight,
    lowrank_up_weight,
    per_feature_parameters,
    cotangent,
):
    devices = lax.axis_size("dp")
    chips = devices // 2
    device = lax.axis_index("dp")
    chip, core = device // 2, device % 2
    row_count = inputs.shape[0]
    slots = 2 * row_count
    share = EMBED // devices
    pair_share = 2 * share
    units = channel_value_weight.shape[0]
    half_units = chips * units

    def own_cut(x, which):
        return lax.dynamic_slice_in_dim(x, which * OWN, OWN, x.ndim - 1)

    def own_rows(x, which):
        return lax.dynamic_slice_in_dim(x, which * row_count, row_count, 0)

    pair_rows = in_order(
        1,
        own_cut(attention_projections, core),
        swap(own_cut(attention_projections, 1 - core), 1),
        1,
    )
    lora = jnp.concatenate([lowrank_down_weight, lowrank_up_weight.T], axis=1)
    vector_rows = jnp.pad(per_feature_parameters.T, ((0, 0), (0, 128 - 18)))
    vector_rows = vector_rows.reshape(share // 4, OWN)
    first_rows = 3 * pair_share
    misc_rows = share + share // 4 + (share // 4) % 16
    block = jnp.concatenate(
        [
            pair_rows[:3].reshape(first_rows, OWN),
            lora,
            jnp.pad(vector_rows, ((0, (share // 4) % 16), (0, 0))),
        ],
        axis=0,
    )
    half = half_units // 2
    quarter = OWN // 2
    first = Gather(block, 0).step()
    w_o_part = Gather(pair_rows[3], 4).step().step()
    key_in, raw, cot, _ = meet([], channel_key_weight, inputs, cotangent, first.held)
    key_cut = key_in.reshape(share, chips, 2, units)

    def key_columns(which):
        return lax.dynamic_index_in_dim(key_cut, which, 2, keepdims=False).reshape(share, half_units)

    key_rows = in_order(1, key_columns(core), swap(key_columns(1 - core), 1), 0)
    tokens = in_order(1, raw, swap(raw, 1), 0)
    cot = in_order(1, cot, swap(cot, 1), 0)
    key_rows, tokens, cot = meet([first, w_o_part], key_rows, tokens, cot)
    first = first.split((0, 1))
    for part in first:
        part.step()
    key_part = Gather(key_rows, 2).step()
    (tokens,) = meet(first, tokens)
    for part in first:
        part.step()
    value_block, *_ = meet([key_part], channel_value_weight, *[part.held for part in first])
    key_part.step()
    value_part = Gather(value_block, 2).step()
    (tokens,) = meet(first + [key_part, value_part, w_o_part], tokens)
    key_parts = key_part.split((2, 3))
    for part in key_parts:
        part.step()
    w_r, w_k, w_v, misc = assemble(
        first,
        [(i * pair_share, pair_share, [(0, quarter)] * 2) for i in range(3)]
        + [(first_rows, misc_rows, [(0, quarter)] * 2)],
    )
    misc = misc.reshape(chips, 1, misc_rows, OWN)
    misc = in_order(1, misc, swap(misc, 1), 1)
    value_part.step()
    w_o_part.step()
    lora = misc[:, :, :share].reshape(EMBED, OWN)
    down, up_t = lora[:, :256], lax.dynamic_slice_in_dim(lora[:, 256:], core * OWN, OWN, 0)
    vectors = misc[:, :, share : share + share // 4].reshape(EMBED, 128)[:, :18].T
    vectors = vectors.astype(jnp.float32)
    own_vectors = own_cut(vectors, core)
    used = jnp.concatenate([own_vectors[7:12], own_vectors[16:18], own_vectors[:1]], axis=0)
    length = lax.dynamic_index_in_dim(lengths, chip, 0)
    live = (lax.iota(jnp.int32, slots) < length)[:, None]

    *mixes, queries, keys, values, decay_low, rate_low, gate_rows, hid = front_forward(
        tokens, vectors, w_r, w_k, w_v, down, up_t
    )
    terms = meet(
        key_parts + [value_part, w_o_part],
        queries, keys, values, decay_low, rate_low, gate_rows,
    )
    value_parts = value_part.split((2, 3))
    for part in key_parts + value_parts:
        part.step()
    w_o_part.step()
    blocks = slots // (CHUNK * STEP_CHUNKS)
    early = blocks // 2
    zero_state = jnp.zeros((2, CHUNK, LANES), jnp.float32)
    gated, *saved, _ = wkv_forward(0, blocks, length, used, zero_state, terms)
    gated, cot, tokens = meet(key_parts + value_parts + [w_o_part], gated, cot, tokens)
    for part in value_parts:
        part.step()
    gated, *_ = meet([w_o_part], gated, *[part.held for part in value_parts])
    gated_all = in_order(1, gated, swap(gated, 1), 1)
    (w_o_own,) = assemble([w_o_part])
    w_o = in_order(1, w_o_own, swap(w_o_own, 1), 1)
    (key_weight,) = assemble(key_parts)
    residual = tokens.astype(jnp.float32) + product(gated_all, w_o)
    ffn_in = narrow(ffn_mix(residual, vectors))
    positive = jax.nn.relu(product(ffn_in, key_weight))
    hidden = narrow(jnp.square(positive))
    out_narrow = jnp.where(live, cot, jnp.zeros_like(cot))
    value_cuts = ((0, quarter), (quarter, OWN), (OWN, EMBED))
    value_grads = [
        narrow(weight_gradient(hidden, out_narrow[:, lo:hi])).reshape(chips, units, hi - lo)
        for lo, hi in value_cuts
    ]
    w_o_rows = lax.dynamic_slice_in_dim(w_o, core * OWN, OWN, 0)
    hidden, positive, out_narrow, w_o_rows, *value_grads = meet(
        value_parts, hidden, positive, out_narrow, w_o_rows, *value_grads
    )
    (value_weight,) = assemble(value_parts)

    value_scatter = [Scatter(x, kind).step() for kind, x in zip((2, 3, 4), value_grads)]
    late_scatter = value_scatter.pop()
    pre_narrow = narrow(2.0 * positive * input_gradient_rows(out_narrow, value_weight))
    ffn_in_grad = narrow(input_gradient_rows(pre_narrow, key_weight))
    other_grad = swap(ffn_in_grad, 1)
    grad_key = narrow(weight_gradient(ffn_in, pre_narrow)).reshape(chips, pair_share, half_units)
    residual_grad, attended_grad, gated_grad, ffn_vec = ffn_backward(
        length, residual, cot, ffn_in_grad, other_grad, vectors, w_o_rows
    )
    grad_o = narrow(weight_gradient(gated_all, own_cut(attended_grad, core)))
    grad_o = grad_o.reshape(chips, pair_share, OWN)
    key_scatter = [
        Scatter(
            jnp.concatenate(
                [
                    grad_key[:, :, i * half : (i + 1) * half],
                    grad_o[:, :, i * quarter : (i + 1) * quarter],
                ],
                axis=-1,
            ),
            2 + i,
        ).prepare()
        for i in range(2)
    ]
    gated_grad, *sent = meet(value_scatter, gated_grad, *[m.sent[0] for m in key_scatter])
    for part, x in zip(key_scatter, sent):
        part.sent = [x]
        part.step()
    for part in value_scatter:
        part.step()
    terms = [*terms, gated_grad, *saved]
    zero_sums = jnp.zeros((8, OWN), jnp.float32)
    *before, sums, state = wkv_backward(
        early, blocks - early, length, used, zero_state, zero_sums, terms
    )
    state, sums = meet(value_scatter + [late_scatter], state, sums)
    together(value_scatter)
    late_scatter.step()
    *low_grads, own_vec, _ = wkv_backward(0, early, length, used, state, sums, terms, before)
    *low_grads, own_vec = meet(
        key_scatter + value_scatter + [late_scatter], *low_grads, own_vec
    )
    for part in key_scatter:
        part.step()
    together(value_scatter)
    if pair_share == 64:
        sent_a, kept_a, sent_b, kept_b = att_gradients(
            (mixes[0], mixes[2], mixes[3]), low_grads[:3]
        )
        att_scatter = [Scatter.begun(sent_a, kept_a, 2), Scatter.begun(sent_b, kept_b, 3)]
    else:
        grads = [narrow(weight_gradient(mixes[m], g)) for m, g in zip((0, 2, 3), low_grads)]
        att_scatter = [
            Scatter(jnp.concatenate(x, axis=1).reshape(chips, pair_share, 3 * quarter), 2 + i).prepare()
            for i, x in enumerate(
                ((grads[0], grads[2][:, :quarter]), (grads[1], grads[2][:, quarter:]))
            )
        ]
    own_vec, *sent = meet([], own_vec, *[m.sent[0] for m in att_scatter])
    for part, x in zip(att_scatter, sent):
        part.sent = [x]
        part.step()
    token_part, misc_grad = front_backward(
        tokens, vectors, w_r, w_k, w_v, down, up_t, (mixes[1], mixes[4], mixes[5]), hid,
        low_grads, own_vec, ffn_vec,
    )
    token_part, misc_grad, hidden = meet(
        key_scatter + value_scatter, token_part, misc_grad, hidden
    )
    misc_grad = misc_grad.reshape(chips, 2, share, 640)
    misc_mine = lax.dynamic_index_in_dim(misc_grad, core, 1, keepdims=False)
    misc_other = narrow(lax.dynamic_index_in_dim(misc_grad, 1 - core, 1, keepdims=False))
    misc_sum = misc_mine + swap(misc_other, 1).astype(jnp.float32)
    misc_sum = jnp.concatenate([misc_sum[..., :320], misc_sum[..., 320:]], axis=1)
    misc_scatter = Scatter(misc_sum, 3)
    masks = chip_masks()
    misc_scatter.steps = [[masks[0], masks[1], masks[0] | masks[1]]] + misc_scatter.steps[2:]
    misc_scatter.step()
    (token_part,) = meet(att_scatter + [misc_scatter], token_part)
    for part in att_scatter:
        part.step()
    together(key_scatter)
    late_scatter.step()
    ffn_part = product(hidden, value_weight)
    token_part, ffn_part = meet(att_scatter + key_scatter + [late_scatter], token_part, ffn_part)
    last_parts = att_scatter + [misc_scatter]
    if len(misc_scatter.steps) == 2:
        for part in last_parts:
            part.steps = [[masks[2], masks[3], masks[2] | masks[3]]]
    together(last_parts)
    together(key_scatter)
    late_scatter.step()
    input_gradient = (
        own_rows(residual_grad, core)
        + own_rows(token_part, core)
        + swap(own_rows(token_part, 1 - core), 1)
    )
    ffn_out = own_rows(ffn_part, core) + swap(own_rows(ffn_part, 1 - core), 1)
    output = narrow(jnp.where(own_rows(live, core), own_rows(residual, core) + ffn_out, 0.0))
    value_sum = jnp.concatenate(
        [x.run().total() for x in value_scatter + [late_scatter]], axis=1
    )
    key_sum = jnp.concatenate([x.run().total() for x in key_scatter], axis=1)
    input_gradient, value_sum, key_sum = meet(last_parts, input_gradient, value_sum, key_sum)
    while last_parts[0].steps:
        together(last_parts)
    last_sum = jnp.concatenate([x.total() for x in last_parts], axis=1)
    wide = 3 * quarter
    each_half = half + quarter
    pair_sum = jnp.concatenate(
        [
            last_sum[:, :OWN],
            last_sum[:, wide : wide + OWN],
            last_sum[:, OWN:wide],
            last_sum[:, wide + OWN : 2 * wide],
            key_sum[:, half:each_half],
            key_sum[:, each_half + half :],
            key_sum[:, :half],
            key_sum[:, each_half : each_half + half],
        ],
        axis=1,
    )
    misc_sum = last_sum[:, 2 * wide :]
    misc_sum = jnp.concatenate([misc_sum[:share], misc_sum[share:]], axis=1)
    pair_sum = pair_sum.reshape(2, share, -1)
    mine = lax.dynamic_index_in_dim(pair_sum, core, 0, keepdims=False)
    theirs = swap(lax.dynamic_index_in_dim(pair_sum, 1 - core, 0, keepdims=False), 1)
    shard_mixer = jnp.stack(
        [
            in_order(1, mine[:, i * OWN : (i + 1) * OWN], theirs[:, i * OWN : (i + 1) * OWN], 1)
            for i in range(4)
        ]
    )
    shard_key = in_order(
        1,
        mine[:, 4 * OWN :].reshape(share, chips, 1, units),
        theirs[:, 4 * OWN :].reshape(share, chips, 1, units),
        2,
    ).reshape(share, 2 * half_units)
    return (
        output,
        input_gradient,
        shard_mixer,
        shard_key,
        value_sum,
        misc_sum[:, :256],
        misc_sum[:, 256:512].T,
        misc_sum[:, 512:530].T,
    )


def solution(mesh):
    in_specs = (
        P("dp", None),
        P(),
        P(None, "dp", None),
        P("dp", None),
        P("dp", None),
        P("dp", None),
        P(None, "dp"),
        P(None, "dp"),
        P("dp", None),
    )
    out_specs = (
        P("dp", None),
        P("dp", None),
        P(None, "dp", None),
        P("dp", None),
        P("dp", None),
        P("dp", None),
        P(None, "dp"),
        P(None, "dp"),
    )
    return jax.shard_map(local, mesh=mesh, in_specs=in_specs, out_specs=out_specs, check_vma=False)
```

```python
from functools import partial

import jax
import jax.numpy as jnp
from jax import lax
from jax.experimental import pallas as pl
from jax.experimental.pallas import tpu as pltpu
from jax.sharding import PartitionSpec as P

HEADS = 16
HEAD_SIZE = 64
DECAY_RANK = 64
RATE_RANK = 64
EMBED = 1024
OWN = EMBED // 2
PRECISE = lax.Precision.HIGHEST


CHUNK = 64
LANES = 256
GROUP_HEADS = 4
STEP_CHUNKS = 2
SMALL = pl.CostEstimate(flops=1, bytes_accessed=1, transcendentals=0)

NN = (((1,), (0,)), ((), ()))
NT = (((1,), (1,)), ((), ()))
TN = (((0,), (0,)), ((), ()))


def halves(x):
    high = x.astype(jnp.bfloat16)
    return high, (x - high.astype(jnp.float32)).astype(jnp.bfloat16)


def dot32(a, b, dims):
    return lax.dot_general(a, b, dims, preferred_element_type=jnp.float32)


def mul(left, right, dims=NN):
    rows = left[0].shape[0]
    both = dot32(jnp.concatenate(left, axis=0), right[0], dims)
    return both[:rows] + both[rows:] + dot32(left[0], right[1], dims)


def tmul(left, right, masks):
    full = (
        dot32(left[0], right[0], TN) + dot32(left[1], right[0], TN) + dot32(left[0], right[1], TN)
    )
    return sum(full[h * CHUNK : (h + 1) * CHUNK] * masks[h][:1].astype(jnp.float32) for h in range(GROUP_HEADS))


def spread(pair, masks):
    return tuple(
        jnp.concatenate([part * masks[h] for h in range(GROUP_HEADS)], axis=0) for part in pair
    )


def stack(first, second):
    return tuple(jnp.concatenate([x, y], axis=0) for x, y in zip(first, second))


def head_masks():
    lane = lax.broadcasted_iota(jnp.int32, (CHUNK, LANES), 1) // CHUNK
    return [(lane == h).astype(jnp.float32).astype(jnp.bfloat16) for h in range(GROUP_HEADS)]


def places():
    row = lax.broadcasted_iota(jnp.int32, (CHUNK, LANES), 0)
    col = lax.broadcasted_iota(jnp.int32, (CHUNK, LANES), 1) % CHUNK
    return row, col


def running_sum(x, upper=False):
    row = lax.broadcasted_iota(jnp.int32, (CHUNK, CHUNK), 0)
    col = lax.broadcasted_iota(jnp.int32, (CHUNK, CHUNK), 1)
    ones = (row <= col if upper else col <= row).astype(jnp.float32).astype(jnp.bfloat16)
    high, rest = halves(x)
    low = (x - high.astype(jnp.float32) - rest.astype(jnp.float32)).astype(jnp.bfloat16)
    return dot32(ones, high, NN) + dot32(ones, rest, NN) + dot32(ones, low, NN)


def scaled_forms(q, w, k, a, b):
    total = running_sum(w)
    before = total - w
    middle = total[CHUNK // 2 - 1 : CHUNK // 2]
    end = total[CHUNK - 1 :]
    ea = jnp.exp(before - middle)
    eq = jnp.exp(total - middle)
    eb = jnp.exp(middle - total)
    ee = jnp.exp(end - total)
    return (a * ea, q * eq, b * eb, k * eb, b * ee, k * ee), (ea, eq, eb, ee), (jnp.exp(middle), jnp.exp(end))


def each(fn, *columns):
    return [fn(*row) for row in zip(*columns)]


def block_ones():
    row = lax.broadcasted_iota(jnp.int32, (LANES, LANES), 0) // CHUNK
    col = lax.broadcasted_iota(jnp.int32, (LANES, LANES), 1) // CHUNK
    return (row == col).astype(jnp.float32).astype(jnp.bfloat16)


def head_sum(x, ones):
    rows = x.shape[0]
    both = dot32(jnp.concatenate(halves(x), axis=0), ones, NN)
    return both[:rows] + both[rows:]


def prepared(keys, decay_low, rate_low, live, vec, ones):
    sig = jax.nn.sigmoid(vec[0] + decay_low)
    log_decay = (-0.6065306597126334) * sig * live
    rates = jax.nn.sigmoid(vec[1] + rate_low)
    scaled = keys * vec[2]
    inverse = lax.rsqrt(head_sum(scaled * scaled, ones) + 1e-06)
    unit_keys = scaled * inverse
    factor = (1.0 + (rates - 1.0) * vec[3]) * live
    return log_decay, keys * factor, -unit_keys, unit_keys * rates * live, sig, rates, inverse, factor


def read_out(o, q, k, v, vec, ones):
    centred = o - head_sum(o, ones) * (1.0 / CHUNK)
    scale = lax.rsqrt(head_sum(centred * centred, ones) * (1.0 / CHUNK) + 0.00064)
    normed = centred * scale
    weight = head_sum(q * k * vec[4], ones)
    return normed, scale, weight, normed * vec[5] + vec[6] + weight * v


def unit_slices():
    return [
        (slice(c * CHUNK, (c + 1) * CHUNK), slice(g * LANES, (g + 1) * LANES))
        for c in range(STEP_CHUNKS)
        for g in range(2)
    ]


def unit_live(length, step):
    row = lax.broadcasted_iota(jnp.int32, (CHUNK, LANES), 0)
    start = step * (STEP_CHUNKS * CHUNK)
    live = [(row + (start + c * CHUNK) < length).astype(jnp.float32) for c in range(STEP_CHUNKS)]
    return [live[c] for c in range(STEP_CHUNKS) for g in range(2)]


def unit_vectors(vec_ref):
    vec = [[vec_ref[i : i + 1, g * LANES : (g + 1) * LANES] for i in range(7)] for g in range(2)]
    return [vec[g] for c in range(STEP_CHUNKS) for g in range(2)]


def forward_kernel(base, *refs):
    len_ref, vec_ref, start_ref, q_ref, keys_ref, v_ref, dl_ref, rl_ref, gate_ref = refs[:9]
    (
        out_ref, o_ref, t_ref, aqb_ref, aak_ref, aqk_ref, y_ref, z_ref, trt_ref, qe_ref, state_ref,
    ) = refs[-11:]

    @pl.when(pl.program_id(0) == 0)
    def _():
        state_ref[...] = start_ref[...]

    masks = head_masks()
    row, col = places()
    strict = (col < row).astype(jnp.float32)
    within = (col <= row).astype(jnp.float32)
    eye = (col == row).astype(jnp.float32)
    ones = block_ones()
    units = unit_slices()
    live = unit_live(len_ref[0], pl.program_id(0) + base)
    vec = unit_vectors(vec_ref)
    load = lambda ref: [ref[u] for u in units]
    q, keys, v = load(q_ref), load(keys_ref), load(v_ref)
    ready = each(
        lambda x, y, z, m, n: prepared(x, y, z, m, n, ones), keys, load(dl_ref), load(rl_ref), live, vec
    )
    w, k, a, b = ([x[i] for x in ready] for i in range(4))
    forms = each(scaled_forms, q, w, k, a, b)
    ah, qh, bh, kh, bt, kt = ([f[0][i] for f in forms] for i in range(6))
    emid = [f[2][0] for f in forms]
    eend = [f[2][1] for f in forms]
    aq = each(lambda x, y: halves(jnp.concatenate([x, y], axis=0)), ah, qh)
    with_b = each(lambda l, r: mul(l, spread(halves(r), masks), NT), aq, bh)
    with_k = each(lambda l, r: mul(l, spread(halves(r), masks), NT), aq, kh)
    aab = [x[:CHUNK] * strict for x in with_b]
    aqb = [halves(x[CHUNK:] * within) for x in with_b]
    aak = [halves(x[:CHUNK] * strict) for x in with_k]
    aqk = [halves(x[CHUNK:] * within) for x in with_k]
    p = [halves(x * (row // 8 == col // 8)) for x in aab]
    t = [eye + x * (row // 8 == col // 8) for x in aab]
    p2 = each(lambda x: halves(mul(x, spread(x, masks))), p)
    both = each(lambda x, y: mul(stack(x, halves(y)), spread(x, masks)), p2, t)
    p4 = [halves(x[:CHUNK]) for x in both]
    t = each(lambda x, y: x + y[CHUNK:], t, both)
    t = each(lambda x, y: x + mul(halves(x), spread(y, masks)), t, p4)
    for size in (8, 16, 32):
        corner = ((row // size) % 2 == 1) & (col // size == row // size - 1)
        ts = [halves(x) for x in t]
        n = [halves(x * corner) for x in aab]
        tn = each(lambda x, y: halves(mul(x, spread(y, masks))), ts, n)
        t = each(lambda x, y, z: x + mul(y, spread(z, masks)), t, tn, ts)
    ts = [halves(x) for x in t]
    vs = [halves(x) for x in v]
    vm = [spread(x, masks) for x in vs]
    wide = each(lambda x, y, e: mul(x, spread(halves(y * e), masks)), ts, ah, emid)
    r0 = each(mul, aak, vm)
    y0 = each(lambda x, y: mul(x, spread(halves(y), masks)), ts, r0)
    wides = [halves(x) for x in wide]
    qe = each(lambda x, e, y, z: x * e + mul(y, spread(z, masks)), qh, emid, aqb, wides)
    y0s = [halves(x) for x in y0]
    part = each(lambda x, y, z, u: mul(x, spread(y, masks)) + mul(z, u), aqb, y0s, aqk, vm)
    bts = [halves(x) for x in bt]
    diag = [eye * e for e in eend]
    tr = each(lambda x, y, d: tmul(x, y, masks) + d, bts, wides, diag)
    trt = each(lambda x, y, d: tmul(y, x, masks) + d, bts, wides, diag)
    inject = each(lambda x, y, z, u: tmul(stack(x, halves(y)), stack(z, u), masks), bts, kt, y0s, vs)
    wq = each(lambda x, y: stack(x, halves(y)), wides, qe)
    z = []
    out = []
    for c in range(STEP_CHUNKS):
        for g in range(2):
            i = c * 2 + g
            now = state_ref[g]
            nows = spread(halves(now), masks)
            state_ref[g] = mul(halves(tr[i]), nows) + inject[i]
            z.append(now)
            out.append(mul(wq[i], nows))
    o = each(lambda x, y: x[CHUNK:] + y, out, part)
    mixed = each(lambda x, y, z, m, n: read_out(x, y, z, m, n, ones)[3], o, q, k, v, vec)
    for i, u in enumerate(units):
        out_ref[u] = (mixed[i] * gate_ref[u]).astype(jnp.bfloat16)
        o_ref[u] = o[i]
        y_ref[u] = out[i][:CHUNK] + y0[i]
        t_ref[u] = t[i]
        aqb_ref[u] = with_b[i][CHUNK:] * within
        aak_ref[u] = with_k[i][:CHUNK] * strict
        aqk_ref[u] = with_k[i][CHUNK:] * within
        z_ref[u] = z[i]
        trt_ref[u] = trt[i]
        qe_ref[u] = qe[i]


def backward_kernel(base, *refs):
    (
        len_ref, vec_ref, start_ref, sums_ref, q_ref, keys_ref, v_ref, dl_ref, rl_ref, gate_ref,
        g_ref, o_ref, t_ref, aqb_ref, aak_ref, aqk_ref, y_ref, z_ref, trt_ref, qe_ref,
    ) = refs[:20]
    dq_ref, dkeys_ref, dv_ref, ddl_ref, drl_ref, dgate_ref, dvec_ref, state_ref = refs[-8:]
    step = base + pl.num_programs(0) - 1 - pl.program_id(0)

    @pl.when(pl.program_id(0) == 0)
    def _():
        state_ref[...] = start_ref[...]
        dvec_ref[...] = sums_ref[...]

    masks = head_masks()
    row, col = places()
    strict = (col < row).astype(jnp.float32)
    within = (col <= row).astype(jnp.float32)
    ones = block_ones()
    units = unit_slices()
    live = unit_live(len_ref[0], step)
    vec = unit_vectors(vec_ref)
    load = lambda ref: [ref[u] for u in units]
    q, keys, v, g = load(q_ref), load(keys_ref), load(v_ref), load(g_ref)
    ready = each(
        lambda x, y, z, m, n: prepared(x, y, z, m, n, ones), keys, load(dl_ref), load(rl_ref), live, vec
    )
    w, k, a, b, sig, rates, inverse, factor = ([x[i] for x in ready] for i in range(8))
    seen = each(lambda x, y, z, m, n: read_out(x, y, z, m, n, ones), load(o_ref), q, k, v, vec)
    normed, scale, weight, mixed = ([x[i] for x in seen] for i in range(4))
    gate = load(gate_ref)
    dgate = each(lambda x, y: x * y, g, mixed)
    dmix = each(lambda x, y: x * y, g, gate)
    dn = each(lambda x, n: x * n[5], dmix, vec)
    do = each(
        lambda x, n, r: r
        * (x - head_sum(x, ones) * (1.0 / CHUNK) - n * (head_sum(x * n, ones) * (1.0 / CHUNK))),
        dn, normed, scale,
    )
    dweight = each(lambda x, y: head_sum(x * y, ones), dmix, v)
    do = [halves(x) for x in do]
    qe, trt, t, aqb, aak, aqk, ys = (
        [halves(x) for x in load(ref)]
        for ref in (qe_ref, trt_ref, t_ref, aqb_ref, aak_ref, aqk_ref, y_ref)
    )
    z = load(z_ref)
    vs = [halves(x) for x in v]
    h = each(lambda x, y: tmul(x, y, masks), qe, do)
    dz = [None] * len(units)
    for c in reversed(range(STEP_CHUNKS)):
        for g in range(2):
            i = c * 2 + g
            now = state_ref[g]
            dz[i] = now
            state_ref[g] = mul(trt[i], spread(halves(now), masks)) + h[i]
    dzs = [spread(halves(x), masks) for x in dz]
    zs = [spread(halves(x), masks) for x in z]
    forms = each(scaled_forms, q, w, k, a, b)
    ah, qh, bh, kh, bt, kt = ([f[0][i] for f in forms] for i in range(6))
    ea, eq, eb, ee = ([f[1][i] for f in forms] for i in range(4))
    emid = [f[2][0] for f in forms]
    eend = [f[2][1] for f in forms]
    from_end = each(lambda x, y, s: mul(halves(jnp.concatenate([x, y], axis=0)), s), bt, kt, dzs)
    dy = each(lambda x, y, s: halves(tmul(x, y, masks) + s[:CHUNK]), aqb, do, from_end)
    dr = each(lambda x, y: halves(tmul(x, y, masks)), t, dy)
    ro = each(stack, dr, do)
    dv = each(lambda x, y, s, f: tmul(stack(x, y), s, masks) + f[CHUNK:], aak, aqk, ro, from_end)
    mask2 = jnp.concatenate([strict, within], axis=0)
    dab = each(lambda s, y: halves(mul(s, spread(y, masks), NT) * mask2), ro, ys)
    dak = each(lambda s, y: halves(mul(s, spread(y, masks), NT) * mask2), ro, vs)
    dst = each(lambda s, y: mul(s, y, NT), ro, zs)
    daq = each(
        lambda s, e, x, bb, y, kk: s * e + mul(x, spread(halves(bb), masks)) + mul(y, spread(halves(kk), masks)),
        dst, emid, dab, bh, dak, kh,
    )
    aq = each(lambda x, y: halves(jnp.concatenate([x, y], axis=0)), ah, qh)
    dbh = each(lambda x, y: tmul(x, y, masks), dab, aq)
    dkh = each(lambda x, y: tmul(x, y, masks), dak, aq)
    dend = each(lambda y, x, s: mul(stack(y, x), s, NT), ys, vs, dzs)
    row_of_ones = jnp.ones((8, LANES), jnp.bfloat16)
    sums = lambda x: jnp.sum(x, axis=0, keepdims=True)
    for i, u in enumerate(units):
        da = daq[i][:CHUNK] * ea[i]
        dq = daq[i][CHUNK:] * eq[i]
        dbt = dend[i][:CHUNK] * ee[i]
        dkt = dend[i][CHUNK:] * ee[i]
        db = dbh[i] * eb[i] + dbt
        dk = dkh[i] * eb[i] + dkt
        pa = da * a[i]
        diff = dq * q[i] - db * b[i] - dk * k[i] + pa
        zz = spread(halves(z[i] * dz[i]), masks)
        carry = (dot32(row_of_ones, zz[0], NT) + dot32(row_of_ones, zz[1], NT))[:1] * eend[i]
        carry = carry + sums(dbt * b[i] + dkt * k[i])
        dw = running_sum(diff, upper=True) - pa + carry
        from_bonus = dweight[i] * vec[i][4]
        dk = dk + from_bonus * q[i]
        dq_ref[u] = (dq + from_bonus * k[i]).astype(jnp.bfloat16)
        dv_ref[u] = (dv[i] + weight[i] * dmix[i]).astype(jnp.bfloat16)
        dgate_ref[u] = dgate[i].astype(jnp.bfloat16)
        unit_keys = -a[i]
        db = db * live[i]
        du = db * rates[i] - da
        dscaled = inverse[i] * (du - unit_keys * head_sum(du * unit_keys, ones))
        dkl = dk * keys[i] * live[i]
        drl = (db * unit_keys + dkl * vec[i][3]) * rates[i] * (1.0 - rates[i])
        ddl = dw * w[i] * (1.0 - sig[i])
        dkeys_ref[u] = (dk * factor[i] + dscaled * vec[i][2]).astype(jnp.bfloat16)
        ddl_ref[u] = ddl.astype(jnp.bfloat16)
        drl_ref[u] = drl.astype(jnp.bfloat16)
        parts = (
            ddl, drl, dscaled * keys[i], dkl * (rates[i] - 1.0),
            dweight[i] * q[i] * k[i], dmix[i] * normed[i], dmix[i],
        )
        lanes = u[1]
        for j, x in enumerate(parts):
            dvec_ref[j : j + 1, lanes] += sums(x)


def wkv_call(kernel, base, steps, small, arrays, outs, sums, previous, name):
    tokens, width = arrays[0].shape
    rows = CHUNK * STEP_CHUNKS
    last = base + steps - 1
    turned = kernel is backward_kernel
    spec = pl.BlockSpec((rows, width), lambda i: (last - i if turned else base + i, 0))
    state = pl.BlockSpec((2, CHUNK, LANES), lambda i: (0, 0, 0))
    whole = pl.BlockSpec((8, width), lambda i: (0, 0))
    shape = jax.ShapeDtypeStruct
    first = [pl.BlockSpec(memory_space=pltpu.SMEM), whole, state] + [whole] * sums
    held = list(previous or ())
    start = len(first) + len(arrays)
    return pl.pallas_call(
        partial(kernel, base),
        grid=(steps,),
        in_specs=first + [spec] * len(arrays) + [pl.BlockSpec(memory_space=pl.ANY)] * len(held),
        out_specs=[spec] * len(outs) + [whole] * sums + [state],
        out_shape=[shape((tokens, width), dtype) for dtype in outs]
        + [shape((8, width), jnp.float32)] * sums
        + [shape((2, CHUNK, LANES), jnp.float32)],
        input_output_aliases={start + i: i for i in range(len(held))},
        compiler_params=pltpu.CompilerParams(vmem_limit_bytes=56 << 20),
        cost_estimate=SMALL,
        name=name,
    )(*small, *arrays, *held)


def wkv_forward(base, steps, length, vec, state, arrays, previous=None):
    outs = [jnp.bfloat16] + [jnp.float32] * 9
    return wkv_call(
        forward_kernel, base, steps, (length, vec, state), arrays, outs, 0, previous, "wkv_forward"
    )


def wkv_backward(base, steps, length, vec, state, sums, arrays, previous=None):
    outs = [jnp.bfloat16] * 6
    return wkv_call(
        backward_kernel, base, steps, (length, vec, state, sums), arrays, outs, 1, previous,
        "wkv_backward",
    )


ROWS = 128


def row_norm(x):
    centred = x - jnp.mean(x, axis=-1, keepdims=True)
    scale = lax.rsqrt(jnp.mean(centred * centred, axis=-1, keepdims=True) + 1e-05)
    return centred * scale, scale


def shifted(x, edge, down):
    rows = x.shape[0]
    row = lax.broadcasted_iota(jnp.int32, x.shape, 0)
    if down:
        return jnp.where(row == 0, edge, pltpu.roll(x, 1, 0))
    return jnp.where(row == rows - 1, edge, pltpu.roll(x, rows - 1, 0))


def below(x, upper):
    lane = lax.broadcasted_iota(jnp.int32, x.shape, 1)
    keep = (lane >= DECAY_RANK) if upper else (lane < DECAY_RANK)
    return jnp.where(keep, x, jnp.zeros_like(x))


def front_kernel(
    x_ref, vec_ref, wr_ref, wk_ref, wv_ref, down_ref, up_ref,
    m0_ref, m1_ref, m2_ref, m3_ref, m4_ref, m5_ref,
    q_ref, k_ref, v_ref, dl_ref, rl_ref, gate_ref, hid_ref,
    edge_ref,
):
    @pl.when(pl.program_id(0) == 0)
    def _():
        edge_ref[...] = jnp.zeros_like(edge_ref)

    unit, _ = row_norm(x_ref[...].astype(jnp.float32))
    normed = unit * vec_ref[12:13] + vec_ref[13:14]
    change = shifted(normed, edge_ref[:1], True) - normed
    edge_ref[:1] = normed[ROWS - 1 :]
    mixes = []
    for j, ref in enumerate((m0_ref, m1_ref, m2_ref, m3_ref, m4_ref, m5_ref)):
        mixes.append((normed + change * vec_ref[j : j + 1]).astype(jnp.bfloat16))
        ref[...] = mixes[j]
    q_ref[...] = dot32(mixes[0], wr_ref[...], NN)
    k_ref[...] = dot32(mixes[2], wk_ref[...], NN)
    v_ref[...] = dot32(mixes[3], wv_ref[...], NN)
    first = down_ref[:, :128]
    pre_decay, pre_rate = dot32(mixes[1], first, NN), dot32(mixes[4], first, NN)
    pre_gate = dot32(mixes[5], down_ref[:, 128:], NN)
    lane = lax.broadcasted_iota(jnp.int32, pre_decay.shape, 1)
    pair = jnp.where(lane < DECAY_RANK, jnp.tanh(pre_decay), pre_rate)
    gate = jax.nn.sigmoid(pre_gate)
    hid_ref[:, :128] = pair
    hid_ref[:, 128:] = gate
    narrow_pair = pair.astype(jnp.bfloat16)
    dl_ref[...] = dot32(below(narrow_pair, False), up_ref[:, :128], NT)
    rl_ref[...] = dot32(below(narrow_pair, True), up_ref[:, :128], NT)
    gate_ref[...] = dot32(gate.astype(jnp.bfloat16), up_ref[:, 128:], NT)


def front_forward(x, vectors, w_r, w_k, w_v, down, up):
    tokens, width = x.shape
    wide = pl.BlockSpec((ROWS, width), lambda i: (i, 0))
    own = pl.BlockSpec((ROWS, OWN), lambda i: (i, 0))
    hid = pl.BlockSpec((ROWS, 256), lambda i: (i, 0))
    whole = lambda a: pl.BlockSpec(a.shape, lambda i: (0, 0))
    shape = jax.ShapeDtypeStruct
    return pl.pallas_call(
        front_kernel,
        grid=(tokens // ROWS,),
        in_specs=[wide] + [whole(a) for a in (vectors, w_r, w_k, w_v, down, up)],
        out_specs=[wide] * 6 + [own] * 6 + [hid],
        out_shape=[shape((tokens, width), jnp.bfloat16)] * 6
        + [shape((tokens, OWN), jnp.float32)] * 6
        + [shape((tokens, 256), jnp.float32)],
        scratch_shapes=[pltpu.VMEM((8, width), jnp.float32)],
        compiler_params=pltpu.CompilerParams(vmem_limit_bytes=48 << 20),
        cost_estimate=SMALL,
        name="front_forward",
    )(x, vectors, w_r, w_k, w_v, down, up)


def front_back_kernel(
    x_ref, before_ref, vec_ref, wr_ref, wk_ref, wv_ref, down_ref, up_ref,
    m1_ref, m4_ref, m5_ref, hid_ref,
    dq_ref, dk_ref, dv_ref, ddl_ref, drl_ref, dgate_ref, own_vec_ref, ffn_vec_ref,
    dx_ref, mine_ref, other_ref,
    edge_ref, sums_ref, misc_ref,
):
    step = pl.num_programs(0) - 1 - pl.program_id(0)
    core = lax.axis_index("dp") % 2
    own_start = pl.multiple_of(core * OWN, OWN)

    @pl.when(pl.program_id(0) == 0)
    def _():
        edge_ref[...] = jnp.zeros_like(edge_ref)
        sums_ref[...] = jnp.zeros_like(sums_ref)
        misc_ref[...] = jnp.zeros_like(misc_ref)

    unit, scale = row_norm(x_ref[...].astype(jnp.float32))
    gain, offset = vec_ref[12:13], vec_ref[13:14]
    normed = unit * gain + offset
    tail, _ = row_norm(before_ref[...].astype(jnp.float32))
    edge = (tail[15:] * gain + offset) * jnp.where(step == 0, 0.0, 1.0)
    change = shifted(normed, edge, True) - normed
    ddl, drl, dgate = ddl_ref[...], drl_ref[...], dgate_ref[...]
    hid = hid_ref[...]
    pair, gate = hid[:, :128], hid[:, 128:]
    lane = lax.broadcasted_iota(jnp.int32, pair.shape, 1)
    first_up, last_up = up_ref[:, :128], up_ref[:, 128:]
    pair_grad = jnp.where(
        lane < DECAY_RANK,
        dot32(ddl, first_up, NN) * (1.0 - pair * pair),
        dot32(drl, first_up, NN),
    ).astype(jnp.bfloat16)
    gate_grad = (dot32(dgate, last_up, NN) * gate * (1.0 - gate)).astype(jnp.bfloat16)
    narrow_pair, narrow_gate = pair.astype(jnp.bfloat16), gate.astype(jnp.bfloat16)
    own_rows = pl.ds(own_start, OWN)
    misc_ref[own_rows, 256:384] += dot32(ddl, below(narrow_pair, False), TN) + dot32(
        drl, below(narrow_pair, True), TN
    )
    misc_ref[own_rows, 384:512] += dot32(dgate, narrow_gate, TN)
    decay_part, rate_part = below(pair_grad, False), below(pair_grad, True)
    misc_ref[:, :128] += dot32(m1_ref[...], decay_part, TN) + dot32(m4_ref[...], rate_part, TN)
    misc_ref[:, 128:256] += dot32(m5_ref[...], gate_grad, TN)
    first_down = down_ref[:, :128]
    grads = (
        lambda: dot32(dq_ref[...], wr_ref[...], NT),
        lambda: dot32(decay_part, first_down, NT),
        lambda: dot32(dk_ref[...], wk_ref[...], NT),
        lambda: dot32(dv_ref[...], wv_ref[...], NT),
        lambda: dot32(rate_part, first_down, NT),
        lambda: dot32(gate_grad, down_ref[:, 128:], NT),
    )
    total = jnp.zeros_like(change)
    moved = jnp.zeros_like(change)
    for j, grad in enumerate(grads):
        now = grad()
        total = total + now
        moved = moved + now * vec_ref[j : j + 1]
        sums_ref[j : j + 1] += jnp.sum(now * change, axis=0, keepdims=True)
    dnormed = total - moved + shifted(moved, edge_ref[:1], False)
    edge_ref[:1] = moved[:1]
    sums_ref[12:13] += jnp.sum(dnormed * unit, axis=0, keepdims=True)
    sums_ref[13:14] += jnp.sum(dnormed, axis=0, keepdims=True)
    dunit = dnormed * gain
    dx_ref[...] = scale * (
        dunit
        - jnp.mean(dunit, axis=-1, keepdims=True)
        - unit * jnp.mean(dunit * unit, axis=-1, keepdims=True)
    )

    @pl.when(step == 0)
    def _():
        sums_ref[6:7] = ffn_vec_ref[0:1] * 0.5
        sums_ref[14:16] = ffn_vec_ref[1:3] * 0.5
        zeros = jnp.zeros((1, OWN), jnp.float32)
        for target, source in ((7, 0), (8, 1), (9, 2), (10, 3), (11, 4), (16, 5), (17, 6)):
            mine = own_vec_ref[source : source + 1]
            sums_ref[target : target + 1] = jnp.concatenate(
                [jnp.where(core == 0, mine, zeros), jnp.where(core == 0, zeros, mine)], axis=1
            )
        for block in range(EMBED // 128):
            lanes = slice(block * 128, (block + 1) * 128)
            misc_ref[lanes, 512:640] = sums_ref[:, lanes].T
        share = mine_ref.shape[1]
        for chip in range(mine_ref.shape[0]):
            low = misc_ref[2 * chip * share : (2 * chip + 1) * share]
            high = misc_ref[(2 * chip + 1) * share : (2 * chip + 2) * share]
            mine_ref[chip] = jnp.where(core == 0, low, high)
            other_ref[chip] = jnp.where(core == 0, high, low).astype(jnp.bfloat16)


def front_backward(
    x, vectors, w_r, w_k, w_v, down, up, mixes, hid, grads, own_vec, ffn_vec
):
    tokens, width = x.shape
    devices = lax.axis_size("dp")
    pieces = (devices // 2, EMBED // devices, 640)
    steps = tokens // ROWS
    wide = pl.BlockSpec((ROWS, width), lambda i: (steps - 1 - i, 0))
    before = pl.BlockSpec(
        (16, width), lambda i: (jnp.maximum((steps - 1 - i) * (ROWS // 16) - 1, 0), 0)
    )
    own = pl.BlockSpec((ROWS, OWN), lambda i: (steps - 1 - i, 0))
    hid_spec = pl.BlockSpec((ROWS, 256), lambda i: (steps - 1 - i, 0))
    whole = lambda a: pl.BlockSpec(a.shape, lambda i: (0, 0))
    shape = jax.ShapeDtypeStruct
    return pl.pallas_call(
        front_back_kernel,
        grid=(steps,),
        in_specs=[wide, before]
        + [whole(a) for a in (vectors, w_r, w_k, w_v, down, up)]
        + [wide] * 3
        + [hid_spec]
        + [own] * 6
        + [whole(own_vec), whole(ffn_vec)],
        out_specs=[wide] + [pl.BlockSpec(pieces, lambda i: (0, 0, 0))] * 2,
        out_shape=[
            shape((tokens, width), jnp.float32),
            shape(pieces, jnp.float32),
            shape(pieces, jnp.bfloat16),
        ],
        scratch_shapes=[
            pltpu.VMEM((8, width), jnp.float32),
            pltpu.VMEM((128, width), jnp.float32),
            pltpu.VMEM((EMBED, 640), jnp.float32),
        ],
        compiler_params=pltpu.CompilerParams(vmem_limit_bytes=48 << 20),
        cost_estimate=SMALL,
        name="front_backward",
    )(x, x, vectors, w_r, w_k, w_v, down, up, *mixes, hid, *grads, own_vec, ffn_vec)


def ffn_back_kernel(
    len_ref, res_ref, before_ref, cot_ref, mine_ref, other_ref, vec_ref, wo_ref,
    grad_ref, narrow_ref, gated_ref, dvec_ref,
    edge_ref,
):
    step = pl.num_programs(0) - 1 - pl.program_id(0)

    @pl.when(pl.program_id(0) == 0)
    def _():
        edge_ref[...] = jnp.zeros_like(edge_ref)
        dvec_ref[...] = jnp.zeros_like(dvec_ref)

    gain, offset, coefficient = vec_ref[14:15], vec_ref[15:16], vec_ref[6:7]
    unit, scale = row_norm(res_ref[...])
    normed = unit * gain + offset
    tail, _ = row_norm(before_ref[...])
    edge = (tail[7:] * gain + offset) * jnp.where(step == 0, 0.0, 1.0)
    change = shifted(normed, edge, True) - normed
    grad = mine_ref[...].astype(jnp.float32) + other_ref[...].astype(jnp.float32)
    moved = grad * coefficient
    dnormed = grad - moved + shifted(moved, edge_ref[:1], False)
    edge_ref[:1] = moved[:1]
    sums = lambda x: jnp.sum(x, axis=0, keepdims=True)
    dvec_ref[0:1] += sums(grad * change)
    dvec_ref[1:2] += sums(dnormed * unit)
    dvec_ref[2:3] += sums(dnormed)
    dunit = dnormed * gain
    row = lax.broadcasted_iota(jnp.int32, grad.shape, 0) + step * ROWS
    out_grad = jnp.where(row < len_ref[0], cot_ref[...].astype(jnp.float32), 0.0)
    total = out_grad + scale * (
        dunit
        - jnp.mean(dunit, axis=-1, keepdims=True)
        - unit * jnp.mean(dunit * unit, axis=-1, keepdims=True)
    )
    grad_ref[...] = total
    small = total.astype(jnp.bfloat16)
    narrow_ref[...] = small
    gated_ref[...] = dot32(small, wo_ref[...], NT)


def ffn_backward(length, residual, cot, mine, other, vectors, w_o_rows):
    tokens, width = residual.shape
    steps = tokens // ROWS
    wide = pl.BlockSpec((ROWS, width), lambda i: (steps - 1 - i, 0))
    before = pl.BlockSpec(
        (8, width), lambda i: (jnp.maximum((steps - 1 - i) * (ROWS // 8) - 1, 0), 0)
    )
    own = pl.BlockSpec((ROWS, OWN), lambda i: (steps - 1 - i, 0))
    whole = lambda a: pl.BlockSpec(a.shape, lambda i: (0, 0))
    shape = jax.ShapeDtypeStruct
    return pl.pallas_call(
        ffn_back_kernel,
        grid=(steps,),
        in_specs=[pl.BlockSpec(memory_space=pltpu.SMEM), wide, before]
        + [wide] * 3
        + [whole(vectors), whole(w_o_rows)],
        out_specs=[wide, wide, own, pl.BlockSpec((8, width), lambda i: (0, 0))],
        out_shape=[
            shape((tokens, width), jnp.float32),
            shape((tokens, width), jnp.bfloat16),
            shape((tokens, OWN), jnp.float32),
            shape((8, width), jnp.float32),
        ],
        scratch_shapes=[pltpu.VMEM((8, width), jnp.float32)],
        compiler_params=pltpu.CompilerParams(vmem_limit_bytes=48 << 20),
        cost_estimate=SMALL,
        name="ffn_backward",
    )(length, residual, residual, cot, mine, other, vectors, w_o_rows)


def att_grad_kernel(m0_ref, m2_ref, m3_ref, dq_ref, dk_ref, dv_ref, send_a, keep_a, send_b, keep_b):
    chip = lax.axis_index("dp") // 2
    by_x, by_y = chip % 2 == 0, (chip // 2) % 2 == 0
    quarter = OWN // 2
    dv = dv_ref[...]
    first = ((m0_ref, dq_ref[...], 0, OWN), (m3_ref, dv[:, :quarter], OWN, quarter))
    second = ((m2_ref, dk_ref[...], 0, OWN), (m3_ref, dv[:, quarter:], OWN, quarter))
    for z in range(4):
        rows = slice(z * 256, (z + 1) * 256)
        for left, right, lane, width in first:
            block = dot32(left[:, rows], right, TN).astype(jnp.bfloat16)
            lanes = slice(lane, lane + width)
            for y in range(2):
                low, high = block[y * 128 : y * 128 + 64], block[y * 128 + 64 : y * 128 + 128]
                send_a[2 * z + y, :, lanes] = jnp.where(by_x, high, low)
                keep_a[2 * z + y, :, lanes] = jnp.where(by_x, low, high)
        for left, right, lane, width in second:
            block = dot32(left[:, rows], right, TN).astype(jnp.bfloat16)
            lanes = slice(lane, lane + width)
            for x in range(2):
                low, high = block[x * 64 : x * 64 + 64], block[128 + x * 64 : 128 + x * 64 + 64]
                send_b[2 * z + x, :, lanes] = jnp.where(by_y, high, low)
                keep_b[2 * z + x, :, lanes] = jnp.where(by_y, low, high)


def att_gradients(mixes, grads):
    space = pl.BlockSpec(memory_space=pltpu.VMEM)
    return pl.pallas_call(
        att_grad_kernel,
        in_specs=[space] * 6,
        out_specs=[space] * 4,
        out_shape=[jax.ShapeDtypeStruct((8, 64, OWN + OWN // 2), jnp.bfloat16)] * 4,
        compiler_params=pltpu.CompilerParams(vmem_limit_bytes=40 << 20),
        cost_estimate=SMALL,
        name="att_gradients",
    )(*mixes, *grads)


def swap(block, mask):
    size = lax.axis_size("dp")
    return lax.ppermute(block, "dp", [(i, i ^ mask) for i in range(size)])


def bit_of(mask):
    return (lax.axis_index("dp") // mask) % 2


def in_order(mask, own, other, axis):
    lower = bit_of(mask) == 0
    return jnp.where(
        lower, jnp.concatenate([own, other], axis=axis), jnp.concatenate([other, own], axis=axis)
    )


def chip_masks():
    size = lax.axis_size("dp")
    masks = []
    while 2 << len(masks) < size:
        masks.append(2 << len(masks))
    return masks


def steps_of(kind):
    masks = chip_masks()
    near, far = [[mask] for mask in masks[:2]], [[mask] for mask in masks[2:][::-1]]
    first = [[far[0][0], far[1][0], far[0][0] | far[1][0]]] if len(far) == 2 else far
    return [first + near[::-1], first + near, far + near[::-1], far + near, near + far][kind]


def meet(movers, *arrays):
    held = lax.optimization_barrier(tuple(tuple(m.arrived) for m in movers) + arrays)
    for mover, arrived in zip(movers, held):
        mover.arrived = list(arrived)
    return held[len(movers) :]


class Gather:
    def __init__(self, block, kind, places=(0,)):
        self.steps = steps_of(kind)
        self.held = block[None]
        self.places = [0]
        self.arrived = []
        self.masks = []

    def merge(self):
        if self.arrived:
            self.held = jnp.concatenate([self.held] + self.arrived, axis=0)
            self.places = self.places + [p ^ (m // 2) for m in self.masks for p in self.places]
            self.arrived = []

    def step(self):
        if self.steps:
            self.merge()
            self.masks = self.steps.pop(0)
            self.arrived = [swap(self.held, mask) for mask in self.masks]
        return self

    def run(self):
        while self.steps:
            self.step()
        return self

    def split(self, kinds):
        width = self.held.shape[-1] // len(kinds)
        out = []
        for i, kind in enumerate(kinds):
            part = Gather.__new__(Gather)
            cut = slice(i * width, (i + 1) * width)
            part.steps = steps_of(kind)[len(steps_of(kind)) - len(self.steps) :]
            part.held = self.held[..., cut]
            part.arrived = [x[..., cut] for x in self.arrived]
            part.places, part.masks = self.places, self.masks
            out.append(part)
        return out


def place_kernel(places, cuts, *refs):
    sources, outs = refs[: len(places)], refs[len(places) :]
    chip = lax.axis_index("dp") // 2
    for source, (part, list_of) in zip(sources, places):
        for j, place in enumerate(list_of):
            for out, (first, rows, lanes) in zip(outs, cuts):
                start = pl.multiple_of((chip ^ place) * rows, rows)
                lane, width = lanes[part]
                at = sum(w for _, w in lanes[:part])
                out[pl.ds(start, rows), at : at + width] = source[
                    j, first : first + rows, lane : lane + width
                ]


def assemble(gathers, cuts=None):
    gathers = [g.run() for g in gathers]
    rows = gathers[0].held.shape[1]
    cuts = cuts or ((0, rows, [(0, g.held.shape[2]) for g in gathers]),)
    sources, places = [], []
    for i, g in enumerate(gathers):
        sources += [g.held] + g.arrived
        shifts = [0] + [mask // 2 for mask in g.masks]
        places += [(i, [p ^ shift for p in g.places]) for shift in shifts]
    count = lax.axis_size("dp") // 2
    if any(cut[1] % 16 for cut in cuts):
        return assemble_plain(sources, places, cuts, count)
    space = pl.BlockSpec(memory_space=pltpu.VMEM)
    return pl.pallas_call(
        partial(place_kernel, places, cuts),
        in_specs=[space] * len(sources),
        out_specs=[space] * len(cuts),
        out_shape=[
            jax.ShapeDtypeStruct((count * n, sum(w for _, w in lanes)), sources[0].dtype)
            for _, n, lanes in cuts
        ],
        compiler_params=pltpu.CompilerParams(vmem_limit_bytes=32 << 20),
        cost_estimate=SMALL,
        name="assemble",
    )(*sources)


def assemble_plain(sources, places, cuts, count):
    chip = lax.axis_index("dp") // 2
    parts = []
    for part in sorted({part for part, _ in places}):
        blocks = jnp.concatenate([x for x, (at, _) in zip(sources, places) if at == part])
        where = [p for at, list_of in places if at == part for p in list_of]
        blocks = jnp.stack([blocks[where.index(i)] for i in range(count)])
        parts.append(jnp.take(blocks, chip ^ lax.iota(jnp.int32, count), axis=0))
    return [
        jnp.concatenate(
            [x[:, first : first + n, at : at + w] for x, (at, w) in zip(parts, lanes)], axis=-1
        ).reshape(count * n, -1)
        for first, n, lanes in cuts
    ]


class Scatter:
    def __init__(self, parts, kind):
        self.steps = steps_of(kind)[::-1]
        self.axes = chip_masks()[::-1]
        self.sources = [parts.reshape((2,) * len(self.axes) + parts.shape[1:])]
        self.arrived = []
        self.sent = None

    @classmethod
    def begun(cls, sent, kept, kind):
        out = cls.__new__(cls)
        out.steps = steps_of(kind)[::-1]
        out.axes = [axis for axis in chip_masks()[::-1] if axis != out.steps[0][0]]
        out.sources = [kept.reshape((2,) * len(out.axes) + kept.shape[1:])]
        out.arrived = []
        out.sent = [sent.reshape(out.sources[0].shape)]
        return out

    def pick(self, sources, mask, gone):
        out = []
        for x in sources:
            for place in reversed(range(len(self.axes))):
                axis = self.axes[place]
                if axis in gone:
                    which = bit_of(axis) if not mask & axis else 1 - bit_of(axis)
                    x = lax.dynamic_index_in_dim(x, which, place, keepdims=False)
            out.append(x)
        return out

    def prepare(self):
        if self.sent is not None:
            return self
        masks = self.steps[0]
        sources = self.sources + self.arrived
        gone = [axis for axis in self.axes if any(mask & axis for mask in masks)]
        self.sent = [
            sum(x.astype(jnp.float32) for x in self.pick(sources, mask, gone)).astype(jnp.bfloat16)
            for mask in masks
        ]
        self.sources = self.pick(sources, 0, gone)
        self.axes = [axis for axis in self.axes if axis not in gone]
        self.arrived = []
        return self

    def step(self):
        return together([self])[0]

    def run(self):
        while self.steps:
            self.step()
        return self

    def total(self):
        return sum(x.astype(jnp.float32) for x in self.sources + self.arrived)


def together(parts):
    if not parts[0].steps:
        return parts
    for part in parts:
        part.prepare()
    for i, mask in enumerate(parts[0].steps[0]):
        sent = [part.sent[i] for part in parts]
        got = swap(sent[0] if len(sent) == 1 else jnp.concatenate(sent, axis=-1), mask)
        at = 0
        for part, x in zip(parts, sent):
            part.arrived.append(got[..., at : at + x.shape[-1]])
            at += x.shape[-1]
    for part in parts:
        part.steps.pop(0)
        part.sent = None
    return parts


def norm_rows(features, gain_row, offset_row):
    average = jnp.mean(features, axis=-1, keepdims=True)
    centred = features - average
    variance = jnp.mean(centred * centred, axis=-1, keepdims=True)
    return centred * lax.rsqrt(variance + 1e-05) * gain_row + offset_row


def product(operand, weight_matrix):
    return jnp.dot(operand, weight_matrix, preferred_element_type=jnp.float32)


def input_gradient_rows(upstream_gradient, weight_matrix):
    return lax.dot_general(
        upstream_gradient,
        weight_matrix,
        (((1,), (1,)), ((), ())),
        preferred_element_type=jnp.float32,
    )


def weight_gradient(operand, upstream_gradient):
    return lax.dot_general(
        operand, upstream_gradient, (((0,), (0,)), ((), ())), preferred_element_type=jnp.float32
    )


def earlier(rows):
    return jnp.concatenate([jnp.zeros_like(rows[:1]), rows[:-1]], axis=0)


def ffn_mix(residual, vectors):
    second = norm_rows(residual, vectors[14], vectors[15])
    return second + (earlier(second) - second) * vectors[6]


def narrow(x):
    return x.astype(jnp.bfloat16)


def local(
    inputs,
    lengths,
    attention_projections,
    channel_key_weight,
    channel_value_weight,
    lowrank_down_weight,
    lowrank_up_weight,
    per_feature_parameters,
    cotangent,
):
    devices = lax.axis_size("dp")
    chips = devices // 2
    device = lax.axis_index("dp")
    chip, core = device // 2, device % 2
    row_count = inputs.shape[0]
    slots = 2 * row_count
    share = EMBED // devices
    pair_share = 2 * share
    units = channel_value_weight.shape[0]
    half_units = chips * units

    def own_cut(x, which):
        return lax.dynamic_slice_in_dim(x, which * OWN, OWN, x.ndim - 1)

    def own_rows(x, which):
        return lax.dynamic_slice_in_dim(x, which * row_count, row_count, 0)

    pair_rows = in_order(
        1,
        own_cut(attention_projections, core),
        swap(own_cut(attention_projections, 1 - core), 1),
        1,
    )
    lora = jnp.concatenate([lowrank_down_weight, lowrank_up_weight.T], axis=1)
    vector_rows = jnp.pad(per_feature_parameters.T, ((0, 0), (0, 128 - 18)))
    vector_rows = vector_rows.reshape(share // 4, OWN)
    first_rows = 3 * pair_share
    misc_rows = share + share // 4 + (share // 4) % 16
    block = jnp.concatenate(
        [
            pair_rows[:3].reshape(first_rows, OWN),
            lora,
            jnp.pad(vector_rows, ((0, (share // 4) % 16), (0, 0))),
        ],
        axis=0,
    )
    half = half_units // 2
    quarter = OWN // 2
    first = Gather(block, 0).step()
    w_o_part = Gather(pair_rows[3], 4).step().step()
    key_in, raw, cot, _ = meet([], channel_key_weight, inputs, cotangent, first.held)
    key_cut = key_in.reshape(share, chips, 2, units)

    def key_columns(which):
        return lax.dynamic_index_in_dim(key_cut, which, 2, keepdims=False).reshape(share, half_units)

    key_rows = in_order(1, key_columns(core), swap(key_columns(1 - core), 1), 0)
    tokens = in_order(1, raw, swap(raw, 1), 0)
    cot = in_order(1, cot, swap(cot, 1), 0)
    key_rows, tokens, cot = meet([first, w_o_part], key_rows, tokens, cot)
    first = first.split((0, 1))
    for part in first:
        part.step()
    key_part = Gather(key_rows, 2).step()
    (tokens,) = meet(first, tokens)
    for part in first:
        part.step()
    value_block, *_ = meet([key_part], channel_value_weight, *[part.held for part in first])
    key_part.step()
    value_part = Gather(value_block, 2).step()
    (tokens,) = meet(first + [key_part, value_part, w_o_part], tokens)
    key_parts = key_part.split((2, 3))
    for part in key_parts:
        part.step()
    w_r, w_k, w_v, misc = assemble(
        first,
        [(i * pair_share, pair_share, [(0, quarter)] * 2) for i in range(3)]
        + [(first_rows, misc_rows, [(0, quarter)] * 2)],
    )
    misc = misc.reshape(chips, 1, misc_rows, OWN)
    misc = in_order(1, misc, swap(misc, 1), 1)
    value_part.step()
    w_o_part.step()
    lora = misc[:, :, :share].reshape(EMBED, OWN)
    down, up_t = lora[:, :256], lax.dynamic_slice_in_dim(lora[:, 256:], core * OWN, OWN, 0)
    vectors = misc[:, :, share : share + share // 4].reshape(EMBED, 128)[:, :18].T
    vectors = vectors.astype(jnp.float32)
    own_vectors = own_cut(vectors, core)
    used = jnp.concatenate([own_vectors[7:12], own_vectors[16:18], own_vectors[:1]], axis=0)
    length = lax.dynamic_index_in_dim(lengths, chip, 0)
    live = (lax.iota(jnp.int32, slots) < length)[:, None]

    *mixes, queries, keys, values, decay_low, rate_low, gate_rows, hid = front_forward(
        tokens, vectors, w_r, w_k, w_v, down, up_t
    )
    terms = meet(
        key_parts + [value_part, w_o_part],
        queries, keys, values, decay_low, rate_low, gate_rows,
    )
    value_parts = value_part.split((2, 3))
    for part in key_parts + value_parts:
        part.step()
    w_o_part.step()
    blocks = slots // (CHUNK * STEP_CHUNKS)
    early = blocks // 2
    zero_state = jnp.zeros((2, CHUNK, LANES), jnp.float32)
    *before, state = wkv_forward(0, early, length, used, zero_state, terms)
    (state,) = meet(value_parts, state)
    for part in value_parts:
        part.step()
    state, *_ = meet([], state, *[part.held for part in value_parts])
    gated, *saved, _ = wkv_forward(early, blocks - early, length, used, state, terms, before)
    gated, cot, tokens = meet(key_parts + [w_o_part], gated, cot, tokens)
    gated_all = in_order(1, gated, swap(gated, 1), 1)
    (w_o_own,) = assemble([w_o_part])
    w_o = in_order(1, w_o_own, swap(w_o_own, 1), 1)
    (key_weight,) = assemble(key_parts)
    residual = tokens.astype(jnp.float32) + product(gated_all, w_o)
    ffn_in = narrow(ffn_mix(residual, vectors))
    positive = jax.nn.relu(product(ffn_in, key_weight))
    hidden = narrow(jnp.square(positive))
    out_narrow = jnp.where(live, cot, jnp.zeros_like(cot))
    value_cuts = ((0, quarter), (quarter, OWN), (OWN, EMBED))
    value_grads = [
        narrow(weight_gradient(hidden, out_narrow[:, lo:hi])).reshape(chips, units, hi - lo)
        for lo, hi in value_cuts
    ]
    w_o_rows = lax.dynamic_slice_in_dim(w_o, core * OWN, OWN, 0)
    hidden, positive, out_narrow, w_o_rows, *value_grads = meet(
        value_parts, hidden, positive, out_narrow, w_o_rows, *value_grads
    )
    (value_weight,) = assemble(value_parts)

    value_scatter = [Scatter(x, kind).step() for kind, x in zip((2, 3, 4), value_grads)]
    late_scatter = value_scatter.pop()
    pre_narrow = narrow(2.0 * positive * input_gradient_rows(out_narrow, value_weight))
    ffn_in_grad = narrow(input_gradient_rows(pre_narrow, key_weight))
    other_grad = swap(ffn_in_grad, 1)
    grad_key = narrow(weight_gradient(ffn_in, pre_narrow)).reshape(chips, pair_share, half_units)
    residual_grad, attended_grad, gated_grad, ffn_vec = ffn_backward(
        length, residual, cot, ffn_in_grad, other_grad, vectors, w_o_rows
    )
    grad_o = narrow(weight_gradient(gated_all, own_cut(attended_grad, core)))
    grad_o = grad_o.reshape(chips, pair_share, OWN)
    key_scatter = [Scatter(grad_key[:, :, i * half : (i + 1) * half], 2 + i) for i in range(2)]
    o_scatter = [Scatter(grad_o[:, :, i * quarter : (i + 1) * quarter], 2 + i) for i in range(2)]
    key_pairs = list(zip(key_scatter, o_scatter))
    for part in key_scatter + o_scatter:
        part.prepare()
    gated_grad, *sent = meet(
        value_scatter, gated_grad, *[m.sent[0] for m in key_scatter + o_scatter]
    )
    for part, x in zip(key_scatter + o_scatter, sent):
        part.sent = [x]
    for pair in key_pairs:
        together(pair)
    for part in value_scatter:
        part.step()
    terms = [*terms, gated_grad, *saved]
    zero_sums = jnp.zeros((8, OWN), jnp.float32)
    *before, sums, state = wkv_backward(
        early, blocks - early, length, used, zero_state, zero_sums, terms
    )
    state, sums = meet(value_scatter + [late_scatter], state, sums)
    together(value_scatter)
    late_scatter.step()
    *low_grads, own_vec, _ = wkv_backward(0, early, length, used, state, sums, terms, before)
    key_all = key_scatter + o_scatter
    *low_grads, own_vec = meet(key_all + value_scatter + [late_scatter], *low_grads, own_vec)
    if pair_share == 64:
        sent_a, kept_a, sent_b, kept_b = att_gradients(
            (mixes[0], mixes[2], mixes[3]), low_grads[:3]
        )
        att_scatter = [Scatter.begun(sent_a, kept_a, 2), Scatter.begun(sent_b, kept_b, 3)]
    else:
        grads = [narrow(weight_gradient(mixes[m], g)) for m, g in zip((0, 2, 3), low_grads)]
        att_scatter = [
            Scatter(jnp.concatenate(x, axis=1).reshape(chips, pair_share, 3 * quarter), 2 + i).prepare()
            for i, x in enumerate(
                ((grads[0], grads[2][:, :quarter]), (grads[1], grads[2][:, quarter:]))
            )
        ]
    own_vec, *sent = meet([], own_vec, *[m.sent[0] for m in att_scatter])
    for part, x in zip(att_scatter, sent):
        part.sent = [x]
        part.step()
    for pair in key_pairs:
        together(pair)
    together(value_scatter)
    token_part, misc_mine, misc_other = front_backward(
        tokens, vectors, w_r, w_k, w_v, down, up_t, (mixes[1], mixes[4], mixes[5]), hid,
        low_grads, own_vec, ffn_vec,
    )
    token_part, misc_mine, misc_other, hidden = meet(
        key_all + value_scatter, token_part, misc_mine, misc_other, hidden
    )
    misc_sum = misc_mine + swap(misc_other, 1).astype(jnp.float32)
    misc_sum = jnp.concatenate([misc_sum[..., :320], misc_sum[..., 320:]], axis=1)
    misc_scatter = Scatter(misc_sum, 3)
    masks = chip_masks()
    misc_scatter.steps = [[masks[0], masks[1], masks[0] | masks[1]]] + misc_scatter.steps[2:]
    together(key_all)
    misc_scatter.step()
    (token_part,) = meet(att_scatter, token_part)
    for part in att_scatter:
        part.step()
    (token_part,) = meet(key_all, token_part)
    together(key_all)
    late_scatter.step()
    ffn_part = product(hidden, value_weight)
    token_part, ffn_part = meet(
        att_scatter + [misc_scatter, late_scatter], token_part, ffn_part
    )
    last_parts = att_scatter + [misc_scatter]
    if len(misc_scatter.steps) == 2:
        for part in last_parts:
            part.steps = [[masks[2], masks[3], masks[2] | masks[3]]]
    together(last_parts)
    late_scatter.step()
    input_gradient = (
        own_rows(residual_grad, core)
        + own_rows(token_part, core)
        + swap(own_rows(token_part, 1 - core), 1)
    )
    ffn_out = own_rows(ffn_part, core) + swap(own_rows(ffn_part, 1 - core), 1)
    output = narrow(jnp.where(own_rows(live, core), own_rows(residual, core) + ffn_out, 0.0))
    value_sum = jnp.concatenate(
        [x.run().total() for x in value_scatter + [late_scatter]], axis=1
    )
    while key_scatter[0].steps:
        together(key_all)
    key_sum = jnp.concatenate([x.total() for x in key_all], axis=1).reshape(2, share, -1)

    def exchange(x):
        mine = lax.dynamic_index_in_dim(x, core, 0, keepdims=False)
        return mine, swap(lax.dynamic_index_in_dim(x, 1 - core, 0, keepdims=False), 1)

    key_mine, key_theirs = exchange(key_sum)
    input_gradient, value_sum, key_mine, key_theirs = meet(
        last_parts, input_gradient, value_sum, key_mine, key_theirs
    )
    while last_parts[0].steps:
        together(last_parts)
    first_sum, second_sum, misc_sum = [x.total() for x in last_parts]
    misc_sum = jnp.concatenate([misc_sum[:share], misc_sum[share:]], axis=1)
    att_sum = jnp.concatenate(
        [first_sum[:, :OWN], second_sum[:, :OWN], first_sum[:, OWN:], second_sum[:, OWN:]], axis=1
    )
    mine, theirs = exchange(att_sum.reshape(2, share, -1))
    mine = jnp.concatenate([mine, key_mine[:, half_units:]], axis=1)
    theirs = jnp.concatenate([theirs, key_theirs[:, half_units:]], axis=1)
    shard_mixer = jnp.stack(
        [
            in_order(1, mine[:, i * OWN : (i + 1) * OWN], theirs[:, i * OWN : (i + 1) * OWN], 1)
            for i in range(4)
        ]
    )
    shard_key = in_order(
        1,
        key_mine[:, :half_units].reshape(share, chips, 1, units),
        key_theirs[:, :half_units].reshape(share, chips, 1, units),
        2,
    ).reshape(share, 2 * half_units)
    return (
        output,
        input_gradient,
        shard_mixer,
        shard_key,
        value_sum,
        misc_sum[:, :256],
        misc_sum[:, 256:512].T,
        misc_sum[:, 512:530].T,
    )


def solution(mesh):
    in_specs = (
        P("dp", None),
        P(),
        P(None, "dp", None),
        P("dp", None),
        P("dp", None),
        P("dp", None),
        P(None, "dp"),
        P(None, "dp"),
        P("dp", None),
    )
    out_specs = (
        P("dp", None),
        P("dp", None),
        P(None, "dp", None),
        P("dp", None),
        P("dp", None),
        P("dp", None),
        P(None, "dp"),
        P(None, "dp"),
    )
    return jax.shard_map(local, mesh=mesh, in_specs=in_specs, out_specs=out_specs, check_vma=False)
```

```python
from functools import partial

import jax
import jax.numpy as jnp
from jax import lax
from jax.experimental import pallas as pl
from jax.experimental.pallas import tpu as pltpu
from jax.sharding import PartitionSpec as P

HEADS = 16
HEAD_SIZE = 64
DECAY_RANK = 64
RATE_RANK = 64
EMBED = 1024
OWN = EMBED // 2
PRECISE = lax.Precision.HIGHEST


CHUNK = 64
LANES = 256
GROUP_HEADS = 4
STEP_CHUNKS = 2
SMALL = pl.CostEstimate(flops=1, bytes_accessed=1, transcendentals=0)

NN = (((1,), (0,)), ((), ()))
NT = (((1,), (1,)), ((), ()))
TN = (((0,), (0,)), ((), ()))


def halves(x):
    high = x.astype(jnp.bfloat16)
    return high, (x - high.astype(jnp.float32)).astype(jnp.bfloat16)


def dot32(a, b, dims):
    return lax.dot_general(a, b, dims, preferred_element_type=jnp.float32)


def mul(left, right, dims=NN):
    rows = left[0].shape[0]
    both = dot32(jnp.concatenate(left, axis=0), right[0], dims)
    return both[:rows] + both[rows:] + dot32(left[0], right[1], dims)


def tmul(left, right, masks):
    full = (
        dot32(left[0], right[0], TN) + dot32(left[1], right[0], TN) + dot32(left[0], right[1], TN)
    )
    return sum(full[h * CHUNK : (h + 1) * CHUNK] * masks[h][:1].astype(jnp.float32) for h in range(GROUP_HEADS))


def spread(pair, masks):
    return tuple(
        jnp.concatenate([part * masks[h] for h in range(GROUP_HEADS)], axis=0) for part in pair
    )


def stack(first, second):
    return tuple(jnp.concatenate([x, y], axis=0) for x, y in zip(first, second))


def head_masks():
    lane = lax.broadcasted_iota(jnp.int32, (CHUNK, LANES), 1) // CHUNK
    return [(lane == h).astype(jnp.float32).astype(jnp.bfloat16) for h in range(GROUP_HEADS)]


def places():
    row = lax.broadcasted_iota(jnp.int32, (CHUNK, LANES), 0)
    col = lax.broadcasted_iota(jnp.int32, (CHUNK, LANES), 1) % CHUNK
    return row, col


def running_sum(x, upper=False):
    row = lax.broadcasted_iota(jnp.int32, (CHUNK, CHUNK), 0)
    col = lax.broadcasted_iota(jnp.int32, (CHUNK, CHUNK), 1)
    ones = (row <= col if upper else col <= row).astype(jnp.float32).astype(jnp.bfloat16)
    high, rest = halves(x)
    low = (x - high.astype(jnp.float32) - rest.astype(jnp.float32)).astype(jnp.bfloat16)
    return dot32(ones, high, NN) + dot32(ones, rest, NN) + dot32(ones, low, NN)


def scaled_forms(q, w, k, a, b):
    total = running_sum(w)
    before = total - w
    middle = total[CHUNK // 2 - 1 : CHUNK // 2]
    end = total[CHUNK - 1 :]
    ea = jnp.exp(before - middle)
    eq = jnp.exp(total - middle)
    eb = jnp.exp(middle - total)
    ee = jnp.exp(end - total)
    return (a * ea, q * eq, b * eb, k * eb, b * ee, k * ee), (ea, eq, eb, ee), (jnp.exp(middle), jnp.exp(end))


def each(fn, *columns):
    return [fn(*row) for row in zip(*columns)]


def block_ones():
    row = lax.broadcasted_iota(jnp.int32, (LANES, LANES), 0) // CHUNK
    col = lax.broadcasted_iota(jnp.int32, (LANES, LANES), 1) // CHUNK
    return (row == col).astype(jnp.float32).astype(jnp.bfloat16)


def head_sum(x, ones):
    rows = x.shape[0]
    both = dot32(jnp.concatenate(halves(x), axis=0), ones, NN)
    return both[:rows] + both[rows:]


def prepared(keys, decay_low, rate_low, live, vec, ones):
    sig = jax.nn.sigmoid(vec[0] + decay_low)
    log_decay = (-0.6065306597126334) * sig * live
    rates = jax.nn.sigmoid(vec[1] + rate_low)
    scaled = keys * vec[2]
    inverse = lax.rsqrt(head_sum(scaled * scaled, ones) + 1e-06)
    unit_keys = scaled * inverse
    factor = (1.0 + (rates - 1.0) * vec[3]) * live
    return log_decay, keys * factor, -unit_keys, unit_keys * rates * live, sig, rates, inverse, factor


def read_out(o, q, k, v, vec, ones):
    centred = o - head_sum(o, ones) * (1.0 / CHUNK)
    scale = lax.rsqrt(head_sum(centred * centred, ones) * (1.0 / CHUNK) + 0.00064)
    normed = centred * scale
    weight = head_sum(q * k * vec[4], ones)
    return normed, scale, weight, normed * vec[5] + vec[6] + weight * v


def unit_slices():
    return [
        (slice(c * CHUNK, (c + 1) * CHUNK), slice(g * LANES, (g + 1) * LANES))
        for c in range(STEP_CHUNKS)
        for g in range(2)
    ]


def unit_live(length, step):
    row = lax.broadcasted_iota(jnp.int32, (CHUNK, LANES), 0)
    start = step * (STEP_CHUNKS * CHUNK)
    live = [(row + (start + c * CHUNK) < length).astype(jnp.float32) for c in range(STEP_CHUNKS)]
    return [live[c] for c in range(STEP_CHUNKS) for g in range(2)]


def unit_vectors(vec_ref):
    vec = [[vec_ref[i : i + 1, g * LANES : (g + 1) * LANES] for i in range(7)] for g in range(2)]
    return [vec[g] for c in range(STEP_CHUNKS) for g in range(2)]


def forward_kernel(base, *refs):
    len_ref, vec_ref, start_ref, q_ref, keys_ref, v_ref, dl_ref, rl_ref, gate_ref = refs[:9]
    (
        out_ref, o_ref, t_ref, aqb_ref, aak_ref, aqk_ref, y_ref, z_ref, trt_ref, qe_ref, state_ref,
    ) = refs[-11:]

    @pl.when(pl.program_id(0) == 0)
    def _():
        state_ref[...] = start_ref[...]

    masks = head_masks()
    row, col = places()
    strict = (col < row).astype(jnp.float32)
    within = (col <= row).astype(jnp.float32)
    eye = (col == row).astype(jnp.float32)
    ones = block_ones()
    units = unit_slices()
    live = unit_live(len_ref[0], pl.program_id(0) + base)
    vec = unit_vectors(vec_ref)
    load = lambda ref: [ref[u] for u in units]
    q, keys, v = load(q_ref), load(keys_ref), load(v_ref)
    ready = each(
        lambda x, y, z, m, n: prepared(x, y, z, m, n, ones), keys, load(dl_ref), load(rl_ref), live, vec
    )
    w, k, a, b = ([x[i] for x in ready] for i in range(4))
    forms = each(scaled_forms, q, w, k, a, b)
    ah, qh, bh, kh, bt, kt = ([f[0][i] for f in forms] for i in range(6))
    emid = [f[2][0] for f in forms]
    eend = [f[2][1] for f in forms]
    aq = each(lambda x, y: halves(jnp.concatenate([x, y], axis=0)), ah, qh)
    with_b = each(lambda l, r: mul(l, spread(halves(r), masks), NT), aq, bh)
    with_k = each(lambda l, r: mul(l, spread(halves(r), masks), NT), aq, kh)
    aab = [x[:CHUNK] * strict for x in with_b]
    aqb = [halves(x[CHUNK:] * within) for x in with_b]
    aak = [halves(x[:CHUNK] * strict) for x in with_k]
    aqk = [halves(x[CHUNK:] * within) for x in with_k]
    p = [halves(x * (row // 8 == col // 8)) for x in aab]
    t = [eye + x * (row // 8 == col // 8) for x in aab]
    p2 = each(lambda x: halves(mul(x, spread(x, masks))), p)
    both = each(lambda x, y: mul(stack(x, halves(y)), spread(x, masks)), p2, t)
    p4 = [halves(x[:CHUNK]) for x in both]
    t = each(lambda x, y: x + y[CHUNK:], t, both)
    t = each(lambda x, y: x + mul(halves(x), spread(y, masks)), t, p4)
    for size in (8, 16, 32):
        corner = ((row // size) % 2 == 1) & (col // size == row // size - 1)
        ts = [halves(x) for x in t]
        n = [halves(x * corner) for x in aab]
        tn = each(lambda x, y: halves(mul(x, spread(y, masks))), ts, n)
        t = each(lambda x, y, z: x + mul(y, spread(z, masks)), t, tn, ts)
    ts = [halves(x) for x in t]
    vs = [halves(x) for x in v]
    vm = [spread(x, masks) for x in vs]
    wide = each(lambda x, y, e: mul(x, spread(halves(y * e), masks)), ts, ah, emid)
    r0 = each(mul, aak, vm)
    y0 = each(lambda x, y: mul(x, spread(halves(y), masks)), ts, r0)
    wides = [halves(x) for x in wide]
    qe = each(lambda x, e, y, z: x * e + mul(y, spread(z, masks)), qh, emid, aqb, wides)
    y0s = [halves(x) for x in y0]
    part = each(lambda x, y, z, u: mul(x, spread(y, masks)) + mul(z, u), aqb, y0s, aqk, vm)
    bts = [halves(x) for x in bt]
    diag = [eye * e for e in eend]
    tr = each(lambda x, y, d: tmul(x, y, masks) + d, bts, wides, diag)
    trt = each(lambda x, y, d: tmul(y, x, masks) + d, bts, wides, diag)
    inject = each(lambda x, y, z, u: tmul(stack(x, halves(y)), stack(z, u), masks), bts, kt, y0s, vs)
    wq = each(lambda x, y: stack(x, halves(y)), wides, qe)
    z = []
    out = []
    for c in range(STEP_CHUNKS):
        for g in range(2):
            i = c * 2 + g
            now = state_ref[g]
            nows = spread(halves(now), masks)
            state_ref[g] = mul(halves(tr[i]), nows) + inject[i]
            z.append(now)
            out.append(mul(wq[i], nows))
    o = each(lambda x, y: x[CHUNK:] + y, out, part)
    mixed = each(lambda x, y, z, m, n: read_out(x, y, z, m, n, ones)[3], o, q, k, v, vec)
    for i, u in enumerate(units):
        out_ref[u] = (mixed[i] * gate_ref[u]).astype(jnp.bfloat16)
        o_ref[u] = o[i]
        y_ref[u] = out[i][:CHUNK] + y0[i]
        t_ref[u] = t[i]
        aqb_ref[u] = with_b[i][CHUNK:] * within
        aak_ref[u] = with_k[i][:CHUNK] * strict
        aqk_ref[u] = with_k[i][CHUNK:] * within
        z_ref[u] = z[i]
        trt_ref[u] = trt[i]
        qe_ref[u] = qe[i]


def backward_kernel(base, *refs):
    (
        len_ref, vec_ref, start_ref, sums_ref, q_ref, keys_ref, v_ref, dl_ref, rl_ref, gate_ref,
        g_ref, o_ref, t_ref, aqb_ref, aak_ref, aqk_ref, y_ref, z_ref, trt_ref, qe_ref,
    ) = refs[:20]
    dq_ref, dkeys_ref, dv_ref, ddl_ref, drl_ref, dgate_ref, dvec_ref, state_ref = refs[-8:]
    step = base + pl.num_programs(0) - 1 - pl.program_id(0)

    @pl.when(pl.program_id(0) == 0)
    def _():
        state_ref[...] = start_ref[...]
        dvec_ref[...] = sums_ref[...]

    masks = head_masks()
    row, col = places()
    strict = (col < row).astype(jnp.float32)
    within = (col <= row).astype(jnp.float32)
    ones = block_ones()
    units = unit_slices()
    live = unit_live(len_ref[0], step)
    vec = unit_vectors(vec_ref)
    load = lambda ref: [ref[u] for u in units]
    q, keys, v, g = load(q_ref), load(keys_ref), load(v_ref), load(g_ref)
    ready = each(
        lambda x, y, z, m, n: prepared(x, y, z, m, n, ones), keys, load(dl_ref), load(rl_ref), live, vec
    )
    w, k, a, b, sig, rates, inverse, factor = ([x[i] for x in ready] for i in range(8))
    seen = each(lambda x, y, z, m, n: read_out(x, y, z, m, n, ones), load(o_ref), q, k, v, vec)
    normed, scale, weight, mixed = ([x[i] for x in seen] for i in range(4))
    gate = load(gate_ref)
    dgate = each(lambda x, y: x * y, g, mixed)
    dmix = each(lambda x, y: x * y, g, gate)
    dn = each(lambda x, n: x * n[5], dmix, vec)
    do = each(
        lambda x, n, r: r
        * (x - head_sum(x, ones) * (1.0 / CHUNK) - n * (head_sum(x * n, ones) * (1.0 / CHUNK))),
        dn, normed, scale,
    )
    dweight = each(lambda x, y: head_sum(x * y, ones), dmix, v)
    do = [halves(x) for x in do]
    qe, trt, t, aqb, aak, aqk, ys = (
        [halves(x) for x in load(ref)]
        for ref in (qe_ref, trt_ref, t_ref, aqb_ref, aak_ref, aqk_ref, y_ref)
    )
    z = load(z_ref)
    vs = [halves(x) for x in v]
    h = each(lambda x, y: tmul(x, y, masks), qe, do)
    dz = [None] * len(units)
    for c in reversed(range(STEP_CHUNKS)):
        for g in range(2):
            i = c * 2 + g
            now = state_ref[g]
            dz[i] = now
            state_ref[g] = mul(trt[i], spread(halves(now), masks)) + h[i]
    dzs = [spread(halves(x), masks) for x in dz]
    zs = [spread(halves(x), masks) for x in z]
    forms = each(scaled_forms, q, w, k, a, b)
    ah, qh, bh, kh, bt, kt = ([f[0][i] for f in forms] for i in range(6))
    ea, eq, eb, ee = ([f[1][i] for f in forms] for i in range(4))
    emid = [f[2][0] for f in forms]
    eend = [f[2][1] for f in forms]
    from_end = each(lambda x, y, s: mul(halves(jnp.concatenate([x, y], axis=0)), s), bt, kt, dzs)
    dy = each(lambda x, y, s: halves(tmul(x, y, masks) + s[:CHUNK]), aqb, do, from_end)
    dr = each(lambda x, y: halves(tmul(x, y, masks)), t, dy)
    ro = each(stack, dr, do)
    dv = each(lambda x, y, s, f: tmul(stack(x, y), s, masks) + f[CHUNK:], aak, aqk, ro, from_end)
    mask2 = jnp.concatenate([strict, within], axis=0)
    dab = each(lambda s, y: halves(mul(s, spread(y, masks), NT) * mask2), ro, ys)
    dak = each(lambda s, y: halves(mul(s, spread(y, masks), NT) * mask2), ro, vs)
    dst = each(lambda s, y: mul(s, y, NT), ro, zs)
    daq = each(
        lambda s, e, x, bb, y, kk: s * e + mul(x, spread(halves(bb), masks)) + mul(y, spread(halves(kk), masks)),
        dst, emid, dab, bh, dak, kh,
    )
    aq = each(lambda x, y: halves(jnp.concatenate([x, y], axis=0)), ah, qh)
    dbh = each(lambda x, y: tmul(x, y, masks), dab, aq)
    dkh = each(lambda x, y: tmul(x, y, masks), dak, aq)
    dend = each(lambda y, x, s: mul(stack(y, x), s, NT), ys, vs, dzs)
    row_of_ones = jnp.ones((8, LANES), jnp.bfloat16)
    sums = lambda x: jnp.sum(x, axis=0, keepdims=True)
    for i, u in enumerate(units):
        da = daq[i][:CHUNK] * ea[i]
        dq = daq[i][CHUNK:] * eq[i]
        dbt = dend[i][:CHUNK] * ee[i]
        dkt = dend[i][CHUNK:] * ee[i]
        db = dbh[i] * eb[i] + dbt
        dk = dkh[i] * eb[i] + dkt
        pa = da * a[i]
        diff = dq * q[i] - db * b[i] - dk * k[i] + pa
        zz = spread(halves(z[i] * dz[i]), masks)
        carry = (dot32(row_of_ones, zz[0], NT) + dot32(row_of_ones, zz[1], NT))[:1] * eend[i]
        carry = carry + sums(dbt * b[i] + dkt * k[i])
        dw = running_sum(diff, upper=True) - pa + carry
        from_bonus = dweight[i] * vec[i][4]
        dk = dk + from_bonus * q[i]
        dq_ref[u] = (dq + from_bonus * k[i]).astype(jnp.bfloat16)
        dv_ref[u] = (dv[i] + weight[i] * dmix[i]).astype(jnp.bfloat16)
        dgate_ref[u] = dgate[i].astype(jnp.bfloat16)
        unit_keys = -a[i]
        db = db * live[i]
        du = db * rates[i] - da
        dscaled = inverse[i] * (du - unit_keys * head_sum(du * unit_keys, ones))
        dkl = dk * keys[i] * live[i]
        drl = (db * unit_keys + dkl * vec[i][3]) * rates[i] * (1.0 - rates[i])
        ddl = dw * w[i] * (1.0 - sig[i])
        dkeys_ref[u] = (dk * factor[i] + dscaled * vec[i][2]).astype(jnp.bfloat16)
        ddl_ref[u] = ddl.astype(jnp.bfloat16)
        drl_ref[u] = drl.astype(jnp.bfloat16)
        parts = (
            ddl, drl, dscaled * keys[i], dkl * (rates[i] - 1.0),
            dweight[i] * q[i] * k[i], dmix[i] * normed[i], dmix[i],
        )
        lanes = u[1]
        for j, x in enumerate(parts):
            dvec_ref[j : j + 1, lanes] += sums(x)


def wkv_call(kernel, base, steps, small, arrays, outs, sums, previous, name):
    tokens, width = arrays[0].shape
    rows = CHUNK * STEP_CHUNKS
    last = base + steps - 1
    turned = kernel is backward_kernel
    spec = pl.BlockSpec((rows, width), lambda i: (last - i if turned else base + i, 0))
    state = pl.BlockSpec((2, CHUNK, LANES), lambda i: (0, 0, 0))
    whole = pl.BlockSpec((8, width), lambda i: (0, 0))
    shape = jax.ShapeDtypeStruct
    first = [pl.BlockSpec(memory_space=pltpu.SMEM), whole, state] + [whole] * sums
    held = list(previous or ())
    start = len(first) + len(arrays)
    return pl.pallas_call(
        partial(kernel, base),
        grid=(steps,),
        in_specs=first + [spec] * len(arrays) + [pl.BlockSpec(memory_space=pl.ANY)] * len(held),
        out_specs=[spec] * len(outs) + [whole] * sums + [state],
        out_shape=[shape((tokens, width), dtype) for dtype in outs]
        + [shape((8, width), jnp.float32)] * sums
        + [shape((2, CHUNK, LANES), jnp.float32)],
        input_output_aliases={start + i: i for i in range(len(held))},
        compiler_params=pltpu.CompilerParams(vmem_limit_bytes=24 << 20),
        cost_estimate=SMALL,
        name=name,
    )(*small, *arrays, *held)


def wkv_forward(base, steps, length, vec, state, arrays, previous=None):
    outs = [jnp.bfloat16] + [jnp.float32] * 9
    return wkv_call(
        forward_kernel, base, steps, (length, vec, state), arrays, outs, 0, previous, "wkv_forward"
    )


def wkv_backward(base, steps, length, vec, state, sums, arrays, previous=None):
    outs = [jnp.bfloat16] * 6
    return wkv_call(
        backward_kernel, base, steps, (length, vec, state, sums), arrays, outs, 1, previous,
        "wkv_backward",
    )


ROWS = 128


def row_norm(x):
    centred = x - jnp.mean(x, axis=-1, keepdims=True)
    scale = lax.rsqrt(jnp.mean(centred * centred, axis=-1, keepdims=True) + 1e-05)
    return centred * scale, scale


def shifted(x, edge, down):
    rows = x.shape[0]
    row = lax.broadcasted_iota(jnp.int32, x.shape, 0)
    if down:
        return jnp.where(row == 0, edge, pltpu.roll(x, 1, 0))
    return jnp.where(row == rows - 1, edge, pltpu.roll(x, rows - 1, 0))


def below(x, upper):
    lane = lax.broadcasted_iota(jnp.int32, x.shape, 1)
    keep = (lane >= DECAY_RANK) if upper else (lane < DECAY_RANK)
    return jnp.where(keep, x, jnp.zeros_like(x))


def front_kernel(
    x_ref, vec_ref, wr_ref, wk_ref, wv_ref, down_ref, up_ref,
    m0_ref, m1_ref, m2_ref, m3_ref, m4_ref, m5_ref,
    q_ref, k_ref, v_ref, dl_ref, rl_ref, gate_ref, hid_ref,
    edge_ref,
):
    @pl.when(pl.program_id(0) == 0)
    def _():
        edge_ref[...] = jnp.zeros_like(edge_ref)

    unit, _ = row_norm(x_ref[...].astype(jnp.float32))
    normed = unit * vec_ref[12:13] + vec_ref[13:14]
    change = shifted(normed, edge_ref[:1], True) - normed
    edge_ref[:1] = normed[ROWS - 1 :]
    mixes = []
    for j, ref in enumerate((m0_ref, m1_ref, m2_ref, m3_ref, m4_ref, m5_ref)):
        mixes.append((normed + change * vec_ref[j : j + 1]).astype(jnp.bfloat16))
        ref[...] = mixes[j]
    q_ref[...] = dot32(mixes[0], wr_ref[...], NN)
    k_ref[...] = dot32(mixes[2], wk_ref[...], NN)
    v_ref[...] = dot32(mixes[3], wv_ref[...], NN)
    first = down_ref[:, :128]
    pre_decay, pre_rate = dot32(mixes[1], first, NN), dot32(mixes[4], first, NN)
    pre_gate = dot32(mixes[5], down_ref[:, 128:], NN)
    lane = lax.broadcasted_iota(jnp.int32, pre_decay.shape, 1)
    pair = jnp.where(lane < DECAY_RANK, jnp.tanh(pre_decay), pre_rate)
    gate = jax.nn.sigmoid(pre_gate)
    hid_ref[:, :128] = pair
    hid_ref[:, 128:] = gate
    narrow_pair = pair.astype(jnp.bfloat16)
    dl_ref[...] = dot32(below(narrow_pair, False), up_ref[:, :128], NT)
    rl_ref[...] = dot32(below(narrow_pair, True), up_ref[:, :128], NT)
    gate_ref[...] = dot32(gate.astype(jnp.bfloat16), up_ref[:, 128:], NT)


def front_forward(x, vectors, w_r, w_k, w_v, down, up):
    tokens, width = x.shape
    wide = pl.BlockSpec((ROWS, width), lambda i: (i, 0))
    own = pl.BlockSpec((ROWS, OWN), lambda i: (i, 0))
    hid = pl.BlockSpec((ROWS, 256), lambda i: (i, 0))
    whole = lambda a: pl.BlockSpec(a.shape, lambda i: (0, 0))
    shape = jax.ShapeDtypeStruct
    return pl.pallas_call(
        front_kernel,
        grid=(tokens // ROWS,),
        in_specs=[wide] + [whole(a) for a in (vectors, w_r, w_k, w_v, down, up)],
        out_specs=[wide] * 6 + [own] * 6 + [hid],
        out_shape=[shape((tokens, width), jnp.bfloat16)] * 6
        + [shape((tokens, OWN), jnp.float32)] * 6
        + [shape((tokens, 256), jnp.float32)],
        scratch_shapes=[pltpu.VMEM((8, width), jnp.float32)],
        compiler_params=pltpu.CompilerParams(vmem_limit_bytes=24 << 20),
        cost_estimate=SMALL,
        name="front_forward",
    )(x, vectors, w_r, w_k, w_v, down, up)


def front_back_kernel(
    x_ref, before_ref, vec_ref, wr_ref, wk_ref, wv_ref, down_ref, up_ref,
    m1_ref, m4_ref, m5_ref, hid_ref,
    dq_ref, dk_ref, dv_ref, ddl_ref, drl_ref, dgate_ref, own_vec_ref, ffn_vec_ref,
    dx_ref, mine_ref, other_ref,
    edge_ref, sums_ref, misc_ref,
):
    step = pl.num_programs(0) - 1 - pl.program_id(0)
    core = lax.axis_index("dp") % 2
    own_start = pl.multiple_of(core * OWN, OWN)

    @pl.when(pl.program_id(0) == 0)
    def _():
        edge_ref[...] = jnp.zeros_like(edge_ref)
        sums_ref[...] = jnp.zeros_like(sums_ref)
        misc_ref[...] = jnp.zeros_like(misc_ref)

    unit, scale = row_norm(x_ref[...].astype(jnp.float32))
    gain, offset = vec_ref[12:13], vec_ref[13:14]
    normed = unit * gain + offset
    tail, _ = row_norm(before_ref[...].astype(jnp.float32))
    edge = (tail[15:] * gain + offset) * jnp.where(step == 0, 0.0, 1.0)
    change = shifted(normed, edge, True) - normed
    ddl, drl, dgate = ddl_ref[...], drl_ref[...], dgate_ref[...]
    hid = hid_ref[...]
    pair, gate = hid[:, :128], hid[:, 128:]
    lane = lax.broadcasted_iota(jnp.int32, pair.shape, 1)
    first_up, last_up = up_ref[:, :128], up_ref[:, 128:]
    pair_grad = jnp.where(
        lane < DECAY_RANK,
        dot32(ddl, first_up, NN) * (1.0 - pair * pair),
        dot32(drl, first_up, NN),
    ).astype(jnp.bfloat16)
    gate_grad = (dot32(dgate, last_up, NN) * gate * (1.0 - gate)).astype(jnp.bfloat16)
    narrow_pair, narrow_gate = pair.astype(jnp.bfloat16), gate.astype(jnp.bfloat16)
    own_rows = pl.ds(own_start, OWN)
    misc_ref[own_rows, 256:384] += dot32(ddl, below(narrow_pair, False), TN) + dot32(
        drl, below(narrow_pair, True), TN
    )
    misc_ref[own_rows, 384:512] += dot32(dgate, narrow_gate, TN)
    decay_part, rate_part = below(pair_grad, False), below(pair_grad, True)
    misc_ref[:, :128] += dot32(m1_ref[...], decay_part, TN) + dot32(m4_ref[...], rate_part, TN)
    misc_ref[:, 128:256] += dot32(m5_ref[...], gate_grad, TN)
    first_down = down_ref[:, :128]
    grads = (
        lambda: dot32(dq_ref[...], wr_ref[...], NT),
        lambda: dot32(decay_part, first_down, NT),
        lambda: dot32(dk_ref[...], wk_ref[...], NT),
        lambda: dot32(dv_ref[...], wv_ref[...], NT),
        lambda: dot32(rate_part, first_down, NT),
        lambda: dot32(gate_grad, down_ref[:, 128:], NT),
    )
    total = jnp.zeros_like(change)
    moved = jnp.zeros_like(change)
    for j, grad in enumerate(grads):
        now = grad()
        total = total + now
        moved = moved + now * vec_ref[j : j + 1]
        sums_ref[j : j + 1] += jnp.sum(now * change, axis=0, keepdims=True)
    dnormed = total - moved + shifted(moved, edge_ref[:1], False)
    edge_ref[:1] = moved[:1]
    sums_ref[12:13] += jnp.sum(dnormed * unit, axis=0, keepdims=True)
    sums_ref[13:14] += jnp.sum(dnormed, axis=0, keepdims=True)
    dunit = dnormed * gain
    dx_ref[...] = scale * (
        dunit
        - jnp.mean(dunit, axis=-1, keepdims=True)
        - unit * jnp.mean(dunit * unit, axis=-1, keepdims=True)
    )

    @pl.when(step == 0)
    def _():
        sums_ref[6:7] = ffn_vec_ref[0:1] * 0.5
        sums_ref[14:16] = ffn_vec_ref[1:3] * 0.5
        zeros = jnp.zeros((1, OWN), jnp.float32)
        for target, source in ((7, 0), (8, 1), (9, 2), (10, 3), (11, 4), (16, 5), (17, 6)):
            mine = own_vec_ref[source : source + 1]
            sums_ref[target : target + 1] = jnp.concatenate(
                [jnp.where(core == 0, mine, zeros), jnp.where(core == 0, zeros, mine)], axis=1
            )
        for block in range(EMBED // 128):
            lanes = slice(block * 128, (block + 1) * 128)
            misc_ref[lanes, 512:640] = sums_ref[:, lanes].T
        share = mine_ref.shape[1]
        for chip in range(mine_ref.shape[0]):
            low = misc_ref[2 * chip * share : (2 * chip + 1) * share]
            high = misc_ref[(2 * chip + 1) * share : (2 * chip + 2) * share]
            mine_ref[chip] = jnp.where(core == 0, low, high)
            other_ref[chip] = jnp.where(core == 0, high, low).astype(jnp.bfloat16)


def front_backward(
    x, vectors, w_r, w_k, w_v, down, up, mixes, hid, grads, own_vec, ffn_vec
):
    tokens, width = x.shape
    devices = lax.axis_size("dp")
    pieces = (devices // 2, EMBED // devices, 640)
    steps = tokens // ROWS
    wide = pl.BlockSpec((ROWS, width), lambda i: (steps - 1 - i, 0))
    before = pl.BlockSpec(
        (16, width), lambda i: (jnp.maximum((steps - 1 - i) * (ROWS // 16) - 1, 0), 0)
    )
    own = pl.BlockSpec((ROWS, OWN), lambda i: (steps - 1 - i, 0))
    hid_spec = pl.BlockSpec((ROWS, 256), lambda i: (steps - 1 - i, 0))
    whole = lambda a: pl.BlockSpec(a.shape, lambda i: (0, 0))
    shape = jax.ShapeDtypeStruct
    return pl.pallas_call(
        front_back_kernel,
        grid=(steps,),
        in_specs=[wide, before]
        + [whole(a) for a in (vectors, w_r, w_k, w_v, down, up)]
        + [wide] * 3
        + [hid_spec]
        + [own] * 6
        + [whole(own_vec), whole(ffn_vec)],
        out_specs=[wide] + [pl.BlockSpec(pieces, lambda i: (0, 0, 0))] * 2,
        out_shape=[
            shape((tokens, width), jnp.float32),
            shape(pieces, jnp.float32),
            shape(pieces, jnp.bfloat16),
        ],
        scratch_shapes=[
            pltpu.VMEM((8, width), jnp.float32),
            pltpu.VMEM((128, width), jnp.float32),
            pltpu.VMEM((EMBED, 640), jnp.float32),
        ],
        compiler_params=pltpu.CompilerParams(vmem_limit_bytes=24 << 20),
        cost_estimate=SMALL,
        name="front_backward",
    )(x, x, vectors, w_r, w_k, w_v, down, up, *mixes, hid, *grads, own_vec, ffn_vec)


def ffn_back_kernel(
    len_ref, res_ref, before_ref, cot_ref, mine_ref, other_ref, vec_ref, wo_ref,
    grad_ref, narrow_ref, gated_ref, dvec_ref,
    edge_ref,
):
    step = pl.num_programs(0) - 1 - pl.program_id(0)

    @pl.when(pl.program_id(0) == 0)
    def _():
        edge_ref[...] = jnp.zeros_like(edge_ref)
        dvec_ref[...] = jnp.zeros_like(dvec_ref)

    gain, offset, coefficient = vec_ref[14:15], vec_ref[15:16], vec_ref[6:7]
    unit, scale = row_norm(res_ref[...])
    normed = unit * gain + offset
    tail, _ = row_norm(before_ref[...])
    edge = (tail[7:] * gain + offset) * jnp.where(step == 0, 0.0, 1.0)
    change = shifted(normed, edge, True) - normed
    grad = mine_ref[...].astype(jnp.float32) + other_ref[...].astype(jnp.float32)
    moved = grad * coefficient
    dnormed = grad - moved + shifted(moved, edge_ref[:1], False)
    edge_ref[:1] = moved[:1]
    sums = lambda x: jnp.sum(x, axis=0, keepdims=True)
    dvec_ref[0:1] += sums(grad * change)
    dvec_ref[1:2] += sums(dnormed * unit)
    dvec_ref[2:3] += sums(dnormed)
    dunit = dnormed * gain
    row = lax.broadcasted_iota(jnp.int32, grad.shape, 0) + step * ROWS
    out_grad = jnp.where(row < len_ref[0], cot_ref[...].astype(jnp.float32), 0.0)
    total = out_grad + scale * (
        dunit
        - jnp.mean(dunit, axis=-1, keepdims=True)
        - unit * jnp.mean(dunit * unit, axis=-1, keepdims=True)
    )
    grad_ref[...] = total
    small = total.astype(jnp.bfloat16)
    narrow_ref[...] = small
    gated_ref[...] = dot32(small, wo_ref[...], NT)


def ffn_backward(length, residual, cot, mine, other, vectors, w_o_rows):
    tokens, width = residual.shape
    steps = tokens // ROWS
    wide = pl.BlockSpec((ROWS, width), lambda i: (steps - 1 - i, 0))
    before = pl.BlockSpec(
        (8, width), lambda i: (jnp.maximum((steps - 1 - i) * (ROWS // 8) - 1, 0), 0)
    )
    own = pl.BlockSpec((ROWS, OWN), lambda i: (steps - 1 - i, 0))
    whole = lambda a: pl.BlockSpec(a.shape, lambda i: (0, 0))
    shape = jax.ShapeDtypeStruct
    return pl.pallas_call(
        ffn_back_kernel,
        grid=(steps,),
        in_specs=[pl.BlockSpec(memory_space=pltpu.SMEM), wide, before]
        + [wide] * 3
        + [whole(vectors), whole(w_o_rows)],
        out_specs=[wide, wide, own, pl.BlockSpec((8, width), lambda i: (0, 0))],
        out_shape=[
            shape((tokens, width), jnp.float32),
            shape((tokens, width), jnp.bfloat16),
            shape((tokens, OWN), jnp.float32),
            shape((8, width), jnp.float32),
        ],
        scratch_shapes=[pltpu.VMEM((8, width), jnp.float32)],
        compiler_params=pltpu.CompilerParams(vmem_limit_bytes=24 << 20),
        cost_estimate=SMALL,
        name="ffn_backward",
    )(length, residual, residual, cot, mine, other, vectors, w_o_rows)


def att_grad_kernel(m0_ref, m2_ref, m3_ref, dq_ref, dk_ref, dv_ref, send_a, keep_a, send_b, keep_b):
    chip = lax.axis_index("dp") // 2
    by_x, by_y = chip % 2 == 0, (chip // 2) % 2 == 0
    quarter = OWN // 2
    dv = dv_ref[...]
    first = ((m0_ref, dq_ref[...], 0, OWN), (m3_ref, dv[:, :quarter], OWN, quarter))
    second = ((m2_ref, dk_ref[...], 0, OWN), (m3_ref, dv[:, quarter:], OWN, quarter))
    for z in range(4):
        rows = slice(z * 256, (z + 1) * 256)
        for left, right, lane, width in first:
            block = dot32(left[:, rows], right, TN).astype(jnp.bfloat16)
            lanes = slice(lane, lane + width)
            for y in range(2):
                low, high = block[y * 128 : y * 128 + 64], block[y * 128 + 64 : y * 128 + 128]
                send_a[2 * z + y, :, lanes] = jnp.where(by_x, high, low)
                keep_a[2 * z + y, :, lanes] = jnp.where(by_x, low, high)
        for left, right, lane, width in second:
            block = dot32(left[:, rows], right, TN).astype(jnp.bfloat16)
            lanes = slice(lane, lane + width)
            for x in range(2):
                low, high = block[x * 64 : x * 64 + 64], block[128 + x * 64 : 128 + x * 64 + 64]
                send_b[2 * z + x, :, lanes] = jnp.where(by_y, high, low)
                keep_b[2 * z + x, :, lanes] = jnp.where(by_y, low, high)


def att_gradients(mixes, grads):
    space = pl.BlockSpec(memory_space=pltpu.VMEM)
    return pl.pallas_call(
        att_grad_kernel,
        in_specs=[space] * 6,
        out_specs=[space] * 4,
        out_shape=[jax.ShapeDtypeStruct((8, 64, OWN + OWN // 2), jnp.bfloat16)] * 4,
        compiler_params=pltpu.CompilerParams(vmem_limit_bytes=16 << 20),
        cost_estimate=SMALL,
        name="att_gradients",
    )(*mixes, *grads)


def swap(block, mask):
    size = lax.axis_size("dp")
    return lax.ppermute(block, "dp", [(i, i ^ mask) for i in range(size)])


def bit_of(mask):
    return (lax.axis_index("dp") // mask) % 2


def in_order(mask, own, other, axis):
    lower = bit_of(mask) == 0
    return jnp.where(
        lower, jnp.concatenate([own, other], axis=axis), jnp.concatenate([other, own], axis=axis)
    )


def chip_masks():
    size = lax.axis_size("dp")
    masks = []
    while 2 << len(masks) < size:
        masks.append(2 << len(masks))
    return masks


def steps_of(kind):
    masks = chip_masks()
    near, far = [[mask] for mask in masks[:2]], [[mask] for mask in masks[2:][::-1]]
    first = [[far[0][0], far[1][0], far[0][0] | far[1][0]]] if len(far) == 2 else far
    return [first + near[::-1], first + near, far + near[::-1], far + near, near + far][kind]


class Held:
    def __init__(self, value):
        self.value = value


def meet(movers, *arrays):
    held = []
    for mover in movers:
        held += [x[0] for x in mover.arrived if x[0] not in held]
    out = lax.optimization_barrier(tuple(x.value for x in held) + arrays)
    for x, value in zip(held, out):
        x.value = value
    return out[len(held) :]


def read(arrived):
    return [x.value if lanes is None else x.value[..., lanes] for x, lanes in arrived]


class Gather:
    def __init__(self, block, kind, places=(0,)):
        self.steps = steps_of(kind)
        self.held = block[None]
        self.places = [0]
        self.arrived = []
        self.masks = []

    def merge(self):
        if self.arrived:
            self.held = jnp.concatenate([self.held] + read(self.arrived), axis=0)
            self.places = self.places + [p ^ (m // 2) for m in self.masks for p in self.places]
            self.arrived = []

    def step(self):
        if self.steps:
            self.merge()
            self.masks = self.steps.pop(0)
            self.arrived = [(Held(swap(self.held, mask)), None) for mask in self.masks]
        return self

    def run(self):
        while self.steps:
            self.step()
        return self

    def split(self, kinds):
        width = self.held.shape[-1] // len(kinds)
        out = []
        for i, kind in enumerate(kinds):
            part = Gather.__new__(Gather)
            cut = slice(i * width, (i + 1) * width)
            part.steps = steps_of(kind)[len(steps_of(kind)) - len(self.steps) :]
            part.held = self.held[..., cut]
            part.arrived = [(x, cut) for x, _ in self.arrived]
            part.places, part.masks = self.places, self.masks
            out.append(part)
        return out


def place_kernel(places, cuts, *refs):
    sources, outs = refs[: len(places)], refs[len(places) :]
    chip = lax.axis_index("dp") // 2
    for source, (part, list_of) in zip(sources, places):
        for j, place in enumerate(list_of):
            for out, (first, rows, lanes) in zip(outs, cuts):
                start = pl.multiple_of((chip ^ place) * rows, rows)
                lane, width = lanes[part]
                at = sum(w for _, w in lanes[:part])
                out[pl.ds(start, rows), at : at + width] = source[
                    j, first : first + rows, lane : lane + width
                ]


def assemble(gathers, cuts=None):
    gathers = [g.run() for g in gathers]
    rows = gathers[0].held.shape[1]
    cuts = cuts or ((0, rows, [(0, g.held.shape[2]) for g in gathers]),)
    sources, places = [], []
    for i, g in enumerate(gathers):
        sources += [g.held] + read(g.arrived)
        shifts = [0] + [mask // 2 for mask in g.masks]
        places += [(i, [p ^ shift for p in g.places]) for shift in shifts]
    count = lax.axis_size("dp") // 2
    if any(cut[1] % 16 for cut in cuts):
        return assemble_plain(sources, places, cuts, count)
    space = pl.BlockSpec(memory_space=pltpu.VMEM)
    return pl.pallas_call(
        partial(place_kernel, places, cuts),
        in_specs=[space] * len(sources),
        out_specs=[space] * len(cuts),
        out_shape=[
            jax.ShapeDtypeStruct((count * n, sum(w for _, w in lanes)), sources[0].dtype)
            for _, n, lanes in cuts
        ],
        compiler_params=pltpu.CompilerParams(vmem_limit_bytes=16 << 20),
        cost_estimate=SMALL,
        name="assemble",
    )(*sources)


def assemble_plain(sources, places, cuts, count):
    chip = lax.axis_index("dp") // 2
    parts = []
    for part in sorted({part for part, _ in places}):
        blocks = jnp.concatenate([x for x, (at, _) in zip(sources, places) if at == part])
        where = [p for at, list_of in places if at == part for p in list_of]
        blocks = jnp.stack([blocks[where.index(i)] for i in range(count)])
        parts.append(jnp.take(blocks, chip ^ lax.iota(jnp.int32, count), axis=0))
    return [
        jnp.concatenate(
            [x[:, first : first + n, at : at + w] for x, (at, w) in zip(parts, lanes)], axis=-1
        ).reshape(count * n, -1)
        for first, n, lanes in cuts
    ]


class Scatter:
    def __init__(self, parts, kind):
        self.steps = steps_of(kind)[::-1]
        self.axes = chip_masks()[::-1]
        self.sources = [parts.reshape((2,) * len(self.axes) + parts.shape[1:])]
        self.arrived = []
        self.sent = None

    @classmethod
    def begun(cls, sent, kept, kind):
        out = cls.__new__(cls)
        out.steps = steps_of(kind)[::-1]
        out.axes = [axis for axis in chip_masks()[::-1] if axis != out.steps[0][0]]
        out.sources = [kept.reshape((2,) * len(out.axes) + kept.shape[1:])]
        out.arrived = []
        out.sent = [sent.reshape(out.sources[0].shape)]
        return out

    def pick(self, sources, mask, gone):
        out = []
        for x in sources:
            for place in reversed(range(len(self.axes))):
                axis = self.axes[place]
                if axis in gone:
                    which = bit_of(axis) if not mask & axis else 1 - bit_of(axis)
                    x = lax.dynamic_index_in_dim(x, which, place, keepdims=False)
            out.append(x)
        return out

    def prepare(self):
        if self.sent is not None:
            return self
        masks = self.steps[0]
        sources = self.sources + read(self.arrived)
        gone = [axis for axis in self.axes if any(mask & axis for mask in masks)]
        self.sent = [
            sum(x.astype(jnp.float32) for x in self.pick(sources, mask, gone)).astype(jnp.bfloat16)
            for mask in masks
        ]
        self.sources = self.pick(sources, 0, gone)
        self.axes = [axis for axis in self.axes if axis not in gone]
        self.arrived = []
        return self

    def step(self):
        return together([self])[0]

    def run(self):
        while self.steps:
            self.step()
        return self

    def total(self):
        return sum(x.astype(jnp.float32) for x in self.sources + read(self.arrived))


def together(parts):
    if not parts[0].steps:
        return parts
    for part in parts:
        part.prepare()
    for i, mask in enumerate(parts[0].steps[0]):
        sent = [part.sent[i] for part in parts]
        got = Held(swap(sent[0] if len(sent) == 1 else jnp.concatenate(sent, axis=-1), mask))
        at = 0
        for part, x in zip(parts, sent):
            lanes = slice(at, at + x.shape[-1]) if len(sent) > 1 else None
            part.arrived.append((got, lanes))
            at += x.shape[-1]
    for part in parts:
        part.steps.pop(0)
        part.sent = None
    return parts


def norm_rows(features, gain_row, offset_row):
    average = jnp.mean(features, axis=-1, keepdims=True)
    centred = features - average
    variance = jnp.mean(centred * centred, axis=-1, keepdims=True)
    return centred * lax.rsqrt(variance + 1e-05) * gain_row + offset_row


def product(operand, weight_matrix):
    return jnp.dot(operand, weight_matrix, preferred_element_type=jnp.float32)


def input_gradient_rows(upstream_gradient, weight_matrix):
    return lax.dot_general(
        upstream_gradient,
        weight_matrix,
        (((1,), (1,)), ((), ())),
        preferred_element_type=jnp.float32,
    )


def weight_gradient(operand, upstream_gradient):
    return lax.dot_general(
        operand, upstream_gradient, (((0,), (0,)), ((), ())), preferred_element_type=jnp.float32
    )


def earlier(rows):
    return jnp.concatenate([jnp.zeros_like(rows[:1]), rows[:-1]], axis=0)


def ffn_mix(residual, vectors):
    second = norm_rows(residual, vectors[14], vectors[15])
    return second + (earlier(second) - second) * vectors[6]


def narrow(x):
    return x.astype(jnp.bfloat16)


def local(
    inputs,
    lengths,
    attention_projections,
    channel_key_weight,
    channel_value_weight,
    lowrank_down_weight,
    lowrank_up_weight,
    per_feature_parameters,
    cotangent,
):
    devices = lax.axis_size("dp")
    chips = devices // 2
    device = lax.axis_index("dp")
    chip, core = device // 2, device % 2
    row_count = inputs.shape[0]
    slots = 2 * row_count
    share = EMBED // devices
    pair_share = 2 * share
    units = channel_value_weight.shape[0]
    half_units = chips * units

    def own_cut(x, which):
        return lax.dynamic_slice_in_dim(x, which * OWN, OWN, x.ndim - 1)

    def own_rows(x, which):
        return lax.dynamic_slice_in_dim(x, which * row_count, row_count, 0)

    pair_rows = in_order(
        1,
        own_cut(attention_projections, core),
        swap(own_cut(attention_projections, 1 - core), 1),
        1,
    )
    lora = jnp.concatenate([lowrank_down_weight, lowrank_up_weight.T], axis=1)
    vector_rows = jnp.pad(per_feature_parameters.T, ((0, 0), (0, 128 - 18)))
    vector_rows = vector_rows.reshape(share // 4, OWN)
    first_rows = 3 * pair_share
    misc_rows = share + share // 4 + (share // 4) % 16
    block = jnp.concatenate(
        [
            pair_rows[:3].reshape(first_rows, OWN),
            lora,
            jnp.pad(vector_rows, ((0, (share // 4) % 16), (0, 0))),
        ],
        axis=0,
    )
    half = half_units // 2
    quarter = OWN // 2
    first = Gather(block, 0).step()
    w_o_part = Gather(pair_rows[3], 4).step().step()
    key_in, raw, cot, _ = meet([], channel_key_weight, inputs, cotangent, first.held)
    key_cut = key_in.reshape(share, chips, 2, units)

    def key_columns(which):
        return lax.dynamic_index_in_dim(key_cut, which, 2, keepdims=False).reshape(share, half_units)

    key_rows = in_order(1, key_columns(core), swap(key_columns(1 - core), 1), 0)
    tokens = in_order(1, raw, swap(raw, 1), 0)
    cot = in_order(1, cot, swap(cot, 1), 0)
    key_rows, tokens, cot = meet([first, w_o_part], key_rows, tokens, cot)
    first = first.split((0, 1))
    for part in first:
        part.step()
    key_part = Gather(key_rows, 2).step()
    (tokens,) = meet(first, tokens)
    for part in first:
        part.step()
    value_block, *_ = meet([key_part], channel_value_weight, *[part.held for part in first])
    key_part.step()
    value_part = Gather(value_block, 2).step()
    (tokens,) = meet(first + [key_part, value_part, w_o_part], tokens)
    key_parts = key_part.split((2, 3))
    for part in key_parts:
        part.step()
    w_r, w_k, w_v, misc = assemble(
        first,
        [(i * pair_share, pair_share, [(0, quarter)] * 2) for i in range(3)]
        + [(first_rows, misc_rows, [(0, quarter)] * 2)],
    )
    misc = misc.reshape(chips, 1, misc_rows, OWN)
    misc = in_order(1, misc, swap(misc, 1), 1)
    value_part.step()
    w_o_part.step()
    lora = misc[:, :, :share].reshape(EMBED, OWN)
    down, up_t = lora[:, :256], lax.dynamic_slice_in_dim(lora[:, 256:], core * OWN, OWN, 0)
    vectors = misc[:, :, share : share + share // 4].reshape(EMBED, 128)[:, :18].T
    vectors = vectors.astype(jnp.float32)
    own_vectors = own_cut(vectors, core)
    used = jnp.concatenate([own_vectors[7:12], own_vectors[16:18], own_vectors[:1]], axis=0)
    length = lax.dynamic_index_in_dim(lengths, chip, 0)
    live = (lax.iota(jnp.int32, slots) < length)[:, None]

    *mixes, queries, keys, values, decay_low, rate_low, gate_rows, hid = front_forward(
        tokens, vectors, w_r, w_k, w_v, down, up_t
    )
    terms = meet(
        key_parts + [value_part, w_o_part],
        queries, keys, values, decay_low, rate_low, gate_rows,
    )
    value_parts = value_part.split((2, 3))
    for part in key_parts + value_parts:
        part.step()
    w_o_part.step()
    blocks = slots // (CHUNK * STEP_CHUNKS)
    early = blocks // 2
    zero_state = jnp.zeros((2, CHUNK, LANES), jnp.float32)
    *before, state = wkv_forward(0, early, length, used, zero_state, terms)
    (state,) = meet(value_parts, state)
    for part in value_parts:
        part.step()
    state, *_ = meet([], state, *[part.held for part in value_parts])
    gated, *saved, _ = wkv_forward(early, blocks - early, length, used, state, terms, before)
    gated, cot, tokens = meet(key_parts + [w_o_part], gated, cot, tokens)
    gated_all = in_order(1, gated, swap(gated, 1), 1)
    (w_o_own,) = assemble([w_o_part])
    w_o = in_order(1, w_o_own, swap(w_o_own, 1), 1)
    (key_weight,) = assemble(key_parts)
    residual = tokens.astype(jnp.float32) + product(gated_all, w_o)
    ffn_in = narrow(ffn_mix(residual, vectors))
    (ffn_in,) = meet(value_parts, ffn_in)
    positive = jax.nn.relu(product(ffn_in, key_weight))
    hidden = narrow(jnp.square(positive))
    out_narrow = jnp.where(live, cot, jnp.zeros_like(cot))
    value_cuts = ((0, quarter), (quarter, OWN), (OWN, EMBED))
    value_grads = [
        narrow(weight_gradient(hidden, out_narrow[:, lo:hi])).reshape(chips, units, hi - lo)
        for lo, hi in value_cuts
    ]
    w_o_rows = lax.dynamic_slice_in_dim(w_o, core * OWN, OWN, 0)
    hidden, positive, out_narrow, w_o_rows, *value_grads = meet(
        value_parts, hidden, positive, out_narrow, w_o_rows, *value_grads
    )
    (value_weight,) = assemble(value_parts)

    value_scatter = [Scatter(x, kind).step() for kind, x in zip((2, 3, 4), value_grads)]
    late_scatter = value_scatter.pop()
    pre_narrow = narrow(2.0 * positive * input_gradient_rows(out_narrow, value_weight))
    ffn_in_grad = narrow(input_gradient_rows(pre_narrow, key_weight))
    other_grad = swap(ffn_in_grad, 1)
    grad_key = narrow(weight_gradient(ffn_in, pre_narrow)).reshape(chips, pair_share, half_units)
    residual_grad, attended_grad, gated_grad, ffn_vec = ffn_backward(
        length, residual, cot, ffn_in_grad, other_grad, vectors, w_o_rows
    )
    grad_o = narrow(weight_gradient(gated_all, own_cut(attended_grad, core)))
    grad_o = grad_o.reshape(chips, pair_share, OWN)
    key_scatter = [Scatter(grad_key[:, :, i * half : (i + 1) * half], 2 + i) for i in range(2)]
    o_scatter = [Scatter(grad_o[:, :, i * quarter : (i + 1) * quarter], 2 + i) for i in range(2)]
    key_pairs = list(zip(key_scatter, o_scatter))
    for part in key_scatter + o_scatter:
        part.prepare()
    gated_grad, *sent = meet(
        value_scatter, gated_grad, *[m.sent[0] for m in key_scatter + o_scatter]
    )
    for part, x in zip(key_scatter + o_scatter, sent):
        part.sent = [x]
    for pair in key_pairs:
        together(pair)
    for part in value_scatter:
        part.step()
    terms = [*terms, gated_grad, *saved]
    zero_sums = jnp.zeros((8, OWN), jnp.float32)
    *before, sums, state = wkv_backward(
        early, blocks - early, length, used, zero_state, zero_sums, terms
    )
    state, sums = meet(value_scatter + [late_scatter], state, sums)
    together(value_scatter)
    late_scatter.step()
    *low_grads, own_vec, _ = wkv_backward(0, early, length, used, state, sums, terms, before)
    key_all = key_scatter + o_scatter
    *low_grads, own_vec = meet(key_all + value_scatter + [late_scatter], *low_grads, own_vec)
    if pair_share == 64:
        sent_a, kept_a, sent_b, kept_b = att_gradients(
            (mixes[0], mixes[2], mixes[3]), low_grads[:3]
        )
        att_scatter = [Scatter.begun(sent_a, kept_a, 2), Scatter.begun(sent_b, kept_b, 3)]
    else:
        grads = [narrow(weight_gradient(mixes[m], g)) for m, g in zip((0, 2, 3), low_grads)]
        att_scatter = [
            Scatter(jnp.concatenate(x, axis=1).reshape(chips, pair_share, 3 * quarter), 2 + i).prepare()
            for i, x in enumerate(
                ((grads[0], grads[2][:, :quarter]), (grads[1], grads[2][:, quarter:]))
            )
        ]
    own_vec, *sent = meet([], own_vec, *[m.sent[0] for m in att_scatter])
    for part, x in zip(att_scatter, sent):
        part.sent = [x]
        part.step()
    for pair in key_pairs:
        together(pair)
    together(value_scatter)
    token_part, misc_mine, misc_other = front_backward(
        tokens, vectors, w_r, w_k, w_v, down, up_t, (mixes[1], mixes[4], mixes[5]), hid,
        low_grads, own_vec, ffn_vec,
    )
    token_part, misc_mine, misc_other, hidden = meet(
        key_all + value_scatter, token_part, misc_mine, misc_other, hidden
    )
    misc_sum = misc_mine + swap(misc_other, 1).astype(jnp.float32)
    misc_sum = jnp.concatenate([misc_sum[..., :320], misc_sum[..., 320:]], axis=1)
    misc_scatter = Scatter(misc_sum, 3)
    masks = chip_masks()
    misc_scatter.steps = [[masks[0], masks[1], masks[0] | masks[1]]] + misc_scatter.steps[2:]
    together(key_all)
    misc_scatter.step()
    (token_part,) = meet(att_scatter, token_part)
    for part in att_scatter:
        part.step()
    (token_part,) = meet(key_all, token_part)
    together(key_all)
    late_scatter.step()
    ffn_part = product(hidden, value_weight)
    token_part, ffn_part = meet(
        att_scatter + [misc_scatter, late_scatter], token_part, ffn_part
    )
    last_parts = att_scatter + [misc_scatter]
    if len(misc_scatter.steps) == 2:
        for part in last_parts:
            part.steps = [[masks[2], masks[3], masks[2] | masks[3]]]
    together(last_parts)
    late_scatter.step()
    input_gradient = (
        own_rows(residual_grad, core)
        + own_rows(token_part, core)
        + swap(own_rows(token_part, 1 - core), 1)
    )
    ffn_out = own_rows(ffn_part, core) + swap(own_rows(ffn_part, 1 - core), 1)
    output = narrow(jnp.where(own_rows(live, core), own_rows(residual, core) + ffn_out, 0.0))
    value_sum = jnp.concatenate(
        [x.run().total() for x in value_scatter + [late_scatter]], axis=1
    )
    while key_scatter[0].steps:
        together(key_all)
    key_sum = jnp.concatenate([x.total() for x in key_all], axis=1).reshape(2, share, -1)

    def exchange(x):
        mine = lax.dynamic_index_in_dim(x, core, 0, keepdims=False)
        return mine, swap(lax.dynamic_index_in_dim(x, 1 - core, 0, keepdims=False), 1)

    key_mine, key_theirs = exchange(key_sum)
    input_gradient, value_sum, key_mine, key_theirs = meet(
        last_parts, input_gradient, value_sum, key_mine, key_theirs
    )
    while last_parts[0].steps:
        together(last_parts)
    first_sum, second_sum, misc_sum = [x.total() for x in last_parts]
    misc_sum = jnp.concatenate([misc_sum[:share], misc_sum[share:]], axis=1)
    att_sum = jnp.concatenate(
        [first_sum[:, :OWN], second_sum[:, :OWN], first_sum[:, OWN:], second_sum[:, OWN:]], axis=1
    )
    mine, theirs = exchange(att_sum.reshape(2, share, -1))
    mine = jnp.concatenate([mine, key_mine[:, half_units:]], axis=1)
    theirs = jnp.concatenate([theirs, key_theirs[:, half_units:]], axis=1)
    shard_mixer = jnp.stack(
        [
            in_order(1, mine[:, i * OWN : (i + 1) * OWN], theirs[:, i * OWN : (i + 1) * OWN], 1)
            for i in range(4)
        ]
    )
    shard_key = in_order(
        1,
        key_mine[:, :half_units].reshape(share, chips, 1, units),
        key_theirs[:, :half_units].reshape(share, chips, 1, units),
        2,
    ).reshape(share, 2 * half_units)
    return (
        output,
        input_gradient,
        shard_mixer,
        shard_key,
        value_sum,
        misc_sum[:, :256],
        misc_sum[:, 256:512].T,
        misc_sum[:, 512:530].T,
    )


def solution(mesh):
    in_specs = (
        P("dp", None),
        P(),
        P(None, "dp", None),
        P("dp", None),
        P("dp", None),
        P("dp", None),
        P(None, "dp"),
        P(None, "dp"),
        P("dp", None),
    )
    out_specs = (
        P("dp", None),
        P("dp", None),
        P(None, "dp", None),
        P("dp", None),
        P("dp", None),
        P("dp", None),
        P(None, "dp"),
        P(None, "dp"),
    )
    return jax.shard_map(local, mesh=mesh, in_specs=in_specs, out_specs=out_specs, check_vma=False)
```

```python
from functools import partial

import jax
import jax.numpy as jnp
from jax import lax
from jax.experimental import pallas as pl
from jax.experimental.pallas import tpu as pltpu
from jax.sharding import PartitionSpec as P

HEADS = 16
HEAD_SIZE = 64
DECAY_RANK = 64
RATE_RANK = 64
EMBED = 1024
OWN = EMBED // 2
PRECISE = lax.Precision.HIGHEST


CHUNK = 64
LANES = 256
GROUP_HEADS = 4
STEP_CHUNKS = 2
SMALL = pl.CostEstimate(flops=1, bytes_accessed=1, transcendentals=0)

NN = (((1,), (0,)), ((), ()))
NT = (((1,), (1,)), ((), ()))
TN = (((0,), (0,)), ((), ()))


def halves(x):
    high = x.astype(jnp.bfloat16)
    return high, (x - high.astype(jnp.float32)).astype(jnp.bfloat16)


def dot32(a, b, dims):
    return lax.dot_general(a, b, dims, preferred_element_type=jnp.float32)


def mul(left, right, dims=NN):
    rows = left[0].shape[0]
    both = dot32(jnp.concatenate(left, axis=0), right[0], dims)
    return both[:rows] + both[rows:] + dot32(left[0], right[1], dims)


def tmul(left, right, masks):
    full = (
        dot32(left[0], right[0], TN) + dot32(left[1], right[0], TN) + dot32(left[0], right[1], TN)
    )
    return sum(full[h * CHUNK : (h + 1) * CHUNK] * masks[h][:1].astype(jnp.float32) for h in range(GROUP_HEADS))


def spread(pair, masks):
    return tuple(
        jnp.concatenate([part * masks[h] for h in range(GROUP_HEADS)], axis=0) for part in pair
    )


def stack(first, second):
    return tuple(jnp.concatenate([x, y], axis=0) for x, y in zip(first, second))


def head_masks():
    lane = lax.broadcasted_iota(jnp.int32, (CHUNK, LANES), 1) // CHUNK
    return [(lane == h).astype(jnp.float32).astype(jnp.bfloat16) for h in range(GROUP_HEADS)]


def places():
    row = lax.broadcasted_iota(jnp.int32, (CHUNK, LANES), 0)
    col = lax.broadcasted_iota(jnp.int32, (CHUNK, LANES), 1) % CHUNK
    return row, col


def running_sum(x, upper=False):
    row = lax.broadcasted_iota(jnp.int32, (CHUNK, CHUNK), 0)
    col = lax.broadcasted_iota(jnp.int32, (CHUNK, CHUNK), 1)
    ones = (row <= col if upper else col <= row).astype(jnp.float32).astype(jnp.bfloat16)
    high, rest = halves(x)
    low = (x - high.astype(jnp.float32) - rest.astype(jnp.float32)).astype(jnp.bfloat16)
    return dot32(ones, high, NN) + dot32(ones, rest, NN) + dot32(ones, low, NN)


def scaled_forms(q, w, k, a, b):
    total = running_sum(w)
    before = total - w
    middle = total[CHUNK // 2 - 1 : CHUNK // 2]
    end = total[CHUNK - 1 :]
    ea = jnp.exp(before - middle)
    eq = jnp.exp(total - middle)
    eb = jnp.exp(middle - total)
    ee = jnp.exp(end - total)
    return (a * ea, q * eq, b * eb, k * eb, b * ee, k * ee), (ea, eq, eb, ee), (jnp.exp(middle), jnp.exp(end))


def each(fn, *columns):
    return [fn(*row) for row in zip(*columns)]


def block_ones():
    row = lax.broadcasted_iota(jnp.int32, (LANES, LANES), 0) // CHUNK
    col = lax.broadcasted_iota(jnp.int32, (LANES, LANES), 1) // CHUNK
    return (row == col).astype(jnp.float32).astype(jnp.bfloat16)


def head_sum(x, ones):
    rows = x.shape[0]
    both = dot32(jnp.concatenate(halves(x), axis=0), ones, NN)
    return both[:rows] + both[rows:]


def prepared(keys, decay_low, rate_low, live, vec, ones):
    sig = jax.nn.sigmoid(vec[0] + decay_low)
    log_decay = (-0.6065306597126334) * sig * live
    rates = jax.nn.sigmoid(vec[1] + rate_low)
    scaled = keys * vec[2]
    inverse = lax.rsqrt(head_sum(scaled * scaled, ones) + 1e-06)
    unit_keys = scaled * inverse
    factor = (1.0 + (rates - 1.0) * vec[3]) * live
    return log_decay, keys * factor, -unit_keys, unit_keys * rates * live, sig, rates, inverse, factor


def read_out(o, q, k, v, vec, ones):
    centred = o - head_sum(o, ones) * (1.0 / CHUNK)
    scale = lax.rsqrt(head_sum(centred * centred, ones) * (1.0 / CHUNK) + 0.00064)
    normed = centred * scale
    weight = head_sum(q * k * vec[4], ones)
    return normed, scale, weight, normed * vec[5] + vec[6] + weight * v


def unit_slices():
    return [
        (slice(c * CHUNK, (c + 1) * CHUNK), slice(g * LANES, (g + 1) * LANES))
        for c in range(STEP_CHUNKS)
        for g in range(2)
    ]


def unit_live(length, step):
    row = lax.broadcasted_iota(jnp.int32, (CHUNK, LANES), 0)
    start = step * (STEP_CHUNKS * CHUNK)
    live = [(row + (start + c * CHUNK) < length).astype(jnp.float32) for c in range(STEP_CHUNKS)]
    return [live[c] for c in range(STEP_CHUNKS) for g in range(2)]


def unit_vectors(vec_ref):
    vec = [[vec_ref[i : i + 1, g * LANES : (g + 1) * LANES] for i in range(7)] for g in range(2)]
    return [vec[g] for c in range(STEP_CHUNKS) for g in range(2)]


def forward_kernel(base, *refs):
    len_ref, vec_ref, start_ref, q_ref, keys_ref, v_ref, dl_ref, rl_ref, gate_ref = refs[:9]
    (
        out_ref, o_ref, t_ref, aqb_ref, aak_ref, aqk_ref, y_ref, z_ref, trt_ref, qe_ref, state_ref,
    ) = refs[-11:]

    @pl.when(pl.program_id(0) == 0)
    def _():
        state_ref[...] = start_ref[...]

    masks = head_masks()
    row, col = places()
    strict = (col < row).astype(jnp.float32)
    within = (col <= row).astype(jnp.float32)
    eye = (col == row).astype(jnp.float32)
    ones = block_ones()
    units = unit_slices()
    live = unit_live(len_ref[0], pl.program_id(0) + base)
    vec = unit_vectors(vec_ref)
    load = lambda ref: [ref[u] for u in units]
    q, keys, v = load(q_ref), load(keys_ref), load(v_ref)
    ready = each(
        lambda x, y, z, m, n: prepared(x, y, z, m, n, ones), keys, load(dl_ref), load(rl_ref), live, vec
    )
    w, k, a, b = ([x[i] for x in ready] for i in range(4))
    forms = each(scaled_forms, q, w, k, a, b)
    ah, qh, bh, kh, bt, kt = ([f[0][i] for f in forms] for i in range(6))
    emid = [f[2][0] for f in forms]
    eend = [f[2][1] for f in forms]
    aq = each(lambda x, y: halves(jnp.concatenate([x, y], axis=0)), ah, qh)
    with_b = each(lambda l, r: mul(l, spread(halves(r), masks), NT), aq, bh)
    with_k = each(lambda l, r: mul(l, spread(halves(r), masks), NT), aq, kh)
    aab = [x[:CHUNK] * strict for x in with_b]
    aqb = [halves(x[CHUNK:] * within) for x in with_b]
    aak = [halves(x[:CHUNK] * strict) for x in with_k]
    aqk = [halves(x[CHUNK:] * within) for x in with_k]
    p = [halves(x * (row // 8 == col // 8)) for x in aab]
    t = [eye + x * (row // 8 == col // 8) for x in aab]
    p2 = each(lambda x: halves(mul(x, spread(x, masks))), p)
    both = each(lambda x, y: mul(stack(x, halves(y)), spread(x, masks)), p2, t)
    p4 = [halves(x[:CHUNK]) for x in both]
    t = each(lambda x, y: x + y[CHUNK:], t, both)
    t = each(lambda x, y: x + mul(halves(x), spread(y, masks)), t, p4)
    for size in (8, 16, 32):
        corner = ((row // size) % 2 == 1) & (col // size == row // size - 1)
        ts = [halves(x) for x in t]
        n = [halves(x * corner) for x in aab]
        tn = each(lambda x, y: halves(mul(x, spread(y, masks))), ts, n)
        t = each(lambda x, y, z: x + mul(y, spread(z, masks)), t, tn, ts)
    ts = [halves(x) for x in t]
    vs = [halves(x) for x in v]
    vm = [spread(x, masks) for x in vs]
    wide = each(lambda x, y, e: mul(x, spread(halves(y * e), masks)), ts, ah, emid)
    r0 = each(mul, aak, vm)
    y0 = each(lambda x, y: mul(x, spread(halves(y), masks)), ts, r0)
    wides = [halves(x) for x in wide]
    qe = each(lambda x, e, y, z: x * e + mul(y, spread(z, masks)), qh, emid, aqb, wides)
    y0s = [halves(x) for x in y0]
    part = each(lambda x, y, z, u: mul(x, spread(y, masks)) + mul(z, u), aqb, y0s, aqk, vm)
    bts = [halves(x) for x in bt]
    diag = [eye * e for e in eend]
    tr = each(lambda x, y, d: tmul(x, y, masks) + d, bts, wides, diag)
    trt = each(lambda x, y, d: tmul(y, x, masks) + d, bts, wides, diag)
    inject = each(lambda x, y, z, u: tmul(stack(x, halves(y)), stack(z, u), masks), bts, kt, y0s, vs)
    wq = each(lambda x, y: stack(x, halves(y)), wides, qe)
    z = []
    out = []
    for c in range(STEP_CHUNKS):
        for g in range(2):
            i = c * 2 + g
            now = state_ref[g]
            nows = spread(halves(now), masks)
            state_ref[g] = mul(halves(tr[i]), nows) + inject[i]
            z.append(now)
            out.append(mul(wq[i], nows))
    o = each(lambda x, y: x[CHUNK:] + y, out, part)
    mixed = each(lambda x, y, z, m, n: read_out(x, y, z, m, n, ones)[3], o, q, k, v, vec)
    for i, u in enumerate(units):
        out_ref[u] = (mixed[i] * gate_ref[u]).astype(jnp.bfloat16)
        o_ref[u] = o[i]
        y_ref[u] = out[i][:CHUNK] + y0[i]
        t_ref[u] = t[i]
        aqb_ref[u] = with_b[i][CHUNK:] * within
        aak_ref[u] = with_k[i][:CHUNK] * strict
        aqk_ref[u] = with_k[i][CHUNK:] * within
        z_ref[u] = z[i]
        trt_ref[u] = trt[i]
        qe_ref[u] = qe[i]


def backward_kernel(base, *refs):
    (
        len_ref, vec_ref, start_ref, sums_ref, q_ref, keys_ref, v_ref, dl_ref, rl_ref, gate_ref,
        g_ref, o_ref, t_ref, aqb_ref, aak_ref, aqk_ref, y_ref, z_ref, trt_ref, qe_ref,
    ) = refs[:20]
    dq_ref, dkeys_ref, dv_ref, ddl_ref, drl_ref, dgate_ref, dvec_ref, state_ref = refs[-8:]
    step = base + pl.num_programs(0) - 1 - pl.program_id(0)

    @pl.when(pl.program_id(0) == 0)
    def _():
        state_ref[...] = start_ref[...]
        dvec_ref[...] = sums_ref[...]

    masks = head_masks()
    row, col = places()
    strict = (col < row).astype(jnp.float32)
    within = (col <= row).astype(jnp.float32)
    ones = block_ones()
    units = unit_slices()
    live = unit_live(len_ref[0], step)
    vec = unit_vectors(vec_ref)
    load = lambda ref: [ref[u] for u in units]
    q, keys, v, g = load(q_ref), load(keys_ref), load(v_ref), load(g_ref)
    ready = each(
        lambda x, y, z, m, n: prepared(x, y, z, m, n, ones), keys, load(dl_ref), load(rl_ref), live, vec
    )
    w, k, a, b, sig, rates, inverse, factor = ([x[i] for x in ready] for i in range(8))
    seen = each(lambda x, y, z, m, n: read_out(x, y, z, m, n, ones), load(o_ref), q, k, v, vec)
    normed, scale, weight, mixed = ([x[i] for x in seen] for i in range(4))
    gate = load(gate_ref)
    dgate = each(lambda x, y: x * y, g, mixed)
    dmix = each(lambda x, y: x * y, g, gate)
    dn = each(lambda x, n: x * n[5], dmix, vec)
    do = each(
        lambda x, n, r: r
        * (x - head_sum(x, ones) * (1.0 / CHUNK) - n * (head_sum(x * n, ones) * (1.0 / CHUNK))),
        dn, normed, scale,
    )
    dweight = each(lambda x, y: head_sum(x * y, ones), dmix, v)
    do = [halves(x) for x in do]
    qe, trt, t, aqb, aak, aqk, ys = (
        [halves(x) for x in load(ref)]
        for ref in (qe_ref, trt_ref, t_ref, aqb_ref, aak_ref, aqk_ref, y_ref)
    )
    z = load(z_ref)
    vs = [halves(x) for x in v]
    h = each(lambda x, y: tmul(x, y, masks), qe, do)
    dz = [None] * len(units)
    for c in reversed(range(STEP_CHUNKS)):
        for g in range(2):
            i = c * 2 + g
            now = state_ref[g]
            dz[i] = now
            state_ref[g] = mul(trt[i], spread(halves(now), masks)) + h[i]
    dzs = [spread(halves(x), masks) for x in dz]
    zs = [spread(halves(x), masks) for x in z]
    forms = each(scaled_forms, q, w, k, a, b)
    ah, qh, bh, kh, bt, kt = ([f[0][i] for f in forms] for i in range(6))
    ea, eq, eb, ee = ([f[1][i] for f in forms] for i in range(4))
    emid = [f[2][0] for f in forms]
    eend = [f[2][1] for f in forms]
    from_end = each(lambda x, y, s: mul(halves(jnp.concatenate([x, y], axis=0)), s), bt, kt, dzs)
    dy = each(lambda x, y, s: halves(tmul(x, y, masks) + s[:CHUNK]), aqb, do, from_end)
    dr = each(lambda x, y: halves(tmul(x, y, masks)), t, dy)
    ro = each(stack, dr, do)
    dv = each(lambda x, y, s, f: tmul(stack(x, y), s, masks) + f[CHUNK:], aak, aqk, ro, from_end)
    mask2 = jnp.concatenate([strict, within], axis=0)
    dab = each(lambda s, y: halves(mul(s, spread(y, masks), NT) * mask2), ro, ys)
    dak = each(lambda s, y: halves(mul(s, spread(y, masks), NT) * mask2), ro, vs)
    dst = each(lambda s, y: mul(s, y, NT), ro, zs)
    daq = each(
        lambda s, e, x, bb, y, kk: s * e + mul(x, spread(halves(bb), masks)) + mul(y, spread(halves(kk), masks)),
        dst, emid, dab, bh, dak, kh,
    )
    aq = each(lambda x, y: halves(jnp.concatenate([x, y], axis=0)), ah, qh)
    dbh = each(lambda x, y: tmul(x, y, masks), dab, aq)
    dkh = each(lambda x, y: tmul(x, y, masks), dak, aq)
    dend = each(lambda y, x, s: mul(stack(y, x), s, NT), ys, vs, dzs)
    row_of_ones = jnp.ones((8, LANES), jnp.bfloat16)
    sums = lambda x: jnp.sum(x, axis=0, keepdims=True)
    for i, u in enumerate(units):
        da = daq[i][:CHUNK] * ea[i]
        dq = daq[i][CHUNK:] * eq[i]
        dbt = dend[i][:CHUNK] * ee[i]
        dkt = dend[i][CHUNK:] * ee[i]
        db = dbh[i] * eb[i] + dbt
        dk = dkh[i] * eb[i] + dkt
        pa = da * a[i]
        diff = dq * q[i] - db * b[i] - dk * k[i] + pa
        zz = spread(halves(z[i] * dz[i]), masks)
        carry = (dot32(row_of_ones, zz[0], NT) + dot32(row_of_ones, zz[1], NT))[:1] * eend[i]
        carry = carry + sums(dbt * b[i] + dkt * k[i])
        dw = running_sum(diff, upper=True) - pa + carry
        from_bonus = dweight[i] * vec[i][4]
        dk = dk + from_bonus * q[i]
        dq_ref[u] = (dq + from_bonus * k[i]).astype(jnp.bfloat16)
        dv_ref[u] = (dv[i] + weight[i] * dmix[i]).astype(jnp.bfloat16)
        dgate_ref[u] = dgate[i].astype(jnp.bfloat16)
        unit_keys = -a[i]
        db = db * live[i]
        du = db * rates[i] - da
        dscaled = inverse[i] * (du - unit_keys * head_sum(du * unit_keys, ones))
        dkl = dk * keys[i] * live[i]
        drl = (db * unit_keys + dkl * vec[i][3]) * rates[i] * (1.0 - rates[i])
        ddl = dw * w[i] * (1.0 - sig[i])
        dkeys_ref[u] = (dk * factor[i] + dscaled * vec[i][2]).astype(jnp.bfloat16)
        ddl_ref[u] = ddl.astype(jnp.bfloat16)
        drl_ref[u] = drl.astype(jnp.bfloat16)
        parts = (
            ddl, drl, dscaled * keys[i], dkl * (rates[i] - 1.0),
            dweight[i] * q[i] * k[i], dmix[i] * normed[i], dmix[i],
        )
        lanes = u[1]
        for j, x in enumerate(parts):
            dvec_ref[j : j + 1, lanes] += sums(x)


def wkv_call(kernel, base, steps, small, arrays, outs, sums, previous, name):
    tokens, width = arrays[0].shape
    rows = CHUNK * STEP_CHUNKS
    last = base + steps - 1
    turned = kernel is backward_kernel
    spec = pl.BlockSpec((rows, width), lambda i: (last - i if turned else base + i, 0))
    state = pl.BlockSpec((2, CHUNK, LANES), lambda i: (0, 0, 0))
    whole = pl.BlockSpec((8, width), lambda i: (0, 0))
    shape = jax.ShapeDtypeStruct
    first = [pl.BlockSpec(memory_space=pltpu.SMEM), whole, state] + [whole] * sums
    held = list(previous or ())
    start = len(first) + len(arrays)
    return pl.pallas_call(
        partial(kernel, base),
        grid=(steps,),
        in_specs=first + [spec] * len(arrays) + [pl.BlockSpec(memory_space=pl.ANY)] * len(held),
        out_specs=[spec] * len(outs) + [whole] * sums + [state],
        out_shape=[shape((tokens, width), dtype) for dtype in outs]
        + [shape((8, width), jnp.float32)] * sums
        + [shape((2, CHUNK, LANES), jnp.float32)],
        input_output_aliases={start + i: i for i in range(len(held))},
        compiler_params=pltpu.CompilerParams(vmem_limit_bytes=60 << 20),
        cost_estimate=SMALL,
        name=name,
    )(*small, *arrays, *held)


def wkv_forward(base, steps, length, vec, state, arrays, previous=None):
    outs = [jnp.bfloat16] + [jnp.float32] * 9
    return wkv_call(
        forward_kernel, base, steps, (length, vec, state), arrays, outs, 0, previous, "wkv_forward"
    )


def wkv_backward(base, steps, length, vec, state, sums, arrays, previous=None):
    outs = [jnp.bfloat16] * 6
    return wkv_call(
        backward_kernel, base, steps, (length, vec, state, sums), arrays, outs, 1, previous,
        "wkv_backward",
    )


ROWS = 128


def row_norm(x):
    centred = x - jnp.mean(x, axis=-1, keepdims=True)
    scale = lax.rsqrt(jnp.mean(centred * centred, axis=-1, keepdims=True) + 1e-05)
    return centred * scale, scale


def shifted(x, edge, down):
    rows = x.shape[0]
    row = lax.broadcasted_iota(jnp.int32, x.shape, 0)
    if down:
        return jnp.where(row == 0, edge, pltpu.roll(x, 1, 0))
    return jnp.where(row == rows - 1, edge, pltpu.roll(x, rows - 1, 0))


def below(x, upper):
    lane = lax.broadcasted_iota(jnp.int32, x.shape, 1)
    keep = (lane >= DECAY_RANK) if upper else (lane < DECAY_RANK)
    return jnp.where(keep, x, jnp.zeros_like(x))


def front_kernel(
    x_ref, vec_ref, wr_ref, wk_ref, wv_ref, down_ref, up_ref,
    m0_ref, m1_ref, m2_ref, m3_ref, m4_ref, m5_ref,
    q_ref, k_ref, v_ref, dl_ref, rl_ref, gate_ref, hid_ref,
    edge_ref,
):
    @pl.when(pl.program_id(0) == 0)
    def _():
        edge_ref[...] = jnp.zeros_like(edge_ref)

    unit, _ = row_norm(x_ref[...].astype(jnp.float32))
    normed = unit * vec_ref[12:13] + vec_ref[13:14]
    change = shifted(normed, edge_ref[:1], True) - normed
    edge_ref[:1] = normed[ROWS - 1 :]
    mixes = []
    for j, ref in enumerate((m0_ref, m1_ref, m2_ref, m3_ref, m4_ref, m5_ref)):
        mixes.append((normed + change * vec_ref[j : j + 1]).astype(jnp.bfloat16))
        ref[...] = mixes[j]
    q_ref[...] = dot32(mixes[0], wr_ref[...], NN)
    k_ref[...] = dot32(mixes[2], wk_ref[...], NN)
    v_ref[...] = dot32(mixes[3], wv_ref[...], NN)
    first = down_ref[:, :128]
    pre_decay, pre_rate = dot32(mixes[1], first, NN), dot32(mixes[4], first, NN)
    pre_gate = dot32(mixes[5], down_ref[:, 128:], NN)
    lane = lax.broadcasted_iota(jnp.int32, pre_decay.shape, 1)
    pair = jnp.where(lane < DECAY_RANK, jnp.tanh(pre_decay), pre_rate)
    gate = jax.nn.sigmoid(pre_gate)
    hid_ref[:, :128] = pair
    hid_ref[:, 128:] = gate
    narrow_pair = pair.astype(jnp.bfloat16)
    dl_ref[...] = dot32(below(narrow_pair, False), up_ref[:, :128], NT)
    rl_ref[...] = dot32(below(narrow_pair, True), up_ref[:, :128], NT)
    gate_ref[...] = dot32(gate.astype(jnp.bfloat16), up_ref[:, 128:], NT)


def front_forward(x, vectors, w_r, w_k, w_v, down, up):
    tokens, width = x.shape
    wide = pl.BlockSpec((ROWS, width), lambda i: (i, 0))
    own = pl.BlockSpec((ROWS, OWN), lambda i: (i, 0))
    hid = pl.BlockSpec((ROWS, 256), lambda i: (i, 0))
    whole = lambda a: pl.BlockSpec(a.shape, lambda i: (0, 0))
    shape = jax.ShapeDtypeStruct
    return pl.pallas_call(
        front_kernel,
        grid=(tokens // ROWS,),
        in_specs=[wide] + [whole(a) for a in (vectors, w_r, w_k, w_v, down, up)],
        out_specs=[wide] * 6 + [own] * 6 + [hid],
        out_shape=[shape((tokens, width), jnp.bfloat16)] * 6
        + [shape((tokens, OWN), jnp.float32)] * 6
        + [shape((tokens, 256), jnp.float32)],
        scratch_shapes=[pltpu.VMEM((8, width), jnp.float32)],
        compiler_params=pltpu.CompilerParams(vmem_limit_bytes=60 << 20),
        cost_estimate=SMALL,
        name="front_forward",
    )(x, vectors, w_r, w_k, w_v, down, up)


def front_back_kernel(
    x_ref, before_ref, vec_ref, wr_ref, wk_ref, wv_ref, down_ref, up_ref,
    m1_ref, m4_ref, m5_ref, hid_ref,
    dq_ref, dk_ref, dv_ref, ddl_ref, drl_ref, dgate_ref, own_vec_ref, ffn_vec_ref,
    dx_ref, mine_ref, other_ref,
    edge_ref, sums_ref, misc_ref,
):
    step = pl.num_programs(0) - 1 - pl.program_id(0)
    core = lax.axis_index("dp") % 2
    own_start = pl.multiple_of(core * OWN, OWN)

    @pl.when(pl.program_id(0) == 0)
    def _():
        edge_ref[...] = jnp.zeros_like(edge_ref)
        sums_ref[...] = jnp.zeros_like(sums_ref)
        misc_ref[...] = jnp.zeros_like(misc_ref)

    unit, scale = row_norm(x_ref[...].astype(jnp.float32))
    gain, offset = vec_ref[12:13], vec_ref[13:14]
    normed = unit * gain + offset
    tail, _ = row_norm(before_ref[...].astype(jnp.float32))
    edge = (tail[15:] * gain + offset) * jnp.where(step == 0, 0.0, 1.0)
    change = shifted(normed, edge, True) - normed
    ddl, drl, dgate = ddl_ref[...], drl_ref[...], dgate_ref[...]
    hid = hid_ref[...]
    pair, gate = hid[:, :128], hid[:, 128:]
    lane = lax.broadcasted_iota(jnp.int32, pair.shape, 1)
    first_up, last_up = up_ref[:, :128], up_ref[:, 128:]
    pair_grad = jnp.where(
        lane < DECAY_RANK,
        dot32(ddl, first_up, NN) * (1.0 - pair * pair),
        dot32(drl, first_up, NN),
    ).astype(jnp.bfloat16)
    gate_grad = (dot32(dgate, last_up, NN) * gate * (1.0 - gate)).astype(jnp.bfloat16)
    narrow_pair, narrow_gate = pair.astype(jnp.bfloat16), gate.astype(jnp.bfloat16)
    own_rows = pl.ds(own_start, OWN)
    misc_ref[own_rows, 256:384] += dot32(ddl, below(narrow_pair, False), TN) + dot32(
        drl, below(narrow_pair, True), TN
    )
    misc_ref[own_rows, 384:512] += dot32(dgate, narrow_gate, TN)
    decay_part, rate_part = below(pair_grad, False), below(pair_grad, True)
    misc_ref[:, :128] += dot32(m1_ref[...], decay_part, TN) + dot32(m4_ref[...], rate_part, TN)
    misc_ref[:, 128:256] += dot32(m5_ref[...], gate_grad, TN)
    first_down = down_ref[:, :128]
    grads = (
        lambda: dot32(dq_ref[...], wr_ref[...], NT),
        lambda: dot32(decay_part, first_down, NT),
        lambda: dot32(dk_ref[...], wk_ref[...], NT),
        lambda: dot32(dv_ref[...], wv_ref[...], NT),
        lambda: dot32(rate_part, first_down, NT),
        lambda: dot32(gate_grad, down_ref[:, 128:], NT),
    )
    total = jnp.zeros_like(change)
    moved = jnp.zeros_like(change)
    for j, grad in enumerate(grads):
        now = grad()
        total = total + now
        moved = moved + now * vec_ref[j : j + 1]
        sums_ref[j : j + 1] += jnp.sum(now * change, axis=0, keepdims=True)
    dnormed = total - moved + shifted(moved, edge_ref[:1], False)
    edge_ref[:1] = moved[:1]
    sums_ref[12:13] += jnp.sum(dnormed * unit, axis=0, keepdims=True)
    sums_ref[13:14] += jnp.sum(dnormed, axis=0, keepdims=True)
    dunit = dnormed * gain
    dx_ref[...] = scale * (
        dunit
        - jnp.mean(dunit, axis=-1, keepdims=True)
        - unit * jnp.mean(dunit * unit, axis=-1, keepdims=True)
    )

    @pl.when(step == 0)
    def _():
        sums_ref[6:7] = ffn_vec_ref[0:1] * 0.5
        sums_ref[14:16] = ffn_vec_ref[1:3] * 0.5
        zeros = jnp.zeros((1, OWN), jnp.float32)
        for target, source in ((7, 0), (8, 1), (9, 2), (10, 3), (11, 4), (16, 5), (17, 6)):
            mine = own_vec_ref[source : source + 1]
            sums_ref[target : target + 1] = jnp.concatenate(
                [jnp.where(core == 0, mine, zeros), jnp.where(core == 0, zeros, mine)], axis=1
            )
        for block in range(EMBED // 128):
            lanes = slice(block * 128, (block + 1) * 128)
            misc_ref[lanes, 512:640] = sums_ref[:, lanes].T
        share = mine_ref.shape[1]
        for chip in range(mine_ref.shape[0]):
            low = misc_ref[2 * chip * share : (2 * chip + 1) * share]
            high = misc_ref[(2 * chip + 1) * share : (2 * chip + 2) * share]
            mine_ref[chip] = jnp.where(core == 0, low, high)
            other_ref[chip] = jnp.where(core == 0, high, low).astype(jnp.bfloat16)


def front_backward(
    x, vectors, w_r, w_k, w_v, down, up, mixes, hid, grads, own_vec, ffn_vec
):
    tokens, width = x.shape
    devices = lax.axis_size("dp")
    pieces = (devices // 2, EMBED // devices, 640)
    steps = tokens // ROWS
    wide = pl.BlockSpec((ROWS, width), lambda i: (steps - 1 - i, 0))
    before = pl.BlockSpec(
        (16, width), lambda i: (jnp.maximum((steps - 1 - i) * (ROWS // 16) - 1, 0), 0)
    )
    own = pl.BlockSpec((ROWS, OWN), lambda i: (steps - 1 - i, 0))
    hid_spec = pl.BlockSpec((ROWS, 256), lambda i: (steps - 1 - i, 0))
    whole = lambda a: pl.BlockSpec(a.shape, lambda i: (0, 0))
    shape = jax.ShapeDtypeStruct
    return pl.pallas_call(
        front_back_kernel,
        grid=(steps,),
        in_specs=[wide, before]
        + [whole(a) for a in (vectors, w_r, w_k, w_v, down, up)]
        + [wide] * 3
        + [hid_spec]
        + [own] * 6
        + [whole(own_vec), whole(ffn_vec)],
        out_specs=[wide] + [pl.BlockSpec(pieces, lambda i: (0, 0, 0))] * 2,
        out_shape=[
            shape((tokens, width), jnp.float32),
            shape(pieces, jnp.float32),
            shape(pieces, jnp.bfloat16),
        ],
        scratch_shapes=[
            pltpu.VMEM((8, width), jnp.float32),
            pltpu.VMEM((128, width), jnp.float32),
            pltpu.VMEM((EMBED, 640), jnp.float32),
        ],
        compiler_params=pltpu.CompilerParams(vmem_limit_bytes=60 << 20),
        cost_estimate=SMALL,
        name="front_backward",
    )(x, x, vectors, w_r, w_k, w_v, down, up, *mixes, hid, *grads, own_vec, ffn_vec)


def ffn_back_kernel(
    len_ref, res_ref, before_ref, cot_ref, mine_ref, other_ref, vec_ref, wo_ref,
    grad_ref, narrow_ref, gated_ref, dvec_ref,
    edge_ref,
):
    step = pl.num_programs(0) - 1 - pl.program_id(0)

    @pl.when(pl.program_id(0) == 0)
    def _():
        edge_ref[...] = jnp.zeros_like(edge_ref)
        dvec_ref[...] = jnp.zeros_like(dvec_ref)

    gain, offset, coefficient = vec_ref[14:15], vec_ref[15:16], vec_ref[6:7]
    unit, scale = row_norm(res_ref[...])
    normed = unit * gain + offset
    tail, _ = row_norm(before_ref[...])
    edge = (tail[7:] * gain + offset) * jnp.where(step == 0, 0.0, 1.0)
    change = shifted(normed, edge, True) - normed
    grad = mine_ref[...].astype(jnp.float32) + other_ref[...].astype(jnp.float32)
    moved = grad * coefficient
    dnormed = grad - moved + shifted(moved, edge_ref[:1], False)
    edge_ref[:1] = moved[:1]
    sums = lambda x: jnp.sum(x, axis=0, keepdims=True)
    dvec_ref[0:1] += sums(grad * change)
    dvec_ref[1:2] += sums(dnormed * unit)
    dvec_ref[2:3] += sums(dnormed)
    dunit = dnormed * gain
    row = lax.broadcasted_iota(jnp.int32, grad.shape, 0) + step * ROWS
    out_grad = jnp.where(row < len_ref[0], cot_ref[...].astype(jnp.float32), 0.0)
    total = out_grad + scale * (
        dunit
        - jnp.mean(dunit, axis=-1, keepdims=True)
        - unit * jnp.mean(dunit * unit, axis=-1, keepdims=True)
    )
    grad_ref[...] = total
    small = total.astype(jnp.bfloat16)
    narrow_ref[...] = small
    gated_ref[...] = dot32(small, wo_ref[...], NT)


def ffn_backward(length, residual, cot, mine, other, vectors, w_o_rows):
    tokens, width = residual.shape
    steps = tokens // ROWS
    wide = pl.BlockSpec((ROWS, width), lambda i: (steps - 1 - i, 0))
    before = pl.BlockSpec(
        (8, width), lambda i: (jnp.maximum((steps - 1 - i) * (ROWS // 8) - 1, 0), 0)
    )
    own = pl.BlockSpec((ROWS, OWN), lambda i: (steps - 1 - i, 0))
    whole = lambda a: pl.BlockSpec(a.shape, lambda i: (0, 0))
    shape = jax.ShapeDtypeStruct
    return pl.pallas_call(
        ffn_back_kernel,
        grid=(steps,),
        in_specs=[pl.BlockSpec(memory_space=pltpu.SMEM), wide, before]
        + [wide] * 3
        + [whole(vectors), whole(w_o_rows)],
        out_specs=[wide, wide, own, pl.BlockSpec((8, width), lambda i: (0, 0))],
        out_shape=[
            shape((tokens, width), jnp.float32),
            shape((tokens, width), jnp.bfloat16),
            shape((tokens, OWN), jnp.float32),
            shape((8, width), jnp.float32),
        ],
        scratch_shapes=[pltpu.VMEM((8, width), jnp.float32)],
        compiler_params=pltpu.CompilerParams(vmem_limit_bytes=60 << 20),
        cost_estimate=SMALL,
        name="ffn_backward",
    )(length, residual, residual, cot, mine, other, vectors, w_o_rows)


def att_grad_kernel(m0_ref, m2_ref, m3_ref, gated_ref, dq_ref, dk_ref, dv_ref, da_ref,
                    send_a, keep_a, send_b, keep_b):
    chip = lax.axis_index("dp") // 2
    by_x, by_y = chip % 2 == 0, (chip // 2) % 2 == 0
    core = lax.axis_index("dp") % 2
    da = da_ref[:, pl.ds(pl.multiple_of(core * OWN, OWN), OWN)]
    first = ((m0_ref, dq_ref[...]), (gated_ref, da))
    second = ((m2_ref, dk_ref[...]), (m3_ref, dv_ref[...]))
    for half, ((left_a, right_a), (left_b, right_b)) in enumerate(zip(first, second)):
        lanes = slice(half * OWN, (half + 1) * OWN)
        for z in range(4):
            rows = slice(z * 256, (z + 1) * 256)
            block = dot32(left_a[:, rows], right_a, TN).astype(jnp.bfloat16)
            for y in range(2):
                low, high = block[y * 128 : y * 128 + 64], block[y * 128 + 64 : y * 128 + 128]
                send_a[2 * z + y, :, lanes] = jnp.where(by_x, high, low)
                keep_a[2 * z + y, :, lanes] = jnp.where(by_x, low, high)
            block = dot32(left_b[:, rows], right_b, TN).astype(jnp.bfloat16)
            for x in range(2):
                low, high = block[x * 64 : x * 64 + 64], block[128 + x * 64 : 128 + x * 64 + 64]
                send_b[2 * z + x, :, lanes] = jnp.where(by_y, high, low)
                keep_b[2 * z + x, :, lanes] = jnp.where(by_y, low, high)


def att_gradients(mixes, gated, grads, attended_grad):
    space = pl.BlockSpec(memory_space=pltpu.VMEM)
    return pl.pallas_call(
        att_grad_kernel,
        in_specs=[space] * 8,
        out_specs=[space] * 4,
        out_shape=[jax.ShapeDtypeStruct((8, 64, 2 * OWN), jnp.bfloat16)] * 4,
        compiler_params=pltpu.CompilerParams(vmem_limit_bytes=60 << 20),
        cost_estimate=SMALL,
        name="att_gradients",
    )(*mixes, gated, *grads, attended_grad)


def swap(block, mask):
    size = lax.axis_size("dp")
    return lax.ppermute(block, "dp", [(i, i ^ mask) for i in range(size)])


def bit_of(mask):
    return (lax.axis_index("dp") // mask) % 2


def in_order(mask, own, other, axis):
    lower = bit_of(mask) == 0
    return jnp.where(
        lower, jnp.concatenate([own, other], axis=axis), jnp.concatenate([other, own], axis=axis)
    )


def chip_masks():
    size = lax.axis_size("dp")
    masks = []
    while 2 << len(masks) < size:
        masks.append(2 << len(masks))
    return masks


def steps_of(kind):
    masks = chip_masks()
    near, far = [[mask] for mask in masks[:2]], [[mask] for mask in masks[2:][::-1]]
    first = [[far[0][0], far[1][0], far[0][0] | far[1][0]]] if len(far) == 2 else far
    return [first + near[::-1], first + near, far + near[::-1], far + near, near + far][kind]


class Held:
    def __init__(self, value):
        self.value = value


def meet(movers, *arrays):
    held = []
    for mover in movers:
        held += [x[0] for x in mover.arrived if x[0] not in held]
    out = lax.optimization_barrier(tuple(x.value for x in held) + arrays)
    for x, value in zip(held, out):
        x.value = value
    return out[len(held) :]


def read(arrived):
    return [x.value if lanes is None else x.value[..., lanes] for x, lanes in arrived]


class Gather:
    def __init__(self, block, kind, places=(0,)):
        self.steps = steps_of(kind)
        self.held = block[None]
        self.places = [0]
        self.arrived = []
        self.masks = []

    def merge(self):
        if self.arrived:
            self.held = jnp.concatenate([self.held] + read(self.arrived), axis=0)
            self.places = self.places + [p ^ (m // 2) for m in self.masks for p in self.places]
            self.arrived = []

    def step(self):
        if self.steps:
            self.merge()
            self.masks = self.steps.pop(0)
            self.arrived = [(Held(swap(self.held, mask)), None) for mask in self.masks]
        return self

    def run(self):
        while self.steps:
            self.step()
        return self

    def split(self, kinds):
        width = self.held.shape[-1] // len(kinds)
        out = []
        for i, kind in enumerate(kinds):
            part = Gather.__new__(Gather)
            cut = slice(i * width, (i + 1) * width)
            part.steps = steps_of(kind)[len(steps_of(kind)) - len(self.steps) :]
            part.held = self.held[..., cut]
            part.arrived = [(x, cut) for x, _ in self.arrived]
            part.places, part.masks = self.places, self.masks
            out.append(part)
        return out


def place_kernel(places, cuts, *refs):
    sources, outs = refs[: len(places)], refs[len(places) :]
    chip = lax.axis_index("dp") // 2
    for source, (part, list_of) in zip(sources, places):
        for j, place in enumerate(list_of):
            for out, (first, rows, lanes) in zip(outs, cuts):
                start = pl.multiple_of((chip ^ place) * rows, rows)
                lane, width = lanes[part]
                at = sum(w for _, w in lanes[:part])
                out[pl.ds(start, rows), at : at + width] = source[
                    j, first : first + rows, lane : lane + width
                ]


def assemble(gathers, cuts=None):
    gathers = [g.run() for g in gathers]
    rows = gathers[0].held.shape[1]
    cuts = cuts or ((0, rows, [(0, g.held.shape[2]) for g in gathers]),)
    sources, places = [], []
    for i, g in enumerate(gathers):
        sources += [g.held] + read(g.arrived)
        shifts = [0] + [mask // 2 for mask in g.masks]
        places += [(i, [p ^ shift for p in g.places]) for shift in shifts]
    count = lax.axis_size("dp") // 2
    if any(cut[1] % 16 for cut in cuts):
        return assemble_plain(sources, places, cuts, count)
    space = pl.BlockSpec(memory_space=pltpu.VMEM)
    return pl.pallas_call(
        partial(place_kernel, places, cuts),
        in_specs=[space] * len(sources),
        out_specs=[space] * len(cuts),
        out_shape=[
            jax.ShapeDtypeStruct((count * n, sum(w for _, w in lanes)), sources[0].dtype)
            for _, n, lanes in cuts
        ],
        compiler_params=pltpu.CompilerParams(vmem_limit_bytes=32 << 20),
        cost_estimate=SMALL,
        name="assemble",
    )(*sources)


def assemble_plain(sources, places, cuts, count):
    chip = lax.axis_index("dp") // 2
    parts = []
    for part in sorted({part for part, _ in places}):
        blocks = jnp.concatenate([x for x, (at, _) in zip(sources, places) if at == part])
        where = [p for at, list_of in places if at == part for p in list_of]
        blocks = jnp.stack([blocks[where.index(i)] for i in range(count)])
        parts.append(jnp.take(blocks, chip ^ lax.iota(jnp.int32, count), axis=0))
    return [
        jnp.concatenate(
            [x[:, first : first + n, at : at + w] for x, (at, w) in zip(parts, lanes)], axis=-1
        ).reshape(count * n, -1)
        for first, n, lanes in cuts
    ]


class Scatter:
    def __init__(self, parts, kind):
        self.steps = steps_of(kind)[::-1]
        self.axes = chip_masks()[::-1]
        self.sources = [parts.reshape((2,) * len(self.axes) + parts.shape[1:])]
        self.arrived = []
        self.sent = None

    @classmethod
    def begun(cls, sent, kept, kind):
        out = cls.__new__(cls)
        out.steps = steps_of(kind)[::-1]
        out.axes = [axis for axis in chip_masks()[::-1] if axis != out.steps[0][0]]
        out.sources = [kept.reshape((2,) * len(out.axes) + kept.shape[1:])]
        out.arrived = []
        out.sent = [sent.reshape(out.sources[0].shape)]
        return out

    def pick(self, sources, mask, gone):
        out = []
        for x in sources:
            for place in reversed(range(len(self.axes))):
                axis = self.axes[place]
                if axis in gone:
                    which = bit_of(axis) if not mask & axis else 1 - bit_of(axis)
                    x = lax.dynamic_index_in_dim(x, which, place, keepdims=False)
            out.append(x)
        return out

    def prepare(self):
        if self.sent is not None:
            return self
        masks = self.steps[0]
        sources = self.sources + read(self.arrived)
        gone = [axis for axis in self.axes if any(mask & axis for mask in masks)]
        self.sent = [
            sum(x.astype(jnp.float32) for x in self.pick(sources, mask, gone)).astype(jnp.bfloat16)
            for mask in masks
        ]
        self.sources = self.pick(sources, 0, gone)
        self.axes = [axis for axis in self.axes if axis not in gone]
        self.arrived = []
        return self

    def step(self):
        return together([self])[0]

    def run(self):
        while self.steps:
            self.step()
        return self

    def total(self):
        return sum(x.astype(jnp.float32) for x in self.sources + read(self.arrived))


def together(parts):
    if not parts[0].steps:
        return parts
    for part in parts:
        part.prepare()
    for i, mask in enumerate(parts[0].steps[0]):
        sent = [part.sent[i] for part in parts]
        got = Held(swap(sent[0] if len(sent) == 1 else jnp.concatenate(sent, axis=-1), mask))
        at = 0
        for part, x in zip(parts, sent):
            lanes = slice(at, at + x.shape[-1]) if len(sent) > 1 else None
            part.arrived.append((got, lanes))
            at += x.shape[-1]
    for part in parts:
        part.steps.pop(0)
        part.sent = None
    return parts


def norm_rows(features, gain_row, offset_row):
    average = jnp.mean(features, axis=-1, keepdims=True)
    centred = features - average
    variance = jnp.mean(centred * centred, axis=-1, keepdims=True)
    return centred * lax.rsqrt(variance + 1e-05) * gain_row + offset_row


def product(operand, weight_matrix):
    return jnp.dot(operand, weight_matrix, preferred_element_type=jnp.float32)


def input_gradient_rows(upstream_gradient, weight_matrix):
    return lax.dot_general(
        upstream_gradient,
        weight_matrix,
        (((1,), (1,)), ((), ())),
        preferred_element_type=jnp.float32,
    )


def weight_gradient(operand, upstream_gradient):
    return lax.dot_general(
        operand, upstream_gradient, (((0,), (0,)), ((), ())), preferred_element_type=jnp.float32
    )


def earlier(rows):
    return jnp.concatenate([jnp.zeros_like(rows[:1]), rows[:-1]], axis=0)


def ffn_mix(residual, vectors):
    second = norm_rows(residual, vectors[14], vectors[15])
    return second + (earlier(second) - second) * vectors[6]


def narrow(x):
    return x.astype(jnp.bfloat16)


def local(
    inputs,
    lengths,
    attention_projections,
    channel_key_weight,
    channel_value_weight,
    lowrank_down_weight,
    lowrank_up_weight,
    per_feature_parameters,
    cotangent,
):
    devices = lax.axis_size("dp")
    chips = devices // 2
    device = lax.axis_index("dp")
    chip, core = device // 2, device % 2
    row_count = inputs.shape[0]
    slots = 2 * row_count
    share = EMBED // devices
    pair_share = 2 * share
    units = channel_value_weight.shape[0]
    half_units = chips * units

    def own_cut(x, which):
        return lax.dynamic_slice_in_dim(x, which * OWN, OWN, x.ndim - 1)

    def own_rows(x, which):
        return lax.dynamic_slice_in_dim(x, which * row_count, row_count, 0)

    pair_rows = in_order(
        1,
        own_cut(attention_projections, core),
        swap(own_cut(attention_projections, 1 - core), 1),
        1,
    )
    lora = jnp.concatenate([lowrank_down_weight, lowrank_up_weight.T], axis=1)
    vector_rows = jnp.pad(per_feature_parameters.T, ((0, 0), (0, 128 - 18)))
    vector_rows = vector_rows.reshape(share // 4, OWN)
    first_rows = 3 * pair_share
    misc_rows = share + share // 4 + (share // 4) % 16
    block = jnp.concatenate(
        [
            pair_rows[:3].reshape(first_rows, OWN),
            lora,
            jnp.pad(vector_rows, ((0, (share // 4) % 16), (0, 0))),
        ],
        axis=0,
    )
    half = half_units // 2
    quarter = OWN // 2
    first = Gather(block, 0).step()
    w_o_part = Gather(pair_rows[3], 4).step().step()
    key_in, raw, cot, _ = meet([], channel_key_weight, inputs, cotangent, first.held)
    key_cut = key_in.reshape(share, chips, 2, units)

    def key_columns(which):
        return lax.dynamic_index_in_dim(key_cut, which, 2, keepdims=False).reshape(share, half_units)

    key_rows = in_order(1, key_columns(core), swap(key_columns(1 - core), 1), 0)
    tokens = in_order(1, raw, swap(raw, 1), 0)
    cot = in_order(1, cot, swap(cot, 1), 0)
    key_rows, tokens, cot = meet([first, w_o_part], key_rows, tokens, cot)
    first = first.split((0, 1))
    for part in first:
        part.step()
    key_part = Gather(key_rows, 2).step()
    (tokens,) = meet(first, tokens)
    for part in first:
        part.step()
    value_block, *_ = meet([key_part], channel_value_weight, *[part.held for part in first])
    key_part.step()
    value_part = Gather(value_block, 2).step()
    w_o_part.step()
    (tokens,) = meet(first + [key_part, value_part], tokens)
    key_parts = key_part.split((2, 3))
    for part in key_parts:
        part.step()
    w_r, w_k, w_v, misc = assemble(
        first,
        [(i * pair_share, pair_share, [(0, quarter)] * 2) for i in range(3)]
        + [(first_rows, misc_rows, [(0, quarter)] * 2)],
    )
    misc = misc.reshape(chips, 1, misc_rows, OWN)
    misc = in_order(1, misc, swap(misc, 1), 1)
    value_part.step()
    lora = misc[:, :, :share].reshape(EMBED, OWN)
    down, up_t = lora[:, :256], lax.dynamic_slice_in_dim(lora[:, 256:], core * OWN, OWN, 0)
    vectors = misc[:, :, share : share + share // 4].reshape(EMBED, 128)[:, :18].T
    vectors = vectors.astype(jnp.float32)
    own_vectors = own_cut(vectors, core)
    used = jnp.concatenate([own_vectors[7:12], own_vectors[16:18], own_vectors[:1]], axis=0)
    length = lax.dynamic_index_in_dim(lengths, chip, 0)
    live = (lax.iota(jnp.int32, slots) < length)[:, None]

    *mixes, queries, keys, values, decay_low, rate_low, gate_rows, hid = front_forward(
        tokens, vectors, w_r, w_k, w_v, down, up_t
    )
    terms = meet(
        key_parts + [value_part, w_o_part],
        queries, keys, values, decay_low, rate_low, gate_rows,
    )
    value_parts = value_part.split((2, 3))
    for part in key_parts + value_parts:
        part.step()
    w_o_part.step()
    blocks = slots // (CHUNK * STEP_CHUNKS)
    early = blocks // 2
    zero_state = jnp.zeros((2, CHUNK, LANES), jnp.float32)
    *before, state = wkv_forward(0, early, length, used, zero_state, terms)
    (state,) = meet(value_parts, state)
    for part in value_parts:
        part.step()
    state, *_ = meet([], state, *[part.held for part in value_parts])
    gated, *saved, _ = wkv_forward(early, blocks - early, length, used, state, terms, before)
    gated, cot, tokens = meet(key_parts + [w_o_part], gated, cot, tokens)
    gated_all = in_order(1, gated, swap(gated, 1), 1)
    (w_o_own,) = assemble([w_o_part])
    w_o = in_order(1, w_o_own, swap(w_o_own, 1), 1)
    (key_weight,) = assemble(key_parts)
    residual = tokens.astype(jnp.float32) + product(gated_all, w_o)
    ffn_in = narrow(ffn_mix(residual, vectors))
    positive = jax.nn.relu(product(ffn_in, key_weight))
    hidden = narrow(jnp.square(positive))
    out_narrow = jnp.where(live, cot, jnp.zeros_like(cot))
    value_cuts = ((0, quarter), (quarter, OWN), (OWN, EMBED))
    value_grads = [
        narrow(weight_gradient(hidden, out_narrow[:, lo:hi])).reshape(chips, units, hi - lo)
        for lo, hi in value_cuts
    ]
    w_o_rows = lax.dynamic_slice_in_dim(w_o, core * OWN, OWN, 0)
    hidden, positive, out_narrow, w_o_rows, *value_grads = meet(
        value_parts, hidden, positive, out_narrow, w_o_rows, *value_grads
    )
    (value_weight,) = assemble(value_parts)

    value_scatter = [Scatter(x, kind).step() for kind, x in zip((2, 3, 4), value_grads)]
    late_scatter = value_scatter.pop()
    pre_narrow = narrow(2.0 * positive * input_gradient_rows(out_narrow, value_weight))
    ffn_in_grad = narrow(input_gradient_rows(pre_narrow, key_weight))
    other_grad = swap(ffn_in_grad, 1)
    grad_key = narrow(weight_gradient(ffn_in, pre_narrow)).reshape(chips, pair_share, half_units)
    residual_grad, attended_grad, gated_grad, ffn_vec = ffn_backward(
        length, residual, cot, ffn_in_grad, other_grad, vectors, w_o_rows
    )
    key_scatter = [
        Scatter(grad_key[:, :, i * half : (i + 1) * half], 2 + i).prepare() for i in range(2)
    ]
    gated_grad, *sent = meet(value_scatter, gated_grad, *[m.sent[0] for m in key_scatter])
    for part, x in zip(key_scatter, sent):
        part.sent = [x]
        part.step()
    for part in value_scatter:
        part.step()
    terms = [*terms, gated_grad, *saved]
    zero_sums = jnp.zeros((8, OWN), jnp.float32)
    *before, sums, state = wkv_backward(
        early, blocks - early, length, used, zero_state, zero_sums, terms
    )
    state, sums = meet(value_scatter + [late_scatter], state, sums)
    together(value_scatter)
    late_scatter.step()
    *low_grads, own_vec, _ = wkv_backward(0, early, length, used, state, sums, terms, before)
    *low_grads, own_vec = meet(
        key_scatter + value_scatter + [late_scatter], *low_grads, own_vec
    )
    if pair_share == 64:
        sent_a, kept_a, sent_b, kept_b = att_gradients(
            (mixes[0], mixes[2], mixes[3]), gated_all, low_grads[:3], attended_grad
        )
        att_scatter = [Scatter.begun(sent_a, kept_a, 2), Scatter.begun(sent_b, kept_b, 3)]
    else:
        grads = [weight_gradient(mixes[m], g) for m, g in zip((0, 2, 3), low_grads)]
        grad_o = weight_gradient(gated_all, own_cut(attended_grad, core))
        att_scatter = [
            Scatter(
                narrow(jnp.concatenate(x, axis=1)).reshape(chips, pair_share, EMBED), 2 + i
            ).prepare()
            for i, x in enumerate(((grads[0], grad_o), (grads[1], grads[2])))
        ]
    own_vec, *sent = meet([], own_vec, *[m.sent[0] for m in att_scatter])
    for part, x in zip(att_scatter, sent):
        part.sent = [x]
        part.step()
    for part in key_scatter:
        part.step()
    together(value_scatter)
    token_part, misc_mine, misc_other = front_backward(
        tokens, vectors, w_r, w_k, w_v, down, up_t, (mixes[1], mixes[4], mixes[5]), hid,
        low_grads, own_vec, ffn_vec,
    )
    token_part, misc_mine, misc_other = meet(
        key_scatter + value_scatter, token_part, misc_mine, misc_other
    )
    misc_sum = misc_mine + swap(misc_other, 1).astype(jnp.float32)
    misc_sum = jnp.concatenate([misc_sum[..., :320], misc_sum[..., 320:]], axis=1)
    misc_scatter = Scatter(misc_sum, 3)
    masks = chip_masks()
    misc_scatter.steps = [[masks[0], masks[1], masks[0] | masks[1]]] + misc_scatter.steps[2:]
    together(key_scatter)
    misc_scatter.step()
    (token_part,) = meet(att_scatter, token_part)
    for part in att_scatter:
        part.step()
    token_part, hidden = meet(key_scatter, token_part, hidden)
    together(key_scatter)
    late_scatter.step()
    (token_part,) = meet(att_scatter + [misc_scatter, late_scatter], token_part)
    last_parts = att_scatter + [misc_scatter]
    if len(misc_scatter.steps) == 2:
        for part in last_parts:
            part.steps = [[masks[2], masks[3], masks[2] | masks[3]]]
    together(last_parts)
    late_scatter.step()
    ffn_part = product(hidden, value_weight)
    input_gradient = (
        own_rows(residual_grad, core)
        + own_rows(token_part, core)
        + swap(own_rows(token_part, 1 - core), 1)
    )
    ffn_out = own_rows(ffn_part, core) + swap(own_rows(ffn_part, 1 - core), 1)
    output = narrow(jnp.where(own_rows(live, core), own_rows(residual, core) + ffn_out, 0.0))
    value_sum = jnp.concatenate(
        [x.run().total() for x in value_scatter + [late_scatter]], axis=1
    )
    while key_scatter[0].steps:
        together(key_scatter)
    key_sum = jnp.concatenate([x.total() for x in key_scatter], axis=1).reshape(2, share, -1)

    def exchange(x):
        mine = lax.dynamic_index_in_dim(x, core, 0, keepdims=False)
        return mine, swap(lax.dynamic_index_in_dim(x, 1 - core, 0, keepdims=False), 1)

    key_mine, key_theirs = exchange(key_sum)
    input_gradient, value_sum, key_mine, key_theirs = meet(
        last_parts, input_gradient, value_sum, key_mine, key_theirs
    )
    while last_parts[0].steps:
        together(last_parts)
    first_sum, second_sum, misc_sum = [x.total() for x in last_parts]
    misc_sum = jnp.concatenate([misc_sum[:share], misc_sum[share:]], axis=1)
    att_sum = jnp.concatenate(
        [first_sum[:, :OWN], second_sum, first_sum[:, OWN:]], axis=1
    )
    mine, theirs = exchange(att_sum.reshape(2, share, -1))
    shard_mixer = jnp.stack(
        [
            in_order(1, mine[:, i * OWN : (i + 1) * OWN], theirs[:, i * OWN : (i + 1) * OWN], 1)
            for i in range(4)
        ]
    )
    shard_key = in_order(
        1,
        key_mine.reshape(share, chips, 1, units),
        key_theirs.reshape(share, chips, 1, units),
        2,
    ).reshape(share, 2 * half_units)
    return (
        output,
        input_gradient,
        shard_mixer,
        shard_key,
        value_sum,
        misc_sum[:, :256],
        misc_sum[:, 256:512].T,
        misc_sum[:, 512:530].T,
    )


def solution(mesh):
    in_specs = (
        P("dp", None),
        P(),
        P(None, "dp", None),
        P("dp", None),
        P("dp", None),
        P("dp", None),
        P(None, "dp"),
        P(None, "dp"),
        P("dp", None),
    )
    out_specs = (
        P("dp", None),
        P("dp", None),
        P(None, "dp", None),
        P("dp", None),
        P("dp", None),
        P("dp", None),
        P(None, "dp"),
        P(None, "dp"),
    )
    return jax.shard_map(local, mesh=mesh, in_specs=in_specs, out_specs=out_specs, check_vma=False)
```

```python
from functools import partial

import jax
import jax.numpy as jnp
from jax import lax
from jax.experimental import pallas as pl
from jax.experimental.pallas import tpu as pltpu
from jax.sharding import PartitionSpec as P

HEADS = 16
HEAD_SIZE = 64
DECAY_RANK = 64
RATE_RANK = 64
EMBED = 1024
OWN = EMBED // 2
PRECISE = lax.Precision.HIGHEST


CHUNK = 64
LANES = 256
GROUP_HEADS = 4
STEP_CHUNKS = 2
SMALL = pl.CostEstimate(flops=1, bytes_accessed=1, transcendentals=0)

NN = (((1,), (0,)), ((), ()))
NT = (((1,), (1,)), ((), ()))
TN = (((0,), (0,)), ((), ()))


def halves(x):
    high = x.astype(jnp.bfloat16)
    return high, (x - high.astype(jnp.float32)).astype(jnp.bfloat16)


def dot32(a, b, dims):
    return lax.dot_general(a, b, dims, preferred_element_type=jnp.float32)


def mul(left, right, dims=NN):
    rows = left[0].shape[0]
    both = dot32(jnp.concatenate(left, axis=0), right[0], dims)
    return both[:rows] + both[rows:] + dot32(left[0], right[1], dims)


def tmul(left, right, masks):
    full = (
        dot32(left[0], right[0], TN) + dot32(left[1], right[0], TN) + dot32(left[0], right[1], TN)
    )
    return sum(full[h * CHUNK : (h + 1) * CHUNK] * masks[h][:1].astype(jnp.float32) for h in range(GROUP_HEADS))


def spread(pair, masks):
    return tuple(
        jnp.concatenate([part * masks[h] for h in range(GROUP_HEADS)], axis=0) for part in pair
    )


def stack(first, second):
    return tuple(jnp.concatenate([x, y], axis=0) for x, y in zip(first, second))


def head_masks():
    lane = lax.broadcasted_iota(jnp.int32, (CHUNK, LANES), 1) // CHUNK
    return [(lane == h).astype(jnp.float32).astype(jnp.bfloat16) for h in range(GROUP_HEADS)]


def places():
    row = lax.broadcasted_iota(jnp.int32, (CHUNK, LANES), 0)
    col = lax.broadcasted_iota(jnp.int32, (CHUNK, LANES), 1) % CHUNK
    return row, col


def running_sum(x, upper=False):
    row = lax.broadcasted_iota(jnp.int32, (CHUNK, CHUNK), 0)
    col = lax.broadcasted_iota(jnp.int32, (CHUNK, CHUNK), 1)
    ones = (row <= col if upper else col <= row).astype(jnp.float32).astype(jnp.bfloat16)
    high, rest = halves(x)
    low = (x - high.astype(jnp.float32) - rest.astype(jnp.float32)).astype(jnp.bfloat16)
    return dot32(ones, high, NN) + dot32(ones, rest, NN) + dot32(ones, low, NN)


def scaled_forms(q, w, k, a, b):
    total = running_sum(w)
    before = total - w
    middle = total[CHUNK // 2 - 1 : CHUNK // 2]
    end = total[CHUNK - 1 :]
    ea = jnp.exp(before - middle)
    eq = jnp.exp(total - middle)
    eb = jnp.exp(middle - total)
    ee = jnp.exp(end - total)
    return (a * ea, q * eq, b * eb, k * eb, b * ee, k * ee), (ea, eq, eb, ee), (jnp.exp(middle), jnp.exp(end))


def each(fn, *columns):
    return [fn(*row) for row in zip(*columns)]


def block_ones():
    row = lax.broadcasted_iota(jnp.int32, (LANES, LANES), 0) // CHUNK
    col = lax.broadcasted_iota(jnp.int32, (LANES, LANES), 1) // CHUNK
    return (row == col).astype(jnp.float32).astype(jnp.bfloat16)


def head_sum(x, ones):
    rows = x.shape[0]
    both = dot32(jnp.concatenate(halves(x), axis=0), ones, NN)
    return both[:rows] + both[rows:]


def prepared(keys, decay_low, rate_low, live, vec, ones):
    sig = jax.nn.sigmoid(vec[0] + decay_low)
    log_decay = (-0.6065306597126334) * sig * live
    rates = jax.nn.sigmoid(vec[1] + rate_low)
    scaled = keys * vec[2]
    inverse = lax.rsqrt(head_sum(scaled * scaled, ones) + 1e-06)
    unit_keys = scaled * inverse
    factor = (1.0 + (rates - 1.0) * vec[3]) * live
    return log_decay, keys * factor, -unit_keys, unit_keys * rates * live, sig, rates, inverse, factor


def read_out(o, q, k, v, vec, ones):
    centred = o - head_sum(o, ones) * (1.0 / CHUNK)
    scale = lax.rsqrt(head_sum(centred * centred, ones) * (1.0 / CHUNK) + 0.00064)
    normed = centred * scale
    weight = head_sum(q * k * vec[4], ones)
    return normed, scale, weight, normed * vec[5] + vec[6] + weight * v


def unit_slices():
    return [
        (slice(c * CHUNK, (c + 1) * CHUNK), slice(g * LANES, (g + 1) * LANES))
        for c in range(STEP_CHUNKS)
        for g in range(2)
    ]


def unit_live(length, step):
    row = lax.broadcasted_iota(jnp.int32, (CHUNK, LANES), 0)
    start = step * (STEP_CHUNKS * CHUNK)
    live = [(row + (start + c * CHUNK) < length).astype(jnp.float32) for c in range(STEP_CHUNKS)]
    return [live[c] for c in range(STEP_CHUNKS) for g in range(2)]


def unit_vectors(vec_ref):
    vec = [[vec_ref[i : i + 1, g * LANES : (g + 1) * LANES] for i in range(7)] for g in range(2)]
    return [vec[g] for c in range(STEP_CHUNKS) for g in range(2)]


def forward_kernel(base, *refs):
    len_ref, vec_ref, start_ref, q_ref, keys_ref, v_ref, dl_ref, rl_ref, gate_ref = refs[:9]
    (
        out_ref, o_ref, t_ref, aqb_ref, aak_ref, aqk_ref, y_ref, z_ref, trt_ref, qe_ref, state_ref,
    ) = refs[-11:]

    @pl.when(pl.program_id(0) == 0)
    def _():
        state_ref[...] = start_ref[...]

    masks = head_masks()
    row, col = places()
    strict = (col < row).astype(jnp.float32)
    within = (col <= row).astype(jnp.float32)
    eye = (col == row).astype(jnp.float32)
    ones = block_ones()
    units = unit_slices()
    live = unit_live(len_ref[0], pl.program_id(0) + base)
    vec = unit_vectors(vec_ref)
    load = lambda ref: [ref[u] for u in units]
    q, keys, v = load(q_ref), load(keys_ref), load(v_ref)
    ready = each(
        lambda x, y, z, m, n: prepared(x, y, z, m, n, ones), keys, load(dl_ref), load(rl_ref), live, vec
    )
    w, k, a, b = ([x[i] for x in ready] for i in range(4))
    forms = each(scaled_forms, q, w, k, a, b)
    ah, qh, bh, kh, bt, kt = ([f[0][i] for f in forms] for i in range(6))
    emid = [f[2][0] for f in forms]
    eend = [f[2][1] for f in forms]
    aq = each(lambda x, y: halves(jnp.concatenate([x, y], axis=0)), ah, qh)
    with_b = each(lambda l, r: mul(l, spread(halves(r), masks), NT), aq, bh)
    with_k = each(lambda l, r: mul(l, spread(halves(r), masks), NT), aq, kh)
    aab = [x[:CHUNK] * strict for x in with_b]
    aqb = [halves(x[CHUNK:] * within) for x in with_b]
    aak = [halves(x[:CHUNK] * strict) for x in with_k]
    aqk = [halves(x[CHUNK:] * within) for x in with_k]
    p = [halves(x * (row // 8 == col // 8)) for x in aab]
    t = [eye + x * (row // 8 == col // 8) for x in aab]
    p2 = each(lambda x: halves(mul(x, spread(x, masks))), p)
    both = each(lambda x, y: mul(stack(x, halves(y)), spread(x, masks)), p2, t)
    p4 = [halves(x[:CHUNK]) for x in both]
    t = each(lambda x, y: x + y[CHUNK:], t, both)
    t = each(lambda x, y: x + mul(halves(x), spread(y, masks)), t, p4)
    for size in (8, 16, 32):
        corner = ((row // size) % 2 == 1) & (col // size == row // size - 1)
        ts = [halves(x) for x in t]
        n = [halves(x * corner) for x in aab]
        tn = each(lambda x, y: halves(mul(x, spread(y, masks))), ts, n)
        t = each(lambda x, y, z: x + mul(y, spread(z, masks)), t, tn, ts)
    ts = [halves(x) for x in t]
    vs = [halves(x) for x in v]
    vm = [spread(x, masks) for x in vs]
    wide = each(lambda x, y, e: mul(x, spread(halves(y * e), masks)), ts, ah, emid)
    r0 = each(mul, aak, vm)
    y0 = each(lambda x, y: mul(x, spread(halves(y), masks)), ts, r0)
    wides = [halves(x) for x in wide]
    qe = each(lambda x, e, y, z: x * e + mul(y, spread(z, masks)), qh, emid, aqb, wides)
    y0s = [halves(x) for x in y0]
    part = each(lambda x, y, z, u: mul(x, spread(y, masks)) + mul(z, u), aqb, y0s, aqk, vm)
    bts = [halves(x) for x in bt]
    diag = [eye * e for e in eend]
    tr = each(lambda x, y, d: tmul(x, y, masks) + d, bts, wides, diag)
    trt = each(lambda x, y, d: tmul(y, x, masks) + d, bts, wides, diag)
    inject = each(lambda x, y, z, u: tmul(stack(x, halves(y)), stack(z, u), masks), bts, kt, y0s, vs)
    wq = each(lambda x, y: stack(x, halves(y)), wides, qe)
    z = []
    out = []
    for c in range(STEP_CHUNKS):
        for g in range(2):
            i = c * 2 + g
            now = state_ref[g]
            nows = spread(halves(now), masks)
            state_ref[g] = mul(halves(tr[i]), nows) + inject[i]
            z.append(now)
            out.append(mul(wq[i], nows))
    o = each(lambda x, y: x[CHUNK:] + y, out, part)
    mixed = each(lambda x, y, z, m, n: read_out(x, y, z, m, n, ones)[3], o, q, k, v, vec)
    for i, u in enumerate(units):
        out_ref[u] = (mixed[i] * gate_ref[u]).astype(jnp.bfloat16)
        o_ref[u] = o[i]
        y_ref[u] = out[i][:CHUNK] + y0[i]
        t_ref[u] = t[i]
        aqb_ref[u] = with_b[i][CHUNK:] * within
        aak_ref[u] = with_k[i][:CHUNK] * strict
        aqk_ref[u] = with_k[i][CHUNK:] * within
        z_ref[u] = z[i]
        trt_ref[u] = trt[i]
        qe_ref[u] = qe[i]


def backward_kernel(base, *refs):
    (
        len_ref, vec_ref, start_ref, sums_ref, q_ref, keys_ref, v_ref, dl_ref, rl_ref, gate_ref,
        g_ref, o_ref, t_ref, aqb_ref, aak_ref, aqk_ref, y_ref, z_ref, trt_ref, qe_ref,
    ) = refs[:20]
    dq_ref, dkeys_ref, dv_ref, ddl_ref, drl_ref, dgate_ref, dvec_ref, state_ref = refs[-8:]
    step = base + pl.num_programs(0) - 1 - pl.program_id(0)

    @pl.when(pl.program_id(0) == 0)
    def _():
        state_ref[...] = start_ref[...]
        dvec_ref[...] = sums_ref[...]

    masks = head_masks()
    row, col = places()
    strict = (col < row).astype(jnp.float32)
    within = (col <= row).astype(jnp.float32)
    ones = block_ones()
    units = unit_slices()
    live = unit_live(len_ref[0], step)
    vec = unit_vectors(vec_ref)
    load = lambda ref: [ref[u] for u in units]
    q, keys, v, g = load(q_ref), load(keys_ref), load(v_ref), load(g_ref)
    ready = each(
        lambda x, y, z, m, n: prepared(x, y, z, m, n, ones), keys, load(dl_ref), load(rl_ref), live, vec
    )
    w, k, a, b, sig, rates, inverse, factor = ([x[i] for x in ready] for i in range(8))
    seen = each(lambda x, y, z, m, n: read_out(x, y, z, m, n, ones), load(o_ref), q, k, v, vec)
    normed, scale, weight, mixed = ([x[i] for x in seen] for i in range(4))
    gate = load(gate_ref)
    dgate = each(lambda x, y: x * y, g, mixed)
    dmix = each(lambda x, y: x * y, g, gate)
    dn = each(lambda x, n: x * n[5], dmix, vec)
    do = each(
        lambda x, n, r: r
        * (x - head_sum(x, ones) * (1.0 / CHUNK) - n * (head_sum(x * n, ones) * (1.0 / CHUNK))),
        dn, normed, scale,
    )
    dweight = each(lambda x, y: head_sum(x * y, ones), dmix, v)
    do = [halves(x) for x in do]
    qe, trt, t, aqb, aak, aqk, ys = (
        [halves(x) for x in load(ref)]
        for ref in (qe_ref, trt_ref, t_ref, aqb_ref, aak_ref, aqk_ref, y_ref)
    )
    z = load(z_ref)
    vs = [halves(x) for x in v]
    h = each(lambda x, y: tmul(x, y, masks), qe, do)
    dz = [None] * len(units)
    for c in reversed(range(STEP_CHUNKS)):
        for g in range(2):
            i = c * 2 + g
            now = state_ref[g]
            dz[i] = now
            state_ref[g] = mul(trt[i], spread(halves(now), masks)) + h[i]
    dzs = [spread(halves(x), masks) for x in dz]
    zs = [spread(halves(x), masks) for x in z]
    forms = each(scaled_forms, q, w, k, a, b)
    ah, qh, bh, kh, bt, kt = ([f[0][i] for f in forms] for i in range(6))
    ea, eq, eb, ee = ([f[1][i] for f in forms] for i in range(4))
    emid = [f[2][0] for f in forms]
    eend = [f[2][1] for f in forms]
    from_end = each(lambda x, y, s: mul(halves(jnp.concatenate([x, y], axis=0)), s), bt, kt, dzs)
    dy = each(lambda x, y, s: halves(tmul(x, y, masks) + s[:CHUNK]), aqb, do, from_end)
    dr = each(lambda x, y: halves(tmul(x, y, masks)), t, dy)
    ro = each(stack, dr, do)
    dv = each(lambda x, y, s, f: tmul(stack(x, y), s, masks) + f[CHUNK:], aak, aqk, ro, from_end)
    mask2 = jnp.concatenate([strict, within], axis=0)
    dab = each(lambda s, y: halves(mul(s, spread(y, masks), NT) * mask2), ro, ys)
    dak = each(lambda s, y: halves(mul(s, spread(y, masks), NT) * mask2), ro, vs)
    dst = each(lambda s, y: mul(s, y, NT), ro, zs)
    daq = each(
        lambda s, e, x, bb, y, kk: s * e + mul(x, spread(halves(bb), masks)) + mul(y, spread(halves(kk), masks)),
        dst, emid, dab, bh, dak, kh,
    )
    aq = each(lambda x, y: halves(jnp.concatenate([x, y], axis=0)), ah, qh)
    dbh = each(lambda x, y: tmul(x, y, masks), dab, aq)
    dkh = each(lambda x, y: tmul(x, y, masks), dak, aq)
    dend = each(lambda y, x, s: mul(stack(y, x), s, NT), ys, vs, dzs)
    row_of_ones = jnp.ones((8, LANES), jnp.bfloat16)
    sums = lambda x: jnp.sum(x, axis=0, keepdims=True)
    for i, u in enumerate(units):
        da = daq[i][:CHUNK] * ea[i]
        dq = daq[i][CHUNK:] * eq[i]
        dbt = dend[i][:CHUNK] * ee[i]
        dkt = dend[i][CHUNK:] * ee[i]
        db = dbh[i] * eb[i] + dbt
        dk = dkh[i] * eb[i] + dkt
        pa = da * a[i]
        diff = dq * q[i] - db * b[i] - dk * k[i] + pa
        zz = spread(halves(z[i] * dz[i]), masks)
        carry = (dot32(row_of_ones, zz[0], NT) + dot32(row_of_ones, zz[1], NT))[:1] * eend[i]
        carry = carry + sums(dbt * b[i] + dkt * k[i])
        dw = running_sum(diff, upper=True) - pa + carry
        from_bonus = dweight[i] * vec[i][4]
        dk = dk + from_bonus * q[i]
        dq_ref[u] = (dq + from_bonus * k[i]).astype(jnp.bfloat16)
        dv_ref[u] = (dv[i] + weight[i] * dmix[i]).astype(jnp.bfloat16)
        dgate_ref[u] = dgate[i].astype(jnp.bfloat16)
        unit_keys = -a[i]
        db = db * live[i]
        du = db * rates[i] - da
        dscaled = inverse[i] * (du - unit_keys * head_sum(du * unit_keys, ones))
        dkl = dk * keys[i] * live[i]
        drl = (db * unit_keys + dkl * vec[i][3]) * rates[i] * (1.0 - rates[i])
        ddl = dw * w[i] * (1.0 - sig[i])
        dkeys_ref[u] = (dk * factor[i] + dscaled * vec[i][2]).astype(jnp.bfloat16)
        ddl_ref[u] = ddl.astype(jnp.bfloat16)
        drl_ref[u] = drl.astype(jnp.bfloat16)
        parts = (
            ddl, drl, dscaled * keys[i], dkl * (rates[i] - 1.0),
            dweight[i] * q[i] * k[i], dmix[i] * normed[i], dmix[i],
        )
        lanes = u[1]
        for j, x in enumerate(parts):
            dvec_ref[j : j + 1, lanes] += sums(x)


def wkv_call(kernel, base, steps, small, arrays, outs, sums, previous, name):
    tokens, width = arrays[0].shape
    rows = CHUNK * STEP_CHUNKS
    last = base + steps - 1
    turned = kernel is backward_kernel
    spec = pl.BlockSpec((rows, width), lambda i: (last - i if turned else base + i, 0))
    state = pl.BlockSpec((2, CHUNK, LANES), lambda i: (0, 0, 0))
    whole = pl.BlockSpec((8, width), lambda i: (0, 0))
    shape = jax.ShapeDtypeStruct
    first = [pl.BlockSpec(memory_space=pltpu.SMEM), whole, state] + [whole] * sums
    held = list(previous or ())
    start = len(first) + len(arrays)
    return pl.pallas_call(
        partial(kernel, base),
        grid=(steps,),
        in_specs=first + [spec] * len(arrays) + [pl.BlockSpec(memory_space=pl.ANY)] * len(held),
        out_specs=[spec] * len(outs) + [whole] * sums + [state],
        out_shape=[shape((tokens, width), dtype) for dtype in outs]
        + [shape((8, width), jnp.float32)] * sums
        + [shape((2, CHUNK, LANES), jnp.float32)],
        input_output_aliases={start + i: i for i in range(len(held))},
        compiler_params=pltpu.CompilerParams(vmem_limit_bytes=60 << 20),
        cost_estimate=SMALL,
        name=name,
    )(*small, *arrays, *held)


def wkv_forward(base, steps, length, vec, state, arrays, previous=None):
    outs = [jnp.bfloat16] + [jnp.float32] * 9
    return wkv_call(
        forward_kernel, base, steps, (length, vec, state), arrays, outs, 0, previous, "wkv_forward"
    )


def wkv_backward(base, steps, length, vec, state, sums, arrays, previous=None):
    outs = [jnp.bfloat16] * 6
    return wkv_call(
        backward_kernel, base, steps, (length, vec, state, sums), arrays, outs, 1, previous,
        "wkv_backward",
    )


ROWS = 128


def row_norm(x):
    centred = x - jnp.mean(x, axis=-1, keepdims=True)
    scale = lax.rsqrt(jnp.mean(centred * centred, axis=-1, keepdims=True) + 1e-05)
    return centred * scale, scale


def shifted(x, edge, down):
    rows = x.shape[0]
    row = lax.broadcasted_iota(jnp.int32, x.shape, 0)
    if down:
        return jnp.where(row == 0, edge, pltpu.roll(x, 1, 0))
    return jnp.where(row == rows - 1, edge, pltpu.roll(x, rows - 1, 0))


def below(x, upper):
    lane = lax.broadcasted_iota(jnp.int32, x.shape, 1)
    keep = (lane >= DECAY_RANK) if upper else (lane < DECAY_RANK)
    return jnp.where(keep, x, jnp.zeros_like(x))


def front_kernel(
    x_ref, vec_ref, wr_ref, wk_ref, wv_ref, down_ref, up_ref,
    m0_ref, m1_ref, m2_ref, m3_ref, m4_ref, m5_ref,
    q_ref, k_ref, v_ref, dl_ref, rl_ref, gate_ref, hid_ref,
    edge_ref,
):
    @pl.when(pl.program_id(0) == 0)
    def _():
        edge_ref[...] = jnp.zeros_like(edge_ref)

    unit, _ = row_norm(x_ref[...].astype(jnp.float32))
    normed = unit * vec_ref[12:13] + vec_ref[13:14]
    change = shifted(normed, edge_ref[:1], True) - normed
    edge_ref[:1] = normed[ROWS - 1 :]
    mixes = []
    for j, ref in enumerate((m0_ref, m1_ref, m2_ref, m3_ref, m4_ref, m5_ref)):
        mixes.append((normed + change * vec_ref[j : j + 1]).astype(jnp.bfloat16))
        ref[...] = mixes[j]
    q_ref[...] = dot32(mixes[0], wr_ref[...], NN)
    k_ref[...] = dot32(mixes[2], wk_ref[...], NN)
    v_ref[...] = dot32(mixes[3], wv_ref[...], NN)
    first = down_ref[:, :128]
    pre_decay, pre_rate = dot32(mixes[1], first, NN), dot32(mixes[4], first, NN)
    pre_gate = dot32(mixes[5], down_ref[:, 128:], NN)
    lane = lax.broadcasted_iota(jnp.int32, pre_decay.shape, 1)
    pair = jnp.where(lane < DECAY_RANK, jnp.tanh(pre_decay), pre_rate)
    gate = jax.nn.sigmoid(pre_gate)
    hid_ref[:, :128] = pair
    hid_ref[:, 128:] = gate
    narrow_pair = pair.astype(jnp.bfloat16)
    dl_ref[...] = dot32(below(narrow_pair, False), up_ref[:, :128], NT)
    rl_ref[...] = dot32(below(narrow_pair, True), up_ref[:, :128], NT)
    gate_ref[...] = dot32(gate.astype(jnp.bfloat16), up_ref[:, 128:], NT)


def front_forward(x, vectors, w_r, w_k, w_v, down, up):
    tokens, width = x.shape
    wide = pl.BlockSpec((ROWS, width), lambda i: (i, 0))
    own = pl.BlockSpec((ROWS, OWN), lambda i: (i, 0))
    hid = pl.BlockSpec((ROWS, 256), lambda i: (i, 0))
    whole = lambda a: pl.BlockSpec(a.shape, lambda i: (0, 0))
    shape = jax.ShapeDtypeStruct
    return pl.pallas_call(
        front_kernel,
        grid=(tokens // ROWS,),
        in_specs=[wide] + [whole(a) for a in (vectors, w_r, w_k, w_v, down, up)],
        out_specs=[wide] * 6 + [own] * 6 + [hid],
        out_shape=[shape((tokens, width), jnp.bfloat16)] * 6
        + [shape((tokens, OWN), jnp.float32)] * 6
        + [shape((tokens, 256), jnp.float32)],
        scratch_shapes=[pltpu.VMEM((8, width), jnp.float32)],
        compiler_params=pltpu.CompilerParams(vmem_limit_bytes=60 << 20),
        cost_estimate=SMALL,
        name="front_forward",
    )(x, vectors, w_r, w_k, w_v, down, up)


def front_back_kernel(
    x_ref, before_ref, vec_ref, wr_ref, wk_ref, wv_ref, down_ref, up_ref,
    m1_ref, m4_ref, m5_ref, hid_ref,
    dq_ref, dk_ref, dv_ref, ddl_ref, drl_ref, dgate_ref, own_vec_ref, ffn_vec_ref,
    dx_ref, mine_ref, other_ref,
    edge_ref, sums_ref, misc_ref,
):
    step = pl.num_programs(0) - 1 - pl.program_id(0)
    core = lax.axis_index("dp") % 2
    own_start = pl.multiple_of(core * OWN, OWN)

    @pl.when(pl.program_id(0) == 0)
    def _():
        edge_ref[...] = jnp.zeros_like(edge_ref)
        sums_ref[...] = jnp.zeros_like(sums_ref)
        misc_ref[...] = jnp.zeros_like(misc_ref)

    unit, scale = row_norm(x_ref[...].astype(jnp.float32))
    gain, offset = vec_ref[12:13], vec_ref[13:14]
    normed = unit * gain + offset
    tail, _ = row_norm(before_ref[...].astype(jnp.float32))
    edge = (tail[15:] * gain + offset) * jnp.where(step == 0, 0.0, 1.0)
    change = shifted(normed, edge, True) - normed
    ddl, drl, dgate = ddl_ref[...], drl_ref[...], dgate_ref[...]
    hid = hid_ref[...]
    pair, gate = hid[:, :128], hid[:, 128:]
    lane = lax.broadcasted_iota(jnp.int32, pair.shape, 1)
    first_up, last_up = up_ref[:, :128], up_ref[:, 128:]
    pair_grad = jnp.where(
        lane < DECAY_RANK,
        dot32(ddl, first_up, NN) * (1.0 - pair * pair),
        dot32(drl, first_up, NN),
    ).astype(jnp.bfloat16)
    gate_grad = (dot32(dgate, last_up, NN) * gate * (1.0 - gate)).astype(jnp.bfloat16)
    narrow_pair, narrow_gate = pair.astype(jnp.bfloat16), gate.astype(jnp.bfloat16)
    own_rows = pl.ds(own_start, OWN)
    misc_ref[own_rows, 256:384] += dot32(ddl, below(narrow_pair, False), TN) + dot32(
        drl, below(narrow_pair, True), TN
    )
    misc_ref[own_rows, 384:512] += dot32(dgate, narrow_gate, TN)
    decay_part, rate_part = below(pair_grad, False), below(pair_grad, True)
    misc_ref[:, :128] += dot32(m1_ref[...], decay_part, TN) + dot32(m4_ref[...], rate_part, TN)
    misc_ref[:, 128:256] += dot32(m5_ref[...], gate_grad, TN)
    first_down = down_ref[:, :128]
    grads = (
        lambda: dot32(dq_ref[...], wr_ref[...], NT),
        lambda: dot32(decay_part, first_down, NT),
        lambda: dot32(dk_ref[...], wk_ref[...], NT),
        lambda: dot32(dv_ref[...], wv_ref[...], NT),
        lambda: dot32(rate_part, first_down, NT),
        lambda: dot32(gate_grad, down_ref[:, 128:], NT),
    )
    total = jnp.zeros_like(change)
    moved = jnp.zeros_like(change)
    for j, grad in enumerate(grads):
        now = grad()
        total = total + now
        moved = moved + now * vec_ref[j : j + 1]
        sums_ref[j : j + 1] += jnp.sum(now * change, axis=0, keepdims=True)
    dnormed = total - moved + shifted(moved, edge_ref[:1], False)
    edge_ref[:1] = moved[:1]
    sums_ref[12:13] += jnp.sum(dnormed * unit, axis=0, keepdims=True)
    sums_ref[13:14] += jnp.sum(dnormed, axis=0, keepdims=True)
    dunit = dnormed * gain
    dx_ref[...] = scale * (
        dunit
        - jnp.mean(dunit, axis=-1, keepdims=True)
        - unit * jnp.mean(dunit * unit, axis=-1, keepdims=True)
    )

    @pl.when(step == 0)
    def _():
        sums_ref[6:7] = ffn_vec_ref[0:1] * 0.5
        sums_ref[14:16] = ffn_vec_ref[1:3] * 0.5
        zeros = jnp.zeros((1, OWN), jnp.float32)
        for target, source in ((7, 0), (8, 1), (9, 2), (10, 3), (11, 4), (16, 5), (17, 6)):
            mine = own_vec_ref[source : source + 1]
            sums_ref[target : target + 1] = jnp.concatenate(
                [jnp.where(core == 0, mine, zeros), jnp.where(core == 0, zeros, mine)], axis=1
            )
        for block in range(EMBED // 128):
            lanes = slice(block * 128, (block + 1) * 128)
            misc_ref[lanes, 512:640] = sums_ref[:, lanes].T
        share = mine_ref.shape[1]
        for chip in range(mine_ref.shape[0]):
            low = misc_ref[2 * chip * share : (2 * chip + 1) * share]
            high = misc_ref[(2 * chip + 1) * share : (2 * chip + 2) * share]
            mine_ref[chip] = jnp.where(core == 0, low, high)
            other_ref[chip] = jnp.where(core == 0, high, low).astype(jnp.bfloat16)


def front_backward(
    x, vectors, w_r, w_k, w_v, down, up, mixes, hid, grads, own_vec, ffn_vec
):
    tokens, width = x.shape
    devices = lax.axis_size("dp")
    pieces = (devices // 2, EMBED // devices, 640)
    steps = tokens // ROWS
    wide = pl.BlockSpec((ROWS, width), lambda i: (steps - 1 - i, 0))
    before = pl.BlockSpec(
        (16, width), lambda i: (jnp.maximum((steps - 1 - i) * (ROWS // 16) - 1, 0), 0)
    )
    own = pl.BlockSpec((ROWS, OWN), lambda i: (steps - 1 - i, 0))
    hid_spec = pl.BlockSpec((ROWS, 256), lambda i: (steps - 1 - i, 0))
    whole = lambda a: pl.BlockSpec(a.shape, lambda i: (0, 0))
    shape = jax.ShapeDtypeStruct
    return pl.pallas_call(
        front_back_kernel,
        grid=(steps,),
        in_specs=[wide, before]
        + [whole(a) for a in (vectors, w_r, w_k, w_v, down, up)]
        + [wide] * 3
        + [hid_spec]
        + [own] * 6
        + [whole(own_vec), whole(ffn_vec)],
        out_specs=[wide] + [pl.BlockSpec(pieces, lambda i: (0, 0, 0))] * 2,
        out_shape=[
            shape((tokens, width), jnp.float32),
            shape(pieces, jnp.float32),
            shape(pieces, jnp.bfloat16),
        ],
        scratch_shapes=[
            pltpu.VMEM((8, width), jnp.float32),
            pltpu.VMEM((128, width), jnp.float32),
            pltpu.VMEM((EMBED, 640), jnp.float32),
        ],
        compiler_params=pltpu.CompilerParams(vmem_limit_bytes=60 << 20),
        cost_estimate=SMALL,
        name="front_backward",
    )(x, x, vectors, w_r, w_k, w_v, down, up, *mixes, hid, *grads, own_vec, ffn_vec)


def ffn_back_kernel(
    len_ref, res_ref, before_ref, cot_ref, mine_ref, other_ref, vec_ref, wo_ref,
    grad_ref, narrow_ref, gated_ref, dvec_ref,
    edge_ref,
):
    step = pl.num_programs(0) - 1 - pl.program_id(0)

    @pl.when(pl.program_id(0) == 0)
    def _():
        edge_ref[...] = jnp.zeros_like(edge_ref)
        dvec_ref[...] = jnp.zeros_like(dvec_ref)

    gain, offset, coefficient = vec_ref[14:15], vec_ref[15:16], vec_ref[6:7]
    unit, scale = row_norm(res_ref[...])
    normed = unit * gain + offset
    tail, _ = row_norm(before_ref[...])
    edge = (tail[7:] * gain + offset) * jnp.where(step == 0, 0.0, 1.0)
    change = shifted(normed, edge, True) - normed
    grad = mine_ref[...].astype(jnp.float32) + other_ref[...].astype(jnp.float32)
    moved = grad * coefficient
    dnormed = grad - moved + shifted(moved, edge_ref[:1], False)
    edge_ref[:1] = moved[:1]
    sums = lambda x: jnp.sum(x, axis=0, keepdims=True)
    dvec_ref[0:1] += sums(grad * change)
    dvec_ref[1:2] += sums(dnormed * unit)
    dvec_ref[2:3] += sums(dnormed)
    dunit = dnormed * gain
    row = lax.broadcasted_iota(jnp.int32, grad.shape, 0) + step * ROWS
    out_grad = jnp.where(row < len_ref[0], cot_ref[...].astype(jnp.float32), 0.0)
    total = out_grad + scale * (
        dunit
        - jnp.mean(dunit, axis=-1, keepdims=True)
        - unit * jnp.mean(dunit * unit, axis=-1, keepdims=True)
    )
    grad_ref[...] = total
    small = total.astype(jnp.bfloat16)
    core = lax.axis_index("dp") % 2
    narrow_ref[...] = jnp.where(core == 0, small[:, :OWN], small[:, OWN:])
    gated_ref[...] = dot32(small, wo_ref[...], NT)


def ffn_backward(length, residual, cot, mine, other, vectors, w_o_rows):
    tokens, width = residual.shape
    steps = tokens // ROWS
    wide = pl.BlockSpec((ROWS, width), lambda i: (steps - 1 - i, 0))
    before = pl.BlockSpec(
        (8, width), lambda i: (jnp.maximum((steps - 1 - i) * (ROWS // 8) - 1, 0), 0)
    )
    own = pl.BlockSpec((ROWS, OWN), lambda i: (steps - 1 - i, 0))
    whole = lambda a: pl.BlockSpec(a.shape, lambda i: (0, 0))
    shape = jax.ShapeDtypeStruct
    return pl.pallas_call(
        ffn_back_kernel,
        grid=(steps,),
        in_specs=[pl.BlockSpec(memory_space=pltpu.SMEM), wide, before]
        + [wide] * 3
        + [whole(vectors), whole(w_o_rows)],
        out_specs=[wide, own, own, pl.BlockSpec((8, width), lambda i: (0, 0))],
        out_shape=[
            shape((tokens, width), jnp.float32),
            shape((tokens, OWN), jnp.bfloat16),
            shape((tokens, OWN), jnp.float32),
            shape((8, width), jnp.float32),
        ],
        scratch_shapes=[pltpu.VMEM((8, width), jnp.float32)],
        compiler_params=pltpu.CompilerParams(vmem_limit_bytes=60 << 20),
        cost_estimate=SMALL,
        name="ffn_backward",
    )(length, residual, residual, cot, mine, other, vectors, w_o_rows)


def att_grad_kernel(m0_ref, m2_ref, m3_ref, gated_ref, dq_ref, dk_ref, dv_ref, do_ref,
                    send_a, keep_a, send_b, keep_b):
    chip = lax.axis_index("dp") // 2
    by_x, by_y = chip % 2 == 0, (chip // 2) % 2 == 0
    first = ((m0_ref, dq_ref), (gated_ref, do_ref))
    second = ((m2_ref, dk_ref), (m3_ref, dv_ref))
    for half in range(2):
        lanes = slice(half * OWN, (half + 1) * OWN)
        block = dot32(first[half][0][...], first[half][1][...], TN).astype(jnp.bfloat16)
        for y in range(2):
            low, high = block[y * 128 : y * 128 + 64], block[y * 128 + 64 : y * 128 + 128]
            send_a[y, :, lanes] = jnp.where(by_x, high, low)
            keep_a[y, :, lanes] = jnp.where(by_x, low, high)
        block = dot32(second[half][0][...], second[half][1][...], TN).astype(jnp.bfloat16)
        for x in range(2):
            low, high = block[x * 64 : x * 64 + 64], block[128 + x * 64 : 128 + x * 64 + 64]
            send_b[x, :, lanes] = jnp.where(by_y, high, low)
            keep_b[x, :, lanes] = jnp.where(by_y, low, high)


def att_gradients(mixes, gated, grads, own_grad):
    tokens = gated.shape[0]
    left = pl.BlockSpec((tokens, 256), lambda i: (0, i))
    right = pl.BlockSpec((tokens, OWN), lambda i: (0, 0))
    out = pl.BlockSpec((2, 64, 2 * OWN), lambda i: (i, 0, 0))
    return pl.pallas_call(
        att_grad_kernel,
        grid=(4,),
        in_specs=[left] * 4 + [right] * 4,
        out_specs=[out] * 4,
        out_shape=[jax.ShapeDtypeStruct((8, 64, 2 * OWN), jnp.bfloat16)] * 4,
        compiler_params=pltpu.CompilerParams(vmem_limit_bytes=60 << 20),
        cost_estimate=SMALL,
        name="att_gradients",
    )(*mixes, gated, *grads, own_grad)


def swap(block, mask):
    size = lax.axis_size("dp")
    return lax.ppermute(block, "dp", [(i, i ^ mask) for i in range(size)])


def bit_of(mask):
    return (lax.axis_index("dp") // mask) % 2


def in_order(mask, own, other, axis):
    lower = bit_of(mask) == 0
    return jnp.where(
        lower, jnp.concatenate([own, other], axis=axis), jnp.concatenate([other, own], axis=axis)
    )


def chip_masks():
    size = lax.axis_size("dp")
    masks = []
    while 2 << len(masks) < size:
        masks.append(2 << len(masks))
    return masks


def steps_of(kind):
    masks = chip_masks()
    near, far = [[mask] for mask in masks[:2]], [[mask] for mask in masks[2:][::-1]]
    first = [[far[0][0], far[1][0], far[0][0] | far[1][0]]] if len(far) == 2 else far
    return [first + near[::-1], first + near, far + near[::-1], far + near, near + far][kind]


class Held:
    def __init__(self, value):
        self.value = value


def meet(movers, *arrays):
    held = []
    for mover in movers:
        held += [x[0] for x in mover.arrived if x[0] not in held]
    out = lax.optimization_barrier(tuple(x.value for x in held) + arrays)
    for x, value in zip(held, out):
        x.value = value
    return out[len(held) :]


def read(arrived):
    return [x.value if lanes is None else x.value[..., lanes] for x, lanes in arrived]


class Gather:
    def __init__(self, block, kind, places=(0,)):
        self.steps = steps_of(kind)
        self.held = block[None]
        self.places = [0]
        self.arrived = []
        self.masks = []

    def merge(self):
        if self.arrived:
            self.held = jnp.concatenate([self.held] + read(self.arrived), axis=0)
            self.places = self.places + [p ^ (m // 2) for m in self.masks for p in self.places]
            self.arrived = []

    def step(self):
        if self.steps:
            self.merge()
            self.masks = self.steps.pop(0)
            self.arrived = [(Held(swap(self.held, mask)), None) for mask in self.masks]
        return self

    def run(self):
        while self.steps:
            self.step()
        return self

    def split(self, kinds):
        width = self.held.shape[-1] // len(kinds)
        out = []
        for i, kind in enumerate(kinds):
            part = Gather.__new__(Gather)
            cut = slice(i * width, (i + 1) * width)
            part.steps = steps_of(kind)[len(steps_of(kind)) - len(self.steps) :]
            part.held = self.held[..., cut]
            part.arrived = [(x, cut) for x, _ in self.arrived]
            part.places, part.masks = self.places, self.masks
            out.append(part)
        return out


def place_kernel(places, cuts, *refs):
    sources, outs = refs[: len(places)], refs[len(places) :]
    chip = lax.axis_index("dp") // 2
    for source, (part, list_of) in zip(sources, places):
        for j, place in enumerate(list_of):
            for out, (first, rows, lanes) in zip(outs, cuts):
                start = pl.multiple_of((chip ^ place) * rows, rows)
                lane, width = lanes[part]
                at = sum(w for _, w in lanes[:part])
                out[pl.ds(start, rows), at : at + width] = source[
                    j, first : first + rows, lane : lane + width
                ]


def assemble(gathers, cuts=None):
    gathers = [g.run() for g in gathers]
    rows = gathers[0].held.shape[1]
    cuts = cuts or ((0, rows, [(0, g.held.shape[2]) for g in gathers]),)
    sources, places = [], []
    for i, g in enumerate(gathers):
        sources += [g.held] + read(g.arrived)
        shifts = [0] + [mask // 2 for mask in g.masks]
        places += [(i, [p ^ shift for p in g.places]) for shift in shifts]
    count = lax.axis_size("dp") // 2
    if any(cut[1] % 16 for cut in cuts):
        return assemble_plain(sources, places, cuts, count)
    space = pl.BlockSpec(memory_space=pltpu.VMEM)
    return pl.pallas_call(
        partial(place_kernel, places, cuts),
        in_specs=[space] * len(sources),
        out_specs=[space] * len(cuts),
        out_shape=[
            jax.ShapeDtypeStruct((count * n, sum(w for _, w in lanes)), sources[0].dtype)
            for _, n, lanes in cuts
        ],
        compiler_params=pltpu.CompilerParams(vmem_limit_bytes=32 << 20),
        cost_estimate=SMALL,
        name="assemble",
    )(*sources)


def assemble_plain(sources, places, cuts, count):
    chip = lax.axis_index("dp") // 2
    parts = []
    for part in sorted({part for part, _ in places}):
        blocks = jnp.concatenate([x for x, (at, _) in zip(sources, places) if at == part])
        where = [p for at, list_of in places if at == part for p in list_of]
        blocks = jnp.stack([blocks[where.index(i)] for i in range(count)])
        parts.append(jnp.take(blocks, chip ^ lax.iota(jnp.int32, count), axis=0))
    return [
        jnp.concatenate(
            [x[:, first : first + n, at : at + w] for x, (at, w) in zip(parts, lanes)], axis=-1
        ).reshape(count * n, -1)
        for first, n, lanes in cuts
    ]


class Scatter:
    def __init__(self, parts, kind):
        self.steps = steps_of(kind)[::-1]
        self.axes = chip_masks()[::-1]
        self.sources = [parts.reshape((2,) * len(self.axes) + parts.shape[1:])]
        self.arrived = []
        self.sent = None

    @classmethod
    def begun(cls, sent, kept, kind):
        out = cls.__new__(cls)
        out.steps = steps_of(kind)[::-1]
        out.axes = [axis for axis in chip_masks()[::-1] if axis != out.steps[0][0]]
        out.sources = [kept.reshape((2,) * len(out.axes) + kept.shape[1:])]
        out.arrived = []
        out.sent = [sent.reshape(out.sources[0].shape)]
        return out

    def pick(self, sources, mask, gone):
        out = []
        for x in sources:
            for place in reversed(range(len(self.axes))):
                axis = self.axes[place]
                if axis in gone:
                    which = bit_of(axis) if not mask & axis else 1 - bit_of(axis)
                    x = lax.dynamic_index_in_dim(x, which, place, keepdims=False)
            out.append(x)
        return out

    def prepare(self):
        if self.sent is not None:
            return self
        masks = self.steps[0]
        sources = self.sources + read(self.arrived)
        gone = [axis for axis in self.axes if any(mask & axis for mask in masks)]
        self.sent = [
            sum(x.astype(jnp.float32) for x in self.pick(sources, mask, gone)).astype(jnp.bfloat16)
            for mask in masks
        ]
        self.sources = self.pick(sources, 0, gone)
        self.axes = [axis for axis in self.axes if axis not in gone]
        self.arrived = []
        return self

    def step(self):
        return together([self])[0]

    def run(self):
        while self.steps:
            self.step()
        return self

    def total(self):
        return sum(x.astype(jnp.float32) for x in self.sources + read(self.arrived))


def together(parts):
    if not parts[0].steps:
        return parts
    for part in parts:
        part.prepare()
    for i, mask in enumerate(parts[0].steps[0]):
        sent = [part.sent[i] for part in parts]
        got = Held(swap(sent[0] if len(sent) == 1 else jnp.concatenate(sent, axis=-1), mask))
        at = 0
        for part, x in zip(parts, sent):
            lanes = slice(at, at + x.shape[-1]) if len(sent) > 1 else None
            part.arrived.append((got, lanes))
            at += x.shape[-1]
    for part in parts:
        part.steps.pop(0)
        part.sent = None
    return parts


def norm_rows(features, gain_row, offset_row):
    average = jnp.mean(features, axis=-1, keepdims=True)
    centred = features - average
    variance = jnp.mean(centred * centred, axis=-1, keepdims=True)
    return centred * lax.rsqrt(variance + 1e-05) * gain_row + offset_row


def product(operand, weight_matrix):
    return jnp.dot(operand, weight_matrix, preferred_element_type=jnp.float32)


def input_gradient_rows(upstream_gradient, weight_matrix):
    return lax.dot_general(
        upstream_gradient,
        weight_matrix,
        (((1,), (1,)), ((), ())),
        preferred_element_type=jnp.float32,
    )


def weight_gradient(operand, upstream_gradient):
    return lax.dot_general(
        operand, upstream_gradient, (((0,), (0,)), ((), ())), preferred_element_type=jnp.float32
    )


def earlier(rows):
    return jnp.concatenate([jnp.zeros_like(rows[:1]), rows[:-1]], axis=0)


def ffn_mix(residual, vectors):
    second = norm_rows(residual, vectors[14], vectors[15])
    return second + (earlier(second) - second) * vectors[6]


def narrow(x):
    return x.astype(jnp.bfloat16)


def local(
    inputs,
    lengths,
    attention_projections,
    channel_key_weight,
    channel_value_weight,
    lowrank_down_weight,
    lowrank_up_weight,
    per_feature_parameters,
    cotangent,
):
    devices = lax.axis_size("dp")
    chips = devices // 2
    device = lax.axis_index("dp")
    chip, core = device // 2, device % 2
    row_count = inputs.shape[0]
    slots = 2 * row_count
    share = EMBED // devices
    pair_share = 2 * share
    units = channel_value_weight.shape[0]
    half_units = chips * units

    def own_cut(x, which):
        return lax.dynamic_slice_in_dim(x, which * OWN, OWN, x.ndim - 1)

    def own_rows(x, which):
        return lax.dynamic_slice_in_dim(x, which * row_count, row_count, 0)

    pair_rows = in_order(
        1,
        own_cut(attention_projections, core),
        swap(own_cut(attention_projections, 1 - core), 1),
        1,
    )
    lora = jnp.concatenate([lowrank_down_weight, lowrank_up_weight.T], axis=1)
    vector_rows = jnp.pad(per_feature_parameters.T, ((0, 0), (0, 128 - 18)))
    vector_rows = vector_rows.reshape(share // 4, OWN)
    first_rows = 3 * pair_share
    misc_rows = share + share // 4 + (share // 4) % 16
    block = jnp.concatenate(
        [
            pair_rows[:3].reshape(first_rows, OWN),
            lora,
            jnp.pad(vector_rows, ((0, (share // 4) % 16), (0, 0))),
        ],
        axis=0,
    )
    half = half_units // 2
    quarter = OWN // 2
    first = Gather(block, 0).step()
    w_o_part = Gather(pair_rows[3], 4).step().step()
    key_in, raw, cot, _ = meet([], channel_key_weight, inputs, cotangent, first.held)
    key_cut = key_in.reshape(share, chips, 2, units)

    def key_columns(which):
        return lax.dynamic_index_in_dim(key_cut, which, 2, keepdims=False).reshape(share, half_units)

    key_rows = in_order(1, key_columns(core), swap(key_columns(1 - core), 1), 0)
    tokens = in_order(1, raw, swap(raw, 1), 0)
    cot = in_order(1, cot, swap(cot, 1), 0)
    key_rows, tokens, cot = meet([first, w_o_part], key_rows, tokens, cot)
    first = first.split((0, 1))
    for part in first:
        part.step()
    key_part = Gather(key_rows, 2).step()
    (tokens,) = meet(first, tokens)
    for part in first:
        part.step()
    value_block, *_ = meet([key_part], channel_value_weight, *[part.held for part in first])
    key_part.step()
    value_part = Gather(value_block, 2).step()
    w_o_part.step()
    (tokens,) = meet(first + [key_part, value_part], tokens)
    key_parts = key_part.split((2, 3))
    for part in key_parts:
        part.step()
    w_r, w_k, w_v, misc = assemble(
        first,
        [(i * pair_share, pair_share, [(0, quarter)] * 2) for i in range(3)]
        + [(first_rows, misc_rows, [(0, quarter)] * 2)],
    )
    misc = misc.reshape(chips, 1, misc_rows, OWN)
    misc = in_order(1, misc, swap(misc, 1), 1)
    value_part.step()
    lora = misc[:, :, :share].reshape(EMBED, OWN)
    down, up_t = lora[:, :256], lax.dynamic_slice_in_dim(lora[:, 256:], core * OWN, OWN, 0)
    vectors = misc[:, :, share : share + share // 4].reshape(EMBED, 128)[:, :18].T
    vectors = vectors.astype(jnp.float32)
    own_vectors = own_cut(vectors, core)
    used = jnp.concatenate([own_vectors[7:12], own_vectors[16:18], own_vectors[:1]], axis=0)
    length = lax.dynamic_index_in_dim(lengths, chip, 0)
    live = (lax.iota(jnp.int32, slots) < length)[:, None]

    *mixes, queries, keys, values, decay_low, rate_low, gate_rows, hid = front_forward(
        tokens, vectors, w_r, w_k, w_v, down, up_t
    )
    terms = meet(
        key_parts + [value_part, w_o_part],
        queries, keys, values, decay_low, rate_low, gate_rows,
    )
    value_parts = value_part.split((2, 3))
    for part in key_parts + value_parts:
        part.step()
    w_o_part.step()
    blocks = slots // (CHUNK * STEP_CHUNKS)
    zero_state = jnp.zeros((2, CHUNK, LANES), jnp.float32)
    gated, *saved, _ = wkv_forward(0, blocks, length, used, zero_state, terms)
    gated, cot, tokens = meet(key_parts + value_parts + [w_o_part], gated, cot, tokens)
    for part in value_parts:
        part.step()
    gated, *_ = meet([], gated, *[part.held for part in value_parts])
    gated_all = in_order(1, gated, swap(gated, 1), 1)
    (w_o_own,) = assemble([w_o_part])
    w_o = in_order(1, w_o_own, swap(w_o_own, 1), 1)
    (key_weight,) = assemble(key_parts)
    residual = tokens.astype(jnp.float32) + product(gated_all, w_o)
    ffn_in = narrow(ffn_mix(residual, vectors))
    positive = jax.nn.relu(product(ffn_in, key_weight))
    hidden = narrow(jnp.square(positive))
    out_narrow = jnp.where(live, cot, jnp.zeros_like(cot))
    grad_value = narrow(weight_gradient(hidden, out_narrow)).reshape(chips, units, EMBED)
    w_o_rows = lax.dynamic_slice_in_dim(w_o, core * OWN, OWN, 0)
    hidden, positive, out_narrow, w_o_rows, grad_value = meet(
        value_parts, hidden, positive, out_narrow, w_o_rows, grad_value
    )
    (value_weight,) = assemble(value_parts)

    value_scatter = [
        Scatter(grad_value[..., i * OWN : (i + 1) * OWN], 2 + i).step() for i in range(2)
    ]
    pre_narrow = narrow(2.0 * positive * input_gradient_rows(out_narrow, value_weight))
    ffn_in_grad = narrow(input_gradient_rows(pre_narrow, key_weight))
    other_grad = swap(ffn_in_grad, 1)
    grad_key = narrow(weight_gradient(ffn_in, pre_narrow)).reshape(chips, pair_share, half_units)
    residual_grad, own_grad, gated_grad, ffn_vec = ffn_backward(
        length, residual, cot, ffn_in_grad, other_grad, vectors, w_o_rows
    )
    key_scatter = [
        Scatter(grad_key[:, :, i * half : (i + 1) * half], 2 + i).prepare() for i in range(2)
    ]
    gated_grad, *sent = meet(value_scatter, gated_grad, *[m.sent[0] for m in key_scatter])
    for part, x in zip(key_scatter, sent):
        part.sent = [x]
        part.step()
    for part in value_scatter:
        part.step()
    terms = [*terms, gated_grad, *saved]
    zero_sums = jnp.zeros((8, OWN), jnp.float32)
    *low_grads, own_vec, _ = wkv_backward(
        0, blocks, length, used, zero_state, zero_sums, terms
    )
    *low_grads, own_vec = meet(key_scatter + value_scatter, *low_grads, own_vec)
    if pair_share == 64:
        sent_a, kept_a, sent_b, kept_b = att_gradients(
            (mixes[0], mixes[2], mixes[3]), gated_all, low_grads[:3], own_grad
        )
        att_scatter = [Scatter.begun(sent_a, kept_a, 2), Scatter.begun(sent_b, kept_b, 3)]
    else:
        grads = [weight_gradient(mixes[m], g) for m, g in zip((0, 2, 3), low_grads)]
        grad_o = weight_gradient(gated_all, own_grad)
        att_scatter = [
            Scatter(
                narrow(jnp.concatenate(x, axis=1)).reshape(chips, pair_share, EMBED), 2 + i
            ).prepare()
            for i, x in enumerate(((grads[0], grad_o), (grads[1], grads[2])))
        ]
    own_vec, *sent = meet([], own_vec, *[m.sent[0] for m in att_scatter])
    for part, x in zip(att_scatter, sent):
        part.sent = [x]
        part.step()
    for part in key_scatter:
        part.step()
    together(value_scatter)
    token_part, misc_mine, misc_other = front_backward(
        tokens, vectors, w_r, w_k, w_v, down, up_t, (mixes[1], mixes[4], mixes[5]), hid,
        low_grads, own_vec, ffn_vec,
    )
    token_part, misc_mine, misc_other = meet(
        key_scatter + value_scatter, token_part, misc_mine, misc_other
    )
    misc_sum = misc_mine + swap(misc_other, 1).astype(jnp.float32)
    misc_sum = jnp.concatenate([misc_sum[..., :320], misc_sum[..., 320:]], axis=1)
    misc_scatter = Scatter(misc_sum, 3)
    together(key_scatter)
    together(value_scatter)
    (token_part,) = meet(att_scatter, token_part)
    for part in att_scatter:
        part.step()
    misc_scatter.step()
    token_part, hidden = meet(key_scatter + [misc_scatter], token_part, hidden)
    misc_scatter.step()
    together(key_scatter)
    (token_part,) = meet(att_scatter + [misc_scatter], token_part)
    masks = chip_masks()
    last_parts = att_scatter + [misc_scatter]
    if len(misc_scatter.steps) == 2:
        for part in last_parts:
            part.steps = [[masks[2], masks[3], masks[2] | masks[3]]]
    together(last_parts)
    ffn_part = product(hidden, value_weight)
    input_gradient = (
        own_rows(residual_grad, core)
        + own_rows(token_part, core)
        + swap(own_rows(token_part, 1 - core), 1)
    )
    ffn_out = own_rows(ffn_part, core) + swap(own_rows(ffn_part, 1 - core), 1)
    output = narrow(jnp.where(own_rows(live, core), own_rows(residual, core) + ffn_out, 0.0))
    value_sum = jnp.concatenate(
        [x.run().total() for x in value_scatter], axis=1
    )
    while key_scatter[0].steps:
        together(key_scatter)
    key_sum = jnp.concatenate([x.total() for x in key_scatter], axis=1).reshape(2, share, -1)

    def exchange(x):
        mine = lax.dynamic_index_in_dim(x, core, 0, keepdims=False)
        return mine, swap(lax.dynamic_index_in_dim(x, 1 - core, 0, keepdims=False), 1)

    key_mine, key_theirs = exchange(key_sum)
    input_gradient, value_sum, key_mine, key_theirs = meet(
        last_parts, input_gradient, value_sum, key_mine, key_theirs
    )
    while last_parts[0].steps:
        together(last_parts)
    first_sum, second_sum, misc_sum = [x.total() for x in last_parts]
    misc_sum = jnp.concatenate([misc_sum[:share], misc_sum[share:]], axis=1)
    att_sum = jnp.concatenate(
        [first_sum[:, :OWN], second_sum, first_sum[:, OWN:]], axis=1
    )
    mine, theirs = exchange(att_sum.reshape(2, share, -1))
    shard_mixer = jnp.stack(
        [
            in_order(1, mine[:, i * OWN : (i + 1) * OWN], theirs[:, i * OWN : (i + 1) * OWN], 1)
            for i in range(4)
        ]
    )
    shard_key = in_order(
        1,
        key_mine.reshape(share, chips, 1, units),
        key_theirs.reshape(share, chips, 1, units),
        2,
    ).reshape(share, 2 * half_units)
    return (
        output,
        input_gradient,
        shard_mixer,
        shard_key,
        value_sum,
        misc_sum[:, :256],
        misc_sum[:, 256:512].T,
        misc_sum[:, 512:530].T,
    )


def solution(mesh):
    in_specs = (
        P("dp", None),
        P(),
        P(None, "dp", None),
        P("dp", None),
        P("dp", None),
        P("dp", None),
        P(None, "dp"),
        P(None, "dp"),
        P("dp", None),
    )
    out_specs = (
        P("dp", None),
        P("dp", None),
        P(None, "dp", None),
        P("dp", None),
        P("dp", None),
        P("dp", None),
        P(None, "dp"),
        P(None, "dp"),
    )
    return jax.shard_map(local, mesh=mesh, in_specs=in_specs, out_specs=out_specs, check_vma=False)
```

```python
from functools import partial

import jax
import jax.numpy as jnp
from jax import lax
from jax.experimental import pallas as pl
from jax.experimental.pallas import tpu as pltpu
from jax.sharding import PartitionSpec as P

HEADS = 16
HEAD_SIZE = 64
DECAY_RANK = 64
RATE_RANK = 64
EMBED = 1024
OWN = EMBED // 2
PRECISE = lax.Precision.HIGHEST


CHUNK = 64
LANES = 256
GROUP_HEADS = 4
STEP_CHUNKS = 2
SMALL = pl.CostEstimate(flops=1, bytes_accessed=1, transcendentals=0)

NN = (((1,), (0,)), ((), ()))
NT = (((1,), (1,)), ((), ()))
TN = (((0,), (0,)), ((), ()))


def halves(x):
    high = x.astype(jnp.bfloat16)
    return high, (x - high.astype(jnp.float32)).astype(jnp.bfloat16)


def dot32(a, b, dims):
    return lax.dot_general(a, b, dims, preferred_element_type=jnp.float32)


def mul(left, right, dims=NN):
    rows = left[0].shape[0]
    both = dot32(jnp.concatenate(left, axis=0), right[0], dims)
    return both[:rows] + both[rows:] + dot32(left[0], right[1], dims)


def tmul(left, right, masks):
    full = (
        dot32(left[0], right[0], TN) + dot32(left[1], right[0], TN) + dot32(left[0], right[1], TN)
    )
    return sum(full[h * CHUNK : (h + 1) * CHUNK] * masks[h][:1].astype(jnp.float32) for h in range(GROUP_HEADS))


def spread(pair, masks):
    return tuple(
        jnp.concatenate([part * masks[h] for h in range(GROUP_HEADS)], axis=0) for part in pair
    )


def stack(first, second):
    return tuple(jnp.concatenate([x, y], axis=0) for x, y in zip(first, second))


def head_masks():
    lane = lax.broadcasted_iota(jnp.int32, (CHUNK, LANES), 1) // CHUNK
    return [(lane == h).astype(jnp.float32).astype(jnp.bfloat16) for h in range(GROUP_HEADS)]


def places():
    row = lax.broadcasted_iota(jnp.int32, (CHUNK, LANES), 0)
    col = lax.broadcasted_iota(jnp.int32, (CHUNK, LANES), 1) % CHUNK
    return row, col


def running_sum(x, upper=False):
    row = lax.broadcasted_iota(jnp.int32, (CHUNK, CHUNK), 0)
    col = lax.broadcasted_iota(jnp.int32, (CHUNK, CHUNK), 1)
    ones = (row <= col if upper else col <= row).astype(jnp.float32).astype(jnp.bfloat16)
    high, rest = halves(x)
    low = (x - high.astype(jnp.float32) - rest.astype(jnp.float32)).astype(jnp.bfloat16)
    return dot32(ones, high, NN) + dot32(ones, rest, NN) + dot32(ones, low, NN)


def scaled_forms(q, w, k, a, b):
    total = running_sum(w)
    before = total - w
    middle = total[CHUNK // 2 - 1 : CHUNK // 2]
    end = total[CHUNK - 1 :]
    ea = jnp.exp(before - middle)
    eq = jnp.exp(total - middle)
    eb = jnp.exp(middle - total)
    ee = jnp.exp(end - total)
    return (a * ea, q * eq, b * eb, k * eb, b * ee, k * ee), (ea, eq, eb, ee), (jnp.exp(middle), jnp.exp(end))


def each(fn, *columns):
    return [fn(*row) for row in zip(*columns)]


def block_ones():
    row = lax.broadcasted_iota(jnp.int32, (LANES, LANES), 0) // CHUNK
    col = lax.broadcasted_iota(jnp.int32, (LANES, LANES), 1) // CHUNK
    return (row == col).astype(jnp.float32).astype(jnp.bfloat16)


def head_sum(x, ones):
    rows = x.shape[0]
    both = dot32(jnp.concatenate(halves(x), axis=0), ones, NN)
    return both[:rows] + both[rows:]


def prepared(keys, decay_low, rate_low, live, vec, ones):
    sig = jax.nn.sigmoid(vec[0] + decay_low)
    log_decay = (-0.6065306597126334) * sig * live
    rates = jax.nn.sigmoid(vec[1] + rate_low)
    scaled = keys * vec[2]
    inverse = lax.rsqrt(head_sum(scaled * scaled, ones) + 1e-06)
    unit_keys = scaled * inverse
    factor = (1.0 + (rates - 1.0) * vec[3]) * live
    return log_decay, keys * factor, -unit_keys, unit_keys * rates * live, sig, rates, inverse, factor


def read_out(o, q, k, v, vec, ones):
    centred = o - head_sum(o, ones) * (1.0 / CHUNK)
    scale = lax.rsqrt(head_sum(centred * centred, ones) * (1.0 / CHUNK) + 0.00064)
    normed = centred * scale
    weight = head_sum(q * k * vec[4], ones)
    return normed, scale, weight, normed * vec[5] + vec[6] + weight * v


def unit_slices():
    return [
        (slice(c * CHUNK, (c + 1) * CHUNK), slice(g * LANES, (g + 1) * LANES))
        for c in range(STEP_CHUNKS)
        for g in range(2)
    ]


def unit_live(length, step):
    row = lax.broadcasted_iota(jnp.int32, (CHUNK, LANES), 0)
    start = step * (STEP_CHUNKS * CHUNK)
    live = [(row + (start + c * CHUNK) < length).astype(jnp.float32) for c in range(STEP_CHUNKS)]
    return [live[c] for c in range(STEP_CHUNKS) for g in range(2)]


def unit_vectors(vec_ref):
    vec = [[vec_ref[i : i + 1, g * LANES : (g + 1) * LANES] for i in range(7)] for g in range(2)]
    return [vec[g] for c in range(STEP_CHUNKS) for g in range(2)]


def forward_kernel(base, *refs):
    len_ref, vec_ref, start_ref, q_ref, keys_ref, v_ref, dl_ref, rl_ref, gate_ref = refs[:9]
    (
        out_ref, o_ref, t_ref, aqb_ref, aak_ref, aqk_ref, y_ref, z_ref, trt_ref, qe_ref, state_ref,
    ) = refs[-11:]

    @pl.when(pl.program_id(0) == 0)
    def _():
        state_ref[...] = start_ref[...]

    masks = head_masks()
    row, col = places()
    strict = (col < row).astype(jnp.float32)
    within = (col <= row).astype(jnp.float32)
    eye = (col == row).astype(jnp.float32)
    ones = block_ones()
    units = unit_slices()
    live = unit_live(len_ref[0], pl.program_id(0) + base)
    vec = unit_vectors(vec_ref)
    load = lambda ref: [ref[u] for u in units]
    q, keys, v = load(q_ref), load(keys_ref), load(v_ref)
    ready = each(
        lambda x, y, z, m, n: prepared(x, y, z, m, n, ones), keys, load(dl_ref), load(rl_ref), live, vec
    )
    w, k, a, b = ([x[i] for x in ready] for i in range(4))
    forms = each(scaled_forms, q, w, k, a, b)
    ah, qh, bh, kh, bt, kt = ([f[0][i] for f in forms] for i in range(6))
    emid = [f[2][0] for f in forms]
    eend = [f[2][1] for f in forms]
    aq = each(lambda x, y: halves(jnp.concatenate([x, y], axis=0)), ah, qh)
    with_b = each(lambda l, r: mul(l, spread(halves(r), masks), NT), aq, bh)
    with_k = each(lambda l, r: mul(l, spread(halves(r), masks), NT), aq, kh)
    aab = [x[:CHUNK] * strict for x in with_b]
    aqb = [halves(x[CHUNK:] * within) for x in with_b]
    aak = [halves(x[:CHUNK] * strict) for x in with_k]
    aqk = [halves(x[CHUNK:] * within) for x in with_k]
    p = [halves(x * (row // 8 == col // 8)) for x in aab]
    t = [eye + x * (row // 8 == col // 8) for x in aab]
    p2 = each(lambda x: halves(mul(x, spread(x, masks))), p)
    both = each(lambda x, y: mul(stack(x, halves(y)), spread(x, masks)), p2, t)
    p4 = [halves(x[:CHUNK]) for x in both]
    t = each(lambda x, y: x + y[CHUNK:], t, both)
    t = each(lambda x, y: x + mul(halves(x), spread(y, masks)), t, p4)
    for size in (8, 16, 32):
        corner = ((row // size) % 2 == 1) & (col // size == row // size - 1)
        ts = [halves(x) for x in t]
        n = [halves(x * corner) for x in aab]
        tn = each(lambda x, y: halves(mul(x, spread(y, masks))), ts, n)
        t = each(lambda x, y, z: x + mul(y, spread(z, masks)), t, tn, ts)
    ts = [halves(x) for x in t]
    vs = [halves(x) for x in v]
    vm = [spread(x, masks) for x in vs]
    wide = each(lambda x, y, e: mul(x, spread(halves(y * e), masks)), ts, ah, emid)
    r0 = each(mul, aak, vm)
    y0 = each(lambda x, y: mul(x, spread(halves(y), masks)), ts, r0)
    wides = [halves(x) for x in wide]
    qe = each(lambda x, e, y, z: x * e + mul(y, spread(z, masks)), qh, emid, aqb, wides)
    y0s = [halves(x) for x in y0]
    part = each(lambda x, y, z, u: mul(x, spread(y, masks)) + mul(z, u), aqb, y0s, aqk, vm)
    bts = [halves(x) for x in bt]
    diag = [eye * e for e in eend]
    tr = each(lambda x, y, d: tmul(x, y, masks) + d, bts, wides, diag)
    trt = each(lambda x, y, d: tmul(y, x, masks) + d, bts, wides, diag)
    inject = each(lambda x, y, z, u: tmul(stack(x, halves(y)), stack(z, u), masks), bts, kt, y0s, vs)
    wq = each(lambda x, y: stack(x, halves(y)), wides, qe)
    z = []
    out = []
    for c in range(STEP_CHUNKS):
        for g in range(2):
            i = c * 2 + g
            now = state_ref[g]
            nows = spread(halves(now), masks)
            state_ref[g] = mul(halves(tr[i]), nows) + inject[i]
            z.append(now)
            out.append(mul(wq[i], nows))
    o = each(lambda x, y: x[CHUNK:] + y, out, part)
    mixed = each(lambda x, y, z, m, n: read_out(x, y, z, m, n, ones)[3], o, q, k, v, vec)
    for i, u in enumerate(units):
        out_ref[u] = (mixed[i] * gate_ref[u]).astype(jnp.bfloat16)
        o_ref[u] = o[i]
        y_ref[u] = out[i][:CHUNK] + y0[i]
        t_ref[u] = t[i]
        aqb_ref[u] = with_b[i][CHUNK:] * within
        aak_ref[u] = with_k[i][:CHUNK] * strict
        aqk_ref[u] = with_k[i][CHUNK:] * within
        z_ref[u] = z[i]
        trt_ref[u] = trt[i]
        qe_ref[u] = qe[i]


def backward_kernel(base, *refs):
    (
        len_ref, vec_ref, start_ref, sums_ref, q_ref, keys_ref, v_ref, dl_ref, rl_ref, gate_ref,
        g_ref, o_ref, t_ref, aqb_ref, aak_ref, aqk_ref, y_ref, z_ref, trt_ref, qe_ref,
    ) = refs[:20]
    dq_ref, dkeys_ref, dv_ref, ddl_ref, drl_ref, dgate_ref, dvec_ref, state_ref = refs[-8:]
    step = base + pl.num_programs(0) - 1 - pl.program_id(0)

    @pl.when(pl.program_id(0) == 0)
    def _():
        state_ref[...] = start_ref[...]
        dvec_ref[...] = sums_ref[...]

    masks = head_masks()
    row, col = places()
    strict = (col < row).astype(jnp.float32)
    within = (col <= row).astype(jnp.float32)
    ones = block_ones()
    units = unit_slices()
    live = unit_live(len_ref[0], step)
    vec = unit_vectors(vec_ref)
    load = lambda ref: [ref[u] for u in units]
    q, keys, v, g = load(q_ref), load(keys_ref), load(v_ref), load(g_ref)
    ready = each(
        lambda x, y, z, m, n: prepared(x, y, z, m, n, ones), keys, load(dl_ref), load(rl_ref), live, vec
    )
    w, k, a, b, sig, rates, inverse, factor = ([x[i] for x in ready] for i in range(8))
    seen = each(lambda x, y, z, m, n: read_out(x, y, z, m, n, ones), load(o_ref), q, k, v, vec)
    normed, scale, weight, mixed = ([x[i] for x in seen] for i in range(4))
    gate = load(gate_ref)
    dgate = each(lambda x, y: x * y, g, mixed)
    dmix = each(lambda x, y: x * y, g, gate)
    dn = each(lambda x, n: x * n[5], dmix, vec)
    do = each(
        lambda x, n, r: r
        * (x - head_sum(x, ones) * (1.0 / CHUNK) - n * (head_sum(x * n, ones) * (1.0 / CHUNK))),
        dn, normed, scale,
    )
    dweight = each(lambda x, y: head_sum(x * y, ones), dmix, v)
    do = [halves(x) for x in do]
    qe, trt, t, aqb, aak, aqk, ys = (
        [halves(x) for x in load(ref)]
        for ref in (qe_ref, trt_ref, t_ref, aqb_ref, aak_ref, aqk_ref, y_ref)
    )
    z = load(z_ref)
    vs = [halves(x) for x in v]
    h = each(lambda x, y: tmul(x, y, masks), qe, do)
    dz = [None] * len(units)
    for c in reversed(range(STEP_CHUNKS)):
        for g in range(2):
            i = c * 2 + g
            now = state_ref[g]
            dz[i] = now
            state_ref[g] = mul(trt[i], spread(halves(now), masks)) + h[i]
    dzs = [spread(halves(x), masks) for x in dz]
    zs = [spread(halves(x), masks) for x in z]
    forms = each(scaled_forms, q, w, k, a, b)
    ah, qh, bh, kh, bt, kt = ([f[0][i] for f in forms] for i in range(6))
    ea, eq, eb, ee = ([f[1][i] for f in forms] for i in range(4))
    emid = [f[2][0] for f in forms]
    eend = [f[2][1] for f in forms]
    from_end = each(lambda x, y, s: mul(halves(jnp.concatenate([x, y], axis=0)), s), bt, kt, dzs)
    dy = each(lambda x, y, s: halves(tmul(x, y, masks) + s[:CHUNK]), aqb, do, from_end)
    dr = each(lambda x, y: halves(tmul(x, y, masks)), t, dy)
    ro = each(stack, dr, do)
    dv = each(lambda x, y, s, f: tmul(stack(x, y), s, masks) + f[CHUNK:], aak, aqk, ro, from_end)
    mask2 = jnp.concatenate([strict, within], axis=0)
    dab = each(lambda s, y: halves(mul(s, spread(y, masks), NT) * mask2), ro, ys)
    dak = each(lambda s, y: halves(mul(s, spread(y, masks), NT) * mask2), ro, vs)
    dst = each(lambda s, y: mul(s, y, NT), ro, zs)
    daq = each(
        lambda s, e, x, bb, y, kk: s * e + mul(x, spread(halves(bb), masks)) + mul(y, spread(halves(kk), masks)),
        dst, emid, dab, bh, dak, kh,
    )
    aq = each(lambda x, y: halves(jnp.concatenate([x, y], axis=0)), ah, qh)
    dbh = each(lambda x, y: tmul(x, y, masks), dab, aq)
    dkh = each(lambda x, y: tmul(x, y, masks), dak, aq)
    dend = each(lambda y, x, s: mul(stack(y, x), s, NT), ys, vs, dzs)
    row_of_ones = jnp.ones((8, LANES), jnp.bfloat16)
    sums = lambda x: jnp.sum(x, axis=0, keepdims=True)
    for i, u in enumerate(units):
        da = daq[i][:CHUNK] * ea[i]
        dq = daq[i][CHUNK:] * eq[i]
        dbt = dend[i][:CHUNK] * ee[i]
        dkt = dend[i][CHUNK:] * ee[i]
        db = dbh[i] * eb[i] + dbt
        dk = dkh[i] * eb[i] + dkt
        pa = da * a[i]
        diff = dq * q[i] - db * b[i] - dk * k[i] + pa
        zz = spread(halves(z[i] * dz[i]), masks)
        carry = (dot32(row_of_ones, zz[0], NT) + dot32(row_of_ones, zz[1], NT))[:1] * eend[i]
        carry = carry + sums(dbt * b[i] + dkt * k[i])
        dw = running_sum(diff, upper=True) - pa + carry
        from_bonus = dweight[i] * vec[i][4]
        dk = dk + from_bonus * q[i]
        dq_ref[u] = (dq + from_bonus * k[i]).astype(jnp.bfloat16)
        dv_ref[u] = (dv[i] + weight[i] * dmix[i]).astype(jnp.bfloat16)
        dgate_ref[u] = dgate[i].astype(jnp.bfloat16)
        unit_keys = -a[i]
        db = db * live[i]
        du = db * rates[i] - da
        dscaled = inverse[i] * (du - unit_keys * head_sum(du * unit_keys, ones))
        dkl = dk * keys[i] * live[i]
        drl = (db * unit_keys + dkl * vec[i][3]) * rates[i] * (1.0 - rates[i])
        ddl = dw * w[i] * (1.0 - sig[i])
        dkeys_ref[u] = (dk * factor[i] + dscaled * vec[i][2]).astype(jnp.bfloat16)
        ddl_ref[u] = ddl.astype(jnp.bfloat16)
        drl_ref[u] = drl.astype(jnp.bfloat16)
        parts = (
            ddl, drl, dscaled * keys[i], dkl * (rates[i] - 1.0),
            dweight[i] * q[i] * k[i], dmix[i] * normed[i], dmix[i],
        )
        lanes = u[1]
        for j, x in enumerate(parts):
            dvec_ref[j : j + 1, lanes] += sums(x)


def wkv_call(kernel, base, steps, small, arrays, outs, sums, previous, name):
    tokens, width = arrays[0].shape
    rows = CHUNK * STEP_CHUNKS
    last = base + steps - 1
    turned = kernel is backward_kernel
    spec = pl.BlockSpec((rows, width), lambda i: (last - i if turned else base + i, 0))
    state = pl.BlockSpec((2, CHUNK, LANES), lambda i: (0, 0, 0))
    whole = pl.BlockSpec((8, width), lambda i: (0, 0))
    shape = jax.ShapeDtypeStruct
    first = [pl.BlockSpec(memory_space=pltpu.SMEM), whole, state] + [whole] * sums
    held = list(previous or ())
    start = len(first) + len(arrays)
    return pl.pallas_call(
        partial(kernel, base),
        grid=(steps,),
        in_specs=first + [spec] * len(arrays) + [pl.BlockSpec(memory_space=pl.ANY)] * len(held),
        out_specs=[spec] * len(outs) + [whole] * sums + [state],
        out_shape=[shape((tokens, width), dtype) for dtype in outs]
        + [shape((8, width), jnp.float32)] * sums
        + [shape((2, CHUNK, LANES), jnp.float32)],
        input_output_aliases={start + i: i for i in range(len(held))},
        compiler_params=pltpu.CompilerParams(vmem_limit_bytes=60 << 20),
        cost_estimate=SMALL,
        name=name,
    )(*small, *arrays, *held)


def wkv_forward(base, steps, length, vec, state, arrays, previous=None):
    outs = [jnp.bfloat16] + [jnp.float32] * 9
    return wkv_call(
        forward_kernel, base, steps, (length, vec, state), arrays, outs, 0, previous, "wkv_forward"
    )


def wkv_backward(base, steps, length, vec, state, sums, arrays, previous=None):
    outs = [jnp.bfloat16] * 6
    return wkv_call(
        backward_kernel, base, steps, (length, vec, state, sums), arrays, outs, 1, previous,
        "wkv_backward",
    )


ROWS = 128


def row_norm(x):
    centred = x - jnp.mean(x, axis=-1, keepdims=True)
    scale = lax.rsqrt(jnp.mean(centred * centred, axis=-1, keepdims=True) + 1e-05)
    return centred * scale, scale


def shifted(x, edge, down):
    rows = x.shape[0]
    row = lax.broadcasted_iota(jnp.int32, x.shape, 0)
    if down:
        return jnp.where(row == 0, edge, pltpu.roll(x, 1, 0))
    return jnp.where(row == rows - 1, edge, pltpu.roll(x, rows - 1, 0))


def below(x, upper):
    lane = lax.broadcasted_iota(jnp.int32, x.shape, 1)
    keep = (lane >= DECAY_RANK) if upper else (lane < DECAY_RANK)
    return jnp.where(keep, x, jnp.zeros_like(x))


def front_kernel(
    x_ref, vec_ref, wr_ref, wk_ref, wv_ref, down_ref, up_ref,
    m0_ref, m1_ref, m2_ref, m3_ref, m4_ref, m5_ref,
    q_ref, k_ref, v_ref, dl_ref, rl_ref, gate_ref, hid_ref,
    edge_ref,
):
    @pl.when(pl.program_id(0) == 0)
    def _():
        edge_ref[...] = jnp.zeros_like(edge_ref)

    unit, _ = row_norm(x_ref[...].astype(jnp.float32))
    normed = unit * vec_ref[12:13] + vec_ref[13:14]
    change = shifted(normed, edge_ref[:1], True) - normed
    edge_ref[:1] = normed[ROWS - 1 :]
    mixes = []
    for j, ref in enumerate((m0_ref, m1_ref, m2_ref, m3_ref, m4_ref, m5_ref)):
        mixes.append((normed + change * vec_ref[j : j + 1]).astype(jnp.bfloat16))
        ref[...] = mixes[j]
    q_ref[...] = dot32(mixes[0], wr_ref[...], NN)
    k_ref[...] = dot32(mixes[2], wk_ref[...], NN)
    v_ref[...] = dot32(mixes[3], wv_ref[...], NN)
    first = down_ref[:, :128]
    pre_decay, pre_rate = dot32(mixes[1], first, NN), dot32(mixes[4], first, NN)
    pre_gate = dot32(mixes[5], down_ref[:, 128:], NN)
    lane = lax.broadcasted_iota(jnp.int32, pre_decay.shape, 1)
    pair = jnp.where(lane < DECAY_RANK, jnp.tanh(pre_decay), pre_rate)
    gate = jax.nn.sigmoid(pre_gate)
    hid_ref[:, :128] = pair
    hid_ref[:, 128:] = gate
    narrow_pair = pair.astype(jnp.bfloat16)
    dl_ref[...] = dot32(below(narrow_pair, False), up_ref[:, :128], NT)
    rl_ref[...] = dot32(below(narrow_pair, True), up_ref[:, :128], NT)
    gate_ref[...] = dot32(gate.astype(jnp.bfloat16), up_ref[:, 128:], NT)


def front_forward(x, vectors, w_r, w_k, w_v, down, up):
    tokens, width = x.shape
    wide = pl.BlockSpec((ROWS, width), lambda i: (i, 0))
    own = pl.BlockSpec((ROWS, OWN), lambda i: (i, 0))
    hid = pl.BlockSpec((ROWS, 256), lambda i: (i, 0))
    whole = lambda a: pl.BlockSpec(a.shape, lambda i: (0, 0))
    shape = jax.ShapeDtypeStruct
    return pl.pallas_call(
        front_kernel,
        grid=(tokens // ROWS,),
        in_specs=[wide] + [whole(a) for a in (vectors, w_r, w_k, w_v, down, up)],
        out_specs=[wide] * 6 + [own] * 6 + [hid],
        out_shape=[shape((tokens, width), jnp.bfloat16)] * 6
        + [shape((tokens, OWN), jnp.float32)] * 6
        + [shape((tokens, 256), jnp.float32)],
        scratch_shapes=[pltpu.VMEM((8, width), jnp.float32)],
        compiler_params=pltpu.CompilerParams(vmem_limit_bytes=60 << 20),
        cost_estimate=SMALL,
        name="front_forward",
    )(x, vectors, w_r, w_k, w_v, down, up)


def front_back_kernel(
    x_ref, before_ref, vec_ref, wr_ref, wk_ref, wv_ref, down_ref, up_ref,
    m1_ref, m4_ref, m5_ref, hid_ref,
    dq_ref, dk_ref, dv_ref, ddl_ref, drl_ref, dgate_ref, own_vec_ref, ffn_vec_ref,
    dx_ref, mine_ref, other_ref,
    edge_ref, sums_ref, misc_ref,
):
    step = pl.num_programs(0) - 1 - pl.program_id(0)
    core = lax.axis_index("dp") % 2
    own_start = pl.multiple_of(core * OWN, OWN)

    @pl.when(pl.program_id(0) == 0)
    def _():
        edge_ref[...] = jnp.zeros_like(edge_ref)
        sums_ref[...] = jnp.zeros_like(sums_ref)
        misc_ref[...] = jnp.zeros_like(misc_ref)

    unit, scale = row_norm(x_ref[...].astype(jnp.float32))
    gain, offset = vec_ref[12:13], vec_ref[13:14]
    normed = unit * gain + offset
    tail, _ = row_norm(before_ref[...].astype(jnp.float32))
    edge = (tail[15:] * gain + offset) * jnp.where(step == 0, 0.0, 1.0)
    change = shifted(normed, edge, True) - normed
    ddl, drl, dgate = ddl_ref[...], drl_ref[...], dgate_ref[...]
    hid = hid_ref[...]
    pair, gate = hid[:, :128], hid[:, 128:]
    lane = lax.broadcasted_iota(jnp.int32, pair.shape, 1)
    first_up, last_up = up_ref[:, :128], up_ref[:, 128:]
    pair_grad = jnp.where(
        lane < DECAY_RANK,
        dot32(ddl, first_up, NN) * (1.0 - pair * pair),
        dot32(drl, first_up, NN),
    ).astype(jnp.bfloat16)
    gate_grad = (dot32(dgate, last_up, NN) * gate * (1.0 - gate)).astype(jnp.bfloat16)
    narrow_pair, narrow_gate = pair.astype(jnp.bfloat16), gate.astype(jnp.bfloat16)
    own_rows = pl.ds(own_start, OWN)
    misc_ref[own_rows, 256:384] += dot32(ddl, below(narrow_pair, False), TN) + dot32(
        drl, below(narrow_pair, True), TN
    )
    misc_ref[own_rows, 384:512] += dot32(dgate, narrow_gate, TN)
    decay_part, rate_part = below(pair_grad, False), below(pair_grad, True)
    misc_ref[:, :128] += dot32(m1_ref[...], decay_part, TN) + dot32(m4_ref[...], rate_part, TN)
    misc_ref[:, 128:256] += dot32(m5_ref[...], gate_grad, TN)
    first_down = down_ref[:, :128]
    grads = (
        lambda: dot32(dq_ref[...], wr_ref[...], NT),
        lambda: dot32(decay_part, first_down, NT),
        lambda: dot32(dk_ref[...], wk_ref[...], NT),
        lambda: dot32(dv_ref[...], wv_ref[...], NT),
        lambda: dot32(rate_part, first_down, NT),
        lambda: dot32(gate_grad, down_ref[:, 128:], NT),
    )
    total = jnp.zeros_like(change)
    moved = jnp.zeros_like(change)
    for j, grad in enumerate(grads):
        now = grad()
        total = total + now
        moved = moved + now * vec_ref[j : j + 1]
        sums_ref[j : j + 1] += jnp.sum(now * change, axis=0, keepdims=True)
    dnormed = total - moved + shifted(moved, edge_ref[:1], False)
    edge_ref[:1] = moved[:1]
    sums_ref[12:13] += jnp.sum(dnormed * unit, axis=0, keepdims=True)
    sums_ref[13:14] += jnp.sum(dnormed, axis=0, keepdims=True)
    dunit = dnormed * gain
    dx_ref[...] = scale * (
        dunit
        - jnp.mean(dunit, axis=-1, keepdims=True)
        - unit * jnp.mean(dunit * unit, axis=-1, keepdims=True)
    )

    @pl.when(step == 0)
    def _():
        sums_ref[6:7] = ffn_vec_ref[0:1] * 0.5
        sums_ref[14:16] = ffn_vec_ref[1:3] * 0.5
        zeros = jnp.zeros((1, OWN), jnp.float32)
        for target, source in ((7, 0), (8, 1), (9, 2), (10, 3), (11, 4), (16, 5), (17, 6)):
            mine = own_vec_ref[source : source + 1]
            sums_ref[target : target + 1] = jnp.concatenate(
                [jnp.where(core == 0, mine, zeros), jnp.where(core == 0, zeros, mine)], axis=1
            )
        for block in range(EMBED // 128):
            lanes = slice(block * 128, (block + 1) * 128)
            misc_ref[lanes, 512:640] = sums_ref[:, lanes].T
        share = mine_ref.shape[1]
        for chip in range(mine_ref.shape[0]):
            low = misc_ref[2 * chip * share : (2 * chip + 1) * share]
            high = misc_ref[(2 * chip + 1) * share : (2 * chip + 2) * share]
            mine_ref[chip] = jnp.where(core == 0, low, high)
            other_ref[chip] = jnp.where(core == 0, high, low).astype(jnp.bfloat16)


def front_backward(
    x, vectors, w_r, w_k, w_v, down, up, mixes, hid, grads, own_vec, ffn_vec
):
    tokens, width = x.shape
    devices = lax.axis_size("dp")
    pieces = (devices // 2, EMBED // devices, 640)
    steps = tokens // ROWS
    wide = pl.BlockSpec((ROWS, width), lambda i: (steps - 1 - i, 0))
    before = pl.BlockSpec(
        (16, width), lambda i: (jnp.maximum((steps - 1 - i) * (ROWS // 16) - 1, 0), 0)
    )
    own = pl.BlockSpec((ROWS, OWN), lambda i: (steps - 1 - i, 0))
    hid_spec = pl.BlockSpec((ROWS, 256), lambda i: (steps - 1 - i, 0))
    whole = lambda a: pl.BlockSpec(a.shape, lambda i: (0, 0))
    shape = jax.ShapeDtypeStruct
    return pl.pallas_call(
        front_back_kernel,
        grid=(steps,),
        in_specs=[wide, before]
        + [whole(a) for a in (vectors, w_r, w_k, w_v, down, up)]
        + [wide] * 3
        + [hid_spec]
        + [own] * 6
        + [whole(own_vec), whole(ffn_vec)],
        out_specs=[wide] + [pl.BlockSpec(pieces, lambda i: (0, 0, 0))] * 2,
        out_shape=[
            shape((tokens, width), jnp.float32),
            shape(pieces, jnp.float32),
            shape(pieces, jnp.bfloat16),
        ],
        scratch_shapes=[
            pltpu.VMEM((8, width), jnp.float32),
            pltpu.VMEM((128, width), jnp.float32),
            pltpu.VMEM((EMBED, 640), jnp.float32),
        ],
        compiler_params=pltpu.CompilerParams(vmem_limit_bytes=60 << 20),
        cost_estimate=SMALL,
        name="front_backward",
    )(x, x, vectors, w_r, w_k, w_v, down, up, *mixes, hid, *grads, own_vec, ffn_vec)


def ffn_back_kernel(
    len_ref, res_ref, before_ref, cot_ref, mine_ref, other_ref, mixed_ref, vec_ref, wo_ref,
    grad_ref, gated_ref, dvec_ref, do_ref,
    edge_ref, sum_ref,
):
    step = pl.num_programs(0) - 1 - pl.program_id(0)

    @pl.when(pl.program_id(0) == 0)
    def _():
        edge_ref[...] = jnp.zeros_like(edge_ref)
        dvec_ref[...] = jnp.zeros_like(dvec_ref)
        sum_ref[...] = jnp.zeros_like(sum_ref)

    gain, offset, coefficient = vec_ref[14:15], vec_ref[15:16], vec_ref[6:7]
    unit, scale = row_norm(res_ref[...])
    normed = unit * gain + offset
    tail, _ = row_norm(before_ref[...])
    edge = (tail[7:] * gain + offset) * jnp.where(step == 0, 0.0, 1.0)
    change = shifted(normed, edge, True) - normed
    grad = mine_ref[...].astype(jnp.float32) + other_ref[...].astype(jnp.float32)
    moved = grad * coefficient
    dnormed = grad - moved + shifted(moved, edge_ref[:1], False)
    edge_ref[:1] = moved[:1]
    sums = lambda x: jnp.sum(x, axis=0, keepdims=True)
    dvec_ref[0:1] += sums(grad * change)
    dvec_ref[1:2] += sums(dnormed * unit)
    dvec_ref[2:3] += sums(dnormed)
    dunit = dnormed * gain
    row = lax.broadcasted_iota(jnp.int32, grad.shape, 0) + step * ROWS
    out_grad = jnp.where(row < len_ref[0], cot_ref[...].astype(jnp.float32), 0.0)
    total = out_grad + scale * (
        dunit
        - jnp.mean(dunit, axis=-1, keepdims=True)
        - unit * jnp.mean(dunit * unit, axis=-1, keepdims=True)
    )
    grad_ref[...] = total
    small = total.astype(jnp.bfloat16)
    core = lax.axis_index("dp") % 2
    own = jnp.where(core == 0, total[:, :OWN], total[:, OWN:]).astype(jnp.bfloat16)
    sum_ref[...] += dot32(mixed_ref[...], own, TN)

    @pl.when(step == 0)
    def _():
        do_ref[...] = sum_ref[...].astype(jnp.bfloat16)

    gated_ref[...] = dot32(small, wo_ref[...], NT)


def ffn_backward(length, residual, cot, mine, other, gated, vectors, w_o_rows):
    tokens, width = residual.shape
    steps = tokens // ROWS
    wide = pl.BlockSpec((ROWS, width), lambda i: (steps - 1 - i, 0))
    before = pl.BlockSpec(
        (8, width), lambda i: (jnp.maximum((steps - 1 - i) * (ROWS // 8) - 1, 0), 0)
    )
    own = pl.BlockSpec((ROWS, OWN), lambda i: (steps - 1 - i, 0))
    whole = lambda a: pl.BlockSpec(a.shape, lambda i: (0, 0))
    shape = jax.ShapeDtypeStruct
    return pl.pallas_call(
        ffn_back_kernel,
        grid=(steps,),
        in_specs=[pl.BlockSpec(memory_space=pltpu.SMEM), wide, before]
        + [wide] * 4
        + [whole(vectors), whole(w_o_rows)],
        out_specs=[
            wide, own, pl.BlockSpec((8, width), lambda i: (0, 0)),
            pl.BlockSpec((EMBED, OWN), lambda i: (0, 0)),
        ],
        out_shape=[
            shape((tokens, width), jnp.float32),
            shape((tokens, OWN), jnp.float32),
            shape((8, width), jnp.float32),
            shape((EMBED, OWN), jnp.bfloat16),
        ],
        scratch_shapes=[
            pltpu.VMEM((8, width), jnp.float32), pltpu.VMEM((EMBED, OWN), jnp.float32),
        ],
        compiler_params=pltpu.CompilerParams(vmem_limit_bytes=60 << 20),
        cost_estimate=SMALL,
        name="ffn_backward",
    )(length, residual, residual, cot, mine, other, gated, vectors, w_o_rows)


def att_grad_kernel(m0_ref, m2_ref, m3_ref, dq_ref, dk_ref, dv_ref, send_a, keep_a, send_b, keep_b):
    chip = lax.axis_index("dp") // 2
    by_x, by_y = chip % 2 == 0, (chip // 2) % 2 == 0
    quarter = OWN // 2
    dv = dv_ref[...]
    first = ((m0_ref, dq_ref[...], 0, OWN), (m3_ref, dv[:, :quarter], OWN, quarter))
    second = ((m2_ref, dk_ref[...], 0, OWN), (m3_ref, dv[:, quarter:], OWN, quarter))
    for left, right, lane, width in first:
        block = dot32(left[...], right, TN).astype(jnp.bfloat16)
        lanes = slice(lane, lane + width)
        for y in range(2):
            low, high = block[y * 128 : y * 128 + 64], block[y * 128 + 64 : y * 128 + 128]
            send_a[y, :, lanes] = jnp.where(by_x, high, low)
            keep_a[y, :, lanes] = jnp.where(by_x, low, high)
    for left, right, lane, width in second:
        block = dot32(left[...], right, TN).astype(jnp.bfloat16)
        lanes = slice(lane, lane + width)
        for x in range(2):
            low, high = block[x * 64 : x * 64 + 64], block[128 + x * 64 : 128 + x * 64 + 64]
            send_b[x, :, lanes] = jnp.where(by_y, high, low)
            keep_b[x, :, lanes] = jnp.where(by_y, low, high)


def att_gradients(mixes, grads):
    tokens = mixes[0].shape[0]
    left = pl.BlockSpec((tokens, 256), lambda i: (0, i))
    right = pl.BlockSpec((tokens, OWN), lambda i: (0, 0))
    out = pl.BlockSpec((2, 64, OWN + OWN // 2), lambda i: (i, 0, 0))
    return pl.pallas_call(
        att_grad_kernel,
        grid=(4,),
        in_specs=[left] * 3 + [right] * 3,
        out_specs=[out] * 4,
        out_shape=[jax.ShapeDtypeStruct((8, 64, OWN + OWN // 2), jnp.bfloat16)] * 4,
        compiler_params=pltpu.CompilerParams(vmem_limit_bytes=60 << 20),
        cost_estimate=SMALL,
        name="att_gradients",
    )(*mixes, *grads)


def swap(block, mask):
    size = lax.axis_size("dp")
    return lax.ppermute(block, "dp", [(i, i ^ mask) for i in range(size)])


def bit_of(mask):
    return (lax.axis_index("dp") // mask) % 2


def in_order(mask, own, other, axis):
    lower = bit_of(mask) == 0
    return jnp.where(
        lower, jnp.concatenate([own, other], axis=axis), jnp.concatenate([other, own], axis=axis)
    )


def chip_masks():
    size = lax.axis_size("dp")
    masks = []
    while 2 << len(masks) < size:
        masks.append(2 << len(masks))
    return masks


def steps_of(kind):
    masks = chip_masks()
    near, far = [[mask] for mask in masks[:2]], [[mask] for mask in masks[2:][::-1]]
    first = [[far[0][0], far[1][0], far[0][0] | far[1][0]]] if len(far) == 2 else far
    return [first + near[::-1], first + near, far + near[::-1], far + near, near + far][kind]


class Held:
    def __init__(self, value):
        self.value = value


def meet(movers, *arrays):
    held = []
    for mover in movers:
        held += [x[0] for x in mover.arrived if x[0] not in held]
    out = lax.optimization_barrier(tuple(x.value for x in held) + arrays)
    for x, value in zip(held, out):
        x.value = value
    return out[len(held) :]


def read(arrived):
    out = []
    for x, lanes, pieces in arrived:
        value = x.value if lanes is None else x.value[..., lanes]
        width = value.shape[-1] // pieces
        value = [value[..., i * width : (i + 1) * width] for i in range(pieces)]
        out.append(value[0] if pieces == 1 else jnp.concatenate(value, axis=-2))
    return out


class Gather:
    def __init__(self, block, kind, places=(0,)):
        self.steps = steps_of(kind)
        self.held = block[None]
        self.places = [0]
        self.arrived = []
        self.masks = []

    def merge(self):
        if self.arrived:
            self.held = jnp.concatenate([self.held] + read(self.arrived), axis=0)
            self.places = self.places + [p ^ (m // 2) for m in self.masks for p in self.places]
            self.arrived = []

    def step(self):
        if self.steps:
            self.merge()
            self.masks = self.steps.pop(0)
            self.arrived = [(Held(swap(self.held, mask)), None, 1) for mask in self.masks]
        return self

    def run(self):
        while self.steps:
            self.step()
        return self

    def split(self, kinds):
        width = self.held.shape[-1] // len(kinds)
        out = []
        for i, kind in enumerate(kinds):
            part = Gather.__new__(Gather)
            cut = slice(i * width, (i + 1) * width)
            part.steps = steps_of(kind)[len(steps_of(kind)) - len(self.steps) :]
            part.held = self.held[..., cut]
            part.arrived = [(x, cut, 1) for x, _, _ in self.arrived]
            part.places, part.masks = self.places, self.masks
            out.append(part)
        return out


def place_kernel(places, cuts, *refs):
    sources, outs = refs[: len(places)], refs[len(places) :]
    chip = lax.axis_index("dp") // 2
    for source, (part, list_of) in zip(sources, places):
        for j, place in enumerate(list_of):
            for out, (first, rows, lanes) in zip(outs, cuts):
                start = pl.multiple_of((chip ^ place) * rows, rows)
                lane, width = lanes[part]
                at = sum(w for _, w in lanes[:part])
                out[pl.ds(start, rows), at : at + width] = source[
                    j, first : first + rows, lane : lane + width
                ]


def assemble(gathers, cuts=None):
    gathers = [g.run() for g in gathers]
    rows = gathers[0].held.shape[1]
    cuts = cuts or ((0, rows, [(0, g.held.shape[2]) for g in gathers]),)
    sources, places = [], []
    for i, g in enumerate(gathers):
        sources += [g.held] + read(g.arrived)
        shifts = [0] + [mask // 2 for mask in g.masks]
        places += [(i, [p ^ shift for p in g.places]) for shift in shifts]
    count = lax.axis_size("dp") // 2
    if any(cut[1] % 16 for cut in cuts):
        return assemble_plain(sources, places, cuts, count)
    space = pl.BlockSpec(memory_space=pltpu.VMEM)
    return pl.pallas_call(
        partial(place_kernel, places, cuts),
        in_specs=[space] * len(sources),
        out_specs=[space] * len(cuts),
        out_shape=[
            jax.ShapeDtypeStruct((count * n, sum(w for _, w in lanes)), sources[0].dtype)
            for _, n, lanes in cuts
        ],
        compiler_params=pltpu.CompilerParams(vmem_limit_bytes=32 << 20),
        cost_estimate=SMALL,
        name="assemble",
    )(*sources)


def assemble_plain(sources, places, cuts, count):
    chip = lax.axis_index("dp") // 2
    parts = []
    for part in sorted({part for part, _ in places}):
        blocks = jnp.concatenate([x for x, (at, _) in zip(sources, places) if at == part])
        where = [p for at, list_of in places if at == part for p in list_of]
        blocks = jnp.stack([blocks[where.index(i)] for i in range(count)])
        parts.append(jnp.take(blocks, chip ^ lax.iota(jnp.int32, count), axis=0))
    return [
        jnp.concatenate(
            [x[:, first : first + n, at : at + w] for x, (at, w) in zip(parts, lanes)], axis=-1
        ).reshape(count * n, -1)
        for first, n, lanes in cuts
    ]


class Scatter:
    def __init__(self, parts, kind):
        self.steps = steps_of(kind)[::-1]
        self.axes = chip_masks()[::-1]
        self.sources = [parts.reshape((2,) * len(self.axes) + parts.shape[1:])]
        self.arrived = []
        self.sent = None

    @classmethod
    def begun(cls, sent, kept, kind):
        out = cls.__new__(cls)
        out.steps = steps_of(kind)[::-1]
        out.axes = [axis for axis in chip_masks()[::-1] if axis != out.steps[0][0]]
        out.sources = [kept.reshape((2,) * len(out.axes) + kept.shape[1:])]
        out.arrived = []
        out.sent = [sent.reshape(out.sources[0].shape)]
        return out

    def pick(self, sources, mask, gone):
        out = []
        for x in sources:
            for place in reversed(range(len(self.axes))):
                axis = self.axes[place]
                if axis in gone:
                    which = bit_of(axis) if not mask & axis else 1 - bit_of(axis)
                    x = lax.dynamic_index_in_dim(x, which, place, keepdims=False)
            out.append(x)
        return out

    def prepare(self):
        if self.sent is not None:
            return self
        masks = self.steps[0]
        sources = self.sources + read(self.arrived)
        gone = [axis for axis in self.axes if any(mask & axis for mask in masks)]
        self.sent = [
            sum(x.astype(jnp.float32) for x in self.pick(sources, mask, gone)).astype(jnp.bfloat16)
            for mask in masks
        ]
        self.sources = self.pick(sources, 0, gone)
        self.axes = [axis for axis in self.axes if axis not in gone]
        self.arrived = []
        return self

    def step(self):
        return together([self])[0]

    def run(self):
        while self.steps:
            self.step()
        return self

    def total(self):
        return sum(x.astype(jnp.float32) for x in self.sources + read(self.arrived))


def together(parts):
    if not parts[0].steps:
        return parts
    for part in parts:
        part.prepare()
    rows = min(part.sent[0].shape[-2] for part in parts)
    for i, mask in enumerate(parts[0].steps[0]):
        sent = [
            [x[..., at : at + rows, :] for at in range(0, x.shape[-2], rows)]
            for x in (part.sent[i] for part in parts)
        ]
        flat = [x for pieces in sent for x in pieces]
        got = Held(swap(flat[0] if len(flat) == 1 else jnp.concatenate(flat, axis=-1), mask))
        at = 0
        for part, pieces in zip(parts, sent):
            width = sum(x.shape[-1] for x in pieces)
            lanes = slice(at, at + width) if len(flat) > 1 else None
            part.arrived.append((got, lanes, len(pieces)))
            at += width
    for part in parts:
        part.steps.pop(0)
        part.sent = None
    return parts


def norm_rows(features, gain_row, offset_row):
    average = jnp.mean(features, axis=-1, keepdims=True)
    centred = features - average
    variance = jnp.mean(centred * centred, axis=-1, keepdims=True)
    return centred * lax.rsqrt(variance + 1e-05) * gain_row + offset_row


def product(operand, weight_matrix):
    return jnp.dot(operand, weight_matrix, preferred_element_type=jnp.float32)


def input_gradient_rows(upstream_gradient, weight_matrix):
    return lax.dot_general(
        upstream_gradient,
        weight_matrix,
        (((1,), (1,)), ((), ())),
        preferred_element_type=jnp.float32,
    )


def weight_gradient(operand, upstream_gradient):
    return lax.dot_general(
        operand, upstream_gradient, (((0,), (0,)), ((), ())), preferred_element_type=jnp.float32
    )


def earlier(rows):
    return jnp.concatenate([jnp.zeros_like(rows[:1]), rows[:-1]], axis=0)


def ffn_mix(residual, vectors):
    second = norm_rows(residual, vectors[14], vectors[15])
    return second + (earlier(second) - second) * vectors[6]


def narrow(x):
    return x.astype(jnp.bfloat16)


def local(
    inputs,
    lengths,
    attention_projections,
    channel_key_weight,
    channel_value_weight,
    lowrank_down_weight,
    lowrank_up_weight,
    per_feature_parameters,
    cotangent,
):
    devices = lax.axis_size("dp")
    chips = devices // 2
    device = lax.axis_index("dp")
    chip, core = device // 2, device % 2
    row_count = inputs.shape[0]
    slots = 2 * row_count
    share = EMBED // devices
    pair_share = 2 * share
    units = channel_value_weight.shape[0]
    half_units = chips * units

    def own_cut(x, which):
        return lax.dynamic_slice_in_dim(x, which * OWN, OWN, x.ndim - 1)

    def own_rows(x, which):
        return lax.dynamic_slice_in_dim(x, which * row_count, row_count, 0)

    pair_rows = in_order(
        1,
        own_cut(attention_projections, core),
        swap(own_cut(attention_projections, 1 - core), 1),
        1,
    )
    lora = jnp.concatenate([lowrank_down_weight, lowrank_up_weight.T], axis=1)
    vector_rows = jnp.pad(per_feature_parameters.T, ((0, 0), (0, 128 - 18)))
    vector_rows = vector_rows.reshape(share // 4, OWN)
    first_rows = 3 * pair_share
    misc_rows = share + share // 4 + (share // 4) % 16
    block = jnp.concatenate(
        [
            pair_rows[:3].reshape(first_rows, OWN),
            lora,
            jnp.pad(vector_rows, ((0, (share // 4) % 16), (0, 0))),
        ],
        axis=0,
    )
    half = half_units // 2
    quarter = OWN // 2
    first = Gather(block, 0).step()
    w_o_part = Gather(pair_rows[3], 4).step().step()
    key_in, raw, cot, _ = meet([], channel_key_weight, inputs, cotangent, first.held)
    key_cut = key_in.reshape(share, chips, 2, units)

    def key_columns(which):
        return lax.dynamic_index_in_dim(key_cut, which, 2, keepdims=False).reshape(share, half_units)

    key_rows = in_order(1, key_columns(core), swap(key_columns(1 - core), 1), 0)
    tokens = in_order(1, raw, swap(raw, 1), 0)
    cot = in_order(1, cot, swap(cot, 1), 0)
    key_rows, tokens, cot = meet([first, w_o_part], key_rows, tokens, cot)
    first = first.split((0, 1))
    for part in first:
        part.step()
    key_part = Gather(key_rows, 2).step()
    (tokens,) = meet(first, tokens)
    for part in first:
        part.step()
    value_block, *_ = meet([key_part], channel_value_weight, *[part.held for part in first])
    key_part.step()
    value_part = Gather(value_block, 2).step()
    w_o_part.step()
    (tokens,) = meet(first + [key_part, value_part], tokens)
    key_parts = key_part.split((2, 3))
    for part in key_parts:
        part.step()
    w_r, w_k, w_v, misc = assemble(
        first,
        [(i * pair_share, pair_share, [(0, quarter)] * 2) for i in range(3)]
        + [(first_rows, misc_rows, [(0, quarter)] * 2)],
    )
    misc = misc.reshape(chips, 1, misc_rows, OWN)
    misc = in_order(1, misc, swap(misc, 1), 1)
    value_part.step()
    lora = misc[:, :, :share].reshape(EMBED, OWN)
    down, up_t = lora[:, :256], lax.dynamic_slice_in_dim(lora[:, 256:], core * OWN, OWN, 0)
    vectors = misc[:, :, share : share + share // 4].reshape(EMBED, 128)[:, :18].T
    vectors = vectors.astype(jnp.float32)
    own_vectors = own_cut(vectors, core)
    used = jnp.concatenate([own_vectors[7:12], own_vectors[16:18], own_vectors[:1]], axis=0)
    length = lax.dynamic_index_in_dim(lengths, chip, 0)
    live = (lax.iota(jnp.int32, slots) < length)[:, None]

    *mixes, queries, keys, values, decay_low, rate_low, gate_rows, hid = front_forward(
        tokens, vectors, w_r, w_k, w_v, down, up_t
    )
    terms = meet(
        key_parts + [value_part, w_o_part],
        queries, keys, values, decay_low, rate_low, gate_rows,
    )
    value_parts = value_part.split((2, 3))
    for part in key_parts + value_parts:
        part.step()
    w_o_part.step()
    blocks = slots // (CHUNK * STEP_CHUNKS)
    zero_state = jnp.zeros((2, CHUNK, LANES), jnp.float32)
    gated, *saved, _ = wkv_forward(0, blocks, length, used, zero_state, terms)
    gated, cot, tokens = meet(key_parts + value_parts + [w_o_part], gated, cot, tokens)
    for part in value_parts:
        part.step()
    gated, *_ = meet([], gated, *[part.held for part in value_parts])
    gated_all = in_order(1, gated, swap(gated, 1), 1)
    (w_o_own,) = assemble([w_o_part])
    w_o = in_order(1, w_o_own, swap(w_o_own, 1), 1)
    (key_weight,) = assemble(key_parts)
    residual = tokens.astype(jnp.float32) + product(gated_all, w_o)
    ffn_in = narrow(ffn_mix(residual, vectors))
    positive = jax.nn.relu(product(ffn_in, key_weight))
    hidden = narrow(jnp.square(positive))
    out_narrow = jnp.where(live, cot, jnp.zeros_like(cot))
    grad_value = narrow(weight_gradient(hidden, out_narrow)).reshape(chips, units, EMBED)
    w_o_rows = lax.dynamic_slice_in_dim(w_o, core * OWN, OWN, 0)
    hidden, positive, out_narrow, w_o_rows, grad_value = meet(
        value_parts, hidden, positive, out_narrow, w_o_rows, grad_value
    )
    (value_weight,) = assemble(value_parts)

    value_scatter = [
        Scatter(grad_value[..., i * OWN : (i + 1) * OWN], 2 + i).step() for i in range(2)
    ]
    pre_narrow = narrow(2.0 * positive * input_gradient_rows(out_narrow, value_weight))
    ffn_in_grad = narrow(input_gradient_rows(pre_narrow, key_weight))
    other_grad = swap(ffn_in_grad, 1)
    grad_key = narrow(weight_gradient(ffn_in, pre_narrow)).reshape(chips, pair_share, half_units)
    residual_grad, gated_grad, ffn_vec, grad_o = ffn_backward(
        length, residual, cot, ffn_in_grad, other_grad, gated_all, vectors, w_o_rows
    )
    key_scatter = [
        Scatter(grad_key[:, :, i * half : (i + 1) * half], 2 + i).prepare() for i in range(2)
    ]
    o_scatter = Scatter(grad_o.reshape(chips, pair_share, OWN), 4).prepare()
    gated_grad, *sent = meet([], gated_grad, *[m.sent[0] for m in key_scatter + [o_scatter]])
    for part, x in zip(key_scatter + [o_scatter], sent):
        part.sent = [x]
        part.step()
    ffn_scatter = key_scatter + value_scatter
    ffn_pairs = list(zip(key_scatter, value_scatter))
    terms = [*terms, gated_grad, *saved]
    zero_sums = jnp.zeros((8, OWN), jnp.float32)
    *low_grads, own_vec, _ = wkv_backward(
        0, blocks, length, used, zero_state, zero_sums, terms
    )
    *low_grads, own_vec = meet(ffn_scatter + [o_scatter], *low_grads, own_vec)
    if pair_share == 64:
        sent_a, kept_a, sent_b, kept_b = att_gradients(
            (mixes[0], mixes[2], mixes[3]), low_grads[:3]
        )
        att_scatter = [Scatter.begun(sent_a, kept_a, 2), Scatter.begun(sent_b, kept_b, 3)]
    else:
        grads = [narrow(weight_gradient(mixes[m], g)) for m, g in zip((0, 2, 3), low_grads)]
        att_scatter = [
            Scatter(jnp.concatenate(x, axis=1).reshape(chips, pair_share, 3 * quarter), 2 + i).prepare()
            for i, x in enumerate(
                ((grads[0], grads[2][:, :quarter]), (grads[1], grads[2][:, quarter:]))
            )
        ]
    own_vec, *sent = meet([], own_vec, *[m.sent[0] for m in att_scatter])
    for part, x in zip(att_scatter, sent):
        part.sent = [x]
        part.step()
    for pair in ffn_pairs:
        together(pair)
    o_scatter.step()
    token_part, misc_mine, misc_other = front_backward(
        tokens, vectors, w_r, w_k, w_v, down, up_t, (mixes[1], mixes[4], mixes[5]), hid,
        low_grads, own_vec, ffn_vec,
    )
    token_part, misc_mine, misc_other = meet(
        ffn_scatter + [o_scatter], token_part, misc_mine, misc_other
    )
    misc_sum = misc_mine + swap(misc_other, 1).astype(jnp.float32)
    misc_sum = jnp.concatenate([misc_sum[..., :320], misc_sum[..., 320:]], axis=1)
    misc_scatter = Scatter(misc_sum, 3)
    together(ffn_scatter)
    o_scatter.step()
    (token_part,) = meet(att_scatter, token_part)
    for part in att_scatter:
        part.step()
    misc_scatter.step()
    token_part, hidden = meet(ffn_scatter + [misc_scatter, o_scatter], token_part, hidden)
    misc_scatter.step()
    together(ffn_scatter)
    o_scatter.step()
    (token_part,) = meet(att_scatter + [misc_scatter], token_part)
    masks = chip_masks()
    last_parts = att_scatter + [misc_scatter]
    if len(misc_scatter.steps) == 2:
        for part in last_parts:
            part.steps = [[masks[2], masks[3], masks[2] | masks[3]]]
    together(last_parts)
    ffn_part = product(hidden, value_weight)
    input_gradient = (
        own_rows(residual_grad, core)
        + own_rows(token_part, core)
        + swap(own_rows(token_part, 1 - core), 1)
    )
    ffn_out = own_rows(ffn_part, core) + swap(own_rows(ffn_part, 1 - core), 1)
    output = narrow(jnp.where(own_rows(live, core), own_rows(residual, core) + ffn_out, 0.0))
    while ffn_scatter[0].steps:
        together(ffn_scatter)
    value_sum = jnp.concatenate(
        [x.run().total() for x in value_scatter], axis=1
    )
    key_sum = jnp.concatenate(
        [x.total() for x in key_scatter] + [o_scatter.run().total()], axis=1
    ).reshape(2, share, -1)

    def exchange(x):
        mine = lax.dynamic_index_in_dim(x, core, 0, keepdims=False)
        return mine, swap(lax.dynamic_index_in_dim(x, 1 - core, 0, keepdims=False), 1)

    key_mine, key_theirs = exchange(key_sum)
    input_gradient, value_sum, key_mine, key_theirs = meet(
        last_parts, input_gradient, value_sum, key_mine, key_theirs
    )
    while last_parts[0].steps:
        together(last_parts)
    first_sum, second_sum, misc_sum = [x.total() for x in last_parts]
    misc_sum = jnp.concatenate([misc_sum[:share], misc_sum[share:]], axis=1)
    att_sum = jnp.concatenate(
        [first_sum[:, :OWN], second_sum[:, :OWN], first_sum[:, OWN:], second_sum[:, OWN:]], axis=1
    )
    mine, theirs = exchange(att_sum.reshape(2, share, -1))
    mine = jnp.concatenate([mine, key_mine[:, half_units:]], axis=1)
    theirs = jnp.concatenate([theirs, key_theirs[:, half_units:]], axis=1)
    shard_mixer = jnp.stack(
        [
            in_order(1, mine[:, i * OWN : (i + 1) * OWN], theirs[:, i * OWN : (i + 1) * OWN], 1)
            for i in range(4)
        ]
    )
    shard_key = in_order(
        1,
        key_mine[:, :half_units].reshape(share, chips, 1, units),
        key_theirs[:, :half_units].reshape(share, chips, 1, units),
        2,
    ).reshape(share, 2 * half_units)
    return (
        output,
        input_gradient,
        shard_mixer,
        shard_key,
        value_sum,
        misc_sum[:, :256],
        misc_sum[:, 256:512].T,
        misc_sum[:, 512:530].T,
    )


def solution(mesh):
    in_specs = (
        P("dp", None),
        P(),
        P(None, "dp", None),
        P("dp", None),
        P("dp", None),
        P("dp", None),
        P(None, "dp"),
        P(None, "dp"),
        P("dp", None),
    )
    out_specs = (
        P("dp", None),
        P("dp", None),
        P(None, "dp", None),
        P("dp", None),
        P("dp", None),
        P("dp", None),
        P(None, "dp"),
        P(None, "dp"),
    )
    return jax.shard_map(local, mesh=mesh, in_specs=in_specs, out_specs=out_specs, check_vma=False)
```

```python
from functools import partial

import jax
import jax.numpy as jnp
from jax import lax
from jax.experimental import pallas as pl
from jax.experimental.pallas import tpu as pltpu
from jax.sharding import PartitionSpec as P

HEADS = 16
HEAD_SIZE = 64
DECAY_RANK = 64
RATE_RANK = 64
EMBED = 1024
OWN = EMBED // 2
PRECISE = lax.Precision.HIGHEST


CHUNK = 64
LANES = 256
GROUP_HEADS = 4
STEP_CHUNKS = 2
SMALL = pl.CostEstimate(flops=1, bytes_accessed=1, transcendentals=0)

NN = (((1,), (0,)), ((), ()))
NT = (((1,), (1,)), ((), ()))
TN = (((0,), (0,)), ((), ()))


def halves(x):
    high = x.astype(jnp.bfloat16)
    return high, (x - high.astype(jnp.float32)).astype(jnp.bfloat16)


def dot32(a, b, dims):
    return lax.dot_general(a, b, dims, preferred_element_type=jnp.float32)


def mul(left, right, dims=NN):
    rows = left[0].shape[0]
    both = dot32(jnp.concatenate(left, axis=0), right[0], dims)
    return both[:rows] + both[rows:] + dot32(left[0], right[1], dims)


def tmul(left, right, masks):
    full = (
        dot32(left[0], right[0], TN) + dot32(left[1], right[0], TN) + dot32(left[0], right[1], TN)
    )
    return sum(full[h * CHUNK : (h + 1) * CHUNK] * masks[h][:1].astype(jnp.float32) for h in range(GROUP_HEADS))


def spread(pair, masks):
    return tuple(
        jnp.concatenate([part * masks[h] for h in range(GROUP_HEADS)], axis=0) for part in pair
    )


def stack(first, second):
    return tuple(jnp.concatenate([x, y], axis=0) for x, y in zip(first, second))


def head_masks():
    lane = lax.broadcasted_iota(jnp.int32, (CHUNK, LANES), 1) // CHUNK
    return [(lane == h).astype(jnp.float32).astype(jnp.bfloat16) for h in range(GROUP_HEADS)]


def places():
    row = lax.broadcasted_iota(jnp.int32, (CHUNK, LANES), 0)
    col = lax.broadcasted_iota(jnp.int32, (CHUNK, LANES), 1) % CHUNK
    return row, col


def running_sum(x, upper=False):
    row = lax.broadcasted_iota(jnp.int32, (CHUNK, CHUNK), 0)
    col = lax.broadcasted_iota(jnp.int32, (CHUNK, CHUNK), 1)
    ones = (row <= col if upper else col <= row).astype(jnp.float32).astype(jnp.bfloat16)
    high, rest = halves(x)
    low = (x - high.astype(jnp.float32) - rest.astype(jnp.float32)).astype(jnp.bfloat16)
    return dot32(ones, high, NN) + dot32(ones, rest, NN) + dot32(ones, low, NN)


def scaled_forms(q, w, k, a, b):
    total = running_sum(w)
    before = total - w
    middle = total[CHUNK // 2 - 1 : CHUNK // 2]
    end = total[CHUNK - 1 :]
    ea = jnp.exp(before - middle)
    eq = jnp.exp(total - middle)
    eb = jnp.exp(middle - total)
    ee = jnp.exp(end - total)
    return (a * ea, q * eq, b * eb, k * eb, b * ee, k * ee), (ea, eq, eb, ee), (jnp.exp(middle), jnp.exp(end))


def each(fn, *columns):
    return [fn(*row) for row in zip(*columns)]


def block_ones():
    row = lax.broadcasted_iota(jnp.int32, (LANES, LANES), 0) // CHUNK
    col = lax.broadcasted_iota(jnp.int32, (LANES, LANES), 1) // CHUNK
    return (row == col).astype(jnp.float32).astype(jnp.bfloat16)


def head_sum(x, ones):
    rows = x.shape[0]
    both = dot32(jnp.concatenate(halves(x), axis=0), ones, NN)
    return both[:rows] + both[rows:]


def prepared(keys, decay_low, rate_low, live, vec, ones):
    sig = jax.nn.sigmoid(vec[0] + decay_low)
    log_decay = (-0.6065306597126334) * sig * live
    rates = jax.nn.sigmoid(vec[1] + rate_low)
    scaled = keys * vec[2]
    inverse = lax.rsqrt(head_sum(scaled * scaled, ones) + 1e-06)
    unit_keys = scaled * inverse
    factor = (1.0 + (rates - 1.0) * vec[3]) * live
    return log_decay, keys * factor, -unit_keys, unit_keys * rates * live, sig, rates, inverse, factor


def read_out(o, q, k, v, vec, ones):
    centred = o - head_sum(o, ones) * (1.0 / CHUNK)
    scale = lax.rsqrt(head_sum(centred * centred, ones) * (1.0 / CHUNK) + 0.00064)
    normed = centred * scale
    weight = head_sum(q * k * vec[4], ones)
    return normed, scale, weight, normed * vec[5] + vec[6] + weight * v


def unit_slices():
    return [
        (slice(c * CHUNK, (c + 1) * CHUNK), slice(g * LANES, (g + 1) * LANES))
        for c in range(STEP_CHUNKS)
        for g in range(2)
    ]


def unit_live(length, step):
    row = lax.broadcasted_iota(jnp.int32, (CHUNK, LANES), 0)
    start = step * (STEP_CHUNKS * CHUNK)
    live = [(row + (start + c * CHUNK) < length).astype(jnp.float32) for c in range(STEP_CHUNKS)]
    return [live[c] for c in range(STEP_CHUNKS) for g in range(2)]


def unit_vectors(vec_ref):
    vec = [[vec_ref[i : i + 1, g * LANES : (g + 1) * LANES] for i in range(7)] for g in range(2)]
    return [vec[g] for c in range(STEP_CHUNKS) for g in range(2)]


def forward_kernel(base, *refs):
    len_ref, vec_ref, start_ref, q_ref, keys_ref, v_ref, dl_ref, rl_ref, gate_ref = refs[:9]
    (
        out_ref, o_ref, t_ref, aqb_ref, aak_ref, aqk_ref, y_ref, z_ref, trt_ref, qe_ref, state_ref,
    ) = refs[-11:]

    @pl.when(pl.program_id(0) == 0)
    def _():
        state_ref[...] = start_ref[...]

    masks = head_masks()
    row, col = places()
    strict = (col < row).astype(jnp.float32)
    within = (col <= row).astype(jnp.float32)
    eye = (col == row).astype(jnp.float32)
    ones = block_ones()
    units = unit_slices()
    live = unit_live(len_ref[0], pl.program_id(0) + base)
    vec = unit_vectors(vec_ref)
    load = lambda ref: [ref[u] for u in units]
    q, keys, v = load(q_ref), load(keys_ref), load(v_ref)
    ready = each(
        lambda x, y, z, m, n: prepared(x, y, z, m, n, ones), keys, load(dl_ref), load(rl_ref), live, vec
    )
    w, k, a, b = ([x[i] for x in ready] for i in range(4))
    forms = each(scaled_forms, q, w, k, a, b)
    ah, qh, bh, kh, bt, kt = ([f[0][i] for f in forms] for i in range(6))
    emid = [f[2][0] for f in forms]
    eend = [f[2][1] for f in forms]
    aq = each(lambda x, y: halves(jnp.concatenate([x, y], axis=0)), ah, qh)
    with_b = each(lambda l, r: mul(l, spread(halves(r), masks), NT), aq, bh)
    with_k = each(lambda l, r: mul(l, spread(halves(r), masks), NT), aq, kh)
    aab = [x[:CHUNK] * strict for x in with_b]
    aqb = [halves(x[CHUNK:] * within) for x in with_b]
    aak = [halves(x[:CHUNK] * strict) for x in with_k]
    aqk = [halves(x[CHUNK:] * within) for x in with_k]
    p = [halves(x * (row // 8 == col // 8)) for x in aab]
    t = [eye + x * (row // 8 == col // 8) for x in aab]
    p2 = each(lambda x: halves(mul(x, spread(x, masks))), p)
    both = each(lambda x, y: mul(stack(x, halves(y)), spread(x, masks)), p2, t)
    p4 = [halves(x[:CHUNK]) for x in both]
    t = each(lambda x, y: x + y[CHUNK:], t, both)
    t = each(lambda x, y: x + mul(halves(x), spread(y, masks)), t, p4)
    for size in (8, 16, 32):
        corner = ((row // size) % 2 == 1) & (col // size == row // size - 1)
        ts = [halves(x) for x in t]
        n = [halves(x * corner) for x in aab]
        tn = each(lambda x, y: halves(mul(x, spread(y, masks))), ts, n)
        t = each(lambda x, y, z: x + mul(y, spread(z, masks)), t, tn, ts)
    ts = [halves(x) for x in t]
    vs = [halves(x) for x in v]
    vm = [spread(x, masks) for x in vs]
    wide = each(lambda x, y, e: mul(x, spread(halves(y * e), masks)), ts, ah, emid)
    r0 = each(mul, aak, vm)
    y0 = each(lambda x, y: mul(x, spread(halves(y), masks)), ts, r0)
    wides = [halves(x) for x in wide]
    qe = each(lambda x, e, y, z: x * e + mul(y, spread(z, masks)), qh, emid, aqb, wides)
    y0s = [halves(x) for x in y0]
    part = each(lambda x, y, z, u: mul(x, spread(y, masks)) + mul(z, u), aqb, y0s, aqk, vm)
    bts = [halves(x) for x in bt]
    diag = [eye * e for e in eend]
    tr = each(lambda x, y, d: tmul(x, y, masks) + d, bts, wides, diag)
    trt = each(lambda x, y, d: tmul(y, x, masks) + d, bts, wides, diag)
    inject = each(lambda x, y, z, u: tmul(stack(x, halves(y)), stack(z, u), masks), bts, kt, y0s, vs)
    wq = each(lambda x, y: stack(x, halves(y)), wides, qe)
    z = []
    out = []
    for c in range(STEP_CHUNKS):
        for g in range(2):
            i = c * 2 + g
            now = state_ref[g]
            nows = spread(halves(now), masks)
            state_ref[g] = mul(halves(tr[i]), nows) + inject[i]
            z.append(now)
            out.append(mul(wq[i], nows))
    o = each(lambda x, y: x[CHUNK:] + y, out, part)
    mixed = each(lambda x, y, z, m, n: read_out(x, y, z, m, n, ones)[3], o, q, k, v, vec)
    for i, u in enumerate(units):
        out_ref[u] = (mixed[i] * gate_ref[u]).astype(jnp.bfloat16)
        o_ref[u] = o[i]
        y_ref[u] = out[i][:CHUNK] + y0[i]
        t_ref[u] = t[i]
        aqb_ref[u] = with_b[i][CHUNK:] * within
        aak_ref[u] = with_k[i][:CHUNK] * strict
        aqk_ref[u] = with_k[i][CHUNK:] * within
        z_ref[u] = z[i]
        trt_ref[u] = trt[i]
        qe_ref[u] = qe[i]


def backward_kernel(base, *refs):
    (
        len_ref, vec_ref, start_ref, sums_ref, q_ref, keys_ref, v_ref, dl_ref, rl_ref, gate_ref,
        g_ref, o_ref, t_ref, aqb_ref, aak_ref, aqk_ref, y_ref, z_ref, trt_ref, qe_ref,
    ) = refs[:20]
    dq_ref, dkeys_ref, dv_ref, ddl_ref, drl_ref, dgate_ref, dvec_ref, state_ref = refs[-8:]
    step = base + pl.num_programs(0) - 1 - pl.program_id(0)

    @pl.when(pl.program_id(0) == 0)
    def _():
        state_ref[...] = start_ref[...]
        dvec_ref[...] = sums_ref[...]

    masks = head_masks()
    row, col = places()
    strict = (col < row).astype(jnp.float32)
    within = (col <= row).astype(jnp.float32)
    ones = block_ones()
    units = unit_slices()
    live = unit_live(len_ref[0], step)
    vec = unit_vectors(vec_ref)
    load = lambda ref: [ref[u] for u in units]
    q, keys, v, g = load(q_ref), load(keys_ref), load(v_ref), load(g_ref)
    ready = each(
        lambda x, y, z, m, n: prepared(x, y, z, m, n, ones), keys, load(dl_ref), load(rl_ref), live, vec
    )
    w, k, a, b, sig, rates, inverse, factor = ([x[i] for x in ready] for i in range(8))
    seen = each(lambda x, y, z, m, n: read_out(x, y, z, m, n, ones), load(o_ref), q, k, v, vec)
    normed, scale, weight, mixed = ([x[i] for x in seen] for i in range(4))
    gate = load(gate_ref)
    dgate = each(lambda x, y: x * y, g, mixed)
    dmix = each(lambda x, y: x * y, g, gate)
    dn = each(lambda x, n: x * n[5], dmix, vec)
    do = each(
        lambda x, n, r: r
        * (x - head_sum(x, ones) * (1.0 / CHUNK) - n * (head_sum(x * n, ones) * (1.0 / CHUNK))),
        dn, normed, scale,
    )
    dweight = each(lambda x, y: head_sum(x * y, ones), dmix, v)
    do = [halves(x) for x in do]
    qe, trt, t, aqb, aak, aqk, ys = (
        [halves(x) for x in load(ref)]
        for ref in (qe_ref, trt_ref, t_ref, aqb_ref, aak_ref, aqk_ref, y_ref)
    )
    z = load(z_ref)
    vs = [halves(x) for x in v]
    h = each(lambda x, y: tmul(x, y, masks), qe, do)
    dz = [None] * len(units)
    for c in reversed(range(STEP_CHUNKS)):
        for g in range(2):
            i = c * 2 + g
            now = state_ref[g]
            dz[i] = now
            state_ref[g] = mul(trt[i], spread(halves(now), masks)) + h[i]
    dzs = [spread(halves(x), masks) for x in dz]
    zs = [spread(halves(x), masks) for x in z]
    forms = each(scaled_forms, q, w, k, a, b)
    ah, qh, bh, kh, bt, kt = ([f[0][i] for f in forms] for i in range(6))
    ea, eq, eb, ee = ([f[1][i] for f in forms] for i in range(4))
    emid = [f[2][0] for f in forms]
    eend = [f[2][1] for f in forms]
    from_end = each(lambda x, y, s: mul(halves(jnp.concatenate([x, y], axis=0)), s), bt, kt, dzs)
    dy = each(lambda x, y, s: halves(tmul(x, y, masks) + s[:CHUNK]), aqb, do, from_end)
    dr = each(lambda x, y: halves(tmul(x, y, masks)), t, dy)
    ro = each(stack, dr, do)
    dv = each(lambda x, y, s, f: tmul(stack(x, y), s, masks) + f[CHUNK:], aak, aqk, ro, from_end)
    mask2 = jnp.concatenate([strict, within], axis=0)
    dab = each(lambda s, y: halves(mul(s, spread(y, masks), NT) * mask2), ro, ys)
    dak = each(lambda s, y: halves(mul(s, spread(y, masks), NT) * mask2), ro, vs)
    dst = each(lambda s, y: mul(s, y, NT), ro, zs)
    daq = each(
        lambda s, e, x, bb, y, kk: s * e + mul(x, spread(halves(bb), masks)) + mul(y, spread(halves(kk), masks)),
        dst, emid, dab, bh, dak, kh,
    )
    aq = each(lambda x, y: halves(jnp.concatenate([x, y], axis=0)), ah, qh)
    dbh = each(lambda x, y: tmul(x, y, masks), dab, aq)
    dkh = each(lambda x, y: tmul(x, y, masks), dak, aq)
    dend = each(lambda y, x, s: mul(stack(y, x), s, NT), ys, vs, dzs)
    row_of_ones = jnp.ones((8, LANES), jnp.bfloat16)
    sums = lambda x: jnp.sum(x, axis=0, keepdims=True)
    for i, u in enumerate(units):
        da = daq[i][:CHUNK] * ea[i]
        dq = daq[i][CHUNK:] * eq[i]
        dbt = dend[i][:CHUNK] * ee[i]
        dkt = dend[i][CHUNK:] * ee[i]
        db = dbh[i] * eb[i] + dbt
        dk = dkh[i] * eb[i] + dkt
        pa = da * a[i]
        diff = dq * q[i] - db * b[i] - dk * k[i] + pa
        zz = spread(halves(z[i] * dz[i]), masks)
        carry = (dot32(row_of_ones, zz[0], NT) + dot32(row_of_ones, zz[1], NT))[:1] * eend[i]
        carry = carry + sums(dbt * b[i] + dkt * k[i])
        dw = running_sum(diff, upper=True) - pa + carry
        from_bonus = dweight[i] * vec[i][4]
        dk = dk + from_bonus * q[i]
        dq_ref[u] = (dq + from_bonus * k[i]).astype(jnp.bfloat16)
        dv_ref[u] = (dv[i] + weight[i] * dmix[i]).astype(jnp.bfloat16)
        dgate_ref[u] = dgate[i].astype(jnp.bfloat16)
        unit_keys = -a[i]
        db = db * live[i]
        du = db * rates[i] - da
        dscaled = inverse[i] * (du - unit_keys * head_sum(du * unit_keys, ones))
        dkl = dk * keys[i] * live[i]
        drl = (db * unit_keys + dkl * vec[i][3]) * rates[i] * (1.0 - rates[i])
        ddl = dw * w[i] * (1.0 - sig[i])
        dkeys_ref[u] = (dk * factor[i] + dscaled * vec[i][2]).astype(jnp.bfloat16)
        ddl_ref[u] = ddl.astype(jnp.bfloat16)
        drl_ref[u] = drl.astype(jnp.bfloat16)
        parts = (
            ddl, drl, dscaled * keys[i], dkl * (rates[i] - 1.0),
            dweight[i] * q[i] * k[i], dmix[i] * normed[i], dmix[i],
        )
        lanes = u[1]
        for j, x in enumerate(parts):
            dvec_ref[j : j + 1, lanes] += sums(x)


def wkv_call(kernel, base, steps, small, arrays, outs, sums, previous, name):
    tokens, width = arrays[0].shape
    rows = CHUNK * STEP_CHUNKS
    last = base + steps - 1
    turned = kernel is backward_kernel
    spec = pl.BlockSpec((rows, width), lambda i: (last - i if turned else base + i, 0))
    state = pl.BlockSpec((2, CHUNK, LANES), lambda i: (0, 0, 0))
    whole = pl.BlockSpec((8, width), lambda i: (0, 0))
    shape = jax.ShapeDtypeStruct
    first = [pl.BlockSpec(memory_space=pltpu.SMEM), whole, state] + [whole] * sums
    held = list(previous or ())
    start = len(first) + len(arrays)
    return pl.pallas_call(
        partial(kernel, base),
        grid=(steps,),
        in_specs=first + [spec] * len(arrays) + [pl.BlockSpec(memory_space=pl.ANY)] * len(held),
        out_specs=[spec] * len(outs) + [whole] * sums + [state],
        out_shape=[shape((tokens, width), dtype) for dtype in outs]
        + [shape((8, width), jnp.float32)] * sums
        + [shape((2, CHUNK, LANES), jnp.float32)],
        input_output_aliases={start + i: i for i in range(len(held))},
        compiler_params=pltpu.CompilerParams(vmem_limit_bytes=60 << 20),
        cost_estimate=SMALL,
        name=name,
    )(*small, *arrays, *held)


def wkv_forward(base, steps, length, vec, state, arrays, previous=None):
    outs = [jnp.bfloat16] + [jnp.float32] * 9
    return wkv_call(
        forward_kernel, base, steps, (length, vec, state), arrays, outs, 0, previous, "wkv_forward"
    )


def wkv_backward(base, steps, length, vec, state, sums, arrays, previous=None):
    outs = [jnp.bfloat16] * 6
    return wkv_call(
        backward_kernel, base, steps, (length, vec, state, sums), arrays, outs, 1, previous,
        "wkv_backward",
    )


ROWS = 128


def row_norm(x):
    centred = x - jnp.mean(x, axis=-1, keepdims=True)
    scale = lax.rsqrt(jnp.mean(centred * centred, axis=-1, keepdims=True) + 1e-05)
    return centred * scale, scale


def shifted(x, edge, down):
    rows = x.shape[0]
    row = lax.broadcasted_iota(jnp.int32, x.shape, 0)
    if down:
        return jnp.where(row == 0, edge, pltpu.roll(x, 1, 0))
    return jnp.where(row == rows - 1, edge, pltpu.roll(x, rows - 1, 0))


def below(x, upper):
    lane = lax.broadcasted_iota(jnp.int32, x.shape, 1)
    keep = (lane >= DECAY_RANK) if upper else (lane < DECAY_RANK)
    return jnp.where(keep, x, jnp.zeros_like(x))


def front_kernel(
    x_ref, vec_ref, wr_ref, wk_ref, wv_ref, down_ref, up_ref,
    m0_ref, m1_ref, m2_ref, m3_ref, m4_ref, m5_ref,
    q_ref, k_ref, v_ref, dl_ref, rl_ref, gate_ref, hid_ref,
    edge_ref,
):
    @pl.when(pl.program_id(0) == 0)
    def _():
        edge_ref[...] = jnp.zeros_like(edge_ref)

    unit, _ = row_norm(x_ref[...].astype(jnp.float32))
    normed = unit * vec_ref[12:13] + vec_ref[13:14]
    change = shifted(normed, edge_ref[:1], True) - normed
    edge_ref[:1] = normed[ROWS - 1 :]
    mixes = []
    for j, ref in enumerate((m0_ref, m1_ref, m2_ref, m3_ref, m4_ref, m5_ref)):
        mixes.append((normed + change * vec_ref[j : j + 1]).astype(jnp.bfloat16))
        ref[...] = mixes[j]
    q_ref[...] = dot32(mixes[0], wr_ref[...], NN)
    k_ref[...] = dot32(mixes[2], wk_ref[...], NN)
    v_ref[...] = dot32(mixes[3], wv_ref[...], NN)
    first = down_ref[:, :128]
    pre_decay, pre_rate = dot32(mixes[1], first, NN), dot32(mixes[4], first, NN)
    pre_gate = dot32(mixes[5], down_ref[:, 128:], NN)
    lane = lax.broadcasted_iota(jnp.int32, pre_decay.shape, 1)
    pair = jnp.where(lane < DECAY_RANK, jnp.tanh(pre_decay), pre_rate)
    gate = jax.nn.sigmoid(pre_gate)
    hid_ref[:, :128] = pair
    hid_ref[:, 128:] = gate
    narrow_pair = pair.astype(jnp.bfloat16)
    dl_ref[...] = dot32(below(narrow_pair, False), up_ref[:, :128], NT)
    rl_ref[...] = dot32(below(narrow_pair, True), up_ref[:, :128], NT)
    gate_ref[...] = dot32(gate.astype(jnp.bfloat16), up_ref[:, 128:], NT)


def front_forward(x, vectors, w_r, w_k, w_v, down, up):
    tokens, width = x.shape
    wide = pl.BlockSpec((ROWS, width), lambda i: (i, 0))
    own = pl.BlockSpec((ROWS, OWN), lambda i: (i, 0))
    hid = pl.BlockSpec((ROWS, 256), lambda i: (i, 0))
    whole = lambda a: pl.BlockSpec(a.shape, lambda i: (0, 0))
    shape = jax.ShapeDtypeStruct
    return pl.pallas_call(
        front_kernel,
        grid=(tokens // ROWS,),
        in_specs=[wide] + [whole(a) for a in (vectors, w_r, w_k, w_v, down, up)],
        out_specs=[wide] * 6 + [own] * 6 + [hid],
        out_shape=[shape((tokens, width), jnp.bfloat16)] * 6
        + [shape((tokens, OWN), jnp.float32)] * 6
        + [shape((tokens, 256), jnp.float32)],
        scratch_shapes=[pltpu.VMEM((8, width), jnp.float32)],
        compiler_params=pltpu.CompilerParams(vmem_limit_bytes=60 << 20),
        cost_estimate=SMALL,
        name="front_forward",
    )(x, vectors, w_r, w_k, w_v, down, up)


def front_back_kernel(
    x_ref, before_ref, vec_ref, wr_ref, wk_ref, wv_ref, down_ref, up_ref,
    m1_ref, m4_ref, m5_ref, hid_ref,
    dq_ref, dk_ref, dv_ref, ddl_ref, drl_ref, dgate_ref, own_vec_ref, ffn_vec_ref,
    dx_ref, mine_ref, other_ref,
    edge_ref, sums_ref, misc_ref,
):
    step = pl.num_programs(0) - 1 - pl.program_id(0)
    core = lax.axis_index("dp") % 2
    own_start = pl.multiple_of(core * OWN, OWN)

    @pl.when(pl.program_id(0) == 0)
    def _():
        edge_ref[...] = jnp.zeros_like(edge_ref)
        sums_ref[...] = jnp.zeros_like(sums_ref)
        misc_ref[...] = jnp.zeros_like(misc_ref)

    unit, scale = row_norm(x_ref[...].astype(jnp.float32))
    gain, offset = vec_ref[12:13], vec_ref[13:14]
    normed = unit * gain + offset
    tail, _ = row_norm(before_ref[...].astype(jnp.float32))
    edge = (tail[15:] * gain + offset) * jnp.where(step == 0, 0.0, 1.0)
    change = shifted(normed, edge, True) - normed
    ddl, drl, dgate = ddl_ref[...], drl_ref[...], dgate_ref[...]
    hid = hid_ref[...]
    pair, gate = hid[:, :128], hid[:, 128:]
    lane = lax.broadcasted_iota(jnp.int32, pair.shape, 1)
    first_up, last_up = up_ref[:, :128], up_ref[:, 128:]
    pair_grad = jnp.where(
        lane < DECAY_RANK,
        dot32(ddl, first_up, NN) * (1.0 - pair * pair),
        dot32(drl, first_up, NN),
    ).astype(jnp.bfloat16)
    gate_grad = (dot32(dgate, last_up, NN) * gate * (1.0 - gate)).astype(jnp.bfloat16)
    narrow_pair, narrow_gate = pair.astype(jnp.bfloat16), gate.astype(jnp.bfloat16)
    own_rows = pl.ds(own_start, OWN)
    misc_ref[own_rows, 256:384] += dot32(ddl, below(narrow_pair, False), TN) + dot32(
        drl, below(narrow_pair, True), TN
    )
    misc_ref[own_rows, 384:512] += dot32(dgate, narrow_gate, TN)
    decay_part, rate_part = below(pair_grad, False), below(pair_grad, True)
    misc_ref[:, :128] += dot32(m1_ref[...], decay_part, TN) + dot32(m4_ref[...], rate_part, TN)
    misc_ref[:, 128:256] += dot32(m5_ref[...], gate_grad, TN)
    first_down = down_ref[:, :128]
    grads = (
        lambda: dot32(dq_ref[...], wr_ref[...], NT),
        lambda: dot32(decay_part, first_down, NT),
        lambda: dot32(dk_ref[...], wk_ref[...], NT),
        lambda: dot32(dv_ref[...], wv_ref[...], NT),
        lambda: dot32(rate_part, first_down, NT),
        lambda: dot32(gate_grad, down_ref[:, 128:], NT),
    )
    total = jnp.zeros_like(change)
    moved = jnp.zeros_like(change)
    for j, grad in enumerate(grads):
        now = grad()
        total = total + now
        moved = moved + now * vec_ref[j : j + 1]
        sums_ref[j : j + 1] += jnp.sum(now * change, axis=0, keepdims=True)
    dnormed = total - moved + shifted(moved, edge_ref[:1], False)
    edge_ref[:1] = moved[:1]
    sums_ref[12:13] += jnp.sum(dnormed * unit, axis=0, keepdims=True)
    sums_ref[13:14] += jnp.sum(dnormed, axis=0, keepdims=True)
    dunit = dnormed * gain
    dx_ref[...] = scale * (
        dunit
        - jnp.mean(dunit, axis=-1, keepdims=True)
        - unit * jnp.mean(dunit * unit, axis=-1, keepdims=True)
    )

    @pl.when(step == 0)
    def _():
        sums_ref[6:7] = ffn_vec_ref[0:1] * 0.5
        sums_ref[14:16] = ffn_vec_ref[1:3] * 0.5
        zeros = jnp.zeros((1, OWN), jnp.float32)
        for target, source in ((7, 0), (8, 1), (9, 2), (10, 3), (11, 4), (16, 5), (17, 6)):
            mine = own_vec_ref[source : source + 1]
            sums_ref[target : target + 1] = jnp.concatenate(
                [jnp.where(core == 0, mine, zeros), jnp.where(core == 0, zeros, mine)], axis=1
            )
        for block in range(EMBED // 128):
            lanes = slice(block * 128, (block + 1) * 128)
            misc_ref[lanes, 512:640] = sums_ref[:, lanes].T
        share = mine_ref.shape[1]
        for chip in range(mine_ref.shape[0]):
            low = misc_ref[2 * chip * share : (2 * chip + 1) * share]
            high = misc_ref[(2 * chip + 1) * share : (2 * chip + 2) * share]
            mine_ref[chip] = jnp.where(core == 0, low, high)
            other_ref[chip] = jnp.where(core == 0, high, low).astype(jnp.bfloat16)


def front_backward(
    x, vectors, w_r, w_k, w_v, down, up, mixes, hid, grads, own_vec, ffn_vec
):
    tokens, width = x.shape
    devices = lax.axis_size("dp")
    pieces = (devices // 2, EMBED // devices, 640)
    steps = tokens // ROWS
    wide = pl.BlockSpec((ROWS, width), lambda i: (steps - 1 - i, 0))
    before = pl.BlockSpec(
        (16, width), lambda i: (jnp.maximum((steps - 1 - i) * (ROWS // 16) - 1, 0), 0)
    )
    own = pl.BlockSpec((ROWS, OWN), lambda i: (steps - 1 - i, 0))
    hid_spec = pl.BlockSpec((ROWS, 256), lambda i: (steps - 1 - i, 0))
    whole = lambda a: pl.BlockSpec(a.shape, lambda i: (0, 0))
    shape = jax.ShapeDtypeStruct
    return pl.pallas_call(
        front_back_kernel,
        grid=(steps,),
        in_specs=[wide, before]
        + [whole(a) for a in (vectors, w_r, w_k, w_v, down, up)]
        + [wide] * 3
        + [hid_spec]
        + [own] * 6
        + [whole(own_vec), whole(ffn_vec)],
        out_specs=[wide] + [pl.BlockSpec(pieces, lambda i: (0, 0, 0))] * 2,
        out_shape=[
            shape((tokens, width), jnp.float32),
            shape(pieces, jnp.float32),
            shape(pieces, jnp.bfloat16),
        ],
        scratch_shapes=[
            pltpu.VMEM((8, width), jnp.float32),
            pltpu.VMEM((128, width), jnp.float32),
            pltpu.VMEM((EMBED, 640), jnp.float32),
        ],
        compiler_params=pltpu.CompilerParams(vmem_limit_bytes=60 << 20),
        cost_estimate=SMALL,
        name="front_backward",
    )(x, x, vectors, w_r, w_k, w_v, down, up, *mixes, hid, *grads, own_vec, ffn_vec)


def ffn_back_kernel(
    len_ref, res_ref, before_ref, cot_ref, mine_ref, other_ref, vec_ref, wo_ref,
    grad_ref, narrow_ref, gated_ref, dvec_ref,
    edge_ref,
):
    step = pl.num_programs(0) - 1 - pl.program_id(0)

    @pl.when(pl.program_id(0) == 0)
    def _():
        edge_ref[...] = jnp.zeros_like(edge_ref)
        dvec_ref[...] = jnp.zeros_like(dvec_ref)

    gain, offset, coefficient = vec_ref[14:15], vec_ref[15:16], vec_ref[6:7]
    unit, scale = row_norm(res_ref[...])
    normed = unit * gain + offset
    tail, _ = row_norm(before_ref[...])
    edge = (tail[7:] * gain + offset) * jnp.where(step == 0, 0.0, 1.0)
    change = shifted(normed, edge, True) - normed
    grad = mine_ref[...].astype(jnp.float32) + other_ref[...].astype(jnp.float32)
    moved = grad * coefficient
    dnormed = grad - moved + shifted(moved, edge_ref[:1], False)
    edge_ref[:1] = moved[:1]
    sums = lambda x: jnp.sum(x, axis=0, keepdims=True)
    dvec_ref[0:1] += sums(grad * change)
    dvec_ref[1:2] += sums(dnormed * unit)
    dvec_ref[2:3] += sums(dnormed)
    dunit = dnormed * gain
    row = lax.broadcasted_iota(jnp.int32, grad.shape, 0) + step * ROWS
    out_grad = jnp.where(row < len_ref[0], cot_ref[...].astype(jnp.float32), 0.0)
    total = out_grad + scale * (
        dunit
        - jnp.mean(dunit, axis=-1, keepdims=True)
        - unit * jnp.mean(dunit * unit, axis=-1, keepdims=True)
    )
    grad_ref[...] = total
    small = total.astype(jnp.bfloat16)
    core = lax.axis_index("dp") % 2
    narrow_ref[...] = jnp.where(core == 0, small[:, :OWN], small[:, OWN:])
    gated_ref[...] = dot32(small, wo_ref[...], NT)


def ffn_backward(length, residual, cot, mine, other, vectors, w_o_rows):
    tokens, width = residual.shape
    steps = tokens // ROWS
    wide = pl.BlockSpec((ROWS, width), lambda i: (steps - 1 - i, 0))
    before = pl.BlockSpec(
        (8, width), lambda i: (jnp.maximum((steps - 1 - i) * (ROWS // 8) - 1, 0), 0)
    )
    own = pl.BlockSpec((ROWS, OWN), lambda i: (steps - 1 - i, 0))
    whole = lambda a: pl.BlockSpec(a.shape, lambda i: (0, 0))
    shape = jax.ShapeDtypeStruct
    return pl.pallas_call(
        ffn_back_kernel,
        grid=(steps,),
        in_specs=[pl.BlockSpec(memory_space=pltpu.SMEM), wide, before]
        + [wide] * 3
        + [whole(vectors), whole(w_o_rows)],
        out_specs=[wide, own, own, pl.BlockSpec((8, width), lambda i: (0, 0))],
        out_shape=[
            shape((tokens, width), jnp.float32),
            shape((tokens, OWN), jnp.bfloat16),
            shape((tokens, OWN), jnp.float32),
            shape((8, width), jnp.float32),
        ],
        scratch_shapes=[pltpu.VMEM((8, width), jnp.float32)],
        compiler_params=pltpu.CompilerParams(vmem_limit_bytes=60 << 20),
        cost_estimate=SMALL,
        name="ffn_backward",
    )(length, residual, residual, cot, mine, other, vectors, w_o_rows)


def att_grad_kernel(m0_ref, m2_ref, m3_ref, gated_ref, dq_ref, dk_ref, dv_ref, do_ref,
                    send_a, keep_a, send_b, keep_b):
    chip = lax.axis_index("dp") // 2
    by_x, by_y = chip % 2 == 0, (chip // 2) % 2 == 0
    first = ((m0_ref, dq_ref), (gated_ref, do_ref))
    second = ((m2_ref, dk_ref), (m3_ref, dv_ref))
    for half in range(2):
        lanes = slice(half * OWN, (half + 1) * OWN)
        block = dot32(first[half][0][...], first[half][1][...], TN).astype(jnp.bfloat16)
        for y in range(2):
            low, high = block[y * 128 : y * 128 + 64], block[y * 128 + 64 : y * 128 + 128]
            send_a[y, :, lanes] = jnp.where(by_x, high, low)
            keep_a[y, :, lanes] = jnp.where(by_x, low, high)
        block = dot32(second[half][0][...], second[half][1][...], TN).astype(jnp.bfloat16)
        for x in range(2):
            low, high = block[x * 64 : x * 64 + 64], block[128 + x * 64 : 128 + x * 64 + 64]
            send_b[x, :, lanes] = jnp.where(by_y, high, low)
            keep_b[x, :, lanes] = jnp.where(by_y, low, high)


def att_gradients(mixes, gated, grads, own_grad):
    tokens = gated.shape[0]
    left = pl.BlockSpec((tokens, 256), lambda i: (0, i))
    right = pl.BlockSpec((tokens, OWN), lambda i: (0, 0))
    out = pl.BlockSpec((2, 64, 2 * OWN), lambda i: (i, 0, 0))
    return pl.pallas_call(
        att_grad_kernel,
        grid=(4,),
        in_specs=[left] * 4 + [right] * 4,
        out_specs=[out] * 4,
        out_shape=[jax.ShapeDtypeStruct((8, 64, 2 * OWN), jnp.bfloat16)] * 4,
        compiler_params=pltpu.CompilerParams(vmem_limit_bytes=60 << 20),
        cost_estimate=SMALL,
        name="att_gradients",
    )(*mixes, gated, *grads, own_grad)


def swap(block, mask):
    size = lax.axis_size("dp")
    return lax.ppermute(block, "dp", [(i, i ^ mask) for i in range(size)])


def bit_of(mask):
    return (lax.axis_index("dp") // mask) % 2


def in_order(mask, own, other, axis):
    lower = bit_of(mask) == 0
    return jnp.where(
        lower, jnp.concatenate([own, other], axis=axis), jnp.concatenate([other, own], axis=axis)
    )


def chip_masks():
    size = lax.axis_size("dp")
    masks = []
    while 2 << len(masks) < size:
        masks.append(2 << len(masks))
    return masks


def steps_of(kind):
    masks = chip_masks()
    near, far = [[mask] for mask in masks[:2]], [[mask] for mask in masks[2:][::-1]]
    first = [[far[0][0], far[1][0], far[0][0] | far[1][0]]] if len(far) == 2 else far
    return [first + near[::-1], first + near, far + near[::-1], far + near, near + far][kind]


class Held:
    def __init__(self, value):
        self.value = value


def meet(movers, *arrays):
    held = []
    for mover in movers:
        held += [x[0] for x in mover.arrived if x[0] not in held]
    out = lax.optimization_barrier(tuple(x.value for x in held) + arrays)
    for x, value in zip(held, out):
        x.value = value
    return out[len(held) :]


def read(arrived):
    return [x.value if lanes is None else x.value[..., lanes] for x, lanes in arrived]


class Gather:
    def __init__(self, block, kind, places=(0,)):
        self.steps = steps_of(kind)
        self.held = block[None]
        self.places = [0]
        self.arrived = []
        self.masks = []

    def merge(self):
        if self.arrived:
            self.held = jnp.concatenate([self.held] + read(self.arrived), axis=0)
            self.places = self.places + [p ^ (m // 2) for m in self.masks for p in self.places]
            self.arrived = []

    def step(self):
        if self.steps:
            self.merge()
            self.masks = self.steps.pop(0)
            self.arrived = [(Held(swap(self.held, mask)), None) for mask in self.masks]
        return self

    def run(self):
        while self.steps:
            self.step()
        return self

    def split(self, kinds):
        width = self.held.shape[-1] // len(kinds)
        out = []
        for i, kind in enumerate(kinds):
            part = Gather.__new__(Gather)
            cut = slice(i * width, (i + 1) * width)
            part.steps = steps_of(kind)[len(steps_of(kind)) - len(self.steps) :]
            part.held = self.held[..., cut]
            part.arrived = [(x, cut) for x, _ in self.arrived]
            part.places, part.masks = self.places, self.masks
            out.append(part)
        return out


def place_kernel(places, cuts, *refs):
    sources, outs = refs[: len(places)], refs[len(places) :]
    chip = lax.axis_index("dp") // 2
    for source, (part, list_of) in zip(sources, places):
        for j, place in enumerate(list_of):
            for out, (first, rows, lanes) in zip(outs, cuts):
                start = pl.multiple_of((chip ^ place) * rows, rows)
                lane, width = lanes[part]
                at = sum(w for _, w in lanes[:part])
                out[pl.ds(start, rows), at : at + width] = source[
                    j, first : first + rows, lane : lane + width
                ]


def assemble(gathers, cuts=None):
    gathers = [g.run() for g in gathers]
    rows = gathers[0].held.shape[1]
    cuts = cuts or ((0, rows, [(0, g.held.shape[2]) for g in gathers]),)
    sources, places = [], []
    for i, g in enumerate(gathers):
        sources += [g.held] + read(g.arrived)
        shifts = [0] + [mask // 2 for mask in g.masks]
        places += [(i, [p ^ shift for p in g.places]) for shift in shifts]
    count = lax.axis_size("dp") // 2
    if any(cut[1] % 16 for cut in cuts):
        return assemble_plain(sources, places, cuts, count)
    space = pl.BlockSpec(memory_space=pltpu.VMEM)
    return pl.pallas_call(
        partial(place_kernel, places, cuts),
        in_specs=[space] * len(sources),
        out_specs=[space] * len(cuts),
        out_shape=[
            jax.ShapeDtypeStruct((count * n, sum(w for _, w in lanes)), sources[0].dtype)
            for _, n, lanes in cuts
        ],
        compiler_params=pltpu.CompilerParams(vmem_limit_bytes=32 << 20),
        cost_estimate=SMALL,
        name="assemble",
    )(*sources)


def assemble_plain(sources, places, cuts, count):
    chip = lax.axis_index("dp") // 2
    parts = []
    for part in sorted({part for part, _ in places}):
        blocks = jnp.concatenate([x for x, (at, _) in zip(sources, places) if at == part])
        where = [p for at, list_of in places if at == part for p in list_of]
        blocks = jnp.stack([blocks[where.index(i)] for i in range(count)])
        parts.append(jnp.take(blocks, chip ^ lax.iota(jnp.int32, count), axis=0))
    return [
        jnp.concatenate(
            [x[:, first : first + n, at : at + w] for x, (at, w) in zip(parts, lanes)], axis=-1
        ).reshape(count * n, -1)
        for first, n, lanes in cuts
    ]


class Scatter:
    def __init__(self, parts, kind):
        self.steps = steps_of(kind)[::-1]
        self.axes = chip_masks()[::-1]
        self.sources = [parts.reshape((2,) * len(self.axes) + parts.shape[1:])]
        self.arrived = []
        self.sent = None

    @classmethod
    def begun(cls, sent, kept, kind):
        out = cls.__new__(cls)
        out.steps = steps_of(kind)[::-1]
        out.axes = [axis for axis in chip_masks()[::-1] if axis != out.steps[0][0]]
        out.sources = [kept.reshape((2,) * len(out.axes) + kept.shape[1:])]
        out.arrived = []
        out.sent = [sent.reshape(out.sources[0].shape)]
        return out

    def pick(self, sources, mask, gone):
        out = []
        for x in sources:
            for place in reversed(range(len(self.axes))):
                axis = self.axes[place]
                if axis in gone:
                    which = bit_of(axis) if not mask & axis else 1 - bit_of(axis)
                    x = lax.dynamic_index_in_dim(x, which, place, keepdims=False)
            out.append(x)
        return out

    def prepare(self):
        if self.sent is not None:
            return self
        masks = self.steps[0]
        sources = self.sources + read(self.arrived)
        gone = [axis for axis in self.axes if any(mask & axis for mask in masks)]
        self.sent = [
            sum(x.astype(jnp.float32) for x in self.pick(sources, mask, gone)).astype(jnp.bfloat16)
            for mask in masks
        ]
        self.sources = self.pick(sources, 0, gone)
        self.axes = [axis for axis in self.axes if axis not in gone]
        self.arrived = []
        return self

    def step(self):
        return together([self])[0]

    def run(self):
        while self.steps:
            self.step()
        return self

    def total(self):
        return sum(x.astype(jnp.float32) for x in self.sources + read(self.arrived))


def together(parts):
    if not parts[0].steps:
        return parts
    for part in parts:
        part.prepare()
    for i, mask in enumerate(parts[0].steps[0]):
        sent = [part.sent[i] for part in parts]
        got = Held(swap(sent[0] if len(sent) == 1 else jnp.concatenate(sent, axis=-1), mask))
        at = 0
        for part, x in zip(parts, sent):
            lanes = slice(at, at + x.shape[-1]) if len(sent) > 1 else None
            part.arrived.append((got, lanes))
            at += x.shape[-1]
    for part in parts:
        part.steps.pop(0)
        part.sent_now, part.sent = part.sent[0], None
    return parts


def norm_rows(features, gain_row, offset_row):
    average = jnp.mean(features, axis=-1, keepdims=True)
    centred = features - average
    variance = jnp.mean(centred * centred, axis=-1, keepdims=True)
    return centred * lax.rsqrt(variance + 1e-05) * gain_row + offset_row


def product(operand, weight_matrix):
    return jnp.dot(operand, weight_matrix, preferred_element_type=jnp.float32)


def input_gradient_rows(upstream_gradient, weight_matrix):
    return lax.dot_general(
        upstream_gradient,
        weight_matrix,
        (((1,), (1,)), ((), ())),
        preferred_element_type=jnp.float32,
    )


def weight_gradient(operand, upstream_gradient):
    return lax.dot_general(
        operand, upstream_gradient, (((0,), (0,)), ((), ())), preferred_element_type=jnp.float32
    )


def earlier(rows):
    return jnp.concatenate([jnp.zeros_like(rows[:1]), rows[:-1]], axis=0)


def ffn_mix(residual, vectors):
    second = norm_rows(residual, vectors[14], vectors[15])
    return second + (earlier(second) - second) * vectors[6]


def narrow(x):
    return x.astype(jnp.bfloat16)


def local(
    inputs,
    lengths,
    attention_projections,
    channel_key_weight,
    channel_value_weight,
    lowrank_down_weight,
    lowrank_up_weight,
    per_feature_parameters,
    cotangent,
):
    devices = lax.axis_size("dp")
    chips = devices // 2
    device = lax.axis_index("dp")
    chip, core = device // 2, device % 2
    row_count = inputs.shape[0]
    slots = 2 * row_count
    share = EMBED // devices
    pair_share = 2 * share
    units = channel_value_weight.shape[0]
    half_units = chips * units

    def own_cut(x, which):
        return lax.dynamic_slice_in_dim(x, which * OWN, OWN, x.ndim - 1)

    def own_rows(x, which):
        return lax.dynamic_slice_in_dim(x, which * row_count, row_count, 0)

    pair_rows = in_order(
        1,
        own_cut(attention_projections, core),
        swap(own_cut(attention_projections, 1 - core), 1),
        1,
    )
    lora = jnp.concatenate([lowrank_down_weight, lowrank_up_weight.T], axis=1)
    vector_rows = jnp.pad(per_feature_parameters.T, ((0, 0), (0, 128 - 18)))
    vector_rows = vector_rows.reshape(share // 4, OWN)
    first_rows = 3 * pair_share
    misc_rows = share + share // 4 + (share // 4) % 16
    block = jnp.concatenate(
        [
            pair_rows[:3].reshape(first_rows, OWN),
            lora,
            jnp.pad(vector_rows, ((0, (share // 4) % 16), (0, 0))),
        ],
        axis=0,
    )
    half = half_units // 2
    quarter = OWN // 2
    first = Gather(block, 0).step()
    w_o_part = Gather(pair_rows[3], 4).step().step()
    key_in, raw, cot, _ = meet([], channel_key_weight, inputs, cotangent, first.held)
    key_cut = key_in.reshape(share, chips, 2, units)

    def key_columns(which):
        return lax.dynamic_index_in_dim(key_cut, which, 2, keepdims=False).reshape(share, half_units)

    key_rows = in_order(1, key_columns(core), swap(key_columns(1 - core), 1), 0)
    tokens = in_order(1, raw, swap(raw, 1), 0)
    cot = in_order(1, cot, swap(cot, 1), 0)
    key_rows, tokens, cot = meet([first, w_o_part], key_rows, tokens, cot)
    first = first.split((0, 1))
    for part in first:
        part.step()
    key_part = Gather(key_rows, 2).step()
    (tokens,) = meet(first, tokens)
    for part in first:
        part.step()
    value_block, *_ = meet([key_part], channel_value_weight, *[part.held for part in first])
    key_part.step()
    value_part = Gather(value_block, 2).step()
    w_o_part.step()
    (tokens,) = meet(first + [key_part, value_part], tokens)
    key_parts = key_part.split((2, 3))
    for part in key_parts:
        part.step()
    w_r, w_k, w_v, misc = assemble(
        first,
        [(i * pair_share, pair_share, [(0, quarter)] * 2) for i in range(3)]
        + [(first_rows, misc_rows, [(0, quarter)] * 2)],
    )
    misc = misc.reshape(chips, 1, misc_rows, OWN)
    misc = in_order(1, misc, swap(misc, 1), 1)
    value_part.step()
    lora = misc[:, :, :share].reshape(EMBED, OWN)
    down, up_t = lora[:, :256], lax.dynamic_slice_in_dim(lora[:, 256:], core * OWN, OWN, 0)
    vectors = misc[:, :, share : share + share // 4].reshape(EMBED, 128)[:, :18].T
    vectors = vectors.astype(jnp.float32)
    own_vectors = own_cut(vectors, core)
    used = jnp.concatenate([own_vectors[7:12], own_vectors[16:18], own_vectors[:1]], axis=0)
    length = lax.dynamic_index_in_dim(lengths, chip, 0)
    live = (lax.iota(jnp.int32, slots) < length)[:, None]

    *mixes, queries, keys, values, decay_low, rate_low, gate_rows, hid = front_forward(
        tokens, vectors, w_r, w_k, w_v, down, up_t
    )
    terms = meet(
        key_parts + [value_part, w_o_part],
        queries, keys, values, decay_low, rate_low, gate_rows,
    )
    value_parts = value_part.split((2, 3))
    for part in key_parts + value_parts:
        part.step()
    w_o_part.step()
    blocks = slots // (CHUNK * STEP_CHUNKS)
    zero_state = jnp.zeros((2, CHUNK, LANES), jnp.float32)
    gated, *saved, _ = wkv_forward(0, blocks, length, used, zero_state, terms)
    gated, cot, tokens = meet(key_parts + value_parts + [w_o_part], gated, cot, tokens)
    for part in value_parts:
        part.step()
    gated, *_ = meet([], gated, *[part.held for part in value_parts])
    gated_all = in_order(1, gated, swap(gated, 1), 1)
    (w_o_own,) = assemble([w_o_part])
    w_o = in_order(1, w_o_own, swap(w_o_own, 1), 1)
    (key_weight,) = assemble(key_parts)
    residual = tokens.astype(jnp.float32) + product(gated_all, w_o)
    ffn_in = narrow(ffn_mix(residual, vectors))
    positive = jax.nn.relu(product(ffn_in, key_weight))
    hidden = narrow(jnp.square(positive))
    out_narrow = jnp.where(live, cot, jnp.zeros_like(cot))
    grad_value = narrow(weight_gradient(hidden, out_narrow)).reshape(chips, units, EMBED)
    w_o_rows = lax.dynamic_slice_in_dim(w_o, core * OWN, OWN, 0)
    value_scatter = [
        Scatter(grad_value[..., i * OWN : (i + 1) * OWN], 2 + i).prepare() for i in range(2)
    ]
    hidden, positive, out_narrow, w_o_rows, *sent = meet(
        value_parts, hidden, positive, out_narrow, w_o_rows, *[m.sent[0] for m in value_scatter]
    )
    for part, x in zip(value_scatter, sent):
        part.sent = [x]
        part.step()
    (value_weight,) = assemble(value_parts)

    pre_narrow = narrow(2.0 * positive * input_gradient_rows(out_narrow, value_weight))
    ffn_in_grad = narrow(input_gradient_rows(pre_narrow, key_weight))
    other_grad = swap(ffn_in_grad, 1)
    grad_key = narrow(weight_gradient(ffn_in, pre_narrow)).reshape(chips, pair_share, half_units)
    residual_grad, own_grad, gated_grad, ffn_vec = ffn_backward(
        length, residual, cot, ffn_in_grad, other_grad, vectors, w_o_rows
    )
    key_scatter = [
        Scatter(grad_key[:, :, i * half : (i + 1) * half], 2 + i).prepare() for i in range(2)
    ]
    gated_grad, *sent = meet([], gated_grad, *[m.sent[0] for m in key_scatter])
    for part, x in zip(key_scatter, sent):
        part.sent = [x]
        part.step()
    terms = [*terms, gated_grad, *saved]
    zero_sums = jnp.zeros((8, OWN), jnp.float32)
    early = blocks // 2
    *before, sums, state = wkv_backward(
        early, blocks - early, length, used, zero_state, zero_sums, terms
    )
    state, sums = meet(value_scatter, state, sums)
    for part in value_scatter:
        part.step()
    *low_grads, own_vec, _ = wkv_backward(0, early, length, used, state, sums, terms, before)
    if pair_share == 64:
        sent_a, kept_a, sent_b, kept_b = att_gradients(
            (mixes[0], mixes[2], mixes[3]), gated_all, low_grads[:3], own_grad
        )
        att_scatter = [Scatter.begun(sent_a, kept_a, 2), Scatter.begun(sent_b, kept_b, 3)]
    else:
        grads = [weight_gradient(mixes[m], g) for m, g in zip((0, 2, 3), low_grads)]
        grad_o = weight_gradient(gated_all, own_grad)
        att_scatter = [
            Scatter(
                narrow(jnp.concatenate(x, axis=1)).reshape(chips, pair_share, EMBED), 2 + i
            ).prepare()
            for i, x in enumerate(((grads[0], grad_o), (grads[1], grads[2])))
        ]
    own_vec, *sent = meet(
        key_scatter + value_scatter, own_vec, *[m.sent[0] for m in att_scatter]
    )
    for part, x in zip(att_scatter, sent):
        part.sent = [x]
        part.step()
    for part in key_scatter:
        part.step()
    together(value_scatter)
    own_vec, *_ = meet([], own_vec, *[m.sent_now for m in key_scatter])
    token_part, misc_mine, misc_other = front_backward(
        tokens, vectors, w_r, w_k, w_v, down, up_t, (mixes[1], mixes[4], mixes[5]), hid,
        low_grads, own_vec, ffn_vec,
    )
    misc_other = swap(misc_other, 1)
    token_part, misc_mine, misc_other = meet(
        att_scatter + key_scatter + value_scatter, token_part, misc_mine, misc_other
    )
    for part in att_scatter:
        part.step()
    misc_sum = misc_mine + misc_other.astype(jnp.float32)
    misc_sum = jnp.concatenate([misc_sum[..., :320], misc_sum[..., 320:]], axis=1)
    misc_scatter = Scatter(misc_sum, 3).step()
    together(key_scatter)
    together(value_scatter)
    token_part, hidden = meet(key_scatter + [misc_scatter], token_part, hidden)
    misc_scatter.step()
    together(key_scatter)
    (token_part,) = meet(att_scatter + [misc_scatter], token_part)
    masks = chip_masks()
    last_parts = att_scatter + [misc_scatter]
    if len(misc_scatter.steps) == 2:
        for part in last_parts:
            part.steps = [[masks[2], masks[3], masks[2] | masks[3]]]
    together(last_parts)
    ffn_part = product(hidden, value_weight)
    input_gradient = (
        own_rows(residual_grad, core)
        + own_rows(token_part, core)
        + swap(own_rows(token_part, 1 - core), 1)
    )
    ffn_out = own_rows(ffn_part, core) + swap(own_rows(ffn_part, 1 - core), 1)
    output = narrow(jnp.where(own_rows(live, core), own_rows(residual, core) + ffn_out, 0.0))
    value_sum = jnp.concatenate(
        [x.run().total() for x in value_scatter], axis=1
    )
    while key_scatter[0].steps:
        together(key_scatter)
    key_sum = jnp.concatenate([x.total() for x in key_scatter], axis=1).reshape(2, share, -1)

    def exchange(x):
        mine = lax.dynamic_index_in_dim(x, core, 0, keepdims=False)
        return mine, swap(lax.dynamic_index_in_dim(x, 1 - core, 0, keepdims=False), 1)

    key_mine, key_theirs = exchange(key_sum)
    input_gradient, value_sum, key_mine, key_theirs = meet(
        last_parts, input_gradient, value_sum, key_mine, key_theirs
    )
    while last_parts[0].steps:
        together(last_parts)
    first_sum, second_sum, misc_sum = [x.total() for x in last_parts]
    misc_sum = jnp.concatenate([misc_sum[:share], misc_sum[share:]], axis=1)
    att_sum = jnp.concatenate(
        [first_sum[:, :OWN], second_sum, first_sum[:, OWN:]], axis=1
    )
    mine, theirs = exchange(att_sum.reshape(2, share, -1))
    shard_mixer = jnp.stack(
        [
            in_order(1, mine[:, i * OWN : (i + 1) * OWN], theirs[:, i * OWN : (i + 1) * OWN], 1)
            for i in range(4)
        ]
    )
    shard_key = in_order(
        1,
        key_mine.reshape(share, chips, 1, units),
        key_theirs.reshape(share, chips, 1, units),
        2,
    ).reshape(share, 2 * half_units)
    return (
        output,
        input_gradient,
        shard_mixer,
        shard_key,
        value_sum,
        misc_sum[:, :256],
        misc_sum[:, 256:512].T,
        misc_sum[:, 512:530].T,
    )


def solution(mesh):
    in_specs = (
        P("dp", None),
        P(),
        P(None, "dp", None),
        P("dp", None),
        P("dp", None),
        P("dp", None),
        P(None, "dp"),
        P(None, "dp"),
        P("dp", None),
    )
    out_specs = (
        P("dp", None),
        P("dp", None),
        P(None, "dp", None),
        P("dp", None),
        P("dp", None),
        P("dp", None),
        P(None, "dp"),
        P(None, "dp"),
    )
    return jax.shard_map(local, mesh=mesh, in_specs=in_specs, out_specs=out_specs, check_vma=False)
```

```python
from functools import partial

import jax
import jax.numpy as jnp
from jax import lax
from jax.experimental import pallas as pl
from jax.experimental.pallas import tpu as pltpu
from jax.sharding import PartitionSpec as P

HEADS = 16
HEAD_SIZE = 64
DECAY_RANK = 64
RATE_RANK = 64
EMBED = 1024
OWN = EMBED // 2
PRECISE = lax.Precision.HIGHEST


CHUNK = 64
LANES = 256
GROUP_HEADS = 4
STEP_CHUNKS = 2
SMALL = pl.CostEstimate(flops=1, bytes_accessed=1, transcendentals=0)

NN = (((1,), (0,)), ((), ()))
NT = (((1,), (1,)), ((), ()))
TN = (((0,), (0,)), ((), ()))


def halves(x):
    high = x.astype(jnp.bfloat16)
    return high, (x - high.astype(jnp.float32)).astype(jnp.bfloat16)


def dot32(a, b, dims):
    return lax.dot_general(a, b, dims, preferred_element_type=jnp.float32)


def mul(left, right, dims=NN):
    rows = left[0].shape[0]
    both = dot32(jnp.concatenate(left, axis=0), right[0], dims)
    return both[:rows] + both[rows:] + dot32(left[0], right[1], dims)


def tmul(left, right, masks):
    full = (
        dot32(left[0], right[0], TN) + dot32(left[1], right[0], TN) + dot32(left[0], right[1], TN)
    )
    return sum(full[h * CHUNK : (h + 1) * CHUNK] * masks[h][:1].astype(jnp.float32) for h in range(GROUP_HEADS))


def spread(pair, masks):
    return tuple(
        jnp.concatenate([part * masks[h] for h in range(GROUP_HEADS)], axis=0) for part in pair
    )


def stack(first, second):
    return tuple(jnp.concatenate([x, y], axis=0) for x, y in zip(first, second))


def head_masks():
    lane = lax.broadcasted_iota(jnp.int32, (CHUNK, LANES), 1) // CHUNK
    return [(lane == h).astype(jnp.float32).astype(jnp.bfloat16) for h in range(GROUP_HEADS)]


def places():
    row = lax.broadcasted_iota(jnp.int32, (CHUNK, LANES), 0)
    col = lax.broadcasted_iota(jnp.int32, (CHUNK, LANES), 1) % CHUNK
    return row, col


def running_sum(x, upper=False):
    row = lax.broadcasted_iota(jnp.int32, (CHUNK, CHUNK), 0)
    col = lax.broadcasted_iota(jnp.int32, (CHUNK, CHUNK), 1)
    ones = (row <= col if upper else col <= row).astype(jnp.float32).astype(jnp.bfloat16)
    high, rest = halves(x)
    low = (x - high.astype(jnp.float32) - rest.astype(jnp.float32)).astype(jnp.bfloat16)
    return dot32(ones, high, NN) + dot32(ones, rest, NN) + dot32(ones, low, NN)


def scaled_forms(q, w, k, a, b):
    total = running_sum(w)
    before = total - w
    middle = total[CHUNK // 2 - 1 : CHUNK // 2]
    end = total[CHUNK - 1 :]
    ea = jnp.exp(before - middle)
    eq = jnp.exp(total - middle)
    eb = jnp.exp(middle - total)
    ee = jnp.exp(end - total)
    return (a * ea, q * eq, b * eb, k * eb, b * ee, k * ee), (ea, eq, eb, ee), (jnp.exp(middle), jnp.exp(end))


def each(fn, *columns):
    return [fn(*row) for row in zip(*columns)]


def block_ones():
    row = lax.broadcasted_iota(jnp.int32, (LANES, LANES), 0) // CHUNK
    col = lax.broadcasted_iota(jnp.int32, (LANES, LANES), 1) // CHUNK
    return (row == col).astype(jnp.float32).astype(jnp.bfloat16)


def head_sum(x, ones):
    rows = x.shape[0]
    both = dot32(jnp.concatenate(halves(x), axis=0), ones, NN)
    return both[:rows] + both[rows:]


def prepared(keys, decay_low, rate_low, live, vec, ones):
    sig = jax.nn.sigmoid(vec[0] + decay_low)
    log_decay = (-0.6065306597126334) * sig * live
    rates = jax.nn.sigmoid(vec[1] + rate_low)
    scaled = keys * vec[2]
    inverse = lax.rsqrt(head_sum(scaled * scaled, ones) + 1e-06)
    unit_keys = scaled * inverse
    factor = (1.0 + (rates - 1.0) * vec[3]) * live
    return log_decay, keys * factor, -unit_keys, unit_keys * rates * live, sig, rates, inverse, factor


def read_out(o, q, k, v, vec, ones):
    centred = o - head_sum(o, ones) * (1.0 / CHUNK)
    scale = lax.rsqrt(head_sum(centred * centred, ones) * (1.0 / CHUNK) + 0.00064)
    normed = centred * scale
    weight = head_sum(q * k * vec[4], ones)
    return normed, scale, weight, normed * vec[5] + vec[6] + weight * v


def unit_slices():
    return [
        (slice(c * CHUNK, (c + 1) * CHUNK), slice(g * LANES, (g + 1) * LANES))
        for c in range(STEP_CHUNKS)
        for g in range(2)
    ]


def unit_live(length, step):
    row = lax.broadcasted_iota(jnp.int32, (CHUNK, LANES), 0)
    start = step * (STEP_CHUNKS * CHUNK)
    live = [(row + (start + c * CHUNK) < length).astype(jnp.float32) for c in range(STEP_CHUNKS)]
    return [live[c] for c in range(STEP_CHUNKS) for g in range(2)]


def unit_vectors(vec_ref):
    vec = [[vec_ref[i : i + 1, g * LANES : (g + 1) * LANES] for i in range(7)] for g in range(2)]
    return [vec[g] for c in range(STEP_CHUNKS) for g in range(2)]


def forward_kernel(base, *refs):
    len_ref, vec_ref, start_ref, q_ref, keys_ref, v_ref, dl_ref, rl_ref, gate_ref = refs[:9]
    (
        out_ref, o_ref, t_ref, aqb_ref, aak_ref, aqk_ref, y_ref, z_ref, trt_ref, qe_ref, state_ref,
    ) = refs[-11:]

    @pl.when(pl.program_id(0) == 0)
    def _():
        state_ref[...] = start_ref[...]

    masks = head_masks()
    row, col = places()
    strict = (col < row).astype(jnp.float32)
    within = (col <= row).astype(jnp.float32)
    eye = (col == row).astype(jnp.float32)
    ones = block_ones()
    units = unit_slices()
    live = unit_live(len_ref[0], pl.program_id(0) + base)
    vec = unit_vectors(vec_ref)
    load = lambda ref: [ref[u] for u in units]
    q, keys, v = load(q_ref), load(keys_ref), load(v_ref)
    ready = each(
        lambda x, y, z, m, n: prepared(x, y, z, m, n, ones), keys, load(dl_ref), load(rl_ref), live, vec
    )
    w, k, a, b = ([x[i] for x in ready] for i in range(4))
    forms = each(scaled_forms, q, w, k, a, b)
    ah, qh, bh, kh, bt, kt = ([f[0][i] for f in forms] for i in range(6))
    emid = [f[2][0] for f in forms]
    eend = [f[2][1] for f in forms]
    aq = each(lambda x, y: halves(jnp.concatenate([x, y], axis=0)), ah, qh)
    with_b = each(lambda l, r: mul(l, spread(halves(r), masks), NT), aq, bh)
    with_k = each(lambda l, r: mul(l, spread(halves(r), masks), NT), aq, kh)
    aab = [x[:CHUNK] * strict for x in with_b]
    aqb = [halves(x[CHUNK:] * within) for x in with_b]
    aak = [halves(x[:CHUNK] * strict) for x in with_k]
    aqk = [halves(x[CHUNK:] * within) for x in with_k]
    p = [halves(x * (row // 8 == col // 8)) for x in aab]
    t = [eye + x * (row // 8 == col // 8) for x in aab]
    p2 = each(lambda x: halves(mul(x, spread(x, masks))), p)
    both = each(lambda x, y: mul(stack(x, halves(y)), spread(x, masks)), p2, t)
    p4 = [halves(x[:CHUNK]) for x in both]
    t = each(lambda x, y: x + y[CHUNK:], t, both)
    t = each(lambda x, y: x + mul(halves(x), spread(y, masks)), t, p4)
    for size in (8, 16, 32):
        corner = ((row // size) % 2 == 1) & (col // size == row // size - 1)
        ts = [halves(x) for x in t]
        n = [halves(x * corner) for x in aab]
        tn = each(lambda x, y: halves(mul(x, spread(y, masks))), ts, n)
        t = each(lambda x, y, z: x + mul(y, spread(z, masks)), t, tn, ts)
    ts = [halves(x) for x in t]
    vs = [halves(x) for x in v]
    vm = [spread(x, masks) for x in vs]
    wide = each(lambda x, y, e: mul(x, spread(halves(y * e), masks)), ts, ah, emid)
    r0 = each(mul, aak, vm)
    y0 = each(lambda x, y: mul(x, spread(halves(y), masks)), ts, r0)
    wides = [halves(x) for x in wide]
    qe = each(lambda x, e, y, z: x * e + mul(y, spread(z, masks)), qh, emid, aqb, wides)
    y0s = [halves(x) for x in y0]
    part = each(lambda x, y, z, u: mul(x, spread(y, masks)) + mul(z, u), aqb, y0s, aqk, vm)
    bts = [halves(x) for x in bt]
    diag = [eye * e for e in eend]
    tr = each(lambda x, y, d: tmul(x, y, masks) + d, bts, wides, diag)
    trt = each(lambda x, y, d: tmul(y, x, masks) + d, bts, wides, diag)
    inject = each(lambda x, y, z, u: tmul(stack(x, halves(y)), stack(z, u), masks), bts, kt, y0s, vs)
    wq = each(lambda x, y: stack(x, halves(y)), wides, qe)
    z = []
    out = []
    for c in range(STEP_CHUNKS):
        for g in range(2):
            i = c * 2 + g
            now = state_ref[g]
            nows = spread(halves(now), masks)
            state_ref[g] = mul(halves(tr[i]), nows) + inject[i]
            z.append(now)
            out.append(mul(wq[i], nows))
    o = each(lambda x, y: x[CHUNK:] + y, out, part)
    mixed = each(lambda x, y, z, m, n: read_out(x, y, z, m, n, ones)[3], o, q, k, v, vec)
    for i, u in enumerate(units):
        out_ref[u] = (mixed[i] * gate_ref[u]).astype(jnp.bfloat16)
        o_ref[u] = o[i]
        y_ref[u] = out[i][:CHUNK] + y0[i]
        t_ref[u] = t[i]
        aqb_ref[u] = with_b[i][CHUNK:] * within
        aak_ref[u] = with_k[i][:CHUNK] * strict
        aqk_ref[u] = with_k[i][CHUNK:] * within
        z_ref[u] = z[i]
        trt_ref[u] = trt[i]
        qe_ref[u] = qe[i]


def backward_kernel(base, *refs):
    (
        len_ref, vec_ref, start_ref, sums_ref, q_ref, keys_ref, v_ref, dl_ref, rl_ref, gate_ref,
        g_ref, o_ref, t_ref, aqb_ref, aak_ref, aqk_ref, y_ref, z_ref, trt_ref, qe_ref,
    ) = refs[:20]
    dq_ref, dkeys_ref, dv_ref, ddl_ref, drl_ref, dgate_ref, dvec_ref, state_ref = refs[-8:]
    step = base + pl.num_programs(0) - 1 - pl.program_id(0)

    @pl.when(pl.program_id(0) == 0)
    def _():
        state_ref[...] = start_ref[...]
        dvec_ref[...] = sums_ref[...]

    masks = head_masks()
    row, col = places()
    strict = (col < row).astype(jnp.float32)
    within = (col <= row).astype(jnp.float32)
    ones = block_ones()
    units = unit_slices()
    live = unit_live(len_ref[0], step)
    vec = unit_vectors(vec_ref)
    load = lambda ref: [ref[u] for u in units]
    q, keys, v, g = load(q_ref), load(keys_ref), load(v_ref), load(g_ref)
    ready = each(
        lambda x, y, z, m, n: prepared(x, y, z, m, n, ones), keys, load(dl_ref), load(rl_ref), live, vec
    )
    w, k, a, b, sig, rates, inverse, factor = ([x[i] for x in ready] for i in range(8))
    seen = each(lambda x, y, z, m, n: read_out(x, y, z, m, n, ones), load(o_ref), q, k, v, vec)
    normed, scale, weight, mixed = ([x[i] for x in seen] for i in range(4))
    gate = load(gate_ref)
    dgate = each(lambda x, y: x * y, g, mixed)
    dmix = each(lambda x, y: x * y, g, gate)
    dn = each(lambda x, n: x * n[5], dmix, vec)
    do = each(
        lambda x, n, r: r
        * (x - head_sum(x, ones) * (1.0 / CHUNK) - n * (head_sum(x * n, ones) * (1.0 / CHUNK))),
        dn, normed, scale,
    )
    dweight = each(lambda x, y: head_sum(x * y, ones), dmix, v)
    do = [halves(x) for x in do]
    qe, trt, t, aqb, aak, aqk, ys = (
        [halves(x) for x in load(ref)]
        for ref in (qe_ref, trt_ref, t_ref, aqb_ref, aak_ref, aqk_ref, y_ref)
    )
    z = load(z_ref)
    vs = [halves(x) for x in v]
    h = each(lambda x, y: tmul(x, y, masks), qe, do)
    dz = [None] * len(units)
    for c in reversed(range(STEP_CHUNKS)):
        for g in range(2):
            i = c * 2 + g
            now = state_ref[g]
            dz[i] = now
            state_ref[g] = mul(trt[i], spread(halves(now), masks)) + h[i]
    dzs = [spread(halves(x), masks) for x in dz]
    zs = [spread(halves(x), masks) for x in z]
    forms = each(scaled_forms, q, w, k, a, b)
    ah, qh, bh, kh, bt, kt = ([f[0][i] for f in forms] for i in range(6))
    ea, eq, eb, ee = ([f[1][i] for f in forms] for i in range(4))
    emid = [f[2][0] for f in forms]
    eend = [f[2][1] for f in forms]
    from_end = each(lambda x, y, s: mul(halves(jnp.concatenate([x, y], axis=0)), s), bt, kt, dzs)
    dy = each(lambda x, y, s: halves(tmul(x, y, masks) + s[:CHUNK]), aqb, do, from_end)
    dr = each(lambda x, y: halves(tmul(x, y, masks)), t, dy)
    ro = each(stack, dr, do)
    dv = each(lambda x, y, s, f: tmul(stack(x, y), s, masks) + f[CHUNK:], aak, aqk, ro, from_end)
    mask2 = jnp.concatenate([strict, within], axis=0)
    dab = each(lambda s, y: halves(mul(s, spread(y, masks), NT) * mask2), ro, ys)
    dak = each(lambda s, y: halves(mul(s, spread(y, masks), NT) * mask2), ro, vs)
    dst = each(lambda s, y: mul(s, y, NT), ro, zs)
    daq = each(
        lambda s, e, x, bb, y, kk: s * e + mul(x, spread(halves(bb), masks)) + mul(y, spread(halves(kk), masks)),
        dst, emid, dab, bh, dak, kh,
    )
    aq = each(lambda x, y: halves(jnp.concatenate([x, y], axis=0)), ah, qh)
    dbh = each(lambda x, y: tmul(x, y, masks), dab, aq)
    dkh = each(lambda x, y: tmul(x, y, masks), dak, aq)
    dend = each(lambda y, x, s: mul(stack(y, x), s, NT), ys, vs, dzs)
    row_of_ones = jnp.ones((8, LANES), jnp.bfloat16)
    sums = lambda x: jnp.sum(x, axis=0, keepdims=True)
    for i, u in enumerate(units):
        da = daq[i][:CHUNK] * ea[i]
        dq = daq[i][CHUNK:] * eq[i]
        dbt = dend[i][:CHUNK] * ee[i]
        dkt = dend[i][CHUNK:] * ee[i]
        db = dbh[i] * eb[i] + dbt
        dk = dkh[i] * eb[i] + dkt
        pa = da * a[i]
        diff = dq * q[i] - db * b[i] - dk * k[i] + pa
        zz = spread(halves(z[i] * dz[i]), masks)
        carry = (dot32(row_of_ones, zz[0], NT) + dot32(row_of_ones, zz[1], NT))[:1] * eend[i]
        carry = carry + sums(dbt * b[i] + dkt * k[i])
        dw = running_sum(diff, upper=True) - pa + carry
        from_bonus = dweight[i] * vec[i][4]
        dk = dk + from_bonus * q[i]
        dq_ref[u] = (dq + from_bonus * k[i]).astype(jnp.bfloat16)
        dv_ref[u] = (dv[i] + weight[i] * dmix[i]).astype(jnp.bfloat16)
        dgate_ref[u] = dgate[i].astype(jnp.bfloat16)
        unit_keys = -a[i]
        db = db * live[i]
        du = db * rates[i] - da
        dscaled = inverse[i] * (du - unit_keys * head_sum(du * unit_keys, ones))
        dkl = dk * keys[i] * live[i]
        drl = (db * unit_keys + dkl * vec[i][3]) * rates[i] * (1.0 - rates[i])
        ddl = dw * w[i] * (1.0 - sig[i])
        dkeys_ref[u] = (dk * factor[i] + dscaled * vec[i][2]).astype(jnp.bfloat16)
        ddl_ref[u] = ddl.astype(jnp.bfloat16)
        drl_ref[u] = drl.astype(jnp.bfloat16)
        parts = (
            ddl, drl, dscaled * keys[i], dkl * (rates[i] - 1.0),
            dweight[i] * q[i] * k[i], dmix[i] * normed[i], dmix[i],
        )
        lanes = u[1]
        for j, x in enumerate(parts):
            dvec_ref[j : j + 1, lanes] += sums(x)


def wkv_call(kernel, base, steps, small, arrays, outs, sums, previous, name):
    tokens, width = arrays[0].shape
    rows = CHUNK * STEP_CHUNKS
    last = base + steps - 1
    turned = kernel is backward_kernel
    spec = pl.BlockSpec((rows, width), lambda i: (last - i if turned else base + i, 0))
    state = pl.BlockSpec((2, CHUNK, LANES), lambda i: (0, 0, 0))
    whole = pl.BlockSpec((8, width), lambda i: (0, 0))
    shape = jax.ShapeDtypeStruct
    first = [pl.BlockSpec(memory_space=pltpu.SMEM), whole, state] + [whole] * sums
    held = list(previous or ())
    start = len(first) + len(arrays)
    return pl.pallas_call(
        partial(kernel, base),
        grid=(steps,),
        in_specs=first + [spec] * len(arrays) + [pl.BlockSpec(memory_space=pl.ANY)] * len(held),
        out_specs=[spec] * len(outs) + [whole] * sums + [state],
        out_shape=[shape((tokens, width), dtype) for dtype in outs]
        + [shape((8, width), jnp.float32)] * sums
        + [shape((2, CHUNK, LANES), jnp.float32)],
        input_output_aliases={start + i: i for i in range(len(held))},
        compiler_params=pltpu.CompilerParams(vmem_limit_bytes=60 << 20),
        cost_estimate=SMALL,
        name=name,
    )(*small, *arrays, *held)


def wkv_forward(base, steps, length, vec, state, arrays, previous=None):
    outs = [jnp.bfloat16] + [jnp.float32] * 9
    return wkv_call(
        forward_kernel, base, steps, (length, vec, state), arrays, outs, 0, previous, "wkv_forward"
    )


def wkv_backward(base, steps, length, vec, state, sums, arrays, previous=None):
    outs = [jnp.bfloat16] * 6
    return wkv_call(
        backward_kernel, base, steps, (length, vec, state, sums), arrays, outs, 1, previous,
        "wkv_backward",
    )


ROWS = 128


def row_norm(x):
    centred = x - jnp.mean(x, axis=-1, keepdims=True)
    scale = lax.rsqrt(jnp.mean(centred * centred, axis=-1, keepdims=True) + 1e-05)
    return centred * scale, scale


def shifted(x, edge, down):
    rows = x.shape[0]
    row = lax.broadcasted_iota(jnp.int32, x.shape, 0)
    if down:
        return jnp.where(row == 0, edge, pltpu.roll(x, 1, 0))
    return jnp.where(row == rows - 1, edge, pltpu.roll(x, rows - 1, 0))


def below(x, upper):
    lane = lax.broadcasted_iota(jnp.int32, x.shape, 1)
    keep = (lane >= DECAY_RANK) if upper else (lane < DECAY_RANK)
    return jnp.where(keep, x, jnp.zeros_like(x))


def front_kernel(
    x_ref, vec_ref, wr_ref, wk_ref, wv_ref, down_ref, up_ref,
    m0_ref, m1_ref, m2_ref, m3_ref, m4_ref, m5_ref,
    q_ref, k_ref, v_ref, dl_ref, rl_ref, gate_ref, hid_ref,
    edge_ref,
):
    @pl.when(pl.program_id(0) == 0)
    def _():
        edge_ref[...] = jnp.zeros_like(edge_ref)

    unit, _ = row_norm(x_ref[...].astype(jnp.float32))
    normed = unit * vec_ref[12:13] + vec_ref[13:14]
    change = shifted(normed, edge_ref[:1], True) - normed
    edge_ref[:1] = normed[ROWS - 1 :]
    mixes = []
    for j, ref in enumerate((m0_ref, m1_ref, m2_ref, m3_ref, m4_ref, m5_ref)):
        mixes.append((normed + change * vec_ref[j : j + 1]).astype(jnp.bfloat16))
        ref[...] = mixes[j]
    q_ref[...] = dot32(mixes[0], wr_ref[...], NN)
    k_ref[...] = dot32(mixes[2], wk_ref[...], NN)
    v_ref[...] = dot32(mixes[3], wv_ref[...], NN)
    first = down_ref[:, :128]
    pre_decay, pre_rate = dot32(mixes[1], first, NN), dot32(mixes[4], first, NN)
    pre_gate = dot32(mixes[5], down_ref[:, 128:], NN)
    lane = lax.broadcasted_iota(jnp.int32, pre_decay.shape, 1)
    pair = jnp.where(lane < DECAY_RANK, jnp.tanh(pre_decay), pre_rate)
    gate = jax.nn.sigmoid(pre_gate)
    hid_ref[:, :128] = pair
    hid_ref[:, 128:] = gate
    narrow_pair = pair.astype(jnp.bfloat16)
    dl_ref[...] = dot32(below(narrow_pair, False), up_ref[:, :128], NT)
    rl_ref[...] = dot32(below(narrow_pair, True), up_ref[:, :128], NT)
    gate_ref[...] = dot32(gate.astype(jnp.bfloat16), up_ref[:, 128:], NT)


def front_forward(x, vectors, w_r, w_k, w_v, down, up):
    tokens, width = x.shape
    wide = pl.BlockSpec((ROWS, width), lambda i: (i, 0))
    own = pl.BlockSpec((ROWS, OWN), lambda i: (i, 0))
    hid = pl.BlockSpec((ROWS, 256), lambda i: (i, 0))
    whole = lambda a: pl.BlockSpec(a.shape, lambda i: (0, 0))
    shape = jax.ShapeDtypeStruct
    return pl.pallas_call(
        front_kernel,
        grid=(tokens // ROWS,),
        in_specs=[wide] + [whole(a) for a in (vectors, w_r, w_k, w_v, down, up)],
        out_specs=[wide] * 6 + [own] * 6 + [hid],
        out_shape=[shape((tokens, width), jnp.bfloat16)] * 6
        + [shape((tokens, OWN), jnp.float32)] * 6
        + [shape((tokens, 256), jnp.float32)],
        scratch_shapes=[pltpu.VMEM((8, width), jnp.float32)],
        compiler_params=pltpu.CompilerParams(vmem_limit_bytes=60 << 20),
        cost_estimate=SMALL,
        name="front_forward",
    )(x, vectors, w_r, w_k, w_v, down, up)


def attend_kernel(
    own_ref, other_ref, w_own_ref, w_other_ref, x_ref, vec_ref,
    res_ref, ffn_ref, all_ref, rows_ref,
    edge_ref,
):
    core = lax.axis_index("dp") % 2
    own_rows = pl.ds(pl.multiple_of(core * OWN, OWN), OWN)
    other_rows = pl.ds(pl.multiple_of((1 - core) * OWN, OWN), OWN)

    def ordered(x, y):
        return jnp.concatenate([jnp.where(core == 0, x, y), jnp.where(core == 0, y, x)], axis=1)

    @pl.when(pl.program_id(0) == 0)
    def _():
        edge_ref[...] = jnp.zeros_like(edge_ref)
        rows_ref[...] = ordered(w_own_ref[own_rows], w_other_ref[own_rows])

    own, other = own_ref[...], other_ref[...]
    all_ref[...] = ordered(own, other)
    parts = [
        dot32(own, ref[own_rows], NN) + dot32(other, ref[other_rows], NN)
        for ref in (w_own_ref, w_other_ref)
    ]
    residual = x_ref[...].astype(jnp.float32) + ordered(*parts)
    res_ref[...] = residual
    unit, _ = row_norm(residual)
    normed = unit * vec_ref[14:15] + vec_ref[15:16]
    change = shifted(normed, edge_ref[:1], True) - normed
    edge_ref[:1] = normed[ROWS - 1 :]
    ffn_ref[...] = (normed + change * vec_ref[6:7]).astype(jnp.bfloat16)


def attend(own, other, w_own, w_other, x, vectors):
    tokens, width = x.shape
    wide = pl.BlockSpec((ROWS, width), lambda i: (i, 0))
    half = pl.BlockSpec((ROWS, OWN), lambda i: (i, 0))
    whole = lambda a: pl.BlockSpec(a.shape, lambda i: (0, 0))
    shape = jax.ShapeDtypeStruct
    return pl.pallas_call(
        attend_kernel,
        grid=(tokens // ROWS,),
        in_specs=[half, half, whole(w_own), whole(w_other), wide, whole(vectors)],
        out_specs=[wide] * 3 + [pl.BlockSpec((OWN, width), lambda i: (0, 0))],
        out_shape=[
            shape((tokens, width), jnp.float32),
            shape((tokens, width), jnp.bfloat16),
            shape((tokens, width), jnp.bfloat16),
            shape((OWN, width), jnp.bfloat16),
        ],
        scratch_shapes=[pltpu.VMEM((8, width), jnp.float32)],
        compiler_params=pltpu.CompilerParams(vmem_limit_bytes=60 << 20),
        cost_estimate=SMALL,
        name="attend",
    )(own, other, w_own, w_other, x, vectors)


def front_back_kernel(
    x_ref, before_ref, vec_ref, wr_ref, wk_ref, wv_ref, down_ref, up_ref,
    m1_ref, m4_ref, m5_ref, hid_ref,
    dq_ref, dk_ref, dv_ref, ddl_ref, drl_ref, dgate_ref, own_vec_ref, ffn_vec_ref,
    dx_ref, mine_ref, other_ref,
    edge_ref, sums_ref, misc_ref,
):
    step = pl.num_programs(0) - 1 - pl.program_id(0)
    core = lax.axis_index("dp") % 2
    own_start = pl.multiple_of(core * OWN, OWN)

    @pl.when(pl.program_id(0) == 0)
    def _():
        edge_ref[...] = jnp.zeros_like(edge_ref)
        sums_ref[...] = jnp.zeros_like(sums_ref)
        misc_ref[...] = jnp.zeros_like(misc_ref)

    unit, scale = row_norm(x_ref[...].astype(jnp.float32))
    gain, offset = vec_ref[12:13], vec_ref[13:14]
    normed = unit * gain + offset
    tail, _ = row_norm(before_ref[...].astype(jnp.float32))
    edge = (tail[15:] * gain + offset) * jnp.where(step == 0, 0.0, 1.0)
    change = shifted(normed, edge, True) - normed
    ddl, drl, dgate = ddl_ref[...], drl_ref[...], dgate_ref[...]
    hid = hid_ref[...]
    pair, gate = hid[:, :128], hid[:, 128:]
    lane = lax.broadcasted_iota(jnp.int32, pair.shape, 1)
    first_up, last_up = up_ref[:, :128], up_ref[:, 128:]
    pair_grad = jnp.where(
        lane < DECAY_RANK,
        dot32(ddl, first_up, NN) * (1.0 - pair * pair),
        dot32(drl, first_up, NN),
    ).astype(jnp.bfloat16)
    gate_grad = (dot32(dgate, last_up, NN) * gate * (1.0 - gate)).astype(jnp.bfloat16)
    narrow_pair, narrow_gate = pair.astype(jnp.bfloat16), gate.astype(jnp.bfloat16)
    own_rows = pl.ds(own_start, OWN)
    misc_ref[own_rows, 256:384] += dot32(ddl, below(narrow_pair, False), TN) + dot32(
        drl, below(narrow_pair, True), TN
    )
    misc_ref[own_rows, 384:512] += dot32(dgate, narrow_gate, TN)
    decay_part, rate_part = below(pair_grad, False), below(pair_grad, True)
    misc_ref[:, :128] += dot32(m1_ref[...], decay_part, TN) + dot32(m4_ref[...], rate_part, TN)
    misc_ref[:, 128:256] += dot32(m5_ref[...], gate_grad, TN)
    first_down = down_ref[:, :128]
    grads = (
        lambda: dot32(dq_ref[...], wr_ref[...], NT),
        lambda: dot32(decay_part, first_down, NT),
        lambda: dot32(dk_ref[...], wk_ref[...], NT),
        lambda: dot32(dv_ref[...], wv_ref[...], NT),
        lambda: dot32(rate_part, first_down, NT),
        lambda: dot32(gate_grad, down_ref[:, 128:], NT),
    )
    total = jnp.zeros_like(change)
    moved = jnp.zeros_like(change)
    for j, grad in enumerate(grads):
        now = grad()
        total = total + now
        moved = moved + now * vec_ref[j : j + 1]
        sums_ref[j : j + 1] += jnp.sum(now * change, axis=0, keepdims=True)
    dnormed = total - moved + shifted(moved, edge_ref[:1], False)
    edge_ref[:1] = moved[:1]
    sums_ref[12:13] += jnp.sum(dnormed * unit, axis=0, keepdims=True)
    sums_ref[13:14] += jnp.sum(dnormed, axis=0, keepdims=True)
    dunit = dnormed * gain
    dx_ref[...] = scale * (
        dunit
        - jnp.mean(dunit, axis=-1, keepdims=True)
        - unit * jnp.mean(dunit * unit, axis=-1, keepdims=True)
    )

    @pl.when(step == 0)
    def _():
        sums_ref[6:7] = ffn_vec_ref[0:1] * 0.5
        sums_ref[14:16] = ffn_vec_ref[1:3] * 0.5
        zeros = jnp.zeros((1, OWN), jnp.float32)
        for target, source in ((7, 0), (8, 1), (9, 2), (10, 3), (11, 4), (16, 5), (17, 6)):
            mine = own_vec_ref[source : source + 1]
            sums_ref[target : target + 1] = jnp.concatenate(
                [jnp.where(core == 0, mine, zeros), jnp.where(core == 0, zeros, mine)], axis=1
            )
        for block in range(EMBED // 128):
            lanes = slice(block * 128, (block + 1) * 128)
            misc_ref[lanes, 512:640] = sums_ref[:, lanes].T
        share = mine_ref.shape[1]
        for chip in range(mine_ref.shape[0]):
            low = misc_ref[2 * chip * share : (2 * chip + 1) * share]
            high = misc_ref[(2 * chip + 1) * share : (2 * chip + 2) * share]
            mine_ref[chip] = jnp.where(core == 0, low, high)
            other_ref[chip] = jnp.where(core == 0, high, low).astype(jnp.bfloat16)


def front_backward(
    x, vectors, w_r, w_k, w_v, down, up, mixes, hid, grads, own_vec, ffn_vec
):
    tokens, width = x.shape
    devices = lax.axis_size("dp")
    pieces = (devices // 2, EMBED // devices, 640)
    steps = tokens // ROWS
    wide = pl.BlockSpec((ROWS, width), lambda i: (steps - 1 - i, 0))
    before = pl.BlockSpec(
        (16, width), lambda i: (jnp.maximum((steps - 1 - i) * (ROWS // 16) - 1, 0), 0)
    )
    own = pl.BlockSpec((ROWS, OWN), lambda i: (steps - 1 - i, 0))
    hid_spec = pl.BlockSpec((ROWS, 256), lambda i: (steps - 1 - i, 0))
    whole = lambda a: pl.BlockSpec(a.shape, lambda i: (0, 0))
    shape = jax.ShapeDtypeStruct
    return pl.pallas_call(
        front_back_kernel,
        grid=(steps,),
        in_specs=[wide, before]
        + [whole(a) for a in (vectors, w_r, w_k, w_v, down, up)]
        + [wide] * 3
        + [hid_spec]
        + [own] * 6
        + [whole(own_vec), whole(ffn_vec)],
        out_specs=[wide] + [pl.BlockSpec(pieces, lambda i: (0, 0, 0))] * 2,
        out_shape=[
            shape((tokens, width), jnp.float32),
            shape(pieces, jnp.float32),
            shape(pieces, jnp.bfloat16),
        ],
        scratch_shapes=[
            pltpu.VMEM((8, width), jnp.float32),
            pltpu.VMEM((128, width), jnp.float32),
            pltpu.VMEM((EMBED, 640), jnp.float32),
        ],
        compiler_params=pltpu.CompilerParams(vmem_limit_bytes=60 << 20),
        cost_estimate=SMALL,
        name="front_backward",
    )(x, x, vectors, w_r, w_k, w_v, down, up, *mixes, hid, *grads, own_vec, ffn_vec)


def ffn_back_kernel(
    len_ref, res_ref, before_ref, cot_ref, mine_ref, other_ref, vec_ref, wo_ref,
    grad_ref, narrow_ref, gated_ref, dvec_ref,
    edge_ref,
):
    step = pl.num_programs(0) - 1 - pl.program_id(0)

    @pl.when(pl.program_id(0) == 0)
    def _():
        edge_ref[...] = jnp.zeros_like(edge_ref)
        dvec_ref[...] = jnp.zeros_like(dvec_ref)

    gain, offset, coefficient = vec_ref[14:15], vec_ref[15:16], vec_ref[6:7]
    unit, scale = row_norm(res_ref[...])
    normed = unit * gain + offset
    tail, _ = row_norm(before_ref[...])
    edge = (tail[7:] * gain + offset) * jnp.where(step == 0, 0.0, 1.0)
    change = shifted(normed, edge, True) - normed
    grad = mine_ref[...].astype(jnp.float32) + other_ref[...].astype(jnp.float32)
    moved = grad * coefficient
    dnormed = grad - moved + shifted(moved, edge_ref[:1], False)
    edge_ref[:1] = moved[:1]
    sums = lambda x: jnp.sum(x, axis=0, keepdims=True)
    dvec_ref[0:1] += sums(grad * change)
    dvec_ref[1:2] += sums(dnormed * unit)
    dvec_ref[2:3] += sums(dnormed)
    dunit = dnormed * gain
    row = lax.broadcasted_iota(jnp.int32, grad.shape, 0) + step * ROWS
    out_grad = jnp.where(row < len_ref[0], cot_ref[...].astype(jnp.float32), 0.0)
    total = out_grad + scale * (
        dunit
        - jnp.mean(dunit, axis=-1, keepdims=True)
        - unit * jnp.mean(dunit * unit, axis=-1, keepdims=True)
    )
    grad_ref[...] = total
    small = total.astype(jnp.bfloat16)
    core = lax.axis_index("dp") % 2
    narrow_ref[...] = jnp.where(core == 0, small[:, :OWN], small[:, OWN:])
    gated_ref[...] = dot32(small, wo_ref[...], NT)


def ffn_backward(length, residual, cot, mine, other, vectors, w_o_rows):
    tokens, width = residual.shape
    steps = tokens // ROWS
    wide = pl.BlockSpec((ROWS, width), lambda i: (steps - 1 - i, 0))
    before = pl.BlockSpec(
        (8, width), lambda i: (jnp.maximum((steps - 1 - i) * (ROWS // 8) - 1, 0), 0)
    )
    own = pl.BlockSpec((ROWS, OWN), lambda i: (steps - 1 - i, 0))
    whole = lambda a: pl.BlockSpec(a.shape, lambda i: (0, 0))
    shape = jax.ShapeDtypeStruct
    return pl.pallas_call(
        ffn_back_kernel,
        grid=(steps,),
        in_specs=[pl.BlockSpec(memory_space=pltpu.SMEM), wide, before]
        + [wide] * 3
        + [whole(vectors), whole(w_o_rows)],
        out_specs=[wide, own, own, pl.BlockSpec((8, width), lambda i: (0, 0))],
        out_shape=[
            shape((tokens, width), jnp.float32),
            shape((tokens, OWN), jnp.bfloat16),
            shape((tokens, OWN), jnp.float32),
            shape((8, width), jnp.float32),
        ],
        scratch_shapes=[pltpu.VMEM((8, width), jnp.float32)],
        compiler_params=pltpu.CompilerParams(vmem_limit_bytes=60 << 20),
        cost_estimate=SMALL,
        name="ffn_backward",
    )(length, residual, residual, cot, mine, other, vectors, w_o_rows)


def att_grad_kernel(m0_ref, m2_ref, m3_ref, gated_ref, dq_ref, dk_ref, dv_ref, do_ref,
                    send_a, keep_a, send_b, keep_b):
    chip = lax.axis_index("dp") // 2
    by_x, by_y = chip % 2 == 0, (chip // 2) % 2 == 0
    first = ((m0_ref, dq_ref), (gated_ref, do_ref))
    second = ((m2_ref, dk_ref), (m3_ref, dv_ref))
    for half in range(2):
        lanes = slice(half * OWN, (half + 1) * OWN)
        block = dot32(first[half][0][...], first[half][1][...], TN).astype(jnp.bfloat16)
        for y in range(2):
            low, high = block[y * 128 : y * 128 + 64], block[y * 128 + 64 : y * 128 + 128]
            send_a[y, :, lanes] = jnp.where(by_x, high, low)
            keep_a[y, :, lanes] = jnp.where(by_x, low, high)
        block = dot32(second[half][0][...], second[half][1][...], TN).astype(jnp.bfloat16)
        for x in range(2):
            low, high = block[x * 64 : x * 64 + 64], block[128 + x * 64 : 128 + x * 64 + 64]
            send_b[x, :, lanes] = jnp.where(by_y, high, low)
            keep_b[x, :, lanes] = jnp.where(by_y, low, high)


def att_gradients(mixes, gated, grads, own_grad):
    tokens = gated.shape[0]
    left = pl.BlockSpec((tokens, 256), lambda i: (0, i))
    right = pl.BlockSpec((tokens, OWN), lambda i: (0, 0))
    out = pl.BlockSpec((2, 64, 2 * OWN), lambda i: (i, 0, 0))
    return pl.pallas_call(
        att_grad_kernel,
        grid=(4,),
        in_specs=[left] * 4 + [right] * 4,
        out_specs=[out] * 4,
        out_shape=[jax.ShapeDtypeStruct((8, 64, 2 * OWN), jnp.bfloat16)] * 4,
        compiler_params=pltpu.CompilerParams(vmem_limit_bytes=60 << 20),
        cost_estimate=SMALL,
        name="att_gradients",
    )(*mixes, gated, *grads, own_grad)


def swap(block, mask):
    size = lax.axis_size("dp")
    return lax.ppermute(block, "dp", [(i, i ^ mask) for i in range(size)])


def bit_of(mask):
    return (lax.axis_index("dp") // mask) % 2


def in_order(mask, own, other, axis):
    lower = bit_of(mask) == 0
    return jnp.where(
        lower, jnp.concatenate([own, other], axis=axis), jnp.concatenate([other, own], axis=axis)
    )


def chip_masks():
    size = lax.axis_size("dp")
    masks = []
    while 2 << len(masks) < size:
        masks.append(2 << len(masks))
    return masks


def steps_of(kind):
    masks = chip_masks()
    near, far = [[mask] for mask in masks[:2]], [[mask] for mask in masks[2:][::-1]]
    first = [[far[0][0], far[1][0], far[0][0] | far[1][0]]] if len(far) == 2 else far
    return [first + near[::-1], first + near, far + near[::-1], far + near, near + far][kind]


class Held:
    def __init__(self, value):
        self.value = value


def meet(movers, *arrays):
    held = []
    for mover in movers:
        held += [x[0] for x in mover.arrived if x[0] not in held]
    out = lax.optimization_barrier(tuple(x.value for x in held) + arrays)
    for x, value in zip(held, out):
        x.value = value
    return out[len(held) :]


def read(arrived):
    return [x.value if lanes is None else x.value[..., lanes] for x, lanes in arrived]


class Gather:
    def __init__(self, block, kind, places=(0,)):
        self.steps = steps_of(kind)
        self.held = block[None]
        self.places = [0]
        self.arrived = []
        self.masks = []

    def merge(self):
        if self.arrived:
            self.held = jnp.concatenate([self.held] + read(self.arrived), axis=0)
            self.places = self.places + [p ^ (m // 2) for m in self.masks for p in self.places]
            self.arrived = []

    def step(self):
        if self.steps:
            self.merge()
            self.masks = self.steps.pop(0)
            self.arrived = [(Held(swap(self.held, mask)), None) for mask in self.masks]
        return self

    def run(self):
        while self.steps:
            self.step()
        return self

    def split(self, kinds):
        width = self.held.shape[-1] // len(kinds)
        out = []
        for i, kind in enumerate(kinds):
            part = Gather.__new__(Gather)
            cut = slice(i * width, (i + 1) * width)
            part.steps = steps_of(kind)[len(steps_of(kind)) - len(self.steps) :]
            part.held = self.held[..., cut]
            part.arrived = [(x, cut) for x, _ in self.arrived]
            part.places, part.masks = self.places, self.masks
            out.append(part)
        return out


def place_kernel(places, cuts, *refs):
    sources, outs = refs[: len(places)], refs[len(places) :]
    chip = lax.axis_index("dp") // 2
    for source, (part, list_of) in zip(sources, places):
        for j, place in enumerate(list_of):
            for out, (first, rows, lanes) in zip(outs, cuts):
                start = pl.multiple_of((chip ^ place) * rows, rows)
                lane, width = lanes[part]
                at = sum(w for _, w in lanes[:part])
                out[pl.ds(start, rows), at : at + width] = source[
                    j, first : first + rows, lane : lane + width
                ]


def assemble(gathers, cuts=None):
    gathers = [g.run() for g in gathers]
    rows = gathers[0].held.shape[1]
    cuts = cuts or ((0, rows, [(0, g.held.shape[2]) for g in gathers]),)
    sources, places = [], []
    for i, g in enumerate(gathers):
        sources += [g.held] + read(g.arrived)
        shifts = [0] + [mask // 2 for mask in g.masks]
        places += [(i, [p ^ shift for p in g.places]) for shift in shifts]
    count = lax.axis_size("dp") // 2
    if any(cut[1] % 16 for cut in cuts):
        return assemble_plain(sources, places, cuts, count)
    space = pl.BlockSpec(memory_space=pltpu.VMEM)
    return pl.pallas_call(
        partial(place_kernel, places, cuts),
        in_specs=[space] * len(sources),
        out_specs=[space] * len(cuts),
        out_shape=[
            jax.ShapeDtypeStruct((count * n, sum(w for _, w in lanes)), sources[0].dtype)
            for _, n, lanes in cuts
        ],
        compiler_params=pltpu.CompilerParams(vmem_limit_bytes=32 << 20),
        cost_estimate=SMALL,
        name="assemble",
    )(*sources)


def assemble_plain(sources, places, cuts, count):
    chip = lax.axis_index("dp") // 2
    parts = []
    for part in sorted({part for part, _ in places}):
        blocks = jnp.concatenate([x for x, (at, _) in zip(sources, places) if at == part])
        where = [p for at, list_of in places if at == part for p in list_of]
        blocks = jnp.stack([blocks[where.index(i)] for i in range(count)])
        parts.append(jnp.take(blocks, chip ^ lax.iota(jnp.int32, count), axis=0))
    return [
        jnp.concatenate(
            [x[:, first : first + n, at : at + w] for x, (at, w) in zip(parts, lanes)], axis=-1
        ).reshape(count * n, -1)
        for first, n, lanes in cuts
    ]


class Scatter:
    def __init__(self, parts, kind):
        self.steps = steps_of(kind)[::-1]
        self.axes = chip_masks()[::-1]
        self.sources = [parts.reshape((2,) * len(self.axes) + parts.shape[1:])]
        self.arrived = []
        self.sent = None

    @classmethod
    def begun(cls, sent, kept, kind):
        out = cls.__new__(cls)
        out.steps = steps_of(kind)[::-1]
        out.axes = [axis for axis in chip_masks()[::-1] if axis != out.steps[0][0]]
        out.sources = [kept.reshape((2,) * len(out.axes) + kept.shape[1:])]
        out.arrived = []
        out.sent = [sent.reshape(out.sources[0].shape)]
        return out

    def pick(self, sources, mask, gone):
        out = []
        for x in sources:
            for place in reversed(range(len(self.axes))):
                axis = self.axes[place]
                if axis in gone:
                    which = bit_of(axis) if not mask & axis else 1 - bit_of(axis)
                    x = lax.dynamic_index_in_dim(x, which, place, keepdims=False)
            out.append(x)
        return out

    def prepare(self):
        if self.sent is not None:
            return self
        masks = self.steps[0]
        sources = self.sources + read(self.arrived)
        gone = [axis for axis in self.axes if any(mask & axis for mask in masks)]
        self.sent = [
            sum(x.astype(jnp.float32) for x in self.pick(sources, mask, gone)).astype(jnp.bfloat16)
            for mask in masks
        ]
        self.sources = self.pick(sources, 0, gone)
        self.axes = [axis for axis in self.axes if axis not in gone]
        self.arrived = []
        return self

    def step(self):
        return together([self])[0]

    def run(self):
        while self.steps:
            self.step()
        return self

    def total(self):
        return sum(x.astype(jnp.float32) for x in self.sources + read(self.arrived))


def together(parts):
    if not parts[0].steps:
        return parts
    for part in parts:
        part.prepare()
    for i, mask in enumerate(parts[0].steps[0]):
        sent = [part.sent[i] for part in parts]
        got = Held(swap(sent[0] if len(sent) == 1 else jnp.concatenate(sent, axis=-1), mask))
        at = 0
        for part, x in zip(parts, sent):
            lanes = slice(at, at + x.shape[-1]) if len(sent) > 1 else None
            part.arrived.append((got, lanes))
            at += x.shape[-1]
    for part in parts:
        part.steps.pop(0)
        part.sent_now, part.sent = part.sent[0], None
    return parts


def norm_rows(features, gain_row, offset_row):
    average = jnp.mean(features, axis=-1, keepdims=True)
    centred = features - average
    variance = jnp.mean(centred * centred, axis=-1, keepdims=True)
    return centred * lax.rsqrt(variance + 1e-05) * gain_row + offset_row


def product(operand, weight_matrix):
    return jnp.dot(operand, weight_matrix, preferred_element_type=jnp.float32)


def input_gradient_rows(upstream_gradient, weight_matrix):
    return lax.dot_general(
        upstream_gradient,
        weight_matrix,
        (((1,), (1,)), ((), ())),
        preferred_element_type=jnp.float32,
    )


def weight_gradient(operand, upstream_gradient):
    return lax.dot_general(
        operand, upstream_gradient, (((0,), (0,)), ((), ())), preferred_element_type=jnp.float32
    )


def earlier(rows):
    return jnp.concatenate([jnp.zeros_like(rows[:1]), rows[:-1]], axis=0)


def ffn_mix(residual, vectors):
    second = norm_rows(residual, vectors[14], vectors[15])
    return second + (earlier(second) - second) * vectors[6]


def narrow(x):
    return x.astype(jnp.bfloat16)


def local(
    inputs,
    lengths,
    attention_projections,
    channel_key_weight,
    channel_value_weight,
    lowrank_down_weight,
    lowrank_up_weight,
    per_feature_parameters,
    cotangent,
):
    devices = lax.axis_size("dp")
    chips = devices // 2
    device = lax.axis_index("dp")
    chip, core = device // 2, device % 2
    row_count = inputs.shape[0]
    slots = 2 * row_count
    share = EMBED // devices
    pair_share = 2 * share
    units = channel_value_weight.shape[0]
    half_units = chips * units

    def own_cut(x, which):
        return lax.dynamic_slice_in_dim(x, which * OWN, OWN, x.ndim - 1)

    def own_rows(x, which):
        return lax.dynamic_slice_in_dim(x, which * row_count, row_count, 0)

    pair_rows = in_order(
        1,
        own_cut(attention_projections, core),
        swap(own_cut(attention_projections, 1 - core), 1),
        1,
    )
    lora = jnp.concatenate([lowrank_down_weight, lowrank_up_weight.T], axis=1)
    vector_rows = jnp.pad(per_feature_parameters.T, ((0, 0), (0, 128 - 18)))
    vector_rows = vector_rows.reshape(share // 4, OWN)
    first_rows = 3 * pair_share
    misc_rows = share + share // 4 + (share // 4) % 16
    block = jnp.concatenate(
        [
            pair_rows[:3].reshape(first_rows, OWN),
            lora,
            jnp.pad(vector_rows, ((0, (share // 4) % 16), (0, 0))),
        ],
        axis=0,
    )
    half = half_units // 2
    quarter = OWN // 2
    first = Gather(block, 0).step()
    w_o_part = Gather(pair_rows[3], 4).step().step()
    key_in, raw, cot, _ = meet([], channel_key_weight, inputs, cotangent, first.held)
    key_cut = key_in.reshape(share, chips, 2, units)

    def key_columns(which):
        return lax.dynamic_index_in_dim(key_cut, which, 2, keepdims=False).reshape(share, half_units)

    key_rows = in_order(1, key_columns(core), swap(key_columns(1 - core), 1), 0)
    tokens = in_order(1, raw, swap(raw, 1), 0)
    cot = in_order(1, cot, swap(cot, 1), 0)
    key_rows, tokens, cot = meet([first, w_o_part], key_rows, tokens, cot)
    first = first.split((0, 1))
    for part in first:
        part.step()
    key_part = Gather(key_rows, 2).step()
    (tokens,) = meet(first, tokens)
    for part in first:
        part.step()
    value_block, *_ = meet([key_part], channel_value_weight, *[part.held for part in first])
    key_part.step()
    value_part = Gather(value_block, 2).step()
    w_o_part.step()
    (tokens,) = meet(first + [key_part, value_part], tokens)
    key_parts = key_part.split((2, 3))
    for part in key_parts:
        part.step()
    w_r, w_k, w_v, misc = assemble(
        first,
        [(i * pair_share, pair_share, [(0, quarter)] * 2) for i in range(3)]
        + [(first_rows, misc_rows, [(0, quarter)] * 2)],
    )
    misc = misc.reshape(chips, 1, misc_rows, OWN)
    misc = in_order(1, misc, swap(misc, 1), 1)
    value_part.step()
    lora = misc[:, :, :share].reshape(EMBED, OWN)
    down, up_t = lora[:, :256], lax.dynamic_slice_in_dim(lora[:, 256:], core * OWN, OWN, 0)
    vectors = misc[:, :, share : share + share // 4].reshape(EMBED, 128)[:, :18].T
    vectors = vectors.astype(jnp.float32)
    own_vectors = own_cut(vectors, core)
    used = jnp.concatenate([own_vectors[7:12], own_vectors[16:18], own_vectors[:1]], axis=0)
    length = lax.dynamic_index_in_dim(lengths, chip, 0)
    live = (lax.iota(jnp.int32, slots) < length)[:, None]

    *mixes, queries, keys, values, decay_low, rate_low, gate_rows, hid = front_forward(
        tokens, vectors, w_r, w_k, w_v, down, up_t
    )
    terms = meet(
        key_parts + [value_part, w_o_part],
        queries, keys, values, decay_low, rate_low, gate_rows,
    )
    value_parts = value_part.split((2, 3))
    for part in key_parts + value_parts:
        part.step()
    w_o_part.step()
    blocks = slots // (CHUNK * STEP_CHUNKS)
    zero_state = jnp.zeros((2, CHUNK, LANES), jnp.float32)
    gated, *saved, _ = wkv_forward(0, blocks, length, used, zero_state, terms)
    gated, cot, tokens = meet(key_parts + value_parts + [w_o_part], gated, cot, tokens)
    for part in value_parts:
        part.step()
    gated, *_ = meet([], gated, *[part.held for part in value_parts])
    (w_o_own,) = assemble([w_o_part])
    residual, ffn_in, gated_all, w_o_rows = attend(
        gated, swap(gated, 1), w_o_own, swap(w_o_own, 1), tokens, vectors
    )
    (key_weight,) = assemble(key_parts)
    positive = jax.nn.relu(product(ffn_in, key_weight))
    hidden = narrow(jnp.square(positive))
    out_narrow = jnp.where(live, cot, jnp.zeros_like(cot))
    grad_value = narrow(weight_gradient(hidden, out_narrow)).reshape(chips, units, EMBED)
    value_scatter = [
        Scatter(grad_value[..., i * OWN : (i + 1) * OWN], 2 + i).prepare() for i in range(2)
    ]
    hidden, positive, out_narrow, *sent = meet(
        value_parts, hidden, positive, out_narrow, *[m.sent[0] for m in value_scatter]
    )
    for part, x in zip(value_scatter, sent):
        part.sent = [x]
        part.step()
    (value_weight,) = assemble(value_parts)

    pre_narrow = narrow(2.0 * positive * input_gradient_rows(out_narrow, value_weight))
    ffn_in_grad = narrow(input_gradient_rows(pre_narrow, key_weight))
    other_grad = swap(ffn_in_grad, 1)
    grad_key = narrow(weight_gradient(ffn_in, pre_narrow)).reshape(chips, pair_share, half_units)
    residual_grad, own_grad, gated_grad, ffn_vec = ffn_backward(
        length, residual, cot, ffn_in_grad, other_grad, vectors, w_o_rows
    )
    key_scatter = [
        Scatter(grad_key[:, :, i * half : (i + 1) * half], 2 + i).prepare() for i in range(2)
    ]
    gated_grad, *sent = meet([], gated_grad, *[m.sent[0] for m in key_scatter])
    for part, x in zip(key_scatter, sent):
        part.sent = [x]
        part.step()
    terms = [*terms, gated_grad, *saved]
    zero_sums = jnp.zeros((8, OWN), jnp.float32)
    early = blocks // 2
    *before, sums, state = wkv_backward(
        early, blocks - early, length, used, zero_state, zero_sums, terms
    )
    state, sums = meet(value_scatter, state, sums)
    for part in value_scatter:
        part.step()
    *low_grads, own_vec, _ = wkv_backward(0, early, length, used, state, sums, terms, before)
    if pair_share == 64:
        sent_a, kept_a, sent_b, kept_b = att_gradients(
            (mixes[0], mixes[2], mixes[3]), gated_all, low_grads[:3], own_grad
        )
        att_scatter = [Scatter.begun(sent_a, kept_a, 2), Scatter.begun(sent_b, kept_b, 3)]
    else:
        grads = [weight_gradient(mixes[m], g) for m, g in zip((0, 2, 3), low_grads)]
        grad_o = weight_gradient(gated_all, own_grad)
        att_scatter = [
            Scatter(
                narrow(jnp.concatenate(x, axis=1)).reshape(chips, pair_share, EMBED), 2 + i
            ).prepare()
            for i, x in enumerate(((grads[0], grad_o), (grads[1], grads[2])))
        ]
    own_vec, *sent = meet(
        key_scatter + value_scatter, own_vec, *[m.sent[0] for m in att_scatter]
    )
    for part, x in zip(att_scatter, sent):
        part.sent = [x]
        part.step()
    for part in key_scatter:
        part.step()
    together(value_scatter)
    own_vec, *_ = meet([], own_vec, *[m.sent_now for m in key_scatter])
    token_part, misc_mine, misc_other = front_backward(
        tokens, vectors, w_r, w_k, w_v, down, up_t, (mixes[1], mixes[4], mixes[5]), hid,
        low_grads, own_vec, ffn_vec,
    )
    misc_other = swap(misc_other, 1)
    token_part, misc_mine, misc_other = meet(
        att_scatter + key_scatter + value_scatter, token_part, misc_mine, misc_other
    )
    for part in att_scatter:
        part.prepare()
    misc_mine, misc_other, *sent = meet(
        key_scatter + value_scatter, misc_mine, misc_other, *[m.sent[0] for m in att_scatter]
    )
    for part, x in zip(att_scatter, sent):
        part.sent = [x]
        part.step()
    misc_sum = misc_mine + misc_other.astype(jnp.float32)
    misc_sum = jnp.concatenate([misc_sum[..., :320], misc_sum[..., 320:]], axis=1)
    misc_scatter = Scatter(misc_sum, 3).step()
    meet(key_scatter + value_scatter, misc_scatter.sent_now)
    together(key_scatter)
    together(value_scatter)
    (token_part,) = meet([misc_scatter], token_part)
    misc_scatter.step()
    token_part, hidden, _ = meet(key_scatter, token_part, hidden, misc_scatter.sent_now)
    together(key_scatter)
    (token_part,) = meet(att_scatter + [misc_scatter], token_part)
    masks = chip_masks()
    last_parts = att_scatter + [misc_scatter]
    if len(misc_scatter.steps) == 2:
        for part in last_parts:
            part.steps = [[masks[2], masks[3], masks[2] | masks[3]]]
    together(last_parts)
    ffn_part = product(hidden, value_weight)
    input_gradient = (
        own_rows(residual_grad, core)
        + own_rows(token_part, core)
        + swap(own_rows(token_part, 1 - core), 1)
    )
    ffn_out = own_rows(ffn_part, core) + swap(own_rows(ffn_part, 1 - core), 1)
    output = narrow(jnp.where(own_rows(live, core), own_rows(residual, core) + ffn_out, 0.0))
    value_sum = jnp.concatenate(
        [x.run().total() for x in value_scatter], axis=1
    )
    while key_scatter[0].steps:
        together(key_scatter)
    key_sum = jnp.concatenate([x.total() for x in key_scatter], axis=1).reshape(2, share, -1)

    def exchange(x):
        mine = lax.dynamic_index_in_dim(x, core, 0, keepdims=False)
        return mine, swap(lax.dynamic_index_in_dim(x, 1 - core, 0, keepdims=False), 1)

    key_mine, key_theirs = exchange(key_sum)
    input_gradient, value_sum, key_mine, key_theirs = meet(
        last_parts, input_gradient, value_sum, key_mine, key_theirs
    )
    while last_parts[0].steps:
        together(last_parts)
    first_sum, second_sum, misc_sum = [x.total() for x in last_parts]
    misc_sum = jnp.concatenate([misc_sum[:share], misc_sum[share:]], axis=1)
    att_sum = jnp.concatenate(
        [first_sum[:, :OWN], second_sum, first_sum[:, OWN:]], axis=1
    )
    mine, theirs = exchange(att_sum.reshape(2, share, -1))
    shard_mixer = jnp.stack(
        [
            in_order(1, mine[:, i * OWN : (i + 1) * OWN], theirs[:, i * OWN : (i + 1) * OWN], 1)
            for i in range(4)
        ]
    )
    shard_key = in_order(
        1,
        key_mine.reshape(share, chips, 1, units),
        key_theirs.reshape(share, chips, 1, units),
        2,
    ).reshape(share, 2 * half_units)
    return (
        output,
        input_gradient,
        shard_mixer,
        shard_key,
        value_sum,
        misc_sum[:, :256],
        misc_sum[:, 256:512].T,
        misc_sum[:, 512:530].T,
    )


def solution(mesh):
    in_specs = (
        P("dp", None),
        P(),
        P(None, "dp", None),
        P("dp", None),
        P("dp", None),
        P("dp", None),
        P(None, "dp"),
        P(None, "dp"),
        P("dp", None),
    )
    out_specs = (
        P("dp", None),
        P("dp", None),
        P(None, "dp", None),
        P("dp", None),
        P("dp", None),
        P("dp", None),
        P(None, "dp"),
        P(None, "dp"),
    )
    return jax.shard_map(local, mesh=mesh, in_specs=in_specs, out_specs=out_specs, check_vma=False)
```

```python
from functools import partial

import jax
import jax.numpy as jnp
from jax import lax
from jax.experimental import pallas as pl
from jax.experimental.pallas import tpu as pltpu
from jax.sharding import PartitionSpec as P

HEADS = 16
HEAD_SIZE = 64
DECAY_RANK = 64
RATE_RANK = 64
EMBED = 1024
OWN = EMBED // 2
PRECISE = lax.Precision.HIGHEST


CHUNK = 64
LANES = 256
GROUP_HEADS = 4
STEP_CHUNKS = 2
SMALL = pl.CostEstimate(flops=1, bytes_accessed=1, transcendentals=0)

NN = (((1,), (0,)), ((), ()))
NT = (((1,), (1,)), ((), ()))
TN = (((0,), (0,)), ((), ()))


def halves(x):
    high = x.astype(jnp.bfloat16)
    return high, (x - high.astype(jnp.float32)).astype(jnp.bfloat16)


def whole(x):
    return (x.astype(jnp.bfloat16),)


def dot32(a, b, dims):
    return lax.dot_general(a, b, dims, preferred_element_type=jnp.float32)


def mul(left, right, dims=NN):
    if len(left) == 1 or len(right) == 1:
        return dot32(left[0], right[0], dims)
    rows = left[0].shape[0]
    both = dot32(jnp.concatenate(left, axis=0), right[0], dims)
    return both[:rows] + both[rows:] + dot32(left[0], right[1], dims)


def tmul(left, right, masks):
    full = dot32(left[0], right[0], TN)
    if len(left) > 1 and len(right) > 1:
        full = full + dot32(left[1], right[0], TN) + dot32(left[0], right[1], TN)
    return sum(full[h * CHUNK : (h + 1) * CHUNK] * masks[h][:1].astype(jnp.float32) for h in range(GROUP_HEADS))


def spread(pair, masks):
    return tuple(
        jnp.concatenate([part * masks[h] for h in range(GROUP_HEADS)], axis=0) for part in pair
    )


def stack(first, second):
    return tuple(jnp.concatenate([x, y], axis=0) for x, y in zip(first, second))


def head_masks():
    lane = lax.broadcasted_iota(jnp.int32, (CHUNK, LANES), 1) // CHUNK
    return [(lane == h).astype(jnp.float32).astype(jnp.bfloat16) for h in range(GROUP_HEADS)]


def places():
    row = lax.broadcasted_iota(jnp.int32, (CHUNK, LANES), 0)
    col = lax.broadcasted_iota(jnp.int32, (CHUNK, LANES), 1) % CHUNK
    return row, col


def running_sum(x, upper=False):
    row = lax.broadcasted_iota(jnp.int32, (CHUNK, CHUNK), 0)
    col = lax.broadcasted_iota(jnp.int32, (CHUNK, CHUNK), 1)
    ones = (row <= col if upper else col <= row).astype(jnp.float32).astype(jnp.bfloat16)
    high, rest = halves(x)
    low = (x - high.astype(jnp.float32) - rest.astype(jnp.float32)).astype(jnp.bfloat16)
    return dot32(ones, high, NN) + dot32(ones, rest, NN) + dot32(ones, low, NN)


def scaled_forms(q, w, k, a, b):
    total = running_sum(w)
    before = total - w
    middle = total[CHUNK // 2 - 1 : CHUNK // 2]
    end = total[CHUNK - 1 :]
    ea = jnp.exp(before - middle)
    eq = jnp.exp(total - middle)
    eb = jnp.exp(middle - total)
    ee = jnp.exp(end - total)
    return (a * ea, q * eq, b * eb, k * eb, b * ee, k * ee), (ea, eq, eb, ee), (jnp.exp(middle), jnp.exp(end))


def each(fn, *columns):
    return [fn(*row) for row in zip(*columns)]


def block_ones():
    row = lax.broadcasted_iota(jnp.int32, (LANES, LANES), 0) // CHUNK
    col = lax.broadcasted_iota(jnp.int32, (LANES, LANES), 1) // CHUNK
    return (row == col).astype(jnp.float32).astype(jnp.bfloat16)


def head_sum(x, ones):
    rows = x.shape[0]
    both = dot32(jnp.concatenate(halves(x), axis=0), ones, NN)
    return both[:rows] + both[rows:]


def prepared(keys, decay_low, rate_low, live, vec, ones):
    sig = jax.nn.sigmoid(vec[0] + decay_low)
    log_decay = (-0.6065306597126334) * sig * live
    rates = jax.nn.sigmoid(vec[1] + rate_low)
    scaled = keys * vec[2]
    inverse = lax.rsqrt(head_sum(scaled * scaled, ones) + 1e-06)
    unit_keys = scaled * inverse
    factor = (1.0 + (rates - 1.0) * vec[3]) * live
    return log_decay, keys * factor, -unit_keys, unit_keys * rates * live, sig, rates, inverse, factor


def read_out(o, q, k, v, vec, ones):
    centred = o - head_sum(o, ones) * (1.0 / CHUNK)
    scale = lax.rsqrt(head_sum(centred * centred, ones) * (1.0 / CHUNK) + 0.00064)
    normed = centred * scale
    weight = head_sum(q * k * vec[4], ones)
    return normed, scale, weight, normed * vec[5] + vec[6] + weight * v


def unit_slices():
    return [
        (slice(c * CHUNK, (c + 1) * CHUNK), slice(g * LANES, (g + 1) * LANES))
        for c in range(STEP_CHUNKS)
        for g in range(2)
    ]


def unit_live(length, step):
    row = lax.broadcasted_iota(jnp.int32, (CHUNK, LANES), 0)
    start = step * (STEP_CHUNKS * CHUNK)
    live = [(row + (start + c * CHUNK) < length).astype(jnp.float32) for c in range(STEP_CHUNKS)]
    return [live[c] for c in range(STEP_CHUNKS) for g in range(2)]


def unit_vectors(vec_ref):
    vec = [[vec_ref[i : i + 1, g * LANES : (g + 1) * LANES] for i in range(7)] for g in range(2)]
    return [vec[g] for c in range(STEP_CHUNKS) for g in range(2)]


def forward_kernel(base, *refs):
    len_ref, vec_ref, start_ref, q_ref, keys_ref, v_ref, dl_ref, rl_ref, gate_ref = refs[:9]
    (
        out_ref, o_ref, t_ref, aqb_ref, aak_ref, aqk_ref, y_ref, z_ref, trt_ref, qe_ref, state_ref,
    ) = refs[-11:]

    @pl.when(pl.program_id(0) == 0)
    def _():
        state_ref[...] = start_ref[...]

    masks = head_masks()
    row, col = places()
    strict = (col < row).astype(jnp.float32)
    within = (col <= row).astype(jnp.float32)
    eye = (col == row).astype(jnp.float32)
    ones = block_ones()
    units = unit_slices()
    live = unit_live(len_ref[0], pl.program_id(0) + base)
    vec = unit_vectors(vec_ref)
    load = lambda ref: [ref[u] for u in units]
    q, keys, v = load(q_ref), load(keys_ref), load(v_ref)
    ready = each(
        lambda x, y, z, m, n: prepared(x, y, z, m, n, ones), keys, load(dl_ref), load(rl_ref), live, vec
    )
    w, k, a, b = ([x[i] for x in ready] for i in range(4))
    forms = each(scaled_forms, q, w, k, a, b)
    ah, qh, bh, kh, bt, kt = ([f[0][i] for f in forms] for i in range(6))
    emid = [f[2][0] for f in forms]
    eend = [f[2][1] for f in forms]
    aq = each(lambda x, y: halves(jnp.concatenate([x, y], axis=0)), ah, qh)
    with_b = each(lambda l, r: mul(l, spread(halves(r), masks), NT), aq, bh)
    with_k = each(lambda l, r: mul(l, spread(halves(r), masks), NT), aq, kh)
    aab = [x[:CHUNK] * strict for x in with_b]
    aqb = [halves(x[CHUNK:] * within) for x in with_b]
    aak = [halves(x[:CHUNK] * strict) for x in with_k]
    aqk = [halves(x[CHUNK:] * within) for x in with_k]
    p = [halves(x * (row // 8 == col // 8)) for x in aab]
    t = [eye + x * (row // 8 == col // 8) for x in aab]
    p2 = each(lambda x: halves(mul(x, spread(x, masks))), p)
    both = each(lambda x, y: mul(stack(x, halves(y)), spread(x, masks)), p2, t)
    p4 = [halves(x[:CHUNK]) for x in both]
    t = each(lambda x, y: x + y[CHUNK:], t, both)
    t = each(lambda x, y: x + mul(halves(x), spread(y, masks)), t, p4)
    for size in (8, 16, 32):
        corner = ((row // size) % 2 == 1) & (col // size == row // size - 1)
        ts = [halves(x) for x in t]
        n = [halves(x * corner) for x in aab]
        tn = each(lambda x, y: halves(mul(x, spread(y, masks))), ts, n)
        t = each(lambda x, y, z: x + mul(y, spread(z, masks)), t, tn, ts)
    ts = [halves(x) for x in t]
    vs = [halves(x) for x in v]
    vm = [spread(x, masks) for x in vs]
    wide = each(lambda x, y, e: mul(x, spread(halves(y * e), masks)), ts, ah, emid)
    r0 = each(mul, aak, vm)
    y0 = each(lambda x, y: mul(x, spread(halves(y), masks)), ts, r0)
    wides = [halves(x) for x in wide]
    qe = each(lambda x, e, y, z: x * e + mul(y, spread(z, masks)), qh, emid, aqb, wides)
    y0s = [halves(x) for x in y0]
    part = each(lambda x, y, z, u: mul(x, spread(y, masks)) + mul(z, u), aqb, y0s, aqk, vm)
    bts = [halves(x) for x in bt]
    diag = [eye * e for e in eend]
    tr = each(lambda x, y, d: tmul(x, y, masks) + d, bts, wides, diag)
    trt = each(lambda x, y, d: tmul(y, x, masks) + d, bts, wides, diag)
    inject = each(lambda x, y, z, u: tmul(stack(x, halves(y)), stack(z, u), masks), bts, kt, y0s, vs)
    wq = each(lambda x, y: stack(x, halves(y)), wides, qe)
    z = []
    out = []
    for c in range(STEP_CHUNKS):
        for g in range(2):
            i = c * 2 + g
            now = state_ref[g]
            nows = spread(halves(now), masks)
            state_ref[g] = mul(halves(tr[i]), nows) + inject[i]
            z.append(now)
            out.append(mul(wq[i], nows))
    o = each(lambda x, y: x[CHUNK:] + y, out, part)
    mixed = each(lambda x, y, z, m, n: read_out(x, y, z, m, n, ones)[3], o, q, k, v, vec)
    for i, u in enumerate(units):
        out_ref[u] = (mixed[i] * gate_ref[u]).astype(jnp.bfloat16)
        o_ref[u] = o[i]
        y_ref[u] = (out[i][:CHUNK] + y0[i]).astype(jnp.bfloat16)
        t_ref[u] = ts[i][0]
        aqb_ref[u] = aqb[i][0]
        aak_ref[u] = aak[i][0]
        aqk_ref[u] = aqk[i][0]
        z_ref[u] = z[i]
        trt_ref[u] = trt[i].astype(jnp.bfloat16)
        qe_ref[u] = qe[i].astype(jnp.bfloat16)


def backward_kernel(base, *refs):
    (
        len_ref, vec_ref, start_ref, sums_ref, q_ref, keys_ref, v_ref, dl_ref, rl_ref, gate_ref,
        g_ref, o_ref, t_ref, aqb_ref, aak_ref, aqk_ref, y_ref, z_ref, trt_ref, qe_ref,
    ) = refs[:20]
    dq_ref, dkeys_ref, dv_ref, ddl_ref, drl_ref, dgate_ref, dvec_ref, state_ref = refs[-8:]
    step = base + pl.num_programs(0) - 1 - pl.program_id(0)

    @pl.when(pl.program_id(0) == 0)
    def _():
        state_ref[...] = start_ref[...]
        dvec_ref[...] = sums_ref[...]

    masks = head_masks()
    row, col = places()
    strict = (col < row).astype(jnp.float32)
    within = (col <= row).astype(jnp.float32)
    ones = block_ones()
    units = unit_slices()
    live = unit_live(len_ref[0], step)
    vec = unit_vectors(vec_ref)
    load = lambda ref: [ref[u] for u in units]
    q, keys, v, g = load(q_ref), load(keys_ref), load(v_ref), load(g_ref)
    ready = each(
        lambda x, y, z, m, n: prepared(x, y, z, m, n, ones), keys, load(dl_ref), load(rl_ref), live, vec
    )
    w, k, a, b, sig, rates, inverse, factor = ([x[i] for x in ready] for i in range(8))
    seen = each(lambda x, y, z, m, n: read_out(x, y, z, m, n, ones), load(o_ref), q, k, v, vec)
    normed, scale, weight, mixed = ([x[i] for x in seen] for i in range(4))
    gate = load(gate_ref)
    dgate = each(lambda x, y: x * y, g, mixed)
    dmix = each(lambda x, y: x * y, g, gate)
    dn = each(lambda x, n: x * n[5], dmix, vec)
    do = each(
        lambda x, n, r: r
        * (x - head_sum(x, ones) * (1.0 / CHUNK) - n * (head_sum(x * n, ones) * (1.0 / CHUNK))),
        dn, normed, scale,
    )
    dweight = each(lambda x, y: head_sum(x * y, ones), dmix, v)
    do = [whole(x) for x in do]
    qe, trt, t, aqb, aak, aqk, ys = (
        [(x,) for x in load(ref)]
        for ref in (qe_ref, trt_ref, t_ref, aqb_ref, aak_ref, aqk_ref, y_ref)
    )
    z = load(z_ref)
    vs = [whole(x) for x in v]
    h = each(lambda x, y: tmul(x, y, masks), qe, do)
    dz = [None] * len(units)
    for c in reversed(range(STEP_CHUNKS)):
        for g in range(2):
            i = c * 2 + g
            now = state_ref[g]
            dz[i] = now
            state_ref[g] = mul(trt[i], spread(whole(now), masks)) + h[i]
    dzs = [spread(whole(x), masks) for x in dz]
    zs = [spread(whole(x), masks) for x in z]
    forms = each(scaled_forms, q, w, k, a, b)
    ah, qh, bh, kh, bt, kt = ([f[0][i] for f in forms] for i in range(6))
    ea, eq, eb, ee = ([f[1][i] for f in forms] for i in range(4))
    emid = [f[2][0] for f in forms]
    eend = [f[2][1] for f in forms]
    from_end = each(lambda x, y, s: mul(whole(jnp.concatenate([x, y], axis=0)), s), bt, kt, dzs)
    dy = each(lambda x, y, s: whole(tmul(x, y, masks) + s[:CHUNK]), aqb, do, from_end)
    dr = each(lambda x, y: whole(tmul(x, y, masks)), t, dy)
    ro = each(stack, dr, do)
    dv = each(lambda x, y, s, f: tmul(stack(x, y), s, masks) + f[CHUNK:], aak, aqk, ro, from_end)
    mask2 = jnp.concatenate([strict, within], axis=0)
    dab = each(lambda s, y: whole(mul(s, spread(y, masks), NT) * mask2), ro, ys)
    dak = each(lambda s, y: whole(mul(s, spread(y, masks), NT) * mask2), ro, vs)
    dst = each(lambda s, y: mul(s, y, NT), ro, zs)
    bhs, khs = [whole(x) for x in bh], [whole(x) for x in kh]
    inside = each(
        lambda x, bb, y, kk: mul(x, spread(bb, masks)) + mul(y, spread(kk, masks)), dab, bhs, dak, khs
    )
    outside = each(lambda s, e: s * e, dst, emid)
    daq = each(lambda x, y: x + y, inside, outside)
    aq = each(lambda x, y: whole(jnp.concatenate([x, y], axis=0)), ah, qh)
    dbh = each(lambda x, y: tmul(x, y, masks), dab, aq)
    dkh = each(lambda x, y: tmul(x, y, masks), dak, aq)
    dend = each(lambda y, x, s: mul(stack(y, x), s, NT), ys, vs, dzs)
    row_of_ones = jnp.ones((8, LANES), jnp.bfloat16)
    sums = lambda x: jnp.sum(x, axis=0, keepdims=True)
    for i, u in enumerate(units):
        da = daq[i][:CHUNK] * ea[i]
        dq = daq[i][CHUNK:] * eq[i]
        dbt = dend[i][:CHUNK] * ee[i]
        dkt = dend[i][CHUNK:] * ee[i]
        db = dbh[i] * eb[i] + dbt
        dk = dkh[i] * eb[i] + dkt
        paq = inside[i] * aq[i][0].astype(jnp.float32)
        pa = paq[:CHUNK] + outside[i][:CHUNK] * ah[i]
        diff = pa + paq[CHUNK:] + outside[i][CHUNK:] * qh[i]
        diff = diff - dbh[i] * bhs[i][0].astype(jnp.float32) - dkh[i] * khs[i][0].astype(jnp.float32)
        diff = diff - dbt * b[i] - dkt * k[i]
        zz = spread(halves(z[i] * dz[i]), masks)
        carry = (dot32(row_of_ones, zz[0], NT) + dot32(row_of_ones, zz[1], NT))[:1] * eend[i]
        carry = carry + sums(dbt * b[i] + dkt * k[i])
        dw = running_sum(diff, upper=True) - pa + carry
        from_bonus = dweight[i] * vec[i][4]
        dk = dk + from_bonus * q[i]
        dq_ref[u] = (dq + from_bonus * k[i]).astype(jnp.bfloat16)
        dv_ref[u] = (dv[i] + weight[i] * dmix[i]).astype(jnp.bfloat16)
        dgate_ref[u] = dgate[i].astype(jnp.bfloat16)
        unit_keys = -a[i]
        db = db * live[i]
        du = db * rates[i] - da
        dscaled = inverse[i] * (du - unit_keys * head_sum(du * unit_keys, ones))
        dkl = dk * keys[i] * live[i]
        drl = (db * unit_keys + dkl * vec[i][3]) * rates[i] * (1.0 - rates[i])
        ddl = dw * w[i] * (1.0 - sig[i])
        dkeys_ref[u] = (dk * factor[i] + dscaled * vec[i][2]).astype(jnp.bfloat16)
        ddl_ref[u] = ddl.astype(jnp.bfloat16)
        drl_ref[u] = drl.astype(jnp.bfloat16)
        parts = (
            ddl, drl, dscaled * keys[i], dkl * (rates[i] - 1.0),
            dweight[i] * q[i] * k[i], dmix[i] * normed[i], dmix[i],
        )
        lanes = u[1]
        for j, x in enumerate(parts):
            dvec_ref[j : j + 1, lanes] += sums(x)


def wkv_call(kernel, base, steps, small, arrays, outs, sums, previous, name):
    tokens, width = arrays[0].shape
    rows = CHUNK * STEP_CHUNKS
    last = base + steps - 1
    turned = kernel is backward_kernel
    spec = pl.BlockSpec((rows, width), lambda i: (last - i if turned else base + i, 0))
    state = pl.BlockSpec((2, CHUNK, LANES), lambda i: (0, 0, 0))
    whole = pl.BlockSpec((8, width), lambda i: (0, 0))
    shape = jax.ShapeDtypeStruct
    first = [pl.BlockSpec(memory_space=pltpu.SMEM), whole, state] + [whole] * sums
    held = list(previous or ())
    start = len(first) + len(arrays)
    return pl.pallas_call(
        partial(kernel, base),
        grid=(steps,),
        in_specs=first + [spec] * len(arrays) + [pl.BlockSpec(memory_space=pl.ANY)] * len(held),
        out_specs=[spec] * len(outs) + [whole] * sums + [state],
        out_shape=[shape((tokens, width), dtype) for dtype in outs]
        + [shape((8, width), jnp.float32)] * sums
        + [shape((2, CHUNK, LANES), jnp.float32)],
        input_output_aliases={start + i: i for i in range(len(held))},
        compiler_params=pltpu.CompilerParams(vmem_limit_bytes=60 << 20),
        cost_estimate=SMALL,
        name=name,
    )(*small, *arrays, *held)


def wkv_forward(base, steps, length, vec, state, arrays, previous=None):
    outs = [jnp.bfloat16, jnp.float32] + [jnp.bfloat16] * 5 + [jnp.float32] + [jnp.bfloat16] * 2
    return wkv_call(
        forward_kernel, base, steps, (length, vec, state), arrays, outs, 0, previous, "wkv_forward"
    )


def wkv_backward(base, steps, length, vec, state, sums, arrays, previous=None):
    outs = [jnp.bfloat16] * 6
    return wkv_call(
        backward_kernel, base, steps, (length, vec, state, sums), arrays, outs, 1, previous,
        "wkv_backward",
    )


ROWS = 128


def row_norm(x):
    centred = x - jnp.mean(x, axis=-1, keepdims=True)
    scale = lax.rsqrt(jnp.mean(centred * centred, axis=-1, keepdims=True) + 1e-05)
    return centred * scale, scale


def shifted(x, edge, down):
    rows = x.shape[0]
    row = lax.broadcasted_iota(jnp.int32, x.shape, 0)
    if down:
        return jnp.where(row == 0, edge, pltpu.roll(x, 1, 0))
    return jnp.where(row == rows - 1, edge, pltpu.roll(x, rows - 1, 0))


def below(x, upper):
    lane = lax.broadcasted_iota(jnp.int32, x.shape, 1)
    keep = (lane >= DECAY_RANK) if upper else (lane < DECAY_RANK)
    return jnp.where(keep, x, jnp.zeros_like(x))


def front_kernel(
    x_ref, vec_ref, wr_ref, wk_ref, wv_ref, down_ref, up_ref,
    m0_ref, m1_ref, m2_ref, m3_ref, m4_ref, m5_ref,
    q_ref, k_ref, v_ref, dl_ref, rl_ref, gate_ref, hid_ref,
    edge_ref,
):
    @pl.when(pl.program_id(0) == 0)
    def _():
        edge_ref[...] = jnp.zeros_like(edge_ref)

    unit, _ = row_norm(x_ref[...].astype(jnp.float32))
    normed = unit * vec_ref[12:13] + vec_ref[13:14]
    change = shifted(normed, edge_ref[:1], True) - normed
    edge_ref[:1] = normed[ROWS - 1 :]
    mixes = []
    for j, ref in enumerate((m0_ref, m1_ref, m2_ref, m3_ref, m4_ref, m5_ref)):
        mixes.append((normed + change * vec_ref[j : j + 1]).astype(jnp.bfloat16))
        ref[...] = mixes[j]
    q_ref[...] = dot32(mixes[0], wr_ref[...], NN)
    k_ref[...] = dot32(mixes[2], wk_ref[...], NN)
    v_ref[...] = dot32(mixes[3], wv_ref[...], NN)
    first = down_ref[:, :128]
    pre_decay, pre_rate = dot32(mixes[1], first, NN), dot32(mixes[4], first, NN)
    pre_gate = dot32(mixes[5], down_ref[:, 128:], NN)
    lane = lax.broadcasted_iota(jnp.int32, pre_decay.shape, 1)
    pair = jnp.where(lane < DECAY_RANK, jnp.tanh(pre_decay), pre_rate)
    gate = jax.nn.sigmoid(pre_gate)
    hid_ref[:, :128] = pair
    hid_ref[:, 128:] = gate
    narrow_pair = pair.astype(jnp.bfloat16)
    dl_ref[...] = dot32(below(narrow_pair, False), up_ref[:, :128], NT)
    rl_ref[...] = dot32(below(narrow_pair, True), up_ref[:, :128], NT)
    gate_ref[...] = dot32(gate.astype(jnp.bfloat16), up_ref[:, 128:], NT)


def front_forward(x, vectors, w_r, w_k, w_v, down, up):
    tokens, width = x.shape
    wide = pl.BlockSpec((ROWS, width), lambda i: (i, 0))
    own = pl.BlockSpec((ROWS, OWN), lambda i: (i, 0))
    hid = pl.BlockSpec((ROWS, 256), lambda i: (i, 0))
    whole = lambda a: pl.BlockSpec(a.shape, lambda i: (0, 0))
    shape = jax.ShapeDtypeStruct
    return pl.pallas_call(
        front_kernel,
        grid=(tokens // ROWS,),
        in_specs=[wide] + [whole(a) for a in (vectors, w_r, w_k, w_v, down, up)],
        out_specs=[wide] * 6 + [own] * 6 + [hid],
        out_shape=[shape((tokens, width), jnp.bfloat16)] * 6
        + [shape((tokens, OWN), jnp.float32)] * 6
        + [shape((tokens, 256), jnp.float32)],
        scratch_shapes=[pltpu.VMEM((8, width), jnp.float32)],
        compiler_params=pltpu.CompilerParams(vmem_limit_bytes=60 << 20),
        cost_estimate=SMALL,
        name="front_forward",
    )(x, vectors, w_r, w_k, w_v, down, up)


def front_back_kernel(
    x_ref, before_ref, vec_ref, wr_ref, wk_ref, wv_ref, down_ref, up_ref,
    m1_ref, m4_ref, m5_ref, hid_ref,
    dq_ref, dk_ref, dv_ref, ddl_ref, drl_ref, dgate_ref, own_vec_ref, ffn_vec_ref,
    dx_ref, mine_ref, other_ref,
    edge_ref, sums_ref, misc_ref,
):
    step = pl.num_programs(0) - 1 - pl.program_id(0)
    core = lax.axis_index("dp") % 2
    own_start = pl.multiple_of(core * OWN, OWN)

    @pl.when(pl.program_id(0) == 0)
    def _():
        edge_ref[...] = jnp.zeros_like(edge_ref)
        sums_ref[...] = jnp.zeros_like(sums_ref)
        misc_ref[...] = jnp.zeros_like(misc_ref)

    unit, scale = row_norm(x_ref[...].astype(jnp.float32))
    gain, offset = vec_ref[12:13], vec_ref[13:14]
    normed = unit * gain + offset
    tail, _ = row_norm(before_ref[...].astype(jnp.float32))
    edge = (tail[15:] * gain + offset) * jnp.where(step == 0, 0.0, 1.0)
    change = shifted(normed, edge, True) - normed
    ddl, drl, dgate = ddl_ref[...], drl_ref[...], dgate_ref[...]
    hid = hid_ref[...]
    pair, gate = hid[:, :128], hid[:, 128:]
    lane = lax.broadcasted_iota(jnp.int32, pair.shape, 1)
    first_up, last_up = up_ref[:, :128], up_ref[:, 128:]
    pair_grad = jnp.where(
        lane < DECAY_RANK,
        dot32(ddl, first_up, NN) * (1.0 - pair * pair),
        dot32(drl, first_up, NN),
    ).astype(jnp.bfloat16)
    gate_grad = (dot32(dgate, last_up, NN) * gate * (1.0 - gate)).astype(jnp.bfloat16)
    narrow_pair, narrow_gate = pair.astype(jnp.bfloat16), gate.astype(jnp.bfloat16)
    own_rows = pl.ds(own_start, OWN)
    misc_ref[own_rows, 256:384] += dot32(ddl, below(narrow_pair, False), TN) + dot32(
        drl, below(narrow_pair, True), TN
    )
    misc_ref[own_rows, 384:512] += dot32(dgate, narrow_gate, TN)
    decay_part, rate_part = below(pair_grad, False), below(pair_grad, True)
    misc_ref[:, :128] += dot32(m1_ref[...], decay_part, TN) + dot32(m4_ref[...], rate_part, TN)
    misc_ref[:, 128:256] += dot32(m5_ref[...], gate_grad, TN)
    first_down = down_ref[:, :128]
    grads = (
        lambda: dot32(dq_ref[...], wr_ref[...], NT),
        lambda: dot32(decay_part, first_down, NT),
        lambda: dot32(dk_ref[...], wk_ref[...], NT),
        lambda: dot32(dv_ref[...], wv_ref[...], NT),
        lambda: dot32(rate_part, first_down, NT),
        lambda: dot32(gate_grad, down_ref[:, 128:], NT),
    )
    total = jnp.zeros_like(change)
    moved = jnp.zeros_like(change)
    for j, grad in enumerate(grads):
        now = grad()
        total = total + now
        moved = moved + now * vec_ref[j : j + 1]
        sums_ref[j : j + 1] += jnp.sum(now * change, axis=0, keepdims=True)
    dnormed = total - moved + shifted(moved, edge_ref[:1], False)
    edge_ref[:1] = moved[:1]
    sums_ref[12:13] += jnp.sum(dnormed * unit, axis=0, keepdims=True)
    sums_ref[13:14] += jnp.sum(dnormed, axis=0, keepdims=True)
    dunit = dnormed * gain
    dx_ref[...] = scale * (
        dunit
        - jnp.mean(dunit, axis=-1, keepdims=True)
        - unit * jnp.mean(dunit * unit, axis=-1, keepdims=True)
    )

    @pl.when(step == 0)
    def _():
        sums_ref[6:7] = ffn_vec_ref[0:1] * 0.5
        sums_ref[14:16] = ffn_vec_ref[1:3] * 0.5
        zeros = jnp.zeros((1, OWN), jnp.float32)
        for target, source in ((7, 0), (8, 1), (9, 2), (10, 3), (11, 4), (16, 5), (17, 6)):
            mine = own_vec_ref[source : source + 1]
            sums_ref[target : target + 1] = jnp.concatenate(
                [jnp.where(core == 0, mine, zeros), jnp.where(core == 0, zeros, mine)], axis=1
            )
        for block in range(EMBED // 128):
            lanes = slice(block * 128, (block + 1) * 128)
            misc_ref[lanes, 512:640] = sums_ref[:, lanes].T
        share = mine_ref.shape[1]
        for chip in range(mine_ref.shape[0]):
            low = misc_ref[2 * chip * share : (2 * chip + 1) * share]
            high = misc_ref[(2 * chip + 1) * share : (2 * chip + 2) * share]
            mine_ref[chip] = jnp.where(core == 0, low, high)
            other_ref[chip] = jnp.where(core == 0, high, low).astype(jnp.bfloat16)


def front_backward(
    x, vectors, w_r, w_k, w_v, down, up, mixes, hid, grads, own_vec, ffn_vec
):
    tokens, width = x.shape
    devices = lax.axis_size("dp")
    pieces = (devices // 2, EMBED // devices, 640)
    steps = tokens // ROWS
    wide = pl.BlockSpec((ROWS, width), lambda i: (steps - 1 - i, 0))
    before = pl.BlockSpec(
        (16, width), lambda i: (jnp.maximum((steps - 1 - i) * (ROWS // 16) - 1, 0), 0)
    )
    own = pl.BlockSpec((ROWS, OWN), lambda i: (steps - 1 - i, 0))
    hid_spec = pl.BlockSpec((ROWS, 256), lambda i: (steps - 1 - i, 0))
    whole = lambda a: pl.BlockSpec(a.shape, lambda i: (0, 0))
    shape = jax.ShapeDtypeStruct
    return pl.pallas_call(
        front_back_kernel,
        grid=(steps,),
        in_specs=[wide, before]
        + [whole(a) for a in (vectors, w_r, w_k, w_v, down, up)]
        + [wide] * 3
        + [hid_spec]
        + [own] * 6
        + [whole(own_vec), whole(ffn_vec)],
        out_specs=[wide] + [pl.BlockSpec(pieces, lambda i: (0, 0, 0))] * 2,
        out_shape=[
            shape((tokens, width), jnp.float32),
            shape(pieces, jnp.float32),
            shape(pieces, jnp.bfloat16),
        ],
        scratch_shapes=[
            pltpu.VMEM((8, width), jnp.float32),
            pltpu.VMEM((128, width), jnp.float32),
            pltpu.VMEM((EMBED, 640), jnp.float32),
        ],
        compiler_params=pltpu.CompilerParams(vmem_limit_bytes=60 << 20),
        cost_estimate=SMALL,
        name="front_backward",
    )(x, x, vectors, w_r, w_k, w_v, down, up, *mixes, hid, *grads, own_vec, ffn_vec)


def ffn_back_kernel(
    len_ref, res_ref, before_ref, cot_ref, mine_ref, other_ref, vec_ref, wo_ref,
    grad_ref, narrow_ref, gated_ref, dvec_ref,
    edge_ref,
):
    step = pl.num_programs(0) - 1 - pl.program_id(0)

    @pl.when(pl.program_id(0) == 0)
    def _():
        edge_ref[...] = jnp.zeros_like(edge_ref)
        dvec_ref[...] = jnp.zeros_like(dvec_ref)

    gain, offset, coefficient = vec_ref[14:15], vec_ref[15:16], vec_ref[6:7]
    unit, scale = row_norm(res_ref[...])
    normed = unit * gain + offset
    tail, _ = row_norm(before_ref[...])
    edge = (tail[7:] * gain + offset) * jnp.where(step == 0, 0.0, 1.0)
    change = shifted(normed, edge, True) - normed
    grad = mine_ref[...].astype(jnp.float32) + other_ref[...].astype(jnp.float32)
    moved = grad * coefficient
    dnormed = grad - moved + shifted(moved, edge_ref[:1], False)
    edge_ref[:1] = moved[:1]
    sums = lambda x: jnp.sum(x, axis=0, keepdims=True)
    dvec_ref[0:1] += sums(grad * change)
    dvec_ref[1:2] += sums(dnormed * unit)
    dvec_ref[2:3] += sums(dnormed)
    dunit = dnormed * gain
    row = lax.broadcasted_iota(jnp.int32, grad.shape, 0) + step * ROWS
    out_grad = jnp.where(row < len_ref[0], cot_ref[...].astype(jnp.float32), 0.0)
    total = out_grad + scale * (
        dunit
        - jnp.mean(dunit, axis=-1, keepdims=True)
        - unit * jnp.mean(dunit * unit, axis=-1, keepdims=True)
    )
    grad_ref[...] = total
    small = total.astype(jnp.bfloat16)
    core = lax.axis_index("dp") % 2
    narrow_ref[...] = jnp.where(core == 0, small[:, :OWN], small[:, OWN:])
    gated_ref[...] = dot32(small, wo_ref[...], NT)


def ffn_backward(length, residual, cot, mine, other, vectors, w_o_rows):
    tokens, width = residual.shape
    steps = tokens // ROWS
    wide = pl.BlockSpec((ROWS, width), lambda i: (steps - 1 - i, 0))
    before = pl.BlockSpec(
        (8, width), lambda i: (jnp.maximum((steps - 1 - i) * (ROWS // 8) - 1, 0), 0)
    )
    own = pl.BlockSpec((ROWS, OWN), lambda i: (steps - 1 - i, 0))
    whole = lambda a: pl.BlockSpec(a.shape, lambda i: (0, 0))
    shape = jax.ShapeDtypeStruct
    return pl.pallas_call(
        ffn_back_kernel,
        grid=(steps,),
        in_specs=[pl.BlockSpec(memory_space=pltpu.SMEM), wide, before]
        + [wide] * 3
        + [whole(vectors), whole(w_o_rows)],
        out_specs=[wide, own, own, pl.BlockSpec((8, width), lambda i: (0, 0))],
        out_shape=[
            shape((tokens, width), jnp.float32),
            shape((tokens, OWN), jnp.bfloat16),
            shape((tokens, OWN), jnp.float32),
            shape((8, width), jnp.float32),
        ],
        scratch_shapes=[pltpu.VMEM((8, width), jnp.float32)],
        compiler_params=pltpu.CompilerParams(vmem_limit_bytes=60 << 20),
        cost_estimate=SMALL,
        name="ffn_backward",
    )(length, residual, residual, cot, mine, other, vectors, w_o_rows)


def att_grad_kernel(m0_ref, m2_ref, m3_ref, gated_ref, dq_ref, dk_ref, dv_ref, do_ref,
                    send_a, keep_a, send_b, keep_b):
    chip = lax.axis_index("dp") // 2
    by_x, by_y = chip % 2 == 0, (chip // 2) % 2 == 0
    first = ((m0_ref, dq_ref), (gated_ref, do_ref))
    second = ((m2_ref, dk_ref), (m3_ref, dv_ref))
    for half in range(2):
        lanes = slice(half * OWN, (half + 1) * OWN)
        block = dot32(first[half][0][...], first[half][1][...], TN).astype(jnp.bfloat16)
        for y in range(2):
            low, high = block[y * 128 : y * 128 + 64], block[y * 128 + 64 : y * 128 + 128]
            send_a[y, :, lanes] = jnp.where(by_x, high, low)
            keep_a[y, :, lanes] = jnp.where(by_x, low, high)
        block = dot32(second[half][0][...], second[half][1][...], TN).astype(jnp.bfloat16)
        for x in range(2):
            low, high = block[x * 64 : x * 64 + 64], block[128 + x * 64 : 128 + x * 64 + 64]
            send_b[x, :, lanes] = jnp.where(by_y, high, low)
            keep_b[x, :, lanes] = jnp.where(by_y, low, high)


def att_gradients(mixes, gated, grads, own_grad):
    tokens = gated.shape[0]
    left = pl.BlockSpec((tokens, 256), lambda i: (0, i))
    right = pl.BlockSpec((tokens, OWN), lambda i: (0, 0))
    out = pl.BlockSpec((2, 64, 2 * OWN), lambda i: (i, 0, 0))
    return pl.pallas_call(
        att_grad_kernel,
        grid=(4,),
        in_specs=[left] * 4 + [right] * 4,
        out_specs=[out] * 4,
        out_shape=[jax.ShapeDtypeStruct((8, 64, 2 * OWN), jnp.bfloat16)] * 4,
        compiler_params=pltpu.CompilerParams(vmem_limit_bytes=60 << 20),
        cost_estimate=SMALL,
        name="att_gradients",
    )(*mixes, gated, *grads, own_grad)


def swap(block, mask):
    size = lax.axis_size("dp")
    return lax.ppermute(block, "dp", [(i, i ^ mask) for i in range(size)])


def bit_of(mask):
    return (lax.axis_index("dp") // mask) % 2


def in_order(mask, own, other, axis):
    lower = bit_of(mask) == 0
    return jnp.where(
        lower, jnp.concatenate([own, other], axis=axis), jnp.concatenate([other, own], axis=axis)
    )


def chip_masks():
    size = lax.axis_size("dp")
    masks = []
    while 2 << len(masks) < size:
        masks.append(2 << len(masks))
    return masks


def steps_of(kind):
    masks = chip_masks()
    near, far = [[mask] for mask in masks[:2]], [[mask] for mask in masks[2:][::-1]]
    first = [[far[0][0], far[1][0], far[0][0] | far[1][0]]] if len(far) == 2 else far
    return [first + near[::-1], first + near, far + near[::-1], far + near, near + far][kind]


class Held:
    def __init__(self, value):
        self.value = value


def meet(movers, *arrays):
    held = []
    for mover in movers:
        held += [x[0] for x in mover.arrived if x[0] not in held]
    out = lax.optimization_barrier(tuple(x.value for x in held) + arrays)
    for x, value in zip(held, out):
        x.value = value
    return out[len(held) :]


def read(arrived):
    return [x.value if lanes is None else x.value[..., lanes] for x, lanes in arrived]


class Gather:
    def __init__(self, block, kind, places=(0,)):
        self.steps = steps_of(kind)
        self.held = block[None]
        self.places = [0]
        self.arrived = []
        self.masks = []

    def merge(self):
        if self.arrived:
            self.held = jnp.concatenate([self.held] + read(self.arrived), axis=0)
            self.places = self.places + [p ^ (m // 2) for m in self.masks for p in self.places]
            self.arrived = []

    def step(self):
        if self.steps:
            self.merge()
            self.masks = self.steps.pop(0)
            self.arrived = [(Held(swap(self.held, mask)), None) for mask in self.masks]
        return self

    def run(self):
        while self.steps:
            self.step()
        return self

    def split(self, kinds):
        width = self.held.shape[-1] // len(kinds)
        out = []
        for i, kind in enumerate(kinds):
            part = Gather.__new__(Gather)
            cut = slice(i * width, (i + 1) * width)
            part.steps = steps_of(kind)[len(steps_of(kind)) - len(self.steps) :]
            part.held = self.held[..., cut]
            part.arrived = [(x, cut) for x, _ in self.arrived]
            part.places, part.masks = self.places, self.masks
            out.append(part)
        return out


def place_kernel(places, cuts, *refs):
    sources, outs = refs[: len(places)], refs[len(places) :]
    chip = lax.axis_index("dp") // 2
    for source, (part, list_of) in zip(sources, places):
        for j, place in enumerate(list_of):
            for out, (first, rows, lanes) in zip(outs, cuts):
                start = pl.multiple_of((chip ^ place) * rows, rows)
                lane, width = lanes[part]
                at = sum(w for _, w in lanes[:part])
                out[pl.ds(start, rows), at : at + width] = source[
                    j, first : first + rows, lane : lane + width
                ]


def assemble(gathers, cuts=None):
    gathers = [g.run() for g in gathers]
    rows = gathers[0].held.shape[1]
    cuts = cuts or ((0, rows, [(0, g.held.shape[2]) for g in gathers]),)
    sources, places = [], []
    for i, g in enumerate(gathers):
        sources += [g.held] + read(g.arrived)
        shifts = [0] + [mask // 2 for mask in g.masks]
        places += [(i, [p ^ shift for p in g.places]) for shift in shifts]
    count = lax.axis_size("dp") // 2
    if any(cut[1] % 16 for cut in cuts):
        return assemble_plain(sources, places, cuts, count)
    space = pl.BlockSpec(memory_space=pltpu.VMEM)
    return pl.pallas_call(
        partial(place_kernel, places, cuts),
        in_specs=[space] * len(sources),
        out_specs=[space] * len(cuts),
        out_shape=[
            jax.ShapeDtypeStruct((count * n, sum(w for _, w in lanes)), sources[0].dtype)
            for _, n, lanes in cuts
        ],
        compiler_params=pltpu.CompilerParams(vmem_limit_bytes=32 << 20),
        cost_estimate=SMALL,
        name="assemble",
    )(*sources)


def assemble_plain(sources, places, cuts, count):
    chip = lax.axis_index("dp") // 2
    parts = []
    for part in sorted({part for part, _ in places}):
        blocks = jnp.concatenate([x for x, (at, _) in zip(sources, places) if at == part])
        where = [p for at, list_of in places if at == part for p in list_of]
        blocks = jnp.stack([blocks[where.index(i)] for i in range(count)])
        parts.append(jnp.take(blocks, chip ^ lax.iota(jnp.int32, count), axis=0))
    return [
        jnp.concatenate(
            [x[:, first : first + n, at : at + w] for x, (at, w) in zip(parts, lanes)], axis=-1
        ).reshape(count * n, -1)
        for first, n, lanes in cuts
    ]


class Scatter:
    def __init__(self, parts, kind):
        self.steps = steps_of(kind)[::-1]
        self.axes = chip_masks()[::-1]
        self.sources = [parts.reshape((2,) * len(self.axes) + parts.shape[1:])]
        self.arrived = []
        self.sent = None

    @classmethod
    def begun(cls, sent, kept, kind):
        out = cls.__new__(cls)
        out.steps = steps_of(kind)[::-1]
        out.axes = [axis for axis in chip_masks()[::-1] if axis != out.steps[0][0]]
        out.sources = [kept.reshape((2,) * len(out.axes) + kept.shape[1:])]
        out.arrived = []
        out.sent = [sent.reshape(out.sources[0].shape)]
        return out

    def pick(self, sources, mask, gone):
        out = []
        for x in sources:
            for place in reversed(range(len(self.axes))):
                axis = self.axes[place]
                if axis in gone:
                    which = bit_of(axis) if not mask & axis else 1 - bit_of(axis)
                    x = lax.dynamic_index_in_dim(x, which, place, keepdims=False)
            out.append(x)
        return out

    def prepare(self):
        if self.sent is not None:
            return self
        masks = self.steps[0]
        sources = self.sources + read(self.arrived)
        gone = [axis for axis in self.axes if any(mask & axis for mask in masks)]
        self.sent = [
            sum(x.astype(jnp.float32) for x in self.pick(sources, mask, gone)).astype(jnp.bfloat16)
            for mask in masks
        ]
        self.sources = self.pick(sources, 0, gone)
        self.axes = [axis for axis in self.axes if axis not in gone]
        self.arrived = []
        return self

    def step(self):
        return together([self])[0]

    def run(self):
        while self.steps:
            self.step()
        return self

    def total(self):
        return sum(x.astype(jnp.float32) for x in self.sources + read(self.arrived))


def together(parts):
    if not parts[0].steps:
        return parts
    for part in parts:
        part.prepare()
    for i, mask in enumerate(parts[0].steps[0]):
        sent = [part.sent[i] for part in parts]
        got = Held(swap(sent[0] if len(sent) == 1 else jnp.concatenate(sent, axis=-1), mask))
        at = 0
        for part, x in zip(parts, sent):
            lanes = slice(at, at + x.shape[-1]) if len(sent) > 1 else None
            part.arrived.append((got, lanes))
            at += x.shape[-1]
    for part in parts:
        part.steps.pop(0)
        part.sent_now, part.sent = part.sent[0], None
    return parts


def norm_rows(features, gain_row, offset_row):
    average = jnp.mean(features, axis=-1, keepdims=True)
    centred = features - average
    variance = jnp.mean(centred * centred, axis=-1, keepdims=True)
    return centred * lax.rsqrt(variance + 1e-05) * gain_row + offset_row


def product(operand, weight_matrix):
    return jnp.dot(operand, weight_matrix, preferred_element_type=jnp.float32)


def input_gradient_rows(upstream_gradient, weight_matrix):
    return lax.dot_general(
        upstream_gradient,
        weight_matrix,
        (((1,), (1,)), ((), ())),
        preferred_element_type=jnp.float32,
    )


def weight_gradient(operand, upstream_gradient):
    return lax.dot_general(
        operand, upstream_gradient, (((0,), (0,)), ((), ())), preferred_element_type=jnp.float32
    )


def earlier(rows):
    return jnp.concatenate([jnp.zeros_like(rows[:1]), rows[:-1]], axis=0)


def ffn_mix(residual, vectors):
    second = norm_rows(residual, vectors[14], vectors[15])
    return second + (earlier(second) - second) * vectors[6]


def narrow(x):
    return x.astype(jnp.bfloat16)


def local(
    inputs,
    lengths,
    attention_projections,
    channel_key_weight,
    channel_value_weight,
    lowrank_down_weight,
    lowrank_up_weight,
    per_feature_parameters,
    cotangent,
):
    devices = lax.axis_size("dp")
    chips = devices // 2
    device = lax.axis_index("dp")
    chip, core = device // 2, device % 2
    row_count = inputs.shape[0]
    slots = 2 * row_count
    share = EMBED // devices
    pair_share = 2 * share
    units = channel_value_weight.shape[0]
    half_units = chips * units

    def own_cut(x, which):
        return lax.dynamic_slice_in_dim(x, which * OWN, OWN, x.ndim - 1)

    def own_rows(x, which):
        return lax.dynamic_slice_in_dim(x, which * row_count, row_count, 0)

    pair_rows = in_order(
        1,
        own_cut(attention_projections, core),
        swap(own_cut(attention_projections, 1 - core), 1),
        1,
    )
    lora = jnp.concatenate([lowrank_down_weight, lowrank_up_weight.T], axis=1)
    vector_rows = jnp.pad(per_feature_parameters.T, ((0, 0), (0, 128 - 18)))
    vector_rows = vector_rows.reshape(share // 4, OWN)
    first_rows = 3 * pair_share
    misc_rows = share + share // 4 + (share // 4) % 16
    block = jnp.concatenate(
        [
            pair_rows[:3].reshape(first_rows, OWN),
            lora,
            jnp.pad(vector_rows, ((0, (share // 4) % 16), (0, 0))),
        ],
        axis=0,
    )
    half = half_units // 2
    quarter = OWN // 2
    first = Gather(block, 0).step()
    w_o_part = Gather(pair_rows[3], 4).step().step()
    key_in, raw, cot, _ = meet([], channel_key_weight, inputs, cotangent, first.held)
    key_cut = key_in.reshape(share, chips, 2, units)

    def key_columns(which):
        return lax.dynamic_index_in_dim(key_cut, which, 2, keepdims=False).reshape(share, half_units)

    key_rows = in_order(1, key_columns(core), swap(key_columns(1 - core), 1), 0)
    tokens = in_order(1, raw, swap(raw, 1), 0)
    cot = in_order(1, cot, swap(cot, 1), 0)
    key_rows, tokens, cot = meet([first, w_o_part], key_rows, tokens, cot)
    first = first.split((0, 1))
    for part in first:
        part.step()
    key_part = Gather(key_rows, 2).step()
    (tokens,) = meet(first, tokens)
    for part in first:
        part.step()
    value_block, *_ = meet([key_part], channel_value_weight, *[part.held for part in first])
    key_part.step()
    value_part = Gather(value_block, 2).step()
    w_o_part.step()
    (tokens,) = meet(first + [key_part, value_part], tokens)
    key_parts = key_part.split((2, 3))
    for part in key_parts:
        part.step()
    w_r, w_k, w_v, misc = assemble(
        first,
        [(i * pair_share, pair_share, [(0, quarter)] * 2) for i in range(3)]
        + [(first_rows, misc_rows, [(0, quarter)] * 2)],
    )
    misc = misc.reshape(chips, 1, misc_rows, OWN)
    misc = in_order(1, misc, swap(misc, 1), 1)
    value_part.step()
    lora = misc[:, :, :share].reshape(EMBED, OWN)
    down, up_t = lora[:, :256], lax.dynamic_slice_in_dim(lora[:, 256:], core * OWN, OWN, 0)
    vectors = misc[:, :, share : share + share // 4].reshape(EMBED, 128)[:, :18].T
    vectors = vectors.astype(jnp.float32)
    own_vectors = own_cut(vectors, core)
    used = jnp.concatenate([own_vectors[7:12], own_vectors[16:18], own_vectors[:1]], axis=0)
    length = lax.dynamic_index_in_dim(lengths, chip, 0)
    live = (lax.iota(jnp.int32, slots) < length)[:, None]

    *mixes, queries, keys, values, decay_low, rate_low, gate_rows, hid = front_forward(
        tokens, vectors, w_r, w_k, w_v, down, up_t
    )
    terms = meet(
        key_parts + [value_part, w_o_part],
        queries, keys, values, decay_low, rate_low, gate_rows,
    )
    value_parts = value_part.split((2, 3))
    for part in key_parts + value_parts:
        part.step()
    w_o_part.step()
    blocks = slots // (CHUNK * STEP_CHUNKS)
    zero_state = jnp.zeros((2, CHUNK, LANES), jnp.float32)
    gated, *saved, _ = wkv_forward(0, blocks, length, used, zero_state, terms)
    gated, cot, tokens = meet(key_parts + value_parts, gated, cot, tokens)
    for part in value_parts:
        part.step()
    gated, *_ = meet([w_o_part] + key_parts, gated, *[part.held for part in value_parts])
    gated_all = in_order(1, gated, swap(gated, 1), 1)
    (w_o_own,) = assemble([w_o_part])
    w_o = in_order(1, w_o_own, swap(w_o_own, 1), 1)
    (key_weight,) = assemble(key_parts)
    residual = tokens.astype(jnp.float32) + product(gated_all, w_o)
    ffn_in = narrow(ffn_mix(residual, vectors))
    positive = jax.nn.relu(product(ffn_in, key_weight))
    hidden = narrow(jnp.square(positive))
    out_narrow = jnp.where(live, cot, jnp.zeros_like(cot))
    grad_value = narrow(weight_gradient(hidden, out_narrow)).reshape(chips, units, EMBED)
    w_o_rows = lax.dynamic_slice_in_dim(w_o, core * OWN, OWN, 0)
    value_scatter = [
        Scatter(grad_value[..., i * OWN : (i + 1) * OWN], 2 + i).prepare() for i in range(2)
    ]
    hidden, positive, out_narrow, w_o_rows, *sent = meet(
        value_parts, hidden, positive, out_narrow, w_o_rows, *[m.sent[0] for m in value_scatter]
    )
    for part, x in zip(value_scatter, sent):
        part.sent = [x]
        part.step()
    (value_weight,) = assemble(value_parts)

    pre_narrow = narrow(2.0 * positive * input_gradient_rows(out_narrow, value_weight))
    ffn_in_grad = narrow(input_gradient_rows(pre_narrow, key_weight))
    other_grad = swap(ffn_in_grad, 1)
    grad_key = narrow(weight_gradient(ffn_in, pre_narrow)).reshape(chips, pair_share, half_units)
    residual_grad, own_grad, gated_grad, ffn_vec = ffn_backward(
        length, residual, cot, ffn_in_grad, other_grad, vectors, w_o_rows
    )
    key_scatter = [
        Scatter(grad_key[:, :, i * half : (i + 1) * half], 2 + i).prepare() for i in range(2)
    ]
    gated_grad, *sent = meet([], gated_grad, *[m.sent[0] for m in key_scatter])
    for part, x in zip(key_scatter, sent):
        part.sent = [x]
        part.step()
    terms = [*terms, gated_grad, *saved]
    zero_sums = jnp.zeros((8, OWN), jnp.float32)
    early = blocks // 2
    *before, sums, state = wkv_backward(
        early, blocks - early, length, used, zero_state, zero_sums, terms
    )
    state, sums = meet(value_scatter, state, sums)
    for part in value_scatter:
        part.step()
    *low_grads, own_vec, _ = wkv_backward(0, early, length, used, state, sums, terms, before)
    if pair_share == 64:
        sent_a, kept_a, sent_b, kept_b = att_gradients(
            (mixes[0], mixes[2], mixes[3]), gated_all, low_grads[:3], own_grad
        )
        att_scatter = [Scatter.begun(sent_a, kept_a, 2), Scatter.begun(sent_b, kept_b, 3)]
    else:
        grads = [weight_gradient(mixes[m], g) for m, g in zip((0, 2, 3), low_grads)]
        grad_o = weight_gradient(gated_all, own_grad)
        att_scatter = [
            Scatter(
                narrow(jnp.concatenate(x, axis=1)).reshape(chips, pair_share, EMBED), 2 + i
            ).prepare()
            for i, x in enumerate(((grads[0], grad_o), (grads[1], grads[2])))
        ]
    own_vec, *sent = meet(
        key_scatter + value_scatter, own_vec, *[m.sent[0] for m in att_scatter]
    )
    for part, x in zip(att_scatter, sent):
        part.sent = [x]
        part.step()
    for part in key_scatter:
        part.step()
    together(value_scatter)
    own_vec, *_ = meet([], own_vec, *[m.sent_now for m in key_scatter])
    token_part, misc_mine, misc_other = front_backward(
        tokens, vectors, w_r, w_k, w_v, down, up_t, (mixes[1], mixes[4], mixes[5]), hid,
        low_grads, own_vec, ffn_vec,
    )
    misc_other = swap(misc_other, 1)
    token_part, misc_mine, misc_other = meet(
        att_scatter + key_scatter + value_scatter, token_part, misc_mine, misc_other
    )
    for part in att_scatter:
        part.step()
    misc_sum = misc_mine + misc_other.astype(jnp.float32)
    misc_sum = jnp.concatenate([misc_sum[..., :320], misc_sum[..., 320:]], axis=1)
    misc_scatter = Scatter(misc_sum, 3).step()
    together(key_scatter)
    together(value_scatter)
    token_part, hidden = meet(key_scatter + [misc_scatter], token_part, hidden)
    misc_scatter.step()
    together(key_scatter)
    (token_part,) = meet(att_scatter + [misc_scatter], token_part)
    masks = chip_masks()
    last_parts = att_scatter + [misc_scatter]
    if len(misc_scatter.steps) == 2:
        for part in last_parts:
            part.steps = [[masks[2], masks[3], masks[2] | masks[3]]]
    together(last_parts)
    ffn_part = product(hidden, value_weight)
    input_gradient = (
        own_rows(residual_grad, core)
        + own_rows(token_part, core)
        + swap(own_rows(token_part, 1 - core), 1)
    )
    ffn_out = own_rows(ffn_part, core) + swap(own_rows(ffn_part, 1 - core), 1)
    output = narrow(jnp.where(own_rows(live, core), own_rows(residual, core) + ffn_out, 0.0))
    value_sum = jnp.concatenate(
        [x.run().total() for x in value_scatter], axis=1
    )
    while key_scatter[0].steps:
        together(key_scatter)
    key_sum = jnp.concatenate([x.total() for x in key_scatter], axis=1).reshape(2, share, -1)

    def exchange(x):
        mine = lax.dynamic_index_in_dim(x, core, 0, keepdims=False)
        return mine, swap(lax.dynamic_index_in_dim(x, 1 - core, 0, keepdims=False), 1)

    key_mine, key_theirs = exchange(key_sum)
    input_gradient, value_sum, key_mine, key_theirs = meet(
        last_parts, input_gradient, value_sum, key_mine, key_theirs
    )
    while last_parts[0].steps:
        together(last_parts)
    first_sum, second_sum, misc_sum = [x.total() for x in last_parts]
    misc_sum = jnp.concatenate([misc_sum[:share], misc_sum[share:]], axis=1)
    att_sum = jnp.concatenate(
        [first_sum[:, :OWN], second_sum, first_sum[:, OWN:]], axis=1
    )
    mine, theirs = exchange(att_sum.reshape(2, share, -1))
    shard_mixer = jnp.stack(
        [
            in_order(1, mine[:, i * OWN : (i + 1) * OWN], theirs[:, i * OWN : (i + 1) * OWN], 1)
            for i in range(4)
        ]
    )
    shard_key = in_order(
        1,
        key_mine.reshape(share, chips, 1, units),
        key_theirs.reshape(share, chips, 1, units),
        2,
    ).reshape(share, 2 * half_units)
    return (
        output,
        input_gradient,
        shard_mixer,
        shard_key,
        value_sum,
        misc_sum[:, :256],
        misc_sum[:, 256:512].T,
        misc_sum[:, 512:530].T,
    )


def solution(mesh):
    in_specs = (
        P("dp", None),
        P(),
        P(None, "dp", None),
        P("dp", None),
        P("dp", None),
        P("dp", None),
        P(None, "dp"),
        P(None, "dp"),
        P("dp", None),
    )
    out_specs = (
        P("dp", None),
        P("dp", None),
        P(None, "dp", None),
        P("dp", None),
        P("dp", None),
        P("dp", None),
        P(None, "dp"),
        P(None, "dp"),
    )
    return jax.shard_map(local, mesh=mesh, in_specs=in_specs, out_specs=out_specs, check_vma=False)
```

```python
from functools import partial

import jax
import jax.numpy as jnp
from jax import lax
from jax.experimental import pallas as pl
from jax.experimental.pallas import tpu as pltpu
from jax.sharding import PartitionSpec as P

HEADS = 16
HEAD_SIZE = 64
DECAY_RANK = 64
RATE_RANK = 64
EMBED = 1024
OWN = EMBED // 2
PRECISE = lax.Precision.HIGHEST


CHUNK = 64
LANES = 256
GROUP_HEADS = 4
STEP_CHUNKS = 2
SMALL = pl.CostEstimate(flops=1, bytes_accessed=1, transcendentals=0)

NN = (((1,), (0,)), ((), ()))
NT = (((1,), (1,)), ((), ()))
TN = (((0,), (0,)), ((), ()))


def halves(x):
    high = x.astype(jnp.bfloat16)
    return high, (x - high.astype(jnp.float32)).astype(jnp.bfloat16)


def whole(x):
    return (x.astype(jnp.bfloat16),)


def dot32(a, b, dims):
    return lax.dot_general(a, b, dims, preferred_element_type=jnp.float32)


def mul(left, right, dims=NN):
    if len(left) == 1 or len(right) == 1:
        return dot32(left[0], right[0], dims)
    rows = left[0].shape[0]
    both = dot32(jnp.concatenate(left, axis=0), right[0], dims)
    return both[:rows] + both[rows:] + dot32(left[0], right[1], dims)


def tmul(left, right, masks):
    full = dot32(left[0], right[0], TN)
    if len(left) > 1 and len(right) > 1:
        full = full + dot32(left[1], right[0], TN) + dot32(left[0], right[1], TN)
    return sum(full[h * CHUNK : (h + 1) * CHUNK] * masks[h][:1].astype(jnp.float32) for h in range(GROUP_HEADS))


def spread(pair, masks):
    return tuple(
        jnp.concatenate([part * masks[h] for h in range(GROUP_HEADS)], axis=0) for part in pair
    )


def stack(first, second):
    return tuple(jnp.concatenate([x, y], axis=0) for x, y in zip(first, second))


def head_masks():
    lane = lax.broadcasted_iota(jnp.int32, (CHUNK, LANES), 1) // CHUNK
    return [(lane == h).astype(jnp.float32).astype(jnp.bfloat16) for h in range(GROUP_HEADS)]


def places():
    row = lax.broadcasted_iota(jnp.int32, (CHUNK, LANES), 0)
    col = lax.broadcasted_iota(jnp.int32, (CHUNK, LANES), 1) % CHUNK
    return row, col


def running_sum(x, upper=False):
    row = lax.broadcasted_iota(jnp.int32, (CHUNK, CHUNK), 0)
    col = lax.broadcasted_iota(jnp.int32, (CHUNK, CHUNK), 1)
    ones = (row <= col if upper else col <= row).astype(jnp.float32).astype(jnp.bfloat16)
    high, rest = halves(x)
    low = (x - high.astype(jnp.float32) - rest.astype(jnp.float32)).astype(jnp.bfloat16)
    return dot32(ones, high, NN) + dot32(ones, rest, NN) + dot32(ones, low, NN)


def scaled_forms(q, w, k, a, b):
    total = running_sum(w)
    before = total - w
    middle = total[CHUNK // 2 - 1 : CHUNK // 2]
    end = total[CHUNK - 1 :]
    ea = jnp.exp(before - middle)
    eq = jnp.exp(total - middle)
    eb = jnp.exp(middle - total)
    ee = jnp.exp(end - total)
    return (a * ea, q * eq, b * eb, k * eb, b * ee, k * ee), (ea, eq, eb, ee), (jnp.exp(middle), jnp.exp(end))


def each(fn, *columns):
    return [fn(*row) for row in zip(*columns)]


def block_ones():
    row = lax.broadcasted_iota(jnp.int32, (LANES, LANES), 0) // CHUNK
    col = lax.broadcasted_iota(jnp.int32, (LANES, LANES), 1) // CHUNK
    return (row == col).astype(jnp.float32).astype(jnp.bfloat16)


def head_sum(x, ones):
    rows = x.shape[0]
    both = dot32(jnp.concatenate(halves(x), axis=0), ones, NN)
    return both[:rows] + both[rows:]


def prepared(keys, decay_low, rate_low, live, vec, ones):
    sig = jax.nn.sigmoid(vec[0] + decay_low)
    log_decay = (-0.6065306597126334) * sig * live
    rates = jax.nn.sigmoid(vec[1] + rate_low)
    scaled = keys * vec[2]
    inverse = lax.rsqrt(head_sum(scaled * scaled, ones) + 1e-06)
    unit_keys = scaled * inverse
    factor = (1.0 + (rates - 1.0) * vec[3]) * live
    return log_decay, keys * factor, -unit_keys, unit_keys * rates * live, sig, rates, inverse, factor


def read_out(o, q, k, v, vec, ones):
    centred = o - head_sum(o, ones) * (1.0 / CHUNK)
    scale = lax.rsqrt(head_sum(centred * centred, ones) * (1.0 / CHUNK) + 0.00064)
    normed = centred * scale
    weight = head_sum(q * k * vec[4], ones)
    return normed, scale, weight, normed * vec[5] + vec[6] + weight * v


def unit_slices():
    return [
        (slice(c * CHUNK, (c + 1) * CHUNK), slice(g * LANES, (g + 1) * LANES))
        for c in range(STEP_CHUNKS)
        for g in range(2)
    ]


def unit_live(length, step):
    row = lax.broadcasted_iota(jnp.int32, (CHUNK, LANES), 0)
    start = step * (STEP_CHUNKS * CHUNK)
    live = [(row + (start + c * CHUNK) < length).astype(jnp.float32) for c in range(STEP_CHUNKS)]
    return [live[c] for c in range(STEP_CHUNKS) for g in range(2)]


def unit_vectors(vec_ref):
    vec = [[vec_ref[i : i + 1, g * LANES : (g + 1) * LANES] for i in range(7)] for g in range(2)]
    return [vec[g] for c in range(STEP_CHUNKS) for g in range(2)]


def forward_kernel(base, *refs):
    len_ref, vec_ref, start_ref, q_ref, keys_ref, v_ref, dl_ref, rl_ref, gate_ref = refs[:9]
    (
        out_ref, o_ref, t_ref, aqb_ref, aak_ref, aqk_ref, y_ref, z_ref, trt_ref, qe_ref, state_ref,
    ) = refs[-11:]

    @pl.when(pl.program_id(0) == 0)
    def _():
        state_ref[...] = start_ref[...]

    masks = head_masks()
    row, col = places()
    strict = (col < row).astype(jnp.float32)
    within = (col <= row).astype(jnp.float32)
    eye = (col == row).astype(jnp.float32)
    ones = block_ones()
    units = unit_slices()
    live = unit_live(len_ref[0], pl.program_id(0) + base)
    vec = unit_vectors(vec_ref)
    load = lambda ref: [ref[u] for u in units]
    q, keys, v = load(q_ref), load(keys_ref), load(v_ref)
    ready = each(
        lambda x, y, z, m, n: prepared(x, y, z, m, n, ones), keys, load(dl_ref), load(rl_ref), live, vec
    )
    w, k, a, b = ([x[i] for x in ready] for i in range(4))
    forms = each(scaled_forms, q, w, k, a, b)
    ah, qh, bh, kh, bt, kt = ([f[0][i] for f in forms] for i in range(6))
    emid = [f[2][0] for f in forms]
    eend = [f[2][1] for f in forms]
    aq = each(lambda x, y: halves(jnp.concatenate([x, y], axis=0)), ah, qh)
    with_b = each(lambda l, r: mul(l, spread(halves(r), masks), NT), aq, bh)
    with_k = each(lambda l, r: mul(l, spread(halves(r), masks), NT), aq, kh)
    aab = [x[:CHUNK] * strict for x in with_b]
    aqb = [halves(x[CHUNK:] * within) for x in with_b]
    aak = [halves(x[:CHUNK] * strict) for x in with_k]
    aqk = [halves(x[CHUNK:] * within) for x in with_k]
    p = [halves(x * (row // 8 == col // 8)) for x in aab]
    t = [eye + x * (row // 8 == col // 8) for x in aab]
    p2 = each(lambda x: halves(mul(x, spread(x, masks))), p)
    both = each(lambda x, y: mul(stack(x, halves(y)), spread(x, masks)), p2, t)
    p4 = [halves(x[:CHUNK]) for x in both]
    t = each(lambda x, y: x + y[CHUNK:], t, both)
    t = each(lambda x, y: x + mul(halves(x), spread(y, masks)), t, p4)
    for size in (8, 16, 32):
        corner = ((row // size) % 2 == 1) & (col // size == row // size - 1)
        ts = [halves(x) for x in t]
        n = [halves(x * corner) for x in aab]
        tn = each(lambda x, y: halves(mul(x, spread(y, masks))), ts, n)
        t = each(lambda x, y, z: x + mul(y, spread(z, masks)), t, tn, ts)
    ts = [halves(x) for x in t]
    vs = [halves(x) for x in v]
    vm = [spread(x, masks) for x in vs]
    wide = each(lambda x, y, e: mul(x, spread(halves(y * e), masks)), ts, ah, emid)
    r0 = each(mul, aak, vm)
    y0 = each(lambda x, y: mul(x, spread(halves(y), masks)), ts, r0)
    wides = [halves(x) for x in wide]
    qe = each(lambda x, e, y, z: x * e + mul(y, spread(z, masks)), qh, emid, aqb, wides)
    y0s = [halves(x) for x in y0]
    part = each(lambda x, y, z, u: mul(x, spread(y, masks)) + mul(z, u), aqb, y0s, aqk, vm)
    bts = [halves(x) for x in bt]
    diag = [eye * e for e in eend]
    tr = each(lambda x, y, d: tmul(x, y, masks) + d, bts, wides, diag)
    trt = each(lambda x, y, d: tmul(y, x, masks) + d, bts, wides, diag)
    inject = each(lambda x, y, z, u: tmul(stack(x, halves(y)), stack(z, u), masks), bts, kt, y0s, vs)
    wq = each(lambda x, y: stack(x, halves(y)), wides, qe)
    z = []
    out = []
    for c in range(STEP_CHUNKS):
        for g in range(2):
            i = c * 2 + g
            now = state_ref[g]
            nows = spread(halves(now), masks)
            state_ref[g] = mul(halves(tr[i]), nows) + inject[i]
            z.append(now)
            out.append(mul(wq[i], nows))
    o = each(lambda x, y: x[CHUNK:] + y, out, part)
    mixed = each(lambda x, y, z, m, n: read_out(x, y, z, m, n, ones)[3], o, q, k, v, vec)
    for i, u in enumerate(units):
        out_ref[u] = (mixed[i] * gate_ref[u]).astype(jnp.bfloat16)
        o_ref[u] = o[i]
        y_ref[u] = (out[i][:CHUNK] + y0[i]).astype(jnp.bfloat16)
        t_ref[u] = ts[i][0]
        aqb_ref[u] = aqb[i][0]
        aak_ref[u] = aak[i][0]
        aqk_ref[u] = aqk[i][0]
        z_ref[u] = z[i]
        trt_ref[u] = trt[i].astype(jnp.bfloat16)
        qe_ref[u] = qe[i].astype(jnp.bfloat16)


def backward_kernel(base, *refs):
    (
        len_ref, vec_ref, start_ref, sums_ref, q_ref, keys_ref, v_ref, dl_ref, rl_ref, gate_ref,
        g_ref, o_ref, t_ref, aqb_ref, aak_ref, aqk_ref, y_ref, z_ref, trt_ref, qe_ref,
    ) = refs[:20]
    dq_ref, dkeys_ref, dv_ref, ddl_ref, drl_ref, dgate_ref, dvec_ref, state_ref = refs[-8:]
    step = base + pl.num_programs(0) - 1 - pl.program_id(0)

    @pl.when(pl.program_id(0) == 0)
    def _():
        state_ref[...] = start_ref[...]
        dvec_ref[...] = sums_ref[...]

    masks = head_masks()
    row, col = places()
    strict = (col < row).astype(jnp.float32)
    within = (col <= row).astype(jnp.float32)
    ones = block_ones()
    units = unit_slices()
    live = unit_live(len_ref[0], step)
    vec = unit_vectors(vec_ref)
    load = lambda ref: [ref[u] for u in units]
    q, keys, v, g = load(q_ref), load(keys_ref), load(v_ref), load(g_ref)
    ready = each(
        lambda x, y, z, m, n: prepared(x, y, z, m, n, ones), keys, load(dl_ref), load(rl_ref), live, vec
    )
    w, k, a, b, sig, rates, inverse, factor = ([x[i] for x in ready] for i in range(8))
    seen = each(lambda x, y, z, m, n: read_out(x, y, z, m, n, ones), load(o_ref), q, k, v, vec)
    normed, scale, weight, mixed = ([x[i] for x in seen] for i in range(4))
    gate = load(gate_ref)
    dgate = each(lambda x, y: x * y, g, mixed)
    dmix = each(lambda x, y: x * y, g, gate)
    dn = each(lambda x, n: x * n[5], dmix, vec)
    do = each(
        lambda x, n, r: r
        * (x - head_sum(x, ones) * (1.0 / CHUNK) - n * (head_sum(x * n, ones) * (1.0 / CHUNK))),
        dn, normed, scale,
    )
    dweight = each(lambda x, y: head_sum(x * y, ones), dmix, v)
    do = [whole(x) for x in do]
    qe, trt, t, aqb, aak, aqk, ys = (
        [(x,) for x in load(ref)]
        for ref in (qe_ref, trt_ref, t_ref, aqb_ref, aak_ref, aqk_ref, y_ref)
    )
    z = load(z_ref)
    vs = [whole(x) for x in v]
    h = each(lambda x, y: tmul(x, y, masks), qe, do)
    dz = [None] * len(units)
    for c in reversed(range(STEP_CHUNKS)):
        for g in range(2):
            i = c * 2 + g
            now = state_ref[g]
            dz[i] = now
            state_ref[g] = mul(trt[i], spread(whole(now), masks)) + h[i]
    dzs = [spread(whole(x), masks) for x in dz]
    zs = [spread(whole(x), masks) for x in z]
    forms = each(scaled_forms, q, w, k, a, b)
    ah, qh, bh, kh, bt, kt = ([f[0][i] for f in forms] for i in range(6))
    ea, eq, eb, ee = ([f[1][i] for f in forms] for i in range(4))
    emid = [f[2][0] for f in forms]
    eend = [f[2][1] for f in forms]
    from_end = each(lambda x, y, s: mul(whole(jnp.concatenate([x, y], axis=0)), s), bt, kt, dzs)
    dy = each(lambda x, y, s: whole(tmul(x, y, masks) + s[:CHUNK]), aqb, do, from_end)
    dr = each(lambda x, y: whole(tmul(x, y, masks)), t, dy)
    ro = each(stack, dr, do)
    dv = each(lambda x, y, s, f: tmul(stack(x, y), s, masks) + f[CHUNK:], aak, aqk, ro, from_end)
    mask2 = jnp.concatenate([strict, within], axis=0)
    dab = each(lambda s, y: whole(mul(s, spread(y, masks), NT) * mask2), ro, ys)
    dak = each(lambda s, y: whole(mul(s, spread(y, masks), NT) * mask2), ro, vs)
    dst = each(lambda s, y: mul(s, y, NT), ro, zs)
    bhs, khs = [whole(x) for x in bh], [whole(x) for x in kh]
    inside = each(
        lambda x, bb, y, kk: mul(x, spread(bb, masks)) + mul(y, spread(kk, masks)), dab, bhs, dak, khs
    )
    outside = each(lambda s, e: s * e, dst, emid)
    daq = each(lambda x, y: x + y, inside, outside)
    aq = each(lambda x, y: whole(jnp.concatenate([x, y], axis=0)), ah, qh)
    dbh = each(lambda x, y: tmul(x, y, masks), dab, aq)
    dkh = each(lambda x, y: tmul(x, y, masks), dak, aq)
    dend = each(lambda y, x, s: mul(stack(y, x), s, NT), ys, vs, dzs)
    row_of_ones = jnp.ones((8, LANES), jnp.bfloat16)
    sums = lambda x: jnp.sum(x, axis=0, keepdims=True)
    for i, u in enumerate(units):
        da = daq[i][:CHUNK] * ea[i]
        dq = daq[i][CHUNK:] * eq[i]
        dbt = dend[i][:CHUNK] * ee[i]
        dkt = dend[i][CHUNK:] * ee[i]
        db = dbh[i] * eb[i] + dbt
        dk = dkh[i] * eb[i] + dkt
        paq = inside[i] * aq[i][0].astype(jnp.float32)
        pa = paq[:CHUNK] + outside[i][:CHUNK] * ah[i]
        diff = pa + paq[CHUNK:] + outside[i][CHUNK:] * qh[i]
        diff = diff - dbh[i] * bhs[i][0].astype(jnp.float32) - dkh[i] * khs[i][0].astype(jnp.float32)
        diff = diff - dbt * b[i] - dkt * k[i]
        zz = spread(halves(z[i] * dz[i]), masks)
        carry = (dot32(row_of_ones, zz[0], NT) + dot32(row_of_ones, zz[1], NT))[:1] * eend[i]
        carry = carry + sums(dbt * b[i] + dkt * k[i])
        dw = running_sum(diff, upper=True) - pa + carry
        from_bonus = dweight[i] * vec[i][4]
        dk = dk + from_bonus * q[i]
        dq_ref[u] = (dq + from_bonus * k[i]).astype(jnp.bfloat16)
        dv_ref[u] = (dv[i] + weight[i] * dmix[i]).astype(jnp.bfloat16)
        dgate_ref[u] = dgate[i].astype(jnp.bfloat16)
        unit_keys = -a[i]
        db = db * live[i]
        du = db * rates[i] - da
        dscaled = inverse[i] * (du - unit_keys * head_sum(du * unit_keys, ones))
        dkl = dk * keys[i] * live[i]
        drl = (db * unit_keys + dkl * vec[i][3]) * rates[i] * (1.0 - rates[i])
        ddl = dw * w[i] * (1.0 - sig[i])
        dkeys_ref[u] = (dk * factor[i] + dscaled * vec[i][2]).astype(jnp.bfloat16)
        ddl_ref[u] = ddl.astype(jnp.bfloat16)
        drl_ref[u] = drl.astype(jnp.bfloat16)
        parts = (
            ddl, drl, dscaled * keys[i], dkl * (rates[i] - 1.0),
            dweight[i] * q[i] * k[i], dmix[i] * normed[i], dmix[i],
        )
        lanes = u[1]
        for j, x in enumerate(parts):
            dvec_ref[j : j + 1, lanes] += sums(x)


def wkv_call(kernel, base, steps, small, arrays, outs, sums, previous, name):
    tokens, width = arrays[0].shape
    rows = CHUNK * STEP_CHUNKS
    last = base + steps - 1
    turned = kernel is backward_kernel
    spec = pl.BlockSpec((rows, width), lambda i: (last - i if turned else base + i, 0))
    state = pl.BlockSpec((2, CHUNK, LANES), lambda i: (0, 0, 0))
    whole = pl.BlockSpec((8, width), lambda i: (0, 0))
    shape = jax.ShapeDtypeStruct
    first = [pl.BlockSpec(memory_space=pltpu.SMEM), whole, state] + [whole] * sums
    held = list(previous or ())
    start = len(first) + len(arrays)
    return pl.pallas_call(
        partial(kernel, base),
        grid=(steps,),
        in_specs=first + [spec] * len(arrays) + [pl.BlockSpec(memory_space=pl.ANY)] * len(held),
        out_specs=[spec] * len(outs) + [whole] * sums + [state],
        out_shape=[shape((tokens, width), dtype) for dtype in outs]
        + [shape((8, width), jnp.float32)] * sums
        + [shape((2, CHUNK, LANES), jnp.float32)],
        input_output_aliases={start + i: i for i in range(len(held))},
        compiler_params=pltpu.CompilerParams(vmem_limit_bytes=60 << 20),
        cost_estimate=SMALL,
        name=name,
    )(*small, *arrays, *held)


def wkv_forward(base, steps, length, vec, state, arrays, previous=None):
    outs = [jnp.bfloat16, jnp.float32] + [jnp.bfloat16] * 5 + [jnp.float32] + [jnp.bfloat16] * 2
    return wkv_call(
        forward_kernel, base, steps, (length, vec, state), arrays, outs, 0, previous, "wkv_forward"
    )


def wkv_backward(base, steps, length, vec, state, sums, arrays, previous=None):
    outs = [jnp.bfloat16] * 6
    return wkv_call(
        backward_kernel, base, steps, (length, vec, state, sums), arrays, outs, 1, previous,
        "wkv_backward",
    )


ROWS = 128


def row_norm(x):
    centred = x - jnp.mean(x, axis=-1, keepdims=True)
    scale = lax.rsqrt(jnp.mean(centred * centred, axis=-1, keepdims=True) + 1e-05)
    return centred * scale, scale


def shifted(x, edge, down):
    rows = x.shape[0]
    row = lax.broadcasted_iota(jnp.int32, x.shape, 0)
    if down:
        return jnp.where(row == 0, edge, pltpu.roll(x, 1, 0))
    return jnp.where(row == rows - 1, edge, pltpu.roll(x, rows - 1, 0))


def below(x, upper):
    lane = lax.broadcasted_iota(jnp.int32, x.shape, 1)
    keep = (lane >= DECAY_RANK) if upper else (lane < DECAY_RANK)
    return jnp.where(keep, x, jnp.zeros_like(x))


def front_kernel(
    x_ref, vec_ref, wr_ref, wk_ref, wv_ref, down_ref, up_ref,
    m0_ref, m1_ref, m2_ref, m3_ref, m4_ref, m5_ref,
    q_ref, k_ref, v_ref, dl_ref, rl_ref, gate_ref, hid_ref,
    edge_ref,
):
    @pl.when(pl.program_id(0) == 0)
    def _():
        edge_ref[...] = jnp.zeros_like(edge_ref)

    unit, _ = row_norm(x_ref[...].astype(jnp.float32))
    normed = unit * vec_ref[12:13] + vec_ref[13:14]
    change = shifted(normed, edge_ref[:1], True) - normed
    edge_ref[:1] = normed[ROWS - 1 :]
    mixes = []
    for j, ref in enumerate((m0_ref, m1_ref, m2_ref, m3_ref, m4_ref, m5_ref)):
        mixes.append((normed + change * vec_ref[j : j + 1]).astype(jnp.bfloat16))
        ref[...] = mixes[j]
    q_ref[...] = dot32(mixes[0], wr_ref[...], NN)
    k_ref[...] = dot32(mixes[2], wk_ref[...], NN)
    v_ref[...] = dot32(mixes[3], wv_ref[...], NN)
    first = down_ref[:, :128]
    pre_decay, pre_rate = dot32(mixes[1], first, NN), dot32(mixes[4], first, NN)
    pre_gate = dot32(mixes[5], down_ref[:, 128:], NN)
    lane = lax.broadcasted_iota(jnp.int32, pre_decay.shape, 1)
    pair = jnp.where(lane < DECAY_RANK, jnp.tanh(pre_decay), pre_rate)
    gate = jax.nn.sigmoid(pre_gate)
    hid_ref[:, :128] = pair
    hid_ref[:, 128:] = gate
    narrow_pair = pair.astype(jnp.bfloat16)
    dl_ref[...] = dot32(below(narrow_pair, False), up_ref[:, :128], NT)
    rl_ref[...] = dot32(below(narrow_pair, True), up_ref[:, :128], NT)
    gate_ref[...] = dot32(gate.astype(jnp.bfloat16), up_ref[:, 128:], NT)


def front_forward(x, vectors, w_r, w_k, w_v, down, up):
    tokens, width = x.shape
    wide = pl.BlockSpec((ROWS, width), lambda i: (i, 0))
    own = pl.BlockSpec((ROWS, OWN), lambda i: (i, 0))
    hid = pl.BlockSpec((ROWS, 256), lambda i: (i, 0))
    whole = lambda a: pl.BlockSpec(a.shape, lambda i: (0, 0))
    shape = jax.ShapeDtypeStruct
    return pl.pallas_call(
        front_kernel,
        grid=(tokens // ROWS,),
        in_specs=[wide] + [whole(a) for a in (vectors, w_r, w_k, w_v, down, up)],
        out_specs=[wide] * 6 + [own] * 6 + [hid],
        out_shape=[shape((tokens, width), jnp.bfloat16)] * 6
        + [shape((tokens, OWN), jnp.float32)] * 6
        + [shape((tokens, 256), jnp.float32)],
        scratch_shapes=[pltpu.VMEM((8, width), jnp.float32)],
        compiler_params=pltpu.CompilerParams(vmem_limit_bytes=60 << 20),
        cost_estimate=SMALL,
        name="front_forward",
    )(x, vectors, w_r, w_k, w_v, down, up)


def front_back_kernel(
    x_ref, before_ref, vec_ref, wr_ref, wk_ref, wv_ref, down_ref, up_ref,
    m1_ref, m4_ref, m5_ref, hid_ref,
    dq_ref, dk_ref, dv_ref, ddl_ref, drl_ref, dgate_ref, own_vec_ref, ffn_vec_ref,
    dx_ref, mine_ref, other_ref,
    edge_ref, sums_ref, misc_ref,
):
    step = pl.num_programs(0) - 1 - pl.program_id(0)
    core = lax.axis_index("dp") % 2
    own_start = pl.multiple_of(core * OWN, OWN)

    @pl.when(pl.program_id(0) == 0)
    def _():
        edge_ref[...] = jnp.zeros_like(edge_ref)
        sums_ref[...] = jnp.zeros_like(sums_ref)
        misc_ref[...] = jnp.zeros_like(misc_ref)

    unit, scale = row_norm(x_ref[...].astype(jnp.float32))
    gain, offset = vec_ref[12:13], vec_ref[13:14]
    normed = unit * gain + offset
    tail, _ = row_norm(before_ref[...].astype(jnp.float32))
    edge = (tail[15:] * gain + offset) * jnp.where(step == 0, 0.0, 1.0)
    change = shifted(normed, edge, True) - normed
    ddl, drl, dgate = ddl_ref[...], drl_ref[...], dgate_ref[...]
    hid = hid_ref[...]
    pair, gate = hid[:, :128], hid[:, 128:]
    lane = lax.broadcasted_iota(jnp.int32, pair.shape, 1)
    first_up, last_up = up_ref[:, :128], up_ref[:, 128:]
    pair_grad = jnp.where(
        lane < DECAY_RANK,
        dot32(ddl, first_up, NN) * (1.0 - pair * pair),
        dot32(drl, first_up, NN),
    ).astype(jnp.bfloat16)
    gate_grad = (dot32(dgate, last_up, NN) * gate * (1.0 - gate)).astype(jnp.bfloat16)
    narrow_pair, narrow_gate = pair.astype(jnp.bfloat16), gate.astype(jnp.bfloat16)
    own_rows = pl.ds(own_start, OWN)
    misc_ref[own_rows, 256:384] += dot32(ddl, below(narrow_pair, False), TN) + dot32(
        drl, below(narrow_pair, True), TN
    )
    misc_ref[own_rows, 384:512] += dot32(dgate, narrow_gate, TN)
    decay_part, rate_part = below(pair_grad, False), below(pair_grad, True)
    misc_ref[:, :128] += dot32(m1_ref[...], decay_part, TN) + dot32(m4_ref[...], rate_part, TN)
    misc_ref[:, 128:256] += dot32(m5_ref[...], gate_grad, TN)
    first_down = down_ref[:, :128]
    grads = (
        lambda: dot32(dq_ref[...], wr_ref[...], NT),
        lambda: dot32(decay_part, first_down, NT),
        lambda: dot32(dk_ref[...], wk_ref[...], NT),
        lambda: dot32(dv_ref[...], wv_ref[...], NT),
        lambda: dot32(rate_part, first_down, NT),
        lambda: dot32(gate_grad, down_ref[:, 128:], NT),
    )
    total = jnp.zeros_like(change)
    moved = jnp.zeros_like(change)
    for j, grad in enumerate(grads):
        now = grad()
        total = total + now
        moved = moved + now * vec_ref[j : j + 1]
        sums_ref[j : j + 1] += jnp.sum(now * change, axis=0, keepdims=True)
    dnormed = total - moved + shifted(moved, edge_ref[:1], False)
    edge_ref[:1] = moved[:1]
    sums_ref[12:13] += jnp.sum(dnormed * unit, axis=0, keepdims=True)
    sums_ref[13:14] += jnp.sum(dnormed, axis=0, keepdims=True)
    dunit = dnormed * gain
    dx_ref[...] = scale * (
        dunit
        - jnp.mean(dunit, axis=-1, keepdims=True)
        - unit * jnp.mean(dunit * unit, axis=-1, keepdims=True)
    )

    @pl.when(step == 0)
    def _():
        sums_ref[6:7] = ffn_vec_ref[0:1] * 0.5
        sums_ref[14:16] = ffn_vec_ref[1:3] * 0.5
        zeros = jnp.zeros((1, OWN), jnp.float32)
        for target, source in ((7, 0), (8, 1), (9, 2), (10, 3), (11, 4), (16, 5), (17, 6)):
            mine = own_vec_ref[source : source + 1]
            sums_ref[target : target + 1] = jnp.concatenate(
                [jnp.where(core == 0, mine, zeros), jnp.where(core == 0, zeros, mine)], axis=1
            )
        for block in range(EMBED // 128):
            lanes = slice(block * 128, (block + 1) * 128)
            misc_ref[lanes, 512:640] = sums_ref[:, lanes].T
        share = mine_ref.shape[1]
        for chip in range(mine_ref.shape[0]):
            low = misc_ref[2 * chip * share : (2 * chip + 1) * share]
            high = misc_ref[(2 * chip + 1) * share : (2 * chip + 2) * share]
            mine_ref[chip] = jnp.where(core == 0, low, high)
            other_ref[chip] = jnp.where(core == 0, high, low).astype(jnp.bfloat16)


def front_backward(
    x, vectors, w_r, w_k, w_v, down, up, mixes, hid, grads, own_vec, ffn_vec
):
    tokens, width = x.shape
    devices = lax.axis_size("dp")
    pieces = (devices // 2, EMBED // devices, 640)
    steps = tokens // ROWS
    wide = pl.BlockSpec((ROWS, width), lambda i: (steps - 1 - i, 0))
    before = pl.BlockSpec(
        (16, width), lambda i: (jnp.maximum((steps - 1 - i) * (ROWS // 16) - 1, 0), 0)
    )
    own = pl.BlockSpec((ROWS, OWN), lambda i: (steps - 1 - i, 0))
    hid_spec = pl.BlockSpec((ROWS, 256), lambda i: (steps - 1 - i, 0))
    whole = lambda a: pl.BlockSpec(a.shape, lambda i: (0, 0))
    shape = jax.ShapeDtypeStruct
    return pl.pallas_call(
        front_back_kernel,
        grid=(steps,),
        in_specs=[wide, before]
        + [whole(a) for a in (vectors, w_r, w_k, w_v, down, up)]
        + [wide] * 3
        + [hid_spec]
        + [own] * 6
        + [whole(own_vec), whole(ffn_vec)],
        out_specs=[wide] + [pl.BlockSpec(pieces, lambda i: (0, 0, 0))] * 2,
        out_shape=[
            shape((tokens, width), jnp.float32),
            shape(pieces, jnp.float32),
            shape(pieces, jnp.bfloat16),
        ],
        scratch_shapes=[
            pltpu.VMEM((8, width), jnp.float32),
            pltpu.VMEM((128, width), jnp.float32),
            pltpu.VMEM((EMBED, 640), jnp.float32),
        ],
        compiler_params=pltpu.CompilerParams(vmem_limit_bytes=60 << 20),
        cost_estimate=SMALL,
        name="front_backward",
    )(x, x, vectors, w_r, w_k, w_v, down, up, *mixes, hid, *grads, own_vec, ffn_vec)


def ffn_back_kernel(
    len_ref, res_ref, before_ref, cot_ref, mine_ref, other_ref, vec_ref, wo_ref,
    grad_ref, narrow_ref, gated_ref, dvec_ref,
    edge_ref,
):
    step = pl.num_programs(0) - 1 - pl.program_id(0)

    @pl.when(pl.program_id(0) == 0)
    def _():
        edge_ref[...] = jnp.zeros_like(edge_ref)
        dvec_ref[...] = jnp.zeros_like(dvec_ref)

    gain, offset, coefficient = vec_ref[14:15], vec_ref[15:16], vec_ref[6:7]
    unit, scale = row_norm(res_ref[...])
    normed = unit * gain + offset
    tail, _ = row_norm(before_ref[...])
    edge = (tail[7:] * gain + offset) * jnp.where(step == 0, 0.0, 1.0)
    change = shifted(normed, edge, True) - normed
    grad = mine_ref[...].astype(jnp.float32) + other_ref[...].astype(jnp.float32)
    moved = grad * coefficient
    dnormed = grad - moved + shifted(moved, edge_ref[:1], False)
    edge_ref[:1] = moved[:1]
    sums = lambda x: jnp.sum(x, axis=0, keepdims=True)
    dvec_ref[0:1] += sums(grad * change)
    dvec_ref[1:2] += sums(dnormed * unit)
    dvec_ref[2:3] += sums(dnormed)
    dunit = dnormed * gain
    row = lax.broadcasted_iota(jnp.int32, grad.shape, 0) + step * ROWS
    out_grad = jnp.where(row < len_ref[0], cot_ref[...].astype(jnp.float32), 0.0)
    total = out_grad + scale * (
        dunit
        - jnp.mean(dunit, axis=-1, keepdims=True)
        - unit * jnp.mean(dunit * unit, axis=-1, keepdims=True)
    )
    grad_ref[...] = total
    small = total.astype(jnp.bfloat16)
    core = lax.axis_index("dp") % 2
    narrow_ref[...] = jnp.where(core == 0, small[:, :OWN], small[:, OWN:])
    gated_ref[...] = dot32(small, wo_ref[...], NT)


def ffn_backward(length, residual, cot, mine, other, vectors, w_o_rows):
    tokens, width = residual.shape
    steps = tokens // ROWS
    wide = pl.BlockSpec((ROWS, width), lambda i: (steps - 1 - i, 0))
    before = pl.BlockSpec(
        (8, width), lambda i: (jnp.maximum((steps - 1 - i) * (ROWS // 8) - 1, 0), 0)
    )
    own = pl.BlockSpec((ROWS, OWN), lambda i: (steps - 1 - i, 0))
    whole = lambda a: pl.BlockSpec(a.shape, lambda i: (0, 0))
    shape = jax.ShapeDtypeStruct
    return pl.pallas_call(
        ffn_back_kernel,
        grid=(steps,),
        in_specs=[pl.BlockSpec(memory_space=pltpu.SMEM), wide, before]
        + [wide] * 3
        + [whole(vectors), whole(w_o_rows)],
        out_specs=[wide, own, own, pl.BlockSpec((8, width), lambda i: (0, 0))],
        out_shape=[
            shape((tokens, width), jnp.float32),
            shape((tokens, OWN), jnp.bfloat16),
            shape((tokens, OWN), jnp.float32),
            shape((8, width), jnp.float32),
        ],
        scratch_shapes=[pltpu.VMEM((8, width), jnp.float32)],
        compiler_params=pltpu.CompilerParams(vmem_limit_bytes=60 << 20),
        cost_estimate=SMALL,
        name="ffn_backward",
    )(length, residual, residual, cot, mine, other, vectors, w_o_rows)


def att_grad_kernel(m0_ref, m2_ref, m3_ref, gated_ref, dq_ref, dk_ref, dv_ref, do_ref,
                    send_a, keep_a, send_b, keep_b):
    chip = lax.axis_index("dp") // 2
    by_x, by_y = chip % 2 == 0, (chip // 2) % 2 == 0
    first = ((m0_ref, dq_ref), (gated_ref, do_ref))
    second = ((m2_ref, dk_ref), (m3_ref, dv_ref))
    for half in range(2):
        lanes = slice(half * OWN, (half + 1) * OWN)
        block = dot32(first[half][0][...], first[half][1][...], TN).astype(jnp.bfloat16)
        for y in range(2):
            low, high = block[y * 128 : y * 128 + 64], block[y * 128 + 64 : y * 128 + 128]
            send_a[y, :, lanes] = jnp.where(by_x, high, low)
            keep_a[y, :, lanes] = jnp.where(by_x, low, high)
        block = dot32(second[half][0][...], second[half][1][...], TN).astype(jnp.bfloat16)
        for x in range(2):
            low, high = block[x * 64 : x * 64 + 64], block[128 + x * 64 : 128 + x * 64 + 64]
            send_b[x, :, lanes] = jnp.where(by_y, high, low)
            keep_b[x, :, lanes] = jnp.where(by_y, low, high)


def att_gradients(mixes, gated, grads, own_grad):
    tokens = gated.shape[0]
    left = pl.BlockSpec((tokens, 256), lambda i: (0, i))
    right = pl.BlockSpec((tokens, OWN), lambda i: (0, 0))
    out = pl.BlockSpec((2, 64, 2 * OWN), lambda i: (i, 0, 0))
    return pl.pallas_call(
        att_grad_kernel,
        grid=(4,),
        in_specs=[left] * 4 + [right] * 4,
        out_specs=[out] * 4,
        out_shape=[jax.ShapeDtypeStruct((8, 64, 2 * OWN), jnp.bfloat16)] * 4,
        compiler_params=pltpu.CompilerParams(vmem_limit_bytes=60 << 20),
        cost_estimate=SMALL,
        name="att_gradients",
    )(*mixes, gated, *grads, own_grad)


def swap(block, mask):
    size = lax.axis_size("dp")
    return lax.ppermute(block, "dp", [(i, i ^ mask) for i in range(size)])


def bit_of(mask):
    return (lax.axis_index("dp") // mask) % 2


def in_order(mask, own, other, axis):
    lower = bit_of(mask) == 0
    return jnp.where(
        lower, jnp.concatenate([own, other], axis=axis), jnp.concatenate([other, own], axis=axis)
    )


def chip_masks():
    size = lax.axis_size("dp")
    masks = []
    while 2 << len(masks) < size:
        masks.append(2 << len(masks))
    return masks


def steps_of(kind):
    masks = chip_masks()
    near, far = [[mask] for mask in masks[:2]], [[mask] for mask in masks[2:][::-1]]
    first = [[far[0][0], far[1][0], far[0][0] | far[1][0]]] if len(far) == 2 else far
    return [first + near[::-1], first + near, far + near[::-1], far + near, near + far][kind]


class Held:
    def __init__(self, value):
        self.value = value


def meet(movers, *arrays):
    held = []
    for mover in movers:
        held += [x[0] for x in mover.arrived if x[0] not in held]
    out = lax.optimization_barrier(tuple(x.value for x in held) + arrays)
    for x, value in zip(held, out):
        x.value = value
    return out[len(held) :]


def read(arrived):
    return [x.value if lanes is None else x.value[..., lanes] for x, lanes in arrived]


class Gather:
    def __init__(self, block, kind, places=(0,)):
        self.steps = steps_of(kind)
        self.held = block[None]
        self.places = [0]
        self.arrived = []
        self.masks = []

    def merge(self):
        if self.arrived:
            self.held = jnp.concatenate([self.held] + read(self.arrived), axis=0)
            self.places = self.places + [p ^ (m // 2) for m in self.masks for p in self.places]
            self.arrived = []

    def step(self):
        if self.steps:
            self.merge()
            self.masks = self.steps.pop(0)
            self.arrived = [(Held(swap(self.held, mask)), None) for mask in self.masks]
        return self

    def run(self):
        while self.steps:
            self.step()
        return self

    def split(self, kinds):
        width = self.held.shape[-1] // len(kinds)
        out = []
        for i, kind in enumerate(kinds):
            part = Gather.__new__(Gather)
            cut = slice(i * width, (i + 1) * width)
            part.steps = steps_of(kind)[len(steps_of(kind)) - len(self.steps) :]
            part.held = self.held[..., cut]
            part.arrived = [(x, cut) for x, _ in self.arrived]
            part.places, part.masks = self.places, self.masks
            out.append(part)
        return out


def place_kernel(places, cuts, *refs):
    sources, outs = refs[: len(places)], refs[len(places) :]
    chip = lax.axis_index("dp") // 2
    for source, (part, list_of) in zip(sources, places):
        for j, place in enumerate(list_of):
            for out, (first, rows, lanes) in zip(outs, cuts):
                start = pl.multiple_of((chip ^ place) * rows, rows)
                lane, width = lanes[part]
                at = sum(w for _, w in lanes[:part])
                out[pl.ds(start, rows), at : at + width] = source[
                    j, first : first + rows, lane : lane + width
                ]


def assemble(gathers, cuts=None):
    gathers = [g.run() for g in gathers]
    rows = gathers[0].held.shape[1]
    cuts = cuts or ((0, rows, [(0, g.held.shape[2]) for g in gathers]),)
    sources, places = [], []
    for i, g in enumerate(gathers):
        sources += [g.held] + read(g.arrived)
        shifts = [0] + [mask // 2 for mask in g.masks]
        places += [(i, [p ^ shift for p in g.places]) for shift in shifts]
    count = lax.axis_size("dp") // 2
    if any(cut[1] % 16 for cut in cuts):
        return assemble_plain(sources, places, cuts, count)
    space = pl.BlockSpec(memory_space=pltpu.VMEM)
    return pl.pallas_call(
        partial(place_kernel, places, cuts),
        in_specs=[space] * len(sources),
        out_specs=[space] * len(cuts),
        out_shape=[
            jax.ShapeDtypeStruct((count * n, sum(w for _, w in lanes)), sources[0].dtype)
            for _, n, lanes in cuts
        ],
        compiler_params=pltpu.CompilerParams(vmem_limit_bytes=32 << 20),
        cost_estimate=SMALL,
        name="assemble",
    )(*sources)


def assemble_plain(sources, places, cuts, count):
    chip = lax.axis_index("dp") // 2
    parts = []
    for part in sorted({part for part, _ in places}):
        blocks = jnp.concatenate([x for x, (at, _) in zip(sources, places) if at == part])
        where = [p for at, list_of in places if at == part for p in list_of]
        blocks = jnp.stack([blocks[where.index(i)] for i in range(count)])
        parts.append(jnp.take(blocks, chip ^ lax.iota(jnp.int32, count), axis=0))
    return [
        jnp.concatenate(
            [x[:, first : first + n, at : at + w] for x, (at, w) in zip(parts, lanes)], axis=-1
        ).reshape(count * n, -1)
        for first, n, lanes in cuts
    ]


class Scatter:
    def __init__(self, parts, kind):
        self.steps = steps_of(kind)[::-1]
        self.axes = chip_masks()[::-1]
        self.sources = [parts.reshape((2,) * len(self.axes) + parts.shape[1:])]
        self.arrived = []
        self.sent = None

    @classmethod
    def begun(cls, sent, kept, kind):
        out = cls.__new__(cls)
        out.steps = steps_of(kind)[::-1]
        out.axes = [axis for axis in chip_masks()[::-1] if axis != out.steps[0][0]]
        out.sources = [kept.reshape((2,) * len(out.axes) + kept.shape[1:])]
        out.arrived = []
        out.sent = [sent.reshape(out.sources[0].shape)]
        return out

    def pick(self, sources, mask, gone):
        out = []
        for x in sources:
            for place in reversed(range(len(self.axes))):
                axis = self.axes[place]
                if axis in gone:
                    which = bit_of(axis) if not mask & axis else 1 - bit_of(axis)
                    x = lax.dynamic_index_in_dim(x, which, place, keepdims=False)
            out.append(x)
        return out

    def prepare(self):
        if self.sent is not None:
            return self
        masks = self.steps[0]
        sources = self.sources + read(self.arrived)
        gone = [axis for axis in self.axes if any(mask & axis for mask in masks)]
        self.sent = [
            sum(x.astype(jnp.float32) for x in self.pick(sources, mask, gone)).astype(jnp.bfloat16)
            for mask in masks
        ]
        self.sources = self.pick(sources, 0, gone)
        self.axes = [axis for axis in self.axes if axis not in gone]
        self.arrived = []
        return self

    def step(self):
        return together([self])[0]

    def run(self):
        while self.steps:
            self.step()
        return self

    def total(self):
        return sum(x.astype(jnp.float32) for x in self.sources + read(self.arrived))


def together(parts):
    if not parts[0].steps:
        return parts
    for part in parts:
        part.prepare()
    for i, mask in enumerate(parts[0].steps[0]):
        sent = [part.sent[i] for part in parts]
        got = Held(swap(sent[0] if len(sent) == 1 else jnp.concatenate(sent, axis=-1), mask))
        at = 0
        for part, x in zip(parts, sent):
            lanes = slice(at, at + x.shape[-1]) if len(sent) > 1 else None
            part.arrived.append((got, lanes))
            at += x.shape[-1]
    for part in parts:
        part.steps.pop(0)
        part.sent_now, part.sent = part.sent[0], None
    return parts


def norm_rows(features, gain_row, offset_row):
    average = jnp.mean(features, axis=-1, keepdims=True)
    centred = features - average
    variance = jnp.mean(centred * centred, axis=-1, keepdims=True)
    return centred * lax.rsqrt(variance + 1e-05) * gain_row + offset_row


def product(operand, weight_matrix):
    return jnp.dot(operand, weight_matrix, preferred_element_type=jnp.float32)


def input_gradient_rows(upstream_gradient, weight_matrix):
    return lax.dot_general(
        upstream_gradient,
        weight_matrix,
        (((1,), (1,)), ((), ())),
        preferred_element_type=jnp.float32,
    )


def weight_gradient(operand, upstream_gradient):
    return lax.dot_general(
        operand, upstream_gradient, (((0,), (0,)), ((), ())), preferred_element_type=jnp.float32
    )


def earlier(rows):
    return jnp.concatenate([jnp.zeros_like(rows[:1]), rows[:-1]], axis=0)


def ffn_mix(residual, vectors):
    second = norm_rows(residual, vectors[14], vectors[15])
    return second + (earlier(second) - second) * vectors[6]


def narrow(x):
    return x.astype(jnp.bfloat16)


def local(
    inputs,
    lengths,
    attention_projections,
    channel_key_weight,
    channel_value_weight,
    lowrank_down_weight,
    lowrank_up_weight,
    per_feature_parameters,
    cotangent,
):
    devices = lax.axis_size("dp")
    chips = devices // 2
    device = lax.axis_index("dp")
    chip, core = device // 2, device % 2
    row_count = inputs.shape[0]
    slots = 2 * row_count
    share = EMBED // devices
    pair_share = 2 * share
    units = channel_value_weight.shape[0]
    half_units = chips * units

    def own_cut(x, which):
        return lax.dynamic_slice_in_dim(x, which * OWN, OWN, x.ndim - 1)

    def own_rows(x, which):
        return lax.dynamic_slice_in_dim(x, which * row_count, row_count, 0)

    pair_rows = in_order(
        1,
        own_cut(attention_projections, core),
        swap(own_cut(attention_projections, 1 - core), 1),
        1,
    )
    lora = jnp.concatenate([lowrank_down_weight, lowrank_up_weight.T], axis=1)
    vector_rows = jnp.pad(per_feature_parameters.T, ((0, 0), (0, 128 - 18)))
    vector_rows = vector_rows.reshape(share // 4, OWN)
    first_rows = 3 * pair_share
    misc_rows = share + share // 4 + (share // 4) % 16
    block = jnp.concatenate(
        [
            pair_rows[:3].reshape(first_rows, OWN),
            lora,
            jnp.pad(vector_rows, ((0, (share // 4) % 16), (0, 0))),
        ],
        axis=0,
    )
    half = half_units // 2
    quarter = OWN // 2
    first = Gather(block, 0).step()
    w_o_part = Gather(pair_rows[3], 4).step().step()
    key_in, raw, cot, _ = meet([], channel_key_weight, inputs, cotangent, first.held)
    key_cut = key_in.reshape(share, chips, 2, units)

    def key_columns(which):
        return lax.dynamic_index_in_dim(key_cut, which, 2, keepdims=False).reshape(share, half_units)

    key_rows = in_order(1, key_columns(core), swap(key_columns(1 - core), 1), 0)
    tokens = in_order(1, raw, swap(raw, 1), 0)
    cot = in_order(1, cot, swap(cot, 1), 0)
    key_rows, tokens, cot = meet([first, w_o_part], key_rows, tokens, cot)
    first = first.split((0, 1))
    for part in first:
        part.step()
    key_part = Gather(key_rows, 2).step()
    (tokens,) = meet(first, tokens)
    for part in first:
        part.step()
    value_block, *_ = meet([key_part], channel_value_weight, *[part.held for part in first])
    key_part.step()
    value_part = Gather(value_block, 2).step()
    w_o_part.step()
    (tokens,) = meet(first + [key_part, value_part], tokens)
    key_parts = key_part.split((2, 3))
    for part in key_parts:
        part.step()
    w_r, w_k, w_v, misc = assemble(
        first,
        [(i * pair_share, pair_share, [(0, quarter)] * 2) for i in range(3)]
        + [(first_rows, misc_rows, [(0, quarter)] * 2)],
    )
    misc = misc.reshape(chips, 1, misc_rows, OWN)
    misc = in_order(1, misc, swap(misc, 1), 1)
    value_part.step()
    lora = misc[:, :, :share].reshape(EMBED, OWN)
    down, up_t = lora[:, :256], lax.dynamic_slice_in_dim(lora[:, 256:], core * OWN, OWN, 0)
    vectors = misc[:, :, share : share + share // 4].reshape(EMBED, 128)[:, :18].T
    vectors = vectors.astype(jnp.float32)
    own_vectors = own_cut(vectors, core)
    used = jnp.concatenate([own_vectors[7:12], own_vectors[16:18], own_vectors[:1]], axis=0)
    length = lax.dynamic_index_in_dim(lengths, chip, 0)
    live = (lax.iota(jnp.int32, slots) < length)[:, None]

    *mixes, queries, keys, values, decay_low, rate_low, gate_rows, hid = front_forward(
        tokens, vectors, w_r, w_k, w_v, down, up_t
    )
    terms = meet(
        key_parts + [value_part, w_o_part],
        queries, keys, values, decay_low, rate_low, gate_rows,
    )
    value_parts = value_part.split((2, 3))
    for part in key_parts + value_parts:
        part.step()
    w_o_part.step()
    blocks = slots // (CHUNK * STEP_CHUNKS)
    zero_state = jnp.zeros((2, CHUNK, LANES), jnp.float32)
    gated, *saved, _ = wkv_forward(0, blocks, length, used, zero_state, terms)
    gated, cot, tokens = meet(key_parts + value_parts, gated, cot, tokens)
    for part in value_parts:
        part.step()
    gated, *_ = meet([w_o_part] + key_parts, gated, *[part.held for part in value_parts])
    gated_all = in_order(1, gated, swap(gated, 1), 1)
    (w_o_own,) = assemble([w_o_part])
    w_o = in_order(1, w_o_own, swap(w_o_own, 1), 1)
    (key_weight,) = assemble(key_parts)
    residual = tokens.astype(jnp.float32) + product(gated_all, w_o)
    ffn_in = narrow(ffn_mix(residual, vectors))
    positive = jax.nn.relu(product(ffn_in, key_weight))
    hidden = narrow(jnp.square(positive))
    out_narrow = jnp.where(live, cot, jnp.zeros_like(cot))
    grad_value = narrow(weight_gradient(hidden, out_narrow)).reshape(chips, units, EMBED)
    w_o_rows = lax.dynamic_slice_in_dim(w_o, core * OWN, OWN, 0)
    value_scatter = [
        Scatter(grad_value[..., i * OWN : (i + 1) * OWN], 2 + i).prepare() for i in range(2)
    ]
    hidden, positive, out_narrow, w_o_rows, *sent = meet(
        value_parts, hidden, positive, out_narrow, w_o_rows, *[m.sent[0] for m in value_scatter]
    )
    for part, x in zip(value_scatter, sent):
        part.sent = [x]
        part.step()
    (value_weight,) = assemble(value_parts)

    pre_narrow = narrow(2.0 * positive * input_gradient_rows(out_narrow, value_weight))
    ffn_in_grad = narrow(input_gradient_rows(pre_narrow, key_weight))
    other_grad = swap(ffn_in_grad, 1)
    grad_key = narrow(weight_gradient(ffn_in, pre_narrow)).reshape(chips, pair_share, half_units)
    residual_grad, own_grad, gated_grad, ffn_vec = ffn_backward(
        length, residual, cot, ffn_in_grad, other_grad, vectors, w_o_rows
    )
    key_scatter = [
        Scatter(grad_key[:, :, i * half : (i + 1) * half], 2 + i).prepare() for i in range(2)
    ]
    gated_grad, *sent = meet([], gated_grad, *[m.sent[0] for m in key_scatter])
    for part, x in zip(key_scatter, sent):
        part.sent = [x]
        part.step()
    terms = [*terms, gated_grad, *saved]
    zero_sums = jnp.zeros((8, OWN), jnp.float32)
    early = blocks // 2
    *before, sums, state = wkv_backward(
        early, blocks - early, length, used, zero_state, zero_sums, terms
    )
    state, sums = meet(value_scatter, state, sums)
    for part in value_scatter:
        part.step()
    *low_grads, own_vec, _ = wkv_backward(0, early, length, used, state, sums, terms, before)
    if pair_share == 64:
        sent_a, kept_a, sent_b, kept_b = att_gradients(
            (mixes[0], mixes[2], mixes[3]), gated_all, low_grads[:3], own_grad
        )
        att_scatter = [Scatter.begun(sent_a, kept_a, 2), Scatter.begun(sent_b, kept_b, 3)]
    else:
        grads = [weight_gradient(mixes[m], g) for m, g in zip((0, 2, 3), low_grads)]
        grad_o = weight_gradient(gated_all, own_grad)
        att_scatter = [
            Scatter(
                narrow(jnp.concatenate(x, axis=1)).reshape(chips, pair_share, EMBED), 2 + i
            ).prepare()
            for i, x in enumerate(((grads[0], grad_o), (grads[1], grads[2])))
        ]
    own_vec, *sent = meet(
        key_scatter + value_scatter, own_vec, *[m.sent[0] for m in att_scatter]
    )
    for part, x in zip(att_scatter, sent):
        part.sent = [x]
        part.step()
    for part in key_scatter:
        part.step()
    together(value_scatter)
    own_vec, *_ = meet([], own_vec, *[m.sent_now for m in key_scatter])
    token_part, misc_mine, misc_other = front_backward(
        tokens, vectors, w_r, w_k, w_v, down, up_t, (mixes[1], mixes[4], mixes[5]), hid,
        low_grads, own_vec, ffn_vec,
    )
    misc_other = swap(misc_other, 1)
    token_part, misc_mine, misc_other = meet(
        att_scatter + value_scatter, token_part, misc_mine, misc_other
    )
    for part in att_scatter:
        part.step()
    misc_sum = misc_mine + misc_other.astype(jnp.float32)
    misc_sum = jnp.concatenate([misc_sum[..., :320], misc_sum[..., 320:]], axis=1)
    misc_scatter = Scatter(misc_sum, 3).step()
    token_part, hidden = meet(key_scatter + [misc_scatter], token_part, hidden)
    misc_scatter.step()
    together(key_scatter)
    together(value_scatter)
    (token_part,) = meet(att_scatter + [misc_scatter], token_part)
    masks = chip_masks()
    last_parts = att_scatter + [misc_scatter]
    if len(misc_scatter.steps) == 2:
        for part in last_parts:
            part.steps = [[masks[2], masks[3], masks[2] | masks[3]]]
    together(last_parts)
    token_part, hidden, *_ = meet(
        key_scatter + value_scatter, token_part, hidden, *[m.sent_now for m in last_parts]
    )
    together(key_scatter)
    ffn_part = product(hidden, value_weight)
    input_gradient = (
        own_rows(residual_grad, core)
        + own_rows(token_part, core)
        + swap(own_rows(token_part, 1 - core), 1)
    )
    ffn_out = own_rows(ffn_part, core) + swap(own_rows(ffn_part, 1 - core), 1)
    output = narrow(jnp.where(own_rows(live, core), own_rows(residual, core) + ffn_out, 0.0))
    value_sum = jnp.concatenate(
        [x.run().total() for x in value_scatter], axis=1
    )
    while key_scatter[0].steps:
        together(key_scatter)
    key_sum = jnp.concatenate([x.total() for x in key_scatter], axis=1).reshape(2, share, -1)

    def exchange(x):
        mine = lax.dynamic_index_in_dim(x, core, 0, keepdims=False)
        return mine, swap(lax.dynamic_index_in_dim(x, 1 - core, 0, keepdims=False), 1)

    key_mine, key_theirs = exchange(key_sum)
    input_gradient, value_sum, key_mine, key_theirs = meet(
        last_parts, input_gradient, value_sum, key_mine, key_theirs
    )
    while last_parts[0].steps:
        together(last_parts)
    first_sum, second_sum, misc_sum = [x.total() for x in last_parts]
    misc_sum = jnp.concatenate([misc_sum[:share], misc_sum[share:]], axis=1)
    att_sum = jnp.concatenate(
        [first_sum[:, :OWN], second_sum, first_sum[:, OWN:]], axis=1
    )
    mine, theirs = exchange(att_sum.reshape(2, share, -1))
    shard_mixer = jnp.stack(
        [
            in_order(1, mine[:, i * OWN : (i + 1) * OWN], theirs[:, i * OWN : (i + 1) * OWN], 1)
            for i in range(4)
        ]
    )
    shard_key = in_order(
        1,
        key_mine.reshape(share, chips, 1, units),
        key_theirs.reshape(share, chips, 1, units),
        2,
    ).reshape(share, 2 * half_units)
    return (
        output,
        input_gradient,
        shard_mixer,
        shard_key,
        value_sum,
        misc_sum[:, :256],
        misc_sum[:, 256:512].T,
        misc_sum[:, 512:530].T,
    )


def solution(mesh):
    in_specs = (
        P("dp", None),
        P(),
        P(None, "dp", None),
        P("dp", None),
        P("dp", None),
        P("dp", None),
        P(None, "dp"),
        P(None, "dp"),
        P("dp", None),
    )
    out_specs = (
        P("dp", None),
        P("dp", None),
        P(None, "dp", None),
        P("dp", None),
        P("dp", None),
        P("dp", None),
        P(None, "dp"),
        P(None, "dp"),
    )
    return jax.shard_map(local, mesh=mesh, in_specs=in_specs, out_specs=out_specs, check_vma=False)
```

```python
from functools import partial

import jax
import jax.numpy as jnp
from jax import lax
from jax.experimental import pallas as pl
from jax.experimental.pallas import tpu as pltpu
from jax.sharding import PartitionSpec as P

HEADS = 16
HEAD_SIZE = 64
DECAY_RANK = 64
RATE_RANK = 64
EMBED = 1024
OWN = EMBED // 2
PRECISE = lax.Precision.HIGHEST


CHUNK = 64
LANES = 256
GROUP_HEADS = 4
STEP_CHUNKS = 2
SMALL = pl.CostEstimate(flops=1, bytes_accessed=1, transcendentals=0)

NN = (((1,), (0,)), ((), ()))
NT = (((1,), (1,)), ((), ()))
TN = (((0,), (0,)), ((), ()))


def halves(x):
    high = x.astype(jnp.bfloat16)
    return high, (x - high.astype(jnp.float32)).astype(jnp.bfloat16)


def whole(x):
    return (x.astype(jnp.bfloat16),)


def dot32(a, b, dims):
    return lax.dot_general(a, b, dims, preferred_element_type=jnp.float32)


def mul(left, right, dims=NN):
    if len(left) == 1 or len(right) == 1:
        return dot32(left[0], right[0], dims)
    rows = left[0].shape[0]
    both = dot32(jnp.concatenate(left, axis=0), right[0], dims)
    return both[:rows] + both[rows:] + dot32(left[0], right[1], dims)


def tmul(left, right, masks):
    full = dot32(left[0], right[0], TN)
    if len(left) > 1 and len(right) > 1:
        full = full + dot32(left[1], right[0], TN) + dot32(left[0], right[1], TN)
    return sum(full[h * CHUNK : (h + 1) * CHUNK] * masks[h][:1].astype(jnp.float32) for h in range(GROUP_HEADS))


def spread(pair, masks):
    return tuple(
        jnp.concatenate([part * masks[h] for h in range(GROUP_HEADS)], axis=0) for part in pair
    )


def stack(first, second):
    return tuple(jnp.concatenate([x, y], axis=0) for x, y in zip(first, second))


def head_masks():
    lane = lax.broadcasted_iota(jnp.int32, (CHUNK, LANES), 1) // CHUNK
    return [(lane == h).astype(jnp.float32).astype(jnp.bfloat16) for h in range(GROUP_HEADS)]


def places():
    row = lax.broadcasted_iota(jnp.int32, (CHUNK, LANES), 0)
    col = lax.broadcasted_iota(jnp.int32, (CHUNK, LANES), 1) % CHUNK
    return row, col


def running_sum(x, upper=False):
    row = lax.broadcasted_iota(jnp.int32, (CHUNK, CHUNK), 0)
    col = lax.broadcasted_iota(jnp.int32, (CHUNK, CHUNK), 1)
    ones = (row <= col if upper else col <= row).astype(jnp.float32).astype(jnp.bfloat16)
    high, rest = halves(x)
    low = (x - high.astype(jnp.float32) - rest.astype(jnp.float32)).astype(jnp.bfloat16)
    return dot32(ones, high, NN) + dot32(ones, rest, NN) + dot32(ones, low, NN)


def scaled_forms(q, w, k, a, b):
    total = running_sum(w)
    before = total - w
    middle = total[CHUNK // 2 - 1 : CHUNK // 2]
    end = total[CHUNK - 1 :]
    ea = jnp.exp(before - middle)
    eq = jnp.exp(total - middle)
    eb = jnp.exp(middle - total)
    ee = jnp.exp(end - total)
    return (a * ea, q * eq, b * eb, k * eb, b * ee, k * ee), (ea, eq, eb, ee), (jnp.exp(middle), jnp.exp(end))


def each(fn, *columns):
    return [fn(*row) for row in zip(*columns)]


def block_ones():
    row = lax.broadcasted_iota(jnp.int32, (LANES, LANES), 0) // CHUNK
    col = lax.broadcasted_iota(jnp.int32, (LANES, LANES), 1) // CHUNK
    return (row == col).astype(jnp.float32).astype(jnp.bfloat16)


def head_sum(x, ones):
    rows = x.shape[0]
    both = dot32(jnp.concatenate(halves(x), axis=0), ones, NN)
    return both[:rows] + both[rows:]


def prepared(keys, decay_low, rate_low, live, vec, ones):
    sig = jax.nn.sigmoid(vec[0] + decay_low)
    log_decay = (-0.6065306597126334) * sig * live
    rates = jax.nn.sigmoid(vec[1] + rate_low)
    scaled = keys * vec[2]
    inverse = lax.rsqrt(head_sum(scaled * scaled, ones) + 1e-06)
    unit_keys = scaled * inverse
    factor = (1.0 + (rates - 1.0) * vec[3]) * live
    return log_decay, keys * factor, -unit_keys, unit_keys * rates * live, sig, rates, inverse, factor


def read_out(o, q, k, v, vec, ones):
    centred = o - head_sum(o, ones) * (1.0 / CHUNK)
    scale = lax.rsqrt(head_sum(centred * centred, ones) * (1.0 / CHUNK) + 0.00064)
    normed = centred * scale
    weight = head_sum(q * k * vec[4], ones)
    return normed, scale, weight, normed * vec[5] + vec[6] + weight * v


def unit_slices():
    return [
        (slice(c * CHUNK, (c + 1) * CHUNK), slice(g * LANES, (g + 1) * LANES))
        for c in range(STEP_CHUNKS)
        for g in range(2)
    ]


def unit_live(length, step):
    row = lax.broadcasted_iota(jnp.int32, (CHUNK, LANES), 0)
    start = step * (STEP_CHUNKS * CHUNK)
    live = [(row + (start + c * CHUNK) < length).astype(jnp.float32) for c in range(STEP_CHUNKS)]
    return [live[c] for c in range(STEP_CHUNKS) for g in range(2)]


def unit_vectors(vec_ref):
    vec = [[vec_ref[i : i + 1, g * LANES : (g + 1) * LANES] for i in range(7)] for g in range(2)]
    return [vec[g] for c in range(STEP_CHUNKS) for g in range(2)]


def forward_kernel(base, *refs):
    len_ref, vec_ref, start_ref, q_ref, keys_ref, v_ref, dl_ref, rl_ref, gate_ref = refs[:9]
    (
        out_ref, o_ref, t_ref, aqb_ref, aak_ref, aqk_ref, y_ref, z_ref, trt_ref, qe_ref, state_ref,
    ) = refs[-11:]

    @pl.when(pl.program_id(0) == 0)
    def _():
        state_ref[...] = start_ref[...]

    masks = head_masks()
    row, col = places()
    strict = (col < row).astype(jnp.float32)
    within = (col <= row).astype(jnp.float32)
    eye = (col == row).astype(jnp.float32)
    ones = block_ones()
    units = unit_slices()
    live = unit_live(len_ref[0], pl.program_id(0) + base)
    vec = unit_vectors(vec_ref)
    load = lambda ref: [ref[u] for u in units]
    q, keys, v = load(q_ref), load(keys_ref), load(v_ref)
    ready = each(
        lambda x, y, z, m, n: prepared(x, y, z, m, n, ones), keys, load(dl_ref), load(rl_ref), live, vec
    )
    w, k, a, b = ([x[i] for x in ready] for i in range(4))
    forms = each(scaled_forms, q, w, k, a, b)
    ah, qh, bh, kh, bt, kt = ([f[0][i] for f in forms] for i in range(6))
    emid = [f[2][0] for f in forms]
    eend = [f[2][1] for f in forms]
    aq = each(lambda x, y: halves(jnp.concatenate([x, y], axis=0)), ah, qh)
    with_b = each(lambda l, r: mul(l, spread(halves(r), masks), NT), aq, bh)
    with_k = each(lambda l, r: mul(l, spread(halves(r), masks), NT), aq, kh)
    aab = [x[:CHUNK] * strict for x in with_b]
    aqb = [halves(x[CHUNK:] * within) for x in with_b]
    aak = [halves(x[:CHUNK] * strict) for x in with_k]
    aqk = [halves(x[CHUNK:] * within) for x in with_k]
    p = [halves(x * (row // 8 == col // 8)) for x in aab]
    t = [eye + x * (row // 8 == col // 8) for x in aab]
    p2 = each(lambda x: halves(mul(x, spread(x, masks))), p)
    both = each(lambda x, y: mul(stack(x, halves(y)), spread(x, masks)), p2, t)
    p4 = [halves(x[:CHUNK]) for x in both]
    t = each(lambda x, y: x + y[CHUNK:], t, both)
    t = each(lambda x, y: x + mul(halves(x), spread(y, masks)), t, p4)
    for size in (8, 16, 32):
        corner = ((row // size) % 2 == 1) & (col // size == row // size - 1)
        ts = [halves(x) for x in t]
        n = [halves(x * corner) for x in aab]
        tn = each(lambda x, y: halves(mul(x, spread(y, masks))), ts, n)
        t = each(lambda x, y, z: x + mul(y, spread(z, masks)), t, tn, ts)
    ts = [halves(x) for x in t]
    vs = [halves(x) for x in v]
    vm = [spread(x, masks) for x in vs]
    wide = each(lambda x, y, e: mul(x, spread(halves(y * e), masks)), ts, ah, emid)
    r0 = each(mul, aak, vm)
    y0 = each(lambda x, y: mul(x, spread(halves(y), masks)), ts, r0)
    wides = [halves(x) for x in wide]
    qe = each(lambda x, e, y, z: x * e + mul(y, spread(z, masks)), qh, emid, aqb, wides)
    y0s = [halves(x) for x in y0]
    part = each(lambda x, y, z, u: mul(x, spread(y, masks)) + mul(z, u), aqb, y0s, aqk, vm)
    bts = [halves(x) for x in bt]
    diag = [eye * e for e in eend]
    tr = each(lambda x, y, d: tmul(x, y, masks) + d, bts, wides, diag)
    trt = each(lambda x, y, d: tmul(y, x, masks) + d, bts, wides, diag)
    inject = each(lambda x, y, z, u: tmul(stack(x, halves(y)), stack(z, u), masks), bts, kt, y0s, vs)
    wq = each(lambda x, y: stack(x, halves(y)), wides, qe)
    z = []
    out = []
    for c in range(STEP_CHUNKS):
        for g in range(2):
            i = c * 2 + g
            now = state_ref[g]
            nows = spread(halves(now), masks)
            state_ref[g] = mul(halves(tr[i]), nows) + inject[i]
            z.append(now)
            out.append(mul(wq[i], nows))
    o = each(lambda x, y: x[CHUNK:] + y, out, part)
    mixed = each(lambda x, y, z, m, n: read_out(x, y, z, m, n, ones)[3], o, q, k, v, vec)
    for i, u in enumerate(units):
        out_ref[u] = (mixed[i] * gate_ref[u]).astype(jnp.bfloat16)
        o_ref[u] = o[i]
        y_ref[u] = (out[i][:CHUNK] + y0[i]).astype(jnp.bfloat16)
        t_ref[u] = ts[i][0]
        aqb_ref[u] = aqb[i][0]
        aak_ref[u] = aak[i][0]
        aqk_ref[u] = aqk[i][0]
        z_ref[u] = z[i]
        trt_ref[u] = trt[i].astype(jnp.bfloat16)
        qe_ref[u] = qe[i].astype(jnp.bfloat16)


def backward_kernel(base, *refs):
    (
        len_ref, vec_ref, start_ref, sums_ref, q_ref, keys_ref, v_ref, dl_ref, rl_ref, gate_ref,
        g_ref, o_ref, t_ref, aqb_ref, aak_ref, aqk_ref, y_ref, z_ref, trt_ref, qe_ref,
    ) = refs[:20]
    dq_ref, dkeys_ref, dv_ref, ddl_ref, drl_ref, dgate_ref, dvec_ref, state_ref = refs[-8:]
    step = base + pl.num_programs(0) - 1 - pl.program_id(0)

    @pl.when(pl.program_id(0) == 0)
    def _():
        state_ref[...] = start_ref[...]
        dvec_ref[...] = sums_ref[...]

    masks = head_masks()
    row, col = places()
    strict = (col < row).astype(jnp.float32)
    within = (col <= row).astype(jnp.float32)
    ones = block_ones()
    units = unit_slices()
    live = unit_live(len_ref[0], step)
    vec = unit_vectors(vec_ref)
    load = lambda ref: [ref[u] for u in units]
    q, keys, v, g = load(q_ref), load(keys_ref), load(v_ref), load(g_ref)
    ready = each(
        lambda x, y, z, m, n: prepared(x, y, z, m, n, ones), keys, load(dl_ref), load(rl_ref), live, vec
    )
    w, k, a, b, sig, rates, inverse, factor = ([x[i] for x in ready] for i in range(8))
    seen = each(lambda x, y, z, m, n: read_out(x, y, z, m, n, ones), load(o_ref), q, k, v, vec)
    normed, scale, weight, mixed = ([x[i] for x in seen] for i in range(4))
    gate = load(gate_ref)
    dgate = each(lambda x, y: x * y, g, mixed)
    dmix = each(lambda x, y: x * y, g, gate)
    dn = each(lambda x, n: x * n[5], dmix, vec)
    do = each(
        lambda x, n, r: r
        * (x - head_sum(x, ones) * (1.0 / CHUNK) - n * (head_sum(x * n, ones) * (1.0 / CHUNK))),
        dn, normed, scale,
    )
    dweight = each(lambda x, y: head_sum(x * y, ones), dmix, v)
    do = [whole(x) for x in do]
    qe, trt, t, aqb, aak, aqk, ys = (
        [(x,) for x in load(ref)]
        for ref in (qe_ref, trt_ref, t_ref, aqb_ref, aak_ref, aqk_ref, y_ref)
    )
    z = load(z_ref)
    vs = [whole(x) for x in v]
    h = each(lambda x, y: tmul(x, y, masks), qe, do)
    dz = [None] * len(units)
    for c in reversed(range(STEP_CHUNKS)):
        for g in range(2):
            i = c * 2 + g
            now = state_ref[g]
            dz[i] = now
            state_ref[g] = mul(trt[i], spread(whole(now), masks)) + h[i]
    dzs = [spread(whole(x), masks) for x in dz]
    zs = [spread(whole(x), masks) for x in z]
    forms = each(scaled_forms, q, w, k, a, b)
    ah, qh, bh, kh, bt, kt = ([f[0][i] for f in forms] for i in range(6))
    ea, eq, eb, ee = ([f[1][i] for f in forms] for i in range(4))
    emid = [f[2][0] for f in forms]
    eend = [f[2][1] for f in forms]
    from_end = each(lambda x, y, s: mul(whole(jnp.concatenate([x, y], axis=0)), s), bt, kt, dzs)
    dy = each(lambda x, y, s: whole(tmul(x, y, masks) + s[:CHUNK]), aqb, do, from_end)
    dr = each(lambda x, y: whole(tmul(x, y, masks)), t, dy)
    ro = each(stack, dr, do)
    dv = each(lambda x, y, s, f: tmul(stack(x, y), s, masks) + f[CHUNK:], aak, aqk, ro, from_end)
    mask2 = jnp.concatenate([strict, within], axis=0)
    dab = each(lambda s, y: whole(mul(s, spread(y, masks), NT) * mask2), ro, ys)
    dak = each(lambda s, y: whole(mul(s, spread(y, masks), NT) * mask2), ro, vs)
    dst = each(lambda s, y: mul(s, y, NT), ro, zs)
    bhs, khs = [whole(x) for x in bh], [whole(x) for x in kh]
    inside = each(
        lambda x, bb, y, kk: mul(x, spread(bb, masks)) + mul(y, spread(kk, masks)), dab, bhs, dak, khs
    )
    outside = each(lambda s, e: s * e, dst, emid)
    daq = each(lambda x, y: x + y, inside, outside)
    aq = each(lambda x, y: whole(jnp.concatenate([x, y], axis=0)), ah, qh)
    dbh = each(lambda x, y: tmul(x, y, masks), dab, aq)
    dkh = each(lambda x, y: tmul(x, y, masks), dak, aq)
    dend = each(lambda y, x, s: mul(stack(y, x), s, NT), ys, vs, dzs)
    row_of_ones = jnp.ones((8, LANES), jnp.bfloat16)
    sums = lambda x: jnp.sum(x, axis=0, keepdims=True)
    for i, u in enumerate(units):
        da = daq[i][:CHUNK] * ea[i]
        dq = daq[i][CHUNK:] * eq[i]
        dbt = dend[i][:CHUNK] * ee[i]
        dkt = dend[i][CHUNK:] * ee[i]
        db = dbh[i] * eb[i] + dbt
        dk = dkh[i] * eb[i] + dkt
        paq = inside[i] * aq[i][0].astype(jnp.float32)
        pa = paq[:CHUNK] + outside[i][:CHUNK] * ah[i]
        diff = pa + paq[CHUNK:] + outside[i][CHUNK:] * qh[i]
        diff = diff - dbh[i] * bhs[i][0].astype(jnp.float32) - dkh[i] * khs[i][0].astype(jnp.float32)
        diff = diff - dbt * b[i] - dkt * k[i]
        zz = spread(halves(z[i] * dz[i]), masks)
        carry = (dot32(row_of_ones, zz[0], NT) + dot32(row_of_ones, zz[1], NT))[:1] * eend[i]
        carry = carry + sums(dbt * b[i] + dkt * k[i])
        dw = running_sum(diff, upper=True) - pa + carry
        from_bonus = dweight[i] * vec[i][4]
        dk = dk + from_bonus * q[i]
        dq_ref[u] = (dq + from_bonus * k[i]).astype(jnp.bfloat16)
        dv_ref[u] = (dv[i] + weight[i] * dmix[i]).astype(jnp.bfloat16)
        dgate_ref[u] = dgate[i].astype(jnp.bfloat16)
        unit_keys = -a[i]
        db = db * live[i]
        du = db * rates[i] - da
        dscaled = inverse[i] * (du - unit_keys * head_sum(du * unit_keys, ones))
        dkl = dk * keys[i] * live[i]
        drl = (db * unit_keys + dkl * vec[i][3]) * rates[i] * (1.0 - rates[i])
        ddl = dw * w[i] * (1.0 - sig[i])
        dkeys_ref[u] = (dk * factor[i] + dscaled * vec[i][2]).astype(jnp.bfloat16)
        ddl_ref[u] = ddl.astype(jnp.bfloat16)
        drl_ref[u] = drl.astype(jnp.bfloat16)
        parts = (
            ddl, drl, dscaled * keys[i], dkl * (rates[i] - 1.0),
            dweight[i] * q[i] * k[i], dmix[i] * normed[i], dmix[i],
        )
        lanes = u[1]
        for j, x in enumerate(parts):
            dvec_ref[j : j + 1, lanes] += sums(x)


def wkv_call(kernel, base, steps, small, arrays, outs, sums, previous, name):
    tokens, width = arrays[0].shape
    rows = CHUNK * STEP_CHUNKS
    last = base + steps - 1
    turned = kernel is backward_kernel
    spec = pl.BlockSpec((rows, width), lambda i: (last - i if turned else base + i, 0))
    state = pl.BlockSpec((2, CHUNK, LANES), lambda i: (0, 0, 0))
    whole = pl.BlockSpec((8, width), lambda i: (0, 0))
    shape = jax.ShapeDtypeStruct
    first = [pl.BlockSpec(memory_space=pltpu.SMEM), whole, state] + [whole] * sums
    held = list(previous or ())
    start = len(first) + len(arrays)
    return pl.pallas_call(
        partial(kernel, base),
        grid=(steps,),
        in_specs=first + [spec] * len(arrays) + [pl.BlockSpec(memory_space=pl.ANY)] * len(held),
        out_specs=[spec] * len(outs) + [whole] * sums + [state],
        out_shape=[shape((tokens, width), dtype) for dtype in outs]
        + [shape((8, width), jnp.float32)] * sums
        + [shape((2, CHUNK, LANES), jnp.float32)],
        input_output_aliases={start + i: i for i in range(len(held))},
        compiler_params=pltpu.CompilerParams(vmem_limit_bytes=60 << 20),
        cost_estimate=SMALL,
        name=name,
    )(*small, *arrays, *held)


def wkv_forward(base, steps, length, vec, state, arrays, previous=None):
    outs = [jnp.bfloat16, jnp.float32] + [jnp.bfloat16] * 5 + [jnp.float32] + [jnp.bfloat16] * 2
    return wkv_call(
        forward_kernel, base, steps, (length, vec, state), arrays, outs, 0, previous, "wkv_forward"
    )


def wkv_backward(base, steps, length, vec, state, sums, arrays, previous=None):
    outs = [jnp.bfloat16] * 6
    return wkv_call(
        backward_kernel, base, steps, (length, vec, state, sums), arrays, outs, 1, previous,
        "wkv_backward",
    )


ROWS = 128


def row_norm(x):
    centred = x - jnp.mean(x, axis=-1, keepdims=True)
    scale = lax.rsqrt(jnp.mean(centred * centred, axis=-1, keepdims=True) + 1e-05)
    return centred * scale, scale


def shifted(x, edge, down):
    rows = x.shape[0]
    row = lax.broadcasted_iota(jnp.int32, x.shape, 0)
    if down:
        return jnp.where(row == 0, edge, pltpu.roll(x, 1, 0))
    return jnp.where(row == rows - 1, edge, pltpu.roll(x, rows - 1, 0))


def below(x, upper):
    lane = lax.broadcasted_iota(jnp.int32, x.shape, 1)
    keep = (lane >= DECAY_RANK) if upper else (lane < DECAY_RANK)
    return jnp.where(keep, x, jnp.zeros_like(x))


def front_kernel(
    x_ref, vec_ref, wr_ref, wk_ref, wv_ref, down_ref, up_ref,
    m0_ref, m1_ref, m2_ref, m3_ref, m4_ref, m5_ref,
    q_ref, k_ref, v_ref, dl_ref, rl_ref, gate_ref, hid_ref,
    edge_ref,
):
    @pl.when(pl.program_id(0) == 0)
    def _():
        edge_ref[...] = jnp.zeros_like(edge_ref)

    unit, _ = row_norm(x_ref[...].astype(jnp.float32))
    normed = unit * vec_ref[12:13] + vec_ref[13:14]
    change = shifted(normed, edge_ref[:1], True) - normed
    edge_ref[:1] = normed[ROWS - 1 :]
    mixes = []
    for j, ref in enumerate((m0_ref, m1_ref, m2_ref, m3_ref, m4_ref, m5_ref)):
        mixes.append((normed + change * vec_ref[j : j + 1]).astype(jnp.bfloat16))
        ref[...] = mixes[j]
    q_ref[...] = dot32(mixes[0], wr_ref[...], NN)
    k_ref[...] = dot32(mixes[2], wk_ref[...], NN)
    v_ref[...] = dot32(mixes[3], wv_ref[...], NN)
    first = down_ref[:, :128]
    pre_decay, pre_rate = dot32(mixes[1], first, NN), dot32(mixes[4], first, NN)
    pre_gate = dot32(mixes[5], down_ref[:, 128:], NN)
    lane = lax.broadcasted_iota(jnp.int32, pre_decay.shape, 1)
    pair = jnp.where(lane < DECAY_RANK, jnp.tanh(pre_decay), pre_rate)
    gate = jax.nn.sigmoid(pre_gate)
    hid_ref[:, :128] = pair
    hid_ref[:, 128:] = gate
    narrow_pair = pair.astype(jnp.bfloat16)
    dl_ref[...] = dot32(below(narrow_pair, False), up_ref[:, :128], NT)
    rl_ref[...] = dot32(below(narrow_pair, True), up_ref[:, :128], NT)
    gate_ref[...] = dot32(gate.astype(jnp.bfloat16), up_ref[:, 128:], NT)


def front_forward(x, vectors, w_r, w_k, w_v, down, up):
    tokens, width = x.shape
    wide = pl.BlockSpec((ROWS, width), lambda i: (i, 0))
    own = pl.BlockSpec((ROWS, OWN), lambda i: (i, 0))
    hid = pl.BlockSpec((ROWS, 256), lambda i: (i, 0))
    whole = lambda a: pl.BlockSpec(a.shape, lambda i: (0, 0))
    shape = jax.ShapeDtypeStruct
    return pl.pallas_call(
        front_kernel,
        grid=(tokens // ROWS,),
        in_specs=[wide] + [whole(a) for a in (vectors, w_r, w_k, w_v, down, up)],
        out_specs=[wide] * 6 + [own] * 6 + [hid],
        out_shape=[shape((tokens, width), jnp.bfloat16)] * 6
        + [shape((tokens, OWN), jnp.float32)] * 6
        + [shape((tokens, 256), jnp.float32)],
        scratch_shapes=[pltpu.VMEM((8, width), jnp.float32)],
        compiler_params=pltpu.CompilerParams(vmem_limit_bytes=60 << 20),
        cost_estimate=SMALL,
        name="front_forward",
    )(x, vectors, w_r, w_k, w_v, down, up)


def front_back_kernel(
    x_ref, before_ref, vec_ref, wr_ref, wk_ref, wv_ref, down_ref, up_ref,
    m1_ref, m4_ref, m5_ref, hid_ref,
    dq_ref, dk_ref, dv_ref, ddl_ref, drl_ref, dgate_ref, own_vec_ref, ffn_vec_ref,
    dx_ref, mine_ref, other_ref,
    edge_ref, sums_ref, misc_ref,
):
    step = pl.num_programs(0) - 1 - pl.program_id(0)
    core = lax.axis_index("dp") % 2
    own_start = pl.multiple_of(core * OWN, OWN)

    @pl.when(pl.program_id(0) == 0)
    def _():
        edge_ref[...] = jnp.zeros_like(edge_ref)
        sums_ref[...] = jnp.zeros_like(sums_ref)
        misc_ref[...] = jnp.zeros_like(misc_ref)

    unit, scale = row_norm(x_ref[...].astype(jnp.float32))
    gain, offset = vec_ref[12:13], vec_ref[13:14]
    normed = unit * gain + offset
    tail, _ = row_norm(before_ref[...].astype(jnp.float32))
    edge = (tail[15:] * gain + offset) * jnp.where(step == 0, 0.0, 1.0)
    change = shifted(normed, edge, True) - normed
    ddl, drl, dgate = ddl_ref[...], drl_ref[...], dgate_ref[...]
    hid = hid_ref[...]
    pair, gate = hid[:, :128], hid[:, 128:]
    lane = lax.broadcasted_iota(jnp.int32, pair.shape, 1)
    first_up, last_up = up_ref[:, :128], up_ref[:, 128:]
    pair_grad = jnp.where(
        lane < DECAY_RANK,
        dot32(ddl, first_up, NN) * (1.0 - pair * pair),
        dot32(drl, first_up, NN),
    ).astype(jnp.bfloat16)
    gate_grad = (dot32(dgate, last_up, NN) * gate * (1.0 - gate)).astype(jnp.bfloat16)
    narrow_pair, narrow_gate = pair.astype(jnp.bfloat16), gate.astype(jnp.bfloat16)
    own_rows = pl.ds(own_start, OWN)
    misc_ref[own_rows, 256:384] += dot32(ddl, below(narrow_pair, False), TN) + dot32(
        drl, below(narrow_pair, True), TN
    )
    misc_ref[own_rows, 384:512] += dot32(dgate, narrow_gate, TN)
    decay_part, rate_part = below(pair_grad, False), below(pair_grad, True)
    misc_ref[:, :128] += dot32(m1_ref[...], decay_part, TN) + dot32(m4_ref[...], rate_part, TN)
    misc_ref[:, 128:256] += dot32(m5_ref[...], gate_grad, TN)
    first_down = down_ref[:, :128]
    grads = (
        lambda: dot32(dq_ref[...], wr_ref[...], NT),
        lambda: dot32(decay_part, first_down, NT),
        lambda: dot32(dk_ref[...], wk_ref[...], NT),
        lambda: dot32(dv_ref[...], wv_ref[...], NT),
        lambda: dot32(rate_part, first_down, NT),
        lambda: dot32(gate_grad, down_ref[:, 128:], NT),
    )
    total = jnp.zeros_like(change)
    moved = jnp.zeros_like(change)
    for j, grad in enumerate(grads):
        now = grad()
        total = total + now
        moved = moved + now * vec_ref[j : j + 1]
        sums_ref[j : j + 1] += jnp.sum(now * change, axis=0, keepdims=True)
    dnormed = total - moved + shifted(moved, edge_ref[:1], False)
    edge_ref[:1] = moved[:1]
    sums_ref[12:13] += jnp.sum(dnormed * unit, axis=0, keepdims=True)
    sums_ref[13:14] += jnp.sum(dnormed, axis=0, keepdims=True)
    dunit = dnormed * gain
    dx_ref[...] = scale * (
        dunit
        - jnp.mean(dunit, axis=-1, keepdims=True)
        - unit * jnp.mean(dunit * unit, axis=-1, keepdims=True)
    )

    @pl.when(step == 0)
    def _():
        sums_ref[6:7] = ffn_vec_ref[0:1] * 0.5
        sums_ref[14:16] = ffn_vec_ref[1:3] * 0.5
        zeros = jnp.zeros((1, OWN), jnp.float32)
        for target, source in ((7, 0), (8, 1), (9, 2), (10, 3), (11, 4), (16, 5), (17, 6)):
            mine = own_vec_ref[source : source + 1]
            sums_ref[target : target + 1] = jnp.concatenate(
                [jnp.where(core == 0, mine, zeros), jnp.where(core == 0, zeros, mine)], axis=1
            )
        for block in range(EMBED // 128):
            lanes = slice(block * 128, (block + 1) * 128)
            misc_ref[lanes, 512:640] = sums_ref[:, lanes].T
        share = mine_ref.shape[1]
        for chip in range(mine_ref.shape[0]):
            low = misc_ref[2 * chip * share : (2 * chip + 1) * share]
            high = misc_ref[(2 * chip + 1) * share : (2 * chip + 2) * share]
            mine_ref[chip] = jnp.where(core == 0, low, high)
            other_ref[chip] = jnp.where(core == 0, high, low).astype(jnp.bfloat16)


def front_backward(
    x, vectors, w_r, w_k, w_v, down, up, mixes, hid, grads, own_vec, ffn_vec
):
    tokens, width = x.shape
    devices = lax.axis_size("dp")
    pieces = (devices // 2, EMBED // devices, 640)
    steps = tokens // ROWS
    wide = pl.BlockSpec((ROWS, width), lambda i: (steps - 1 - i, 0))
    before = pl.BlockSpec(
        (16, width), lambda i: (jnp.maximum((steps - 1 - i) * (ROWS // 16) - 1, 0), 0)
    )
    own = pl.BlockSpec((ROWS, OWN), lambda i: (steps - 1 - i, 0))
    hid_spec = pl.BlockSpec((ROWS, 256), lambda i: (steps - 1 - i, 0))
    whole = lambda a: pl.BlockSpec(a.shape, lambda i: (0, 0))
    shape = jax.ShapeDtypeStruct
    return pl.pallas_call(
        front_back_kernel,
        grid=(steps,),
        in_specs=[wide, before]
        + [whole(a) for a in (vectors, w_r, w_k, w_v, down, up)]
        + [wide] * 3
        + [hid_spec]
        + [own] * 6
        + [whole(own_vec), whole(ffn_vec)],
        out_specs=[wide] + [pl.BlockSpec(pieces, lambda i: (0, 0, 0))] * 2,
        out_shape=[
            shape((tokens, width), jnp.float32),
            shape(pieces, jnp.float32),
            shape(pieces, jnp.bfloat16),
        ],
        scratch_shapes=[
            pltpu.VMEM((8, width), jnp.float32),
            pltpu.VMEM((128, width), jnp.float32),
            pltpu.VMEM((EMBED, 640), jnp.float32),
        ],
        compiler_params=pltpu.CompilerParams(vmem_limit_bytes=60 << 20),
        cost_estimate=SMALL,
        name="front_backward",
    )(x, x, vectors, w_r, w_k, w_v, down, up, *mixes, hid, *grads, own_vec, ffn_vec)


def ffn_back_kernel(
    len_ref, res_ref, before_ref, cot_ref, mine_ref, other_ref, vec_ref, wo_ref,
    grad_ref, narrow_ref, gated_ref, dvec_ref,
    edge_ref,
):
    step = pl.num_programs(0) - 1 - pl.program_id(0)

    @pl.when(pl.program_id(0) == 0)
    def _():
        edge_ref[...] = jnp.zeros_like(edge_ref)
        dvec_ref[...] = jnp.zeros_like(dvec_ref)

    gain, offset, coefficient = vec_ref[14:15], vec_ref[15:16], vec_ref[6:7]
    unit, scale = row_norm(res_ref[...])
    normed = unit * gain + offset
    tail, _ = row_norm(before_ref[...])
    edge = (tail[7:] * gain + offset) * jnp.where(step == 0, 0.0, 1.0)
    change = shifted(normed, edge, True) - normed
    grad = mine_ref[...].astype(jnp.float32) + other_ref[...].astype(jnp.float32)
    moved = grad * coefficient
    dnormed = grad - moved + shifted(moved, edge_ref[:1], False)
    edge_ref[:1] = moved[:1]
    sums = lambda x: jnp.sum(x, axis=0, keepdims=True)
    dvec_ref[0:1] += sums(grad * change)
    dvec_ref[1:2] += sums(dnormed * unit)
    dvec_ref[2:3] += sums(dnormed)
    dunit = dnormed * gain
    row = lax.broadcasted_iota(jnp.int32, grad.shape, 0) + step * ROWS
    out_grad = jnp.where(row < len_ref[0], cot_ref[...].astype(jnp.float32), 0.0)
    total = out_grad + scale * (
        dunit
        - jnp.mean(dunit, axis=-1, keepdims=True)
        - unit * jnp.mean(dunit * unit, axis=-1, keepdims=True)
    )
    grad_ref[...] = total
    small = total.astype(jnp.bfloat16)
    core = lax.axis_index("dp") % 2
    narrow_ref[...] = jnp.where(core == 0, small[:, :OWN], small[:, OWN:])
    gated_ref[...] = dot32(small, wo_ref[...], NT)


def ffn_backward(length, residual, cot, mine, other, vectors, w_o_rows):
    tokens, width = residual.shape
    steps = tokens // ROWS
    wide = pl.BlockSpec((ROWS, width), lambda i: (steps - 1 - i, 0))
    before = pl.BlockSpec(
        (8, width), lambda i: (jnp.maximum((steps - 1 - i) * (ROWS // 8) - 1, 0), 0)
    )
    own = pl.BlockSpec((ROWS, OWN), lambda i: (steps - 1 - i, 0))
    whole = lambda a: pl.BlockSpec(a.shape, lambda i: (0, 0))
    shape = jax.ShapeDtypeStruct
    return pl.pallas_call(
        ffn_back_kernel,
        grid=(steps,),
        in_specs=[pl.BlockSpec(memory_space=pltpu.SMEM), wide, before]
        + [wide] * 3
        + [whole(vectors), whole(w_o_rows)],
        out_specs=[wide, own, own, pl.BlockSpec((8, width), lambda i: (0, 0))],
        out_shape=[
            shape((tokens, width), jnp.float32),
            shape((tokens, OWN), jnp.bfloat16),
            shape((tokens, OWN), jnp.float32),
            shape((8, width), jnp.float32),
        ],
        scratch_shapes=[pltpu.VMEM((8, width), jnp.float32)],
        compiler_params=pltpu.CompilerParams(vmem_limit_bytes=60 << 20),
        cost_estimate=SMALL,
        name="ffn_backward",
    )(length, residual, residual, cot, mine, other, vectors, w_o_rows)


def att_grad_kernel(m0_ref, m2_ref, m3_ref, dq_ref, dk_ref, dv_ref, send_a, keep_a, send_b, keep_b):
    chip = lax.axis_index("dp") // 2
    by_x, by_y = chip % 2 == 0, (chip // 2) % 2 == 0
    quarter = OWN // 2
    dv = dv_ref[...]
    first = ((m0_ref, dq_ref[...], 0, OWN), (m3_ref, dv[:, :quarter], OWN, quarter))
    second = ((m2_ref, dk_ref[...], 0, OWN), (m3_ref, dv[:, quarter:], OWN, quarter))
    for left, right, lane, width in first:
        block = dot32(left[...], right, TN).astype(jnp.bfloat16)
        lanes = slice(lane, lane + width)
        for y in range(2):
            low, high = block[y * 128 : y * 128 + 64], block[y * 128 + 64 : y * 128 + 128]
            send_a[y, :, lanes] = jnp.where(by_x, high, low)
            keep_a[y, :, lanes] = jnp.where(by_x, low, high)
    for left, right, lane, width in second:
        block = dot32(left[...], right, TN).astype(jnp.bfloat16)
        lanes = slice(lane, lane + width)
        for x in range(2):
            low, high = block[x * 64 : x * 64 + 64], block[128 + x * 64 : 128 + x * 64 + 64]
            send_b[x, :, lanes] = jnp.where(by_y, high, low)
            keep_b[x, :, lanes] = jnp.where(by_y, low, high)


def att_gradients(mixes, grads):
    tokens = mixes[0].shape[0]
    left = pl.BlockSpec((tokens, 256), lambda i: (0, i))
    right = pl.BlockSpec((tokens, OWN), lambda i: (0, 0))
    out = pl.BlockSpec((2, 64, OWN + OWN // 2), lambda i: (i, 0, 0))
    return pl.pallas_call(
        att_grad_kernel,
        grid=(4,),
        in_specs=[left] * 3 + [right] * 3,
        out_specs=[out] * 4,
        out_shape=[jax.ShapeDtypeStruct((8, 64, OWN + OWN // 2), jnp.bfloat16)] * 4,
        compiler_params=pltpu.CompilerParams(vmem_limit_bytes=60 << 20),
        cost_estimate=SMALL,
        name="att_gradients",
    )(*mixes, *grads)


def swap(block, mask):
    size = lax.axis_size("dp")
    return lax.ppermute(block, "dp", [(i, i ^ mask) for i in range(size)])


def bit_of(mask):
    return (lax.axis_index("dp") // mask) % 2


def in_order(mask, own, other, axis):
    lower = bit_of(mask) == 0
    return jnp.where(
        lower, jnp.concatenate([own, other], axis=axis), jnp.concatenate([other, own], axis=axis)
    )


def chip_masks():
    size = lax.axis_size("dp")
    masks = []
    while 2 << len(masks) < size:
        masks.append(2 << len(masks))
    return masks


def steps_of(kind):
    masks = chip_masks()
    near, far = [[mask] for mask in masks[:2]], [[mask] for mask in masks[2:][::-1]]
    first = [[far[0][0], far[1][0], far[0][0] | far[1][0]]] if len(far) == 2 else far
    return [first + near[::-1], first + near, far + near[::-1], far + near, near + far][kind]


class Held:
    def __init__(self, value):
        self.value = value


def meet(movers, *arrays):
    held = []
    for mover in movers:
        held += [x[0] for x in mover.arrived if x[0] not in held]
    out = lax.optimization_barrier(tuple(x.value for x in held) + arrays)
    for x, value in zip(held, out):
        x.value = value
    return out[len(held) :]


def read(arrived):
    return [x.value if lanes is None else x.value[..., lanes] for x, lanes in arrived]


class Gather:
    def __init__(self, block, kind, places=(0,)):
        self.steps = steps_of(kind)
        self.held = block[None]
        self.places = [0]
        self.arrived = []
        self.masks = []

    def merge(self):
        if self.arrived:
            self.held = jnp.concatenate([self.held] + read(self.arrived), axis=0)
            self.places = self.places + [p ^ (m // 2) for m in self.masks for p in self.places]
            self.arrived = []

    def step(self):
        if self.steps:
            self.merge()
            self.masks = self.steps.pop(0)
            self.arrived = [(Held(swap(self.held, mask)), None) for mask in self.masks]
        return self

    def run(self):
        while self.steps:
            self.step()
        return self

    def split(self, kinds):
        width = self.held.shape[-1] // len(kinds)
        out = []
        for i, kind in enumerate(kinds):
            part = Gather.__new__(Gather)
            cut = slice(i * width, (i + 1) * width)
            part.steps = steps_of(kind)[len(steps_of(kind)) - len(self.steps) :]
            part.held = self.held[..., cut]
            part.arrived = [(x, cut) for x, _ in self.arrived]
            part.places, part.masks = self.places, self.masks
            out.append(part)
        return out


def place_kernel(places, cuts, *refs):
    sources, outs = refs[: len(places)], refs[len(places) :]
    chip = lax.axis_index("dp") // 2
    for source, (part, list_of) in zip(sources, places):
        for j, place in enumerate(list_of):
            for out, (first, rows, lanes) in zip(outs, cuts):
                start = pl.multiple_of((chip ^ place) * rows, rows)
                lane, width = lanes[part]
                at = sum(w for _, w in lanes[:part])
                out[pl.ds(start, rows), at : at + width] = source[
                    j, first : first + rows, lane : lane + width
                ]


def assemble(gathers, cuts=None):
    gathers = [g.run() for g in gathers]
    rows = gathers[0].held.shape[1]
    cuts = cuts or ((0, rows, [(0, g.held.shape[2]) for g in gathers]),)
    sources, places = [], []
    for i, g in enumerate(gathers):
        sources += [g.held] + read(g.arrived)
        shifts = [0] + [mask // 2 for mask in g.masks]
        places += [(i, [p ^ shift for p in g.places]) for shift in shifts]
    count = lax.axis_size("dp") // 2
    if any(cut[1] % 16 for cut in cuts):
        return assemble_plain(sources, places, cuts, count)
    space = pl.BlockSpec(memory_space=pltpu.VMEM)
    return pl.pallas_call(
        partial(place_kernel, places, cuts),
        in_specs=[space] * len(sources),
        out_specs=[space] * len(cuts),
        out_shape=[
            jax.ShapeDtypeStruct((count * n, sum(w for _, w in lanes)), sources[0].dtype)
            for _, n, lanes in cuts
        ],
        compiler_params=pltpu.CompilerParams(vmem_limit_bytes=32 << 20),
        cost_estimate=SMALL,
        name="assemble",
    )(*sources)


def assemble_plain(sources, places, cuts, count):
    chip = lax.axis_index("dp") // 2
    parts = []
    for part in sorted({part for part, _ in places}):
        blocks = jnp.concatenate([x for x, (at, _) in zip(sources, places) if at == part])
        where = [p for at, list_of in places if at == part for p in list_of]
        blocks = jnp.stack([blocks[where.index(i)] for i in range(count)])
        parts.append(jnp.take(blocks, chip ^ lax.iota(jnp.int32, count), axis=0))
    return [
        jnp.concatenate(
            [x[:, first : first + n, at : at + w] for x, (at, w) in zip(parts, lanes)], axis=-1
        ).reshape(count * n, -1)
        for first, n, lanes in cuts
    ]


class Scatter:
    def __init__(self, parts, kind):
        self.steps = steps_of(kind)[::-1]
        self.axes = chip_masks()[::-1]
        self.sources = [parts.reshape((2,) * len(self.axes) + parts.shape[1:])]
        self.arrived = []
        self.sent = None

    @classmethod
    def begun(cls, sent, kept, kind):
        out = cls.__new__(cls)
        out.steps = steps_of(kind)[::-1]
        out.axes = [axis for axis in chip_masks()[::-1] if axis != out.steps[0][0]]
        out.sources = [kept.reshape((2,) * len(out.axes) + kept.shape[1:])]
        out.arrived = []
        out.sent = [sent.reshape(out.sources[0].shape)]
        return out

    def pick(self, sources, mask, gone):
        out = []
        for x in sources:
            for place in reversed(range(len(self.axes))):
                axis = self.axes[place]
                if axis in gone:
                    which = bit_of(axis) if not mask & axis else 1 - bit_of(axis)
                    x = lax.dynamic_index_in_dim(x, which, place, keepdims=False)
            out.append(x)
        return out

    def prepare(self):
        if self.sent is not None:
            return self
        masks = self.steps[0]
        sources = self.sources + read(self.arrived)
        gone = [axis for axis in self.axes if any(mask & axis for mask in masks)]
        self.sent = [
            sum(x.astype(jnp.float32) for x in self.pick(sources, mask, gone)).astype(jnp.bfloat16)
            for mask in masks
        ]
        self.sources = self.pick(sources, 0, gone)
        self.axes = [axis for axis in self.axes if axis not in gone]
        self.arrived = []
        return self

    def step(self):
        return together([self])[0]

    def run(self):
        while self.steps:
            self.step()
        return self

    def total(self):
        return sum(x.astype(jnp.float32) for x in self.sources + read(self.arrived))


def together(parts):
    if not parts[0].steps:
        return parts
    for part in parts:
        part.prepare()
    for i, mask in enumerate(parts[0].steps[0]):
        sent = [part.sent[i] for part in parts]
        got = Held(swap(sent[0] if len(sent) == 1 else jnp.concatenate(sent, axis=-1), mask))
        at = 0
        for part, x in zip(parts, sent):
            lanes = slice(at, at + x.shape[-1]) if len(sent) > 1 else None
            part.arrived.append((got, lanes))
            at += x.shape[-1]
    for part in parts:
        part.steps.pop(0)
        part.sent_now, part.sent = part.sent[0], None
    return parts


def norm_rows(features, gain_row, offset_row):
    average = jnp.mean(features, axis=-1, keepdims=True)
    centred = features - average
    variance = jnp.mean(centred * centred, axis=-1, keepdims=True)
    return centred * lax.rsqrt(variance + 1e-05) * gain_row + offset_row


def product(operand, weight_matrix):
    return jnp.dot(operand, weight_matrix, preferred_element_type=jnp.float32)


def input_gradient_rows(upstream_gradient, weight_matrix):
    return lax.dot_general(
        upstream_gradient,
        weight_matrix,
        (((1,), (1,)), ((), ())),
        preferred_element_type=jnp.float32,
    )


def weight_gradient(operand, upstream_gradient):
    return lax.dot_general(
        operand, upstream_gradient, (((0,), (0,)), ((), ())), preferred_element_type=jnp.float32
    )


def earlier(rows):
    return jnp.concatenate([jnp.zeros_like(rows[:1]), rows[:-1]], axis=0)


def ffn_mix(residual, vectors):
    second = norm_rows(residual, vectors[14], vectors[15])
    return second + (earlier(second) - second) * vectors[6]


def narrow(x):
    return x.astype(jnp.bfloat16)


def local(
    inputs,
    lengths,
    attention_projections,
    channel_key_weight,
    channel_value_weight,
    lowrank_down_weight,
    lowrank_up_weight,
    per_feature_parameters,
    cotangent,
):
    devices = lax.axis_size("dp")
    chips = devices // 2
    device = lax.axis_index("dp")
    chip, core = device // 2, device % 2
    row_count = inputs.shape[0]
    slots = 2 * row_count
    share = EMBED // devices
    pair_share = 2 * share
    units = channel_value_weight.shape[0]
    half_units = chips * units

    def own_cut(x, which):
        return lax.dynamic_slice_in_dim(x, which * OWN, OWN, x.ndim - 1)

    def own_rows(x, which):
        return lax.dynamic_slice_in_dim(x, which * row_count, row_count, 0)

    pair_rows = in_order(
        1,
        own_cut(attention_projections, core),
        swap(own_cut(attention_projections, 1 - core), 1),
        1,
    )
    lora = jnp.concatenate([lowrank_down_weight, lowrank_up_weight.T], axis=1)
    vector_rows = jnp.pad(per_feature_parameters.T, ((0, 0), (0, 128 - 18)))
    vector_rows = vector_rows.reshape(share // 4, OWN)
    first_rows = 3 * pair_share
    misc_rows = share + share // 4 + (share // 4) % 16
    block = jnp.concatenate(
        [
            pair_rows[:3].reshape(first_rows, OWN),
            lora,
            jnp.pad(vector_rows, ((0, (share // 4) % 16), (0, 0))),
        ],
        axis=0,
    )
    half = half_units // 2
    quarter = OWN // 2
    first = Gather(block, 0).step()
    w_o_part = Gather(pair_rows[3], 4).step().step()
    key_in, raw, cot, _ = meet([], channel_key_weight, inputs, cotangent, first.held)
    key_cut = key_in.reshape(share, chips, 2, units)

    def key_columns(which):
        return lax.dynamic_index_in_dim(key_cut, which, 2, keepdims=False).reshape(share, half_units)

    key_rows = in_order(1, key_columns(core), swap(key_columns(1 - core), 1), 0)
    tokens = in_order(1, raw, swap(raw, 1), 0)
    cot = in_order(1, cot, swap(cot, 1), 0)
    key_rows, tokens, cot = meet([first, w_o_part], key_rows, tokens, cot)
    first = first.split((0, 1))
    for part in first:
        part.step()
    key_part = Gather(key_rows, 2).step()
    (tokens,) = meet(first, tokens)
    for part in first:
        part.step()
    value_block, *_ = meet([key_part], channel_value_weight, *[part.held for part in first])
    key_part.step()
    value_part = Gather(value_block, 2).step()
    w_o_part.step()
    (tokens,) = meet(first + [key_part, value_part], tokens)
    key_parts = key_part.split((2, 3))
    for part in key_parts:
        part.step()
    w_r, w_k, w_v, misc = assemble(
        first,
        [(i * pair_share, pair_share, [(0, quarter)] * 2) for i in range(3)]
        + [(first_rows, misc_rows, [(0, quarter)] * 2)],
    )
    misc = misc.reshape(chips, 1, misc_rows, OWN)
    misc = in_order(1, misc, swap(misc, 1), 1)
    value_part.step()
    lora = misc[:, :, :share].reshape(EMBED, OWN)
    down, up_t = lora[:, :256], lax.dynamic_slice_in_dim(lora[:, 256:], core * OWN, OWN, 0)
    vectors = misc[:, :, share : share + share // 4].reshape(EMBED, 128)[:, :18].T
    vectors = vectors.astype(jnp.float32)
    own_vectors = own_cut(vectors, core)
    used = jnp.concatenate([own_vectors[7:12], own_vectors[16:18], own_vectors[:1]], axis=0)
    length = lax.dynamic_index_in_dim(lengths, chip, 0)
    live = (lax.iota(jnp.int32, slots) < length)[:, None]

    *mixes, queries, keys, values, decay_low, rate_low, gate_rows, hid = front_forward(
        tokens, vectors, w_r, w_k, w_v, down, up_t
    )
    terms = meet(
        key_parts + [value_part, w_o_part],
        queries, keys, values, decay_low, rate_low, gate_rows,
    )
    value_parts = value_part.split((2, 3))
    for part in key_parts + value_parts:
        part.step()
    w_o_part.step()
    blocks = slots // (CHUNK * STEP_CHUNKS)
    zero_state = jnp.zeros((2, CHUNK, LANES), jnp.float32)
    gated, *saved, _ = wkv_forward(0, blocks, length, used, zero_state, terms)
    gated, cot, tokens = meet(key_parts + value_parts, gated, cot, tokens)
    for part in value_parts:
        part.step()
    gated, *_ = meet([w_o_part] + key_parts, gated, *[part.held for part in value_parts])
    gated_all = in_order(1, gated, swap(gated, 1), 1)
    (w_o_own,) = assemble([w_o_part])
    w_o = in_order(1, w_o_own, swap(w_o_own, 1), 1)
    (key_weight,) = assemble(key_parts)
    residual = tokens.astype(jnp.float32) + product(gated_all, w_o)
    ffn_in = narrow(ffn_mix(residual, vectors))
    positive = jax.nn.relu(product(ffn_in, key_weight))
    hidden = narrow(jnp.square(positive))
    out_narrow = jnp.where(live, cot, jnp.zeros_like(cot))
    grad_value = narrow(weight_gradient(hidden, out_narrow)).reshape(chips, units, EMBED)
    w_o_rows = lax.dynamic_slice_in_dim(w_o, core * OWN, OWN, 0)
    value_scatter = [
        Scatter(grad_value[..., i * OWN : (i + 1) * OWN], 2 + i).prepare() for i in range(2)
    ]
    hidden, positive, out_narrow, w_o_rows, *sent = meet(
        value_parts, hidden, positive, out_narrow, w_o_rows, *[m.sent[0] for m in value_scatter]
    )
    for part, x in zip(value_scatter, sent):
        part.sent = [x]
        part.step()
    (value_weight,) = assemble(value_parts)

    pre_narrow = narrow(2.0 * positive * input_gradient_rows(out_narrow, value_weight))
    ffn_in_grad = narrow(input_gradient_rows(pre_narrow, key_weight))
    other_grad = swap(ffn_in_grad, 1)
    grad_key = narrow(weight_gradient(ffn_in, pre_narrow)).reshape(chips, pair_share, half_units)
    residual_grad, own_grad, gated_grad, ffn_vec = ffn_backward(
        length, residual, cot, ffn_in_grad, other_grad, vectors, w_o_rows
    )
    grad_o = narrow(weight_gradient(gated_all, own_grad)).reshape(chips, pair_share, OWN)
    key_scatter = [Scatter(grad_key[:, :, i * half : (i + 1) * half], 2 + i) for i in range(2)]
    o_scatter = [Scatter(grad_o[:, :, i * quarter : (i + 1) * quarter], 2 + i) for i in range(2)]
    key_pairs = list(zip(key_scatter, o_scatter))
    key_scatter = key_scatter + o_scatter
    for part in key_scatter:
        part.prepare()
    gated_grad, *sent = meet([], gated_grad, *[m.sent[0] for m in key_scatter])
    for part, x in zip(key_scatter, sent):
        part.sent = [x]
    for pair in key_pairs:
        together(pair)
    terms = [*terms, gated_grad, *saved]
    zero_sums = jnp.zeros((8, OWN), jnp.float32)
    early = blocks // 2
    *before, sums, state = wkv_backward(
        early, blocks - early, length, used, zero_state, zero_sums, terms
    )
    state, sums = meet(value_scatter, state, sums)
    for part in value_scatter:
        part.step()
    *low_grads, own_vec, _ = wkv_backward(0, early, length, used, state, sums, terms, before)
    if pair_share == 64:
        sent_a, kept_a, sent_b, kept_b = att_gradients(
            (mixes[0], mixes[2], mixes[3]), low_grads[:3]
        )
        att_scatter = [Scatter.begun(sent_a, kept_a, 2), Scatter.begun(sent_b, kept_b, 3)]
    else:
        grads = [narrow(weight_gradient(mixes[m], g)) for m, g in zip((0, 2, 3), low_grads)]
        att_scatter = [
            Scatter(jnp.concatenate(x, axis=1).reshape(chips, pair_share, 3 * quarter), 2 + i).prepare()
            for i, x in enumerate(
                ((grads[0], grads[2][:, :quarter]), (grads[1], grads[2][:, quarter:]))
            )
        ]
    own_vec, *sent = meet(
        key_scatter + value_scatter, own_vec, *[m.sent[0] for m in att_scatter]
    )
    for part, x in zip(att_scatter, sent):
        part.sent = [x]
        part.step()
    for pair in key_pairs:
        together(pair)
    together(value_scatter)
    own_vec, *_ = meet([], own_vec, *[m.sent_now for m in key_scatter])
    token_part, misc_mine, misc_other = front_backward(
        tokens, vectors, w_r, w_k, w_v, down, up_t, (mixes[1], mixes[4], mixes[5]), hid,
        low_grads, own_vec, ffn_vec,
    )
    misc_other = swap(misc_other, 1)
    token_part, misc_mine, misc_other = meet(
        att_scatter + key_scatter + value_scatter, token_part, misc_mine, misc_other
    )
    for part in att_scatter:
        part.step()
    misc_sum = misc_mine + misc_other.astype(jnp.float32)
    misc_sum = jnp.concatenate([misc_sum[..., :320], misc_sum[..., 320:]], axis=1)
    misc_scatter = Scatter(misc_sum, 3).step()
    together(key_scatter)
    together(value_scatter)
    token_part, hidden = meet(key_scatter + [misc_scatter], token_part, hidden)
    misc_scatter.step()
    together(key_scatter)
    (token_part,) = meet(att_scatter + [misc_scatter], token_part)
    masks = chip_masks()
    last_parts = att_scatter + [misc_scatter]
    if len(misc_scatter.steps) == 2:
        for part in last_parts:
            part.steps = [[masks[2], masks[3], masks[2] | masks[3]]]
    together(last_parts)
    ffn_part = product(hidden, value_weight)
    input_gradient = (
        own_rows(residual_grad, core)
        + own_rows(token_part, core)
        + swap(own_rows(token_part, 1 - core), 1)
    )
    ffn_out = own_rows(ffn_part, core) + swap(own_rows(ffn_part, 1 - core), 1)
    output = narrow(jnp.where(own_rows(live, core), own_rows(residual, core) + ffn_out, 0.0))
    value_sum = jnp.concatenate(
        [x.run().total() for x in value_scatter], axis=1
    )
    while key_scatter[0].steps:
        together(key_scatter)
    key_sum = jnp.concatenate([x.total() for x in key_scatter], axis=1).reshape(2, share, -1)

    def exchange(x):
        mine = lax.dynamic_index_in_dim(x, core, 0, keepdims=False)
        return mine, swap(lax.dynamic_index_in_dim(x, 1 - core, 0, keepdims=False), 1)

    key_mine, key_theirs = exchange(key_sum)
    input_gradient, value_sum, key_mine, key_theirs = meet(
        last_parts, input_gradient, value_sum, key_mine, key_theirs
    )
    while last_parts[0].steps:
        together(last_parts)
    first_sum, second_sum, misc_sum = [x.total() for x in last_parts]
    misc_sum = jnp.concatenate([misc_sum[:share], misc_sum[share:]], axis=1)
    att_sum = jnp.concatenate(
        [first_sum[:, :OWN], second_sum[:, :OWN], first_sum[:, OWN:], second_sum[:, OWN:]], axis=1
    )
    mine, theirs = exchange(att_sum.reshape(2, share, -1))
    mine = jnp.concatenate([mine, key_mine[:, half_units:]], axis=1)
    theirs = jnp.concatenate([theirs, key_theirs[:, half_units:]], axis=1)
    shard_mixer = jnp.stack(
        [
            in_order(1, mine[:, i * OWN : (i + 1) * OWN], theirs[:, i * OWN : (i + 1) * OWN], 1)
            for i in range(4)
        ]
    )
    shard_key = in_order(
        1,
        key_mine[:, :half_units].reshape(share, chips, 1, units),
        key_theirs[:, :half_units].reshape(share, chips, 1, units),
        2,
    ).reshape(share, 2 * half_units)
    return (
        output,
        input_gradient,
        shard_mixer,
        shard_key,
        value_sum,
        misc_sum[:, :256],
        misc_sum[:, 256:512].T,
        misc_sum[:, 512:530].T,
    )


def solution(mesh):
    in_specs = (
        P("dp", None),
        P(),
        P(None, "dp", None),
        P("dp", None),
        P("dp", None),
        P("dp", None),
        P(None, "dp"),
        P(None, "dp"),
        P("dp", None),
    )
    out_specs = (
        P("dp", None),
        P("dp", None),
        P(None, "dp", None),
        P("dp", None),
        P("dp", None),
        P("dp", None),
        P(None, "dp"),
        P(None, "dp"),
    )
    return jax.shard_map(local, mesh=mesh, in_specs=in_specs, out_specs=out_specs, check_vma=False)
```

```python
from functools import partial

import jax
import jax.numpy as jnp
from jax import lax
from jax.experimental import pallas as pl
from jax.experimental.pallas import tpu as pltpu
from jax.sharding import PartitionSpec as P

HEADS = 16
HEAD_SIZE = 64
DECAY_RANK = 64
RATE_RANK = 64
EMBED = 1024
OWN = EMBED // 2
PRECISE = lax.Precision.HIGHEST


CHUNK = 64
LANES = 256
GROUP_HEADS = 4
STEP_CHUNKS = 2
SMALL = pl.CostEstimate(flops=1, bytes_accessed=1, transcendentals=0)

NN = (((1,), (0,)), ((), ()))
NT = (((1,), (1,)), ((), ()))
TN = (((0,), (0,)), ((), ()))


def halves(x):
    high = x.astype(jnp.bfloat16)
    return high, (x - high.astype(jnp.float32)).astype(jnp.bfloat16)


def whole(x):
    return (x.astype(jnp.bfloat16),)


def dot32(a, b, dims):
    return lax.dot_general(a, b, dims, preferred_element_type=jnp.float32)


def mul(left, right, dims=NN):
    if len(left) == 1 or len(right) == 1:
        return dot32(left[0], right[0], dims)
    rows = left[0].shape[0]
    both = dot32(jnp.concatenate(left, axis=0), right[0], dims)
    return both[:rows] + both[rows:] + dot32(left[0], right[1], dims)


def tmul(left, right, masks):
    full = dot32(left[0], right[0], TN)
    if len(left) > 1 and len(right) > 1:
        full = full + dot32(left[1], right[0], TN) + dot32(left[0], right[1], TN)
    return sum(full[h * CHUNK : (h + 1) * CHUNK] * masks[h][:1].astype(jnp.float32) for h in range(GROUP_HEADS))


def spread(pair, masks):
    return tuple(
        jnp.concatenate([part * masks[h] for h in range(GROUP_HEADS)], axis=0) for part in pair
    )


def stack(first, second):
    return tuple(jnp.concatenate([x, y], axis=0) for x, y in zip(first, second))


def head_masks():
    lane = lax.broadcasted_iota(jnp.int32, (CHUNK, LANES), 1) // CHUNK
    return [(lane == h).astype(jnp.float32).astype(jnp.bfloat16) for h in range(GROUP_HEADS)]


def places():
    row = lax.broadcasted_iota(jnp.int32, (CHUNK, LANES), 0)
    col = lax.broadcasted_iota(jnp.int32, (CHUNK, LANES), 1) % CHUNK
    return row, col


def running_sum(x, upper=False):
    row = lax.broadcasted_iota(jnp.int32, (CHUNK, CHUNK), 0)
    col = lax.broadcasted_iota(jnp.int32, (CHUNK, CHUNK), 1)
    ones = (row <= col if upper else col <= row).astype(jnp.float32).astype(jnp.bfloat16)
    high, rest = halves(x)
    low = (x - high.astype(jnp.float32) - rest.astype(jnp.float32)).astype(jnp.bfloat16)
    return dot32(ones, high, NN) + dot32(ones, rest, NN) + dot32(ones, low, NN)


def scaled_forms(q, w, k, a, b):
    total = running_sum(w)
    before = total - w
    middle = total[CHUNK // 2 - 1 : CHUNK // 2]
    end = total[CHUNK - 1 :]
    ea = jnp.exp(before - middle)
    eq = jnp.exp(total - middle)
    eb = jnp.exp(middle - total)
    ee = jnp.exp(end - total)
    return (a * ea, q * eq, b * eb, k * eb, b * ee, k * ee), (ea, eq, eb, ee), (jnp.exp(middle), jnp.exp(end))


def each(fn, *columns):
    return [fn(*row) for row in zip(*columns)]


def block_ones():
    row = lax.broadcasted_iota(jnp.int32, (LANES, LANES), 0) // CHUNK
    col = lax.broadcasted_iota(jnp.int32, (LANES, LANES), 1) // CHUNK
    return (row == col).astype(jnp.float32).astype(jnp.bfloat16)


def head_sum(x, ones):
    rows = x.shape[0]
    both = dot32(jnp.concatenate(halves(x), axis=0), ones, NN)
    return both[:rows] + both[rows:]


def prepared(keys, decay_low, rate_low, live, vec, ones):
    sig = jax.nn.sigmoid(vec[0] + decay_low)
    log_decay = (-0.6065306597126334) * sig * live
    rates = jax.nn.sigmoid(vec[1] + rate_low)
    scaled = keys * vec[2]
    inverse = lax.rsqrt(head_sum(scaled * scaled, ones) + 1e-06)
    unit_keys = scaled * inverse
    factor = (1.0 + (rates - 1.0) * vec[3]) * live
    return log_decay, keys * factor, -unit_keys, unit_keys * rates * live, sig, rates, inverse, factor


def read_out(o, q, k, v, vec, ones):
    centred = o - head_sum(o, ones) * (1.0 / CHUNK)
    scale = lax.rsqrt(head_sum(centred * centred, ones) * (1.0 / CHUNK) + 0.00064)
    normed = centred * scale
    weight = head_sum(q * k * vec[4], ones)
    return normed, scale, weight, normed * vec[5] + vec[6] + weight * v


def unit_slices():
    return [
        (slice(c * CHUNK, (c + 1) * CHUNK), slice(g * LANES, (g + 1) * LANES))
        for c in range(STEP_CHUNKS)
        for g in range(2)
    ]


def unit_live(length, step):
    row = lax.broadcasted_iota(jnp.int32, (CHUNK, LANES), 0)
    start = step * (STEP_CHUNKS * CHUNK)
    live = [(row + (start + c * CHUNK) < length).astype(jnp.float32) for c in range(STEP_CHUNKS)]
    return [live[c] for c in range(STEP_CHUNKS) for g in range(2)]


def unit_vectors(vec_ref):
    vec = [[vec_ref[i : i + 1, g * LANES : (g + 1) * LANES] for i in range(7)] for g in range(2)]
    return [vec[g] for c in range(STEP_CHUNKS) for g in range(2)]


def forward_kernel(base, *refs):
    len_ref, vec_ref, start_ref, q_ref, keys_ref, v_ref, dl_ref, rl_ref, gate_ref = refs[:9]
    (
        out_ref, o_ref, t_ref, aqb_ref, aak_ref, aqk_ref, y_ref, z_ref, trt_ref, qe_ref, state_ref,
    ) = refs[-11:]

    @pl.when(pl.program_id(0) == 0)
    def _():
        state_ref[...] = start_ref[...]

    masks = head_masks()
    row, col = places()
    strict = (col < row).astype(jnp.float32)
    within = (col <= row).astype(jnp.float32)
    eye = (col == row).astype(jnp.float32)
    ones = block_ones()
    units = unit_slices()
    live = unit_live(len_ref[0], pl.program_id(0) + base)
    vec = unit_vectors(vec_ref)
    load = lambda ref: [ref[u] for u in units]
    q, keys, v = load(q_ref), load(keys_ref), load(v_ref)
    ready = each(
        lambda x, y, z, m, n: prepared(x, y, z, m, n, ones), keys, load(dl_ref), load(rl_ref), live, vec
    )
    w, k, a, b = ([x[i] for x in ready] for i in range(4))
    forms = each(scaled_forms, q, w, k, a, b)
    ah, qh, bh, kh, bt, kt = ([f[0][i] for f in forms] for i in range(6))
    emid = [f[2][0] for f in forms]
    eend = [f[2][1] for f in forms]
    aq = each(lambda x, y: halves(jnp.concatenate([x, y], axis=0)), ah, qh)
    with_b = each(lambda l, r: mul(l, spread(halves(r), masks), NT), aq, bh)
    with_k = each(lambda l, r: mul(l, spread(halves(r), masks), NT), aq, kh)
    aab = [x[:CHUNK] * strict for x in with_b]
    aqb = [halves(x[CHUNK:] * within) for x in with_b]
    aak = [halves(x[:CHUNK] * strict) for x in with_k]
    aqk = [halves(x[CHUNK:] * within) for x in with_k]
    p = [halves(x * (row // 8 == col // 8)) for x in aab]
    t = [eye + x * (row // 8 == col // 8) for x in aab]
    p2 = each(lambda x: halves(mul(x, spread(x, masks))), p)
    both = each(lambda x, y: mul(stack(x, halves(y)), spread(x, masks)), p2, t)
    p4 = [halves(x[:CHUNK]) for x in both]
    t = each(lambda x, y: x + y[CHUNK:], t, both)
    t = each(lambda x, y: x + mul(halves(x), spread(y, masks)), t, p4)
    for size in (8, 16, 32):
        corner = ((row // size) % 2 == 1) & (col // size == row // size - 1)
        ts = [halves(x) for x in t]
        n = [halves(x * corner) for x in aab]
        tn = each(lambda x, y: halves(mul(x, spread(y, masks))), ts, n)
        t = each(lambda x, y, z: x + mul(y, spread(z, masks)), t, tn, ts)
    ts = [halves(x) for x in t]
    vs = [halves(x) for x in v]
    vm = [spread(x, masks) for x in vs]
    wide = each(lambda x, y, e: mul(x, spread(halves(y * e), masks)), ts, ah, emid)
    r0 = each(mul, aak, vm)
    y0 = each(lambda x, y: mul(x, spread(halves(y), masks)), ts, r0)
    wides = [halves(x) for x in wide]
    qe = each(lambda x, e, y, z: x * e + mul(y, spread(z, masks)), qh, emid, aqb, wides)
    y0s = [halves(x) for x in y0]
    part = each(lambda x, y, z, u: mul(x, spread(y, masks)) + mul(z, u), aqb, y0s, aqk, vm)
    bts = [halves(x) for x in bt]
    diag = [eye * e for e in eend]
    tr = each(lambda x, y, d: tmul(x, y, masks) + d, bts, wides, diag)
    trt = each(lambda x, y, d: tmul(y, x, masks) + d, bts, wides, diag)
    inject = each(lambda x, y, z, u: tmul(stack(x, halves(y)), stack(z, u), masks), bts, kt, y0s, vs)
    wq = each(lambda x, y: stack(x, halves(y)), wides, qe)
    z = []
    out = []
    for c in range(STEP_CHUNKS):
        for g in range(2):
            i = c * 2 + g
            now = state_ref[g]
            nows = spread(halves(now), masks)
            state_ref[g] = mul(halves(tr[i]), nows) + inject[i]
            z.append(now)
            out.append(mul(wq[i], nows))
    o = each(lambda x, y: x[CHUNK:] + y, out, part)
    mixed = each(lambda x, y, z, m, n: read_out(x, y, z, m, n, ones)[3], o, q, k, v, vec)
    for i, u in enumerate(units):
        out_ref[u] = (mixed[i] * gate_ref[u]).astype(jnp.bfloat16)
        o_ref[u] = o[i]
        y_ref[u] = (out[i][:CHUNK] + y0[i]).astype(jnp.bfloat16)
        t_ref[u] = ts[i][0]
        aqb_ref[u] = aqb[i][0]
        aak_ref[u] = aak[i][0]
        aqk_ref[u] = aqk[i][0]
        z_ref[u] = z[i]
        trt_ref[u] = trt[i].astype(jnp.bfloat16)
        qe_ref[u] = qe[i].astype(jnp.bfloat16)


def backward_kernel(base, *refs):
    (
        len_ref, vec_ref, start_ref, sums_ref, q_ref, keys_ref, v_ref, dl_ref, rl_ref, gate_ref,
        g_ref, o_ref, t_ref, aqb_ref, aak_ref, aqk_ref, y_ref, z_ref, trt_ref, qe_ref,
    ) = refs[:20]
    dq_ref, dkeys_ref, dv_ref, ddl_ref, drl_ref, dgate_ref, dvec_ref, state_ref = refs[-8:]
    step = base + pl.num_programs(0) - 1 - pl.program_id(0)

    @pl.when(pl.program_id(0) == 0)
    def _():
        state_ref[...] = start_ref[...]
        dvec_ref[...] = sums_ref[...]

    masks = head_masks()
    row, col = places()
    strict = (col < row).astype(jnp.float32)
    within = (col <= row).astype(jnp.float32)
    ones = block_ones()
    units = unit_slices()
    live = unit_live(len_ref[0], step)
    vec = unit_vectors(vec_ref)
    load = lambda ref: [ref[u] for u in units]
    q, keys, v, g = load(q_ref), load(keys_ref), load(v_ref), load(g_ref)
    ready = each(
        lambda x, y, z, m, n: prepared(x, y, z, m, n, ones), keys, load(dl_ref), load(rl_ref), live, vec
    )
    w, k, a, b, sig, rates, inverse, factor = ([x[i] for x in ready] for i in range(8))
    seen = each(lambda x, y, z, m, n: read_out(x, y, z, m, n, ones), load(o_ref), q, k, v, vec)
    normed, scale, weight, mixed = ([x[i] for x in seen] for i in range(4))
    gate = load(gate_ref)
    dgate = each(lambda x, y: x * y, g, mixed)
    dmix = each(lambda x, y: x * y, g, gate)
    dn = each(lambda x, n: x * n[5], dmix, vec)
    do = each(
        lambda x, n, r: r
        * (x - head_sum(x, ones) * (1.0 / CHUNK) - n * (head_sum(x * n, ones) * (1.0 / CHUNK))),
        dn, normed, scale,
    )
    dweight = each(lambda x, y: head_sum(x * y, ones), dmix, v)
    do = [whole(x) for x in do]
    qe, trt, t, aqb, aak, aqk, ys = (
        [(x,) for x in load(ref)]
        for ref in (qe_ref, trt_ref, t_ref, aqb_ref, aak_ref, aqk_ref, y_ref)
    )
    z = load(z_ref)
    vs = [whole(x) for x in v]
    h = each(lambda x, y: tmul(x, y, masks), qe, do)
    dz = [None] * len(units)
    for c in reversed(range(STEP_CHUNKS)):
        for g in range(2):
            i = c * 2 + g
            now = state_ref[g]
            dz[i] = now
            state_ref[g] = mul(trt[i], spread(whole(now), masks)) + h[i]
    dzs = [spread(whole(x), masks) for x in dz]
    zs = [spread(whole(x), masks) for x in z]
    forms = each(scaled_forms, q, w, k, a, b)
    ah, qh, bh, kh, bt, kt = ([f[0][i] for f in forms] for i in range(6))
    ea, eq, eb, ee = ([f[1][i] for f in forms] for i in range(4))
    emid = [f[2][0] for f in forms]
    eend = [f[2][1] for f in forms]
    from_end = each(lambda x, y, s: mul(whole(jnp.concatenate([x, y], axis=0)), s), bt, kt, dzs)
    dy = each(lambda x, y, s: whole(tmul(x, y, masks) + s[:CHUNK]), aqb, do, from_end)
    dr = each(lambda x, y: whole(tmul(x, y, masks)), t, dy)
    ro = each(stack, dr, do)
    dv = each(lambda x, y, s, f: tmul(stack(x, y), s, masks) + f[CHUNK:], aak, aqk, ro, from_end)
    mask2 = jnp.concatenate([strict, within], axis=0)
    dab = each(lambda s, y: whole(mul(s, spread(y, masks), NT) * mask2), ro, ys)
    dak = each(lambda s, y: whole(mul(s, spread(y, masks), NT) * mask2), ro, vs)
    dst = each(lambda s, y: mul(s, y, NT), ro, zs)
    bhs, khs = [whole(x) for x in bh], [whole(x) for x in kh]
    inside = each(
        lambda x, bb, y, kk: mul(x, spread(bb, masks)) + mul(y, spread(kk, masks)), dab, bhs, dak, khs
    )
    outside = each(lambda s, e: s * e, dst, emid)
    daq = each(lambda x, y: x + y, inside, outside)
    aq = each(lambda x, y: whole(jnp.concatenate([x, y], axis=0)), ah, qh)
    dbh = each(lambda x, y: tmul(x, y, masks), dab, aq)
    dkh = each(lambda x, y: tmul(x, y, masks), dak, aq)
    dend = each(lambda y, x, s: mul(stack(y, x), s, NT), ys, vs, dzs)
    row_of_ones = jnp.ones((8, LANES), jnp.bfloat16)
    sums = lambda x: jnp.sum(x, axis=0, keepdims=True)
    for i, u in enumerate(units):
        da = daq[i][:CHUNK] * ea[i]
        dq = daq[i][CHUNK:] * eq[i]
        dbt = dend[i][:CHUNK] * ee[i]
        dkt = dend[i][CHUNK:] * ee[i]
        db = dbh[i] * eb[i] + dbt
        dk = dkh[i] * eb[i] + dkt
        paq = inside[i] * aq[i][0].astype(jnp.float32)
        pa = paq[:CHUNK] + outside[i][:CHUNK] * ah[i]
        diff = pa + paq[CHUNK:] + outside[i][CHUNK:] * qh[i]
        diff = diff - dbh[i] * bhs[i][0].astype(jnp.float32) - dkh[i] * khs[i][0].astype(jnp.float32)
        diff = diff - dbt * b[i] - dkt * k[i]
        zz = spread(halves(z[i] * dz[i]), masks)
        carry = (dot32(row_of_ones, zz[0], NT) + dot32(row_of_ones, zz[1], NT))[:1] * eend[i]
        carry = carry + sums(dbt * b[i] + dkt * k[i])
        dw = running_sum(diff, upper=True) - pa + carry
        from_bonus = dweight[i] * vec[i][4]
        dk = dk + from_bonus * q[i]
        dq_ref[u] = (dq + from_bonus * k[i]).astype(jnp.bfloat16)
        dv_ref[u] = (dv[i] + weight[i] * dmix[i]).astype(jnp.bfloat16)
        dgate_ref[u] = dgate[i].astype(jnp.bfloat16)
        unit_keys = -a[i]
        db = db * live[i]
        du = db * rates[i] - da
        dscaled = inverse[i] * (du - unit_keys * head_sum(du * unit_keys, ones))
        dkl = dk * keys[i] * live[i]
        drl = (db * unit_keys + dkl * vec[i][3]) * rates[i] * (1.0 - rates[i])
        ddl = dw * w[i] * (1.0 - sig[i])
        dkeys_ref[u] = (dk * factor[i] + dscaled * vec[i][2]).astype(jnp.bfloat16)
        ddl_ref[u] = ddl.astype(jnp.bfloat16)
        drl_ref[u] = drl.astype(jnp.bfloat16)
        parts = (
            ddl, drl, dscaled * keys[i], dkl * (rates[i] - 1.0),
            dweight[i] * q[i] * k[i], dmix[i] * normed[i], dmix[i],
        )
        lanes = u[1]
        for j, x in enumerate(parts):
            dvec_ref[j : j + 1, lanes] += sums(x)


def wkv_call(kernel, base, steps, small, arrays, outs, sums, previous, name):
    tokens, width = arrays[0].shape
    rows = CHUNK * STEP_CHUNKS
    last = base + steps - 1
    turned = kernel is backward_kernel
    spec = pl.BlockSpec((rows, width), lambda i: (last - i if turned else base + i, 0))
    state = pl.BlockSpec((2, CHUNK, LANES), lambda i: (0, 0, 0))
    whole = pl.BlockSpec((8, width), lambda i: (0, 0))
    shape = jax.ShapeDtypeStruct
    first = [pl.BlockSpec(memory_space=pltpu.SMEM), whole, state] + [whole] * sums
    held = list(previous or ())
    start = len(first) + len(arrays)
    return pl.pallas_call(
        partial(kernel, base),
        grid=(steps,),
        in_specs=first + [spec] * len(arrays) + [pl.BlockSpec(memory_space=pl.ANY)] * len(held),
        out_specs=[spec] * len(outs) + [whole] * sums + [state],
        out_shape=[shape((tokens, width), dtype) for dtype in outs]
        + [shape((8, width), jnp.float32)] * sums
        + [shape((2, CHUNK, LANES), jnp.float32)],
        input_output_aliases={start + i: i for i in range(len(held))},
        compiler_params=pltpu.CompilerParams(vmem_limit_bytes=60 << 20),
        cost_estimate=SMALL,
        name=name,
    )(*small, *arrays, *held)


def wkv_forward(base, steps, length, vec, state, arrays, previous=None):
    outs = [jnp.bfloat16, jnp.float32] + [jnp.bfloat16] * 5 + [jnp.float32] + [jnp.bfloat16] * 2
    return wkv_call(
        forward_kernel, base, steps, (length, vec, state), arrays, outs, 0, previous, "wkv_forward"
    )


def wkv_backward(base, steps, length, vec, state, sums, arrays, previous=None):
    outs = [jnp.bfloat16] * 6
    return wkv_call(
        backward_kernel, base, steps, (length, vec, state, sums), arrays, outs, 1, previous,
        "wkv_backward",
    )


ROWS = 128


def row_norm(x):
    centred = x - jnp.mean(x, axis=-1, keepdims=True)
    scale = lax.rsqrt(jnp.mean(centred * centred, axis=-1, keepdims=True) + 1e-05)
    return centred * scale, scale


def shifted(x, edge, down):
    rows = x.shape[0]
    row = lax.broadcasted_iota(jnp.int32, x.shape, 0)
    if down:
        return jnp.where(row == 0, edge, pltpu.roll(x, 1, 0))
    return jnp.where(row == rows - 1, edge, pltpu.roll(x, rows - 1, 0))


def below(x, upper):
    lane = lax.broadcasted_iota(jnp.int32, x.shape, 1)
    keep = (lane >= DECAY_RANK) if upper else (lane < DECAY_RANK)
    return jnp.where(keep, x, jnp.zeros_like(x))


def front_kernel(
    x_ref, vec_ref, wr_ref, wk_ref, wv_ref, down_ref, up_ref,
    m0_ref, m1_ref, m2_ref, m3_ref, m4_ref, m5_ref,
    q_ref, k_ref, v_ref, dl_ref, rl_ref, gate_ref, hid_ref,
    edge_ref,
):
    @pl.when(pl.program_id(0) == 0)
    def _():
        edge_ref[...] = jnp.zeros_like(edge_ref)

    unit, _ = row_norm(x_ref[...].astype(jnp.float32))
    normed = unit * vec_ref[12:13] + vec_ref[13:14]
    change = shifted(normed, edge_ref[:1], True) - normed
    edge_ref[:1] = normed[ROWS - 1 :]
    mixes = []
    for j, ref in enumerate((m0_ref, m1_ref, m2_ref, m3_ref, m4_ref, m5_ref)):
        mixes.append((normed + change * vec_ref[j : j + 1]).astype(jnp.bfloat16))
        ref[...] = mixes[j]
    q_ref[...] = dot32(mixes[0], wr_ref[...], NN)
    k_ref[...] = dot32(mixes[2], wk_ref[...], NN)
    v_ref[...] = dot32(mixes[3], wv_ref[...], NN)
    first = down_ref[:, :128]
    pre_decay, pre_rate = dot32(mixes[1], first, NN), dot32(mixes[4], first, NN)
    pre_gate = dot32(mixes[5], down_ref[:, 128:], NN)
    lane = lax.broadcasted_iota(jnp.int32, pre_decay.shape, 1)
    pair = jnp.where(lane < DECAY_RANK, jnp.tanh(pre_decay), pre_rate)
    gate = jax.nn.sigmoid(pre_gate)
    hid_ref[:, :128] = pair
    hid_ref[:, 128:] = gate
    narrow_pair = pair.astype(jnp.bfloat16)
    dl_ref[...] = dot32(below(narrow_pair, False), up_ref[:, :128], NT)
    rl_ref[...] = dot32(below(narrow_pair, True), up_ref[:, :128], NT)
    gate_ref[...] = dot32(gate.astype(jnp.bfloat16), up_ref[:, 128:], NT)


def front_forward(x, vectors, w_r, w_k, w_v, down, up):
    tokens, width = x.shape
    wide = pl.BlockSpec((ROWS, width), lambda i: (i, 0))
    own = pl.BlockSpec((ROWS, OWN), lambda i: (i, 0))
    hid = pl.BlockSpec((ROWS, 256), lambda i: (i, 0))
    whole = lambda a: pl.BlockSpec(a.shape, lambda i: (0, 0))
    shape = jax.ShapeDtypeStruct
    return pl.pallas_call(
        front_kernel,
        grid=(tokens // ROWS,),
        in_specs=[wide] + [whole(a) for a in (vectors, w_r, w_k, w_v, down, up)],
        out_specs=[wide] * 6 + [own] * 6 + [hid],
        out_shape=[shape((tokens, width), jnp.bfloat16)] * 6
        + [shape((tokens, OWN), jnp.float32)] * 6
        + [shape((tokens, 256), jnp.float32)],
        scratch_shapes=[pltpu.VMEM((8, width), jnp.float32)],
        compiler_params=pltpu.CompilerParams(vmem_limit_bytes=60 << 20),
        cost_estimate=SMALL,
        name="front_forward",
    )(x, vectors, w_r, w_k, w_v, down, up)


def front_back_kernel(
    x_ref, before_ref, vec_ref, wr_ref, wk_ref, wv_ref, down_ref, up_ref,
    m1_ref, m4_ref, m5_ref, hid_ref,
    dq_ref, dk_ref, dv_ref, ddl_ref, drl_ref, dgate_ref, own_vec_ref, ffn_vec_ref,
    dx_ref, mine_ref, other_ref,
    edge_ref, sums_ref, misc_ref,
):
    step = pl.num_programs(0) - 1 - pl.program_id(0)
    core = lax.axis_index("dp") % 2
    own_start = pl.multiple_of(core * OWN, OWN)

    @pl.when(pl.program_id(0) == 0)
    def _():
        edge_ref[...] = jnp.zeros_like(edge_ref)
        sums_ref[...] = jnp.zeros_like(sums_ref)
        misc_ref[...] = jnp.zeros_like(misc_ref)

    unit, scale = row_norm(x_ref[...].astype(jnp.float32))
    gain, offset = vec_ref[12:13], vec_ref[13:14]
    normed = unit * gain + offset
    tail, _ = row_norm(before_ref[...].astype(jnp.float32))
    edge = (tail[15:] * gain + offset) * jnp.where(step == 0, 0.0, 1.0)
    change = shifted(normed, edge, True) - normed
    ddl, drl, dgate = ddl_ref[...], drl_ref[...], dgate_ref[...]
    hid = hid_ref[...]
    pair, gate = hid[:, :128], hid[:, 128:]
    lane = lax.broadcasted_iota(jnp.int32, pair.shape, 1)
    first_up, last_up = up_ref[:, :128], up_ref[:, 128:]
    pair_grad = jnp.where(
        lane < DECAY_RANK,
        dot32(ddl, first_up, NN) * (1.0 - pair * pair),
        dot32(drl, first_up, NN),
    ).astype(jnp.bfloat16)
    gate_grad = (dot32(dgate, last_up, NN) * gate * (1.0 - gate)).astype(jnp.bfloat16)
    narrow_pair, narrow_gate = pair.astype(jnp.bfloat16), gate.astype(jnp.bfloat16)
    own_rows = pl.ds(own_start, OWN)
    misc_ref[own_rows, 256:384] += dot32(ddl, below(narrow_pair, False), TN) + dot32(
        drl, below(narrow_pair, True), TN
    )
    misc_ref[own_rows, 384:512] += dot32(dgate, narrow_gate, TN)
    decay_part, rate_part = below(pair_grad, False), below(pair_grad, True)
    misc_ref[:, :128] += dot32(m1_ref[...], decay_part, TN) + dot32(m4_ref[...], rate_part, TN)
    misc_ref[:, 128:256] += dot32(m5_ref[...], gate_grad, TN)
    first_down = down_ref[:, :128]
    grads = (
        lambda: dot32(dq_ref[...], wr_ref[...], NT),
        lambda: dot32(decay_part, first_down, NT),
        lambda: dot32(dk_ref[...], wk_ref[...], NT),
        lambda: dot32(dv_ref[...], wv_ref[...], NT),
        lambda: dot32(rate_part, first_down, NT),
        lambda: dot32(gate_grad, down_ref[:, 128:], NT),
    )
    total = jnp.zeros_like(change)
    moved = jnp.zeros_like(change)
    for j, grad in enumerate(grads):
        now = grad()
        total = total + now
        moved = moved + now * vec_ref[j : j + 1]
        sums_ref[j : j + 1] += jnp.sum(now * change, axis=0, keepdims=True)
    dnormed = total - moved + shifted(moved, edge_ref[:1], False)
    edge_ref[:1] = moved[:1]
    sums_ref[12:13] += jnp.sum(dnormed * unit, axis=0, keepdims=True)
    sums_ref[13:14] += jnp.sum(dnormed, axis=0, keepdims=True)
    dunit = dnormed * gain
    dx_ref[...] = scale * (
        dunit
        - jnp.mean(dunit, axis=-1, keepdims=True)
        - unit * jnp.mean(dunit * unit, axis=-1, keepdims=True)
    )

    @pl.when(step == 0)
    def _():
        sums_ref[6:7] = ffn_vec_ref[0:1] * 0.5
        sums_ref[14:16] = ffn_vec_ref[1:3] * 0.5
        zeros = jnp.zeros((1, OWN), jnp.float32)
        for target, source in ((7, 0), (8, 1), (9, 2), (10, 3), (11, 4), (16, 5), (17, 6)):
            mine = own_vec_ref[source : source + 1]
            sums_ref[target : target + 1] = jnp.concatenate(
                [jnp.where(core == 0, mine, zeros), jnp.where(core == 0, zeros, mine)], axis=1
            )
        for block in range(EMBED // 128):
            lanes = slice(block * 128, (block + 1) * 128)
            misc_ref[lanes, 512:640] = sums_ref[:, lanes].T
        share = mine_ref.shape[1]
        for chip in range(mine_ref.shape[0]):
            low = misc_ref[2 * chip * share : (2 * chip + 1) * share]
            high = misc_ref[(2 * chip + 1) * share : (2 * chip + 2) * share]
            mine_ref[chip] = jnp.where(core == 0, low, high)
            other_ref[chip] = jnp.where(core == 0, high, low).astype(jnp.bfloat16)


def front_backward(
    x, vectors, w_r, w_k, w_v, down, up, mixes, hid, grads, own_vec, ffn_vec
):
    tokens, width = x.shape
    devices = lax.axis_size("dp")
    pieces = (devices // 2, EMBED // devices, 640)
    steps = tokens // ROWS
    wide = pl.BlockSpec((ROWS, width), lambda i: (steps - 1 - i, 0))
    before = pl.BlockSpec(
        (16, width), lambda i: (jnp.maximum((steps - 1 - i) * (ROWS // 16) - 1, 0), 0)
    )
    own = pl.BlockSpec((ROWS, OWN), lambda i: (steps - 1 - i, 0))
    hid_spec = pl.BlockSpec((ROWS, 256), lambda i: (steps - 1 - i, 0))
    whole = lambda a: pl.BlockSpec(a.shape, lambda i: (0, 0))
    shape = jax.ShapeDtypeStruct
    return pl.pallas_call(
        front_back_kernel,
        grid=(steps,),
        in_specs=[wide, before]
        + [whole(a) for a in (vectors, w_r, w_k, w_v, down, up)]
        + [wide] * 3
        + [hid_spec]
        + [own] * 6
        + [whole(own_vec), whole(ffn_vec)],
        out_specs=[wide] + [pl.BlockSpec(pieces, lambda i: (0, 0, 0))] * 2,
        out_shape=[
            shape((tokens, width), jnp.float32),
            shape(pieces, jnp.float32),
            shape(pieces, jnp.bfloat16),
        ],
        scratch_shapes=[
            pltpu.VMEM((8, width), jnp.float32),
            pltpu.VMEM((128, width), jnp.float32),
            pltpu.VMEM((EMBED, 640), jnp.float32),
        ],
        compiler_params=pltpu.CompilerParams(vmem_limit_bytes=60 << 20),
        cost_estimate=SMALL,
        name="front_backward",
    )(x, x, vectors, w_r, w_k, w_v, down, up, *mixes, hid, *grads, own_vec, ffn_vec)


def ffn_back_kernel(
    len_ref, res_ref, before_ref, cot_ref, mine_ref, other_ref, vec_ref, wo_ref,
    grad_ref, narrow_ref, gated_ref, dvec_ref,
    edge_ref,
):
    step = pl.num_programs(0) - 1 - pl.program_id(0)

    @pl.when(pl.program_id(0) == 0)
    def _():
        edge_ref[...] = jnp.zeros_like(edge_ref)
        dvec_ref[...] = jnp.zeros_like(dvec_ref)

    gain, offset, coefficient = vec_ref[14:15], vec_ref[15:16], vec_ref[6:7]
    unit, scale = row_norm(res_ref[...])
    normed = unit * gain + offset
    tail, _ = row_norm(before_ref[...])
    edge = (tail[7:] * gain + offset) * jnp.where(step == 0, 0.0, 1.0)
    change = shifted(normed, edge, True) - normed
    grad = mine_ref[...].astype(jnp.float32) + other_ref[...].astype(jnp.float32)
    moved = grad * coefficient
    dnormed = grad - moved + shifted(moved, edge_ref[:1], False)
    edge_ref[:1] = moved[:1]
    sums = lambda x: jnp.sum(x, axis=0, keepdims=True)
    dvec_ref[0:1] += sums(grad * change)
    dvec_ref[1:2] += sums(dnormed * unit)
    dvec_ref[2:3] += sums(dnormed)
    dunit = dnormed * gain
    row = lax.broadcasted_iota(jnp.int32, grad.shape, 0) + step * ROWS
    out_grad = jnp.where(row < len_ref[0], cot_ref[...].astype(jnp.float32), 0.0)
    total = out_grad + scale * (
        dunit
        - jnp.mean(dunit, axis=-1, keepdims=True)
        - unit * jnp.mean(dunit * unit, axis=-1, keepdims=True)
    )
    grad_ref[...] = total
    small = total.astype(jnp.bfloat16)
    core = lax.axis_index("dp") % 2
    narrow_ref[...] = jnp.where(core == 0, small[:, :OWN], small[:, OWN:])
    gated_ref[...] = dot32(small, wo_ref[...], NT)


def ffn_backward(length, residual, cot, mine, other, vectors, w_o_rows):
    tokens, width = residual.shape
    steps = tokens // ROWS
    wide = pl.BlockSpec((ROWS, width), lambda i: (steps - 1 - i, 0))
    before = pl.BlockSpec(
        (8, width), lambda i: (jnp.maximum((steps - 1 - i) * (ROWS // 8) - 1, 0), 0)
    )
    own = pl.BlockSpec((ROWS, OWN), lambda i: (steps - 1 - i, 0))
    whole = lambda a: pl.BlockSpec(a.shape, lambda i: (0, 0))
    shape = jax.ShapeDtypeStruct
    return pl.pallas_call(
        ffn_back_kernel,
        grid=(steps,),
        in_specs=[pl.BlockSpec(memory_space=pltpu.SMEM), wide, before]
        + [wide] * 3
        + [whole(vectors), whole(w_o_rows)],
        out_specs=[wide, own, own, pl.BlockSpec((8, width), lambda i: (0, 0))],
        out_shape=[
            shape((tokens, width), jnp.float32),
            shape((tokens, OWN), jnp.bfloat16),
            shape((tokens, OWN), jnp.float32),
            shape((8, width), jnp.float32),
        ],
        scratch_shapes=[pltpu.VMEM((8, width), jnp.float32)],
        compiler_params=pltpu.CompilerParams(vmem_limit_bytes=60 << 20),
        cost_estimate=SMALL,
        name="ffn_backward",
    )(length, residual, residual, cot, mine, other, vectors, w_o_rows)


def att_grad_kernel(m0_ref, m2_ref, m3_ref, gated_ref, dq_ref, dk_ref, dv_ref, do_ref,
                    send_a, keep_a, send_b, keep_b):
    chip = lax.axis_index("dp") // 2
    by_x, by_y = chip % 2 == 0, (chip // 2) % 2 == 0
    first = ((m0_ref, dq_ref), (gated_ref, do_ref))
    second = ((m2_ref, dk_ref), (m3_ref, dv_ref))
    for half in range(2):
        lanes = slice(half * OWN, (half + 1) * OWN)
        block = dot32(first[half][0][...], first[half][1][...], TN).astype(jnp.bfloat16)
        for y in range(2):
            low, high = block[y * 128 : y * 128 + 64], block[y * 128 + 64 : y * 128 + 128]
            send_a[y, :, lanes] = jnp.where(by_x, high, low)
            keep_a[y, :, lanes] = jnp.where(by_x, low, high)
        block = dot32(second[half][0][...], second[half][1][...], TN).astype(jnp.bfloat16)
        for x in range(2):
            low, high = block[x * 64 : x * 64 + 64], block[128 + x * 64 : 128 + x * 64 + 64]
            send_b[x, :, lanes] = jnp.where(by_y, high, low)
            keep_b[x, :, lanes] = jnp.where(by_y, low, high)


def att_gradients(mixes, gated, grads, own_grad):
    tokens = gated.shape[0]
    left = pl.BlockSpec((tokens, 256), lambda i: (0, i))
    right = pl.BlockSpec((tokens, OWN), lambda i: (0, 0))
    out = pl.BlockSpec((2, 64, 2 * OWN), lambda i: (i, 0, 0))
    return pl.pallas_call(
        att_grad_kernel,
        grid=(4,),
        in_specs=[left] * 4 + [right] * 4,
        out_specs=[out] * 4,
        out_shape=[jax.ShapeDtypeStruct((8, 64, 2 * OWN), jnp.bfloat16)] * 4,
        compiler_params=pltpu.CompilerParams(vmem_limit_bytes=60 << 20),
        cost_estimate=SMALL,
        name="att_gradients",
    )(*mixes, gated, *grads, own_grad)


def swap(block, mask):
    size = lax.axis_size("dp")
    return lax.ppermute(block, "dp", [(i, i ^ mask) for i in range(size)])


def bit_of(mask):
    return (lax.axis_index("dp") // mask) % 2


def in_order(mask, own, other, axis):
    lower = bit_of(mask) == 0
    return jnp.where(
        lower, jnp.concatenate([own, other], axis=axis), jnp.concatenate([other, own], axis=axis)
    )


def chip_masks():
    size = lax.axis_size("dp")
    masks = []
    while 2 << len(masks) < size:
        masks.append(2 << len(masks))
    return masks


def steps_of(kind):
    masks = chip_masks()
    near, far = [[mask] for mask in masks[:2]], [[mask] for mask in masks[2:][::-1]]
    first = [[far[0][0], far[1][0], far[0][0] | far[1][0]]] if len(far) == 2 else far
    return [first + near[::-1], first + near, far + near[::-1], far + near, near + far][kind]


class Held:
    def __init__(self, value):
        self.value = value


def meet(movers, *arrays):
    held = []
    for mover in movers:
        held += [x[0] for x in mover.arrived if x[0] not in held]
    out = lax.optimization_barrier(tuple(x.value for x in held) + arrays)
    for x, value in zip(held, out):
        x.value = value
    return out[len(held) :]


def read(arrived):
    return [x.value if lanes is None else x.value[..., lanes] for x, lanes in arrived]


class Gather:
    def __init__(self, block, kind, places=(0,)):
        self.steps = steps_of(kind)
        self.held = block[None]
        self.places = [0]
        self.arrived = []
        self.masks = []

    def merge(self):
        if self.arrived:
            self.held = jnp.concatenate([self.held] + read(self.arrived), axis=0)
            self.places = self.places + [p ^ (m // 2) for m in self.masks for p in self.places]
            self.arrived = []

    def step(self):
        if self.steps:
            self.merge()
            self.masks = self.steps.pop(0)
            self.arrived = [(Held(swap(self.held, mask)), None) for mask in self.masks]
        return self

    def run(self):
        while self.steps:
            self.step()
        return self

    def split(self, kinds):
        width = self.held.shape[-1] // len(kinds)
        out = []
        for i, kind in enumerate(kinds):
            part = Gather.__new__(Gather)
            cut = slice(i * width, (i + 1) * width)
            part.steps = steps_of(kind)[len(steps_of(kind)) - len(self.steps) :]
            part.held = self.held[..., cut]
            part.arrived = [(x, cut) for x, _ in self.arrived]
            part.places, part.masks = self.places, self.masks
            out.append(part)
        return out


def place_kernel(places, cuts, *refs):
    sources, outs = refs[: len(places)], refs[len(places) :]
    chip = lax.axis_index("dp") // 2
    for source, (part, list_of) in zip(sources, places):
        for j, place in enumerate(list_of):
            for out, (first, rows, lanes) in zip(outs, cuts):
                start = pl.multiple_of((chip ^ place) * rows, rows)
                lane, width = lanes[part]
                at = sum(w for _, w in lanes[:part])
                out[pl.ds(start, rows), at : at + width] = source[
                    j, first : first + rows, lane : lane + width
                ]


def assemble(gathers, cuts=None):
    gathers = [g.run() for g in gathers]
    rows = gathers[0].held.shape[1]
    cuts = cuts or ((0, rows, [(0, g.held.shape[2]) for g in gathers]),)
    sources, places = [], []
    for i, g in enumerate(gathers):
        sources += [g.held] + read(g.arrived)
        shifts = [0] + [mask // 2 for mask in g.masks]
        places += [(i, [p ^ shift for p in g.places]) for shift in shifts]
    count = lax.axis_size("dp") // 2
    if any(cut[1] % 16 for cut in cuts):
        return assemble_plain(sources, places, cuts, count)
    space = pl.BlockSpec(memory_space=pltpu.VMEM)
    return pl.pallas_call(
        partial(place_kernel, places, cuts),
        in_specs=[space] * len(sources),
        out_specs=[space] * len(cuts),
        out_shape=[
            jax.ShapeDtypeStruct((count * n, sum(w for _, w in lanes)), sources[0].dtype)
            for _, n, lanes in cuts
        ],
        compiler_params=pltpu.CompilerParams(vmem_limit_bytes=32 << 20),
        cost_estimate=SMALL,
        name="assemble",
    )(*sources)


def assemble_plain(sources, places, cuts, count):
    chip = lax.axis_index("dp") // 2
    parts = []
    for part in sorted({part for part, _ in places}):
        blocks = jnp.concatenate([x for x, (at, _) in zip(sources, places) if at == part])
        where = [p for at, list_of in places if at == part for p in list_of]
        blocks = jnp.stack([blocks[where.index(i)] for i in range(count)])
        parts.append(jnp.take(blocks, chip ^ lax.iota(jnp.int32, count), axis=0))
    return [
        jnp.concatenate(
            [x[:, first : first + n, at : at + w] for x, (at, w) in zip(parts, lanes)], axis=-1
        ).reshape(count * n, -1)
        for first, n, lanes in cuts
    ]


class Scatter:
    def __init__(self, parts, kind):
        self.steps = steps_of(kind)[::-1]
        self.axes = chip_masks()[::-1]
        self.sources = [parts.reshape((2,) * len(self.axes) + parts.shape[1:])]
        self.arrived = []
        self.sent = None

    @classmethod
    def begun(cls, sent, kept, kind):
        out = cls.__new__(cls)
        out.steps = steps_of(kind)[::-1]
        out.axes = [axis for axis in chip_masks()[::-1] if axis != out.steps[0][0]]
        out.sources = [kept.reshape((2,) * len(out.axes) + kept.shape[1:])]
        out.arrived = []
        out.sent = [sent.reshape(out.sources[0].shape)]
        return out

    def pick(self, sources, mask, gone):
        out = []
        for x in sources:
            for place in reversed(range(len(self.axes))):
                axis = self.axes[place]
                if axis in gone:
                    which = bit_of(axis) if not mask & axis else 1 - bit_of(axis)
                    x = lax.dynamic_index_in_dim(x, which, place, keepdims=False)
            out.append(x)
        return out

    def prepare(self):
        if self.sent is not None:
            return self
        masks = self.steps[0]
        sources = self.sources + read(self.arrived)
        gone = [axis for axis in self.axes if any(mask & axis for mask in masks)]
        self.sent = [
            sum(x.astype(jnp.float32) for x in self.pick(sources, mask, gone)).astype(jnp.bfloat16)
            for mask in masks
        ]
        self.sources = self.pick(sources, 0, gone)
        self.axes = [axis for axis in self.axes if axis not in gone]
        self.arrived = []
        return self

    def step(self):
        return together([self])[0]

    def run(self):
        while self.steps:
            self.step()
        return self

    def total(self):
        return sum(x.astype(jnp.float32) for x in self.sources + read(self.arrived))


def together(parts):
    if not parts[0].steps:
        return parts
    for part in parts:
        part.prepare()
    for i, mask in enumerate(parts[0].steps[0]):
        sent = [part.sent[i] for part in parts]
        got = Held(swap(sent[0] if len(sent) == 1 else jnp.concatenate(sent, axis=-1), mask))
        at = 0
        for part, x in zip(parts, sent):
            lanes = slice(at, at + x.shape[-1]) if len(sent) > 1 else None
            part.arrived.append((got, lanes))
            at += x.shape[-1]
    for part in parts:
        part.steps.pop(0)
        part.sent_now, part.sent = part.sent[0], None
    return parts


def norm_rows(features, gain_row, offset_row):
    average = jnp.mean(features, axis=-1, keepdims=True)
    centred = features - average
    variance = jnp.mean(centred * centred, axis=-1, keepdims=True)
    return centred * lax.rsqrt(variance + 1e-05) * gain_row + offset_row


def product(operand, weight_matrix):
    return jnp.dot(operand, weight_matrix, preferred_element_type=jnp.float32)


def input_gradient_rows(upstream_gradient, weight_matrix):
    return lax.dot_general(
        upstream_gradient,
        weight_matrix,
        (((1,), (1,)), ((), ())),
        preferred_element_type=jnp.float32,
    )


def weight_gradient(operand, upstream_gradient):
    return lax.dot_general(
        operand, upstream_gradient, (((0,), (0,)), ((), ())), preferred_element_type=jnp.float32
    )


def earlier(rows):
    return jnp.concatenate([jnp.zeros_like(rows[:1]), rows[:-1]], axis=0)


def ffn_mix(residual, vectors):
    second = norm_rows(residual, vectors[14], vectors[15])
    return second + (earlier(second) - second) * vectors[6]


def narrow(x):
    return x.astype(jnp.bfloat16)


def local(
    inputs,
    lengths,
    attention_projections,
    channel_key_weight,
    channel_value_weight,
    lowrank_down_weight,
    lowrank_up_weight,
    per_feature_parameters,
    cotangent,
):
    devices = lax.axis_size("dp")
    chips = devices // 2
    device = lax.axis_index("dp")
    chip, core = device // 2, device % 2
    row_count = inputs.shape[0]
    slots = 2 * row_count
    share = EMBED // devices
    pair_share = 2 * share
    units = channel_value_weight.shape[0]
    half_units = chips * units

    def own_cut(x, which):
        return lax.dynamic_slice_in_dim(x, which * OWN, OWN, x.ndim - 1)

    def own_rows(x, which):
        return lax.dynamic_slice_in_dim(x, which * row_count, row_count, 0)

    pair_rows = in_order(
        1,
        own_cut(attention_projections, core),
        swap(own_cut(attention_projections, 1 - core), 1),
        1,
    )
    lora = jnp.concatenate([lowrank_down_weight, lowrank_up_weight.T], axis=1)
    vector_rows = jnp.pad(per_feature_parameters.T, ((0, 0), (0, 128 - 18)))
    vector_rows = vector_rows.reshape(share // 4, OWN)
    first_rows = 3 * pair_share
    misc_rows = share + share // 4 + (share // 4) % 16
    block = jnp.concatenate(
        [
            pair_rows[:3].reshape(first_rows, OWN),
            lora,
            jnp.pad(vector_rows, ((0, (share // 4) % 16), (0, 0))),
        ],
        axis=0,
    )
    half = half_units // 2
    quarter = OWN // 2
    first = Gather(block, 0).step()
    w_o_part = Gather(pair_rows[3], 4).step().step()
    key_in, raw, cot, _ = meet([], channel_key_weight, inputs, cotangent, first.held)
    key_cut = key_in.reshape(share, chips, 2, units)

    def key_columns(which):
        return lax.dynamic_index_in_dim(key_cut, which, 2, keepdims=False).reshape(share, half_units)

    key_rows = in_order(1, key_columns(core), swap(key_columns(1 - core), 1), 0)
    tokens = in_order(1, raw, swap(raw, 1), 0)
    cot = in_order(1, cot, swap(cot, 1), 0)
    key_rows, tokens, cot = meet([first, w_o_part], key_rows, tokens, cot)
    first = first.split((0, 1))
    for part in first:
        part.step()
    key_part = Gather(key_rows, 2).step()
    (tokens,) = meet(first, tokens)
    for part in first:
        part.step()
    value_block, *_ = meet([key_part], channel_value_weight, *[part.held for part in first])
    key_part.step()
    value_part = Gather(value_block, 2).step()
    w_o_part.step()
    (tokens,) = meet(first + [key_part, value_part], tokens)
    key_parts = key_part.split((2, 3))
    for part in key_parts:
        part.step()
    w_r, w_k, w_v, misc = assemble(
        first,
        [(i * pair_share, pair_share, [(0, quarter)] * 2) for i in range(3)]
        + [(first_rows, misc_rows, [(0, quarter)] * 2)],
    )
    misc = misc.reshape(chips, 1, misc_rows, OWN)
    misc = in_order(1, misc, swap(misc, 1), 1)
    value_part.step()
    lora = misc[:, :, :share].reshape(EMBED, OWN)
    down, up_t = lora[:, :256], lax.dynamic_slice_in_dim(lora[:, 256:], core * OWN, OWN, 0)
    vectors = misc[:, :, share : share + share // 4].reshape(EMBED, 128)[:, :18].T
    vectors = vectors.astype(jnp.float32)
    own_vectors = own_cut(vectors, core)
    used = jnp.concatenate([own_vectors[7:12], own_vectors[16:18], own_vectors[:1]], axis=0)
    length = lax.dynamic_index_in_dim(lengths, chip, 0)
    live = (lax.iota(jnp.int32, slots) < length)[:, None]

    *mixes, queries, keys, values, decay_low, rate_low, gate_rows, hid = front_forward(
        tokens, vectors, w_r, w_k, w_v, down, up_t
    )
    terms = meet(
        key_parts + [value_part, w_o_part],
        queries, keys, values, decay_low, rate_low, gate_rows,
    )
    value_parts = value_part.split((2, 3))
    for part in key_parts + value_parts:
        part.step()
    w_o_part.step()
    blocks = slots // (CHUNK * STEP_CHUNKS)
    zero_state = jnp.zeros((2, CHUNK, LANES), jnp.float32)
    gated, *saved, _ = wkv_forward(0, blocks, length, used, zero_state, terms)
    gated, cot, tokens = meet(key_parts + value_parts, gated, cot, tokens)
    for part in value_parts:
        part.step()
    gated, *_ = meet([w_o_part] + key_parts, gated, *[part.held for part in value_parts])
    gated_all = in_order(1, gated, swap(gated, 1), 1)
    (w_o_own,) = assemble([w_o_part])
    w_o = in_order(1, w_o_own, swap(w_o_own, 1), 1)
    (key_weight,) = assemble(key_parts)
    residual = tokens.astype(jnp.float32) + product(gated_all, w_o)
    ffn_in = narrow(ffn_mix(residual, vectors))
    positive = jax.nn.relu(product(ffn_in, key_weight))
    hidden = narrow(jnp.square(positive))
    out_narrow = jnp.where(live, cot, jnp.zeros_like(cot))
    grad_value = narrow(weight_gradient(hidden, out_narrow)).reshape(chips, units, EMBED)
    w_o_rows = lax.dynamic_slice_in_dim(w_o, core * OWN, OWN, 0)
    value_scatter = [
        Scatter(grad_value[..., i * OWN : (i + 1) * OWN], 2 + i).prepare() for i in range(2)
    ]
    hidden, positive, out_narrow, w_o_rows, *sent = meet(
        value_parts, hidden, positive, out_narrow, w_o_rows, *[m.sent[0] for m in value_scatter]
    )
    for part, x in zip(value_scatter, sent):
        part.sent = [x]
        part.step()
    (value_weight,) = assemble(value_parts)

    pre_narrow = narrow(2.0 * positive * input_gradient_rows(out_narrow, value_weight))
    ffn_in_grad = narrow(input_gradient_rows(pre_narrow, key_weight))
    other_grad = swap(ffn_in_grad, 1)
    grad_key = narrow(weight_gradient(ffn_in, pre_narrow)).reshape(chips, pair_share, half_units)
    residual_grad, own_grad, gated_grad, ffn_vec = ffn_backward(
        length, residual, cot, ffn_in_grad, other_grad, vectors, w_o_rows
    )
    key_scatter = [
        Scatter(grad_key[:, :, i * half : (i + 1) * half], 2 + i).prepare() for i in range(2)
    ]
    gated_grad, *sent = meet([], gated_grad, *[m.sent[0] for m in key_scatter])
    for part, x in zip(key_scatter, sent):
        part.sent = [x]
        part.step()
    terms = [*terms, gated_grad, *saved]
    zero_sums = jnp.zeros((8, OWN), jnp.float32)
    early = blocks // 2
    *before, sums, state = wkv_backward(
        early, blocks - early, length, used, zero_state, zero_sums, terms
    )
    state, sums = meet(value_scatter, state, sums)
    for part in value_scatter:
        part.step()
    *low_grads, own_vec, _ = wkv_backward(0, early, length, used, state, sums, terms, before)
    if pair_share == 64:
        sent_a, kept_a, sent_b, kept_b = att_gradients(
            (mixes[0], mixes[2], mixes[3]), gated_all, low_grads[:3], own_grad
        )
        att_scatter = [Scatter.begun(sent_a, kept_a, 2), Scatter.begun(sent_b, kept_b, 3)]
    else:
        grads = [weight_gradient(mixes[m], g) for m, g in zip((0, 2, 3), low_grads)]
        grad_o = weight_gradient(gated_all, own_grad)
        att_scatter = [
            Scatter(
                narrow(jnp.concatenate(x, axis=1)).reshape(chips, pair_share, EMBED), 2 + i
            ).prepare()
            for i, x in enumerate(((grads[0], grad_o), (grads[1], grads[2])))
        ]
    own_vec, *sent = meet(
        key_scatter + value_scatter, own_vec, *[m.sent[0] for m in att_scatter]
    )
    for part, x in zip(att_scatter, sent):
        part.sent = [x]
        part.step()
    for part in key_scatter:
        part.step()
    together(value_scatter)
    own_vec, *_ = meet([], own_vec, *[m.sent_now for m in key_scatter])
    token_part, misc_mine, misc_other = front_backward(
        tokens, vectors, w_r, w_k, w_v, down, up_t, (mixes[1], mixes[4], mixes[5]), hid,
        low_grads, own_vec, ffn_vec,
    )
    misc_other = swap(misc_other, 1)
    token_part, misc_mine, misc_other = meet(
        att_scatter + key_scatter + value_scatter, token_part, misc_mine, misc_other
    )
    for part in att_scatter:
        part.step()
    misc_sum = misc_mine + misc_other.astype(jnp.float32)
    misc_sum = jnp.concatenate([misc_sum[..., :320], misc_sum[..., 320:]], axis=1)
    misc_scatter = Scatter(misc_sum, 3).step()
    together(key_scatter)
    together(value_scatter)
    token_part, hidden = meet(
        att_scatter + key_scatter + value_scatter + [misc_scatter], token_part, hidden
    )
    misc_scatter.step()
    together(key_scatter)
    (token_part,) = meet([misc_scatter], token_part)
    masks = chip_masks()
    last_parts = att_scatter + [misc_scatter]
    if len(misc_scatter.steps) == 2:
        for part in last_parts:
            part.steps = [[masks[2], masks[3], masks[2] | masks[3]]]
    together(last_parts)
    ffn_part = product(hidden, value_weight)
    input_gradient = (
        own_rows(residual_grad, core)
        + own_rows(token_part, core)
        + swap(own_rows(token_part, 1 - core), 1)
    )
    ffn_out = own_rows(ffn_part, core) + swap(own_rows(ffn_part, 1 - core), 1)
    output = narrow(jnp.where(own_rows(live, core), own_rows(residual, core) + ffn_out, 0.0))
    value_sum = jnp.concatenate(
        [x.run().total() for x in value_scatter], axis=1
    )
    while key_scatter[0].steps:
        together(key_scatter)
    key_sum = jnp.concatenate([x.total() for x in key_scatter], axis=1).reshape(2, share, -1)

    def exchange(x):
        mine = lax.dynamic_index_in_dim(x, core, 0, keepdims=False)
        return mine, swap(lax.dynamic_index_in_dim(x, 1 - core, 0, keepdims=False), 1)

    key_mine, key_theirs = exchange(key_sum)
    input_gradient, value_sum, key_mine, key_theirs = meet(
        last_parts, input_gradient, value_sum, key_mine, key_theirs
    )
    while last_parts[0].steps:
        together(last_parts)
    first_sum, second_sum, misc_sum = [x.total() for x in last_parts]
    misc_sum = jnp.concatenate([misc_sum[:share], misc_sum[share:]], axis=1)
    att_sum = jnp.concatenate(
        [first_sum[:, :OWN], second_sum, first_sum[:, OWN:]], axis=1
    )
    mine, theirs = exchange(att_sum.reshape(2, share, -1))
    shard_mixer = jnp.stack(
        [
            in_order(1, mine[:, i * OWN : (i + 1) * OWN], theirs[:, i * OWN : (i + 1) * OWN], 1)
            for i in range(4)
        ]
    )
    shard_key = in_order(
        1,
        key_mine.reshape(share, chips, 1, units),
        key_theirs.reshape(share, chips, 1, units),
        2,
    ).reshape(share, 2 * half_units)
    return (
        output,
        input_gradient,
        shard_mixer,
        shard_key,
        value_sum,
        misc_sum[:, :256],
        misc_sum[:, 256:512].T,
        misc_sum[:, 512:530].T,
    )


def solution(mesh):
    in_specs = (
        P("dp", None),
        P(),
        P(None, "dp", None),
        P("dp", None),
        P("dp", None),
        P("dp", None),
        P(None, "dp"),
        P(None, "dp"),
        P("dp", None),
    )
    out_specs = (
        P("dp", None),
        P("dp", None),
        P(None, "dp", None),
        P("dp", None),
        P("dp", None),
        P("dp", None),
        P(None, "dp"),
        P(None, "dp"),
    )
    return jax.shard_map(local, mesh=mesh, in_specs=in_specs, out_specs=out_specs, check_vma=False)
```

```python
from functools import partial

import jax
import jax.numpy as jnp
from jax import lax
from jax.experimental import pallas as pl
from jax.experimental.pallas import tpu as pltpu
from jax.sharding import PartitionSpec as P

HEADS = 16
HEAD_SIZE = 64
DECAY_RANK = 64
RATE_RANK = 64
EMBED = 1024
OWN = EMBED // 2
PRECISE = lax.Precision.HIGHEST


CHUNK = 64
LANES = 256
GROUP_HEADS = 4
STEP_CHUNKS = 2
SMALL = pl.CostEstimate(flops=1, bytes_accessed=1, transcendentals=0)

NN = (((1,), (0,)), ((), ()))
NT = (((1,), (1,)), ((), ()))
TN = (((0,), (0,)), ((), ()))


def halves(x):
    high = x.astype(jnp.bfloat16)
    return high, (x - high.astype(jnp.float32)).astype(jnp.bfloat16)


def whole(x):
    return (x.astype(jnp.bfloat16),)


def dot32(a, b, dims):
    return lax.dot_general(a, b, dims, preferred_element_type=jnp.float32)


def mul(left, right, dims=NN):
    if len(left) == 1 or len(right) == 1:
        return dot32(left[0], right[0], dims)
    rows = left[0].shape[0]
    both = dot32(jnp.concatenate(left, axis=0), right[0], dims)
    return both[:rows] + both[rows:] + dot32(left[0], right[1], dims)


def tmul(left, right, masks):
    full = dot32(left[0], right[0], TN)
    if len(left) > 1 and len(right) > 1:
        full = full + dot32(left[1], right[0], TN) + dot32(left[0], right[1], TN)
    return sum(full[h * CHUNK : (h + 1) * CHUNK] * masks[h][:1].astype(jnp.float32) for h in range(GROUP_HEADS))


def spread(pair, masks):
    return tuple(
        jnp.concatenate([part * masks[h] for h in range(GROUP_HEADS)], axis=0) for part in pair
    )


def stack(first, second):
    return tuple(jnp.concatenate([x, y], axis=0) for x, y in zip(first, second))


def head_masks():
    lane = lax.broadcasted_iota(jnp.int32, (CHUNK, LANES), 1) // CHUNK
    return [(lane == h).astype(jnp.float32).astype(jnp.bfloat16) for h in range(GROUP_HEADS)]


def places():
    row = lax.broadcasted_iota(jnp.int32, (CHUNK, LANES), 0)
    col = lax.broadcasted_iota(jnp.int32, (CHUNK, LANES), 1) % CHUNK
    return row, col


def running_sum(x, upper=False):
    row = lax.broadcasted_iota(jnp.int32, (CHUNK, CHUNK), 0)
    col = lax.broadcasted_iota(jnp.int32, (CHUNK, CHUNK), 1)
    ones = (row <= col if upper else col <= row).astype(jnp.float32).astype(jnp.bfloat16)
    high, rest = halves(x)
    low = (x - high.astype(jnp.float32) - rest.astype(jnp.float32)).astype(jnp.bfloat16)
    return dot32(ones, high, NN) + dot32(ones, rest, NN) + dot32(ones, low, NN)


def scaled_forms(q, w, k, a, b):
    total = running_sum(w)
    before = total - w
    middle = total[CHUNK // 2 - 1 : CHUNK // 2]
    end = total[CHUNK - 1 :]
    ea = jnp.exp(before - middle)
    eq = jnp.exp(total - middle)
    eb = jnp.exp(middle - total)
    ee = jnp.exp(end - total)
    return (a * ea, q * eq, b * eb, k * eb, b * ee, k * ee), (ea, eq, eb, ee), (jnp.exp(middle), jnp.exp(end))


def each(fn, *columns):
    return [fn(*row) for row in zip(*columns)]


def block_ones():
    row = lax.broadcasted_iota(jnp.int32, (LANES, LANES), 0) // CHUNK
    col = lax.broadcasted_iota(jnp.int32, (LANES, LANES), 1) // CHUNK
    return (row == col).astype(jnp.float32).astype(jnp.bfloat16)


def head_sum(x, ones):
    rows = x.shape[0]
    both = dot32(jnp.concatenate(halves(x), axis=0), ones, NN)
    return both[:rows] + both[rows:]


def prepared(keys, decay_low, rate_low, live, vec, ones):
    sig = jax.nn.sigmoid(vec[0] + decay_low)
    log_decay = (-0.6065306597126334) * sig * live
    rates = jax.nn.sigmoid(vec[1] + rate_low)
    scaled = keys * vec[2]
    inverse = lax.rsqrt(head_sum(scaled * scaled, ones) + 1e-06)
    unit_keys = scaled * inverse
    factor = (1.0 + (rates - 1.0) * vec[3]) * live
    return log_decay, keys * factor, -unit_keys, unit_keys * rates * live, sig, rates, inverse, factor


def read_out(o, q, k, v, vec, ones):
    centred = o - head_sum(o, ones) * (1.0 / CHUNK)
    scale = lax.rsqrt(head_sum(centred * centred, ones) * (1.0 / CHUNK) + 0.00064)
    normed = centred * scale
    weight = head_sum(q * k * vec[4], ones)
    return normed, scale, weight, normed * vec[5] + vec[6] + weight * v


def unit_slices():
    return [
        (slice(c * CHUNK, (c + 1) * CHUNK), slice(g * LANES, (g + 1) * LANES))
        for c in range(STEP_CHUNKS)
        for g in range(2)
    ]


def unit_live(length, step):
    row = lax.broadcasted_iota(jnp.int32, (CHUNK, LANES), 0)
    start = step * (STEP_CHUNKS * CHUNK)
    live = [(row + (start + c * CHUNK) < length).astype(jnp.float32) for c in range(STEP_CHUNKS)]
    return [live[c] for c in range(STEP_CHUNKS) for g in range(2)]


def unit_vectors(vec_ref):
    vec = [[vec_ref[i : i + 1, g * LANES : (g + 1) * LANES] for i in range(7)] for g in range(2)]
    return [vec[g] for c in range(STEP_CHUNKS) for g in range(2)]


def forward_kernel(base, *refs):
    len_ref, vec_ref, start_ref, q_ref, keys_ref, v_ref, dl_ref, rl_ref, gate_ref = refs[:9]
    (
        out_ref, o_ref, t_ref, aqb_ref, aak_ref, aqk_ref, y_ref, z_ref, trt_ref, qe_ref, state_ref,
    ) = refs[-11:]

    @pl.when(pl.program_id(0) == 0)
    def _():
        state_ref[...] = start_ref[...]

    masks = head_masks()
    row, col = places()
    strict = (col < row).astype(jnp.float32)
    within = (col <= row).astype(jnp.float32)
    eye = (col == row).astype(jnp.float32)
    ones = block_ones()
    units = unit_slices()
    live = unit_live(len_ref[0], pl.program_id(0) + base)
    vec = unit_vectors(vec_ref)
    load = lambda ref: [ref[u] for u in units]
    q, keys, v = load(q_ref), load(keys_ref), load(v_ref)
    ready = each(
        lambda x, y, z, m, n: prepared(x, y, z, m, n, ones), keys, load(dl_ref), load(rl_ref), live, vec
    )
    w, k, a, b = ([x[i] for x in ready] for i in range(4))
    forms = each(scaled_forms, q, w, k, a, b)
    ah, qh, bh, kh, bt, kt = ([f[0][i] for f in forms] for i in range(6))
    emid = [f[2][0] for f in forms]
    eend = [f[2][1] for f in forms]
    aq = each(lambda x, y: halves(jnp.concatenate([x, y], axis=0)), ah, qh)
    with_b = each(lambda l, r: mul(l, spread(halves(r), masks), NT), aq, bh)
    with_k = each(lambda l, r: mul(l, spread(halves(r), masks), NT), aq, kh)
    aab = [x[:CHUNK] * strict for x in with_b]
    aqb = [halves(x[CHUNK:] * within) for x in with_b]
    aak = [halves(x[:CHUNK] * strict) for x in with_k]
    aqk = [halves(x[CHUNK:] * within) for x in with_k]
    p = [halves(x * (row // 8 == col // 8)) for x in aab]
    t = [eye + x * (row // 8 == col // 8) for x in aab]
    p2 = each(lambda x: halves(mul(x, spread(x, masks))), p)
    both = each(lambda x, y: mul(stack(x, halves(y)), spread(x, masks)), p2, t)
    p4 = [halves(x[:CHUNK]) for x in both]
    t = each(lambda x, y: x + y[CHUNK:], t, both)
    t = each(lambda x, y: x + mul(halves(x), spread(y, masks)), t, p4)
    for size in (8, 16, 32):
        corner = ((row // size) % 2 == 1) & (col // size == row // size - 1)
        ts = [halves(x) for x in t]
        n = [halves(x * corner) for x in aab]
        tn = each(lambda x, y: halves(mul(x, spread(y, masks))), ts, n)
        t = each(lambda x, y, z: x + mul(y, spread(z, masks)), t, tn, ts)
    ts = [halves(x) for x in t]
    vs = [halves(x) for x in v]
    vm = [spread(x, masks) for x in vs]
    wide = each(lambda x, y, e: mul(x, spread(halves(y * e), masks)), ts, ah, emid)
    r0 = each(mul, aak, vm)
    y0 = each(lambda x, y: mul(x, spread(halves(y), masks)), ts, r0)
    wides = [halves(x) for x in wide]
    qe = each(lambda x, e, y, z: x * e + mul(y, spread(z, masks)), qh, emid, aqb, wides)
    y0s = [halves(x) for x in y0]
    part = each(lambda x, y, z, u: mul(x, spread(y, masks)) + mul(z, u), aqb, y0s, aqk, vm)
    bts = [halves(x) for x in bt]
    diag = [eye * e for e in eend]
    tr = each(lambda x, y, d: tmul(x, y, masks) + d, bts, wides, diag)
    trt = each(lambda x, y, d: tmul(y, x, masks) + d, bts, wides, diag)
    inject = each(lambda x, y, z, u: tmul(stack(x, halves(y)), stack(z, u), masks), bts, kt, y0s, vs)
    wq = each(lambda x, y: stack(x, halves(y)), wides, qe)
    z = []
    out = []
    for c in range(STEP_CHUNKS):
        for g in range(2):
            i = c * 2 + g
            now = state_ref[g]
            nows = spread(halves(now), masks)
            state_ref[g] = mul(halves(tr[i]), nows) + inject[i]
            z.append(now)
            out.append(mul(wq[i], nows))
    o = each(lambda x, y: x[CHUNK:] + y, out, part)
    mixed = each(lambda x, y, z, m, n: read_out(x, y, z, m, n, ones)[3], o, q, k, v, vec)
    for i, u in enumerate(units):
        out_ref[u] = (mixed[i] * gate_ref[u]).astype(jnp.bfloat16)
        o_ref[u] = o[i]
        y_ref[u] = (out[i][:CHUNK] + y0[i]).astype(jnp.bfloat16)
        t_ref[u] = ts[i][0]
        aqb_ref[u] = aqb[i][0]
        aak_ref[u] = aak[i][0]
        aqk_ref[u] = aqk[i][0]
        z_ref[u] = z[i]
        trt_ref[u] = trt[i].astype(jnp.bfloat16)
        qe_ref[u] = qe[i].astype(jnp.bfloat16)


def backward_kernel(base, *refs):
    (
        len_ref, vec_ref, start_ref, sums_ref, q_ref, keys_ref, v_ref, dl_ref, rl_ref, gate_ref,
        g_ref, o_ref, t_ref, aqb_ref, aak_ref, aqk_ref, y_ref, z_ref, trt_ref, qe_ref,
    ) = refs[:20]
    dq_ref, dkeys_ref, dv_ref, ddl_ref, drl_ref, dgate_ref, dvec_ref, state_ref = refs[-8:]
    step = base + pl.num_programs(0) - 1 - pl.program_id(0)

    @pl.when(pl.program_id(0) == 0)
    def _():
        state_ref[...] = start_ref[...]
        dvec_ref[...] = sums_ref[...]

    masks = head_masks()
    row, col = places()
    strict = (col < row).astype(jnp.float32)
    within = (col <= row).astype(jnp.float32)
    ones = block_ones()
    units = unit_slices()
    live = unit_live(len_ref[0], step)
    vec = unit_vectors(vec_ref)
    load = lambda ref: [ref[u] for u in units]
    q, keys, v, g = load(q_ref), load(keys_ref), load(v_ref), load(g_ref)
    ready = each(
        lambda x, y, z, m, n: prepared(x, y, z, m, n, ones), keys, load(dl_ref), load(rl_ref), live, vec
    )
    w, k, a, b, sig, rates, inverse, factor = ([x[i] for x in ready] for i in range(8))
    seen = each(lambda x, y, z, m, n: read_out(x, y, z, m, n, ones), load(o_ref), q, k, v, vec)
    normed, scale, weight, mixed = ([x[i] for x in seen] for i in range(4))
    gate = load(gate_ref)
    dgate = each(lambda x, y: x * y, g, mixed)
    dmix = each(lambda x, y: x * y, g, gate)
    dn = each(lambda x, n: x * n[5], dmix, vec)
    do = each(
        lambda x, n, r: r
        * (x - head_sum(x, ones) * (1.0 / CHUNK) - n * (head_sum(x * n, ones) * (1.0 / CHUNK))),
        dn, normed, scale,
    )
    dweight = each(lambda x, y: head_sum(x * y, ones), dmix, v)
    do = [whole(x) for x in do]
    qe, trt, t, aqb, aak, aqk, ys = (
        [(x,) for x in load(ref)]
        for ref in (qe_ref, trt_ref, t_ref, aqb_ref, aak_ref, aqk_ref, y_ref)
    )
    z = load(z_ref)
    vs = [whole(x) for x in v]
    h = each(lambda x, y: tmul(x, y, masks), qe, do)
    dz = [None] * len(units)
    for c in reversed(range(STEP_CHUNKS)):
        for g in range(2):
            i = c * 2 + g
            now = state_ref[g]
            dz[i] = now
            state_ref[g] = mul(trt[i], spread(whole(now), masks)) + h[i]
    dzs = [spread(whole(x), masks) for x in dz]
    zs = [spread(whole(x), masks) for x in z]
    forms = each(scaled_forms, q, w, k, a, b)
    ah, qh, bh, kh, bt, kt = ([f[0][i] for f in forms] for i in range(6))
    ea, eq, eb, ee = ([f[1][i] for f in forms] for i in range(4))
    emid = [f[2][0] for f in forms]
    eend = [f[2][1] for f in forms]
    from_end = each(lambda x, y, s: mul(whole(jnp.concatenate([x, y], axis=0)), s), bt, kt, dzs)
    dy = each(lambda x, y, s: whole(tmul(x, y, masks) + s[:CHUNK]), aqb, do, from_end)
    dr = each(lambda x, y: whole(tmul(x, y, masks)), t, dy)
    ro = each(stack, dr, do)
    dv = each(lambda x, y, s, f: tmul(stack(x, y), s, masks) + f[CHUNK:], aak, aqk, ro, from_end)
    mask2 = jnp.concatenate([strict, within], axis=0)
    dab = each(lambda s, y: whole(mul(s, spread(y, masks), NT) * mask2), ro, ys)
    dak = each(lambda s, y: whole(mul(s, spread(y, masks), NT) * mask2), ro, vs)
    dst = each(lambda s, y: mul(s, y, NT), ro, zs)
    bhs, khs = [whole(x) for x in bh], [whole(x) for x in kh]
    inside = each(
        lambda x, bb, y, kk: mul(x, spread(bb, masks)) + mul(y, spread(kk, masks)), dab, bhs, dak, khs
    )
    outside = each(lambda s, e: s * e, dst, emid)
    daq = each(lambda x, y: x + y, inside, outside)
    aq = each(lambda x, y: whole(jnp.concatenate([x, y], axis=0)), ah, qh)
    dbh = each(lambda x, y: tmul(x, y, masks), dab, aq)
    dkh = each(lambda x, y: tmul(x, y, masks), dak, aq)
    dend = each(lambda y, x, s: mul(stack(y, x), s, NT), ys, vs, dzs)
    row_of_ones = jnp.ones((8, LANES), jnp.bfloat16)
    sums = lambda x: jnp.sum(x, axis=0, keepdims=True)
    for i, u in enumerate(units):
        da = daq[i][:CHUNK] * ea[i]
        dq = daq[i][CHUNK:] * eq[i]
        dbt = dend[i][:CHUNK] * ee[i]
        dkt = dend[i][CHUNK:] * ee[i]
        db = dbh[i] * eb[i] + dbt
        dk = dkh[i] * eb[i] + dkt
        paq = inside[i] * aq[i][0].astype(jnp.float32)
        pa = paq[:CHUNK] + outside[i][:CHUNK] * ah[i]
        diff = pa + paq[CHUNK:] + outside[i][CHUNK:] * qh[i]
        diff = diff - dbh[i] * bhs[i][0].astype(jnp.float32) - dkh[i] * khs[i][0].astype(jnp.float32)
        diff = diff - dbt * b[i] - dkt * k[i]
        zz = spread(halves(z[i] * dz[i]), masks)
        carry = (dot32(row_of_ones, zz[0], NT) + dot32(row_of_ones, zz[1], NT))[:1] * eend[i]
        carry = carry + sums(dbt * b[i] + dkt * k[i])
        dw = running_sum(diff, upper=True) - pa + carry
        from_bonus = dweight[i] * vec[i][4]
        dk = dk + from_bonus * q[i]
        dq_ref[u] = (dq + from_bonus * k[i]).astype(jnp.bfloat16)
        dv_ref[u] = (dv[i] + weight[i] * dmix[i]).astype(jnp.bfloat16)
        dgate_ref[u] = dgate[i].astype(jnp.bfloat16)
        unit_keys = -a[i]
        db = db * live[i]
        du = db * rates[i] - da
        dscaled = inverse[i] * (du - unit_keys * head_sum(du * unit_keys, ones))
        dkl = dk * keys[i] * live[i]
        drl = (db * unit_keys + dkl * vec[i][3]) * rates[i] * (1.0 - rates[i])
        ddl = dw * w[i] * (1.0 - sig[i])
        dkeys_ref[u] = (dk * factor[i] + dscaled * vec[i][2]).astype(jnp.bfloat16)
        ddl_ref[u] = ddl.astype(jnp.bfloat16)
        drl_ref[u] = drl.astype(jnp.bfloat16)
        parts = (
            ddl, drl, dscaled * keys[i], dkl * (rates[i] - 1.0),
            dweight[i] * q[i] * k[i], dmix[i] * normed[i], dmix[i],
        )
        lanes = u[1]
        for j, x in enumerate(parts):
            dvec_ref[j : j + 1, lanes] += sums(x)


def wkv_call(kernel, base, steps, small, arrays, outs, sums, previous, name):
    tokens, width = arrays[0].shape
    rows = CHUNK * STEP_CHUNKS
    last = base + steps - 1
    turned = kernel is backward_kernel
    spec = pl.BlockSpec((rows, width), lambda i: (last - i if turned else base + i, 0))
    state = pl.BlockSpec((2, CHUNK, LANES), lambda i: (0, 0, 0))
    whole = pl.BlockSpec((8, width), lambda i: (0, 0))
    shape = jax.ShapeDtypeStruct
    first = [pl.BlockSpec(memory_space=pltpu.SMEM), whole, state] + [whole] * sums
    held = list(previous or ())
    start = len(first) + len(arrays)
    return pl.pallas_call(
        partial(kernel, base),
        grid=(steps,),
        in_specs=first + [spec] * len(arrays) + [pl.BlockSpec(memory_space=pl.ANY)] * len(held),
        out_specs=[spec] * len(outs) + [whole] * sums + [state],
        out_shape=[shape((tokens, width), dtype) for dtype in outs]
        + [shape((8, width), jnp.float32)] * sums
        + [shape((2, CHUNK, LANES), jnp.float32)],
        input_output_aliases={start + i: i for i in range(len(held))},
        compiler_params=pltpu.CompilerParams(vmem_limit_bytes=60 << 20),
        cost_estimate=SMALL,
        name=name,
    )(*small, *arrays, *held)


def wkv_forward(base, steps, length, vec, state, arrays, previous=None):
    outs = [jnp.bfloat16, jnp.float32] + [jnp.bfloat16] * 5 + [jnp.float32] + [jnp.bfloat16] * 2
    return wkv_call(
        forward_kernel, base, steps, (length, vec, state), arrays, outs, 0, previous, "wkv_forward"
    )


def wkv_backward(base, steps, length, vec, state, sums, arrays, previous=None):
    outs = [jnp.bfloat16] * 6
    return wkv_call(
        backward_kernel, base, steps, (length, vec, state, sums), arrays, outs, 1, previous,
        "wkv_backward",
    )


ROWS = 128


def row_norm(x):
    centred = x - jnp.mean(x, axis=-1, keepdims=True)
    scale = lax.rsqrt(jnp.mean(centred * centred, axis=-1, keepdims=True) + 1e-05)
    return centred * scale, scale


def shifted(x, edge, down):
    rows = x.shape[0]
    row = lax.broadcasted_iota(jnp.int32, x.shape, 0)
    if down:
        return jnp.where(row == 0, edge, pltpu.roll(x, 1, 0))
    return jnp.where(row == rows - 1, edge, pltpu.roll(x, rows - 1, 0))


def below(x, upper):
    lane = lax.broadcasted_iota(jnp.int32, x.shape, 1)
    keep = (lane >= DECAY_RANK) if upper else (lane < DECAY_RANK)
    return jnp.where(keep, x, jnp.zeros_like(x))


def front_kernel(
    x_ref, vec_ref, wr_ref, wk_ref, wv_ref, down_ref, up_ref,
    m0_ref, m1_ref, m2_ref, m3_ref, m4_ref, m5_ref,
    q_ref, k_ref, v_ref, dl_ref, rl_ref, gate_ref, hid_ref,
    edge_ref,
):
    @pl.when(pl.program_id(0) == 0)
    def _():
        edge_ref[...] = jnp.zeros_like(edge_ref)

    unit, _ = row_norm(x_ref[...].astype(jnp.float32))
    normed = unit * vec_ref[12:13] + vec_ref[13:14]
    change = shifted(normed, edge_ref[:1], True) - normed
    edge_ref[:1] = normed[ROWS - 1 :]
    mixes = []
    for j, ref in enumerate((m0_ref, m1_ref, m2_ref, m3_ref, m4_ref, m5_ref)):
        mixes.append((normed + change * vec_ref[j : j + 1]).astype(jnp.bfloat16))
        ref[...] = mixes[j]
    q_ref[...] = dot32(mixes[0], wr_ref[...], NN)
    k_ref[...] = dot32(mixes[2], wk_ref[...], NN)
    v_ref[...] = dot32(mixes[3], wv_ref[...], NN)
    first = down_ref[:, :128]
    pre_decay, pre_rate = dot32(mixes[1], first, NN), dot32(mixes[4], first, NN)
    pre_gate = dot32(mixes[5], down_ref[:, 128:], NN)
    lane = lax.broadcasted_iota(jnp.int32, pre_decay.shape, 1)
    pair = jnp.where(lane < DECAY_RANK, jnp.tanh(pre_decay), pre_rate)
    gate = jax.nn.sigmoid(pre_gate)
    hid_ref[:, :128] = pair
    hid_ref[:, 128:] = gate
    narrow_pair = pair.astype(jnp.bfloat16)
    dl_ref[...] = dot32(below(narrow_pair, False), up_ref[:, :128], NT)
    rl_ref[...] = dot32(below(narrow_pair, True), up_ref[:, :128], NT)
    gate_ref[...] = dot32(gate.astype(jnp.bfloat16), up_ref[:, 128:], NT)


def front_forward(x, vectors, w_r, w_k, w_v, down, up):
    tokens, width = x.shape
    wide = pl.BlockSpec((ROWS, width), lambda i: (i, 0))
    own = pl.BlockSpec((ROWS, OWN), lambda i: (i, 0))
    hid = pl.BlockSpec((ROWS, 256), lambda i: (i, 0))
    whole = lambda a: pl.BlockSpec(a.shape, lambda i: (0, 0))
    shape = jax.ShapeDtypeStruct
    return pl.pallas_call(
        front_kernel,
        grid=(tokens // ROWS,),
        in_specs=[wide] + [whole(a) for a in (vectors, w_r, w_k, w_v, down, up)],
        out_specs=[wide] * 6 + [own] * 6 + [hid],
        out_shape=[shape((tokens, width), jnp.bfloat16)] * 6
        + [shape((tokens, OWN), jnp.float32)] * 6
        + [shape((tokens, 256), jnp.float32)],
        scratch_shapes=[pltpu.VMEM((8, width), jnp.float32)],
        compiler_params=pltpu.CompilerParams(vmem_limit_bytes=60 << 20),
        cost_estimate=SMALL,
        name="front_forward",
    )(x, vectors, w_r, w_k, w_v, down, up)


def front_back_kernel(
    x_ref, before_ref, vec_ref, wr_ref, wk_ref, wv_ref, down_ref, up_ref,
    m1_ref, m4_ref, m5_ref, hid_ref,
    dq_ref, dk_ref, dv_ref, ddl_ref, drl_ref, dgate_ref, own_vec_ref, ffn_vec_ref,
    dx_ref, mine_ref, other_ref,
    edge_ref, sums_ref, misc_ref,
):
    step = pl.num_programs(0) - 1 - pl.program_id(0)
    core = lax.axis_index("dp") % 2
    own_start = pl.multiple_of(core * OWN, OWN)

    @pl.when(pl.program_id(0) == 0)
    def _():
        edge_ref[...] = jnp.zeros_like(edge_ref)
        sums_ref[...] = jnp.zeros_like(sums_ref)
        misc_ref[...] = jnp.zeros_like(misc_ref)

    unit, scale = row_norm(x_ref[...].astype(jnp.float32))
    gain, offset = vec_ref[12:13], vec_ref[13:14]
    normed = unit * gain + offset
    tail, _ = row_norm(before_ref[...].astype(jnp.float32))
    edge = (tail[15:] * gain + offset) * jnp.where(step == 0, 0.0, 1.0)
    change = shifted(normed, edge, True) - normed
    ddl, drl, dgate = ddl_ref[...], drl_ref[...], dgate_ref[...]
    hid = hid_ref[...]
    pair, gate = hid[:, :128], hid[:, 128:]
    lane = lax.broadcasted_iota(jnp.int32, pair.shape, 1)
    first_up, last_up = up_ref[:, :128], up_ref[:, 128:]
    pair_grad = jnp.where(
        lane < DECAY_RANK,
        dot32(ddl, first_up, NN) * (1.0 - pair * pair),
        dot32(drl, first_up, NN),
    ).astype(jnp.bfloat16)
    gate_grad = (dot32(dgate, last_up, NN) * gate * (1.0 - gate)).astype(jnp.bfloat16)
    narrow_pair, narrow_gate = pair.astype(jnp.bfloat16), gate.astype(jnp.bfloat16)
    own_rows = pl.ds(own_start, OWN)
    misc_ref[own_rows, 256:384] += dot32(ddl, below(narrow_pair, False), TN) + dot32(
        drl, below(narrow_pair, True), TN
    )
    misc_ref[own_rows, 384:512] += dot32(dgate, narrow_gate, TN)
    decay_part, rate_part = below(pair_grad, False), below(pair_grad, True)
    misc_ref[:, :128] += dot32(m1_ref[...], decay_part, TN) + dot32(m4_ref[...], rate_part, TN)
    misc_ref[:, 128:256] += dot32(m5_ref[...], gate_grad, TN)
    first_down = down_ref[:, :128]
    grads = (
        lambda: dot32(dq_ref[...], wr_ref[...], NT),
        lambda: dot32(decay_part, first_down, NT),
        lambda: dot32(dk_ref[...], wk_ref[...], NT),
        lambda: dot32(dv_ref[...], wv_ref[...], NT),
        lambda: dot32(rate_part, first_down, NT),
        lambda: dot32(gate_grad, down_ref[:, 128:], NT),
    )
    total = jnp.zeros_like(change)
    moved = jnp.zeros_like(change)
    for j, grad in enumerate(grads):
        now = grad()
        total = total + now
        moved = moved + now * vec_ref[j : j + 1]
        sums_ref[j : j + 1] += jnp.sum(now * change, axis=0, keepdims=True)
    dnormed = total - moved + shifted(moved, edge_ref[:1], False)
    edge_ref[:1] = moved[:1]
    sums_ref[12:13] += jnp.sum(dnormed * unit, axis=0, keepdims=True)
    sums_ref[13:14] += jnp.sum(dnormed, axis=0, keepdims=True)
    dunit = dnormed * gain
    dx_ref[...] = scale * (
        dunit
        - jnp.mean(dunit, axis=-1, keepdims=True)
        - unit * jnp.mean(dunit * unit, axis=-1, keepdims=True)
    )

    @pl.when(step == 0)
    def _():
        sums_ref[6:7] = ffn_vec_ref[0:1] * 0.5
        sums_ref[14:16] = ffn_vec_ref[1:3] * 0.5
        zeros = jnp.zeros((1, OWN), jnp.float32)
        for target, source in ((7, 0), (8, 1), (9, 2), (10, 3), (11, 4), (16, 5), (17, 6)):
            mine = own_vec_ref[source : source + 1]
            sums_ref[target : target + 1] = jnp.concatenate(
                [jnp.where(core == 0, mine, zeros), jnp.where(core == 0, zeros, mine)], axis=1
            )
        for block in range(EMBED // 128):
            lanes = slice(block * 128, (block + 1) * 128)
            misc_ref[lanes, 512:640] = sums_ref[:, lanes].T
        share = mine_ref.shape[1]
        for chip in range(mine_ref.shape[0]):
            low = misc_ref[2 * chip * share : (2 * chip + 1) * share]
            high = misc_ref[(2 * chip + 1) * share : (2 * chip + 2) * share]
            mine_ref[chip] = jnp.where(core == 0, low, high)
            other_ref[chip] = jnp.where(core == 0, high, low).astype(jnp.bfloat16)


def front_backward(
    x, vectors, w_r, w_k, w_v, down, up, mixes, hid, grads, own_vec, ffn_vec
):
    tokens, width = x.shape
    devices = lax.axis_size("dp")
    pieces = (devices // 2, EMBED // devices, 640)
    steps = tokens // ROWS
    wide = pl.BlockSpec((ROWS, width), lambda i: (steps - 1 - i, 0))
    before = pl.BlockSpec(
        (16, width), lambda i: (jnp.maximum((steps - 1 - i) * (ROWS // 16) - 1, 0), 0)
    )
    own = pl.BlockSpec((ROWS, OWN), lambda i: (steps - 1 - i, 0))
    hid_spec = pl.BlockSpec((ROWS, 256), lambda i: (steps - 1 - i, 0))
    whole = lambda a: pl.BlockSpec(a.shape, lambda i: (0, 0))
    shape = jax.ShapeDtypeStruct
    return pl.pallas_call(
        front_back_kernel,
        grid=(steps,),
        in_specs=[wide, before]
        + [whole(a) for a in (vectors, w_r, w_k, w_v, down, up)]
        + [wide] * 3
        + [hid_spec]
        + [own] * 6
        + [whole(own_vec), whole(ffn_vec)],
        out_specs=[wide] + [pl.BlockSpec(pieces, lambda i: (0, 0, 0))] * 2,
        out_shape=[
            shape((tokens, width), jnp.float32),
            shape(pieces, jnp.float32),
            shape(pieces, jnp.bfloat16),
        ],
        scratch_shapes=[
            pltpu.VMEM((8, width), jnp.float32),
            pltpu.VMEM((128, width), jnp.float32),
            pltpu.VMEM((EMBED, 640), jnp.float32),
        ],
        compiler_params=pltpu.CompilerParams(vmem_limit_bytes=60 << 20),
        cost_estimate=SMALL,
        name="front_backward",
    )(x, x, vectors, w_r, w_k, w_v, down, up, *mixes, hid, *grads, own_vec, ffn_vec)


def ffn_back_kernel(
    len_ref, res_ref, before_ref, cot_ref, mine_ref, other_ref, vec_ref, wo_ref,
    grad_ref, narrow_ref, gated_ref, dvec_ref,
    edge_ref,
):
    step = pl.num_programs(0) - 1 - pl.program_id(0)

    @pl.when(pl.program_id(0) == 0)
    def _():
        edge_ref[...] = jnp.zeros_like(edge_ref)
        dvec_ref[...] = jnp.zeros_like(dvec_ref)

    gain, offset, coefficient = vec_ref[14:15], vec_ref[15:16], vec_ref[6:7]
    unit, scale = row_norm(res_ref[...])
    normed = unit * gain + offset
    tail, _ = row_norm(before_ref[...])
    edge = (tail[7:] * gain + offset) * jnp.where(step == 0, 0.0, 1.0)
    change = shifted(normed, edge, True) - normed
    grad = mine_ref[...].astype(jnp.float32) + other_ref[...].astype(jnp.float32)
    moved = grad * coefficient
    dnormed = grad - moved + shifted(moved, edge_ref[:1], False)
    edge_ref[:1] = moved[:1]
    sums = lambda x: jnp.sum(x, axis=0, keepdims=True)
    dvec_ref[0:1] += sums(grad * change)
    dvec_ref[1:2] += sums(dnormed * unit)
    dvec_ref[2:3] += sums(dnormed)
    dunit = dnormed * gain
    row = lax.broadcasted_iota(jnp.int32, grad.shape, 0) + step * ROWS
    out_grad = jnp.where(row < len_ref[0], cot_ref[...].astype(jnp.float32), 0.0)
    total = out_grad + scale * (
        dunit
        - jnp.mean(dunit, axis=-1, keepdims=True)
        - unit * jnp.mean(dunit * unit, axis=-1, keepdims=True)
    )
    grad_ref[...] = total
    small = total.astype(jnp.bfloat16)
    core = lax.axis_index("dp") % 2
    narrow_ref[...] = jnp.where(core == 0, small[:, :OWN], small[:, OWN:])
    gated_ref[...] = dot32(small, wo_ref[...], NT)


def ffn_backward(length, residual, cot, mine, other, vectors, w_o_rows):
    tokens, width = residual.shape
    steps = tokens // ROWS
    wide = pl.BlockSpec((ROWS, width), lambda i: (steps - 1 - i, 0))
    before = pl.BlockSpec(
        (8, width), lambda i: (jnp.maximum((steps - 1 - i) * (ROWS // 8) - 1, 0), 0)
    )
    own = pl.BlockSpec((ROWS, OWN), lambda i: (steps - 1 - i, 0))
    whole = lambda a: pl.BlockSpec(a.shape, lambda i: (0, 0))
    shape = jax.ShapeDtypeStruct
    return pl.pallas_call(
        ffn_back_kernel,
        grid=(steps,),
        in_specs=[pl.BlockSpec(memory_space=pltpu.SMEM), wide, before]
        + [wide] * 3
        + [whole(vectors), whole(w_o_rows)],
        out_specs=[wide, own, own, pl.BlockSpec((8, width), lambda i: (0, 0))],
        out_shape=[
            shape((tokens, width), jnp.float32),
            shape((tokens, OWN), jnp.bfloat16),
            shape((tokens, OWN), jnp.float32),
            shape((8, width), jnp.float32),
        ],
        scratch_shapes=[pltpu.VMEM((8, width), jnp.float32)],
        compiler_params=pltpu.CompilerParams(vmem_limit_bytes=60 << 20),
        cost_estimate=SMALL,
        name="ffn_backward",
    )(length, residual, residual, cot, mine, other, vectors, w_o_rows)


def att_grad_kernel(m0_ref, m2_ref, m3_ref, gated_ref, dq_ref, dk_ref, dv_ref, do_ref,
                    send_a, keep_a, send_b, keep_b):
    chip = lax.axis_index("dp") // 2
    by_x, by_y = chip % 2 == 0, (chip // 2) % 2 == 0
    first = ((m0_ref, dq_ref), (gated_ref, do_ref))
    second = ((m2_ref, dk_ref), (m3_ref, dv_ref))
    for half in range(2):
        lanes = slice(half * OWN, (half + 1) * OWN)
        block = dot32(first[half][0][...], first[half][1][...], TN).astype(jnp.bfloat16)
        for y in range(2):
            low, high = block[y * 128 : y * 128 + 64], block[y * 128 + 64 : y * 128 + 128]
            send_a[y, :, lanes] = jnp.where(by_x, high, low)
            keep_a[y, :, lanes] = jnp.where(by_x, low, high)
        block = dot32(second[half][0][...], second[half][1][...], TN).astype(jnp.bfloat16)
        for x in range(2):
            low, high = block[x * 64 : x * 64 + 64], block[128 + x * 64 : 128 + x * 64 + 64]
            send_b[x, :, lanes] = jnp.where(by_y, high, low)
            keep_b[x, :, lanes] = jnp.where(by_y, low, high)


def att_gradients(mixes, gated, grads, own_grad):
    tokens = gated.shape[0]
    left = pl.BlockSpec((tokens, 256), lambda i: (0, i))
    right = pl.BlockSpec((tokens, OWN), lambda i: (0, 0))
    out = pl.BlockSpec((2, 64, 2 * OWN), lambda i: (i, 0, 0))
    return pl.pallas_call(
        att_grad_kernel,
        grid=(4,),
        in_specs=[left] * 4 + [right] * 4,
        out_specs=[out] * 4,
        out_shape=[jax.ShapeDtypeStruct((8, 64, 2 * OWN), jnp.bfloat16)] * 4,
        compiler_params=pltpu.CompilerParams(vmem_limit_bytes=60 << 20),
        cost_estimate=SMALL,
        name="att_gradients",
    )(*mixes, gated, *grads, own_grad)


def swap(block, mask):
    size = lax.axis_size("dp")
    return lax.ppermute(block, "dp", [(i, i ^ mask) for i in range(size)])


def bit_of(mask):
    return (lax.axis_index("dp") // mask) % 2


def in_order(mask, own, other, axis):
    lower = bit_of(mask) == 0
    return jnp.where(
        lower, jnp.concatenate([own, other], axis=axis), jnp.concatenate([other, own], axis=axis)
    )


def chip_masks():
    size = lax.axis_size("dp")
    masks = []
    while 2 << len(masks) < size:
        masks.append(2 << len(masks))
    return masks


def steps_of(kind):
    masks = chip_masks()
    near, far = [[mask] for mask in masks[:2]], [[mask] for mask in masks[2:][::-1]]
    first = [[far[0][0], far[1][0], far[0][0] | far[1][0]]] if len(far) == 2 else far
    return [first + near[::-1], first + near, far + near[::-1], far + near, near + far][kind]


class Held:
    def __init__(self, value):
        self.value = value


def meet(movers, *arrays):
    held = []
    for mover in movers:
        held += [x[0] for x in mover.arrived if x[0] not in held]
    out = lax.optimization_barrier(tuple(x.value for x in held) + arrays)
    for x, value in zip(held, out):
        x.value = value
    return out[len(held) :]


def read(arrived):
    return [x.value if lanes is None else x.value[..., lanes] for x, lanes in arrived]


class Gather:
    def __init__(self, block, kind, places=(0,)):
        self.steps = steps_of(kind)
        self.held = block[None]
        self.places = [0]
        self.arrived = []
        self.masks = []

    def merge(self):
        if self.arrived:
            self.held = jnp.concatenate([self.held] + read(self.arrived), axis=0)
            self.places = self.places + [p ^ (m // 2) for m in self.masks for p in self.places]
            self.arrived = []

    def step(self):
        if self.steps:
            self.merge()
            self.masks = self.steps.pop(0)
            self.arrived = [(Held(swap(self.held, mask)), None) for mask in self.masks]
        return self

    def run(self):
        while self.steps:
            self.step()
        return self

    def split(self, kinds):
        width = self.held.shape[-1] // len(kinds)
        out = []
        for i, kind in enumerate(kinds):
            part = Gather.__new__(Gather)
            cut = slice(i * width, (i + 1) * width)
            part.steps = steps_of(kind)[len(steps_of(kind)) - len(self.steps) :]
            part.held = self.held[..., cut]
            part.arrived = [(x, cut) for x, _ in self.arrived]
            part.places, part.masks = self.places, self.masks
            out.append(part)
        return out


def place_kernel(places, cuts, *refs):
    sources, outs = refs[: len(places)], refs[len(places) :]
    chip = lax.axis_index("dp") // 2
    for source, (part, list_of) in zip(sources, places):
        for j, place in enumerate(list_of):
            for out, (first, rows, lanes) in zip(outs, cuts):
                start = pl.multiple_of((chip ^ place) * rows, rows)
                lane, width = lanes[part]
                at = sum(w for _, w in lanes[:part])
                out[pl.ds(start, rows), at : at + width] = source[
                    j, first : first + rows, lane : lane + width
                ]


def assemble(gathers, cuts=None):
    gathers = [g.run() for g in gathers]
    rows = gathers[0].held.shape[1]
    cuts = cuts or ((0, rows, [(0, g.held.shape[2]) for g in gathers]),)
    sources, places = [], []
    for i, g in enumerate(gathers):
        sources += [g.held] + read(g.arrived)
        shifts = [0] + [mask // 2 for mask in g.masks]
        places += [(i, [p ^ shift for p in g.places]) for shift in shifts]
    count = lax.axis_size("dp") // 2
    if any(cut[1] % 16 for cut in cuts):
        return assemble_plain(sources, places, cuts, count)
    space = pl.BlockSpec(memory_space=pltpu.VMEM)
    return pl.pallas_call(
        partial(place_kernel, places, cuts),
        in_specs=[space] * len(sources),
        out_specs=[space] * len(cuts),
        out_shape=[
            jax.ShapeDtypeStruct((count * n, sum(w for _, w in lanes)), sources[0].dtype)
            for _, n, lanes in cuts
        ],
        compiler_params=pltpu.CompilerParams(vmem_limit_bytes=32 << 20),
        cost_estimate=SMALL,
        name="assemble",
    )(*sources)


def assemble_plain(sources, places, cuts, count):
    chip = lax.axis_index("dp") // 2
    parts = []
    for part in sorted({part for part, _ in places}):
        blocks = jnp.concatenate([x for x, (at, _) in zip(sources, places) if at == part])
        where = [p for at, list_of in places if at == part for p in list_of]
        blocks = jnp.stack([blocks[where.index(i)] for i in range(count)])
        parts.append(jnp.take(blocks, chip ^ lax.iota(jnp.int32, count), axis=0))
    return [
        jnp.concatenate(
            [x[:, first : first + n, at : at + w] for x, (at, w) in zip(parts, lanes)], axis=-1
        ).reshape(count * n, -1)
        for first, n, lanes in cuts
    ]


class Scatter:
    def __init__(self, parts, kind):
        self.steps = steps_of(kind)[::-1]
        self.axes = chip_masks()[::-1]
        self.sources = [parts.reshape((2,) * len(self.axes) + parts.shape[1:])]
        self.arrived = []
        self.sent = None

    @classmethod
    def begun(cls, sent, kept, kind):
        out = cls.__new__(cls)
        out.steps = steps_of(kind)[::-1]
        out.axes = [axis for axis in chip_masks()[::-1] if axis != out.steps[0][0]]
        out.sources = [kept.reshape((2,) * len(out.axes) + kept.shape[1:])]
        out.arrived = []
        out.sent = [sent.reshape(out.sources[0].shape)]
        return out

    def pick(self, sources, mask, gone):
        out = []
        for x in sources:
            for place in reversed(range(len(self.axes))):
                axis = self.axes[place]
                if axis in gone:
                    which = bit_of(axis) if not mask & axis else 1 - bit_of(axis)
                    x = lax.dynamic_index_in_dim(x, which, place, keepdims=False)
            out.append(x)
        return out

    def prepare(self):
        if self.sent is not None:
            return self
        masks = self.steps[0]
        sources = self.sources + read(self.arrived)
        gone = [axis for axis in self.axes if any(mask & axis for mask in masks)]
        self.sent = [
            sum(x.astype(jnp.float32) for x in self.pick(sources, mask, gone)).astype(jnp.bfloat16)
            for mask in masks
        ]
        self.sources = self.pick(sources, 0, gone)
        self.axes = [axis for axis in self.axes if axis not in gone]
        self.arrived = []
        return self

    def step(self):
        return together([self])[0]

    def run(self):
        while self.steps:
            self.step()
        return self

    def total(self):
        return sum(x.astype(jnp.float32) for x in self.sources + read(self.arrived))


def together(parts):
    if not parts[0].steps:
        return parts
    for part in parts:
        part.prepare()
    for i, mask in enumerate(parts[0].steps[0]):
        sent = [part.sent[i] for part in parts]
        got = Held(swap(sent[0] if len(sent) == 1 else jnp.concatenate(sent, axis=-1), mask))
        at = 0
        for part, x in zip(parts, sent):
            lanes = slice(at, at + x.shape[-1]) if len(sent) > 1 else None
            part.arrived.append((got, lanes))
            at += x.shape[-1]
    for part in parts:
        part.steps.pop(0)
        part.sent_now, part.sent = part.sent[0], None
    return parts


def norm_rows(features, gain_row, offset_row):
    average = jnp.mean(features, axis=-1, keepdims=True)
    centred = features - average
    variance = jnp.mean(centred * centred, axis=-1, keepdims=True)
    return centred * lax.rsqrt(variance + 1e-05) * gain_row + offset_row


def product(operand, weight_matrix):
    return jnp.dot(operand, weight_matrix, preferred_element_type=jnp.float32)


def input_gradient_rows(upstream_gradient, weight_matrix):
    return lax.dot_general(
        upstream_gradient,
        weight_matrix,
        (((1,), (1,)), ((), ())),
        preferred_element_type=jnp.float32,
    )


def weight_gradient(operand, upstream_gradient):
    return lax.dot_general(
        operand, upstream_gradient, (((0,), (0,)), ((), ())), preferred_element_type=jnp.float32
    )


def earlier(rows):
    return jnp.concatenate([jnp.zeros_like(rows[:1]), rows[:-1]], axis=0)


def ffn_mix(residual, vectors):
    second = norm_rows(residual, vectors[14], vectors[15])
    return second + (earlier(second) - second) * vectors[6]


def narrow(x):
    return x.astype(jnp.bfloat16)


def local(
    inputs,
    lengths,
    attention_projections,
    channel_key_weight,
    channel_value_weight,
    lowrank_down_weight,
    lowrank_up_weight,
    per_feature_parameters,
    cotangent,
):
    devices = lax.axis_size("dp")
    chips = devices // 2
    device = lax.axis_index("dp")
    chip, core = device // 2, device % 2
    row_count = inputs.shape[0]
    slots = 2 * row_count
    share = EMBED // devices
    pair_share = 2 * share
    units = channel_value_weight.shape[0]
    half_units = chips * units

    def own_cut(x, which):
        return lax.dynamic_slice_in_dim(x, which * OWN, OWN, x.ndim - 1)

    def own_rows(x, which):
        return lax.dynamic_slice_in_dim(x, which * row_count, row_count, 0)

    pair_rows = in_order(
        1,
        own_cut(attention_projections, core),
        swap(own_cut(attention_projections, 1 - core), 1),
        1,
    )
    lora = jnp.concatenate([lowrank_down_weight, lowrank_up_weight.T], axis=1)
    vector_rows = jnp.pad(per_feature_parameters.T, ((0, 0), (0, 128 - 18)))
    vector_rows = vector_rows.reshape(share // 4, OWN)
    first_rows = 3 * pair_share
    misc_rows = share + share // 4 + (share // 4) % 16
    block = jnp.concatenate(
        [
            pair_rows[:3].reshape(first_rows, OWN),
            lora,
            jnp.pad(vector_rows, ((0, (share // 4) % 16), (0, 0))),
        ],
        axis=0,
    )
    half = half_units // 2
    quarter = OWN // 2
    first = Gather(block, 0).step()
    w_o_part = Gather(pair_rows[3], 4).step().step()
    key_in, raw, cot, _ = meet([], channel_key_weight, inputs, cotangent, first.held)
    key_cut = key_in.reshape(share, chips, 2, units)

    def key_columns(which):
        return lax.dynamic_index_in_dim(key_cut, which, 2, keepdims=False).reshape(share, half_units)

    key_rows = in_order(1, key_columns(core), swap(key_columns(1 - core), 1), 0)
    tokens = in_order(1, raw, swap(raw, 1), 0)
    cot = in_order(1, cot, swap(cot, 1), 0)
    key_rows, tokens, cot = meet([first, w_o_part], key_rows, tokens, cot)
    first = first.split((0, 1))
    for part in first:
        part.step()
    key_part = Gather(key_rows, 2).step()
    (tokens,) = meet(first, tokens)
    for part in first:
        part.step()
    value_block, *_ = meet([key_part], channel_value_weight, *[part.held for part in first])
    key_part.step()
    value_part = Gather(value_block, 2).step()
    w_o_part.step()
    (tokens,) = meet(first + [key_part, value_part], tokens)
    key_parts = key_part.split((2, 3))
    for part in key_parts:
        part.step()
    w_r, w_k, w_v, misc = assemble(
        first,
        [(i * pair_share, pair_share, [(0, quarter)] * 2) for i in range(3)]
        + [(first_rows, misc_rows, [(0, quarter)] * 2)],
    )
    misc = misc.reshape(chips, 1, misc_rows, OWN)
    misc = in_order(1, misc, swap(misc, 1), 1)
    value_part.step()
    lora = misc[:, :, :share].reshape(EMBED, OWN)
    down, up_t = lora[:, :256], lax.dynamic_slice_in_dim(lora[:, 256:], core * OWN, OWN, 0)
    vectors = misc[:, :, share : share + share // 4].reshape(EMBED, 128)[:, :18].T
    vectors = vectors.astype(jnp.float32)
    own_vectors = own_cut(vectors, core)
    used = jnp.concatenate([own_vectors[7:12], own_vectors[16:18], own_vectors[:1]], axis=0)
    length = lax.dynamic_index_in_dim(lengths, chip, 0)
    live = (lax.iota(jnp.int32, slots) < length)[:, None]

    *mixes, queries, keys, values, decay_low, rate_low, gate_rows, hid = front_forward(
        tokens, vectors, w_r, w_k, w_v, down, up_t
    )
    terms = meet(
        key_parts + [value_part, w_o_part],
        queries, keys, values, decay_low, rate_low, gate_rows,
    )
    value_parts = value_part.split((2, 3))
    for part in key_parts + value_parts:
        part.step()
    w_o_part.step()
    blocks = slots // (CHUNK * STEP_CHUNKS)
    zero_state = jnp.zeros((2, CHUNK, LANES), jnp.float32)
    gated, *saved, _ = wkv_forward(0, blocks, length, used, zero_state, terms)
    gated, cot, tokens = meet(key_parts + value_parts, gated, cot, tokens)
    for part in value_parts:
        part.step()
    gated, *_ = meet([w_o_part] + key_parts, gated, *[part.held for part in value_parts])
    gated_all = in_order(1, gated, swap(gated, 1), 1)
    (w_o_own,) = assemble([w_o_part])
    w_o = in_order(1, w_o_own, swap(w_o_own, 1), 1)
    (key_weight,) = assemble(key_parts)
    residual = tokens.astype(jnp.float32) + product(gated_all, w_o)
    ffn_in = narrow(ffn_mix(residual, vectors))
    positive = jax.nn.relu(product(ffn_in, key_weight))
    hidden = narrow(jnp.square(positive))
    out_narrow = jnp.where(live, cot, jnp.zeros_like(cot))
    grad_value = narrow(weight_gradient(hidden, out_narrow)).reshape(chips, units, EMBED)
    w_o_rows = lax.dynamic_slice_in_dim(w_o, core * OWN, OWN, 0)
    value_scatter = [
        Scatter(grad_value[..., i * OWN : (i + 1) * OWN], 2 + i).prepare() for i in range(2)
    ]
    hidden, positive, out_narrow, w_o_rows, *sent = meet(
        value_parts, hidden, positive, out_narrow, w_o_rows, *[m.sent[0] for m in value_scatter]
    )
    for part, x in zip(value_scatter, sent):
        part.sent = [x]
        part.step()
    (value_weight,) = assemble(value_parts)

    pre_narrow = narrow(2.0 * positive * input_gradient_rows(out_narrow, value_weight))
    ffn_in_grad = narrow(input_gradient_rows(pre_narrow, key_weight))
    other_grad = swap(ffn_in_grad, 1)
    grad_key = narrow(weight_gradient(ffn_in, pre_narrow)).reshape(chips, pair_share, half_units)
    residual_grad, own_grad, gated_grad, ffn_vec = ffn_backward(
        length, residual, cot, ffn_in_grad, other_grad, vectors, w_o_rows
    )
    key_scatter = [
        Scatter(grad_key[:, :, i * half : (i + 1) * half], 2 + i).prepare() for i in range(2)
    ]
    gated_grad, *sent = meet([], gated_grad, *[m.sent[0] for m in key_scatter])
    for part, x in zip(key_scatter, sent):
        part.sent = [x]
        part.step()
    terms = [*terms, gated_grad, *saved]
    zero_sums = jnp.zeros((8, OWN), jnp.float32)
    early = blocks // 2
    *before, sums, state = wkv_backward(
        early, blocks - early, length, used, zero_state, zero_sums, terms
    )
    state, sums = meet(value_scatter, state, sums)
    for part in value_scatter:
        part.step()
    *low_grads, own_vec, _ = wkv_backward(0, early, length, used, state, sums, terms, before)
    if pair_share == 64:
        sent_a, kept_a, sent_b, kept_b = att_gradients(
            (mixes[0], mixes[2], mixes[3]), gated_all, low_grads[:3], own_grad
        )
        att_scatter = [Scatter.begun(sent_a, kept_a, 2), Scatter.begun(sent_b, kept_b, 3)]
    else:
        grads = [weight_gradient(mixes[m], g) for m, g in zip((0, 2, 3), low_grads)]
        grad_o = weight_gradient(gated_all, own_grad)
        att_scatter = [
            Scatter(
                narrow(jnp.concatenate(x, axis=1)).reshape(chips, pair_share, EMBED), 2 + i
            ).prepare()
            for i, x in enumerate(((grads[0], grad_o), (grads[1], grads[2])))
        ]
    own_vec, *sent = meet(
        key_scatter + value_scatter, own_vec, *[m.sent[0] for m in att_scatter]
    )
    for part, x in zip(att_scatter, sent):
        part.sent = [x]
        part.step()
    for part in key_scatter:
        part.step()
    together(value_scatter)
    own_vec, *_ = meet([], own_vec, *[m.sent_now for m in key_scatter])
    token_part, misc_mine, misc_other = front_backward(
        tokens, vectors, w_r, w_k, w_v, down, up_t, (mixes[1], mixes[4], mixes[5]), hid,
        low_grads, own_vec, ffn_vec,
    )
    misc_other = swap(misc_other, 1)
    token_part, misc_mine, misc_other = meet(
        att_scatter + key_scatter + value_scatter, token_part, misc_mine, misc_other
    )
    for part in att_scatter:
        part.step()
    misc_sum = misc_mine + misc_other.astype(jnp.float32)
    misc_sum = jnp.concatenate([misc_sum[..., :320], misc_sum[..., 320:]], axis=1)
    misc_scatter = Scatter(misc_sum, 3).step()
    together(key_scatter)
    together(value_scatter)
    (token_part,) = meet([misc_scatter], token_part)
    misc_scatter.step()
    token_part, _ = meet(key_scatter, token_part, misc_scatter.sent_now)
    together(key_scatter)
    (token_part,) = meet(att_scatter + [misc_scatter], token_part)
    masks = chip_masks()
    last_parts = att_scatter + [misc_scatter]
    if len(misc_scatter.steps) == 2:
        for part in last_parts:
            part.steps = [[masks[2], masks[3], masks[2] | masks[3]]]
    together(last_parts)
    hidden, *_ = meet([], hidden, *[m.sent_now for m in last_parts])
    ffn_part = product(hidden, value_weight)
    input_gradient = (
        own_rows(residual_grad, core)
        + own_rows(token_part, core)
        + swap(own_rows(token_part, 1 - core), 1)
    )
    ffn_out = own_rows(ffn_part, core) + swap(own_rows(ffn_part, 1 - core), 1)
    output = narrow(jnp.where(own_rows(live, core), own_rows(residual, core) + ffn_out, 0.0))
    value_sum = jnp.concatenate(
        [x.run().total() for x in value_scatter], axis=1
    )
    while key_scatter[0].steps:
        together(key_scatter)
    key_sum = jnp.concatenate([x.total() for x in key_scatter], axis=1).reshape(2, share, -1)

    def exchange(x):
        mine = lax.dynamic_index_in_dim(x, core, 0, keepdims=False)
        return mine, swap(lax.dynamic_index_in_dim(x, 1 - core, 0, keepdims=False), 1)

    key_mine, key_theirs = exchange(key_sum)
    input_gradient, value_sum, key_mine, key_theirs = meet(
        last_parts, input_gradient, value_sum, key_mine, key_theirs
    )
    while last_parts[0].steps:
        together(last_parts)
    first_sum, second_sum, misc_sum = [x.total() for x in last_parts]
    misc_sum = jnp.concatenate([misc_sum[:share], misc_sum[share:]], axis=1)
    att_sum = jnp.concatenate(
        [first_sum[:, :OWN], second_sum, first_sum[:, OWN:]], axis=1
    )
    mine, theirs = exchange(att_sum.reshape(2, share, -1))
    shard_mixer = jnp.stack(
        [
            in_order(1, mine[:, i * OWN : (i + 1) * OWN], theirs[:, i * OWN : (i + 1) * OWN], 1)
            for i in range(4)
        ]
    )
    shard_key = in_order(
        1,
        key_mine.reshape(share, chips, 1, units),
        key_theirs.reshape(share, chips, 1, units),
        2,
    ).reshape(share, 2 * half_units)
    return (
        output,
        input_gradient,
        shard_mixer,
        shard_key,
        value_sum,
        misc_sum[:, :256],
        misc_sum[:, 256:512].T,
        misc_sum[:, 512:530].T,
    )


def solution(mesh):
    in_specs = (
        P("dp", None),
        P(),
        P(None, "dp", None),
        P("dp", None),
        P("dp", None),
        P("dp", None),
        P(None, "dp"),
        P(None, "dp"),
        P("dp", None),
    )
    out_specs = (
        P("dp", None),
        P("dp", None),
        P(None, "dp", None),
        P("dp", None),
        P("dp", None),
        P("dp", None),
        P(None, "dp"),
        P(None, "dp"),
    )
    return jax.shard_map(local, mesh=mesh, in_specs=in_specs, out_specs=out_specs, check_vma=False)
```
